32 devices in a mesh: seq: 16 (over z, y, x), tp: 2 (over core).
Axes of the slice: x: 2, y: 2, z: 4, core: 2. Of those that a mesh axis runs over, the one named last changes fastest.
Arguments:
- byte_states: bfloat16 [2, 4096, 1024], P(None, 'seq'), may hold values from -6 to 6
- lengths: int32 [2], replicated, may hold values from 512 to 2048, as said below
- w_patch: bfloat16 [1024, 8192], P(None, 'tp'), may hold values from -0.0625 to 0.0625
- norm_global: bfloat16 [1024], replicated, may hold values from 0.5 to 1.5
- w_in: bfloat16 [1024, 4640], P(None, 'tp'), may hold values from -0.1875 to 0.1875
- conv_w: bfloat16 [4, 2560], P(None, 'tp'), may hold values from -3 to 3
- conv_b: bfloat16 [2560], P('tp'), may hold values from -0.5 to 0.5
- dt_bias: bfloat16 [32], P('tp'), may hold values from -3 to -1
- a_log: bfloat16 [32], P('tp'), may hold values from -12 to 0
- d_skip: bfloat16 [32], P('tp'), may hold values from 0.5 to 1.5
- mix_gain: bfloat16 [2048], P('tp'), may hold values from 0.5 to 1.5
- w_out: bfloat16 [1024, 2048], P(None, 'tp'), may hold values from -0.125 to 0.125
- norm_attn: bfloat16 [1024], replicated, may hold values from 0.5 to 1.5
- w_qkv: bfloat16 [1024, 3072], P(None, 'tp'), may hold values from -0.1875 to 0.1875
- w_o: bfloat16 [1024, 1024], P(None, 'tp'), may hold values from -0.375 to 0.375
- norm_mlp: bfloat16 [1024], replicated, may hold values from 0.5 to 1.5
- w_gate: bfloat16 [1024, 4096], P(None, 'tp'), may hold values from -0.1875 to 0.1875
- w_up: bfloat16 [1024, 4096], P(None, 'tp'), may hold values from -0.1875 to 0.1875
- w_down: bfloat16 [1024, 4096], P(None, 'tp'), may hold values from -0.09375 to 0.09375
- w_head: bfloat16 [1024, 256], P(None, 'tp'), may hold values from -0.1875 to 0.1875
- d_logits: bfloat16 [2, 4096, 256], P(None, 'seq', 'tp'), may hold values from -6 to 6
Outputs:
- logits: float32 [2, 4096, 256], P(None, 'seq', 'tp')
- grad_bytes: float32 [2, 4096, 1024], P(None, 'seq', 'tp')
- grad_w_patch: float32 [1024, 8192], P('seq', 'tp')
- grad_norm_global: float32 [1024], replicated
- grad_w_in: float32 [1024, 4640], P('seq', 'tp')
- grad_conv_w: float32 [4, 2560], P(None, 'tp')
- grad_conv_b: float32 [2560], P('tp')
- grad_dt_bias: float32 [32], P('tp')
- grad_a_log: float32 [32], P('tp')
- grad_d_skip: float32 [32], P('tp')
- grad_mix_gain: float32 [2048], P('tp')
- grad_w_out: float32 [1024, 2048], P('seq', 'tp')
- grad_norm_attn: float32 [1024], replicated
- grad_w_qkv: float32 [1024, 3072], P('seq', 'tp')
- grad_w_o: float32 [1024, 1024], P('seq', 'tp')
- grad_norm_mlp: float32 [1024], replicated
- grad_w_gate: float32 [1024, 4096], P('seq', 'tp')
- grad_w_up: float32 [1024, 4096], P('seq', 'tp')
- grad_w_down: float32 [1024, 4096], P('seq', 'tp')
- grad_w_head: float32 [1024, 256], P('seq', 'tp')
The draws below stay inside these ranges and needn't reach their ends.
Inputs may be any that keep to these rules, and one draw needn't show every extreme that they name: `lengths`: each length is a multiple of 8, and one equals 2048.
All inputs are finite; a program needn't handle non-finite values.
Results may differ from the reference program's by a relative error of at most 0.019.
Values sent between devices are 32-bit elements; how exact they have to be, the bound alone decides.
No kernel may reach another device: no remote copies, remote signals or barrier semaphores. Data moves between devices by JAX's collectives and lax.ppermute only.
A program may use at most 320 MiB of HBM per device.

```python
from functools import partial
import jax
import jax.numpy as jnp
from jax import lax

D = 1024
DI = 2048
NH = 32
HD = 64
NS = 128
LH = 16
AD = 64
FF = 4096
VOC = 256
P_DEV = 32
PATCHES = 512
SBYTES = 4096
SHORT_DOCS = 2
GC = 2320
CC = 1280
N_SEQ = 16


def draw_lengths(key, part):
    key = jax.random.fold_in(key, 7)
    first_key, second_key = jax.random.split(key)
    patch_counts = jax.random.randint(first_key, (SHORT_DOCS,), 2 * P_DEV, 8 * P_DEV + 1, dtype=jnp.int32)
    widest = jax.random.randint(second_key, (), 0, SHORT_DOCS, dtype=jnp.int32)
    patch_counts = jnp.where(jnp.arange(SHORT_DOCS, dtype=jnp.int32) == widest, 8 * P_DEV, patch_counts)
    return (8 * patch_counts).astype(jnp.int32)


def draw_a_log(key, part):
    key = jax.random.fold_in(key, 11)
    lower = jnp.log(0.3 / PATCHES)
    upper = jnp.log(0.3)
    return jax.random.uniform(key, (NH,), jnp.float32, lower, upper).astype(jnp.bfloat16)


def block_scale(key, dims, cuts, low, top_value):
    gain = 1.0
    for axis_at, parts in cuts:
        steps = jax.random.uniform(jax.random.fold_in(jax.random.fold_in(key, 6), axis_at), (parts,), jnp.float32, low / len(cuts), top_value / len(cuts))
        gain = gain * jnp.repeat(jnp.exp(steps), dims[axis_at] // parts).reshape((-1,) + (1,) * (len(dims) - 1 - axis_at))
    return gain


def scatter_about(own_key, dims, width, bound, cuts=(), held_as=jnp.bfloat16):
    loudness = block_scale(own_key, dims, cuts, -0.22, 0.18) if cuts else 1.0
    values = jax.random.normal(own_key, dims, jnp.float32) * width * loudness
    return jnp.minimum(jnp.maximum(values, -bound), bound).astype(held_as)


def setup_inputs(seed: int = 0) -> dict:
    arg_keys = jax.random.split(jax.random.key(seed), 22)
    byte_states = scatter_about(arg_keys[0], (2, SBYTES, D), 1.0, 6.0, ((1, 16),))
    lengths = draw_lengths(jax.random.fold_in(arg_keys[21], 71), 0)
    w_patch = scatter_about(arg_keys[2], (D, 8 * D), (8 * D) ** -0.5, 0.0625, ((1, 2),))
    norm_global = jnp.clip(1.0 + 0.1 * jax.random.normal(arg_keys[3], (D,), jnp.float32), 0.5, 1.5).astype(jnp.bfloat16)
    w_in = scatter_about(arg_keys[4], (D, 2 * GC), D ** -0.5, 0.1875, ((1, 2),))
    conv_w = scatter_about(arg_keys[5], (4, 2 * CC), 4 ** -0.5, 3.0, ((1, 2),))
    conv_b = jnp.clip(jax.random.uniform(arg_keys[6], (2 * CC,), jnp.float32, -0.5, 0.5) * block_scale(arg_keys[6], (2 * CC,), ((0, 2),), -0.4, 0.0), -0.5, 0.5).astype(jnp.bfloat16)
    dt_bias = jnp.clip(-3.0 + 2.0 * jax.random.uniform(arg_keys[7], (NH,), jnp.float32) ** block_scale(arg_keys[7], (NH,), ((0, 2),), -0.2, 0.2), -3.0, -1.0).astype(jnp.bfloat16)
    a_log = draw_a_log(jax.random.fold_in(arg_keys[21], 71), 0)
    d_skip = jnp.clip(0.5 + 1.0 * jax.random.uniform(arg_keys[9], (NH,), jnp.float32) ** block_scale(arg_keys[9], (NH,), ((0, 2),), -0.2, 0.2), 0.5, 1.5).astype(jnp.bfloat16)
    mix_gain = jnp.clip(1.0 + 0.1 * jax.random.normal(arg_keys[10], (DI,), jnp.float32), 0.5, 1.5).astype(jnp.bfloat16)
    w_out = scatter_about(arg_keys[11], (D, DI), DI ** -0.5, 0.125, ((1, 2),))
    norm_attn = jnp.clip(1.0 + 0.1 * jax.random.normal(arg_keys[12], (D,), jnp.float32), 0.5, 1.5).astype(jnp.bfloat16)
    w_qkv = scatter_about(arg_keys[13], (D, 3 * D), D ** -0.5, 0.1875, ((1, 2),))
    w_o = scatter_about(arg_keys[14], (D, D), (D // 4) ** -0.5, 0.375, ((1, 2),))
    norm_mlp = jnp.clip(1.0 + 0.1 * jax.random.normal(arg_keys[15], (D,), jnp.float32), 0.5, 1.5).astype(jnp.bfloat16)
    w_gate = scatter_about(arg_keys[16], (D, FF), D ** -0.5, 0.1875, ((1, 2),))
    w_up = scatter_about(arg_keys[17], (D, FF), D ** -0.5, 0.1875, ((1, 2),))
    w_down = scatter_about(arg_keys[18], (D, FF), FF ** -0.5, 0.09375, ((1, 2),))
    w_head = scatter_about(arg_keys[19], (D, VOC), D ** -0.5, 0.1875, ((1, 2),))
    d_logits = scatter_about(arg_keys[20], (2, SBYTES, VOC), 1.0, 6.0, ((1, 16), (2, 2)))
    return {"byte_states": byte_states, "lengths": lengths, "w_patch": w_patch, "norm_global": norm_global, "w_in": w_in, "conv_w": conv_w, "conv_b": conv_b, "dt_bias": dt_bias, "a_log": a_log, "d_skip": d_skip, "mix_gain": mix_gain, "w_out": w_out, "norm_attn": norm_attn, "w_qkv": w_qkv, "w_o": w_o, "norm_mlp": norm_mlp, "w_gate": w_gate, "w_up": w_up, "w_down": w_down, "w_head": w_head, "d_logits": d_logits}


epsilon = 1e-05
highest = lax.Precision.HIGHEST
masked_score = -1e+30

@jax.custom_vjp
def low(v):
    return lax.optimization_barrier(v.astype(jnp.bfloat16)).astype(jnp.float32)

@jax.custom_vjp
def low_back(v):
    return v

def low_keep(v):
    return (low(v), None)

def low_pass(kept, grad):
    return (grad,)

def back_keep(v):
    return (v, None)

def back_low(kept, grad):
    return (low(grad),)
low.defvjp(low_keep, low_pass)
low_back.defvjp(back_keep, back_low)

def dot_high(left_side, right_side):
    return jnp.einsum('...k,kn->...n', left_side, right_side, precision=highest)

def dot_high_t(left_side, right_side):
    return jnp.einsum('...k,nk->...n', left_side, right_side, precision=highest)

def rms_norm(values, gain_values):
    return values * lax.rsqrt(lax.optimization_barrier(jnp.mean(values * values, axis=-1, keepdims=True)) + epsilon) * gain_values

def segment_ids(lengths):
    ends = jnp.cumsum(lengths // 8, dtype=jnp.int32)
    places = jnp.arange(PATCHES, dtype=jnp.int32)
    short_ids = lax.optimization_barrier(jnp.sum((places[:, None] >= ends[None, :]).astype(jnp.int32), axis=1, dtype=jnp.int32))
    return jnp.stack([jnp.zeros_like(short_ids), short_ids])

def ssd_block(lane_params, carry, block):
    a_logs, skip_values = lane_params
    state, seg_last = carry
    active, step_sizes, seg_now = block
    lanes_count, patch_count = (active.shape[0], active.shape[1])
    head_count = step_sizes.shape[-1]
    inner_width = active.shape[-1] - 2 * NS
    values = active[..., :inner_width].reshape(lanes_count, patch_count, head_count, HD)
    in_keys = active[..., inner_width:inner_width + NS]
    out_keys = active[..., inner_width + NS:]
    cumulative = jnp.cumsum(-step_sizes * jnp.exp(a_logs)[:, None, :], axis=1)
    positions = jnp.arange(patch_count, dtype=jnp.int32)
    allowed = (seg_now[:, :, None] == seg_now[:, None, :]) & (positions[:, None] >= positions[None, :])[None]
    ordered = jnp.moveaxis(cumulative, 1, 2)
    gap_values = ordered[:, :, :, None] - ordered[:, :, None, :]
    open_mask = allowed[:, None]
    decays = jnp.where(open_mask, jnp.exp(jnp.where(open_mask, gap_values, 0.0)), 0.0)
    intersection = jnp.einsum('spn,sjn->spj', out_keys, in_keys, precision=highest)
    mixing = intersection[:, None] * decays * jnp.moveaxis(step_sizes, 1, 2)[:, :, None, :]
    result = jnp.einsum('shpj,sjhd->sphd', mixing, values, precision=highest)
    entering = jnp.exp(cumulative) * (seg_now == seg_last[:, None]).astype(jnp.float32)[..., None]
    result = result + jnp.einsum('spn,shdn->sphd', out_keys, state, precision=highest) * entering[..., None]
    result = result + skip_values[:, None, :, None] * values
    last_same = (seg_now == seg_now[:, -1:]).astype(jnp.float32)
    weight_end = jnp.exp(cumulative[:, -1:] - cumulative) * last_same[..., None] * step_sizes
    state_end = jnp.einsum('sjh,sjhd,sjn->shdn', weight_end, values, in_keys, precision=highest)
    through = jnp.exp(cumulative[:, -1]) * (seg_now[:, -1] == seg_last).astype(jnp.float32)[:, None]
    new_state = through[..., None, None] * state + state_end
    return ((new_state, seg_now[:, -1]), result)

def to_lanes(stacked):
    swapped = jnp.swapaxes(stacked, 1, 2)
    return swapped.reshape((4, stacked.shape[1]) + stacked.shape[3:])

def to_blocks(array_in):
    shaped = array_in.reshape((4, N_SEQ, P_DEV) + array_in.shape[2:])
    return jnp.moveaxis(shaped, 1, 0)

def mixer(u_low, seg, valid, w_in, conv_w, conv_b, dt_bias, a_log, d_skip, mix_gain, w_out):
    streams, patch_count = seg.shape
    proj = low_back(dot_high(u_low, w_in)).reshape(streams, patch_count, 2, -1)
    inner_width = DI // 2
    channels = inner_width + 2 * NS
    gate_in = proj[..., :inner_width]
    xbc = proj[..., inner_width:inner_width + channels]
    dt_raw = proj[..., inner_width + channels:]
    taps = conv_w.reshape(4, 2, channels)
    conv_sum = conv_b.reshape(2, channels) + taps[3] * xbc
    for offset in range(3):
        distance = 3 - offset
        earlier = jnp.pad(xbc, ((0, 0), (distance, 0), (0, 0), (0, 0)))[:, :patch_count]
        seg_earlier = jnp.pad(seg, ((0, 0), (distance, 0)), constant_values=-1)[:, :patch_count]
        same_doc = (seg_earlier == seg).astype(jnp.float32)
        conv_sum = conv_sum + taps[offset] * earlier * same_doc[:, :, None, None]
    active = to_lanes(jax.nn.silu(conv_sum))
    step_sizes = to_lanes(jax.nn.softplus(dt_raw + dt_bias.reshape(2, -1)))
    gate_lanes = to_lanes(gate_in)
    seg_lanes = jnp.repeat(seg, 2, axis=0)
    a_lane = jnp.tile(a_log.reshape(2, -1), (2, 1))
    skip_lane = jnp.tile(d_skip.reshape(2, -1), (2, 1))
    gain_lane = jnp.tile(mix_gain.reshape(2, -1), (2, 1))
    start = (jnp.zeros((4, NH // 2, HD, NS), jnp.float32), jnp.full((4,), -1, jnp.int32))
    stepper = jax.checkpoint(partial(ssd_block, (a_lane, skip_lane)))
    unused_carry, outputs = lax.scan(stepper, start, (to_blocks(active), to_blocks(step_sizes), to_blocks(seg_lanes)))
    result = jnp.moveaxis(outputs, 0, 1).reshape(4, patch_count, -1)
    gated = result * jax.nn.silu(gate_lanes)
    normed = gated * lax.rsqrt(lax.optimization_barrier(jnp.mean(gated * gated, axis=-1, keepdims=True)) + epsilon) * gain_lane[:, None, :]
    normed = jnp.swapaxes(normed.reshape(2, 2, patch_count, -1), 1, 2).reshape(streams, patch_count, -1)
    return low_back(dot_high_t(low(normed), w_out)) * valid[..., None]

def local_section(weights, block):
    norm_attn, w_qkv, w_o, norm_mlp, w_gate, w_up, w_down, w_head = weights
    row_values, byte_mask = block
    row_count, model_width = row_values.shape
    half_width = model_width // 2
    attn_in = low(rms_norm(row_values, norm_attn))
    qkv = low_back(dot_high(attn_in, w_qkv)).reshape(row_count, 2, 3, half_width)
    queries = low(qkv[:, :, 0].reshape(row_count // 8, 8, LH, AD))
    key_heads = low(qkv[:, :, 1].reshape(row_count // 8, 8, LH, AD))
    value_heads = low(qkv[:, :, 2].reshape(row_count // 8, 8, LH, AD))
    scores = low_back(jnp.einsum('pihd,pjhd->phij', queries, key_heads, precision=highest) * 0.125)
    causal = jnp.arange(8, dtype=jnp.int32)[:, None] >= jnp.arange(8, dtype=jnp.int32)[None, :]
    attention_probs = low(jax.nn.softmax(jnp.where(causal, scores, masked_score), axis=-1))
    mixed_heads = low_back(jnp.einsum('phij,pjhd->pihd', attention_probs, value_heads, precision=highest))
    mixed_heads = mixed_heads.reshape(row_count, model_width)
    after_attn = row_values + low_back(dot_high_t(low(mixed_heads), w_o))
    mlp_in = low(rms_norm(after_attn, norm_mlp))
    gate_proj = low_back(dot_high(mlp_in, w_gate))
    up_proj = low_back(dot_high(mlp_in, w_up))
    hidden = low(jax.nn.silu(gate_proj) * up_proj)
    after_mlp = after_attn + low_back(dot_high_t(hidden, w_down))
    return dot_high(low(after_mlp), w_head) * byte_mask[:, None]

def reference(byte_states, lengths, w_patch, norm_global, w_in, conv_w, conv_b, dt_bias, a_log, d_skip, mix_gain, w_out, norm_attn, w_qkv, w_o, norm_mlp, w_gate, w_up, w_down, w_head, d_logits):
    seg = segment_ids(lengths)
    valid = (seg < SHORT_DOCS).astype(jnp.float32)
    byte_mask = jnp.repeat(valid, 8, axis=1)

    def forward(bytes_in, w_patch, norm_global, w_in, conv_w, conv_b, dt_bias, a_log, d_skip, mix_gain, w_out, norm_attn, w_qkv, w_o, norm_mlp, w_gate, w_up, w_down, w_head):
        streams, total_bytes, model_width = bytes_in.shape
        patch_count = total_bytes // 8
        patch_vec = jnp.swapaxes(bytes_in.reshape(streams, patch_count, 8, model_width), 2, 3).reshape(streams, patch_count, 8 * model_width)
        patch_out = low_back(dot_high_t(patch_vec, w_patch))
        u_low = low(rms_norm(patch_out, norm_global))
        global_out = patch_out + mixer(u_low, seg, valid, w_in, conv_w, conv_b, dt_bias, a_log, d_skip, mix_gain, w_out)
        stream_in = bytes_in + jnp.repeat(global_out, 8, axis=1)
        block_rows = 64 * P_DEV
        rows_blocked = stream_in.reshape(-1, block_rows, model_width)
        masks_blocked = byte_mask.reshape(-1, block_rows)
        local_weights = (norm_attn, w_qkv, w_o, norm_mlp, w_gate, w_up, w_down, w_head)
        outputs = lax.map(jax.checkpoint(partial(local_section, local_weights)), (rows_blocked, masks_blocked))
        return outputs.reshape(streams, total_bytes, -1)
    primals = tuple((argument.astype(jnp.float32) for argument in (byte_states, w_patch, norm_global, w_in, conv_w, conv_b, dt_bias, a_log, d_skip, mix_gain, w_out, norm_attn, w_qkv, w_o, norm_mlp, w_gate, w_up, w_down, w_head)))
    logits, pullback = jax.vjp(forward, *primals)
    grads = pullback(d_logits.astype(jnp.float32))
    return (logits, grads[0], grads[1], grads[2], grads[3], grads[4], grads[5], grads[6], grads[7], grads[8], grads[9], grads[10], grads[11], grads[12], grads[13], grads[14], grads[15], grads[16], grads[17], grads[18])
```

```python
from functools import partial

import jax
import jax.numpy as jnp
from jax import lax
from jax.experimental import pallas as pl
from jax.experimental.pallas import tpu as pltpu
from jax.sharding import PartitionSpec as P

NS = 128
AD = 64


epsilon = 1e-05
highest = lax.Precision.HIGHEST
masked_score = -1e30


def dot_plain(left_side, right_side):
    return jnp.dot(left_side, right_side, preferred_element_type=jnp.float32)


def dot_trans(left_side, right_side):
    return lax.dot_general(
        left_side, right_side, (((1,), (1,)), ((), ())), preferred_element_type=jnp.float32
    )


def dot_left(left_side, right_side):
    return lax.dot_general(
        left_side, right_side, (((0,), (0,)), ((), ())), preferred_element_type=jnp.float32
    )


def rms_scale(values):
    return lax.rsqrt(jnp.mean(values * values, axis=-1, keepdims=True) + epsilon)


def rms_back(values, gain_values, grad_out):
    scale = rms_scale(values)
    scaled = gain_values * grad_out
    inner_mean = jnp.mean(values * scaled, axis=-1, keepdims=True)
    grad_values = scale * scaled - values * scale * scale * scale * inner_mean
    grad_gain = jnp.sum(values * scale * grad_out, axis=0)
    return (grad_values, grad_gain)


def swap(block, axis, mask):
    return lax.ppermute(block, axis, [(i, i ^ mask) for i in range(lax.axis_size(axis))])


def tp_sum(block):
    return block + swap(block, "tp", 1)


def seq_bits():
    return lax.axis_size("seq").bit_length() - 1


def seq_sum(block):
    for bit in range(seq_bits()):
        block = block + swap(block, "seq", 1 << bit)
    return block


def bit_order(first):
    bits = list(range(seq_bits()))
    return bits if first == 0 else [1, 0] + bits[2:]


def own_rows(left_side, order):
    parts = lax.axis_size("seq")
    here = lax.axis_index("seq")
    blocks = left_side.T.reshape(parts, left_side.shape[1] // parts, left_side.shape[0])
    places = []
    for place in range(parts):
        relative = 0
        for at, bit in enumerate(order):
            if place >> (len(order) - 1 - at) & 1:
                relative |= 1 << bit
        places.append(lax.dynamic_index_in_dim(blocks, here ^ relative, 0, keepdims=False))
    return jnp.concatenate(places, axis=0)


def reduce_rows(pairs, first):
    order = bit_order(first)
    lefts = [own_rows(left_side, order) for left_side, unused in pairs]
    rights = [right_side for unused, right_side in pairs]

    def product(start, stop):
        parts = [dot_plain(a[start:stop], b) for a, b in zip(lefts, rights)]
        return parts[0] if len(parts) == 1 else jnp.concatenate(parts, axis=1)

    rows = lefts[0].shape[0]
    half, quarter = rows // 2, rows // 4
    got = swap(product(half, rows), "seq", 1 << order[0])
    far = product(quarter, half) + got[quarter:]
    part = product(0, quarter) + got[:quarter] + swap(far, "seq", 1 << order[1])
    for bit in order[2:]:
        rest = part.shape[0] // 2
        part = part[:rest] + swap(part[rest:], "seq", 1 << bit)
    return part


def segment_ids(lengths, place_count):
    ends = jnp.cumsum(lengths // 8, dtype=jnp.int32)
    places = jnp.arange(place_count, dtype=jnp.int32)
    short_ids = jnp.sum(
        (places[:, None] >= ends[None, :]).astype(jnp.int32), axis=1, dtype=jnp.int32
    )
    return jnp.stack([jnp.zeros_like(short_ids), short_ids])


def scan_heads(seg_now, head_size, xbc, dt_raw, conv_weight, conv_bias, dt_shift, a_logs, skips):
    place_count = xbc.shape[0]
    conv_sum = conv_bias + conv_weight[3] * xbc
    for offset in range(3):
        distance = 3 - offset
        earlier = jnp.pad(xbc, ((distance, 0), (0, 0)))[:place_count]
        seg_earlier = jnp.pad(seg_now, (distance, 0), constant_values=-1)[:place_count]
        same_doc = (seg_earlier == seg_now).astype(jnp.float32)
        conv_sum = conv_sum + conv_weight[offset] * earlier * same_doc[:, None]
    active = jax.nn.silu(conv_sum)
    head_count = dt_raw.shape[1]
    inner = head_count * head_size
    values = active[:, :inner].reshape(place_count, head_count, head_size)
    in_keys = active[:, inner : inner + NS]
    out_keys = active[:, inner + NS :]
    step_sizes = jax.nn.softplus(dt_raw + dt_shift)
    decay_rates = -step_sizes * jnp.exp(a_logs)
    chunk = min(place_count, 512)
    triangle = jnp.tril(jnp.ones((chunk, chunk), jnp.float32))
    state = jnp.zeros((head_count, head_size, NS), jnp.float32)
    seg_last = jnp.int32(-1)
    outputs = []
    for start in range(0, place_count, chunk):
        stop = start + chunk
        x, b, c = values[start:stop], in_keys[start:stop], out_keys[start:stop]
        dt, seg = step_sizes[start:stop], seg_now[start:stop]
        cumulative = jnp.dot(triangle, decay_rates[start:stop], precision=highest)
        allowed = (triangle > 0.0) & (seg[:, None] == seg[None, :])
        ordered = cumulative.T
        gaps = ordered[:, :, None] - ordered[:, None, :]
        decays = jnp.where(allowed, jnp.exp(jnp.where(allowed, gaps, 0.0)), 0.0)
        crossing = jnp.einsum("pn,jn->pj", c, b, precision=highest)
        mixing = crossing[None] * decays * dt.T[:, None, :]
        result = jnp.einsum("hpj,jhd->phd", mixing, x, precision=highest)
        if start > 0:
            entering = jnp.exp(cumulative) * (seg == seg_last).astype(jnp.float32)[:, None]
            result = result + entering[..., None] * jnp.einsum(
                "pn,hdn->phd", c, state, precision=highest
            )
        if stop < place_count:
            last_same = (seg == seg[-1]).astype(jnp.float32)[:, None]
            weight = jnp.exp(cumulative[-1:] - cumulative) * last_same * dt
            through = jnp.exp(cumulative[-1]) * (seg[-1] == seg_last).astype(jnp.float32)
            state = through[:, None, None] * state + jnp.einsum(
                "jh,jhd,jn->hdn", weight, x, b, precision=highest
            )
            seg_last = seg[-1]
        outputs.append(result + skips[:, None] * x)
    return jnp.concatenate(outputs, axis=0).reshape(place_count, inner)


def gated_norm(result, gate_in, mix_scale):
    gated = result * jax.nn.silu(gate_in)
    return gated * rms_scale(gated) * mix_scale


def patch_grad_kernel(grad_ref, *refs):
    byte_refs, out_ref, order_ref = refs[:8], refs[8], refs[9]
    width = byte_refs[0].shape[1]
    total = 8 * width

    @pl.when(pl.program_id(0) == 0)
    def _():
        row = lax.broadcasted_iota(jnp.int32, (total, total), 0)
        col = lax.broadcasted_iota(jnp.int32, (total, total), 1)
        order_ref[...] = jnp.where(row == (col % 8) * width + col // 8, 1.0, 0.0).astype(
            jnp.bfloat16
        )

    grad_low = grad_ref[...].astype(jnp.bfloat16)
    wide = jnp.concatenate([ref[...].astype(jnp.bfloat16) for ref in byte_refs], axis=1)
    grad = dot_left(grad_low, wide)
    high = grad.astype(jnp.bfloat16)
    rest = grad - high.astype(jnp.float32)
    mid = rest.astype(jnp.bfloat16)
    low = (rest - mid.astype(jnp.float32)).astype(jnp.bfloat16)
    order = order_ref[...]
    out_ref[...] = dot_plain(high, order) + (dot_plain(mid, order) + dot_plain(low, order))


def patch_grad(grad_rows, bytes_all):
    places, row_block = grad_rows.shape
    feature = bytes_all.shape[1] // 8
    chunk = 128
    steps = feature // chunk

    def byte_spec(j):
        return pl.BlockSpec((places, chunk), lambda i: (0, j * steps + i))

    return pl.pallas_call(
        patch_grad_kernel,
        grid=(steps,),
        in_specs=[pl.BlockSpec((places, row_block), lambda i: (0, 0))]
        + [byte_spec(j) for j in range(8)],
        out_specs=pl.BlockSpec((row_block, 8 * chunk), lambda i: (0, i)),
        out_shape=jax.ShapeDtypeStruct((row_block, 8 * feature), jnp.float32),
        scratch_shapes=[pltpu.VMEM((8 * chunk, 8 * chunk), jnp.bfloat16)],
        compiler_params=pltpu.CompilerParams(vmem_limit_bytes=52 * 1024 * 1024),
    )(grad_rows, *([bytes_all] * 8))


def trade(blocks):
    return lax.all_to_all(blocks, "seq", 0, 0, tiled=True)


def attention_parts(row_values, gain_values, w_qkv):
    row_count = row_values.shape[0]
    attn_in = (row_values * rms_scale(row_values) * gain_values).astype(jnp.bfloat16)
    qkv = dot_plain(attn_in, w_qkv).astype(jnp.bfloat16)
    head_part = qkv.shape[1] // 3
    shaped = qkv.reshape(row_count // 8, 8, 3, head_part // AD, AD)
    queries, key_heads, value_heads = (shaped[:, :, 0], shaped[:, :, 1], shaped[:, :, 2])
    scores = (
        jnp.einsum("pihd,pjhd->phij", queries, key_heads, preferred_element_type=jnp.float32)
        * 0.125
    )
    causal = jnp.arange(8, dtype=jnp.int32)[:, None] >= jnp.arange(8, dtype=jnp.int32)[None, :]
    attention_probs = jax.nn.softmax(jnp.where(causal, scores, masked_score), axis=-1)
    probs_low = attention_probs.astype(jnp.bfloat16)
    mixed_heads = jnp.einsum(
        "phij,pjhd->pihd", probs_low, value_heads, preferred_element_type=jnp.float32
    )
    mixed_low = mixed_heads.reshape(row_count, head_part).astype(jnp.bfloat16)
    return (attn_in, queries, key_heads, value_heads, attention_probs, probs_low, mixed_low)


def mlp_parts(row_values, gain_values, w_gate, w_up):
    mlp_in = (row_values * rms_scale(row_values) * gain_values).astype(jnp.bfloat16)
    gate_proj = dot_plain(mlp_in, w_gate)
    up_proj = dot_plain(mlp_in, w_up)
    hidden_low = (jax.nn.silu(gate_proj) * up_proj).astype(jnp.bfloat16)
    return (mlp_in, gate_proj, up_proj, hidden_low)


def body(
    byte_states,
    lengths,
    w_patch,
    norm_global,
    w_in,
    conv_w,
    conv_b,
    dt_bias,
    a_log,
    d_skip,
    mix_gain,
    w_out,
    norm_attn,
    w_qkv,
    w_o,
    norm_mlp,
    w_gate,
    w_up,
    w_down,
    w_head,
    d_logits,
):
    streams, local_rows, model_width = byte_states.shape
    patch_count = local_rows // 8
    patch_total = streams * patch_count
    row_total = streams * local_rows
    feature = w_patch.shape[1] // 8
    inner_width = w_out.shape[1]
    channels = conv_w.shape[1]
    head_total = dt_bias.shape[0]
    head_cols = w_head.shape[1]
    parts = lax.axis_size("seq")
    tp_index = lax.axis_index("tp")
    seq_index = lax.axis_index("seq")
    places = parts * patch_count
    f32 = jnp.float32

    lanes = parts // streams
    width = inner_width // lanes
    full_head = inner_width // head_total
    own_heads = max(1, width // full_head)
    shared = max(1, full_head // width)
    head_size = width // own_heads
    own_stream = seq_index // lanes
    first_col = (seq_index % lanes) * width
    first_head = first_col // full_head

    seg_full = segment_ids(lengths, places)
    seg_own = lax.dynamic_slice_in_dim(seg_full, seq_index * patch_count, patch_count, 1)
    seg_stream = lax.dynamic_index_in_dim(seg_full, own_stream, 0, keepdims=False)
    valid = (seg_own < lengths.shape[0]).astype(f32).reshape(patch_total, 1)
    byte_valid = jnp.repeat(valid, 8, axis=0)

    grad_logits = d_logits.reshape(row_total, head_cols) * byte_valid.astype(jnp.bfloat16)
    grad_final = tp_sum(dot_trans(grad_logits, w_head))

    grid = byte_states.reshape(streams, patch_count, 8, model_width)
    own_part = lax.dynamic_slice_in_dim(grid, tp_index * feature, feature, 3)
    patch_vec = jnp.swapaxes(own_part, 2, 3).reshape(patch_total, feature * 8)
    patch_out = tp_sum(dot_trans(patch_vec, w_patch))
    gain_global = norm_global.astype(f32)
    u_low = (patch_out * rms_scale(patch_out) * gain_global).astype(jnp.bfloat16)
    proj = dot_plain(u_low, w_in).reshape(streams, patch_count, -1)
    gate_in = proj[..., :inner_width]
    xbc = proj[..., inner_width : inner_width + channels]
    dt_raw = proj[..., inner_width + channels :]

    def by_lane(columns):
        split = columns.reshape(streams, patch_count, lanes, -1)
        return jnp.moveaxis(split, 2, 1).reshape(parts, patch_count, -1)

    def from_lanes(blocks):
        split = blocks.reshape(streams, lanes, patch_count, -1)
        return jnp.moveaxis(split, 1, 2).reshape(streams, patch_count, -1)

    def to_all_lanes(columns):
        wide = jnp.broadcast_to(
            columns[:, None], (streams, lanes, patch_count, columns.shape[-1])
        )
        return wide.reshape(parts, patch_count, -1)

    pad_width = 128 - own_heads
    dt_lanes = by_lane(jnp.repeat(dt_raw, shared, axis=2))
    sent = jnp.concatenate(
        [
            by_lane(xbc[..., :inner_width]),
            to_all_lanes(xbc[..., inner_width:]),
            jnp.pad(dt_lanes, ((0, 0), (0, 0), (0, pad_width))),
        ],
        axis=-1,
    )
    taken = trade(sent).reshape(places, -1)
    scan_width = width + channels - inner_width

    def own_cols(param):
        mine = lax.dynamic_slice_in_dim(param, first_col, width, param.ndim - 1)
        return jnp.concatenate([mine, param[..., inner_width:]], axis=-1).astype(f32)

    def own_head(param):
        return lax.dynamic_slice_in_dim(param, first_head, own_heads, 0).astype(f32)

    scan_args = (
        taken[:, :scan_width],
        taken[:, scan_width : scan_width + own_heads],
        own_cols(conv_w),
        own_cols(conv_b),
        own_head(dt_bias),
        own_head(a_log),
        own_head(d_skip),
    )
    scanned, scan_back = jax.vjp(partial(scan_heads, seg_stream, head_size), *scan_args)
    result = from_lanes(trade(scanned.reshape(parts, patch_count, width)))
    normed, norm_back = jax.vjp(gated_norm, result, gate_in, mix_gain.astype(f32))
    normed_low = normed.reshape(patch_total, inner_width).astype(jnp.bfloat16)

    bytes_wide = own_part.reshape(patch_total, 8 * feature).astype(f32)
    bytes_all = lax.all_gather(bytes_wide, "seq", axis=0, tiled=True)

    global_out = patch_out + valid * tp_sum(dot_trans(normed_low, w_out))
    stream_in = (
        byte_states.reshape(patch_total, 8, model_width).astype(f32) + global_out[:, None, :]
    ).reshape(row_total, model_width)
    gain_attn = norm_attn.astype(f32)
    gain_mlp = norm_mlp.astype(f32)
    attn_saved = attention_parts(stream_in, gain_attn, w_qkv)
    after_attn = stream_in + tp_sum(dot_trans(attn_saved[6], w_o))
    mlp_in, gate_proj, up_proj, hidden_low = mlp_parts(after_attn, gain_mlp, w_gate, w_up)

    grad_mlp_low = grad_final.astype(jnp.bfloat16)
    final_down = reduce_rows([(grad_mlp_low, hidden_low)], 0)
    grad_hidden = dot_plain(grad_mlp_low, w_down)
    sigmoid_gate = jax.nn.sigmoid(gate_proj)
    grad_gate_low = (
        grad_hidden * up_proj * sigmoid_gate * (1.0 + gate_proj * (1.0 - sigmoid_gate))
    ).astype(jnp.bfloat16)
    grad_up_low = (grad_hidden * gate_proj * sigmoid_gate).astype(jnp.bfloat16)
    grad_mlp_in = tp_sum(dot_trans(grad_gate_low, w_gate) + dot_trans(grad_up_low, w_up))
    final_gate = reduce_rows([(mlp_in, grad_gate_low)], 1)
    final_up = reduce_rows([(mlp_in, grad_up_low)], 0)
    after_mlp = after_attn + tp_sum(dot_trans(hidden_low, w_down))
    final_low = after_mlp.astype(jnp.bfloat16)
    logits = dot_plain(final_low, w_head) * byte_valid
    back_mlp, grad_norm_mlp = rms_back(after_attn, gain_mlp, grad_mlp_in)
    grad_mid = grad_final + back_mlp
    attn_in, queries, key_heads, value_heads, attention_probs, probs_low, mixed_low = attn_saved
    grad_attn_low = grad_mid.astype(jnp.bfloat16)
    grad_mixed = dot_plain(grad_attn_low, w_o).astype(jnp.bfloat16).reshape(queries.shape)
    grad_probs = jnp.einsum(
        "pihd,pjhd->phij", grad_mixed, value_heads, preferred_element_type=f32
    )
    grad_scores = (
        attention_probs
        * (grad_probs - jnp.sum(attention_probs * grad_probs, axis=-1, keepdims=True))
    ).astype(jnp.bfloat16)
    grad_queries = (
        jnp.einsum("phij,pjhd->pihd", grad_scores, key_heads, preferred_element_type=f32) * 0.125
    )
    grad_keys = (
        jnp.einsum("phij,pihd->pjhd", grad_scores, queries, preferred_element_type=f32) * 0.125
    )
    grad_values = jnp.einsum("phij,pihd->pjhd", probs_low, grad_mixed, preferred_element_type=f32)
    grad_qkv_low = (
        jnp.stack([grad_queries, grad_keys, grad_values], axis=2)
        .reshape(row_total, -1)
        .astype(jnp.bfloat16)
    )
    grad_attn_in = tp_sum(dot_trans(grad_qkv_low, w_qkv))
    final_attn = reduce_rows(
        [(attn_in, grad_qkv_low), (grad_attn_low, mixed_low), (final_low, grad_logits)], 1
    )
    back_attn, grad_norm_attn = rms_back(stream_in, gain_attn, grad_attn_in)
    grad_stream = grad_mid + back_attn
    grad_global = jnp.sum(grad_stream.reshape(patch_total, 8, model_width), axis=1)
    grad_mix_low = (grad_global * valid).astype(jnp.bfloat16)
    grad_normed = dot_plain(grad_mix_low, w_out).reshape(streams, patch_count, inner_width)
    grad_result, grad_gate_in, grad_mix_gain = norm_back(grad_normed)
    grad_z_low = grad_gate_in.reshape(patch_total, inner_width).astype(jnp.bfloat16)
    grad_scanned = trade(by_lane(grad_result)).reshape(places, width)
    final_mix = reduce_rows([(grad_mix_low, normed_low), (u_low, grad_z_low)], 0)
    scan_grads = scan_back(grad_scanned)
    back_sent = jnp.concatenate(
        [scan_grads[0], jnp.pad(scan_grads[1], ((0, 0), (0, pad_width)))], axis=-1
    )
    back_taken = trade(back_sent.reshape(parts, patch_count, -1))
    grad_x = from_lanes(back_taken[..., :width])
    by_stream = back_taken.reshape(streams, lanes, patch_count, -1)
    grad_bc = jnp.sum(by_stream[..., width:scan_width], axis=1)
    grad_dt = from_lanes(back_taken[..., scan_width : scan_width + own_heads])
    grad_dt = jnp.sum(grad_dt.reshape(streams, patch_count, head_total, shared), axis=-1)
    grad_rest_low = (
        jnp.concatenate([grad_x, grad_bc, grad_dt], axis=-1)
        .reshape(patch_total, -1)
        .astype(jnp.bfloat16)
    )
    grad_u = tp_sum(
        dot_trans(jnp.concatenate([grad_z_low, grad_rest_low], axis=-1), w_in)
    )
    final_rest = reduce_rows([(u_low, grad_rest_low)], 1)
    back_global, grad_norm_global = rms_back(patch_out, gain_global, grad_u)
    grad_patch = grad_global + back_global

    row_block = model_width // parts
    patch_sent = jnp.moveaxis(grad_patch.reshape(patch_total, parts, row_block), 1, 0)
    patch_taken = trade(patch_sent).reshape(-1, row_block)
    final_patch = patch_grad(patch_taken, bytes_all)
    grad_vec = dot_plain(grad_patch.astype(jnp.bfloat16), w_patch)
    grad_vec = grad_vec.reshape(streams, patch_count, feature, 8)
    grad_own = jnp.swapaxes(grad_vec, 2, 3).reshape(streams, local_rows, feature)
    grad_rows = lax.dynamic_slice_in_dim(
        grad_stream.reshape(streams, local_rows, model_width), tp_index * feature, feature, 2
    )
    grad_bytes = grad_rows + grad_own

    def place_cols(grad):
        blank = jnp.zeros(grad.shape[:-1] + (inner_width,), f32)
        mine = lax.dynamic_update_slice_in_dim(
            blank, grad[..., :width], first_col, grad.ndim - 1
        )
        return jnp.concatenate([mine, grad[..., width:]], axis=-1)

    def place_head(grad):
        return lax.dynamic_update_slice_in_dim(
            jnp.zeros((head_total,), f32), grad, first_head, 0
        )

    small = (
        place_cols(scan_grads[2]),
        place_cols(scan_grads[3]),
        place_head(scan_grads[4]),
        place_head(scan_grads[5]),
        place_head(scan_grads[6]),
        grad_mix_gain,
        grad_norm_global,
        grad_norm_attn,
        grad_norm_mlp,
    )
    flat = jnp.concatenate([part.reshape(-1) for part in small])
    count = flat.shape[0]
    fill = -count % 1024
    flat = seq_sum(jnp.pad(flat, (0, fill)).reshape(-1, 128)).reshape(-1)
    small_sums = []
    at = 0
    for part in small:
        small_sums.append(flat[at : at + part.size].reshape(part.shape))
        at += part.size

    qkv_cols, o_cols = w_qkv.shape[1], w_o.shape[1]
    return (
        logits.reshape(streams, local_rows, head_cols),
        grad_bytes,
        final_patch,
        small_sums[6],
        jnp.concatenate([final_mix[:, inner_width:], final_rest], axis=1),
        small_sums[0],
        small_sums[1],
        small_sums[2],
        small_sums[3],
        small_sums[4],
        small_sums[5],
        final_mix[:, :inner_width],
        small_sums[7],
        final_attn[:, :qkv_cols],
        final_attn[:, qkv_cols : qkv_cols + o_cols],
        small_sums[8],
        final_gate,
        final_up,
        final_down,
        final_attn[:, qkv_cols + o_cols :],
    )


def solution(mesh):
    in_specs = (
        P(None, "seq", None),
        P(),
        P(None, "tp"),
        P(),
        P(None, "tp"),
        P(None, "tp"),
        P("tp"),
        P("tp"),
        P("tp"),
        P("tp"),
        P("tp"),
        P(None, "tp"),
        P(),
        P(None, "tp"),
        P(None, "tp"),
        P(),
        P(None, "tp"),
        P(None, "tp"),
        P(None, "tp"),
        P(None, "tp"),
        P(None, "seq", "tp"),
    )
    out_specs = (
        P(None, "seq", "tp"),
        P(None, "seq", "tp"),
        P("seq", "tp"),
        P(),
        P("seq", "tp"),
        P(None, "tp"),
        P("tp"),
        P("tp"),
        P("tp"),
        P("tp"),
        P("tp"),
        P("seq", "tp"),
        P(),
        P("seq", "tp"),
        P("seq", "tp"),
        P(),
        P("seq", "tp"),
        P("seq", "tp"),
        P("seq", "tp"),
        P("seq", "tp"),
    )
    return jax.shard_map(body, mesh=mesh, in_specs=in_specs, out_specs=out_specs, check_vma=False)
```

```python
from functools import partial

import jax
import jax.numpy as jnp
from jax import lax
from jax.experimental import pallas as pl
from jax.experimental.pallas import tpu as pltpu
from jax.sharding import PartitionSpec as P

NS = 128
AD = 64
QUAD = 4


epsilon = 1e-05
highest = lax.Precision.HIGHEST
masked_score = -1e30


def dot_plain(left_side, right_side):
    return jnp.dot(left_side, right_side, preferred_element_type=jnp.float32)


def dot_trans(left_side, right_side):
    return lax.dot_general(
        left_side, right_side, (((1,), (1,)), ((), ())), preferred_element_type=jnp.float32
    )


def dot_left(left_side, right_side):
    return lax.dot_general(
        left_side, right_side, (((0,), (0,)), ((), ())), preferred_element_type=jnp.float32
    )


def rms_scale(values):
    return lax.rsqrt(jnp.mean(values * values, axis=-1, keepdims=True) + epsilon)


def hidden_parts(mlp_in, grad_hidden, w_gate, w_up):
    gate_proj = dot_plain(mlp_in, w_gate)
    up_proj = dot_plain(mlp_in, w_up)
    sigmoid_gate = jax.nn.sigmoid(gate_proj)
    hidden_low = (gate_proj * sigmoid_gate * up_proj).astype(jnp.bfloat16)
    grad_gate_low = (
        grad_hidden * up_proj * sigmoid_gate * (1.0 + gate_proj * (1.0 - sigmoid_gate))
    ).astype(jnp.bfloat16)
    grad_up_low = (grad_hidden * gate_proj * sigmoid_gate).astype(jnp.bfloat16)
    return (hidden_low, grad_gate_low, grad_up_low)


def rms_back(values, gain_values, grad_out):
    scale = rms_scale(values)
    scaled = gain_values * grad_out
    inner_mean = jnp.mean(values * scaled, axis=-1, keepdims=True)
    grad_values = scale * scaled - values * scale * scale * scale * inner_mean
    grad_gain = jnp.sum(values * scale * grad_out, axis=0)
    return (grad_values, grad_gain)


def swap(block, axis, mask):
    return lax.ppermute(block, axis, [(i, i ^ mask) for i in range(lax.axis_size(axis))])


def tp_sum(block):
    return block + swap(block, "tp", 1)


def seq_bits():
    return lax.axis_size("seq").bit_length() - 1


def seq_sum(block):
    for bit in range(seq_bits()):
        block = block + swap(block, "seq", 1 << bit)
    return block


def to_partner(block, bit):
    return swap(block, "seq", 1 << bit)


def line_reduce(part):
    groups = part.shape[0]
    here = lax.axis_index("seq") // QUAD

    def block_at(place):
        return lax.dynamic_index_in_dim(part, jnp.clip(place, 0, groups - 1), 0, keepdims=False)

    def moved(block, step, count):
        senders = range(count) if step > 0 else range(groups - count, groups)
        route = [
            (g * QUAD + q, (g + step) * QUAD + q) for g in senders for q in range(QUAD)
        ]
        return lax.ppermute(block, "seq", route)

    up = moved(block_at(here + groups - 1), 1, 1)
    down = moved(block_at(here - groups + 1), -1, 1)
    for k in range(2, groups):
        up = moved(block_at(here + groups - k) + up, 1, k)
        down = moved(block_at(here - groups + k) + down, -1, k)
    return block_at(here) + up + down


def quad_trade(blocks):
    groups = lax.axis_size("seq") // QUAD
    members = [[g * QUAD + q for q in range(QUAD)] for g in range(groups)]
    return lax.all_to_all(blocks, "seq", 0, 0, axis_index_groups=members, tiled=True)


def grad_blocks_kernel(count, member_ref, *refs):
    lefts, rights = refs[:count], refs[count : 2 * count]
    far_ref, near_ref = refs[2 * count :]
    step = pl.program_id(0)
    groups, unused, rows, unused_depth = lefts[0].shape
    at = 0
    for left_ref, right_ref in zip(lefts, rights):
        left = left_ref[...].reshape(groups * rows, left_ref.shape[3])
        cols = right_ref.shape[1]
        got = dot_plain(left, right_ref[...]).reshape(1, groups, rows, cols)

        @pl.when(step < 2)
        def _():
            far_ref[:, :, :, at : at + cols] = got

        @pl.when(step >= 2)
        def _():
            near_ref[:, :, :, at : at + cols] = got

        at += cols


def grad_blocks(pairs, first):
    parts = lax.axis_size("seq")
    groups = parts // QUAD
    rows = pairs[0][0].shape[1] // parts
    lefts = [left.T.reshape(groups, QUAD, rows, left.shape[0]) for left, unused in pairs]
    rights = [right for unused, right in pairs]
    total = sum(right.shape[1] for right in rights)
    member = (lax.axis_index("seq") % QUAD).astype(jnp.int32).reshape(1)
    here, there = 1 << first, 2 >> first

    def place(i, ref):
        relative = jnp.where(i < 2, here, 0) + (i % 2) * there
        return (0, ref[0] ^ relative, 0, 0)

    shape = jax.ShapeDtypeStruct((2, groups, rows, total), jnp.float32)
    block = (1, groups, rows, total)
    return pl.pallas_call(
        partial(grad_blocks_kernel, len(pairs)),
        grid_spec=pltpu.PrefetchScalarGridSpec(
            num_scalar_prefetch=1,
            grid=(QUAD,),
            in_specs=[pl.BlockSpec((groups, 1, rows, left.shape[3]), place) for left in lefts]
            + [pl.BlockSpec(right.shape, lambda i, ref: (0, 0)) for right in rights],
            out_specs=[
                pl.BlockSpec(block, lambda i, ref: (jnp.minimum(i, 1), 0, 0, 0)),
                pl.BlockSpec(block, lambda i, ref: (jnp.maximum(i - 2, 0), 0, 0, 0)),
            ],
        ),
        out_shape=[shape, shape],
        compiler_params=pltpu.CompilerParams(vmem_limit_bytes=48 * 1024 * 1024),
    )(member, *lefts, *rights)


def reduce_rows(pairs, first):
    far, near = grad_blocks(pairs, first)
    got = to_partner(far, first)
    crossed = to_partner(near[1] + got[1], 1 - first)
    return line_reduce(near[0] + got[0] + crossed)


def segment_ids(lengths, place_count):
    ends = jnp.cumsum(lengths // 8, dtype=jnp.int32)
    places = jnp.arange(place_count, dtype=jnp.int32)
    short_ids = jnp.sum(
        (places[:, None] >= ends[None, :]).astype(jnp.int32), axis=1, dtype=jnp.int32
    )
    return jnp.stack([jnp.zeros_like(short_ids), short_ids])


def scan_heads(seg_now, head_size, xbc, dt_raw, conv_weight, conv_bias, dt_shift, a_logs, skips):
    place_count = xbc.shape[0]
    conv_sum = conv_bias + conv_weight[3] * xbc
    for offset in range(3):
        distance = 3 - offset
        earlier = jnp.pad(xbc, ((distance, 0), (0, 0)))[:place_count]
        seg_earlier = jnp.pad(seg_now, (distance, 0), constant_values=-1)[:place_count]
        same_doc = (seg_earlier == seg_now).astype(jnp.float32)
        conv_sum = conv_sum + conv_weight[offset] * earlier * same_doc[:, None]
    active = jax.nn.silu(conv_sum)
    head_count = dt_raw.shape[1]
    inner = head_count * head_size
    values = active[:, :inner].reshape(place_count, head_count, head_size)
    in_keys = active[:, inner : inner + NS]
    out_keys = active[:, inner + NS :]
    step_sizes = jax.nn.softplus(dt_raw + dt_shift)
    decay_rates = -step_sizes * jnp.exp(a_logs)
    chunk = min(place_count, 512)
    triangle = jnp.tril(jnp.ones((chunk, chunk), jnp.float32))
    state = jnp.zeros((head_count, head_size, NS), jnp.float32)
    seg_last = jnp.int32(-1)
    outputs = []
    for start in range(0, place_count, chunk):
        stop = start + chunk
        x, b, c = values[start:stop], in_keys[start:stop], out_keys[start:stop]
        dt, seg = step_sizes[start:stop], seg_now[start:stop]
        cumulative = jnp.dot(triangle, decay_rates[start:stop], precision=highest)
        allowed = (triangle > 0.0) & (seg[:, None] == seg[None, :])
        ordered = cumulative.T
        gaps = ordered[:, :, None] - ordered[:, None, :]
        decays = jnp.where(allowed, jnp.exp(jnp.where(allowed, gaps, 0.0)), 0.0)
        crossing = jnp.einsum("pn,jn->pj", c, b, precision=highest)
        mixing = crossing[None] * decays * dt.T[:, None, :]
        result = jnp.einsum("hpj,jhd->phd", mixing, x, precision=highest)
        if start > 0:
            entering = jnp.exp(cumulative) * (seg == seg_last).astype(jnp.float32)[:, None]
            result = result + entering[..., None] * jnp.einsum(
                "pn,hdn->phd", c, state, precision=highest
            )
        if stop < place_count:
            last_same = (seg == seg[-1]).astype(jnp.float32)[:, None]
            weight = jnp.exp(cumulative[-1:] - cumulative) * last_same * dt
            through = jnp.exp(cumulative[-1]) * (seg[-1] == seg_last).astype(jnp.float32)
            state = through[:, None, None] * state + jnp.einsum(
                "jh,jhd,jn->hdn", weight, x, b, precision=highest
            )
            seg_last = seg[-1]
        outputs.append(result + skips[:, None] * x)
    return jnp.concatenate(outputs, axis=0).reshape(place_count, inner)


def gated_norm(result, gate_in, mix_scale):
    gated = result * jax.nn.silu(gate_in)
    return gated * rms_scale(gated) * mix_scale


def patch_grad_kernel(grad_ref, *refs):
    byte_refs, out_ref, order_ref = refs[:8], refs[8], refs[9]
    width = byte_refs[0].shape[1]
    total = 8 * width

    @pl.when(pl.program_id(0) == 0)
    def _():
        row = lax.broadcasted_iota(jnp.int32, (total, total), 0)
        col = lax.broadcasted_iota(jnp.int32, (total, total), 1)
        order_ref[...] = jnp.where(row == (col % 8) * width + col // 8, 1.0, 0.0).astype(
            jnp.bfloat16
        )

    grad_low = grad_ref[...].astype(jnp.bfloat16)
    wide = jnp.concatenate([ref[...].astype(jnp.bfloat16) for ref in byte_refs], axis=1)
    grad = dot_left(grad_low, wide)
    high = grad.astype(jnp.bfloat16)
    rest = grad - high.astype(jnp.float32)
    mid = rest.astype(jnp.bfloat16)
    low = (rest - mid.astype(jnp.float32)).astype(jnp.bfloat16)
    order = order_ref[...]
    out_ref[...] = dot_plain(high, order) + (dot_plain(mid, order) + dot_plain(low, order))


def patch_grad(grad_rows, bytes_all):
    places, row_block = grad_rows.shape
    feature = bytes_all.shape[1] // 8
    chunk = 128
    steps = feature // chunk

    def byte_spec(j):
        return pl.BlockSpec((places, chunk), lambda i: (0, j * steps + i))

    return pl.pallas_call(
        patch_grad_kernel,
        grid=(steps,),
        in_specs=[pl.BlockSpec((places, row_block), lambda i: (0, 0))]
        + [byte_spec(j) for j in range(8)],
        out_specs=pl.BlockSpec((row_block, 8 * chunk), lambda i: (0, i)),
        out_shape=jax.ShapeDtypeStruct((row_block, 8 * feature), jnp.float32),
        scratch_shapes=[pltpu.VMEM((8 * chunk, 8 * chunk), jnp.bfloat16)],
        compiler_params=pltpu.CompilerParams(vmem_limit_bytes=52 * 1024 * 1024),
    )(grad_rows, *([bytes_all] * 8))


def shared_grad_kernel(left_ref, right_ref, out_ref):
    out_ref[...] = dot_left(left_ref[...], right_ref[...].astype(jnp.bfloat16))


def shared_grad(left_side, right_side):
    return pl.pallas_call(
        shared_grad_kernel,
        out_shape=jax.ShapeDtypeStruct(
            (left_side.shape[1], right_side.shape[1]), jnp.float32
        ),
        compiler_params=pltpu.CompilerParams(vmem_limit_bytes=32 * 1024 * 1024),
    )(left_side, right_side)


def trade(blocks):
    return lax.all_to_all(blocks, "seq", 0, 0, tiled=True)


def attention_parts(row_values, gain_values, w_qkv):
    row_count = row_values.shape[0]
    attn_in = (row_values * rms_scale(row_values) * gain_values).astype(jnp.bfloat16)
    qkv = dot_plain(attn_in, w_qkv).astype(jnp.bfloat16)
    head_part = qkv.shape[1] // 3
    shaped = qkv.reshape(row_count // 8, 8, 3, head_part // AD, AD)
    queries, key_heads, value_heads = (shaped[:, :, 0], shaped[:, :, 1], shaped[:, :, 2])
    scores = (
        jnp.einsum("pihd,pjhd->phij", queries, key_heads, preferred_element_type=jnp.float32)
        * 0.125
    )
    causal = jnp.arange(8, dtype=jnp.int32)[:, None] >= jnp.arange(8, dtype=jnp.int32)[None, :]
    attention_probs = jax.nn.softmax(jnp.where(causal, scores, masked_score), axis=-1)
    probs_low = attention_probs.astype(jnp.bfloat16)
    mixed_heads = jnp.einsum(
        "phij,pjhd->pihd", probs_low, value_heads, preferred_element_type=jnp.float32
    )
    mixed_low = mixed_heads.reshape(row_count, head_part).astype(jnp.bfloat16)
    return (attn_in, queries, key_heads, value_heads, attention_probs, probs_low, mixed_low)


def body(
    byte_states,
    lengths,
    w_patch,
    norm_global,
    w_in,
    conv_w,
    conv_b,
    dt_bias,
    a_log,
    d_skip,
    mix_gain,
    w_out,
    norm_attn,
    w_qkv,
    w_o,
    norm_mlp,
    w_gate,
    w_up,
    w_down,
    w_head,
    d_logits,
):
    streams, local_rows, model_width = byte_states.shape
    patch_count = local_rows // 8
    patch_total = streams * patch_count
    row_total = streams * local_rows
    feature = w_patch.shape[1] // 8
    inner_width = w_out.shape[1]
    channels = conv_w.shape[1]
    head_total = dt_bias.shape[0]
    head_cols = w_head.shape[1]
    parts = lax.axis_size("seq")
    tp_index = lax.axis_index("tp")
    seq_index = lax.axis_index("seq")
    places = parts * patch_count
    f32 = jnp.float32

    lanes = parts // streams
    width = inner_width // lanes
    full_head = inner_width // head_total
    own_heads = max(1, width // full_head)
    shared = max(1, full_head // width)
    head_size = width // own_heads
    own_stream = seq_index // lanes
    first_col = (seq_index % lanes) * width
    first_head = first_col // full_head

    seg_full = segment_ids(lengths, places)
    seg_own = lax.dynamic_slice_in_dim(seg_full, seq_index * patch_count, patch_count, 1)
    seg_stream = lax.dynamic_index_in_dim(seg_full, own_stream, 0, keepdims=False)
    valid = (seg_own < lengths.shape[0]).astype(f32).reshape(patch_total, 1)
    byte_valid = jnp.repeat(valid, 8, axis=0)

    member = seq_index % QUAD
    raw_logits = d_logits.reshape(row_total, head_cols)
    raw_wide = raw_logits.astype(f32)
    grad_logits = raw_logits * byte_valid.astype(jnp.bfloat16)
    grad_final = tp_sum(dot_trans(grad_logits, w_head))
    near_logits = []
    for other in range(1, QUAD):
        near_seg = lax.dynamic_slice_in_dim(
            seg_full, (seq_index ^ other) * patch_count, patch_count, 1
        )
        near_valid = (near_seg < lengths.shape[0]).astype(f32).reshape(patch_total, 1)
        near_raw = swap(raw_wide, "seq", other)
        near_logits.append(near_raw * jnp.repeat(near_valid, 8, axis=0))
    near_logits = jnp.concatenate(near_logits, axis=0).astype(jnp.bfloat16)
    near_final_low = tp_sum(dot_trans(near_logits, w_head)).astype(jnp.bfloat16)
    grad_mlp_low = grad_final.astype(jnp.bfloat16)
    grad_hidden = dot_plain(grad_mlp_low, w_down)
    hidden_part = w_gate.shape[1] // QUAD

    def own_units(columns):
        return lax.dynamic_slice_in_dim(columns, member * hidden_part, hidden_part, 1)

    near_grad_hidden = dot_plain(near_final_low, own_units(w_down))

    grid = byte_states.reshape(streams, patch_count, 8, model_width)
    own_part = lax.dynamic_slice_in_dim(grid, tp_index * feature, feature, 3)
    patch_vec = jnp.swapaxes(own_part, 2, 3).reshape(patch_total, feature * 8)
    patch_out = tp_sum(dot_trans(patch_vec, w_patch))
    gain_global = norm_global.astype(f32)
    unit_patch = patch_out * rms_scale(patch_out)
    u_low = (unit_patch * gain_global).astype(jnp.bfloat16)
    unit_all = lax.all_gather(unit_patch, "seq", axis=0).reshape(
        parts, streams, patch_count, model_width
    )
    proj = dot_plain(u_low, w_in).reshape(streams, patch_count, -1)
    gate_in = proj[..., :inner_width]
    xbc = proj[..., inner_width : inner_width + channels]
    dt_raw = proj[..., inner_width + channels :]

    def by_lane(columns):
        split = columns.reshape(streams, patch_count, lanes, -1)
        return jnp.moveaxis(split, 2, 1).reshape(parts, patch_count, -1)

    def from_lanes(blocks):
        split = blocks.reshape(streams, lanes, patch_count, -1)
        return jnp.moveaxis(split, 1, 2).reshape(streams, patch_count, -1)

    def to_all_lanes(columns):
        wide = jnp.broadcast_to(
            columns[:, None], (streams, lanes, patch_count, columns.shape[-1])
        )
        return wide.reshape(parts, patch_count, -1)

    pad_width = 128 - own_heads
    dt_lanes = by_lane(jnp.repeat(dt_raw, shared, axis=2))
    sent = jnp.concatenate(
        [
            by_lane(xbc[..., :inner_width]),
            to_all_lanes(xbc[..., inner_width:]),
            jnp.pad(dt_lanes, ((0, 0), (0, 0), (0, pad_width))),
        ],
        axis=-1,
    )
    taken = trade(sent).reshape(places, -1)
    scan_width = width + channels - inner_width

    def own_cols(param):
        mine = lax.dynamic_slice_in_dim(param, first_col, width, param.ndim - 1)
        return jnp.concatenate([mine, param[..., inner_width:]], axis=-1).astype(f32)

    def own_head(param):
        return lax.dynamic_slice_in_dim(param, first_head, own_heads, 0).astype(f32)

    scan_args = (
        taken[:, :scan_width],
        taken[:, scan_width : scan_width + own_heads],
        own_cols(conv_w),
        own_cols(conv_b),
        own_head(dt_bias),
        own_head(a_log),
        own_head(d_skip),
    )
    scanned, scan_back = jax.vjp(partial(scan_heads, seg_stream, head_size), *scan_args)
    result = from_lanes(trade(scanned.reshape(parts, patch_count, width)))
    normed, norm_back = jax.vjp(gated_norm, result, gate_in, mix_gain.astype(f32))
    normed_low = normed.reshape(patch_total, inner_width).astype(jnp.bfloat16)

    bytes_wide = own_part.reshape(patch_total, 8 * feature).astype(f32)
    bytes_all = lax.all_gather(bytes_wide, "seq", axis=0, tiled=True)

    global_out = patch_out + valid * tp_sum(dot_trans(normed_low, w_out))
    stream_in = (
        byte_states.reshape(patch_total, 8, model_width).astype(f32) + global_out[:, None, :]
    ).reshape(row_total, model_width)
    gain_attn = norm_attn.astype(f32)
    gain_mlp = norm_mlp.astype(f32)
    attn_saved = attention_parts(stream_in, gain_attn, w_qkv)
    after_attn = stream_in + tp_sum(dot_trans(attn_saved[6], w_o))
    unit_mlp = after_attn * rms_scale(after_attn)
    mlp_in = (unit_mlp * gain_mlp).astype(jnp.bfloat16)
    hidden_low, grad_gate_low, grad_up_low = hidden_parts(mlp_in, grad_hidden, w_gate, w_up)
    grad_mlp_in = tp_sum(dot_trans(grad_gate_low, w_gate) + dot_trans(grad_up_low, w_up))

    half_width = model_width // 2
    unit_half = lax.dynamic_slice_in_dim(unit_mlp, tp_index * half_width, half_width, 1)
    near_ins = []
    for other in range(1, QUAD):
        own_half = swap(unit_half, "seq", other)
        other_half = swap(own_half, "tp", 1)
        first_half = jnp.where(tp_index == 0, own_half, other_half)
        second_half = jnp.where(tp_index == 0, other_half, own_half)
        near_ins.append(jnp.concatenate([first_half, second_half], axis=1) * gain_mlp)
    near_in_low = jnp.concatenate(near_ins, axis=0).astype(jnp.bfloat16)
    near_hidden, near_gate, near_up = hidden_parts(
        near_in_low, near_grad_hidden, own_units(w_gate), own_units(w_up)
    )
    quad_in = jnp.concatenate([mlp_in, near_in_low], axis=0)
    quad_final = jnp.concatenate([grad_mlp_low, near_final_low], axis=0)
    quad_hidden = jnp.concatenate([own_units(hidden_low), near_hidden], axis=0)
    quad_gate = jnp.concatenate([own_units(grad_gate_low), near_gate], axis=0)
    quad_up = jnp.concatenate([own_units(grad_up_low), near_up], axis=0)
    groups = parts // QUAD

    def reduce_quad(left_side, right_side):
        product = dot_left(left_side, right_side).reshape(groups, -1, hidden_part)
        mine = line_reduce(product).reshape(QUAD, -1, hidden_part)
        return jnp.moveaxis(quad_trade(mine), 0, 1).reshape(-1, QUAD * hidden_part)

    final_down = reduce_quad(quad_final, quad_hidden)
    final_gate = reduce_quad(quad_in, quad_gate)
    final_up = reduce_quad(quad_in, quad_up)
    after_mlp = after_attn + tp_sum(dot_trans(hidden_low, w_down))
    final_low = after_mlp.astype(jnp.bfloat16)
    logits = dot_plain(final_low, w_head) * byte_valid
    back_mlp, grad_norm_mlp = rms_back(after_attn, gain_mlp, grad_mlp_in)
    grad_mid = grad_final + back_mlp
    attn_in, queries, key_heads, value_heads, attention_probs, probs_low, mixed_low = attn_saved
    grad_attn_low = grad_mid.astype(jnp.bfloat16)
    grad_mixed = dot_plain(grad_attn_low, w_o).astype(jnp.bfloat16).reshape(queries.shape)
    grad_probs = jnp.einsum(
        "pihd,pjhd->phij", grad_mixed, value_heads, preferred_element_type=f32
    )
    grad_scores = (
        attention_probs
        * (grad_probs - jnp.sum(attention_probs * grad_probs, axis=-1, keepdims=True))
    ).astype(jnp.bfloat16)
    grad_queries = (
        jnp.einsum("phij,pjhd->pihd", grad_scores, key_heads, preferred_element_type=f32) * 0.125
    )
    grad_keys = (
        jnp.einsum("phij,pihd->pjhd", grad_scores, queries, preferred_element_type=f32) * 0.125
    )
    grad_values = jnp.einsum("phij,pihd->pjhd", probs_low, grad_mixed, preferred_element_type=f32)
    grad_qkv_low = (
        jnp.stack([grad_queries, grad_keys, grad_values], axis=2)
        .reshape(row_total, -1)
        .astype(jnp.bfloat16)
    )
    grad_attn_in = tp_sum(dot_trans(grad_qkv_low, w_qkv))
    attn_cut = 1024 if grad_qkv_low.shape[1] > 1024 else 128
    final_attn = reduce_rows([(attn_in, grad_qkv_low[:, :attn_cut])], 0)
    final_attn = final_attn, reduce_rows(
        [
            (attn_in, grad_qkv_low[:, attn_cut:]),
            (grad_attn_low, mixed_low),
            (final_low, grad_logits),
        ],
        1,
    )
    final_attn = jnp.concatenate(final_attn, axis=1)
    back_attn, grad_norm_attn = rms_back(stream_in, gain_attn, grad_attn_in)
    grad_stream = grad_mid + back_attn
    grad_global = jnp.sum(grad_stream.reshape(patch_total, 8, model_width), axis=1)
    grad_mix_low = (grad_global * valid).astype(jnp.bfloat16)
    grad_normed = dot_plain(grad_mix_low, w_out).reshape(streams, patch_count, inner_width)
    grad_result, grad_gate_in, grad_mix_gain = norm_back(grad_normed)
    grad_z_low = grad_gate_in.reshape(patch_total, inner_width).astype(jnp.bfloat16)
    dealt = trade(jnp.concatenate([by_lane(grad_result), by_lane(grad_gate_in)], axis=-1))
    dealt = dealt.reshape(places, 2 * width)
    grad_scanned = dealt[:, :width]
    final_out = reduce_rows([(grad_mix_low, normed_low)], 0)
    scan_grads = scan_back(grad_scanned)
    unit_stream = lax.dynamic_index_in_dim(unit_all, own_stream, 1, keepdims=False)
    u_stream = (unit_stream * gain_global).astype(jnp.bfloat16).reshape(places, model_width)
    lane_grads = jnp.concatenate([dealt[:, width:], scan_grads[0][:, :width]], axis=1)
    final_lanes = trade(
        dot_left(u_stream, lane_grads.astype(jnp.bfloat16)).reshape(parts, -1, 2 * width)
    )
    final_lanes = jnp.sum(
        final_lanes.reshape(streams, lanes, -1, 2 * width), axis=0
    )
    final_z = jnp.moveaxis(final_lanes[..., :width], 0, 1).reshape(-1, inner_width)
    final_x = jnp.moveaxis(final_lanes[..., width:], 0, 1).reshape(-1, inner_width)
    back_sent = jnp.concatenate(
        [scan_grads[0], jnp.pad(scan_grads[1], ((0, 0), (0, pad_width)))], axis=-1
    )
    back_taken = trade(back_sent.reshape(parts, patch_count, -1))
    grad_x = from_lanes(back_taken[..., :width])
    by_stream = back_taken.reshape(streams, lanes, patch_count, -1)
    grad_bc = jnp.sum(by_stream[..., width:scan_width], axis=1)
    grad_dt = from_lanes(back_taken[..., scan_width : scan_width + own_heads])
    grad_dt = jnp.sum(grad_dt.reshape(streams, patch_count, head_total, shared), axis=-1)
    grad_shared = jnp.concatenate([grad_bc, grad_dt], axis=-1).reshape(patch_total, -1)
    grad_proj_low = jnp.concatenate(
        [grad_z_low, grad_x.reshape(patch_total, -1).astype(jnp.bfloat16)]
        + [grad_shared.astype(jnp.bfloat16)],
        axis=-1,
    )
    grad_u = tp_sum(dot_trans(grad_proj_low, w_in))
    row_block = model_width // parts
    first_row = seq_index * row_block
    unit_rows = lax.dynamic_slice_in_dim(unit_all, first_row, row_block, 3)
    gain_rows = lax.dynamic_slice_in_dim(gain_global, first_row, row_block, 0)
    u_rows = (unit_rows * gain_rows).astype(jnp.bfloat16).reshape(-1, row_block)
    shared_all = lax.all_gather(grad_shared, "seq", axis=0, tiled=True)
    final_shared = shared_grad(u_rows, shared_all)
    back_global, grad_norm_global = rms_back(patch_out, gain_global, grad_u)
    grad_patch = grad_global + back_global

    patch_sent = jnp.moveaxis(grad_patch.reshape(patch_total, parts, row_block), 1, 0)
    patch_taken = trade(patch_sent).reshape(-1, row_block)
    final_patch = patch_grad(patch_taken, bytes_all)
    grad_vec = dot_plain(grad_patch.astype(jnp.bfloat16), w_patch)
    grad_vec = grad_vec.reshape(streams, patch_count, feature, 8)
    grad_own = jnp.swapaxes(grad_vec, 2, 3).reshape(streams, local_rows, feature)
    grad_rows = lax.dynamic_slice_in_dim(
        grad_stream.reshape(streams, local_rows, model_width), tp_index * feature, feature, 2
    )
    grad_bytes = grad_rows + grad_own

    def place_cols(grad):
        blank = jnp.zeros(grad.shape[:-1] + (inner_width,), f32)
        mine = lax.dynamic_update_slice_in_dim(
            blank, grad[..., :width], first_col, grad.ndim - 1
        )
        return jnp.concatenate([mine, grad[..., width:]], axis=-1)

    def place_head(grad):
        return lax.dynamic_update_slice_in_dim(
            jnp.zeros((head_total,), f32), grad, first_head, 0
        )

    small = (
        place_cols(scan_grads[2]),
        place_cols(scan_grads[3]),
        place_head(scan_grads[4]),
        place_head(scan_grads[5]),
        place_head(scan_grads[6]),
        grad_mix_gain,
        grad_norm_global,
        grad_norm_attn,
        grad_norm_mlp,
    )
    flat = jnp.concatenate([part.reshape(-1) for part in small])
    count = flat.shape[0]
    fill = -count % 1024
    flat = seq_sum(jnp.pad(flat, (0, fill)).reshape(-1, 128)).reshape(-1)
    small_sums = []
    at = 0
    for part in small:
        small_sums.append(flat[at : at + part.size].reshape(part.shape))
        at += part.size

    qkv_cols, o_cols = w_qkv.shape[1], w_o.shape[1]
    return (
        logits.reshape(streams, local_rows, head_cols),
        grad_bytes,
        final_patch,
        small_sums[6],
        jnp.concatenate([final_z, final_x, final_shared], axis=1),
        small_sums[0],
        small_sums[1],
        small_sums[2],
        small_sums[3],
        small_sums[4],
        small_sums[5],
        final_out,
        small_sums[7],
        final_attn[:, :qkv_cols],
        final_attn[:, qkv_cols : qkv_cols + o_cols],
        small_sums[8],
        final_gate,
        final_up,
        final_down,
        final_attn[:, qkv_cols + o_cols :],
    )


def solution(mesh):
    in_specs = (
        P(None, "seq", None),
        P(),
        P(None, "tp"),
        P(),
        P(None, "tp"),
        P(None, "tp"),
        P("tp"),
        P("tp"),
        P("tp"),
        P("tp"),
        P("tp"),
        P(None, "tp"),
        P(),
        P(None, "tp"),
        P(None, "tp"),
        P(),
        P(None, "tp"),
        P(None, "tp"),
        P(None, "tp"),
        P(None, "tp"),
        P(None, "seq", "tp"),
    )
    out_specs = (
        P(None, "seq", "tp"),
        P(None, "seq", "tp"),
        P("seq", "tp"),
        P(),
        P("seq", "tp"),
        P(None, "tp"),
        P("tp"),
        P("tp"),
        P("tp"),
        P("tp"),
        P("tp"),
        P("seq", "tp"),
        P(),
        P("seq", "tp"),
        P("seq", "tp"),
        P(),
        P("seq", "tp"),
        P("seq", "tp"),
        P("seq", "tp"),
        P("seq", "tp"),
    )
    return jax.shard_map(body, mesh=mesh, in_specs=in_specs, out_specs=out_specs, check_vma=False)
```

```python
from functools import partial

import jax
import jax.numpy as jnp
from jax import lax
from jax.experimental import pallas as pl
from jax.experimental.pallas import tpu as pltpu
from jax.sharding import PartitionSpec as P

NS = 128
AD = 64
QUAD = 4


epsilon = 1e-05
highest = lax.Precision.HIGHEST
masked_score = -1e30


def dot_plain(left_side, right_side):
    return jnp.dot(left_side, right_side, preferred_element_type=jnp.float32)


def dot_trans(left_side, right_side):
    return lax.dot_general(
        left_side, right_side, (((1,), (1,)), ((), ())), preferred_element_type=jnp.float32
    )


def dot_left(left_side, right_side):
    return lax.dot_general(
        left_side, right_side, (((0,), (0,)), ((), ())), preferred_element_type=jnp.float32
    )


def rms_scale(values):
    return lax.rsqrt(jnp.mean(values * values, axis=-1, keepdims=True) + epsilon)


def hidden_parts(mlp_in, grad_hidden, w_gate, w_up):
    gate_proj = dot_plain(mlp_in, w_gate)
    up_proj = dot_plain(mlp_in, w_up)
    sigmoid_gate = jax.nn.sigmoid(gate_proj)
    hidden_low = (gate_proj * sigmoid_gate * up_proj).astype(jnp.bfloat16)
    grad_gate_low = (
        grad_hidden * up_proj * sigmoid_gate * (1.0 + gate_proj * (1.0 - sigmoid_gate))
    ).astype(jnp.bfloat16)
    grad_up_low = (grad_hidden * gate_proj * sigmoid_gate).astype(jnp.bfloat16)
    return (hidden_low, grad_gate_low, grad_up_low)


def rms_back(values, gain_values, grad_out):
    scale = rms_scale(values)
    scaled = gain_values * grad_out
    inner_mean = jnp.mean(values * scaled, axis=-1, keepdims=True)
    grad_values = scale * scaled - values * scale * scale * scale * inner_mean
    grad_gain = jnp.sum(values * scale * grad_out, axis=0)
    return (grad_values, grad_gain)


def swap(block, axis, mask):
    return lax.ppermute(block, axis, [(i, i ^ mask) for i in range(lax.axis_size(axis))])


def after(value, *earlier):
    return lax.optimization_barrier((value,) + earlier)[0]


def tp_sum(block):
    return block + swap(block, "tp", 1)


def seq_bits():
    return lax.axis_size("seq").bit_length() - 1


def seq_sum(block):
    for bit in range(seq_bits()):
        block = block + swap(block, "seq", 1 << bit)
    return block


def to_partner(block, bit):
    return swap(block, "seq", 1 << bit)


def line_reduce(part, turns):
    groups = part.shape[0]
    here = lax.axis_index("seq") // QUAD

    def block_at(place):
        return lax.dynamic_index_in_dim(part, jnp.clip(place, 0, groups - 1), 0, keepdims=False)

    def moved(block, step, count):
        senders = range(count) if step > 0 else range(groups - count, groups)
        route = [
            (g * QUAD + q, (g + step) * QUAD + q) for g in senders for q in range(QUAD)
        ]
        return lax.ppermute(block, "seq", route)

    up = moved(block_at(here + groups - 1), 1, 1)
    down = moved(block_at(here - groups + 1), -1, 1)
    for k in range(2, groups):
        turn = turns[min(k - 2, len(turns) - 2)]
        up = moved(block_at(here + groups - k) + after(up, turn), 1, k)
        down = moved(block_at(here - groups + k) + after(down, turn), -1, k)
    return block_at(here) + after(up, turns[-1]) + after(down, turns[-1])


def quad_trade(blocks):
    groups = lax.axis_size("seq") // QUAD
    members = [[g * QUAD + q for q in range(QUAD)] for g in range(groups)]
    return lax.all_to_all(blocks, "seq", 0, 0, axis_index_groups=members, tiled=True)


def grad_blocks_kernel(count, member_ref, *refs):
    lefts, rights = refs[:count], refs[count : 2 * count]
    far_ref, near_ref = refs[2 * count :]
    step = pl.program_id(0)
    groups, unused, rows, unused_depth = lefts[0].shape
    at = 0
    for left_ref, right_ref in zip(lefts, rights):
        left = left_ref[...].reshape(groups * rows, left_ref.shape[3])
        cols = right_ref.shape[1]
        got = dot_plain(left, right_ref[...]).reshape(1, groups, rows, cols)

        @pl.when(step < 2)
        def _():
            far_ref[:, :, :, at : at + cols] = got

        @pl.when(step >= 2)
        def _():
            near_ref[:, :, :, at : at + cols] = got

        at += cols


def grad_blocks(pairs, first):
    parts = lax.axis_size("seq")
    groups = parts // QUAD
    rows = pairs[0][0].shape[1] // parts
    lefts = [left.T.reshape(groups, QUAD, rows, left.shape[0]) for left, unused in pairs]
    rights = [right for unused, right in pairs]
    total = sum(right.shape[1] for right in rights)
    member = (lax.axis_index("seq") % QUAD).astype(jnp.int32).reshape(1)
    here, there = 1 << first, 2 >> first

    def place(i, ref):
        relative = jnp.where(i < 2, here, 0) + (i % 2) * there
        return (0, ref[0] ^ relative, 0, 0)

    shape = jax.ShapeDtypeStruct((2, groups, rows, total), jnp.float32)
    block = (1, groups, rows, total)
    return pl.pallas_call(
        partial(grad_blocks_kernel, len(pairs)),
        grid_spec=pltpu.PrefetchScalarGridSpec(
            num_scalar_prefetch=1,
            grid=(QUAD,),
            in_specs=[pl.BlockSpec((groups, 1, rows, left.shape[3]), place) for left in lefts]
            + [pl.BlockSpec(right.shape, lambda i, ref: (0, 0)) for right in rights],
            out_specs=[
                pl.BlockSpec(block, lambda i, ref: (jnp.minimum(i, 1), 0, 0, 0)),
                pl.BlockSpec(block, lambda i, ref: (jnp.maximum(i - 2, 0), 0, 0, 0)),
            ],
        ),
        out_shape=[shape, shape],
        compiler_params=pltpu.CompilerParams(vmem_limit_bytes=48 * 1024 * 1024),
    )(member, *lefts, *rights)


def reduce_rows(blocks, first, cross_turn, near_turn, turns):
    far, near = blocks
    got = after(to_partner(far, first), cross_turn)
    crossed = to_partner(near[1] + got[1], 1 - first)
    return line_reduce(near[0] + got[0] + after(crossed, near_turn), turns)


def segment_ids(lengths, place_count):
    ends = jnp.cumsum(lengths // 8, dtype=jnp.int32)
    places = jnp.arange(place_count, dtype=jnp.int32)
    short_ids = jnp.sum(
        (places[:, None] >= ends[None, :]).astype(jnp.int32), axis=1, dtype=jnp.int32
    )
    return jnp.stack([jnp.zeros_like(short_ids), short_ids])


def scan_heads(seg_now, head_size, xbc, dt_raw, conv_weight, conv_bias, dt_shift, a_logs, skips):
    place_count = xbc.shape[0]
    conv_sum = conv_bias + conv_weight[3] * xbc
    for offset in range(3):
        distance = 3 - offset
        earlier = jnp.pad(xbc, ((distance, 0), (0, 0)))[:place_count]
        seg_earlier = jnp.pad(seg_now, (distance, 0), constant_values=-1)[:place_count]
        same_doc = (seg_earlier == seg_now).astype(jnp.float32)
        conv_sum = conv_sum + conv_weight[offset] * earlier * same_doc[:, None]
    active = jax.nn.silu(conv_sum)
    head_count = dt_raw.shape[1]
    inner = head_count * head_size
    values = active[:, :inner].reshape(place_count, head_count, head_size)
    in_keys = active[:, inner : inner + NS]
    out_keys = active[:, inner + NS :]
    step_sizes = jax.nn.softplus(dt_raw + dt_shift)
    decay_rates = -step_sizes * jnp.exp(a_logs)
    chunk = min(place_count, 512)
    triangle = jnp.tril(jnp.ones((chunk, chunk), jnp.float32))
    state = jnp.zeros((head_count, head_size, NS), jnp.float32)
    seg_last = jnp.int32(-1)
    outputs = []
    for start in range(0, place_count, chunk):
        stop = start + chunk
        x, b, c = values[start:stop], in_keys[start:stop], out_keys[start:stop]
        dt, seg = step_sizes[start:stop], seg_now[start:stop]
        cumulative = jnp.dot(triangle, decay_rates[start:stop], precision=highest)
        allowed = (triangle > 0.0) & (seg[:, None] == seg[None, :])
        ordered = cumulative.T
        gaps = ordered[:, :, None] - ordered[:, None, :]
        decays = jnp.where(allowed, jnp.exp(jnp.where(allowed, gaps, 0.0)), 0.0)
        crossing = jnp.einsum("pn,jn->pj", c, b, precision=highest)
        mixing = crossing[None] * decays * dt.T[:, None, :]
        result = jnp.einsum("hpj,jhd->phd", mixing, x, precision=highest)
        if start > 0:
            entering = jnp.exp(cumulative) * (seg == seg_last).astype(jnp.float32)[:, None]
            result = result + entering[..., None] * jnp.einsum(
                "pn,hdn->phd", c, state, precision=highest
            )
        if stop < place_count:
            last_same = (seg == seg[-1]).astype(jnp.float32)[:, None]
            weight = jnp.exp(cumulative[-1:] - cumulative) * last_same * dt
            through = jnp.exp(cumulative[-1]) * (seg[-1] == seg_last).astype(jnp.float32)
            state = through[:, None, None] * state + jnp.einsum(
                "jh,jhd,jn->hdn", weight, x, b, precision=highest
            )
            seg_last = seg[-1]
        outputs.append(result + skips[:, None] * x)
    return jnp.concatenate(outputs, axis=0).reshape(place_count, inner)


def gated_norm(result, gate_in, mix_scale):
    gated = result * jax.nn.silu(gate_in)
    return gated * rms_scale(gated) * mix_scale


def patch_grad_kernel(grad_ref, *refs):
    byte_refs, out_ref, order_ref = refs[:8], refs[8], refs[9]
    width = byte_refs[0].shape[1]
    total = 8 * width

    @pl.when(pl.program_id(0) == 0)
    def _():
        row = lax.broadcasted_iota(jnp.int32, (total, total), 0)
        col = lax.broadcasted_iota(jnp.int32, (total, total), 1)
        order_ref[...] = jnp.where(row == (col % 8) * width + col // 8, 1.0, 0.0).astype(
            jnp.bfloat16
        )

    grad_low = grad_ref[...].astype(jnp.bfloat16)
    wide = jnp.concatenate([ref[...].astype(jnp.bfloat16) for ref in byte_refs], axis=1)
    grad = dot_left(grad_low, wide)
    high = grad.astype(jnp.bfloat16)
    rest = grad - high.astype(jnp.float32)
    mid = rest.astype(jnp.bfloat16)
    low = (rest - mid.astype(jnp.float32)).astype(jnp.bfloat16)
    order = order_ref[...]
    out_ref[...] = dot_plain(high, order) + (dot_plain(mid, order) + dot_plain(low, order))


def patch_grad(grad_rows, bytes_all):
    places, row_block = grad_rows.shape
    feature = bytes_all.shape[1] // 8
    chunk = 128
    steps = feature // chunk

    def byte_spec(j):
        return pl.BlockSpec((places, chunk), lambda i: (0, j * steps + i))

    return pl.pallas_call(
        patch_grad_kernel,
        grid=(steps,),
        in_specs=[pl.BlockSpec((places, row_block), lambda i: (0, 0))]
        + [byte_spec(j) for j in range(8)],
        out_specs=pl.BlockSpec((row_block, 8 * chunk), lambda i: (0, i)),
        out_shape=jax.ShapeDtypeStruct((row_block, 8 * feature), jnp.float32),
        scratch_shapes=[pltpu.VMEM((8 * chunk, 8 * chunk), jnp.bfloat16)],
        compiler_params=pltpu.CompilerParams(vmem_limit_bytes=52 * 1024 * 1024),
    )(grad_rows, *([bytes_all] * 8))


def shared_grad_kernel(left_ref, right_ref, out_ref):
    out_ref[...] = dot_left(left_ref[...], right_ref[...].astype(jnp.bfloat16))


def shared_grad(left_side, right_side):
    return pl.pallas_call(
        shared_grad_kernel,
        out_shape=jax.ShapeDtypeStruct(
            (left_side.shape[1], right_side.shape[1]), jnp.float32
        ),
        compiler_params=pltpu.CompilerParams(vmem_limit_bytes=32 * 1024 * 1024),
    )(left_side, right_side)


def trade(blocks):
    return lax.all_to_all(blocks, "seq", 0, 0, tiled=True)


def attention_parts(row_values, gain_values, w_qkv):
    row_count = row_values.shape[0]
    attn_in = (row_values * rms_scale(row_values) * gain_values).astype(jnp.bfloat16)
    qkv = dot_plain(attn_in, w_qkv).astype(jnp.bfloat16)
    head_part = qkv.shape[1] // 3
    shaped = qkv.reshape(row_count // 8, 8, 3, head_part // AD, AD)
    queries, key_heads, value_heads = (shaped[:, :, 0], shaped[:, :, 1], shaped[:, :, 2])
    scores = (
        jnp.einsum("pihd,pjhd->phij", queries, key_heads, preferred_element_type=jnp.float32)
        * 0.125
    )
    causal = jnp.arange(8, dtype=jnp.int32)[:, None] >= jnp.arange(8, dtype=jnp.int32)[None, :]
    attention_probs = jax.nn.softmax(jnp.where(causal, scores, masked_score), axis=-1)
    probs_low = attention_probs.astype(jnp.bfloat16)
    mixed_heads = jnp.einsum(
        "phij,pjhd->pihd", probs_low, value_heads, preferred_element_type=jnp.float32
    )
    mixed_low = mixed_heads.reshape(row_count, head_part).astype(jnp.bfloat16)
    return (attn_in, queries, key_heads, value_heads, attention_probs, probs_low, mixed_low)


def body(
    byte_states,
    lengths,
    w_patch,
    norm_global,
    w_in,
    conv_w,
    conv_b,
    dt_bias,
    a_log,
    d_skip,
    mix_gain,
    w_out,
    norm_attn,
    w_qkv,
    w_o,
    norm_mlp,
    w_gate,
    w_up,
    w_down,
    w_head,
    d_logits,
):
    streams, local_rows, model_width = byte_states.shape
    patch_count = local_rows // 8
    patch_total = streams * patch_count
    row_total = streams * local_rows
    feature = w_patch.shape[1] // 8
    inner_width = w_out.shape[1]
    channels = conv_w.shape[1]
    head_total = dt_bias.shape[0]
    head_cols = w_head.shape[1]
    parts = lax.axis_size("seq")
    tp_index = lax.axis_index("tp")
    seq_index = lax.axis_index("seq")
    places = parts * patch_count
    f32 = jnp.float32

    lanes = parts // streams
    width = inner_width // lanes
    full_head = inner_width // head_total
    own_heads = max(1, width // full_head)
    shared = max(1, full_head // width)
    head_size = width // own_heads
    own_stream = seq_index // lanes
    first_col = (seq_index % lanes) * width
    first_head = first_col // full_head

    seg_full = segment_ids(lengths, places)
    seg_own = lax.dynamic_slice_in_dim(seg_full, seq_index * patch_count, patch_count, 1)
    seg_stream = lax.dynamic_index_in_dim(seg_full, own_stream, 0, keepdims=False)
    valid = (seg_own < lengths.shape[0]).astype(f32).reshape(patch_total, 1)
    byte_valid = jnp.repeat(valid, 8, axis=0)

    member = seq_index % QUAD
    raw_logits = d_logits.reshape(row_total, head_cols)
    raw_wide = raw_logits.astype(f32)
    near_raws = [swap(raw_wide, "seq", other) for other in range(1, QUAD)]
    grid = byte_states.reshape(streams, patch_count, 8, model_width)
    own_part = lax.dynamic_slice_in_dim(grid, tp_index * feature, feature, 3)
    patch_vec = jnp.swapaxes(own_part, 2, 3).reshape(patch_total, feature * 8)
    patch_out = tp_sum(dot_trans(patch_vec, w_patch))
    gain_global = norm_global.astype(f32)
    unit_patch = patch_out * rms_scale(patch_out)
    u_low = (unit_patch * gain_global).astype(jnp.bfloat16)
    unit_all = lax.all_gather(unit_patch, "seq", axis=0).reshape(
        parts, streams, patch_count, model_width
    )
    proj = dot_plain(u_low, w_in).reshape(streams, patch_count, -1)
    gate_in = proj[..., :inner_width]
    xbc = proj[..., inner_width : inner_width + channels]
    dt_raw = proj[..., inner_width + channels :]

    def by_lane(columns):
        split = columns.reshape(streams, patch_count, lanes, -1)
        return jnp.moveaxis(split, 2, 1).reshape(parts, patch_count, -1)

    def from_lanes(blocks):
        split = blocks.reshape(streams, lanes, patch_count, -1)
        return jnp.moveaxis(split, 1, 2).reshape(streams, patch_count, -1)

    def to_all_lanes(columns):
        wide = jnp.broadcast_to(
            columns[:, None], (streams, lanes, patch_count, columns.shape[-1])
        )
        return wide.reshape(parts, patch_count, -1)

    pad_width = 128 - own_heads
    dt_lanes = by_lane(jnp.repeat(dt_raw, shared, axis=2))
    sent = jnp.concatenate(
        [
            by_lane(xbc[..., :inner_width]),
            to_all_lanes(xbc[..., inner_width:]),
            jnp.pad(dt_lanes, ((0, 0), (0, 0), (0, pad_width))),
        ],
        axis=-1,
    )
    taken = trade(sent)
    grad_logits = after(raw_logits, sent) * byte_valid.astype(jnp.bfloat16)
    grad_final = tp_sum(dot_trans(grad_logits, w_head))
    near_logits = []
    for other in range(1, QUAD):
        near_seg = lax.dynamic_slice_in_dim(
            seg_full, (seq_index ^ other) * patch_count, patch_count, 1
        )
        near_valid = (near_seg < lengths.shape[0]).astype(f32).reshape(patch_total, 1)
        near_raw = after(near_raws[other - 1], sent)
        near_logits.append(near_raw * jnp.repeat(near_valid, 8, axis=0))
    near_logits = jnp.concatenate(near_logits, axis=0).astype(jnp.bfloat16)
    near_final_low = tp_sum(dot_trans(near_logits, w_head)).astype(jnp.bfloat16)
    grad_mlp_low = grad_final.astype(jnp.bfloat16)
    grad_hidden = dot_plain(grad_mlp_low, w_down)
    hidden_part = w_gate.shape[1] // QUAD

    def own_units(columns):
        return lax.dynamic_slice_in_dim(columns, member * hidden_part, hidden_part, 1)

    near_grad_hidden = dot_plain(near_final_low, own_units(w_down))

    bytes_wide = after(own_part, sent).reshape(patch_total, 8 * feature).astype(f32)
    bytes_all = lax.all_gather(bytes_wide, "seq", axis=0, tiled=True)
    taken = after(taken, grad_hidden, near_grad_hidden, bytes_wide).reshape(places, -1)
    scan_width = width + channels - inner_width

    def own_cols(param):
        mine = lax.dynamic_slice_in_dim(param, first_col, width, param.ndim - 1)
        return jnp.concatenate([mine, param[..., inner_width:]], axis=-1).astype(f32)

    def own_head(param):
        return lax.dynamic_slice_in_dim(param, first_head, own_heads, 0).astype(f32)

    scan_args = (
        taken[:, :scan_width],
        taken[:, scan_width : scan_width + own_heads],
        own_cols(conv_w),
        own_cols(conv_b),
        own_head(dt_bias),
        own_head(a_log),
        own_head(d_skip),
    )
    scanned, scan_back = jax.vjp(partial(scan_heads, seg_stream, head_size), *scan_args)
    result = from_lanes(trade(scanned.reshape(parts, patch_count, width)))
    normed, norm_back = jax.vjp(gated_norm, result, gate_in, mix_gain.astype(f32))
    normed_low = normed.reshape(patch_total, inner_width).astype(jnp.bfloat16)

    global_out = patch_out + valid * tp_sum(dot_trans(normed_low, w_out))
    stream_in = (
        byte_states.reshape(patch_total, 8, model_width).astype(f32) + global_out[:, None, :]
    ).reshape(row_total, model_width)
    gain_attn = norm_attn.astype(f32)
    gain_mlp = norm_mlp.astype(f32)
    attn_saved = attention_parts(stream_in, gain_attn, w_qkv)
    after_attn = stream_in + tp_sum(dot_trans(attn_saved[6], w_o))
    unit_mlp = after_attn * rms_scale(after_attn)
    mlp_in = (unit_mlp * gain_mlp).astype(jnp.bfloat16)
    half_width = model_width // 2
    unit_half = lax.dynamic_slice_in_dim(unit_mlp, tp_index * half_width, half_width, 1)
    mlp_in = after(mlp_in, unit_half)
    hidden_low, grad_gate_low, grad_up_low = hidden_parts(mlp_in, grad_hidden, w_gate, w_up)
    grad_mlp_part = dot_trans(grad_gate_low, w_gate) + dot_trans(grad_up_low, w_up)
    grad_mlp_in = tp_sum(grad_mlp_part)
    near_ins = []
    for other in range(1, QUAD):
        own_half = swap(unit_half, "seq", other)
        other_half = swap(own_half, "tp", 1)
        first_half = jnp.where(tp_index == 0, own_half, other_half)
        second_half = jnp.where(tp_index == 0, other_half, own_half)
        near_ins.append(jnp.concatenate([first_half, second_half], axis=1) * gain_mlp)
    after_mlp = after_attn + tp_sum(dot_trans(after(hidden_low, grad_mlp_part), w_down))
    final_low = after_mlp.astype(jnp.bfloat16)
    logits = dot_plain(final_low, w_head) * byte_valid
    back_mlp, grad_norm_mlp = rms_back(after_attn, gain_mlp, grad_mlp_in)
    grad_mid = grad_final + back_mlp
    attn_in, queries, key_heads, value_heads, attention_probs, probs_low, mixed_low = attn_saved
    grad_attn_low = grad_mid.astype(jnp.bfloat16)
    grad_mixed = dot_plain(grad_attn_low, w_o).astype(jnp.bfloat16).reshape(queries.shape)
    grad_probs = jnp.einsum(
        "pihd,pjhd->phij", grad_mixed, value_heads, preferred_element_type=f32
    )
    grad_scores = (
        attention_probs
        * (grad_probs - jnp.sum(attention_probs * grad_probs, axis=-1, keepdims=True))
    ).astype(jnp.bfloat16)
    grad_queries = (
        jnp.einsum("phij,pjhd->pihd", grad_scores, key_heads, preferred_element_type=f32) * 0.125
    )
    grad_keys = (
        jnp.einsum("phij,pihd->pjhd", grad_scores, queries, preferred_element_type=f32) * 0.125
    )
    grad_values = jnp.einsum("phij,pihd->pjhd", probs_low, grad_mixed, preferred_element_type=f32)
    grad_qkv_low = (
        jnp.stack([grad_queries, grad_keys, grad_values], axis=2)
        .reshape(row_total, -1)
        .astype(jnp.bfloat16)
    )
    grad_attn_part = dot_trans(grad_qkv_low, w_qkv)
    grad_attn_in = tp_sum(grad_attn_part)

    attn_cut = 1024 if grad_qkv_low.shape[1] > 1024 else 128
    attn_in_late = after(attn_in, grad_attn_part)
    attn_blocks = (
        grad_blocks([(attn_in_late, grad_qkv_low[:, :attn_cut])], 0),
        grad_blocks(
            [
                (attn_in_late, grad_qkv_low[:, attn_cut:]),
                (grad_attn_low, mixed_low),
                (final_low, grad_logits),
            ],
            1,
        ),
    )
    near_in_low = after(jnp.concatenate(near_ins, axis=0), attn_blocks[1][0])
    near_in_low = near_in_low.astype(jnp.bfloat16)
    near_hidden, near_gate, near_up = hidden_parts(
        near_in_low, near_grad_hidden, own_units(w_gate), own_units(w_up)
    )
    quad_in = jnp.concatenate([mlp_in, near_in_low], axis=0)
    quad_final = jnp.concatenate([grad_mlp_low, near_final_low], axis=0)
    quad_hidden = jnp.concatenate([own_units(hidden_low), near_hidden], axis=0)
    quad_gate = jnp.concatenate([own_units(grad_gate_low), near_gate], axis=0)
    quad_up = jnp.concatenate([own_units(grad_up_low), near_up], axis=0)
    groups = parts // QUAD

    def quad_product(left_side, right_side):
        return dot_left(left_side, right_side).reshape(groups, -1, hidden_part)

    down_product = quad_product(quad_final, quad_hidden)
    gate_product = quad_product(quad_in, quad_gate)
    up_product = quad_product(quad_in, quad_up)

    grad_attn_in = after(grad_attn_in, down_product, gate_product, up_product)
    back_attn, grad_norm_attn = rms_back(stream_in, gain_attn, grad_attn_in)
    grad_stream = grad_mid + back_attn
    grad_global = jnp.sum(grad_stream.reshape(patch_total, 8, model_width), axis=1)
    grad_mix_low = (grad_global * valid).astype(jnp.bfloat16)
    grad_normed = dot_plain(grad_mix_low, w_out).reshape(streams, patch_count, inner_width)
    grad_result, grad_gate_in, grad_mix_gain = norm_back(grad_normed)
    grad_z_low = grad_gate_in.reshape(patch_total, inner_width).astype(jnp.bfloat16)
    dealing = jnp.concatenate([by_lane(grad_result), by_lane(grad_gate_in)], axis=-1)
    dealt = trade(dealing)
    out_blocks = grad_blocks([(after(grad_mix_low, dealing), normed_low)], 0)
    dealt = after(dealt, out_blocks[1]).reshape(places, 2 * width)
    grad_scanned = dealt[:, :width]
    scan_grads = scan_back(grad_scanned)
    back_sent = jnp.concatenate(
        [scan_grads[0], jnp.pad(scan_grads[1], ((0, 0), (0, pad_width)))], axis=-1
    )
    back_sent = back_sent.reshape(parts, patch_count, -1)
    back_taken = trade(back_sent)
    grad_x = from_lanes(back_taken[..., :width])
    by_stream = back_taken.reshape(streams, lanes, patch_count, -1)
    grad_bc = jnp.sum(by_stream[..., width:scan_width], axis=1)
    grad_dt = from_lanes(back_taken[..., scan_width : scan_width + own_heads])
    grad_dt = jnp.sum(grad_dt.reshape(streams, patch_count, head_total, shared), axis=-1)
    grad_shared = jnp.concatenate([grad_bc, grad_dt], axis=-1).reshape(patch_total, -1)
    grad_proj_low = jnp.concatenate(
        [grad_z_low, grad_x.reshape(patch_total, -1).astype(jnp.bfloat16)]
        + [grad_shared.astype(jnp.bfloat16)],
        axis=-1,
    )
    grad_u_part = dot_trans(grad_proj_low, w_in)
    grad_u = tp_sum(grad_u_part)
    unit_stream = lax.dynamic_index_in_dim(unit_all, own_stream, 1, keepdims=False)
    u_stream = (after(unit_stream, back_sent) * gain_global).astype(jnp.bfloat16).reshape(places, model_width)
    lane_grads = jnp.concatenate([dealt[:, width:], scan_grads[0][:, :width]], axis=1)
    final_lanes = trade(
        dot_left(u_stream, lane_grads.astype(jnp.bfloat16)).reshape(parts, -1, 2 * width)
    )
    final_lanes = jnp.sum(
        final_lanes.reshape(streams, lanes, -1, 2 * width), axis=0
    )
    final_z = jnp.moveaxis(final_lanes[..., :width], 0, 1).reshape(-1, inner_width)
    final_x = jnp.moveaxis(final_lanes[..., width:], 0, 1).reshape(-1, inner_width)
    row_block = model_width // parts
    first_row = seq_index * row_block
    unit_rows = lax.dynamic_slice_in_dim(unit_all, first_row, row_block, 3)
    gain_rows = lax.dynamic_slice_in_dim(gain_global, first_row, row_block, 0)
    u_rows = (unit_rows * gain_rows).astype(jnp.bfloat16).reshape(-1, row_block)
    shared_all = lax.all_gather(grad_shared, "seq", axis=0, tiled=True)
    final_shared = shared_grad(u_rows, shared_all)
    back_global, grad_norm_global = rms_back(patch_out, gain_global, grad_u)
    grad_patch = grad_global + back_global

    patch_sent = jnp.moveaxis(grad_patch.reshape(patch_total, parts, row_block), 1, 0)
    patch_taken = trade(patch_sent)

    turns = (back_sent, grad_u_part, patch_sent)

    def finish_quad(product):
        mine = line_reduce(product, turns).reshape(QUAD, -1, hidden_part)
        return jnp.moveaxis(quad_trade(mine), 0, 1).reshape(-1, QUAD * hidden_part)

    final_down = finish_quad(down_product)
    final_gate = finish_quad(gate_product)
    final_up = finish_quad(up_product)
    late_turns = (grad_u_part, patch_sent, patch_sent)
    final_attn = jnp.concatenate(
        [
            reduce_rows(attn_blocks[0], 0, dealing, back_sent, late_turns),
            reduce_rows(attn_blocks[1], 1, dealing, back_sent, late_turns),
        ],
        axis=1,
    )
    final_out = reduce_rows(out_blocks, 0, back_sent, grad_u_part, (patch_sent,) * 3)
    patch_taken = patch_taken.reshape(-1, row_block)
    final_patch = patch_grad(patch_taken, bytes_all)
    grad_vec = dot_plain(grad_patch.astype(jnp.bfloat16), w_patch)
    grad_vec = grad_vec.reshape(streams, patch_count, feature, 8)
    grad_own = jnp.swapaxes(grad_vec, 2, 3).reshape(streams, local_rows, feature)
    grad_rows = lax.dynamic_slice_in_dim(
        grad_stream.reshape(streams, local_rows, model_width), tp_index * feature, feature, 2
    )
    grad_bytes = grad_rows + grad_own

    def place_cols(grad):
        blank = jnp.zeros(grad.shape[:-1] + (inner_width,), f32)
        mine = lax.dynamic_update_slice_in_dim(
            blank, grad[..., :width], first_col, grad.ndim - 1
        )
        return jnp.concatenate([mine, grad[..., width:]], axis=-1)

    def place_head(grad):
        return lax.dynamic_update_slice_in_dim(
            jnp.zeros((head_total,), f32), grad, first_head, 0
        )

    small = (
        place_cols(scan_grads[2]),
        place_cols(scan_grads[3]),
        place_head(scan_grads[4]),
        place_head(scan_grads[5]),
        place_head(scan_grads[6]),
        grad_mix_gain,
        grad_norm_global,
        grad_norm_attn,
        grad_norm_mlp,
    )
    flat = jnp.concatenate([part.reshape(-1) for part in small])
    count = flat.shape[0]
    fill = -count % 1024
    flat = seq_sum(jnp.pad(flat, (0, fill)).reshape(-1, 128)).reshape(-1)
    small_sums = []
    at = 0
    for part in small:
        small_sums.append(flat[at : at + part.size].reshape(part.shape))
        at += part.size

    qkv_cols, o_cols = w_qkv.shape[1], w_o.shape[1]
    return (
        logits.reshape(streams, local_rows, head_cols),
        grad_bytes,
        final_patch,
        small_sums[6],
        jnp.concatenate([final_z, final_x, final_shared], axis=1),
        small_sums[0],
        small_sums[1],
        small_sums[2],
        small_sums[3],
        small_sums[4],
        small_sums[5],
        final_out,
        small_sums[7],
        final_attn[:, :qkv_cols],
        final_attn[:, qkv_cols : qkv_cols + o_cols],
        small_sums[8],
        final_gate,
        final_up,
        final_down,
        final_attn[:, qkv_cols + o_cols :],
    )


def solution(mesh):
    in_specs = (
        P(None, "seq", None),
        P(),
        P(None, "tp"),
        P(),
        P(None, "tp"),
        P(None, "tp"),
        P("tp"),
        P("tp"),
        P("tp"),
        P("tp"),
        P("tp"),
        P(None, "tp"),
        P(),
        P(None, "tp"),
        P(None, "tp"),
        P(),
        P(None, "tp"),
        P(None, "tp"),
        P(None, "tp"),
        P(None, "tp"),
        P(None, "seq", "tp"),
    )
    out_specs = (
        P(None, "seq", "tp"),
        P(None, "seq", "tp"),
        P("seq", "tp"),
        P(),
        P("seq", "tp"),
        P(None, "tp"),
        P("tp"),
        P("tp"),
        P("tp"),
        P("tp"),
        P("tp"),
        P("seq", "tp"),
        P(),
        P("seq", "tp"),
        P("seq", "tp"),
        P(),
        P("seq", "tp"),
        P("seq", "tp"),
        P("seq", "tp"),
        P("seq", "tp"),
    )
    return jax.shard_map(body, mesh=mesh, in_specs=in_specs, out_specs=out_specs, check_vma=False)
```

```python
from functools import partial

import jax
import jax.numpy as jnp
from jax import lax
from jax.experimental import pallas as pl
from jax.experimental.pallas import tpu as pltpu
from jax.sharding import PartitionSpec as P

NS = 128
AD = 64
QUAD = 4


epsilon = 1e-05
highest = lax.Precision.HIGHEST
masked_score = -1e30


def dot_plain(left_side, right_side):
    return jnp.dot(left_side, right_side, preferred_element_type=jnp.float32)


def dot_trans(left_side, right_side):
    return lax.dot_general(
        left_side, right_side, (((1,), (1,)), ((), ())), preferred_element_type=jnp.float32
    )


def dot_left(left_side, right_side):
    return lax.dot_general(
        left_side, right_side, (((0,), (0,)), ((), ())), preferred_element_type=jnp.float32
    )


def rms_scale(values):
    return lax.rsqrt(jnp.mean(values * values, axis=-1, keepdims=True) + epsilon)


def hidden_parts(mlp_in, grad_hidden, w_gate, w_up):
    gate_proj = dot_plain(mlp_in, w_gate)
    up_proj = dot_plain(mlp_in, w_up)
    sigmoid_gate = jax.nn.sigmoid(gate_proj)
    hidden_low = (gate_proj * sigmoid_gate * up_proj).astype(jnp.bfloat16)
    grad_gate_low = (
        grad_hidden * up_proj * sigmoid_gate * (1.0 + gate_proj * (1.0 - sigmoid_gate))
    ).astype(jnp.bfloat16)
    grad_up_low = (grad_hidden * gate_proj * sigmoid_gate).astype(jnp.bfloat16)
    return (hidden_low, grad_gate_low, grad_up_low)


def rms_back(values, gain_values, grad_out):
    scale = rms_scale(values)
    scaled = gain_values * grad_out
    inner_mean = jnp.mean(values * scaled, axis=-1, keepdims=True)
    grad_values = scale * scaled - values * scale * scale * scale * inner_mean
    grad_gain = jnp.sum(values * scale * grad_out, axis=0)
    return (grad_values, grad_gain)


def swap(block, axis, mask):
    return lax.ppermute(block, axis, [(i, i ^ mask) for i in range(lax.axis_size(axis))])


def after(value, *earlier):
    return lax.optimization_barrier((value,) + earlier)[0]


def tp_sum(block):
    return block + swap(block, "tp", 1)


def to_partner(block, bit):
    return swap(block, "seq", 1 << bit)


def halve(part, axis, bit):
    mine = lax.axis_index("seq") >> bit & 1
    far = lax.dynamic_index_in_dim(part, 1 - mine, axis, keepdims=False)
    return far, lax.dynamic_index_in_dim(part, mine, axis, keepdims=False)


def seq_bits():
    return lax.axis_size("seq").bit_length() - 1


def side_masks():
    return (1, 4, 5)


def side_trade(blocks):
    members = [
        [base | high << 2 | low for high in range(2) for low in range(2)]
        for base in range(lax.axis_size("seq"))
        if base & 5 == 0
    ]
    return lax.all_to_all(blocks, "seq", 0, 0, axis_index_groups=members, tiled=True)


def grad_blocks_kernel(count, member_ref, *refs):
    lefts, rights = refs[:count], refs[count : 2 * count]
    far_ref, near_ref = refs[2 * count :]
    step = pl.program_id(0)
    groups, unused, rows, unused_depth = lefts[0].shape
    at = 0
    for left_ref, right_ref in zip(lefts, rights):
        left = left_ref[...].reshape(groups * rows, left_ref.shape[3])
        cols = right_ref.shape[1]
        got = dot_plain(left, right_ref[...]).reshape(1, groups, rows, cols)

        @pl.when(step < 2)
        def _():
            far_ref[:, :, :, at : at + cols] = got

        @pl.when(step >= 2)
        def _():
            near_ref[:, :, :, at : at + cols] = got

        at += cols


def grad_blocks(pairs, first):
    parts = lax.axis_size("seq")
    groups = parts // QUAD
    rows = pairs[0][0].shape[1] // parts
    lefts = [left.T.reshape(groups, QUAD, rows, left.shape[0]) for left, unused in pairs]
    rights = [right for unused, right in pairs]
    total = sum(right.shape[1] for right in rights)
    member = (lax.axis_index("seq") % QUAD).astype(jnp.int32).reshape(1)
    here, there = 1 << first, 2 >> first

    def place(i, ref):
        relative = jnp.where(i < 2, here, 0) + (i % 2) * there
        return (0, ref[0] ^ relative, 0, 0)

    shape = jax.ShapeDtypeStruct((2, groups, rows, total), jnp.float32)
    block = (1, groups, rows, total)
    return pl.pallas_call(
        partial(grad_blocks_kernel, len(pairs)),
        grid_spec=pltpu.PrefetchScalarGridSpec(
            num_scalar_prefetch=1,
            grid=(QUAD,),
            in_specs=[pl.BlockSpec((groups, 1, rows, left.shape[3]), place) for left in lefts]
            + [pl.BlockSpec(right.shape, lambda i, ref: (0, 0)) for right in rights],
            out_specs=[
                pl.BlockSpec(block, lambda i, ref: (jnp.minimum(i, 1), 0, 0, 0)),
                pl.BlockSpec(block, lambda i, ref: (jnp.maximum(i - 2, 0), 0, 0, 0)),
            ],
        ),
        out_shape=[shape, shape],
        compiler_params=pltpu.CompilerParams(vmem_limit_bytes=48 * 1024 * 1024),
    )(member, *lefts, *rights)


def segment_ids(lengths, place_count):
    ends = jnp.cumsum(lengths // 8, dtype=jnp.int32)
    places = jnp.arange(place_count, dtype=jnp.int32)
    short_ids = jnp.sum(
        (places[:, None] >= ends[None, :]).astype(jnp.int32), axis=1, dtype=jnp.int32
    )
    return jnp.stack([jnp.zeros_like(short_ids), short_ids])


def scan_heads(seg_now, head_size, xbc, dt_raw, conv_weight, conv_bias, dt_shift, a_logs, skips):
    place_count = xbc.shape[0]
    conv_sum = conv_bias + conv_weight[3] * xbc
    for offset in range(3):
        distance = 3 - offset
        earlier = jnp.pad(xbc, ((distance, 0), (0, 0)))[:place_count]
        seg_earlier = jnp.pad(seg_now, (distance, 0), constant_values=-1)[:place_count]
        same_doc = (seg_earlier == seg_now).astype(jnp.float32)
        conv_sum = conv_sum + conv_weight[offset] * earlier * same_doc[:, None]
    active = jax.nn.silu(conv_sum)
    head_count = dt_raw.shape[1]
    inner = head_count * head_size
    values = active[:, :inner].reshape(place_count, head_count, head_size)
    in_keys = active[:, inner : inner + NS]
    out_keys = active[:, inner + NS :]
    step_sizes = jax.nn.softplus(dt_raw + dt_shift)
    decay_rates = -step_sizes * jnp.exp(a_logs)
    chunk = min(place_count, 512)
    triangle = jnp.tril(jnp.ones((chunk, chunk), jnp.float32))
    state = jnp.zeros((head_count, head_size, NS), jnp.float32)
    seg_last = jnp.int32(-1)
    outputs = []
    for start in range(0, place_count, chunk):
        stop = start + chunk
        x, b, c = values[start:stop], in_keys[start:stop], out_keys[start:stop]
        dt, seg = step_sizes[start:stop], seg_now[start:stop]
        cumulative = jnp.dot(triangle, decay_rates[start:stop], precision=highest)
        allowed = (triangle > 0.0) & (seg[:, None] == seg[None, :])
        ordered = cumulative.T
        gaps = ordered[:, :, None] - ordered[:, None, :]
        decays = jnp.where(allowed, jnp.exp(jnp.where(allowed, gaps, 0.0)), 0.0)
        crossing = jnp.einsum("pn,jn->pj", c, b, precision=highest)
        mixing = crossing[None] * decays * dt.T[:, None, :]
        result = jnp.einsum("hpj,jhd->phd", mixing, x, precision=highest)
        if start > 0:
            entering = jnp.exp(cumulative) * (seg == seg_last).astype(jnp.float32)[:, None]
            result = result + entering[..., None] * jnp.einsum(
                "pn,hdn->phd", c, state, precision=highest
            )
        if stop < place_count:
            last_same = (seg == seg[-1]).astype(jnp.float32)[:, None]
            weight = jnp.exp(cumulative[-1:] - cumulative) * last_same * dt
            through = jnp.exp(cumulative[-1]) * (seg[-1] == seg_last).astype(jnp.float32)
            state = through[:, None, None] * state + jnp.einsum(
                "jh,jhd,jn->hdn", weight, x, b, precision=highest
            )
            seg_last = seg[-1]
        outputs.append(result + skips[:, None] * x)
    return jnp.concatenate(outputs, axis=0).reshape(place_count, inner)


def gated_unit(result, gate_in):
    gated = result * jax.nn.silu(gate_in)
    return gated * rms_scale(gated)


def patch_grad_kernel(grad_ref, *refs):
    byte_refs, out_ref, order_ref = refs[:8], refs[8], refs[9]
    width = byte_refs[0].shape[1]
    total = 8 * width

    @pl.when(pl.program_id(0) == 0)
    def _():
        row = lax.broadcasted_iota(jnp.int32, (total, total), 0)
        col = lax.broadcasted_iota(jnp.int32, (total, total), 1)
        order_ref[...] = jnp.where(row == (col % 8) * width + col // 8, 1.0, 0.0).astype(
            jnp.bfloat16
        )

    grad_low = grad_ref[...].astype(jnp.bfloat16)
    wide = jnp.concatenate([ref[...].astype(jnp.bfloat16) for ref in byte_refs], axis=1)
    grad = dot_left(grad_low, wide)
    high = grad.astype(jnp.bfloat16)
    rest = grad - high.astype(jnp.float32)
    mid = rest.astype(jnp.bfloat16)
    low = (rest - mid.astype(jnp.float32)).astype(jnp.bfloat16)
    order = order_ref[...]
    out_ref[...] = dot_plain(high, order) + (dot_plain(mid, order) + dot_plain(low, order))


def patch_grad(grad_rows, bytes_all):
    places, row_block = grad_rows.shape
    feature = bytes_all.shape[1] // 8
    chunk = 128
    steps = feature // chunk

    def byte_spec(j):
        return pl.BlockSpec((places, chunk), lambda i: (0, j * steps + i))

    return pl.pallas_call(
        patch_grad_kernel,
        grid=(steps,),
        in_specs=[pl.BlockSpec((places, row_block), lambda i: (0, 0))]
        + [byte_spec(j) for j in range(8)],
        out_specs=pl.BlockSpec((row_block, 8 * chunk), lambda i: (0, i)),
        out_shape=jax.ShapeDtypeStruct((row_block, 8 * feature), jnp.float32),
        scratch_shapes=[pltpu.VMEM((8 * chunk, 8 * chunk), jnp.bfloat16)],
        compiler_params=pltpu.CompilerParams(vmem_limit_bytes=52 * 1024 * 1024),
    )(grad_rows, *([bytes_all] * 8))


def shared_grad_kernel(left_ref, right_ref, out_ref):
    out_ref[...] = dot_left(left_ref[...], right_ref[...].astype(jnp.bfloat16))


def shared_grad(left_side, right_side):
    return pl.pallas_call(
        shared_grad_kernel,
        out_shape=jax.ShapeDtypeStruct(
            (left_side.shape[1], right_side.shape[1]), jnp.float32
        ),
        compiler_params=pltpu.CompilerParams(vmem_limit_bytes=32 * 1024 * 1024),
    )(left_side, right_side)


def trade(blocks):
    return lax.all_to_all(blocks, "seq", 0, 0, tiled=True)


def grid_iota(shape, axis):
    return lax.broadcasted_iota(jnp.int32, shape, axis)


def dot_fine(left_side, right_side, left_axis, right_axis):
    return lax.dot_general(
        left_side,
        right_side,
        (((left_axis,), (right_axis,)), ((), ())),
        preferred_element_type=jnp.float32,
        precision=highest,
    )


def shifted_down(block, distance):
    rows = grid_iota(block.shape, 0)
    return jnp.where(rows >= distance, pltpu.roll(block, distance, 0), 0.0)


def shifted_up(block, distance):
    count = block.shape[0]
    rows = grid_iota(block.shape, 0)
    return jnp.where(rows < count - distance, pltpu.roll(block, count - distance, 0), 0.0)


def scan_terms(taken_ref, same_ref, conv_ref, head_ref):
    places = taken_ref.shape[0]
    channels = conv_ref.shape[1]
    xbc = taken_ref[:, :channels]
    conv_sum = conv_ref[4:5] + conv_ref[3:4] * xbc
    for k in range(3):
        earlier = shifted_down(xbc, 3 - k) * same_ref[:, k : k + 1]
        conv_sum = conv_sum + conv_ref[k : k + 1] * earlier
    gate = jax.nn.sigmoid(conv_sum)
    active = conv_sum * gate
    raw = taken_ref[:, channels:] + head_ref[0:1]
    steps = jnp.maximum(raw, 0.0) + jnp.log1p(jnp.exp(-jnp.abs(raw)))
    rates = -steps * jnp.exp(head_ref[1:2])
    square = (places, places)
    triangle = jnp.where(grid_iota(square, 0) >= grid_iota(square, 1), 1.0, 0.0)
    running = dot_fine(triangle, rates, 1, 0)
    return xbc, conv_sum, gate, active, raw, steps, rates, triangle, running


def scan_forward_kernel(taken_ref, same_ref, conv_ref, head_ref, seg_col, seg_row, out_ref):
    places, width = out_ref.shape
    terms = scan_terms(taken_ref, same_ref, conv_ref, head_ref)
    active, steps, running = terms[3], terms[5], terms[8]
    values = active[:, :width]
    keys, reads = active[:, width : width + NS], active[:, width + NS :]
    steps_row, running_row = steps.T, running.T
    heads = width // 64
    rows = 128
    for first in range(0, places, rows):
        last = first + rows
        shape = (rows, last)
        allowed = (seg_col[first:last] == seg_row[:, :last]) & (
            grid_iota(shape, 0) + first >= grid_iota(shape, 1)
        )
        crossing = dot_fine(reads[first:last], keys[:last], 1, 1)
        lane = grid_iota((rows, width), 1) // 64
        total = head_ref[2:3] * values[first:last]
        for h in range(heads):
            gaps = running[first:last, h : h + 1] - running_row[h : h + 1, :last]
            decays = jnp.exp(jnp.where(allowed, gaps, masked_score))
            mixing = crossing * decays * steps_row[h : h + 1, :last]
            part = dot_fine(mixing, values[:last], 1, 0)
            total = total + jnp.where(lane == h, part, 0.0)
        out_ref[first:last] = total


def scan_backward_kernel(
    taken_ref,
    same_ref,
    conv_ref,
    head_ref,
    seg_col,
    seg_row,
    grad_ref,
    out_ref,
    conv_grad_ref,
    head_grad_ref,
    values_grad,
    keys_grad,
    reads_grad,
    rows_grad,
    cols_grad,
):
    places, width = values_grad.shape
    terms = scan_terms(taken_ref, same_ref, conv_ref, head_ref)
    xbc, conv_sum, gate, active, raw, steps, rates, triangle, running = terms
    channels = xbc.shape[1]
    values = active[:, :width]
    keys, reads = active[:, width : width + NS], active[:, width + NS :]
    steps_row, running_row = steps.T, running.T
    heads = width // 64
    rows = 128
    grad = grad_ref[...]
    values_grad[...] = head_ref[2:3] * grad
    keys_grad[...] = jnp.zeros_like(keys_grad)
    rows_grad[...] = jnp.zeros_like(rows_grad)
    cols_grad[...] = jnp.zeros_like(cols_grad)
    for first in range(0, places, rows):
        last = first + rows
        shape = (rows, last)
        allowed = (seg_col[first:last] == seg_row[:, :last]) & (
            grid_iota(shape, 0) + first >= grid_iota(shape, 1)
        )
        crossing = dot_fine(reads[first:last], keys[:last], 1, 1)
        crossing_grad = jnp.zeros(shape, jnp.float32)
        grad_rows = grad[first:last]
        lane = grid_iota((rows, width), 1) // 64
        wide_lane = grid_iota((last, width), 1) // 64
        column = grid_iota((rows, 128), 1)
        down = jnp.zeros((rows, 128), jnp.float32)
        for h in range(heads):
            gaps = running[first:last, h : h + 1] - running_row[h : h + 1, :last]
            decays = jnp.exp(jnp.where(allowed, gaps, masked_score))
            step_row = steps_row[h : h + 1, :last]
            weighted = decays * step_row
            mixing = crossing * weighted
            own_grad = jnp.where(lane == h, grad_rows, 0.0)
            mixing_grad = dot_fine(own_grad, values[:last], 1, 1)
            back = dot_fine(mixing, own_grad, 0, 0)
            values_grad[:last] += jnp.where(wide_lane == h, back, 0.0)
            crossing_grad = crossing_grad + mixing_grad * weighted
            step_part = jnp.sum(mixing_grad * crossing * decays, axis=0, keepdims=True)
            gap_part = mixing_grad * mixing
            down = jnp.where(column == h, jnp.sum(gap_part, axis=1, keepdims=True), down)
            cols_grad[h : h + 1, :last] += step_part
            cols_grad[heads + h : heads + h + 1, :last] += step_part * step_row
        rows_grad[first:last] += down
        reads_grad[first:last] = dot_fine(crossing_grad, keys[:last], 1, 0)
        keys_grad[:last] += dot_fine(crossing_grad, reads[first:last], 0, 0)
    turned = cols_grad[...].T
    column = grid_iota(turned.shape, 1)
    step_grad = jnp.where(column < heads, turned, 0.0)
    ended = pltpu.roll(turned, turned.shape[1] - heads, 1)
    running_grad = jnp.where(column < heads, rows_grad[...] - ended, 0.0)
    rates_grad = dot_fine(triangle, running_grad, 0, 0)
    step_grad = step_grad - rates_grad * jnp.exp(head_ref[1:2])
    raw_grad = step_grad * jax.nn.sigmoid(raw)
    out_ref[:, channels:] = raw_grad
    lane = grid_iota((places, width), 1) // 64
    product = jnp.sum(grad * values, axis=0, keepdims=True)
    head_grad_ref[...] = jnp.zeros_like(head_grad_ref)
    head_grad_ref[0:1] = jnp.sum(raw_grad, axis=0, keepdims=True)
    head_grad_ref[1:2] = jnp.sum(rates_grad * rates, axis=0, keepdims=True)
    skip_lane = grid_iota((1, width), 1)
    skip_grad = jnp.zeros((1, width), jnp.float32)
    for h in range(heads):
        own = jnp.sum(jnp.where(skip_lane // 64 == h, product, 0.0), axis=1, keepdims=True)
        skip_grad = jnp.where(skip_lane == h, own, skip_grad)
    head_grad_ref[2:3] = skip_grad
    active_grad = jnp.concatenate([values_grad[...], keys_grad[...], reads_grad[...]], axis=1)
    conv_grad = active_grad * gate * (1.0 + conv_sum * (1.0 - gate))
    back = conv_ref[3:4] * conv_grad
    conv_grad_ref[...] = jnp.zeros_like(conv_grad_ref)
    conv_grad_ref[3:4] = jnp.sum(conv_grad * xbc, axis=0, keepdims=True)
    conv_grad_ref[4:5] = jnp.sum(conv_grad, axis=0, keepdims=True)
    for k in range(3):
        kept = conv_grad * same_ref[:, k : k + 1]
        back = back + conv_ref[k : k + 1] * shifted_up(kept, 3 - k)
        conv_grad_ref[k : k + 1] = jnp.sum(
            kept * shifted_down(xbc, 3 - k), axis=0, keepdims=True
        )
    out_ref[:, :channels] = back


NO_COST = pl.CostEstimate(flops=1024, bytes_accessed=1024, transcendentals=0)
ROOMY = pltpu.CompilerParams(vmem_limit_bytes=56 * 1024 * 1024)


def scan_forward(args, width):
    places = args[0].shape[0]
    return pl.pallas_call(
        scan_forward_kernel,
        out_shape=jax.ShapeDtypeStruct((places, width), jnp.float32),
        compiler_params=ROOMY,
        cost_estimate=NO_COST,
    )(*args)


def scan_backward(args, grad):
    places, width = grad.shape
    channels = args[2].shape[1]
    f32 = jnp.float32
    return pl.pallas_call(
        scan_backward_kernel,
        out_shape=[
            jax.ShapeDtypeStruct((places, channels + 128), f32),
            jax.ShapeDtypeStruct((8, channels), f32),
            jax.ShapeDtypeStruct((8, 128), f32),
        ],
        scratch_shapes=[
            pltpu.VMEM((places, width), f32),
            pltpu.VMEM((places, NS), f32),
            pltpu.VMEM((places, NS), f32),
            pltpu.VMEM((places, 128), f32),
            pltpu.VMEM((128, places), f32),
        ],
        compiler_params=ROOMY,
        cost_estimate=NO_COST,
    )(*args, grad)


def patch_mask(rows):
    row, col = grid_iota((rows, rows), 0), grid_iota((rows, rows), 1)
    return (row // 8 == col // 8) & (col <= row)


def head_probs(queries, keys, lane_mask, allowed):
    scores = dot_trans(jnp.where(lane_mask, queries, 0), keys) * 0.125
    scores = jnp.where(allowed, scores, masked_score)
    top = jnp.max(scores, axis=1, keepdims=True)
    powers = jnp.exp(scores - top)
    return powers / jnp.sum(powers, axis=1, keepdims=True)


def attn_forward_kernel(
    bytes_ref, patch_ref, gain_ref, qkv_w_ref, o_w_ref, x_ref, a_ref, qkv_ref, o_ref, out_ref
):
    rows = bytes_ref.shape[0]
    spread = jnp.where(
        grid_iota((rows, rows // 8), 0) // 8 == grid_iota((rows, rows // 8), 1), 1.0, 0.0
    )
    x = bytes_ref[...].astype(jnp.float32) + dot_fine(spread, patch_ref[...], 1, 0)
    x_ref[...] = x
    attn_in = (x * rms_scale(x) * gain_ref[...]).astype(jnp.bfloat16)
    a_ref[...] = attn_in
    qkv_ref[...] = dot_plain(attn_in, qkv_w_ref[...]).astype(jnp.bfloat16)
    head_cols = o_ref.shape[1]
    block = 128
    allowed = patch_mask(block)
    lane = grid_iota((block, 128), 1) // AD
    for first in range(0, rows, block):
        place = slice(first, first + block)
        for pair in range(head_cols // 128):
            cols = [
                slice(j * head_cols + pair * 128, j * head_cols + pair * 128 + 128)
                for j in range(3)
            ]
            queries, keys, values = [qkv_ref[place, c] for c in cols]
            total = jnp.zeros((block, 128), jnp.float32)
            for h in range(2):
                probs = head_probs(queries, keys, lane == h, allowed).astype(jnp.bfloat16)
                total = jnp.where(lane == h, dot_plain(probs, values), total)
            o_ref[place, pair * 128 : pair * 128 + 128] = total.astype(jnp.bfloat16)
    out_ref[...] = dot_trans(o_ref[...], o_w_ref[...])


def attn_forward(bytes_rows, patch_rows, gain, w_qkv, w_o):
    rows, width = bytes_rows.shape
    block = 256
    cols, head_cols = w_qkv.shape[1], w_o.shape[1]
    f32, bf16 = jnp.float32, jnp.bfloat16

    def by_rows(cols):
        return pl.BlockSpec((block, cols), lambda i: (i, 0))

    def whole(shape):
        return pl.BlockSpec(shape, lambda i: (0, 0))

    return pl.pallas_call(
        attn_forward_kernel,
        grid=(rows // block,),
        in_specs=[
            by_rows(width),
            pl.BlockSpec((block // 8, width), lambda i: (i, 0)),
            whole((1, width)),
            whole(w_qkv.shape),
            whole(w_o.shape),
        ],
        out_specs=[by_rows(width), by_rows(width), by_rows(cols), by_rows(head_cols), by_rows(width)],
        out_shape=[
            jax.ShapeDtypeStruct((rows, width), f32),
            jax.ShapeDtypeStruct((rows, width), bf16),
            jax.ShapeDtypeStruct((rows, cols), bf16),
            jax.ShapeDtypeStruct((rows, head_cols), bf16),
            jax.ShapeDtypeStruct((rows, width), f32),
        ],
        compiler_params=ROOMY,
        cost_estimate=NO_COST,
    )(bytes_rows, patch_rows, gain.reshape(1, width), w_qkv, w_o)


def attn_backward_kernel(
    x_ref,
    final_ref,
    own_ref,
    other_ref,
    gain_ref,
    qkv_ref,
    qkv_w_ref,
    o_w_ref,
    mid_ref,
    low_ref,
    qkv_grad_ref,
    out_ref,
    gain_grad_ref,
):
    rows = x_ref.shape[0]
    back, gain_grad = rms_back(x_ref[...], gain_ref[...], own_ref[...] + other_ref[...])
    mid = final_ref[...] + back
    mid_ref[...] = mid
    low_ref[...] = mid.astype(jnp.bfloat16)
    gain_grad = gain_grad.reshape(1, -1)

    @pl.when(pl.program_id(0) == 0)
    def _():
        gain_grad_ref[...] = gain_grad

    @pl.when(pl.program_id(0) > 0)
    def _():
        gain_grad_ref[...] += gain_grad

    mixed_grad = dot_plain(low_ref[...], o_w_ref[...]).astype(jnp.bfloat16)
    head_cols = mixed_grad.shape[1]
    block = 128
    allowed = patch_mask(block)
    lane = grid_iota((block, 128), 1) // AD
    for first in range(0, rows, block):
        place = slice(first, first + block)
        for pair in range(head_cols // 128):
            cols = [
                slice(j * head_cols + pair * 128, j * head_cols + pair * 128 + 128)
                for j in range(3)
            ]
            queries, keys, values = [qkv_ref[place, c] for c in cols]
            out_grad = mixed_grad[place, pair * 128 : pair * 128 + 128]
            grads = [jnp.zeros((block, 128), jnp.float32)] * 3
            for h in range(2):
                own = lane == h
                probs = head_probs(queries, keys, own, allowed)
                probs_grad = dot_trans(jnp.where(own, out_grad, 0), values)
                inner = jnp.sum(probs * probs_grad, axis=1, keepdims=True)
                scores_grad = (probs * (probs_grad - inner)).astype(jnp.bfloat16)
                parts = (
                    dot_plain(scores_grad, keys) * 0.125,
                    dot_left(scores_grad, queries) * 0.125,
                    dot_left(probs.astype(jnp.bfloat16), out_grad),
                )
                grads = [jnp.where(own, part, grad) for part, grad in zip(parts, grads)]
            for c, grad in zip(cols, grads):
                qkv_grad_ref[place, c] = grad.astype(jnp.bfloat16)
    out_ref[...] = dot_trans(qkv_grad_ref[...], qkv_w_ref[...])


def attn_backward(x_rows, final_grad, own_part, other_part, gain, qkv, w_qkv, w_o):
    rows, width = x_rows.shape
    block = 256
    cols = w_qkv.shape[1]
    f32, bf16 = jnp.float32, jnp.bfloat16

    def by_rows(cols):
        return pl.BlockSpec((block, cols), lambda i: (i, 0))

    def whole(shape):
        return pl.BlockSpec(shape, lambda i: (0, 0))

    return pl.pallas_call(
        attn_backward_kernel,
        grid=(rows // block,),
        in_specs=[by_rows(width)] * 4
        + [whole((1, width)), by_rows(cols), whole(w_qkv.shape), whole(w_o.shape)],
        out_specs=[
            by_rows(width),
            by_rows(width),
            by_rows(cols),
            by_rows(width),
            whole((1, width)),
        ],
        out_shape=[
            jax.ShapeDtypeStruct((rows, width), f32),
            jax.ShapeDtypeStruct((rows, width), bf16),
            jax.ShapeDtypeStruct((rows, cols), bf16),
            jax.ShapeDtypeStruct((rows, width), f32),
            jax.ShapeDtypeStruct((1, width), f32),
        ],
        compiler_params=ROOMY,
        cost_estimate=NO_COST,
    )(x_rows, final_grad, own_part, other_part, gain.reshape(1, width), qkv, w_qkv, w_o)


def body(
    byte_states,
    lengths,
    w_patch,
    norm_global,
    w_in,
    conv_w,
    conv_b,
    dt_bias,
    a_log,
    d_skip,
    mix_gain,
    w_out,
    norm_attn,
    w_qkv,
    w_o,
    norm_mlp,
    w_gate,
    w_up,
    w_down,
    w_head,
    d_logits,
):
    streams, local_rows, model_width = byte_states.shape
    patch_count = local_rows // 8
    patch_total = streams * patch_count
    row_total = streams * local_rows
    feature = w_patch.shape[1] // 8
    inner_width = w_out.shape[1]
    channels = conv_w.shape[1]
    head_total = dt_bias.shape[0]
    head_cols = w_head.shape[1]
    parts = lax.axis_size("seq")
    tp_index = lax.axis_index("tp")
    seq_index = lax.axis_index("seq")
    places = parts * patch_count
    f32 = jnp.float32

    lanes = parts // streams
    width = inner_width // lanes
    full_head = inner_width // head_total
    own_heads = max(1, width // full_head)
    shared = max(1, full_head // width)
    head_size = width // own_heads
    own_stream = seq_index // lanes
    first_col = (seq_index % lanes) * width
    first_head = first_col // full_head

    seg_full = segment_ids(lengths, places)
    seg_own = lax.dynamic_slice_in_dim(seg_full, seq_index * patch_count, patch_count, 1)
    seg_stream = lax.dynamic_index_in_dim(seg_full, own_stream, 0, keepdims=False)
    valid = (seg_own < lengths.shape[0]).astype(f32).reshape(patch_total, 1)
    byte_valid = jnp.repeat(valid, 8, axis=0)

    member = (seq_index >> 2 & 1) * 2 + (seq_index & 1)
    raw_logits = d_logits.reshape(row_total, head_cols)
    raw_wide = raw_logits.astype(f32)
    near_raws = [swap(raw_wide, "seq", mask) for mask in side_masks()]
    grid = byte_states.reshape(streams, patch_count, 8, model_width)
    own_part = lax.dynamic_slice_in_dim(grid, tp_index * feature, feature, 3)
    patch_vec = jnp.swapaxes(own_part, 2, 3).reshape(patch_total, feature * 8)
    patch_out = tp_sum(dot_trans(patch_vec, w_patch))
    gain_global = norm_global.astype(f32)
    unit_patch = patch_out * rms_scale(patch_out)
    u_low = (unit_patch * gain_global).astype(jnp.bfloat16)
    unit_all = lax.all_gather(unit_patch, "seq", axis=0).reshape(
        parts, streams, patch_count, model_width
    )
    proj = dot_plain(u_low, w_in).reshape(streams, patch_count, -1)
    gate_in = proj[..., :inner_width]
    xbc = proj[..., inner_width : inner_width + channels]
    dt_raw = proj[..., inner_width + channels :]

    def by_lane(columns):
        split = columns.reshape(streams, patch_count, lanes, -1)
        return jnp.moveaxis(split, 2, 1).reshape(parts, patch_count, -1)

    def from_lanes(blocks):
        split = blocks.reshape(streams, lanes, patch_count, -1)
        return jnp.moveaxis(split, 1, 2).reshape(streams, patch_count, -1)

    def to_all_lanes(columns):
        wide = jnp.broadcast_to(
            columns[:, None], (streams, lanes, patch_count, columns.shape[-1])
        )
        return wide.reshape(parts, patch_count, -1)

    pad_width = 128 - own_heads
    dt_lanes = by_lane(jnp.repeat(dt_raw, shared, axis=2))
    sent = jnp.concatenate(
        [
            by_lane(xbc[..., :inner_width]),
            to_all_lanes(xbc[..., inner_width:]),
            jnp.pad(dt_lanes, ((0, 0), (0, 0), (0, pad_width))),
        ],
        axis=-1,
    )
    taken = trade(sent)
    grad_logits = after(raw_logits, sent) * byte_valid.astype(jnp.bfloat16)
    grad_final = tp_sum(dot_trans(grad_logits, w_head))
    near_logits = []
    for at, mask in enumerate(side_masks()):
        near_seg = lax.dynamic_slice_in_dim(
            seg_full, (seq_index ^ mask) * patch_count, patch_count, 1
        )
        near_valid = (near_seg < lengths.shape[0]).astype(f32).reshape(patch_total, 1)
        near_raw = after(near_raws[at], sent)
        near_logits.append(near_raw * jnp.repeat(near_valid, 8, axis=0))
    near_logits = jnp.concatenate(near_logits, axis=0).astype(jnp.bfloat16)
    near_final_low = tp_sum(dot_trans(near_logits, w_head)).astype(jnp.bfloat16)
    grad_mlp_low = grad_final.astype(jnp.bfloat16)
    grad_hidden = dot_plain(grad_mlp_low, w_down)
    hidden_part = w_gate.shape[1] // QUAD

    def own_units(columns):
        return lax.dynamic_slice_in_dim(columns, member * hidden_part, hidden_part, 1)

    near_grad_hidden = dot_plain(near_final_low, own_units(w_down))

    bytes_wide = after(own_part, sent).reshape(patch_total, 8 * feature).astype(f32)
    bytes_all = lax.all_gather(bytes_wide, "seq", axis=0, tiled=True)
    taken = after(taken, grad_hidden, near_grad_hidden, bytes_wide).reshape(places, -1)
    scan_width = width + channels - inner_width

    def own_cols(param):
        mine = lax.dynamic_slice_in_dim(param, first_col, width, param.ndim - 1)
        return jnp.concatenate([mine, param[..., inner_width:]], axis=-1).astype(f32)

    def own_head(param):
        return lax.dynamic_slice_in_dim(param, first_head, own_heads, 0).astype(f32)

    use_kernel = places == 512 and width == 128
    if use_kernel:
        padded_seg = jnp.pad(seg_stream, (3, 0), constant_values=-1)
        same = jnp.stack(
            [(padded_seg[k : k + places] == seg_stream).astype(f32) for k in range(3)]
            + [jnp.zeros((places,), f32)] * 5,
            axis=1,
        )
        conv_pack = jnp.concatenate(
            [own_cols(conv_w), own_cols(conv_b)[None], jnp.zeros((3, scan_width), f32)]
        )
        head_pack = jnp.stack(
            [jnp.pad(own_head(dt_bias), (0, 128 - own_heads))]
            + [jnp.pad(own_head(a_log), (0, 128 - own_heads))]
            + [jnp.repeat(own_head(d_skip), head_size)]
            + [jnp.zeros((128,), f32)] * 5
        )
        scan_args = (taken, same, conv_pack, head_pack, seg_stream[:, None], seg_stream[None])
        scanned = scan_forward(scan_args, width)
    else:
        scan_args = (
            taken[:, :scan_width],
            taken[:, scan_width : scan_width + own_heads],
            own_cols(conv_w),
            own_cols(conv_b),
            own_head(dt_bias),
            own_head(a_log),
            own_head(d_skip),
        )
        scanned, scan_back = jax.vjp(partial(scan_heads, seg_stream, head_size), *scan_args)
    result = from_lanes(trade(scanned.reshape(parts, patch_count, width)))
    unit_normed, norm_back = jax.vjp(gated_unit, result, gate_in)
    mix_scale = mix_gain.astype(f32)
    normed_low = (unit_normed * mix_scale).reshape(patch_total, -1).astype(jnp.bfloat16)
    normed_all = lax.all_gather(unit_normed, "seq", axis=0)
    global_out = patch_out + valid * tp_sum(dot_trans(normed_low, w_out))
    gain_attn = norm_attn.astype(f32)
    gain_mlp = norm_mlp.astype(f32)
    stream_in, attn_in, qkv, mixed_low, attn_part = attn_forward(
        byte_states.reshape(row_total, model_width), global_out, gain_attn, w_qkv, w_o
    )
    after_attn = stream_in + tp_sum(attn_part)
    unit_mlp = after_attn * rms_scale(after_attn)
    mlp_in = (unit_mlp * gain_mlp).astype(jnp.bfloat16)
    half_width = model_width // 2
    unit_half = lax.dynamic_slice_in_dim(unit_mlp, tp_index * half_width, half_width, 1)
    mlp_in = after(mlp_in, unit_half)
    hidden_low, grad_gate_low, grad_up_low = hidden_parts(mlp_in, grad_hidden, w_gate, w_up)
    grad_mlp_part = dot_trans(grad_gate_low, w_gate) + dot_trans(grad_up_low, w_up)
    grad_mlp_other = swap(grad_mlp_part, "tp", 1)
    near_ins = []
    for mask in side_masks():
        own_half = swap(unit_half, "seq", mask)
        other_half = swap(own_half, "tp", 1)
        first_half = jnp.where(tp_index == 0, own_half, other_half)
        second_half = jnp.where(tp_index == 0, other_half, own_half)
        near_ins.append(jnp.concatenate([first_half, second_half], axis=1) * gain_mlp)
    after_mlp = after_attn + tp_sum(dot_trans(after(hidden_low, grad_mlp_part), w_down))
    final_low = after_mlp.astype(jnp.bfloat16)
    logits = dot_plain(final_low, w_head) * byte_valid
    grad_mid, grad_attn_low, grad_qkv_low, grad_attn_part, grad_norm_mlp = attn_backward(
        after_attn, grad_final, grad_mlp_part, grad_mlp_other, gain_mlp, qkv, w_qkv, w_o
    )
    grad_norm_mlp = grad_norm_mlp.reshape(-1)
    grad_attn_in = tp_sum(grad_attn_part)

    attn_cut = 1024 if grad_qkv_low.shape[1] > 1024 else 128
    attn_in_late = after(attn_in, grad_attn_part)
    attn_blocks = (
        grad_blocks([(attn_in_late, grad_qkv_low[:, :attn_cut])], 0),
        grad_blocks(
            [
                (attn_in_late, grad_qkv_low[:, attn_cut:]),
                (grad_attn_low, mixed_low),
                (final_low, grad_logits),
            ],
            1,
        ),
    )
    near_in_low = after(jnp.concatenate(near_ins, axis=0), attn_blocks[1][0])
    near_in_low = near_in_low.astype(jnp.bfloat16)
    near_hidden, near_gate, near_up = hidden_parts(
        near_in_low, near_grad_hidden, own_units(w_gate), own_units(w_up)
    )
    quad_in = jnp.concatenate([mlp_in, near_in_low], axis=0)
    quad_final = jnp.concatenate([grad_mlp_low, near_final_low], axis=0)
    quad_hidden = jnp.concatenate([own_units(hidden_low), near_hidden], axis=0)
    quad_gate = jnp.concatenate([own_units(grad_gate_low), near_gate], axis=0)
    quad_up = jnp.concatenate([own_units(grad_up_low), near_up], axis=0)
    mlp_product = jnp.concatenate(
        [
            dot_left(quad_final, quad_hidden),
            dot_left(quad_in, jnp.concatenate([quad_gate, quad_up], axis=1)),
        ],
        axis=1,
    ).reshape((2,) * seq_bits() + (model_width // parts, -1))
    mlp_far, mlp_near = halve(mlp_product, seq_bits() - 2, 1)
    mlp_got = to_partner(mlp_far, 1)
    attn_got = [to_partner(attn_blocks[first][0], first) for first in range(2)]
    grad_attn_in = after(grad_attn_in, mlp_far)
    back_attn, grad_norm_attn = rms_back(stream_in, gain_attn, grad_attn_in)
    grad_stream = grad_mid + back_attn
    grad_global = jnp.sum(grad_stream.reshape(patch_total, 8, model_width), axis=1)
    grad_mix_low = (grad_global * valid).astype(jnp.bfloat16)
    grad_normed = dot_plain(grad_mix_low, w_out).reshape(streams, patch_count, inner_width)
    grad_mix_gain = jnp.sum(grad_normed * unit_normed, axis=(0, 1))
    grad_result, grad_gate_in = norm_back(grad_normed * mix_scale)
    grad_z_low = grad_gate_in.reshape(patch_total, inner_width).astype(jnp.bfloat16)
    row_block = model_width // parts
    mix_rows = (grad_global * valid).reshape(streams, patch_count, parts, row_block)
    mix_rows = jnp.transpose(mix_rows, (2, 1, 0, 3)).reshape(parts, patch_count, -1)
    dealing = jnp.concatenate([by_lane(grad_result), by_lane(grad_gate_in), mix_rows], axis=-1)
    dealt = after(trade(dealing), *attn_got).reshape(places, -1)
    grad_scanned = dealt[:, :width]
    attn_far = [after(attn_blocks[first][1], dealt)[1] + attn_got[first][1] for first in range(2)]
    attn_crossed = [to_partner(attn_far[first], 1 - first) for first in range(2)]
    grad_scanned = after(grad_scanned, *attn_far)
    if use_kernel:
        back_sent, conv_grads, head_grads = scan_backward(scan_args, grad_scanned)
        lane_x = back_sent[:, :width]
        scan_params = (
            conv_grads[:4],
            conv_grads[4],
            head_grads[0, :own_heads],
            head_grads[1, :own_heads],
            head_grads[2, :own_heads],
        )
    else:
        scan_grads = scan_back(grad_scanned)
        back_sent = jnp.concatenate(
            [scan_grads[0], jnp.pad(scan_grads[1], ((0, 0), (0, pad_width)))], axis=-1
        )
        lane_x, scan_params = scan_grads[0][:, :width], scan_grads[2:]
    back_sent = back_sent.reshape(parts, patch_count, -1)
    back_taken = after(trade(back_sent), mlp_got, *attn_crossed)
    grad_x = from_lanes(back_taken[..., :width])
    by_stream = back_taken.reshape(streams, lanes, patch_count, -1)
    grad_bc = jnp.sum(by_stream[..., width:scan_width], axis=1)
    grad_dt = from_lanes(back_taken[..., scan_width : scan_width + own_heads])
    grad_dt = jnp.sum(grad_dt.reshape(streams, patch_count, head_total, shared), axis=-1)
    grad_shared = jnp.concatenate([grad_bc, grad_dt], axis=-1).reshape(patch_total, -1)
    grad_proj_low = jnp.concatenate(
        [grad_z_low, grad_x.reshape(patch_total, -1).astype(jnp.bfloat16)]
        + [grad_shared.astype(jnp.bfloat16)],
        axis=-1,
    )
    grad_u_part = dot_trans(grad_proj_low, w_in)
    grad_u = tp_sum(grad_u_part)
    unit_stream = lax.dynamic_index_in_dim(unit_all, own_stream, 1, keepdims=False)
    u_stream = (after(unit_stream, back_sent) * gain_global).astype(jnp.bfloat16).reshape(places, model_width)
    lane_grads = jnp.concatenate([dealt[:, width : 2 * width], lane_x], axis=1)
    final_lanes = trade(
        dot_left(u_stream, lane_grads.astype(jnp.bfloat16)).reshape(parts, -1, 2 * width)
    )
    final_lanes = jnp.sum(
        final_lanes.reshape(streams, lanes, -1, 2 * width), axis=0
    )
    final_z = jnp.moveaxis(final_lanes[..., :width], 0, 1).reshape(-1, inner_width)
    final_x = jnp.moveaxis(final_lanes[..., width:], 0, 1).reshape(-1, inner_width)
    first_row = seq_index * row_block
    unit_rows = lax.dynamic_slice_in_dim(unit_all, first_row, row_block, 3)
    gain_rows = lax.dynamic_slice_in_dim(gain_global, first_row, row_block, 0)
    u_rows = (unit_rows * gain_rows).astype(jnp.bfloat16).reshape(-1, row_block)
    shared_all = lax.all_gather(grad_shared, "seq", axis=0, tiled=True)
    final_shared = shared_grad(u_rows, shared_all)
    back_global, grad_norm_global = rms_back(patch_out, gain_global, grad_u)
    grad_patch = grad_global + back_global

    patch_sent = jnp.moveaxis(grad_patch.reshape(patch_total, parts, row_block), 1, 0)
    patch_taken = trade(patch_sent)

    part = after(mlp_near, back_taken) + mlp_got
    for bit in range(3, seq_bits()):
        far, near = halve(part, seq_bits() - 1 - bit, bit)
        part = near + to_partner(far, bit)
    mine = part.reshape(QUAD, row_block, -1)
    mlp_final = jnp.moveaxis(side_trade(mine), 0, 1)
    final_down, final_gate, final_up = [
        mlp_final[..., k * hidden_part : (k + 1) * hidden_part].reshape(row_block, -1)
        for k in range(3)
    ]
    part = jnp.concatenate(
        [
            after(attn_blocks[first][1], back_taken)[0] + attn_got[first][0] + attn_crossed[first]
            for first in range(2)
        ],
        axis=-1,
    )
    part = part.reshape((2,) * (seq_bits() - 2) + (row_block, -1))
    for bit in range(2, seq_bits()):
        far, near = halve(part, part.ndim - 3, bit)
        part = near + to_partner(far, bit)
    final_attn = part
    mix_taken = dealt[:, 2 * width :].reshape(parts, patch_count, streams, row_block)
    mix_taken = jnp.moveaxis(mix_taken, 2, 1).reshape(-1, row_block).astype(jnp.bfloat16)
    normed_low_all = (normed_all * mix_scale).reshape(-1, inner_width).astype(jnp.bfloat16)
    final_out = dot_left(mix_taken, normed_low_all)
    patch_taken = patch_taken.reshape(-1, row_block)
    final_patch = patch_grad(patch_taken, bytes_all)
    grad_vec = dot_plain(grad_patch.astype(jnp.bfloat16), w_patch)
    grad_vec = grad_vec.reshape(streams, patch_count, feature, 8)
    grad_own = jnp.swapaxes(grad_vec, 2, 3).reshape(streams, local_rows, feature)
    grad_rows = lax.dynamic_slice_in_dim(
        grad_stream.reshape(streams, local_rows, model_width), tp_index * feature, feature, 2
    )
    grad_bytes = grad_rows + grad_own

    def place_cols(grad):
        blank = jnp.zeros(grad.shape[:-1] + (inner_width,), f32)
        mine = lax.dynamic_update_slice_in_dim(
            blank, grad[..., :width], first_col, grad.ndim - 1
        )
        return jnp.concatenate([mine, grad[..., width:]], axis=-1)

    def place_head(grad):
        return lax.dynamic_update_slice_in_dim(
            jnp.zeros((head_total,), f32), grad, first_head, 0
        )

    small = (
        place_cols(scan_params[0]),
        place_cols(scan_params[1]),
        place_head(scan_params[2]),
        place_head(scan_params[3]),
        place_head(scan_params[4]),
        grad_mix_gain,
        grad_norm_global,
        grad_norm_attn,
        grad_norm_mlp,
    )
    flat = jnp.concatenate([part.reshape(-1) for part in small])
    count = flat.shape[0]
    fill = -count % 1024
    flat = lax.all_gather(jnp.pad(flat, (0, fill)).reshape(-1, 128), "seq", axis=0)
    flat = jnp.sum(flat, axis=0).reshape(-1)
    small_sums = []
    at = 0
    for part in small:
        small_sums.append(flat[at : at + part.size].reshape(part.shape))
        at += part.size

    qkv_cols, o_cols = w_qkv.shape[1], w_o.shape[1]
    return (
        logits.reshape(streams, local_rows, head_cols),
        grad_bytes,
        final_patch,
        small_sums[6],
        jnp.concatenate([final_z, final_x, final_shared], axis=1),
        small_sums[0],
        small_sums[1],
        small_sums[2],
        small_sums[3],
        small_sums[4],
        small_sums[5],
        final_out,
        small_sums[7],
        final_attn[:, :qkv_cols],
        final_attn[:, qkv_cols : qkv_cols + o_cols],
        small_sums[8],
        final_gate,
        final_up,
        final_down,
        final_attn[:, qkv_cols + o_cols :],
    )


def solution(mesh):
    in_specs = (
        P(None, "seq", None),
        P(),
        P(None, "tp"),
        P(),
        P(None, "tp"),
        P(None, "tp"),
        P("tp"),
        P("tp"),
        P("tp"),
        P("tp"),
        P("tp"),
        P(None, "tp"),
        P(),
        P(None, "tp"),
        P(None, "tp"),
        P(),
        P(None, "tp"),
        P(None, "tp"),
        P(None, "tp"),
        P(None, "tp"),
        P(None, "seq", "tp"),
    )
    out_specs = (
        P(None, "seq", "tp"),
        P(None, "seq", "tp"),
        P("seq", "tp"),
        P(),
        P("seq", "tp"),
        P(None, "tp"),
        P("tp"),
        P("tp"),
        P("tp"),
        P("tp"),
        P("tp"),
        P("seq", "tp"),
        P(),
        P("seq", "tp"),
        P("seq", "tp"),
        P(),
        P("seq", "tp"),
        P("seq", "tp"),
        P("seq", "tp"),
        P("seq", "tp"),
    )
    return jax.shard_map(body, mesh=mesh, in_specs=in_specs, out_specs=out_specs, check_vma=False)
```

```python
from functools import partial

import jax
import jax.numpy as jnp
from jax import lax
from jax.experimental import pallas as pl
from jax.experimental.pallas import tpu as pltpu
from jax.sharding import PartitionSpec as P

NS = 128
AD = 64
QUAD = 4


NO_COST = pl.CostEstimate(flops=1024, bytes_accessed=1024, transcendentals=0)
ROOMY = pltpu.CompilerParams(vmem_limit_bytes=56 * 1024 * 1024)

epsilon = 1e-05
highest = lax.Precision.HIGHEST
masked_score = -1e30


def dot_plain(left_side, right_side):
    return jnp.dot(left_side, right_side, preferred_element_type=jnp.float32)


def dot_trans(left_side, right_side):
    return lax.dot_general(
        left_side, right_side, (((1,), (1,)), ((), ())), preferred_element_type=jnp.float32
    )


def dot_left(left_side, right_side):
    return lax.dot_general(
        left_side, right_side, (((0,), (0,)), ((), ())), preferred_element_type=jnp.float32
    )


def rms_scale(values):
    return lax.rsqrt(jnp.mean(values * values, axis=-1, keepdims=True) + epsilon)


def hidden_parts(mlp_in, grad_hidden, w_gate, w_up):
    gate_proj = dot_plain(mlp_in, w_gate)
    up_proj = dot_plain(mlp_in, w_up)
    sigmoid_gate = jax.nn.sigmoid(gate_proj)
    hidden_low = (gate_proj * sigmoid_gate * up_proj).astype(jnp.bfloat16)
    grad_gate_low = (
        grad_hidden * up_proj * sigmoid_gate * (1.0 + gate_proj * (1.0 - sigmoid_gate))
    ).astype(jnp.bfloat16)
    grad_up_low = (grad_hidden * gate_proj * sigmoid_gate).astype(jnp.bfloat16)
    return (hidden_low, grad_gate_low, grad_up_low)


def rms_back(values, gain_values, grad_out):
    scale = rms_scale(values)
    scaled = gain_values * grad_out
    inner_mean = jnp.mean(values * scaled, axis=-1, keepdims=True)
    grad_values = scale * scaled - values * scale * scale * scale * inner_mean
    grad_gain = jnp.sum(values * scale * grad_out, axis=0)
    return (grad_values, grad_gain)


def swap(block, axis, mask):
    return lax.ppermute(block, axis, [(i, i ^ mask) for i in range(lax.axis_size(axis))])


def after(value, *earlier):
    return lax.optimization_barrier((value,) + earlier)[0]


def tp_sum(block):
    return block + swap(block, "tp", 1)


def to_partner(block, bit):
    return swap(block, "seq", 1 << bit)


def halve(part, axis, bit):
    mine = lax.axis_index("seq") >> bit & 1
    far = lax.dynamic_index_in_dim(part, 1 - mine, axis, keepdims=False)
    return far, lax.dynamic_index_in_dim(part, mine, axis, keepdims=False)


def seq_bits():
    return lax.axis_size("seq").bit_length() - 1


def side_masks():
    return (1, 4, 5)


def side_trade(blocks):
    members = [
        [base | high << 2 | low for high in range(2) for low in range(2)]
        for base in range(lax.axis_size("seq"))
        if base & 5 == 0
    ]
    return lax.all_to_all(blocks, "seq", 0, 0, axis_index_groups=members, tiled=True)


def grad_blocks_kernel(pairs, first, relative, rows, member_ref, *refs):
    lefts, rights = refs[: len(pairs)], refs[len(pairs) : 2 * len(pairs)]
    far_ref, near_ref = refs[2 * len(pairs) :]
    other = 1 - first
    at = 0
    for left_ref, right_ref, (low, high) in zip(lefts, rights, pairs):
        got = dot_left(left_ref[...], right_ref[:, low:high])
        places = slice(at, at + high - low)
        for block in range(got.shape[0] // rows):
            place, member = block // QUAD, block % QUAD
            part = got[block * rows : (block + 1) * rows]
            apart = member_ref[0] ^ member
            is_far = apart >> first & 1
            if relative:
                side = apart >> other & 1
            else:
                side = member >> other & 1

            @pl.when(is_far == 1)
            def _():
                if relative:
                    far_ref[side, place, :, places] = part
                else:
                    far_ref[place, side, :, places] = part

            @pl.when(is_far == 0)
            def _():
                if relative:
                    near_ref[side, place, :, places] = part
                else:
                    near_ref[place, side, :, places] = part

        at += high - low


def grad_blocks(terms, first, relative):
    parts = lax.axis_size("seq")
    groups = parts // QUAD
    depth, model_width = terms[0][0].shape
    rows = model_width // parts
    cols = max(128, QUAD * rows)
    places = cols // (QUAD * rows)
    pairs = [(low, high) for unused, unused_right, low, high in terms]
    total = sum(high - low for low, high in pairs)
    member = (lax.axis_index("seq") % QUAD).astype(jnp.int32).reshape(1)
    if relative:
        shape, block = (2, groups, rows, total), (2, places, rows, total)
        out_spec = pl.BlockSpec(block, lambda i, ref: (0, i, 0, 0))
    else:
        shape, block = (groups, 2, rows, total), (places, 2, rows, total)
        out_spec = pl.BlockSpec(block, lambda i, ref: (i, 0, 0, 0))
    out = jax.ShapeDtypeStruct(shape, jnp.float32)
    return pl.pallas_call(
        partial(grad_blocks_kernel, pairs, first, relative, rows),
        grid_spec=pltpu.PrefetchScalarGridSpec(
            num_scalar_prefetch=1,
            grid=(model_width // cols,),
            in_specs=[pl.BlockSpec((depth, cols), lambda i, ref: (0, i)) for term in terms]
            + [pl.BlockSpec(term[1].shape, lambda i, ref: (0, 0)) for term in terms],
            out_specs=[out_spec, out_spec],
        ),
        out_shape=[out, out],
        compiler_params=ROOMY,
        cost_estimate=NO_COST,
    )(member, *[term[0] for term in terms], *[term[1] for term in terms])


def segment_ids(lengths, place_count):
    ends = jnp.cumsum(lengths // 8, dtype=jnp.int32)
    places = jnp.arange(place_count, dtype=jnp.int32)
    short_ids = jnp.sum(
        (places[:, None] >= ends[None, :]).astype(jnp.int32), axis=1, dtype=jnp.int32
    )
    return jnp.stack([jnp.zeros_like(short_ids), short_ids])


def scan_heads(seg_now, head_size, xbc, dt_raw, conv_weight, conv_bias, dt_shift, a_logs, skips):
    place_count = xbc.shape[0]
    conv_sum = conv_bias + conv_weight[3] * xbc
    for offset in range(3):
        distance = 3 - offset
        earlier = jnp.pad(xbc, ((distance, 0), (0, 0)))[:place_count]
        seg_earlier = jnp.pad(seg_now, (distance, 0), constant_values=-1)[:place_count]
        same_doc = (seg_earlier == seg_now).astype(jnp.float32)
        conv_sum = conv_sum + conv_weight[offset] * earlier * same_doc[:, None]
    active = jax.nn.silu(conv_sum)
    head_count = dt_raw.shape[1]
    inner = head_count * head_size
    values = active[:, :inner].reshape(place_count, head_count, head_size)
    in_keys = active[:, inner : inner + NS]
    out_keys = active[:, inner + NS :]
    step_sizes = jax.nn.softplus(dt_raw + dt_shift)
    decay_rates = -step_sizes * jnp.exp(a_logs)
    chunk = min(place_count, 512)
    triangle = jnp.tril(jnp.ones((chunk, chunk), jnp.float32))
    state = jnp.zeros((head_count, head_size, NS), jnp.float32)
    seg_last = jnp.int32(-1)
    outputs = []
    for start in range(0, place_count, chunk):
        stop = start + chunk
        x, b, c = values[start:stop], in_keys[start:stop], out_keys[start:stop]
        dt, seg = step_sizes[start:stop], seg_now[start:stop]
        cumulative = jnp.dot(triangle, decay_rates[start:stop], precision=highest)
        allowed = (triangle > 0.0) & (seg[:, None] == seg[None, :])
        ordered = cumulative.T
        gaps = ordered[:, :, None] - ordered[:, None, :]
        decays = jnp.where(allowed, jnp.exp(jnp.where(allowed, gaps, 0.0)), 0.0)
        crossing = jnp.einsum("pn,jn->pj", c, b, precision=highest)
        mixing = crossing[None] * decays * dt.T[:, None, :]
        result = jnp.einsum("hpj,jhd->phd", mixing, x, precision=highest)
        if start > 0:
            entering = jnp.exp(cumulative) * (seg == seg_last).astype(jnp.float32)[:, None]
            result = result + entering[..., None] * jnp.einsum(
                "pn,hdn->phd", c, state, precision=highest
            )
        if stop < place_count:
            last_same = (seg == seg[-1]).astype(jnp.float32)[:, None]
            weight = jnp.exp(cumulative[-1:] - cumulative) * last_same * dt
            through = jnp.exp(cumulative[-1]) * (seg[-1] == seg_last).astype(jnp.float32)
            state = through[:, None, None] * state + jnp.einsum(
                "jh,jhd,jn->hdn", weight, x, b, precision=highest
            )
            seg_last = seg[-1]
        outputs.append(result + skips[:, None] * x)
    return jnp.concatenate(outputs, axis=0).reshape(place_count, inner)


def gated_unit(result, gate_in):
    gated = result * jax.nn.silu(gate_in)
    return gated * rms_scale(gated)


def patch_far_kernel(grad_ref, gain_ref, bytes_ref, out_ref):
    half = grad_ref.shape[1] // 2
    grad_low = grad_ref[:, half:].astype(jnp.bfloat16)
    out_ref[:half] = dot_left(grad_low, bytes_ref[...].astype(jnp.bfloat16))
    out_ref[half:] = jnp.zeros((out_ref.shape[0] - half, out_ref.shape[1]), jnp.float32)

    @pl.when(pl.program_id(0) == 0)
    def _():
        out_ref[half:, : 2 * half] = gain_ref[...]


def patch_far_grad(grad_rows, gain_part, bytes_all):
    places, cols = grad_rows.shape
    total = bytes_all.shape[1]
    rows = cols // 2 + gain_part.shape[0]
    block = 1024
    return pl.pallas_call(
        patch_far_kernel,
        grid=(total // block,),
        in_specs=[
            pl.BlockSpec((places, cols), lambda i: (0, 0)),
            pl.BlockSpec(gain_part.shape, lambda i: (0, 0)),
            pl.BlockSpec((places, block), lambda i: (0, i)),
        ],
        out_specs=pl.BlockSpec((rows, block), lambda i: (0, i)),
        out_shape=jax.ShapeDtypeStruct((rows, total), jnp.float32),
        compiler_params=ROOMY,
        cost_estimate=NO_COST,
    )(grad_rows, gain_part, bytes_all)


def patch_grad_kernel(grad_ref, *refs):
    byte_refs, got_refs, out_ref, order_ref = refs[:8], refs[8:16], refs[16], refs[17]
    width = byte_refs[0].shape[1]
    total = 8 * width

    @pl.when(pl.program_id(0) == 0)
    def _():
        row = lax.broadcasted_iota(jnp.int32, (total, total), 0)
        col = lax.broadcasted_iota(jnp.int32, (total, total), 1)
        order_ref[...] = jnp.where(row == (col % 8) * width + col // 8, 1.0, 0.0).astype(
            jnp.bfloat16
        )

    grad_low = grad_ref[:, : grad_ref.shape[1] // 2].astype(jnp.bfloat16)
    wide = jnp.concatenate([ref[...].astype(jnp.bfloat16) for ref in byte_refs], axis=1)
    rows = grad_low.shape[1]
    grad = dot_left(grad_low, wide)
    grad = grad + jnp.concatenate([ref[:rows] for ref in got_refs], axis=1)
    high = grad.astype(jnp.bfloat16)
    rest = grad - high.astype(jnp.float32)
    mid = rest.astype(jnp.bfloat16)
    low = (rest - mid.astype(jnp.float32)).astype(jnp.bfloat16)
    order = order_ref[...]
    out_ref[...] = dot_plain(high, order) + (dot_plain(mid, order) + dot_plain(low, order))


def patch_grad(grad_rows, got, bytes_all):
    places, cols = grad_rows.shape
    feature = bytes_all.shape[1] // 8
    chunk = 128
    steps = feature // chunk

    def byte_specs(rows):
        return [
            pl.BlockSpec((rows, chunk), partial(lambda j, i: (0, j * steps + i), j))
            for j in range(8)
        ]

    return pl.pallas_call(
        patch_grad_kernel,
        grid=(steps,),
        in_specs=[pl.BlockSpec((places, cols), lambda i: (0, 0))]
        + byte_specs(places)
        + byte_specs(got.shape[0]),
        out_specs=pl.BlockSpec((cols // 2, 8 * chunk), lambda i: (0, i)),
        out_shape=jax.ShapeDtypeStruct((cols // 2, 8 * feature), jnp.float32),
        scratch_shapes=[pltpu.VMEM((8 * chunk, 8 * chunk), jnp.bfloat16)],
        compiler_params=ROOMY,
        cost_estimate=NO_COST,
    )(grad_rows, *([bytes_all] * 8), *([got] * 8))


def shared_grad_kernel(left_ref, right_ref, out_ref):
    out_ref[...] = dot_left(left_ref[...], right_ref[...].astype(jnp.bfloat16))


def shared_grad(left_side, right_side):
    return pl.pallas_call(
        shared_grad_kernel,
        out_shape=jax.ShapeDtypeStruct(
            (left_side.shape[1], right_side.shape[1]), jnp.float32
        ),
        compiler_params=pltpu.CompilerParams(vmem_limit_bytes=32 * 1024 * 1024),
    )(left_side, right_side)


def trade(blocks):
    return lax.all_to_all(blocks, "seq", 0, 0, tiled=True)


def grid_iota(shape, axis):
    return lax.broadcasted_iota(jnp.int32, shape, axis)


def dot_fine(left_side, right_side, left_axis, right_axis):
    return lax.dot_general(
        left_side,
        right_side,
        (((left_axis,), (right_axis,)), ((), ())),
        preferred_element_type=jnp.float32,
        precision=highest,
    )


def shifted_down(block, distance):
    rows = grid_iota(block.shape, 0)
    return jnp.where(rows >= distance, pltpu.roll(block, distance, 0), 0.0)


def shifted_up(block, distance):
    count = block.shape[0]
    rows = grid_iota(block.shape, 0)
    return jnp.where(rows < count - distance, pltpu.roll(block, count - distance, 0), 0.0)


def scan_terms(taken_ref, same_ref, conv_ref, head_ref):
    places = taken_ref.shape[0]
    channels = conv_ref.shape[1]
    xbc = taken_ref[:, :channels]
    conv_sum = conv_ref[4:5] + conv_ref[3:4] * xbc
    for k in range(3):
        earlier = shifted_down(xbc, 3 - k) * same_ref[:, k : k + 1]
        conv_sum = conv_sum + conv_ref[k : k + 1] * earlier
    gate = jax.nn.sigmoid(conv_sum)
    active = conv_sum * gate
    raw = taken_ref[:, channels:] + head_ref[0:1]
    steps = jnp.maximum(raw, 0.0) + jnp.log1p(jnp.exp(-jnp.abs(raw)))
    rates = -steps * jnp.exp(head_ref[1:2])
    square = (places, places)
    triangle = jnp.where(grid_iota(square, 0) >= grid_iota(square, 1), 1.0, 0.0)
    running = dot_fine(triangle, rates, 1, 0)
    return xbc, conv_sum, gate, active, raw, steps, rates, triangle, running


def scan_forward_kernel(taken_ref, same_ref, conv_ref, head_ref, seg_col, seg_row, out_ref):
    places, width = out_ref.shape
    terms = scan_terms(taken_ref, same_ref, conv_ref, head_ref)
    active, steps, running = terms[3], terms[5], terms[8]
    values = active[:, :width]
    keys, reads = active[:, width : width + NS], active[:, width + NS :]
    steps_row, running_row = steps.T, running.T
    heads = width // 64
    rows = 128
    for first in range(0, places, rows):
        last = first + rows
        shape = (rows, last)
        allowed = (seg_col[first:last] == seg_row[:, :last]) & (
            grid_iota(shape, 0) + first >= grid_iota(shape, 1)
        )
        crossing = dot_fine(reads[first:last], keys[:last], 1, 1)
        lane = grid_iota((rows, width), 1) // 64
        total = head_ref[2:3] * values[first:last]
        for h in range(heads):
            gaps = running[first:last, h : h + 1] - running_row[h : h + 1, :last]
            decays = jnp.exp(jnp.where(allowed, gaps, masked_score))
            mixing = crossing * decays * steps_row[h : h + 1, :last]
            part = dot_fine(mixing, values[:last], 1, 0)
            total = total + jnp.where(lane == h, part, 0.0)
        out_ref[first:last] = total


def scan_backward_kernel(
    taken_ref,
    same_ref,
    conv_ref,
    head_ref,
    seg_col,
    seg_row,
    grad_ref,
    out_ref,
    conv_grad_ref,
    head_grad_ref,
    values_grad,
    keys_grad,
    reads_grad,
    rows_grad,
    cols_grad,
):
    places, width = values_grad.shape
    terms = scan_terms(taken_ref, same_ref, conv_ref, head_ref)
    xbc, conv_sum, gate, active, raw, steps, rates, triangle, running = terms
    channels = xbc.shape[1]
    values = active[:, :width]
    keys, reads = active[:, width : width + NS], active[:, width + NS :]
    steps_row, running_row = steps.T, running.T
    heads = width // 64
    rows = 128
    grad = grad_ref[...]
    values_grad[...] = head_ref[2:3] * grad
    keys_grad[...] = jnp.zeros_like(keys_grad)
    rows_grad[...] = jnp.zeros_like(rows_grad)
    cols_grad[...] = jnp.zeros_like(cols_grad)
    for first in range(0, places, rows):
        last = first + rows
        shape = (rows, last)
        allowed = (seg_col[first:last] == seg_row[:, :last]) & (
            grid_iota(shape, 0) + first >= grid_iota(shape, 1)
        )
        crossing = dot_fine(reads[first:last], keys[:last], 1, 1)
        crossing_grad = jnp.zeros(shape, jnp.float32)
        grad_rows = grad[first:last]
        lane = grid_iota((rows, width), 1) // 64
        wide_lane = grid_iota((last, width), 1) // 64
        column = grid_iota((rows, 128), 1)
        down = jnp.zeros((rows, 128), jnp.float32)
        for h in range(heads):
            gaps = running[first:last, h : h + 1] - running_row[h : h + 1, :last]
            decays = jnp.exp(jnp.where(allowed, gaps, masked_score))
            step_row = steps_row[h : h + 1, :last]
            weighted = decays * step_row
            mixing = crossing * weighted
            own_grad = jnp.where(lane == h, grad_rows, 0.0)
            mixing_grad = dot_fine(own_grad, values[:last], 1, 1)
            back = dot_fine(mixing, own_grad, 0, 0)
            values_grad[:last] += jnp.where(wide_lane == h, back, 0.0)
            crossing_grad = crossing_grad + mixing_grad * weighted
            step_part = jnp.sum(mixing_grad * crossing * decays, axis=0, keepdims=True)
            gap_part = mixing_grad * mixing
            down = jnp.where(column == h, jnp.sum(gap_part, axis=1, keepdims=True), down)
            cols_grad[h : h + 1, :last] += step_part
            cols_grad[heads + h : heads + h + 1, :last] += step_part * step_row
        rows_grad[first:last] += down
        reads_grad[first:last] = dot_fine(crossing_grad, keys[:last], 1, 0)
        keys_grad[:last] += dot_fine(crossing_grad, reads[first:last], 0, 0)
    turned = cols_grad[...].T
    column = grid_iota(turned.shape, 1)
    step_grad = jnp.where(column < heads, turned, 0.0)
    ended = pltpu.roll(turned, turned.shape[1] - heads, 1)
    running_grad = jnp.where(column < heads, rows_grad[...] - ended, 0.0)
    rates_grad = dot_fine(triangle, running_grad, 0, 0)
    step_grad = step_grad - rates_grad * jnp.exp(head_ref[1:2])
    raw_grad = step_grad * jax.nn.sigmoid(raw)
    out_ref[:, channels:] = raw_grad
    lane = grid_iota((places, width), 1) // 64
    product = jnp.sum(grad * values, axis=0, keepdims=True)
    head_grad_ref[...] = jnp.zeros_like(head_grad_ref)
    head_grad_ref[0:1] = jnp.sum(raw_grad, axis=0, keepdims=True)
    head_grad_ref[1:2] = jnp.sum(rates_grad * rates, axis=0, keepdims=True)
    skip_lane = grid_iota((1, width), 1)
    skip_grad = jnp.zeros((1, width), jnp.float32)
    for h in range(heads):
        own = jnp.sum(jnp.where(skip_lane // 64 == h, product, 0.0), axis=1, keepdims=True)
        skip_grad = jnp.where(skip_lane == h, own, skip_grad)
    head_grad_ref[2:3] = skip_grad
    active_grad = jnp.concatenate([values_grad[...], keys_grad[...], reads_grad[...]], axis=1)
    conv_grad = active_grad * gate * (1.0 + conv_sum * (1.0 - gate))
    back = conv_ref[3:4] * conv_grad
    conv_grad_ref[...] = jnp.zeros_like(conv_grad_ref)
    conv_grad_ref[3:4] = jnp.sum(conv_grad * xbc, axis=0, keepdims=True)
    conv_grad_ref[4:5] = jnp.sum(conv_grad, axis=0, keepdims=True)
    for k in range(3):
        kept = conv_grad * same_ref[:, k : k + 1]
        back = back + conv_ref[k : k + 1] * shifted_up(kept, 3 - k)
        conv_grad_ref[k : k + 1] = jnp.sum(
            kept * shifted_down(xbc, 3 - k), axis=0, keepdims=True
        )
    out_ref[:, :channels] = back


def scan_forward(args, width):
    places = args[0].shape[0]
    return pl.pallas_call(
        scan_forward_kernel,
        out_shape=jax.ShapeDtypeStruct((places, width), jnp.float32),
        compiler_params=ROOMY,
        cost_estimate=NO_COST,
    )(*args)


def scan_backward(args, grad):
    places, width = grad.shape
    channels = args[2].shape[1]
    f32 = jnp.float32
    return pl.pallas_call(
        scan_backward_kernel,
        out_shape=[
            jax.ShapeDtypeStruct((places, channels + 128), f32),
            jax.ShapeDtypeStruct((8, channels), f32),
            jax.ShapeDtypeStruct((8, 128), f32),
        ],
        scratch_shapes=[
            pltpu.VMEM((places, width), f32),
            pltpu.VMEM((places, NS), f32),
            pltpu.VMEM((places, NS), f32),
            pltpu.VMEM((places, 128), f32),
            pltpu.VMEM((128, places), f32),
        ],
        compiler_params=ROOMY,
        cost_estimate=NO_COST,
    )(*args, grad)


def patch_lanes(block):
    shape = (block // 8, 8, block)
    return grid_iota(shape, 0) == grid_iota(shape, 2) // 8


def folded(scores, same_patch):
    split = scores.reshape(same_patch.shape)
    return jnp.sum(jnp.where(same_patch, split, 0.0), axis=0)


def unfolded(rows, same_patch):
    spread = jnp.where(same_patch, rows[None], 0.0)
    return spread.reshape(-1, rows.shape[1]).astype(jnp.bfloat16)


def head_probs(queries, keys, same_patch, causal):
    scores = jnp.where(causal, folded(dot_trans(keys, queries), same_patch), masked_score)
    top = jnp.max(scores, axis=0, keepdims=True)
    powers = jnp.exp(scores - top)
    return powers / jnp.sum(powers, axis=0, keepdims=True)


def attn_forward_kernel(
    bytes_ref, patch_ref, gain_ref, qkv_w_ref, o_w_ref, x_ref, a_ref, qkv_ref, o_ref, out_ref
):
    rows = bytes_ref.shape[0]
    spread = jnp.where(
        grid_iota((rows, rows // 8), 0) // 8 == grid_iota((rows, rows // 8), 1), 1.0, 0.0
    )
    x = bytes_ref[...].astype(jnp.float32) + dot_fine(spread, patch_ref[...], 1, 0)
    x_ref[...] = x
    attn_in = (x * rms_scale(x) * gain_ref[...]).astype(jnp.bfloat16)
    a_ref[...] = attn_in
    qkv_ref[...] = dot_plain(attn_in, qkv_w_ref[...]).astype(jnp.bfloat16)
    head_cols = o_ref.shape[1]
    block = 128
    same_patch = patch_lanes(block)
    causal = grid_iota((8, block), 0) <= grid_iota((8, block), 1) % 8
    lane = grid_iota((block, 128), 1) // AD
    for first in range(0, rows, block):
        place = slice(first, first + block)
        for pair in range(head_cols // 128):
            cols = [
                slice(j * head_cols + pair * 128, j * head_cols + pair * 128 + 128)
                for j in range(3)
            ]
            queries, keys, values = [qkv_ref[place, c] for c in cols]
            queries = queries * 0.125
            total = jnp.zeros((block, 128), jnp.float32)
            for h in range(2):
                own_queries = jnp.where(lane == h, queries, 0)
                probs = head_probs(own_queries, keys, same_patch, causal)
                part = dot_left(unfolded(probs, same_patch), values)
                total = jnp.where(lane == h, part, total)
            o_ref[place, pair * 128 : pair * 128 + 128] = total.astype(jnp.bfloat16)
    out_ref[...] = dot_trans(o_ref[...], o_w_ref[...])


def attn_forward(bytes_rows, patch_rows, gain, w_qkv, w_o):
    rows, width = bytes_rows.shape
    block = 256
    cols, head_cols = w_qkv.shape[1], w_o.shape[1]
    f32, bf16 = jnp.float32, jnp.bfloat16

    def by_rows(cols):
        return pl.BlockSpec((block, cols), lambda i: (i, 0))

    def whole(shape):
        return pl.BlockSpec(shape, lambda i: (0, 0))

    return pl.pallas_call(
        attn_forward_kernel,
        grid=(rows // block,),
        in_specs=[
            by_rows(width),
            pl.BlockSpec((block // 8, width), lambda i: (i, 0)),
            whole((1, width)),
            whole(w_qkv.shape),
            whole(w_o.shape),
        ],
        out_specs=[by_rows(width), by_rows(width), by_rows(cols), by_rows(head_cols), by_rows(width)],
        out_shape=[
            jax.ShapeDtypeStruct((rows, width), f32),
            jax.ShapeDtypeStruct((rows, width), bf16),
            jax.ShapeDtypeStruct((rows, cols), bf16),
            jax.ShapeDtypeStruct((rows, head_cols), bf16),
            jax.ShapeDtypeStruct((rows, width), f32),
        ],
        compiler_params=ROOMY,
        cost_estimate=NO_COST,
    )(bytes_rows, patch_rows, gain.reshape(1, width), w_qkv, w_o)


def attn_backward_kernel(
    x_ref,
    final_ref,
    own_ref,
    other_ref,
    gain_ref,
    qkv_ref,
    qkv_w_ref,
    o_w_ref,
    mid_ref,
    low_ref,
    qkv_grad_ref,
    out_ref,
    gain_grad_ref,
):
    rows = x_ref.shape[0]
    back, gain_grad = rms_back(x_ref[...], gain_ref[...], own_ref[...] + other_ref[...])
    mid = final_ref[...] + back
    mid_ref[...] = mid
    low_ref[...] = mid.astype(jnp.bfloat16)
    gain_grad = gain_grad.reshape(1, -1)

    @pl.when(pl.program_id(0) == 0)
    def _():
        gain_grad_ref[...] = gain_grad

    @pl.when(pl.program_id(0) > 0)
    def _():
        gain_grad_ref[...] += gain_grad

    mixed_grad = dot_plain(low_ref[...], o_w_ref[...]).astype(jnp.bfloat16)
    head_cols = mixed_grad.shape[1]
    block = 128
    same_patch = patch_lanes(block)
    causal = grid_iota((8, block), 0) <= grid_iota((8, block), 1) % 8
    lane = grid_iota((block, 128), 1) // AD
    for first in range(0, rows, block):
        place = slice(first, first + block)
        for pair in range(head_cols // 128):
            cols = [
                slice(j * head_cols + pair * 128, j * head_cols + pair * 128 + 128)
                for j in range(3)
            ]
            queries, keys, values = [qkv_ref[place, c] for c in cols]
            out_grad = mixed_grad[place, pair * 128 : pair * 128 + 128]
            grads = [jnp.zeros((block, 128), jnp.float32)] * 3
            for h in range(2):
                own = lane == h
                own_queries = jnp.where(own, queries * 0.125, 0)
                probs = head_probs(own_queries, keys, same_patch, causal)
                own_grad = jnp.where(own, out_grad, 0)
                probs_grad = folded(dot_trans(values, own_grad), same_patch)
                inner = jnp.sum(probs * probs_grad, axis=0, keepdims=True)
                scores_grad = unfolded(probs * (probs_grad - inner), same_patch)
                parts = (
                    dot_left(scores_grad, keys) * 0.125,
                    dot_plain(scores_grad, queries) * 0.125,
                    dot_plain(unfolded(probs, same_patch), out_grad),
                )
                grads = [jnp.where(own, part, grad) for part, grad in zip(parts, grads)]
            for c, grad in zip(cols, grads):
                qkv_grad_ref[place, c] = grad.astype(jnp.bfloat16)
    out_ref[...] = dot_trans(qkv_grad_ref[...], qkv_w_ref[...])


def attn_backward(x_rows, final_grad, own_part, other_part, gain, qkv, w_qkv, w_o):
    rows, width = x_rows.shape
    block = 256
    cols = w_qkv.shape[1]
    f32, bf16 = jnp.float32, jnp.bfloat16

    def by_rows(cols):
        return pl.BlockSpec((block, cols), lambda i: (i, 0))

    def whole(shape):
        return pl.BlockSpec(shape, lambda i: (0, 0))

    return pl.pallas_call(
        attn_backward_kernel,
        grid=(rows // block,),
        in_specs=[by_rows(width)] * 4
        + [whole((1, width)), by_rows(cols), whole(w_qkv.shape), whole(w_o.shape)],
        out_specs=[
            by_rows(width),
            by_rows(width),
            by_rows(cols),
            by_rows(width),
            whole((1, width)),
        ],
        out_shape=[
            jax.ShapeDtypeStruct((rows, width), f32),
            jax.ShapeDtypeStruct((rows, width), bf16),
            jax.ShapeDtypeStruct((rows, cols), bf16),
            jax.ShapeDtypeStruct((rows, width), f32),
            jax.ShapeDtypeStruct((1, width), f32),
        ],
        compiler_params=ROOMY,
        cost_estimate=NO_COST,
    )(x_rows, final_grad, own_part, other_part, gain.reshape(1, width), qkv, w_qkv, w_o)


def body(
    byte_states,
    lengths,
    w_patch,
    norm_global,
    w_in,
    conv_w,
    conv_b,
    dt_bias,
    a_log,
    d_skip,
    mix_gain,
    w_out,
    norm_attn,
    w_qkv,
    w_o,
    norm_mlp,
    w_gate,
    w_up,
    w_down,
    w_head,
    d_logits,
):
    streams, local_rows, model_width = byte_states.shape
    patch_count = local_rows // 8
    patch_total = streams * patch_count
    row_total = streams * local_rows
    feature = w_patch.shape[1] // 8
    inner_width = w_out.shape[1]
    channels = conv_w.shape[1]
    head_total = dt_bias.shape[0]
    head_cols = w_head.shape[1]
    parts = lax.axis_size("seq")
    tp_index = lax.axis_index("tp")
    seq_index = lax.axis_index("seq")
    places = parts * patch_count
    f32 = jnp.float32

    lanes = parts // streams
    width = inner_width // lanes
    full_head = inner_width // head_total
    own_heads = max(1, width // full_head)
    shared = max(1, full_head // width)
    head_size = width // own_heads
    own_stream = seq_index // lanes
    first_col = (seq_index % lanes) * width
    first_head = first_col // full_head

    seg_full = segment_ids(lengths, places)
    seg_own = lax.dynamic_slice_in_dim(seg_full, seq_index * patch_count, patch_count, 1)
    seg_stream = lax.dynamic_index_in_dim(seg_full, own_stream, 0, keepdims=False)
    valid = (seg_own < lengths.shape[0]).astype(f32).reshape(patch_total, 1)
    byte_valid = jnp.repeat(valid, 8, axis=0)

    member = (seq_index >> 2 & 1) * 2 + (seq_index & 1)
    raw_logits = d_logits.reshape(row_total, head_cols)
    raw_wide = raw_logits.astype(f32)
    near_raws = [swap(raw_wide, "seq", mask) for mask in side_masks()]
    grid = byte_states.reshape(streams, patch_count, 8, model_width)
    own_part = lax.dynamic_slice_in_dim(grid, tp_index * feature, feature, 3)
    patch_vec = jnp.swapaxes(own_part, 2, 3).reshape(patch_total, feature * 8)
    patch_out = tp_sum(dot_trans(patch_vec, w_patch))
    gain_global = norm_global.astype(f32)
    unit_patch = patch_out * rms_scale(patch_out)
    u_low = (unit_patch * gain_global).astype(jnp.bfloat16)
    half_width = model_width // 2
    unit_patch_half = lax.dynamic_slice_in_dim(unit_patch, tp_index * half_width, half_width, 1)
    unit_own = lax.all_gather(unit_patch_half, "seq", axis=0, tiled=True)
    unit_other = swap(unit_own, "tp", 1)
    proj = dot_plain(u_low, w_in).reshape(streams, patch_count, -1)
    gate_in = proj[..., :inner_width]
    xbc = proj[..., inner_width : inner_width + channels]
    dt_raw = proj[..., inner_width + channels :]

    def by_lane(columns):
        split = columns.reshape(streams, patch_count, lanes, -1)
        return jnp.moveaxis(split, 2, 1).reshape(parts, patch_count, -1)

    def from_lanes(blocks):
        split = blocks.reshape(streams, lanes, patch_count, -1)
        return jnp.moveaxis(split, 1, 2).reshape(streams, patch_count, -1)

    def to_all_lanes(columns):
        wide = jnp.broadcast_to(
            columns[:, None], (streams, lanes, patch_count, columns.shape[-1])
        )
        return wide.reshape(parts, patch_count, -1)

    pad_width = 128 - own_heads
    dt_lanes = by_lane(jnp.repeat(dt_raw, shared, axis=2))
    sent = jnp.concatenate(
        [
            by_lane(xbc[..., :inner_width]),
            to_all_lanes(xbc[..., inner_width:]),
            jnp.pad(dt_lanes, ((0, 0), (0, 0), (0, pad_width))),
        ],
        axis=-1,
    )
    taken = trade(sent)
    grad_logits = after(raw_logits, sent) * byte_valid.astype(jnp.bfloat16)
    grad_final = tp_sum(dot_trans(grad_logits, w_head))
    near_logits = []
    for at, mask in enumerate(side_masks()):
        near_seg = lax.dynamic_slice_in_dim(
            seg_full, (seq_index ^ mask) * patch_count, patch_count, 1
        )
        near_valid = (near_seg < lengths.shape[0]).astype(f32).reshape(patch_total, 1)
        near_raw = after(near_raws[at], sent)
        near_logits.append(near_raw * jnp.repeat(near_valid, 8, axis=0))
    near_logits = jnp.concatenate(near_logits, axis=0).astype(jnp.bfloat16)
    near_final_low = tp_sum(dot_trans(near_logits, w_head)).astype(jnp.bfloat16)
    grad_mlp_low = grad_final.astype(jnp.bfloat16)
    grad_hidden = dot_plain(grad_mlp_low, w_down)
    hidden_part = w_gate.shape[1] // QUAD

    def own_units(columns):
        return lax.dynamic_slice_in_dim(columns, member * hidden_part, hidden_part, 1)

    near_grad_hidden = dot_plain(near_final_low, own_units(w_down))

    bytes_wide = after(own_part, sent).reshape(patch_total, 8 * feature).astype(f32)
    row_side = [
        [device for device in range(parts) if (device >> 1 & 1) == side] for side in range(2)
    ]
    bytes_all = lax.all_gather(
        bytes_wide, "seq", axis=0, axis_index_groups=row_side, tiled=True
    )
    taken = after(taken, grad_hidden, near_grad_hidden, bytes_wide).reshape(places, -1)
    scan_width = width + channels - inner_width

    def own_cols(param):
        mine = lax.dynamic_slice_in_dim(param, first_col, width, param.ndim - 1)
        return jnp.concatenate([mine, param[..., inner_width:]], axis=-1).astype(f32)

    def own_head(param):
        return lax.dynamic_slice_in_dim(param, first_head, own_heads, 0).astype(f32)

    use_kernel = places == 512 and width == 128
    if use_kernel:
        padded_seg = jnp.pad(seg_stream, (3, 0), constant_values=-1)
        same = jnp.stack(
            [(padded_seg[k : k + places] == seg_stream).astype(f32) for k in range(3)]
            + [jnp.zeros((places,), f32)] * 5,
            axis=1,
        )
        conv_pack = jnp.concatenate(
            [own_cols(conv_w), own_cols(conv_b)[None], jnp.zeros((3, scan_width), f32)]
        )
        head_pack = jnp.stack(
            [jnp.pad(own_head(dt_bias), (0, 128 - own_heads))]
            + [jnp.pad(own_head(a_log), (0, 128 - own_heads))]
            + [jnp.repeat(own_head(d_skip), head_size)]
            + [jnp.zeros((128,), f32)] * 5
        )
        scan_args = (taken, same, conv_pack, head_pack, seg_stream[:, None], seg_stream[None])
        scanned = scan_forward(scan_args, width)
    else:
        scan_args = (
            taken[:, :scan_width],
            taken[:, scan_width : scan_width + own_heads],
            own_cols(conv_w),
            own_cols(conv_b),
            own_head(dt_bias),
            own_head(a_log),
            own_head(d_skip),
        )
        scanned, scan_back = jax.vjp(partial(scan_heads, seg_stream, head_size), *scan_args)
    result = from_lanes(trade(scanned.reshape(parts, patch_count, width)))
    unit_normed, norm_back = jax.vjp(gated_unit, result, gate_in)
    mix_scale = mix_gain.astype(f32)
    normed_low = (unit_normed * mix_scale).reshape(patch_total, -1).astype(jnp.bfloat16)
    normed_all = lax.all_gather(unit_normed, "seq", axis=0)
    global_out = patch_out + valid * tp_sum(dot_trans(normed_low, w_out))
    gain_attn = norm_attn.astype(f32)
    gain_mlp = norm_mlp.astype(f32)
    stream_in, attn_in, qkv, mixed_low, attn_part = attn_forward(
        byte_states.reshape(row_total, model_width), global_out, gain_attn, w_qkv, w_o
    )
    after_attn = stream_in + tp_sum(attn_part)
    unit_mlp = after_attn * rms_scale(after_attn)
    mlp_in = (unit_mlp * gain_mlp).astype(jnp.bfloat16)
    unit_half = lax.dynamic_slice_in_dim(unit_mlp, tp_index * half_width, half_width, 1)
    mlp_in = after(mlp_in, unit_half)
    hidden_low, grad_gate_low, grad_up_low = hidden_parts(mlp_in, grad_hidden, w_gate, w_up)
    grad_mlp_part = dot_trans(grad_gate_low, w_gate) + dot_trans(grad_up_low, w_up)
    near_halves = [swap(unit_half, "seq", mask) for mask in side_masks()]
    grad_mlp_other = after(swap(grad_mlp_part, "tp", 1), near_halves[0], near_halves[1])
    after_mlp = after_attn + tp_sum(dot_trans(after(hidden_low, grad_mlp_part), w_down))
    final_low = after_mlp.astype(jnp.bfloat16)
    logits = dot_plain(final_low, w_head) * byte_valid
    grad_mid, grad_attn_low, grad_qkv_low, grad_attn_part, grad_norm_mlp = attn_backward(
        after_attn, grad_final, grad_mlp_part, grad_mlp_other, gain_mlp, qkv, w_qkv, w_o
    )
    grad_norm_mlp = grad_norm_mlp.reshape(-1)
    grad_attn_in = tp_sum(grad_attn_part)

    near_ins = []
    for near_half in near_halves:
        own_half = after(near_half, grad_attn_part)
        other_half = swap(own_half, "tp", 1)
        first_half = jnp.where(tp_index == 0, own_half, other_half)
        second_half = jnp.where(tp_index == 0, other_half, own_half)
        near_ins.append(jnp.concatenate([first_half, second_half], axis=1) * gain_mlp)
    attn_cut = 1024 if grad_qkv_low.shape[1] > 1024 else 128
    attn_in_late = after(attn_in, grad_attn_part)
    attn_cols = grad_qkv_low.shape[1]
    attn_blocks = (
        grad_blocks([(attn_in_late, grad_qkv_low, 0, attn_cut)], 0, True),
        grad_blocks(
            [
                (attn_in_late, grad_qkv_low, attn_cut, attn_cols),
                (grad_attn_low, mixed_low, 0, mixed_low.shape[1]),
                (final_low, grad_logits, 0, head_cols),
            ],
            1,
            True,
        ),
    )
    near_in_low = after(jnp.concatenate(near_ins, axis=0), attn_blocks[1][0])
    near_in_low = near_in_low.astype(jnp.bfloat16)
    near_hidden, near_gate, near_up = hidden_parts(
        near_in_low, near_grad_hidden, own_units(w_gate), own_units(w_up)
    )
    quad_in = jnp.concatenate([mlp_in, near_in_low], axis=0)
    quad_final = jnp.concatenate([grad_mlp_low, near_final_low], axis=0)
    quad_hidden = jnp.concatenate([own_units(hidden_low), near_hidden], axis=0)
    quad_gate = jnp.concatenate([own_units(grad_gate_low), near_gate], axis=0)
    quad_up = jnp.concatenate([own_units(grad_up_low), near_up], axis=0)
    mlp_far, mlp_near = grad_blocks(
        [
            (quad_final, quad_hidden, 0, hidden_part),
            (quad_in, quad_gate, 0, hidden_part),
            (quad_in, quad_up, 0, hidden_part),
        ],
        1,
        False,
    )
    mlp_got = to_partner(mlp_far, 1)
    attn_got = [to_partner(attn_blocks[first][0], first) for first in range(2)]
    grad_attn_in = after(grad_attn_in, mlp_far)
    back_attn, grad_norm_attn = rms_back(stream_in, gain_attn, grad_attn_in)
    grad_stream = grad_mid + back_attn
    grad_global = jnp.sum(grad_stream.reshape(patch_total, 8, model_width), axis=1)
    grad_mix_low = (grad_global * valid).astype(jnp.bfloat16)
    grad_normed = dot_plain(grad_mix_low, w_out).reshape(streams, patch_count, inner_width)
    grad_mix_gain = jnp.sum(grad_normed * unit_normed, axis=(0, 1))
    grad_result, grad_gate_in = norm_back(grad_normed * mix_scale)
    grad_z_low = grad_gate_in.reshape(patch_total, inner_width).astype(jnp.bfloat16)
    row_block = model_width // parts
    mix_rows = (grad_global * valid).reshape(streams, patch_count, parts, row_block)
    mix_rows = jnp.transpose(mix_rows, (2, 1, 0, 3)).reshape(parts, patch_count, -1)
    dealing = jnp.concatenate([by_lane(grad_result), by_lane(grad_gate_in), mix_rows], axis=-1)
    dealt = after(trade(dealing), bytes_all, unit_other, *attn_got).reshape(places, -1)
    grad_scanned = dealt[:, :width]
    attn_far = [after(attn_blocks[first][1], dealt)[1] + attn_got[first][1] for first in range(2)]
    attn_crossed = [to_partner(attn_far[first], 1 - first) for first in range(2)]
    grad_scanned = after(grad_scanned, *attn_far)
    if use_kernel:
        back_sent, conv_grads, head_grads = scan_backward(scan_args, grad_scanned)
        lane_x = back_sent[:, :width]
        scan_params = (
            conv_grads[:4],
            conv_grads[4],
            head_grads[0, :own_heads],
            head_grads[1, :own_heads],
            head_grads[2, :own_heads],
        )
    else:
        scan_grads = scan_back(grad_scanned)
        back_sent = jnp.concatenate(
            [scan_grads[0], jnp.pad(scan_grads[1], ((0, 0), (0, pad_width)))], axis=-1
        )
        lane_x, scan_params = scan_grads[0][:, :width], scan_grads[2:]
    back_sent = back_sent.reshape(parts, patch_count, -1)
    back_taken = after(trade(back_sent), mlp_got, normed_all, *attn_crossed)
    grad_x = from_lanes(back_taken[..., :width])
    by_stream = back_taken.reshape(streams, lanes, patch_count, -1)
    grad_bc = jnp.sum(by_stream[..., width:scan_width], axis=1)
    grad_dt = from_lanes(back_taken[..., scan_width : scan_width + own_heads])
    grad_dt = jnp.sum(grad_dt.reshape(streams, patch_count, head_total, shared), axis=-1)
    grad_shared = jnp.concatenate([grad_bc, grad_dt], axis=-1).reshape(patch_total, -1)
    grad_proj_low = jnp.concatenate(
        [grad_z_low, grad_x.reshape(patch_total, -1).astype(jnp.bfloat16)]
        + [grad_shared.astype(jnp.bfloat16)],
        axis=-1,
    )
    grad_u_part = dot_trans(grad_proj_low, w_in)
    grad_u = tp_sum(grad_u_part)
    def stream_part(halves):
        split = halves.reshape(parts, streams, patch_count, half_width)
        mine = lax.dynamic_index_in_dim(split, own_stream, 1, keepdims=False)
        return after(mine, grad_u_part).reshape(places, half_width)

    own_cut, other_cut = stream_part(unit_own), stream_part(unit_other)
    unit_stream = jnp.concatenate(
        [
            jnp.where(tp_index == 0, own_cut, other_cut),
            jnp.where(tp_index == 0, other_cut, own_cut),
        ],
        axis=1,
    )
    u_stream = (unit_stream * gain_global).astype(jnp.bfloat16)
    lane_grads = jnp.concatenate([dealt[:, width : 2 * width], lane_x], axis=1)
    final_lanes = trade(
        dot_left(u_stream, lane_grads.astype(jnp.bfloat16)).reshape(parts, -1, 2 * width)
    )
    final_lanes = jnp.sum(
        final_lanes.reshape(streams, lanes, -1, 2 * width), axis=0
    )
    final_z = jnp.moveaxis(final_lanes[..., :width], 0, 1).reshape(-1, inner_width)
    final_x = jnp.moveaxis(final_lanes[..., width:], 0, 1).reshape(-1, inner_width)
    first_row = seq_index * row_block
    first_in_half = first_row % half_width
    unit_rows = jnp.where(
        first_row // half_width == tp_index,
        lax.dynamic_slice_in_dim(unit_own, first_in_half, row_block, 1),
        lax.dynamic_slice_in_dim(unit_other, first_in_half, row_block, 1),
    )
    gain_rows = lax.dynamic_slice_in_dim(gain_global, first_row, row_block, 0)
    u_rows = (unit_rows * gain_rows).astype(jnp.bfloat16)

    def place_cols(grad):
        blank = jnp.zeros(grad.shape[:-1] + (inner_width,), f32)
        mine = lax.dynamic_update_slice_in_dim(
            blank, grad[..., :width], first_col, grad.ndim - 1
        )
        return jnp.concatenate([mine, grad[..., width:]], axis=-1)

    def place_head(grad):
        return lax.dynamic_update_slice_in_dim(
            jnp.zeros((head_total,), f32), grad, first_head, 0
        )

    small = (
        place_cols(scan_params[0]),
        place_cols(scan_params[1]),
        place_head(scan_params[2]),
        place_head(scan_params[3]),
        place_head(scan_params[4]),
        grad_mix_gain,
        grad_norm_attn,
        grad_norm_mlp,
    )
    flat = jnp.concatenate([part.reshape(-1) for part in small])
    shared_cols = grad_shared.shape[1]
    wide_cols = shared_cols + -shared_cols % 128
    flat = jnp.pad(flat, (0, -flat.shape[0] % (8 * wide_cols))).reshape(-1, wide_cols)
    wide = jnp.pad(grad_shared, ((0, 0), (0, wide_cols - shared_cols)))
    gathered = lax.all_gather(jnp.concatenate([wide, flat], axis=0), "seq", axis=0)
    shared_all = gathered[:, :patch_total, :shared_cols].reshape(-1, shared_cols)
    flat = jnp.sum(gathered[:, patch_total:], axis=0).reshape(-1)
    small_sums = []
    at = 0
    for part in small:
        small_sums.append(flat[at : at + part.size].reshape(part.shape))
        at += part.size
    final_shared = shared_grad(u_rows, shared_all)
    back_global, grad_norm_global = rms_back(patch_out, gain_global, grad_u)
    grad_patch = grad_global + back_global

    side_count = parts // 2
    my_side = seq_index >> 1 & 1
    by_block = jnp.moveaxis(grad_patch.reshape(patch_total, parts, row_block), 1, 0)
    by_block = by_block.reshape(parts // 4, 2, 2, patch_total, row_block)
    same_side = lax.dynamic_index_in_dim(by_block, my_side, 1, keepdims=False)
    other_side = lax.dynamic_index_in_dim(by_block, 1 - my_side, 1, keepdims=False)
    patch_rows = jnp.concatenate([same_side, other_side], axis=-1)
    patch_rows = patch_rows.reshape(side_count, patch_total, 2 * row_block)
    gain_part = grad_norm_global.reshape(-1, 2 * row_block)
    gain_count = gain_part.shape[0]
    patch_sent = jnp.concatenate(
        [patch_rows, jnp.broadcast_to(gain_part, (side_count,) + gain_part.shape)], axis=1
    )
    patch_taken = lax.all_to_all(
        patch_sent, "seq", 0, 0, axis_index_groups=row_side, tiled=True
    )

    part = after(mlp_near, back_taken) + mlp_got
    part = part.reshape((2,) * (seq_bits() - 1) + (row_block, -1))
    for bit in range(3, seq_bits()):
        far, near = halve(part, seq_bits() - 1 - bit, bit)
        part = near + to_partner(far, bit)
    mine = part.reshape(QUAD, row_block, -1)
    mlp_final = jnp.moveaxis(side_trade(mine), 0, 1)
    final_down, final_gate, final_up = [
        mlp_final[..., k * hidden_part : (k + 1) * hidden_part].reshape(row_block, -1)
        for k in range(3)
    ]
    part = jnp.concatenate(
        [
            after(attn_blocks[first][1], back_taken)[0] + attn_got[first][0] + attn_crossed[first]
            for first in range(2)
        ],
        axis=-1,
    )
    part = part.reshape((2,) * (seq_bits() - 2) + (row_block, -1))
    for bit in range(2, seq_bits()):
        far, near = halve(part, part.ndim - 3, bit)
        part = near + to_partner(far, bit)
    final_attn = part
    mix_taken = dealt[:, 2 * width :].reshape(parts, patch_count, streams, row_block)
    mix_taken = jnp.moveaxis(mix_taken, 2, 1).reshape(-1, row_block).astype(jnp.bfloat16)
    normed_low_all = (normed_all * mix_scale).reshape(-1, inner_width).astype(jnp.bfloat16)
    final_out = dot_left(mix_taken, normed_low_all)
    gain_side = jnp.sum(patch_taken[:, patch_total:], axis=0)
    patch_taken = patch_taken[:, :patch_total].reshape(-1, 2 * row_block)
    patch_far = patch_far_grad(patch_taken, gain_side, bytes_all)
    patch_got = to_partner(patch_far, 1)
    final_patch = patch_grad(patch_taken, patch_got, bytes_all)
    norm_global_sum = (gain_side + patch_got[row_block:, : 2 * row_block]).reshape(-1)
    grad_vec = dot_plain(grad_patch.astype(jnp.bfloat16), w_patch)
    grad_vec = grad_vec.reshape(streams, patch_count, feature, 8)
    grad_own = jnp.swapaxes(grad_vec, 2, 3).reshape(streams, local_rows, feature)
    grad_rows = lax.dynamic_slice_in_dim(
        grad_stream.reshape(streams, local_rows, model_width), tp_index * feature, feature, 2
    )
    grad_bytes = grad_rows + grad_own

    qkv_cols, o_cols = w_qkv.shape[1], w_o.shape[1]
    return (
        logits.reshape(streams, local_rows, head_cols),
        grad_bytes,
        final_patch,
        norm_global_sum,
        jnp.concatenate([final_z, final_x, final_shared], axis=1),
        small_sums[0],
        small_sums[1],
        small_sums[2],
        small_sums[3],
        small_sums[4],
        small_sums[5],
        final_out,
        small_sums[6],
        final_attn[:, :qkv_cols],
        final_attn[:, qkv_cols : qkv_cols + o_cols],
        small_sums[7],
        final_gate,
        final_up,
        final_down,
        final_attn[:, qkv_cols + o_cols :],
    )


def solution(mesh):
    in_specs = (
        P(None, "seq", None),
        P(),
        P(None, "tp"),
        P(),
        P(None, "tp"),
        P(None, "tp"),
        P("tp"),
        P("tp"),
        P("tp"),
        P("tp"),
        P("tp"),
        P(None, "tp"),
        P(),
        P(None, "tp"),
        P(None, "tp"),
        P(),
        P(None, "tp"),
        P(None, "tp"),
        P(None, "tp"),
        P(None, "tp"),
        P(None, "seq", "tp"),
    )
    out_specs = (
        P(None, "seq", "tp"),
        P(None, "seq", "tp"),
        P("seq", "tp"),
        P(),
        P("seq", "tp"),
        P(None, "tp"),
        P("tp"),
        P("tp"),
        P("tp"),
        P("tp"),
        P("tp"),
        P("seq", "tp"),
        P(),
        P("seq", "tp"),
        P("seq", "tp"),
        P(),
        P("seq", "tp"),
        P("seq", "tp"),
        P("seq", "tp"),
        P("seq", "tp"),
    )
    return jax.shard_map(body, mesh=mesh, in_specs=in_specs, out_specs=out_specs, check_vma=False)
```

```python
from functools import partial

import jax
import jax.numpy as jnp
from jax import lax
from jax.experimental import pallas as pl
from jax.experimental.pallas import tpu as pltpu
from jax.sharding import PartitionSpec as P

NS = 128
AD = 64
QUAD = 4


NO_COST = pl.CostEstimate(flops=1024, bytes_accessed=1024, transcendentals=0)
ROOMY = pltpu.CompilerParams(vmem_limit_bytes=56 * 1024 * 1024)

epsilon = 1e-05
highest = lax.Precision.HIGHEST
masked_score = -1e30


def dot_plain(left_side, right_side):
    return jnp.dot(left_side, right_side, preferred_element_type=jnp.float32)


def dot_trans(left_side, right_side):
    return lax.dot_general(
        left_side, right_side, (((1,), (1,)), ((), ())), preferred_element_type=jnp.float32
    )


def dot_left(left_side, right_side):
    return lax.dot_general(
        left_side, right_side, (((0,), (0,)), ((), ())), preferred_element_type=jnp.float32
    )


def rms_scale(values):
    return lax.rsqrt(jnp.mean(values * values, axis=-1, keepdims=True) + epsilon)


def hidden_parts(mlp_in, grad_hidden, w_gate, w_up):
    gate_proj = dot_plain(mlp_in, w_gate)
    up_proj = dot_plain(mlp_in, w_up)
    sigmoid_gate = jax.nn.sigmoid(gate_proj)
    hidden_low = (gate_proj * sigmoid_gate * up_proj).astype(jnp.bfloat16)
    grad_gate_low = (
        grad_hidden * up_proj * sigmoid_gate * (1.0 + gate_proj * (1.0 - sigmoid_gate))
    ).astype(jnp.bfloat16)
    grad_up_low = (grad_hidden * gate_proj * sigmoid_gate).astype(jnp.bfloat16)
    return (hidden_low, grad_gate_low, grad_up_low)


def rms_back(values, gain_values, grad_out):
    scale = rms_scale(values)
    scaled = gain_values * grad_out
    inner_mean = jnp.mean(values * scaled, axis=-1, keepdims=True)
    grad_values = scale * scaled - values * scale * scale * scale * inner_mean
    grad_gain = jnp.sum(values * scale * grad_out, axis=0)
    return (grad_values, grad_gain)


def swap(block, axis, mask):
    return lax.ppermute(block, axis, [(i, i ^ mask) for i in range(lax.axis_size(axis))])


def after(value, *earlier):
    return lax.optimization_barrier((value,) + earlier)[0]


def tp_sum(block):
    return block + swap(block, "tp", 1)


def to_partner(block, bit):
    return swap(block, "seq", 1 << bit)


def halve(part, axis, bit):
    mine = lax.axis_index("seq") >> bit & 1
    far = lax.dynamic_index_in_dim(part, 1 - mine, axis, keepdims=False)
    return far, lax.dynamic_index_in_dim(part, mine, axis, keepdims=False)


def seq_bits():
    return lax.axis_size("seq").bit_length() - 1


def side_masks():
    return (1, 4, 5)


def side_trade(blocks):
    members = [
        [base | high << 2 | low for high in range(2) for low in range(2)]
        for base in range(lax.axis_size("seq"))
        if base & 5 == 0
    ]
    return lax.all_to_all(blocks, "seq", 0, 0, axis_index_groups=members, tiled=True)


def grad_blocks_kernel(pairs, first, relative, rows, member_ref, *refs):
    lefts, rights = refs[: len(pairs)], refs[len(pairs) : 2 * len(pairs)]
    far_ref, near_ref = refs[2 * len(pairs) :]
    other = 1 - first
    at = 0
    for left_ref, right_ref, (low, high) in zip(lefts, rights, pairs):
        got = dot_left(left_ref[...], right_ref[:, low:high].astype(jnp.bfloat16))
        places = slice(at, at + high - low)
        for block in range(got.shape[0] // rows):
            place, member = block // QUAD, block % QUAD
            part = got[block * rows : (block + 1) * rows]
            apart = member_ref[0] ^ member
            is_far = apart >> first & 1
            if relative:
                side = apart >> other & 1
            else:
                side = member >> other & 1

            @pl.when(is_far == 1)
            def _():
                if relative:
                    far_ref[side, place, :, places] = part
                else:
                    far_ref[place, side, :, places] = part

            @pl.when(is_far == 0)
            def _():
                if relative:
                    near_ref[side, place, :, places] = part
                else:
                    near_ref[place, side, :, places] = part

        at += high - low


def grad_blocks(terms, first, relative):
    parts = lax.axis_size("seq")
    groups = parts // QUAD
    model_width = terms[0][0].shape[1]
    rows = model_width // parts
    cols = max(128, QUAD * rows)
    places = cols // (QUAD * rows)
    pairs = [(low, high) for unused, unused_right, low, high in terms]
    total = sum(high - low for low, high in pairs)
    member = (lax.axis_index("seq") % QUAD).astype(jnp.int32).reshape(1)
    if relative:
        shape, block = (2, groups, rows, total), (2, places, rows, total)
        out_spec = pl.BlockSpec(block, lambda i, ref: (0, i, 0, 0))
    else:
        shape, block = (groups, 2, rows, total), (places, 2, rows, total)
        out_spec = pl.BlockSpec(block, lambda i, ref: (i, 0, 0, 0))
    out = jax.ShapeDtypeStruct(shape, jnp.float32)
    return pl.pallas_call(
        partial(grad_blocks_kernel, pairs, first, relative, rows),
        grid_spec=pltpu.PrefetchScalarGridSpec(
            num_scalar_prefetch=1,
            grid=(model_width // cols,),
            in_specs=[
                pl.BlockSpec((term[0].shape[0], cols), lambda i, ref: (0, i)) for term in terms
            ]
            + [pl.BlockSpec(term[1].shape, lambda i, ref: (0, 0)) for term in terms],
            out_specs=[out_spec, out_spec],
        ),
        out_shape=[out, out],
        compiler_params=ROOMY,
        cost_estimate=NO_COST,
    )(member, *[term[0] for term in terms], *[term[1] for term in terms])


def segment_ids(lengths, place_count):
    ends = jnp.cumsum(lengths // 8, dtype=jnp.int32)
    places = jnp.arange(place_count, dtype=jnp.int32)
    short_ids = jnp.sum(
        (places[:, None] >= ends[None, :]).astype(jnp.int32), axis=1, dtype=jnp.int32
    )
    return jnp.stack([jnp.zeros_like(short_ids), short_ids])


def scan_heads(seg_now, head_size, xbc, dt_raw, conv_weight, conv_bias, dt_shift, a_logs, skips):
    place_count = xbc.shape[0]
    conv_sum = conv_bias + conv_weight[3] * xbc
    for offset in range(3):
        distance = 3 - offset
        earlier = jnp.pad(xbc, ((distance, 0), (0, 0)))[:place_count]
        seg_earlier = jnp.pad(seg_now, (distance, 0), constant_values=-1)[:place_count]
        same_doc = (seg_earlier == seg_now).astype(jnp.float32)
        conv_sum = conv_sum + conv_weight[offset] * earlier * same_doc[:, None]
    active = jax.nn.silu(conv_sum)
    head_count = dt_raw.shape[1]
    inner = head_count * head_size
    values = active[:, :inner].reshape(place_count, head_count, head_size)
    in_keys = active[:, inner : inner + NS]
    out_keys = active[:, inner + NS :]
    step_sizes = jax.nn.softplus(dt_raw + dt_shift)
    decay_rates = -step_sizes * jnp.exp(a_logs)
    chunk = min(place_count, 512)
    triangle = jnp.tril(jnp.ones((chunk, chunk), jnp.float32))
    state = jnp.zeros((head_count, head_size, NS), jnp.float32)
    seg_last = jnp.int32(-1)
    outputs = []
    for start in range(0, place_count, chunk):
        stop = start + chunk
        x, b, c = values[start:stop], in_keys[start:stop], out_keys[start:stop]
        dt, seg = step_sizes[start:stop], seg_now[start:stop]
        cumulative = jnp.dot(triangle, decay_rates[start:stop], precision=highest)
        allowed = (triangle > 0.0) & (seg[:, None] == seg[None, :])
        ordered = cumulative.T
        gaps = ordered[:, :, None] - ordered[:, None, :]
        decays = jnp.where(allowed, jnp.exp(jnp.where(allowed, gaps, 0.0)), 0.0)
        crossing = jnp.einsum("pn,jn->pj", c, b, precision=highest)
        mixing = crossing[None] * decays * dt.T[:, None, :]
        result = jnp.einsum("hpj,jhd->phd", mixing, x, precision=highest)
        if start > 0:
            entering = jnp.exp(cumulative) * (seg == seg_last).astype(jnp.float32)[:, None]
            result = result + entering[..., None] * jnp.einsum(
                "pn,hdn->phd", c, state, precision=highest
            )
        if stop < place_count:
            last_same = (seg == seg[-1]).astype(jnp.float32)[:, None]
            weight = jnp.exp(cumulative[-1:] - cumulative) * last_same * dt
            through = jnp.exp(cumulative[-1]) * (seg[-1] == seg_last).astype(jnp.float32)
            state = through[:, None, None] * state + jnp.einsum(
                "jh,jhd,jn->hdn", weight, x, b, precision=highest
            )
            seg_last = seg[-1]
        outputs.append(result + skips[:, None] * x)
    return jnp.concatenate(outputs, axis=0).reshape(place_count, inner)


def gated_unit(result, gate_in):
    gated = result * jax.nn.silu(gate_in)
    return gated * rms_scale(gated)


def patch_far_kernel(grad_ref, gain_ref, bytes_ref, out_ref):
    half = grad_ref.shape[1] // 2
    grad_low = grad_ref[:, half:].astype(jnp.bfloat16)
    out_ref[:half] = dot_left(grad_low, bytes_ref[...].astype(jnp.bfloat16))
    out_ref[half:] = jnp.zeros((out_ref.shape[0] - half, out_ref.shape[1]), jnp.float32)

    @pl.when(pl.program_id(0) == 0)
    def _():
        out_ref[half:, : 2 * half] = gain_ref[...]


def patch_far_grad(grad_rows, gain_part, bytes_all):
    places, cols = grad_rows.shape
    total = bytes_all.shape[1]
    rows = cols // 2 + gain_part.shape[0]
    block = 1024
    return pl.pallas_call(
        patch_far_kernel,
        grid=(total // block,),
        in_specs=[
            pl.BlockSpec((places, cols), lambda i: (0, 0)),
            pl.BlockSpec(gain_part.shape, lambda i: (0, 0)),
            pl.BlockSpec((places, block), lambda i: (0, i)),
        ],
        out_specs=pl.BlockSpec((rows, block), lambda i: (0, i)),
        out_shape=jax.ShapeDtypeStruct((rows, total), jnp.float32),
        compiler_params=ROOMY,
        cost_estimate=NO_COST,
    )(grad_rows, gain_part, bytes_all)


def patch_grad_kernel(grad_ref, *refs):
    byte_refs, got_refs, out_ref, order_ref = refs[:8], refs[8:16], refs[16], refs[17]
    width = byte_refs[0].shape[1]
    total = 8 * width

    @pl.when(pl.program_id(0) == 0)
    def _():
        row = lax.broadcasted_iota(jnp.int32, (total, total), 0)
        col = lax.broadcasted_iota(jnp.int32, (total, total), 1)
        order_ref[...] = jnp.where(row == (col % 8) * width + col // 8, 1.0, 0.0).astype(
            jnp.bfloat16
        )

    grad_low = grad_ref[:, : grad_ref.shape[1] // 2].astype(jnp.bfloat16)
    wide = jnp.concatenate([ref[...].astype(jnp.bfloat16) for ref in byte_refs], axis=1)
    rows = grad_low.shape[1]
    grad = dot_left(grad_low, wide)
    grad = grad + jnp.concatenate([ref[:rows] for ref in got_refs], axis=1)
    high = grad.astype(jnp.bfloat16)
    rest = grad - high.astype(jnp.float32)
    mid = rest.astype(jnp.bfloat16)
    low = (rest - mid.astype(jnp.float32)).astype(jnp.bfloat16)
    order = order_ref[...]
    out_ref[...] = dot_plain(high, order) + (dot_plain(mid, order) + dot_plain(low, order))


def patch_grad(grad_rows, got, bytes_all):
    places, cols = grad_rows.shape
    feature = bytes_all.shape[1] // 8
    chunk = 128
    steps = feature // chunk

    def byte_specs(rows):
        return [
            pl.BlockSpec((rows, chunk), partial(lambda j, i: (0, j * steps + i), j))
            for j in range(8)
        ]

    return pl.pallas_call(
        patch_grad_kernel,
        grid=(steps,),
        in_specs=[pl.BlockSpec((places, cols), lambda i: (0, 0))]
        + byte_specs(places)
        + byte_specs(got.shape[0]),
        out_specs=pl.BlockSpec((cols // 2, 8 * chunk), lambda i: (0, i)),
        out_shape=jax.ShapeDtypeStruct((cols // 2, 8 * feature), jnp.float32),
        scratch_shapes=[pltpu.VMEM((8 * chunk, 8 * chunk), jnp.bfloat16)],
        compiler_params=ROOMY,
        cost_estimate=NO_COST,
    )(grad_rows, *([bytes_all] * 8), *([got] * 8))


def trade(blocks):
    return lax.all_to_all(blocks, "seq", 0, 0, tiled=True)


def grid_iota(shape, axis):
    return lax.broadcasted_iota(jnp.int32, shape, axis)


def dot_fine(left_side, right_side, left_axis, right_axis):
    return lax.dot_general(
        left_side,
        right_side,
        (((left_axis,), (right_axis,)), ((), ())),
        preferred_element_type=jnp.float32,
        precision=highest,
    )


def shifted_down(block, distance):
    rows = grid_iota(block.shape, 0)
    return jnp.where(rows >= distance, pltpu.roll(block, distance, 0), 0.0)


def shifted_up(block, distance):
    count = block.shape[0]
    rows = grid_iota(block.shape, 0)
    return jnp.where(rows < count - distance, pltpu.roll(block, count - distance, 0), 0.0)


def scan_terms(taken_ref, same_ref, conv_ref, head_ref):
    places = taken_ref.shape[0]
    channels = conv_ref.shape[1]
    xbc = taken_ref[:, :channels]
    conv_sum = conv_ref[4:5] + conv_ref[3:4] * xbc
    for k in range(3):
        earlier = shifted_down(xbc, 3 - k) * same_ref[:, k : k + 1]
        conv_sum = conv_sum + conv_ref[k : k + 1] * earlier
    gate = jax.nn.sigmoid(conv_sum)
    active = conv_sum * gate
    raw = taken_ref[:, channels:] + head_ref[0:1]
    steps = jnp.maximum(raw, 0.0) + jnp.log1p(jnp.exp(-jnp.abs(raw)))
    rates = -steps * jnp.exp(head_ref[1:2])
    square = (places, places)
    triangle = jnp.where(grid_iota(square, 0) >= grid_iota(square, 1), 1.0, 0.0)
    running = dot_fine(triangle, rates, 1, 0)
    return xbc, conv_sum, gate, active, raw, steps, rates, triangle, running


def scan_forward_kernel(taken_ref, same_ref, conv_ref, head_ref, seg_col, seg_row, out_ref):
    places, width = out_ref.shape
    terms = scan_terms(taken_ref, same_ref, conv_ref, head_ref)
    active, steps, running = terms[3], terms[5], terms[8]
    values = active[:, :width]
    keys, reads = active[:, width : width + NS], active[:, width + NS :]
    steps_row, running_row = steps.T, running.T
    heads = width // 64
    rows = 128
    for first in range(0, places, rows):
        last = first + rows
        shape = (rows, last)
        allowed = (seg_col[first:last] == seg_row[:, :last]) & (
            grid_iota(shape, 0) + first >= grid_iota(shape, 1)
        )
        crossing = dot_fine(reads[first:last], keys[:last], 1, 1)
        lane = grid_iota((rows, width), 1) // 64
        total = head_ref[2:3] * values[first:last]
        for h in range(heads):
            gaps = running[first:last, h : h + 1] - running_row[h : h + 1, :last]
            decays = jnp.exp(jnp.where(allowed, gaps, masked_score))
            mixing = crossing * decays * steps_row[h : h + 1, :last]
            part = dot_fine(mixing, values[:last], 1, 0)
            total = total + jnp.where(lane == h, part, 0.0)
        out_ref[first:last] = total


def scan_backward_kernel(
    taken_ref,
    same_ref,
    conv_ref,
    head_ref,
    seg_col,
    seg_row,
    grad_ref,
    out_ref,
    conv_grad_ref,
    head_grad_ref,
    values_grad,
    keys_grad,
    reads_grad,
    rows_grad,
    cols_grad,
):
    places, width = values_grad.shape
    terms = scan_terms(taken_ref, same_ref, conv_ref, head_ref)
    xbc, conv_sum, gate, active, raw, steps, rates, triangle, running = terms
    channels = xbc.shape[1]
    values = active[:, :width]
    keys, reads = active[:, width : width + NS], active[:, width + NS :]
    steps_row, running_row = steps.T, running.T
    heads = width // 64
    rows = 128
    grad = grad_ref[...]
    values_grad[...] = head_ref[2:3] * grad
    keys_grad[...] = jnp.zeros_like(keys_grad)
    rows_grad[...] = jnp.zeros_like(rows_grad)
    cols_grad[...] = jnp.zeros_like(cols_grad)
    for first in range(0, places, rows):
        last = first + rows
        shape = (rows, last)
        allowed = (seg_col[first:last] == seg_row[:, :last]) & (
            grid_iota(shape, 0) + first >= grid_iota(shape, 1)
        )
        crossing = dot_fine(reads[first:last], keys[:last], 1, 1)
        crossing_grad = jnp.zeros(shape, jnp.float32)
        grad_rows = grad[first:last]
        lane = grid_iota((rows, width), 1) // 64
        wide_lane = grid_iota((last, width), 1) // 64
        column = grid_iota((rows, 128), 1)
        down = jnp.zeros((rows, 128), jnp.float32)
        for h in range(heads):
            gaps = running[first:last, h : h + 1] - running_row[h : h + 1, :last]
            decays = jnp.exp(jnp.where(allowed, gaps, masked_score))
            step_row = steps_row[h : h + 1, :last]
            weighted = decays * step_row
            mixing = crossing * weighted
            own_grad = jnp.where(lane == h, grad_rows, 0.0)
            mixing_grad = dot_fine(own_grad, values[:last], 1, 1)
            back = dot_fine(mixing, own_grad, 0, 0)
            values_grad[:last] += jnp.where(wide_lane == h, back, 0.0)
            crossing_grad = crossing_grad + mixing_grad * weighted
            step_part = jnp.sum(mixing_grad * crossing * decays, axis=0, keepdims=True)
            gap_part = mixing_grad * mixing
            down = jnp.where(column == h, jnp.sum(gap_part, axis=1, keepdims=True), down)
            cols_grad[h : h + 1, :last] += step_part
            cols_grad[heads + h : heads + h + 1, :last] += step_part * step_row
        rows_grad[first:last] += down
        reads_grad[first:last] = dot_fine(crossing_grad, keys[:last], 1, 0)
        keys_grad[:last] += dot_fine(crossing_grad, reads[first:last], 0, 0)
    turned = cols_grad[...].T
    column = grid_iota(turned.shape, 1)
    step_grad = jnp.where(column < heads, turned, 0.0)
    ended = pltpu.roll(turned, turned.shape[1] - heads, 1)
    running_grad = jnp.where(column < heads, rows_grad[...] - ended, 0.0)
    rates_grad = dot_fine(triangle, running_grad, 0, 0)
    step_grad = step_grad - rates_grad * jnp.exp(head_ref[1:2])
    raw_grad = step_grad * jax.nn.sigmoid(raw)
    out_ref[:, channels:] = raw_grad
    lane = grid_iota((places, width), 1) // 64
    product = jnp.sum(grad * values, axis=0, keepdims=True)
    head_grad_ref[...] = jnp.zeros_like(head_grad_ref)
    head_grad_ref[0:1] = jnp.sum(raw_grad, axis=0, keepdims=True)
    head_grad_ref[1:2] = jnp.sum(rates_grad * rates, axis=0, keepdims=True)
    skip_lane = grid_iota((1, width), 1)
    skip_grad = jnp.zeros((1, width), jnp.float32)
    for h in range(heads):
        own = jnp.sum(jnp.where(skip_lane // 64 == h, product, 0.0), axis=1, keepdims=True)
        skip_grad = jnp.where(skip_lane == h, own, skip_grad)
    head_grad_ref[2:3] = skip_grad
    active_grad = jnp.concatenate([values_grad[...], keys_grad[...], reads_grad[...]], axis=1)
    conv_grad = active_grad * gate * (1.0 + conv_sum * (1.0 - gate))
    back = conv_ref[3:4] * conv_grad
    conv_grad_ref[...] = jnp.zeros_like(conv_grad_ref)
    conv_grad_ref[3:4] = jnp.sum(conv_grad * xbc, axis=0, keepdims=True)
    conv_grad_ref[4:5] = jnp.sum(conv_grad, axis=0, keepdims=True)
    for k in range(3):
        kept = conv_grad * same_ref[:, k : k + 1]
        back = back + conv_ref[k : k + 1] * shifted_up(kept, 3 - k)
        conv_grad_ref[k : k + 1] = jnp.sum(
            kept * shifted_down(xbc, 3 - k), axis=0, keepdims=True
        )
    out_ref[:, :channels] = back


def scan_forward(args, width):
    places = args[0].shape[0]
    return pl.pallas_call(
        scan_forward_kernel,
        out_shape=jax.ShapeDtypeStruct((places, width), jnp.float32),
        compiler_params=ROOMY,
        cost_estimate=NO_COST,
    )(*args)


def scan_backward(args, grad):
    places, width = grad.shape
    channels = args[2].shape[1]
    f32 = jnp.float32
    return pl.pallas_call(
        scan_backward_kernel,
        out_shape=[
            jax.ShapeDtypeStruct((places, channels + 128), f32),
            jax.ShapeDtypeStruct((8, channels), f32),
            jax.ShapeDtypeStruct((8, 128), f32),
        ],
        scratch_shapes=[
            pltpu.VMEM((places, width), f32),
            pltpu.VMEM((places, NS), f32),
            pltpu.VMEM((places, NS), f32),
            pltpu.VMEM((places, 128), f32),
            pltpu.VMEM((128, places), f32),
        ],
        compiler_params=ROOMY,
        cost_estimate=NO_COST,
    )(*args, grad)


def patch_lanes(block):
    shape = (block // 8, 8, block)
    return grid_iota(shape, 0) == grid_iota(shape, 2) // 8


def folded(scores, same_patch):
    split = scores.reshape(same_patch.shape)
    return jnp.sum(jnp.where(same_patch, split, 0.0), axis=0)


def unfolded(rows, same_patch):
    spread = jnp.where(same_patch, rows[None], 0.0)
    return spread.reshape(-1, rows.shape[1]).astype(jnp.bfloat16)


def softmax_rows(scores, causal):
    scores = jnp.where(causal, scores, masked_score)
    top = jnp.max(scores, axis=1, keepdims=True)
    powers = jnp.exp(scores - top)
    return powers / jnp.sum(powers, axis=1, keepdims=True)


def head_places(rows, head_cols, block):
    return [
        (slice(first, first + block), [j * head_cols + pair * 128 for j in range(3)])
        for first in range(0, rows, block)
        for pair in range(head_cols // 128)
    ]


def all_scores(qkv_ref, places, lane, same_patch):
    scores = []
    for rows, (query, key, unused) in places:
        queries = qkv_ref[rows, query : query + 128] * 0.125
        keys = qkv_ref[rows, key : key + 128]
        for h in range(2):
            own = jnp.where(lane == h, queries, 0)
            scores.append(folded(dot_trans(keys, own), same_patch))
    return jnp.stack(scores)


def attn_forward_kernel(
    bytes_ref, patch_ref, gain_ref, qkv_w_ref, o_w_ref, x_ref, a_ref, qkv_ref, o_ref, out_ref
):
    rows = bytes_ref.shape[0]
    spread = jnp.broadcast_to(patch_ref[...][:, None], (rows // 8, 8, patch_ref.shape[1]))
    x = bytes_ref[...].astype(jnp.float32) + spread.reshape(bytes_ref.shape)
    x_ref[...] = x
    attn_in = (x * rms_scale(x) * gain_ref[...]).astype(jnp.bfloat16)
    a_ref[...] = attn_in
    qkv_ref[...] = dot_plain(attn_in, qkv_w_ref[...]).astype(jnp.bfloat16)
    head_cols = o_ref.shape[1]
    block = 128
    same_patch = patch_lanes(block)
    causal = grid_iota((8, block), 0) <= grid_iota((8, block), 1) % 8
    lane = grid_iota((block, 128), 1) // AD
    places = head_places(rows, head_cols, block)
    probs = softmax_rows(all_scores(qkv_ref, places, lane, same_patch), causal)
    for at, (row_place, (query, unused, value)) in enumerate(places):
        values = qkv_ref[row_place, value : value + 128]
        parts = [dot_left(unfolded(probs[2 * at + h], same_patch), values) for h in range(2)]
        total = jnp.where(lane == 0, parts[0], parts[1])
        o_ref[row_place, query : query + 128] = total.astype(jnp.bfloat16)
    out_ref[...] = dot_trans(o_ref[...], o_w_ref[...])


def attn_forward(bytes_rows, patch_rows, gain, w_qkv, w_o):
    rows, width = bytes_rows.shape
    block = 256
    cols, head_cols = w_qkv.shape[1], w_o.shape[1]
    f32, bf16 = jnp.float32, jnp.bfloat16

    def by_rows(cols):
        return pl.BlockSpec((block, cols), lambda i: (i, 0))

    def whole(shape):
        return pl.BlockSpec(shape, lambda i: (0, 0))

    return pl.pallas_call(
        attn_forward_kernel,
        grid=(rows // block,),
        in_specs=[
            by_rows(width),
            pl.BlockSpec((block // 8, width), lambda i: (i, 0)),
            whole((1, width)),
            whole(w_qkv.shape),
            whole(w_o.shape),
        ],
        out_specs=[by_rows(width), by_rows(width), by_rows(cols), by_rows(head_cols), by_rows(width)],
        out_shape=[
            jax.ShapeDtypeStruct((rows, width), f32),
            jax.ShapeDtypeStruct((rows, width), bf16),
            jax.ShapeDtypeStruct((rows, cols), bf16),
            jax.ShapeDtypeStruct((rows, head_cols), bf16),
            jax.ShapeDtypeStruct((rows, width), f32),
        ],
        compiler_params=ROOMY,
        cost_estimate=NO_COST,
    )(bytes_rows, patch_rows, gain.reshape(1, width), w_qkv, w_o)


def attn_backward_kernel(
    x_ref,
    final_ref,
    own_ref,
    other_ref,
    gain_ref,
    qkv_ref,
    qkv_w_ref,
    o_w_ref,
    mid_ref,
    low_ref,
    qkv_grad_ref,
    out_ref,
    gain_grad_ref,
):
    rows = x_ref.shape[0]
    back, gain_grad = rms_back(x_ref[...], gain_ref[...], own_ref[...] + other_ref[...])
    mid = final_ref[...] + back
    mid_ref[...] = mid
    low_ref[...] = mid.astype(jnp.bfloat16)
    gain_grad = gain_grad.reshape(1, -1)

    @pl.when(pl.program_id(0) == 0)
    def _():
        gain_grad_ref[...] = gain_grad

    @pl.when(pl.program_id(0) > 0)
    def _():
        gain_grad_ref[...] += gain_grad

    mixed_grad = dot_plain(low_ref[...], o_w_ref[...]).astype(jnp.bfloat16)
    head_cols = mixed_grad.shape[1]
    block = 128
    same_patch = patch_lanes(block)
    causal = grid_iota((8, block), 0) <= grid_iota((8, block), 1) % 8
    lane = grid_iota((block, 128), 1) // AD
    places = head_places(rows, head_cols, block)
    probs = softmax_rows(all_scores(qkv_ref, places, lane, same_patch), causal)
    probs_grads = []
    for row_place, (query, unused, value) in places:
        values = qkv_ref[row_place, value : value + 128]
        out_grad = mixed_grad[row_place, query : query + 128]
        for h in range(2):
            own_grad = jnp.where(lane == h, out_grad, 0)
            probs_grads.append(folded(dot_trans(values, own_grad), same_patch))
    probs_grad = jnp.stack(probs_grads)
    inner = jnp.sum(probs * probs_grad, axis=1, keepdims=True)
    scores_grad = probs * (probs_grad - inner)
    for at, (row_place, cols) in enumerate(places):
        query, key, unused = cols
        queries = qkv_ref[row_place, query : query + 128]
        keys = qkv_ref[row_place, key : key + 128]
        out_grad = mixed_grad[row_place, query : query + 128]
        parts = []
        for h in range(2):
            own_scores = unfolded(scores_grad[2 * at + h], same_patch)
            parts.append(
                (
                    dot_left(own_scores, keys) * 0.125,
                    dot_plain(own_scores, queries) * 0.125,
                    dot_plain(unfolded(probs[2 * at + h], same_patch), out_grad),
                )
            )
        for j in range(3):
            grad = jnp.where(lane == 0, parts[0][j], parts[1][j])
            qkv_grad_ref[row_place, cols[j] : cols[j] + 128] = grad.astype(jnp.bfloat16)
    out_ref[...] = dot_trans(qkv_grad_ref[...], qkv_w_ref[...])


def attn_backward(x_rows, final_grad, own_part, other_part, gain, qkv, w_qkv, w_o):
    rows, width = x_rows.shape
    block = 256
    cols = w_qkv.shape[1]
    f32, bf16 = jnp.float32, jnp.bfloat16

    def by_rows(cols):
        return pl.BlockSpec((block, cols), lambda i: (i, 0))

    def whole(shape):
        return pl.BlockSpec(shape, lambda i: (0, 0))

    return pl.pallas_call(
        attn_backward_kernel,
        grid=(rows // block,),
        in_specs=[by_rows(width)] * 4
        + [whole((1, width)), by_rows(cols), whole(w_qkv.shape), whole(w_o.shape)],
        out_specs=[
            by_rows(width),
            by_rows(width),
            by_rows(cols),
            by_rows(width),
            whole((1, width)),
        ],
        out_shape=[
            jax.ShapeDtypeStruct((rows, width), f32),
            jax.ShapeDtypeStruct((rows, width), bf16),
            jax.ShapeDtypeStruct((rows, cols), bf16),
            jax.ShapeDtypeStruct((rows, width), f32),
            jax.ShapeDtypeStruct((1, width), f32),
        ],
        compiler_params=ROOMY,
        cost_estimate=NO_COST,
    )(x_rows, final_grad, own_part, other_part, gain.reshape(1, width), qkv, w_qkv, w_o)


def mlp_in_kernel(core_ref, x_ref, own_ref, other_ref, gain_ref, out_ref, low_ref, half_ref):
    x = x_ref[...] + (own_ref[...] + other_ref[...])
    out_ref[...] = x
    unit = x * rms_scale(x)
    low_ref[...] = (unit * gain_ref[...]).astype(jnp.bfloat16)
    width = half_ref.shape[1]
    half_ref[...] = jnp.where(core_ref[0] == 0, unit[:, :width], unit[:, width:])


def mlp_in(x_rows, own_part, other_part, gain):
    rows, width = x_rows.shape
    block = 128
    core = lax.axis_index("tp").astype(jnp.int32).reshape(1)

    def by_rows(cols):
        return pl.BlockSpec((block, cols), lambda i, ref: (i, 0))

    return pl.pallas_call(
        mlp_in_kernel,
        grid_spec=pltpu.PrefetchScalarGridSpec(
            num_scalar_prefetch=1,
            grid=(rows // block,),
            in_specs=[by_rows(width)] * 3 + [pl.BlockSpec((1, width), lambda i, ref: (0, 0))],
            out_specs=[by_rows(width), by_rows(width), by_rows(width // 2)],
        ),
        out_shape=[
            jax.ShapeDtypeStruct((rows, width), jnp.float32),
            jax.ShapeDtypeStruct((rows, width), jnp.bfloat16),
            jax.ShapeDtypeStruct((rows, width // 2), jnp.float32),
        ],
        compiler_params=ROOMY,
        cost_estimate=NO_COST,
    )(core, x_rows, own_part, other_part, gain.reshape(1, width))


def mlp_kernel(
    in_ref, grad_ref, gate_w_ref, up_w_ref, hidden_ref, gate_ref, up_ref, out_ref, total_ref
):
    hidden, gate, up = hidden_parts(
        in_ref[...], grad_ref[...], gate_w_ref[...], up_w_ref[...]
    )
    hidden_ref[...] = hidden
    gate_ref[...] = gate
    up_ref[...] = up
    part = dot_trans(gate, gate_w_ref[...]) + dot_trans(up, up_w_ref[...])
    step = pl.program_id(0)

    @pl.when(step == 0)
    def _():
        total_ref[...] = part

    @pl.when(step > 0)
    def _():
        total_ref[...] += part

    @pl.when(step == pl.num_programs(0) - 1)
    def _():
        out_ref[...] = total_ref[...]


def mlp_rows(mlp_low, grad_hidden, w_gate, w_up):
    rows, width = mlp_low.shape
    units = w_gate.shape[1]
    block = 512
    by_units = pl.BlockSpec((rows, block), lambda i: (0, i))
    by_weights = pl.BlockSpec((width, block), lambda i: (0, i))
    whole = pl.BlockSpec((rows, width), lambda i: (0, 0))
    low = jax.ShapeDtypeStruct((rows, units), jnp.bfloat16)
    return pl.pallas_call(
        mlp_kernel,
        grid=(units // block,),
        in_specs=[whole, by_units, by_weights, by_weights],
        out_specs=[by_units, by_units, by_units, whole],
        out_shape=[low, low, low, jax.ShapeDtypeStruct((rows, width), jnp.float32)],
        scratch_shapes=[pltpu.VMEM((rows, width), jnp.float32)],
        compiler_params=ROOMY,
        cost_estimate=NO_COST,
    )(mlp_low, grad_hidden, w_gate, w_up)


def body(
    byte_states,
    lengths,
    w_patch,
    norm_global,
    w_in,
    conv_w,
    conv_b,
    dt_bias,
    a_log,
    d_skip,
    mix_gain,
    w_out,
    norm_attn,
    w_qkv,
    w_o,
    norm_mlp,
    w_gate,
    w_up,
    w_down,
    w_head,
    d_logits,
):
    streams, local_rows, model_width = byte_states.shape
    patch_count = local_rows // 8
    patch_total = streams * patch_count
    row_total = streams * local_rows
    feature = w_patch.shape[1] // 8
    inner_width = w_out.shape[1]
    channels = conv_w.shape[1]
    head_total = dt_bias.shape[0]
    head_cols = w_head.shape[1]
    parts = lax.axis_size("seq")
    tp_index = lax.axis_index("tp")
    seq_index = lax.axis_index("seq")
    places = parts * patch_count
    f32 = jnp.float32

    lanes = parts // streams
    width = inner_width // lanes
    full_head = inner_width // head_total
    own_heads = max(1, width // full_head)
    shared = max(1, full_head // width)
    head_size = width // own_heads
    own_stream = seq_index // lanes
    first_col = (seq_index % lanes) * width
    first_head = first_col // full_head

    seg_full = segment_ids(lengths, places)
    seg_own = lax.dynamic_slice_in_dim(seg_full, seq_index * patch_count, patch_count, 1)
    seg_stream = lax.dynamic_index_in_dim(seg_full, own_stream, 0, keepdims=False)
    valid = (seg_own < lengths.shape[0]).astype(f32).reshape(patch_total, 1)
    byte_valid = jnp.repeat(valid, 8, axis=0)

    member = (seq_index >> 2 & 1) * 2 + (seq_index & 1)
    raw_logits = d_logits.reshape(row_total, head_cols)
    raw_wide = raw_logits.astype(f32)
    near_raws = [swap(raw_wide, "seq", mask) for mask in side_masks()]
    grid = byte_states.reshape(streams, patch_count, 8, model_width)
    own_part = lax.dynamic_slice_in_dim(grid, tp_index * feature, feature, 3)
    patch_vec = jnp.swapaxes(own_part, 2, 3).reshape(patch_total, feature * 8)
    patch_out = tp_sum(dot_trans(patch_vec, w_patch))
    gain_global = norm_global.astype(f32)
    unit_patch = patch_out * rms_scale(patch_out)
    u_low = (unit_patch * gain_global).astype(jnp.bfloat16)
    half_width = model_width // 2
    proj = dot_plain(u_low, w_in).reshape(streams, patch_count, -1)
    gate_in = proj[..., :inner_width]
    xbc = proj[..., inner_width : inner_width + channels]
    dt_raw = proj[..., inner_width + channels :]

    def by_lane(columns):
        split = columns.reshape(streams, patch_count, lanes, -1)
        return jnp.moveaxis(split, 2, 1).reshape(parts, patch_count, -1)

    def from_lanes(blocks):
        split = blocks.reshape(streams, lanes, patch_count, -1)
        return jnp.moveaxis(split, 1, 2).reshape(streams, patch_count, -1)

    def to_all_lanes(columns):
        wide = jnp.broadcast_to(
            columns[:, None], (streams, lanes, patch_count, columns.shape[-1])
        )
        return wide.reshape(parts, patch_count, -1)

    pad_width = 128 - own_heads
    dt_lanes = by_lane(jnp.repeat(dt_raw, shared, axis=2))
    sent = jnp.concatenate(
        [
            by_lane(xbc[..., :inner_width]),
            to_all_lanes(xbc[..., inner_width:]),
            jnp.pad(dt_lanes, ((0, 0), (0, 0), (0, pad_width))),
        ],
        axis=-1,
    )
    taken = trade(sent)
    grad_logits = after(raw_logits, sent) * byte_valid.astype(jnp.bfloat16)
    grad_final = tp_sum(dot_trans(grad_logits, w_head))
    near_logits = []
    for at, mask in enumerate(side_masks()):
        near_seg = lax.dynamic_slice_in_dim(
            seg_full, (seq_index ^ mask) * patch_count, patch_count, 1
        )
        near_valid = (near_seg < lengths.shape[0]).astype(f32).reshape(patch_total, 1)
        near_raw = after(near_raws[at], sent)
        near_logits.append(near_raw * jnp.repeat(near_valid, 8, axis=0))
    near_logits = jnp.concatenate(near_logits, axis=0).astype(jnp.bfloat16)
    near_final_low = tp_sum(dot_trans(near_logits, w_head)).astype(jnp.bfloat16)
    grad_mlp_low = grad_final.astype(jnp.bfloat16)
    grad_hidden = dot_plain(grad_mlp_low, w_down)
    hidden_part = w_gate.shape[1] // QUAD

    def own_units(columns):
        return lax.dynamic_slice_in_dim(columns, member * hidden_part, hidden_part, 1)

    near_grad_hidden = dot_plain(near_final_low, own_units(w_down))

    bytes_wide = after(own_part, sent).reshape(patch_total, 8 * feature).astype(f32)
    row_side = [
        [device for device in range(parts) if (device >> 1 & 1) == side] for side in range(2)
    ]
    bytes_all = lax.all_gather(
        bytes_wide, "seq", axis=0, axis_index_groups=row_side, tiled=True
    )
    unit_patch_half = lax.dynamic_slice_in_dim(unit_patch, tp_index * half_width, half_width, 1)
    unit_own = lax.all_gather(after(unit_patch_half, bytes_wide), "seq", axis=0, tiled=True)
    unit_other = swap(unit_own, "tp", 1)
    taken = after(taken, grad_hidden, near_grad_hidden, bytes_wide).reshape(places, -1)
    scan_width = width + channels - inner_width

    def own_cols(param):
        mine = lax.dynamic_slice_in_dim(param, first_col, width, param.ndim - 1)
        return jnp.concatenate([mine, param[..., inner_width:]], axis=-1).astype(f32)

    def own_head(param):
        return lax.dynamic_slice_in_dim(param, first_head, own_heads, 0).astype(f32)

    use_kernel = places == 512 and width == 128
    if use_kernel:
        padded_seg = jnp.pad(seg_stream, (3, 0), constant_values=-1)
        same = jnp.stack(
            [(padded_seg[k : k + places] == seg_stream).astype(f32) for k in range(3)]
            + [jnp.zeros((places,), f32)] * 5,
            axis=1,
        )
        conv_pack = jnp.concatenate(
            [own_cols(conv_w), own_cols(conv_b)[None], jnp.zeros((3, scan_width), f32)]
        )
        head_pack = jnp.stack(
            [jnp.pad(own_head(dt_bias), (0, 128 - own_heads))]
            + [jnp.pad(own_head(a_log), (0, 128 - own_heads))]
            + [jnp.repeat(own_head(d_skip), head_size)]
            + [jnp.zeros((128,), f32)] * 5
        )
        scan_args = (taken, same, conv_pack, head_pack, seg_stream[:, None], seg_stream[None])
        scanned = scan_forward(scan_args, width)
    else:
        scan_args = (
            taken[:, :scan_width],
            taken[:, scan_width : scan_width + own_heads],
            own_cols(conv_w),
            own_cols(conv_b),
            own_head(dt_bias),
            own_head(a_log),
            own_head(d_skip),
        )
        scanned, scan_back = jax.vjp(partial(scan_heads, seg_stream, head_size), *scan_args)
    result = from_lanes(trade(scanned.reshape(parts, patch_count, width)))
    unit_normed, norm_back = jax.vjp(gated_unit, result, gate_in)
    mix_scale = mix_gain.astype(f32)
    normed_low = (unit_normed * mix_scale).reshape(patch_total, -1).astype(jnp.bfloat16)

    def to_group(whole, quarters):
        split = quarters.reshape(patch_total, QUAD, inner_width // QUAD)
        wide = jnp.broadcast_to(whole[None], (QUAD,) + whole.shape)
        return side_trade(jnp.concatenate([wide, jnp.moveaxis(split, 1, 0)], axis=-1))

    group_got = to_group(unit_patch, unit_normed)
    group_u = (group_got[..., :model_width] * gain_global).astype(jnp.bfloat16)
    own_scale = lax.dynamic_slice_in_dim(
        mix_scale, member * (inner_width // QUAD), inner_width // QUAD, 0
    )
    group_n = (group_got[..., model_width:] * own_scale).astype(jnp.bfloat16)
    group_u = group_u.reshape(-1, model_width)
    group_n = group_n.reshape(-1, inner_width // QUAD)
    global_out = patch_out + valid * tp_sum(dot_trans(normed_low, w_out))
    gain_attn = norm_attn.astype(f32)
    gain_mlp = norm_mlp.astype(f32)
    stream_in, attn_in, qkv, mixed_low, attn_part = attn_forward(
        byte_states.reshape(row_total, model_width), global_out, gain_attn, w_qkv, w_o
    )
    attn_part = after(attn_part, group_got)
    after_attn, mlp_low, unit_half = mlp_in(
        stream_in, attn_part, swap(attn_part, "tp", 1), gain_mlp
    )
    hidden_low, grad_gate_low, grad_up_low, grad_mlp_part = mlp_rows(
        after(mlp_low, unit_half), grad_hidden, w_gate, w_up
    )
    group_halves = side_trade(jnp.broadcast_to(unit_half[None], (QUAD,) + unit_half.shape))
    grad_mlp_other = swap(grad_mlp_part, "tp", 1)
    after_mlp = after_attn + tp_sum(dot_trans(after(hidden_low, grad_mlp_part), w_down))
    final_low = after_mlp.astype(jnp.bfloat16)
    logits = dot_plain(final_low, w_head) * byte_valid
    grad_mid, grad_attn_low, grad_qkv_low, grad_attn_part, grad_norm_mlp = attn_backward(
        after_attn, grad_final, grad_mlp_part, grad_mlp_other, gain_mlp, qkv, w_qkv, w_o
    )
    grad_norm_mlp = grad_norm_mlp.reshape(-1)
    grad_attn_in = tp_sum(grad_attn_part)

    attn_cut = 1024 if grad_qkv_low.shape[1] > 1024 else 128
    attn_in_late = after(attn_in, grad_attn_part, group_halves)
    attn_cols = grad_qkv_low.shape[1]
    attn_blocks = (
        grad_blocks([(attn_in_late, grad_qkv_low, 0, attn_cut)], 0, True),
        grad_blocks(
            [
                (attn_in_late, grad_qkv_low, attn_cut, attn_cols),
                (grad_attn_low, mixed_low, 0, mixed_low.shape[1]),
                (final_low, grad_logits, 0, head_cols),
            ],
            1,
            True,
        ),
    )
    attn_got = [to_partner(attn_blocks[first][0], first) for first in range(2)]
    grad_attn_in = after(grad_attn_in, attn_blocks[0][0], attn_blocks[1][0])
    back_attn, grad_norm_attn = rms_back(stream_in, gain_attn, grad_attn_in)
    grad_stream = grad_mid + back_attn
    grad_global = jnp.sum(grad_stream.reshape(patch_total, 8, model_width), axis=1)
    grad_mix_low = (grad_global * valid).astype(jnp.bfloat16)
    grad_normed = dot_plain(grad_mix_low, w_out).reshape(streams, patch_count, inner_width)
    grad_mix_gain = jnp.sum(grad_normed * unit_normed, axis=(0, 1))
    grad_result, grad_gate_in = norm_back(grad_normed * mix_scale)
    grad_z_low = grad_gate_in.reshape(patch_total, inner_width).astype(jnp.bfloat16)
    row_block = model_width // parts
    dealing = by_lane(grad_result)
    dealt = trade(dealing)
    own_half = after(group_halves, dealing)
    other_half = swap(own_half, "tp", 1)
    group_in = jnp.concatenate(
        [
            jnp.where(tp_index == 0, own_half, other_half),
            jnp.where(tp_index == 0, other_half, own_half),
        ],
        axis=-1,
    )
    group_in = (group_in * gain_mlp).astype(jnp.bfloat16)
    near_in_low = jnp.concatenate(
        [
            lax.dynamic_index_in_dim(group_in, member ^ apart, 0, keepdims=False)
            for apart in range(1, QUAD)
        ],
        axis=0,
    )
    near_hidden, near_gate, near_up = hidden_parts(
        near_in_low, near_grad_hidden, own_units(w_gate), own_units(w_up)
    )
    quad_in = jnp.concatenate([mlp_low, near_in_low], axis=0)
    quad_final = jnp.concatenate([grad_mlp_low, near_final_low], axis=0)
    quad_hidden = jnp.concatenate([own_units(hidden_low), near_hidden], axis=0)
    quad_gate = jnp.concatenate([own_units(grad_gate_low), near_gate], axis=0)
    quad_up = jnp.concatenate([own_units(grad_up_low), near_up], axis=0)
    late_got = to_group(after(grad_global, near_in_low), grad_gate_in)
    group_valid = []
    for high in range(2):
        for low in range(2):
            device = (seq_index & ~5) | high << 2 | low
            group_seg = lax.dynamic_slice_in_dim(
                seg_full, device * patch_count, patch_count, 1
            )
            group_valid.append((group_seg < lengths.shape[0]).astype(f32))
    group_valid = jnp.stack(group_valid).reshape(QUAD, patch_total, 1)
    group_mix = (late_got[..., :model_width] * group_valid).astype(jnp.bfloat16)
    group_mix = group_mix.reshape(-1, model_width)
    group_z = late_got[..., model_width:].reshape(-1, inner_width // QUAD)
    mlp_blocks = [
        grad_blocks(
            [(quad_final, quad_hidden, 0, hidden_part), (quad_in, quad_gate, 0, hidden_part)],
            1,
            False,
        ),
        grad_blocks(
            [
                (quad_in, quad_up, 0, hidden_part),
                (group_mix, group_n, 0, group_n.shape[1]),
                (group_u, group_z, 0, group_z.shape[1]),
            ],
            1,
            False,
        ),
    ]
    mlp_got = [to_partner(far, 1) for far, unused in mlp_blocks]
    dealt = after(dealt, bytes_all, mlp_blocks[0][0], mlp_blocks[1][0], *attn_got)
    dealt = dealt.reshape(places, width)
    grad_scanned = dealt[:, :width]
    attn_far = [after(attn_blocks[first][1], dealt)[1] + attn_got[first][1] for first in range(2)]
    attn_crossed = [to_partner(attn_far[first], 1 - first) for first in range(2)]
    grad_scanned = after(grad_scanned, *attn_far)
    if use_kernel:
        back_sent, conv_grads, head_grads = scan_backward(scan_args, grad_scanned)
        lane_grad = back_sent[:, : scan_width + own_heads]
        scan_params = (
            conv_grads[:4],
            conv_grads[4],
            head_grads[0, :own_heads],
            head_grads[1, :own_heads],
            head_grads[2, :own_heads],
        )
    else:
        scan_grads = scan_back(grad_scanned)
        back_sent = jnp.concatenate(
            [scan_grads[0], jnp.pad(scan_grads[1], ((0, 0), (0, pad_width)))], axis=-1
        )
        lane_grad = jnp.concatenate([scan_grads[0], scan_grads[1]], axis=-1)
        scan_params = scan_grads[2:]
    back_sent = back_sent.reshape(parts, patch_count, -1)
    back_taken = after(trade(back_sent), mlp_got[0], unit_other, *attn_crossed)
    grad_x = from_lanes(back_taken[..., :width])
    by_stream = back_taken.reshape(streams, lanes, patch_count, -1)
    grad_bc = jnp.sum(by_stream[..., width:scan_width], axis=1)
    grad_dt = from_lanes(back_taken[..., scan_width : scan_width + own_heads])
    grad_dt = jnp.sum(grad_dt.reshape(streams, patch_count, head_total, shared), axis=-1)
    grad_shared = jnp.concatenate([grad_bc, grad_dt], axis=-1).reshape(patch_total, -1)
    grad_proj_low = jnp.concatenate(
        [grad_z_low, grad_x.reshape(patch_total, -1).astype(jnp.bfloat16)]
        + [grad_shared.astype(jnp.bfloat16)],
        axis=-1,
    )
    grad_u_part = dot_trans(grad_proj_low, w_in)
    grad_u = tp_sum(grad_u_part)
    back_global, grad_norm_global = rms_back(patch_out, gain_global, grad_u)
    grad_patch = grad_global + back_global

    side_count = parts // 2
    my_side = seq_index >> 1 & 1
    by_block = jnp.moveaxis(grad_patch.reshape(patch_total, parts, row_block), 1, 0)
    by_block = by_block.reshape(parts // 4, 2, 2, patch_total, row_block)
    same_side = lax.dynamic_index_in_dim(by_block, my_side, 1, keepdims=False)
    other_side = lax.dynamic_index_in_dim(by_block, 1 - my_side, 1, keepdims=False)
    patch_rows = jnp.concatenate([same_side, other_side], axis=-1)
    patch_rows = patch_rows.reshape(side_count, patch_total, 2 * row_block)
    gain_part = grad_norm_global.reshape(-1, 2 * row_block)
    gain_count = gain_part.shape[0]
    patch_sent = jnp.concatenate(
        [patch_rows, jnp.broadcast_to(gain_part, (side_count,) + gain_part.shape)], axis=1
    )
    patch_taken = lax.all_to_all(
        patch_sent, "seq", 0, 0, axis_index_groups=row_side, tiled=True
    )

    gain_side = jnp.sum(patch_taken[:, patch_total:], axis=0)
    patch_cols = patch_taken[:, :patch_total].reshape(-1, 2 * row_block)
    patch_far = patch_far_grad(patch_cols, gain_side, bytes_all)
    def stream_part(halves):
        split = halves.reshape(parts, streams, patch_count, half_width)
        mine = lax.dynamic_index_in_dim(split, own_stream, 1, keepdims=False)
        return after(mine, patch_far).reshape(places, half_width)

    own_cut, other_cut = stream_part(unit_own), stream_part(unit_other)
    unit_stream = jnp.concatenate(
        [
            jnp.where(tp_index == 0, own_cut, other_cut),
            jnp.where(tp_index == 0, other_cut, own_cut),
        ],
        axis=1,
    )
    u_stream = (unit_stream * gain_global).astype(jnp.bfloat16)
    scan_width_grads = lane_grad[:, :scan_width]
    lane_high = lane_grad.astype(jnp.bfloat16)
    shared_low = scan_width_grads[:, width:] - lane_high[:, width:scan_width].astype(f32)
    lane_product = dot_left(u_stream, lane_high)
    shared_rest = dot_left(u_stream, shared_low.astype(jnp.bfloat16))
    small = (
        scan_params[0][:, :width],
        scan_params[1][:width],
        scan_params[0][:, width:],
        scan_params[1][width:],
        scan_params[2],
        scan_params[3],
        scan_params[4],
        grad_mix_gain,
        grad_norm_attn,
        grad_norm_mlp,
    )
    small_count = sum(part.size for part in small)
    shared_end = scan_width + own_heads
    fill = -(-small_count // row_block)
    fill += -(shared_end + fill) % 128
    flat = jnp.concatenate([part.reshape(-1) for part in small])
    flat = jnp.pad(flat, (0, fill * row_block - small_count)).reshape(1, row_block, fill)
    lane_sent = jnp.concatenate(
        [
            lane_product[:, :width].reshape(parts, row_block, -1),
            (lane_product[:, width:scan_width] + shared_rest).reshape(parts, row_block, -1),
            lane_product[:, scan_width:].reshape(parts, row_block, -1),
            jnp.broadcast_to(flat, (parts, row_block, fill)),
        ],
        axis=-1,
    )
    lane_got = trade(lane_sent)
    by_stream = jnp.sum(lane_got.reshape(streams, lanes, row_block, -1), axis=0)
    final_x = jnp.moveaxis(by_stream[..., :width], 0, 1).reshape(row_block, -1)
    final_bc = jnp.sum(by_stream[..., width:scan_width], axis=0)
    final_dt = jnp.moveaxis(by_stream[..., scan_width:shared_end], 0, 1)
    final_dt = jnp.sum(final_dt.reshape(row_block, head_total, shared), axis=-1)
    pieces = lane_got[..., shared_end:].reshape(parts, -1)
    by_small, at = [], 0
    for part in small:
        got = pieces[:, at : at + part.size].reshape((parts,) + part.shape)
        by_small.append(got)
        at += part.size

    def lane_cols(got):
        joined = jnp.sum(got.reshape((streams, lanes) + got.shape[1:]), axis=0)
        return jnp.moveaxis(joined, 0, -2).reshape(joined.shape[1:-1] + (-1,))

    def lane_heads(got):
        joined = jnp.sum(got.reshape(streams, lanes, -1), axis=0)
        return jnp.sum(joined.reshape(head_total, shared), axis=-1)

    small_sums = [
        jnp.concatenate([lane_cols(by_small[0]), jnp.sum(by_small[2], axis=0)], axis=-1),
        jnp.concatenate([lane_cols(by_small[1]), jnp.sum(by_small[3], axis=0)], axis=-1),
        lane_heads(by_small[4]),
        lane_heads(by_small[5]),
        lane_heads(by_small[6]),
    ] + [jnp.sum(got, axis=0) for got in by_small[7:]]

    mlp_finals = []
    for blocks, got, turn in zip(mlp_blocks, mlp_got, (back_taken, patch_taken)):
        part = after(blocks[1], turn) + got
        part = part.reshape((2,) * (seq_bits() - 1) + (row_block, -1))
        for bit in range(3, seq_bits()):
            far, near = halve(part, seq_bits() - 1 - bit, bit)
            part = near + to_partner(far, bit)
        mine = part.reshape(QUAD, row_block, -1)
        mlp_finals.append(jnp.moveaxis(side_trade(mine), 0, 1))

    def final_cols(final, low, count):
        return final[..., low : low + count].reshape(row_block, -1)

    quarter = inner_width // QUAD
    final_down = final_cols(mlp_finals[0], 0, hidden_part)
    final_gate = final_cols(mlp_finals[0], hidden_part, hidden_part)
    final_up = final_cols(mlp_finals[1], 0, hidden_part)
    final_out = final_cols(mlp_finals[1], hidden_part, quarter)
    final_z = final_cols(mlp_finals[1], hidden_part + quarter, quarter)
    part = jnp.concatenate(
        [
            after(attn_blocks[first][1], back_taken)[0] + attn_got[first][0] + attn_crossed[first]
            for first in range(2)
        ],
        axis=-1,
    )
    part = part.reshape((2,) * (seq_bits() - 2) + (row_block, -1))
    for bit in range(2, seq_bits()):
        far, near = halve(part, part.ndim - 3, bit)
        part = near + to_partner(far, bit)
    final_attn = part
    patch_got = to_partner(patch_far, 1)
    final_patch = patch_grad(patch_cols, patch_got, bytes_all)
    norm_global_sum = (gain_side + patch_got[row_block:, : 2 * row_block]).reshape(-1)
    grad_vec = dot_plain(after(grad_patch, patch_far).astype(jnp.bfloat16), w_patch)
    grad_vec = grad_vec.reshape(streams, patch_count, feature, 8)
    grad_own = jnp.swapaxes(grad_vec, 2, 3).reshape(streams, local_rows, feature)
    grad_rows = lax.dynamic_slice_in_dim(
        grad_stream.reshape(streams, local_rows, model_width), tp_index * feature, feature, 2
    )
    grad_bytes = grad_rows + grad_own

    qkv_cols, o_cols = w_qkv.shape[1], w_o.shape[1]
    return (
        logits.reshape(streams, local_rows, head_cols),
        grad_bytes,
        final_patch,
        norm_global_sum,
        jnp.concatenate([final_z, final_x, final_bc, final_dt], axis=1),
        small_sums[0],
        small_sums[1],
        small_sums[2],
        small_sums[3],
        small_sums[4],
        small_sums[5],
        final_out,
        small_sums[6],
        final_attn[:, :qkv_cols],
        final_attn[:, qkv_cols : qkv_cols + o_cols],
        small_sums[7],
        final_gate,
        final_up,
        final_down,
        final_attn[:, qkv_cols + o_cols :],
    )


def solution(mesh):
    in_specs = (
        P(None, "seq", None),
        P(),
        P(None, "tp"),
        P(),
        P(None, "tp"),
        P(None, "tp"),
        P("tp"),
        P("tp"),
        P("tp"),
        P("tp"),
        P("tp"),
        P(None, "tp"),
        P(),
        P(None, "tp"),
        P(None, "tp"),
        P(),
        P(None, "tp"),
        P(None, "tp"),
        P(None, "tp"),
        P(None, "tp"),
        P(None, "seq", "tp"),
    )
    out_specs = (
        P(None, "seq", "tp"),
        P(None, "seq", "tp"),
        P("seq", "tp"),
        P(),
        P("seq", "tp"),
        P(None, "tp"),
        P("tp"),
        P("tp"),
        P("tp"),
        P("tp"),
        P("tp"),
        P("seq", "tp"),
        P(),
        P("seq", "tp"),
        P("seq", "tp"),
        P(),
        P("seq", "tp"),
        P("seq", "tp"),
        P("seq", "tp"),
        P("seq", "tp"),
    )
    return jax.shard_map(body, mesh=mesh, in_specs=in_specs, out_specs=out_specs, check_vma=False)
```

```python
from functools import partial

import jax
import jax.numpy as jnp
from jax import lax
from jax.experimental import pallas as pl
from jax.experimental.pallas import tpu as pltpu
from jax.sharding import PartitionSpec as P

NS = 128
AD = 64
QUAD = 4


NO_COST = pl.CostEstimate(flops=1024, bytes_accessed=1024, transcendentals=0)
ROOMY = pltpu.CompilerParams(vmem_limit_bytes=56 * 1024 * 1024)

epsilon = 1e-05
highest = lax.Precision.HIGHEST
masked_score = -1e30


def dot_plain(left_side, right_side):
    return jnp.dot(left_side, right_side, preferred_element_type=jnp.float32)


def dot_trans(left_side, right_side):
    return lax.dot_general(
        left_side, right_side, (((1,), (1,)), ((), ())), preferred_element_type=jnp.float32
    )


def dot_left(left_side, right_side):
    return lax.dot_general(
        left_side, right_side, (((0,), (0,)), ((), ())), preferred_element_type=jnp.float32
    )


def rms_scale(values):
    return lax.rsqrt(jnp.mean(values * values, axis=-1, keepdims=True) + epsilon)


def hidden_parts(mlp_in, grad_hidden, w_gate, w_up):
    gate_proj = dot_plain(mlp_in, w_gate)
    up_proj = dot_plain(mlp_in, w_up)
    sigmoid_gate = jax.nn.sigmoid(gate_proj)
    hidden_low = (gate_proj * sigmoid_gate * up_proj).astype(jnp.bfloat16)
    grad_gate_low = (
        grad_hidden * up_proj * sigmoid_gate * (1.0 + gate_proj * (1.0 - sigmoid_gate))
    ).astype(jnp.bfloat16)
    grad_up_low = (grad_hidden * gate_proj * sigmoid_gate).astype(jnp.bfloat16)
    return (hidden_low, grad_gate_low, grad_up_low)


def rms_back(values, gain_values, grad_out):
    scale = rms_scale(values)
    scaled = gain_values * grad_out
    inner_mean = jnp.mean(values * scaled, axis=-1, keepdims=True)
    grad_values = scale * scaled - values * scale * scale * scale * inner_mean
    grad_gain = jnp.sum(values * scale * grad_out, axis=0)
    return (grad_values, grad_gain)


def swap(block, axis, mask):
    return lax.ppermute(block, axis, [(i, i ^ mask) for i in range(lax.axis_size(axis))])


def after(value, *earlier):
    return lax.optimization_barrier((value,) + earlier)[0]


def tp_sum(block):
    return block + swap(block, "tp", 1)


def to_partner(block, bit):
    return swap(block, "seq", 1 << bit)


def halve(part, axis, bit):
    mine = lax.axis_index("seq") >> bit & 1
    far = lax.dynamic_index_in_dim(part, 1 - mine, axis, keepdims=False)
    return far, lax.dynamic_index_in_dim(part, mine, axis, keepdims=False)


def seq_bits():
    return lax.axis_size("seq").bit_length() - 1


def side_trade(blocks):
    members = [
        [base | high << 2 | low for high in range(2) for low in range(2)]
        for base in range(lax.axis_size("seq"))
        if base & 5 == 0
    ]
    return lax.all_to_all(blocks, "seq", 0, 0, axis_index_groups=members, tiled=True)


def grad_blocks_kernel(pairs, first, relative, rows, member_ref, *refs):
    lefts, rights = refs[: len(pairs)], refs[len(pairs) : 2 * len(pairs)]
    far_ref, near_ref = refs[2 * len(pairs) :]
    other = 1 - first
    at = 0
    for left_ref, right_ref, (low, high) in zip(lefts, rights, pairs):
        got = dot_left(left_ref[...], right_ref[:, low:high].astype(jnp.bfloat16))
        places = slice(at, at + high - low)
        for block in range(got.shape[0] // rows):
            place, member = block // QUAD, block % QUAD
            part = got[block * rows : (block + 1) * rows]
            apart = member_ref[0] ^ member
            is_far = apart >> first & 1
            if relative:
                side = apart >> other & 1
            else:
                side = member >> other & 1

            @pl.when(is_far == 1)
            def _():
                if relative:
                    far_ref[side, place, :, places] = part
                else:
                    far_ref[place, side, :, places] = part

            @pl.when(is_far == 0)
            def _():
                if relative:
                    near_ref[side, place, :, places] = part
                else:
                    near_ref[place, side, :, places] = part

        at += high - low


def grad_blocks(terms, first, relative):
    parts = lax.axis_size("seq")
    groups = parts // QUAD
    model_width = terms[0][0].shape[1]
    rows = model_width // parts
    cols = max(128, QUAD * rows)
    places = cols // (QUAD * rows)
    pairs = [(low, high) for unused, unused_right, low, high in terms]
    total = sum(high - low for low, high in pairs)
    member = (lax.axis_index("seq") % QUAD).astype(jnp.int32).reshape(1)
    if relative:
        shape, block = (2, groups, rows, total), (2, places, rows, total)
        out_spec = pl.BlockSpec(block, lambda i, ref: (0, i, 0, 0))
    else:
        shape, block = (groups, 2, rows, total), (places, 2, rows, total)
        out_spec = pl.BlockSpec(block, lambda i, ref: (i, 0, 0, 0))
    out = jax.ShapeDtypeStruct(shape, jnp.float32)
    return pl.pallas_call(
        partial(grad_blocks_kernel, pairs, first, relative, rows),
        grid_spec=pltpu.PrefetchScalarGridSpec(
            num_scalar_prefetch=1,
            grid=(model_width // cols,),
            in_specs=[
                pl.BlockSpec((term[0].shape[0], cols), lambda i, ref: (0, i)) for term in terms
            ]
            + [pl.BlockSpec(term[1].shape, lambda i, ref: (0, 0)) for term in terms],
            out_specs=[out_spec, out_spec],
        ),
        out_shape=[out, out],
        compiler_params=ROOMY,
        cost_estimate=NO_COST,
    )(member, *[term[0] for term in terms], *[term[1] for term in terms])


def segment_ids(lengths, place_count):
    ends = jnp.cumsum(lengths // 8, dtype=jnp.int32)
    places = jnp.arange(place_count, dtype=jnp.int32)
    short_ids = jnp.sum(
        (places[:, None] >= ends[None, :]).astype(jnp.int32), axis=1, dtype=jnp.int32
    )
    return jnp.stack([jnp.zeros_like(short_ids), short_ids])


def scan_heads(seg_now, head_size, xbc, dt_raw, conv_weight, conv_bias, dt_shift, a_logs, skips):
    place_count = xbc.shape[0]
    conv_sum = conv_bias + conv_weight[3] * xbc
    for offset in range(3):
        distance = 3 - offset
        earlier = jnp.pad(xbc, ((distance, 0), (0, 0)))[:place_count]
        seg_earlier = jnp.pad(seg_now, (distance, 0), constant_values=-1)[:place_count]
        same_doc = (seg_earlier == seg_now).astype(jnp.float32)
        conv_sum = conv_sum + conv_weight[offset] * earlier * same_doc[:, None]
    active = jax.nn.silu(conv_sum)
    head_count = dt_raw.shape[1]
    inner = head_count * head_size
    values = active[:, :inner].reshape(place_count, head_count, head_size)
    in_keys = active[:, inner : inner + NS]
    out_keys = active[:, inner + NS :]
    step_sizes = jax.nn.softplus(dt_raw + dt_shift)
    decay_rates = -step_sizes * jnp.exp(a_logs)
    chunk = min(place_count, 512)
    triangle = jnp.tril(jnp.ones((chunk, chunk), jnp.float32))
    state = jnp.zeros((head_count, head_size, NS), jnp.float32)
    seg_last = jnp.int32(-1)
    outputs = []
    for start in range(0, place_count, chunk):
        stop = start + chunk
        x, b, c = values[start:stop], in_keys[start:stop], out_keys[start:stop]
        dt, seg = step_sizes[start:stop], seg_now[start:stop]
        cumulative = jnp.dot(triangle, decay_rates[start:stop], precision=highest)
        allowed = (triangle > 0.0) & (seg[:, None] == seg[None, :])
        ordered = cumulative.T
        gaps = ordered[:, :, None] - ordered[:, None, :]
        decays = jnp.where(allowed, jnp.exp(jnp.where(allowed, gaps, 0.0)), 0.0)
        crossing = jnp.einsum("pn,jn->pj", c, b, precision=highest)
        mixing = crossing[None] * decays * dt.T[:, None, :]
        result = jnp.einsum("hpj,jhd->phd", mixing, x, precision=highest)
        if start > 0:
            entering = jnp.exp(cumulative) * (seg == seg_last).astype(jnp.float32)[:, None]
            result = result + entering[..., None] * jnp.einsum(
                "pn,hdn->phd", c, state, precision=highest
            )
        if stop < place_count:
            last_same = (seg == seg[-1]).astype(jnp.float32)[:, None]
            weight = jnp.exp(cumulative[-1:] - cumulative) * last_same * dt
            through = jnp.exp(cumulative[-1]) * (seg[-1] == seg_last).astype(jnp.float32)
            state = through[:, None, None] * state + jnp.einsum(
                "jh,jhd,jn->hdn", weight, x, b, precision=highest
            )
            seg_last = seg[-1]
        outputs.append(result + skips[:, None] * x)
    return jnp.concatenate(outputs, axis=0).reshape(place_count, inner)


def gated_unit(result, gate_in):
    gated = result * jax.nn.silu(gate_in)
    return gated * rms_scale(gated)


def patch_far_kernel(grad_ref, gain_ref, bytes_ref, out_ref):
    half = grad_ref.shape[1] // 2
    grad_low = grad_ref[:, half:].astype(jnp.bfloat16)
    out_ref[:half] = dot_left(grad_low, bytes_ref[...].astype(jnp.bfloat16))
    out_ref[half:] = jnp.zeros((out_ref.shape[0] - half, out_ref.shape[1]), jnp.float32)

    @pl.when(pl.program_id(0) == 0)
    def _():
        out_ref[half:, : 2 * half] = gain_ref[...]


def patch_far_grad(grad_rows, gain_part, bytes_all):
    places, cols = grad_rows.shape
    total = bytes_all.shape[1]
    rows = cols // 2 + gain_part.shape[0]
    block = 1024
    return pl.pallas_call(
        patch_far_kernel,
        grid=(total // block,),
        in_specs=[
            pl.BlockSpec((places, cols), lambda i: (0, 0)),
            pl.BlockSpec(gain_part.shape, lambda i: (0, 0)),
            pl.BlockSpec((places, block), lambda i: (0, i)),
        ],
        out_specs=pl.BlockSpec((rows, block), lambda i: (0, i)),
        out_shape=jax.ShapeDtypeStruct((rows, total), jnp.float32),
        compiler_params=ROOMY,
        cost_estimate=NO_COST,
    )(grad_rows, gain_part, bytes_all)


def patch_grad_kernel(grad_ref, *refs):
    byte_refs, got_refs, out_ref, order_ref = refs[:8], refs[8:16], refs[16], refs[17]
    width = byte_refs[0].shape[1]

    @pl.when(pl.program_id(0) == 0)
    def _():
        order_ref[...] = feature_order(width)

    grad_low = grad_ref[:, : grad_ref.shape[1] // 2].astype(jnp.bfloat16)
    wide = jnp.concatenate([ref[...].astype(jnp.bfloat16) for ref in byte_refs], axis=1)
    rows = grad_low.shape[1]
    grad = dot_left(grad_low, wide)
    grad = grad + jnp.concatenate([ref[:rows] for ref in got_refs], axis=1)
    high = grad.astype(jnp.bfloat16)
    rest = grad - high.astype(jnp.float32)
    mid = rest.astype(jnp.bfloat16)
    low = (rest - mid.astype(jnp.float32)).astype(jnp.bfloat16)
    order = order_ref[...]
    out_ref[...] = dot_plain(high, order) + (dot_plain(mid, order) + dot_plain(low, order))


def patch_grad(grad_rows, got, bytes_all):
    places, cols = grad_rows.shape
    feature = bytes_all.shape[1] // 8
    chunk = 128
    steps = feature // chunk

    def byte_specs(rows):
        return [
            pl.BlockSpec((rows, chunk), partial(lambda j, i: (0, j * steps + i), j))
            for j in range(8)
        ]

    return pl.pallas_call(
        patch_grad_kernel,
        grid=(steps,),
        in_specs=[pl.BlockSpec((places, cols), lambda i: (0, 0))]
        + byte_specs(places)
        + byte_specs(got.shape[0]),
        out_specs=pl.BlockSpec((cols // 2, 8 * chunk), lambda i: (0, i)),
        out_shape=jax.ShapeDtypeStruct((cols // 2, 8 * feature), jnp.float32),
        scratch_shapes=[pltpu.VMEM((8 * chunk, 8 * chunk), jnp.bfloat16)],
        compiler_params=ROOMY,
        cost_estimate=NO_COST,
    )(grad_rows, *([bytes_all] * 8), *([got] * 8))


def trade(blocks):
    return lax.all_to_all(blocks, "seq", 0, 0, tiled=True)


def grid_iota(shape, axis):
    return lax.broadcasted_iota(jnp.int32, shape, axis)


def dot_fine(left_side, right_side, left_axis, right_axis):
    return lax.dot_general(
        left_side,
        right_side,
        (((left_axis,), (right_axis,)), ((), ())),
        preferred_element_type=jnp.float32,
        precision=highest,
    )


def shifted_down(block, distance):
    rows = grid_iota(block.shape, 0)
    return jnp.where(rows >= distance, pltpu.roll(block, distance, 0), 0.0)


def shifted_up(block, distance):
    count = block.shape[0]
    rows = grid_iota(block.shape, 0)
    return jnp.where(rows < count - distance, pltpu.roll(block, count - distance, 0), 0.0)


def scan_terms(taken_ref, same_ref, conv_ref, head_ref):
    places = taken_ref.shape[0]
    channels = conv_ref.shape[1]
    xbc = taken_ref[:, :channels]
    conv_sum = conv_ref[4:5] + conv_ref[3:4] * xbc
    for k in range(3):
        earlier = shifted_down(xbc, 3 - k) * same_ref[:, k : k + 1]
        conv_sum = conv_sum + conv_ref[k : k + 1] * earlier
    gate = jax.nn.sigmoid(conv_sum)
    active = conv_sum * gate
    raw = taken_ref[:, channels:] + head_ref[0:1]
    steps = jnp.maximum(raw, 0.0) + jnp.log1p(jnp.exp(-jnp.abs(raw)))
    rates = -steps * jnp.exp(head_ref[1:2])
    square = (places, places)
    triangle = jnp.where(grid_iota(square, 0) >= grid_iota(square, 1), 1.0, 0.0)
    running = dot_fine(triangle, rates, 1, 0)
    return xbc, conv_sum, gate, active, raw, steps, rates, triangle, running


def scan_forward_kernel(taken_ref, same_ref, conv_ref, head_ref, seg_col, seg_row, out_ref):
    places, width = out_ref.shape
    terms = scan_terms(taken_ref, same_ref, conv_ref, head_ref)
    active, steps, running = terms[3], terms[5], terms[8]
    values = active[:, :width]
    keys, reads = active[:, width : width + NS], active[:, width + NS :]
    steps_row, running_row = steps.T, running.T
    heads = width // 64
    rows = 128
    for first in range(0, places, rows):
        last = first + rows
        shape = (rows, last)
        allowed = (seg_col[first:last] == seg_row[:, :last]) & (
            grid_iota(shape, 0) + first >= grid_iota(shape, 1)
        )
        crossing = dot_fine(reads[first:last], keys[:last], 1, 1)
        lane = grid_iota((rows, width), 1) // 64
        total = head_ref[2:3] * values[first:last]
        for h in range(heads):
            gaps = running[first:last, h : h + 1] - running_row[h : h + 1, :last]
            decays = jnp.exp(jnp.where(allowed, gaps, masked_score))
            mixing = crossing * decays * steps_row[h : h + 1, :last]
            part = dot_fine(mixing, values[:last], 1, 0)
            total = total + jnp.where(lane == h, part, 0.0)
        out_ref[first:last] = total


def scan_backward_kernel(
    taken_ref,
    same_ref,
    conv_ref,
    head_ref,
    seg_col,
    seg_row,
    grad_ref,
    out_ref,
    conv_grad_ref,
    head_grad_ref,
    values_grad,
    keys_grad,
    reads_grad,
    rows_grad,
    cols_grad,
):
    places, width = values_grad.shape
    terms = scan_terms(taken_ref, same_ref, conv_ref, head_ref)
    xbc, conv_sum, gate, active, raw, steps, rates, triangle, running = terms
    channels = xbc.shape[1]
    values = active[:, :width]
    keys, reads = active[:, width : width + NS], active[:, width + NS :]
    steps_row, running_row = steps.T, running.T
    heads = width // 64
    rows = 128
    grad = grad_ref[...]
    values_grad[...] = head_ref[2:3] * grad
    keys_grad[...] = jnp.zeros_like(keys_grad)
    rows_grad[...] = jnp.zeros_like(rows_grad)
    cols_grad[...] = jnp.zeros_like(cols_grad)
    for first in range(0, places, rows):
        last = first + rows
        shape = (rows, last)
        allowed = (seg_col[first:last] == seg_row[:, :last]) & (
            grid_iota(shape, 0) + first >= grid_iota(shape, 1)
        )
        crossing = dot_fine(reads[first:last], keys[:last], 1, 1)
        crossing_grad = jnp.zeros(shape, jnp.float32)
        grad_rows = grad[first:last]
        lane = grid_iota((rows, width), 1) // 64
        wide_lane = grid_iota((last, width), 1) // 64
        column = grid_iota((rows, 128), 1)
        down = jnp.zeros((rows, 128), jnp.float32)
        for h in range(heads):
            gaps = running[first:last, h : h + 1] - running_row[h : h + 1, :last]
            decays = jnp.exp(jnp.where(allowed, gaps, masked_score))
            step_row = steps_row[h : h + 1, :last]
            weighted = decays * step_row
            mixing = crossing * weighted
            own_grad = jnp.where(lane == h, grad_rows, 0.0)
            mixing_grad = dot_fine(own_grad, values[:last], 1, 1)
            back = dot_fine(mixing, own_grad, 0, 0)
            values_grad[:last] += jnp.where(wide_lane == h, back, 0.0)
            crossing_grad = crossing_grad + mixing_grad * weighted
            step_part = jnp.sum(mixing_grad * crossing * decays, axis=0, keepdims=True)
            gap_part = mixing_grad * mixing
            down = jnp.where(column == h, jnp.sum(gap_part, axis=1, keepdims=True), down)
            cols_grad[h : h + 1, :last] += step_part
            cols_grad[heads + h : heads + h + 1, :last] += step_part * step_row
        rows_grad[first:last] += down
        reads_grad[first:last] = dot_fine(crossing_grad, keys[:last], 1, 0)
        keys_grad[:last] += dot_fine(crossing_grad, reads[first:last], 0, 0)
    turned = cols_grad[...].T
    column = grid_iota(turned.shape, 1)
    step_grad = jnp.where(column < heads, turned, 0.0)
    ended = pltpu.roll(turned, turned.shape[1] - heads, 1)
    running_grad = jnp.where(column < heads, rows_grad[...] - ended, 0.0)
    rates_grad = dot_fine(triangle, running_grad, 0, 0)
    step_grad = step_grad - rates_grad * jnp.exp(head_ref[1:2])
    raw_grad = step_grad * jax.nn.sigmoid(raw)
    out_ref[:, channels:] = raw_grad
    lane = grid_iota((places, width), 1) // 64
    product = jnp.sum(grad * values, axis=0, keepdims=True)
    head_grad_ref[...] = jnp.zeros_like(head_grad_ref)
    head_grad_ref[0:1] = jnp.sum(raw_grad, axis=0, keepdims=True)
    head_grad_ref[1:2] = jnp.sum(rates_grad * rates, axis=0, keepdims=True)
    skip_lane = grid_iota((1, width), 1)
    skip_grad = jnp.zeros((1, width), jnp.float32)
    for h in range(heads):
        own = jnp.sum(jnp.where(skip_lane // 64 == h, product, 0.0), axis=1, keepdims=True)
        skip_grad = jnp.where(skip_lane == h, own, skip_grad)
    head_grad_ref[2:3] = skip_grad
    active_grad = jnp.concatenate([values_grad[...], keys_grad[...], reads_grad[...]], axis=1)
    conv_grad = active_grad * gate * (1.0 + conv_sum * (1.0 - gate))
    back = conv_ref[3:4] * conv_grad
    conv_grad_ref[...] = jnp.zeros_like(conv_grad_ref)
    conv_grad_ref[3:4] = jnp.sum(conv_grad * xbc, axis=0, keepdims=True)
    conv_grad_ref[4:5] = jnp.sum(conv_grad, axis=0, keepdims=True)
    for k in range(3):
        kept = conv_grad * same_ref[:, k : k + 1]
        back = back + conv_ref[k : k + 1] * shifted_up(kept, 3 - k)
        conv_grad_ref[k : k + 1] = jnp.sum(
            kept * shifted_down(xbc, 3 - k), axis=0, keepdims=True
        )
    out_ref[:, :channels] = back


def scan_forward(args, width):
    places = args[0].shape[0]
    return pl.pallas_call(
        scan_forward_kernel,
        out_shape=jax.ShapeDtypeStruct((places, width), jnp.float32),
        compiler_params=ROOMY,
        cost_estimate=NO_COST,
    )(*args)


def scan_backward(args, grad):
    places, width = grad.shape
    channels = args[2].shape[1]
    f32 = jnp.float32
    return pl.pallas_call(
        scan_backward_kernel,
        out_shape=[
            jax.ShapeDtypeStruct((places, channels + 128), f32),
            jax.ShapeDtypeStruct((8, channels), f32),
            jax.ShapeDtypeStruct((8, 128), f32),
        ],
        scratch_shapes=[
            pltpu.VMEM((places, width), f32),
            pltpu.VMEM((places, NS), f32),
            pltpu.VMEM((places, NS), f32),
            pltpu.VMEM((places, 128), f32),
            pltpu.VMEM((128, places), f32),
        ],
        compiler_params=ROOMY,
        cost_estimate=NO_COST,
    )(*args, grad)


def patch_lanes(block):
    shape = (block // 8, 8, block)
    return grid_iota(shape, 0) == grid_iota(shape, 2) // 8


def folded(scores, same_patch):
    split = scores.reshape(same_patch.shape)
    return jnp.sum(jnp.where(same_patch, split, 0.0), axis=0)


def unfolded(rows, same_patch):
    spread = jnp.where(same_patch, rows[None], 0.0)
    return spread.reshape(-1, rows.shape[1]).astype(jnp.bfloat16)


def softmax_rows(scores, causal):
    scores = jnp.where(causal, scores, masked_score)
    top = jnp.max(scores, axis=1, keepdims=True)
    powers = jnp.exp(scores - top)
    return powers / jnp.sum(powers, axis=1, keepdims=True)


def head_places(rows, head_cols, block):
    return [
        (slice(first, first + block), [j * head_cols + pair * 128 for j in range(3)])
        for first in range(0, rows, block)
        for pair in range(head_cols // 128)
    ]


def all_scores(qkv_ref, places, lane, same_patch):
    scores = []
    for rows, (query, key, unused) in places:
        queries = qkv_ref[rows, query : query + 128] * 0.125
        keys = qkv_ref[rows, key : key + 128]
        for h in range(2):
            own = jnp.where(lane == h, queries, 0)
            scores.append(folded(dot_trans(keys, own), same_patch))
    return jnp.stack(scores)


def attn_forward_kernel(
    bytes_ref, patch_ref, gain_ref, qkv_w_ref, o_w_ref, x_ref, a_ref, qkv_ref, o_ref, out_ref
):
    rows = bytes_ref.shape[0]
    spread = jnp.broadcast_to(patch_ref[...][:, None], (rows // 8, 8, patch_ref.shape[1]))
    x = bytes_ref[...].astype(jnp.float32) + spread.reshape(bytes_ref.shape)
    x_ref[...] = x
    attn_in = (x * rms_scale(x) * gain_ref[...]).astype(jnp.bfloat16)
    a_ref[...] = attn_in
    qkv_ref[...] = dot_plain(attn_in, qkv_w_ref[...]).astype(jnp.bfloat16)
    head_cols = o_ref.shape[1]
    block = 128
    same_patch = patch_lanes(block)
    causal = grid_iota((8, block), 0) <= grid_iota((8, block), 1) % 8
    lane = grid_iota((block, 128), 1) // AD
    places = head_places(rows, head_cols, block)
    probs = softmax_rows(all_scores(qkv_ref, places, lane, same_patch), causal)
    for at, (row_place, (query, unused, value)) in enumerate(places):
        values = qkv_ref[row_place, value : value + 128]
        parts = [dot_left(unfolded(probs[2 * at + h], same_patch), values) for h in range(2)]
        total = jnp.where(lane == 0, parts[0], parts[1])
        o_ref[row_place, query : query + 128] = total.astype(jnp.bfloat16)
    out_ref[...] = dot_trans(o_ref[...], o_w_ref[...])


def attn_forward(bytes_rows, patch_rows, gain, w_qkv, w_o):
    rows, width = bytes_rows.shape
    block = 256
    cols, head_cols = w_qkv.shape[1], w_o.shape[1]
    f32, bf16 = jnp.float32, jnp.bfloat16

    def by_rows(cols):
        return pl.BlockSpec((block, cols), lambda i: (i, 0))

    def whole(shape):
        return pl.BlockSpec(shape, lambda i: (0, 0))

    return pl.pallas_call(
        attn_forward_kernel,
        grid=(rows // block,),
        in_specs=[
            by_rows(width),
            pl.BlockSpec((block // 8, width), lambda i: (i, 0)),
            whole((1, width)),
            whole(w_qkv.shape),
            whole(w_o.shape),
        ],
        out_specs=[by_rows(width), by_rows(width), by_rows(cols), by_rows(head_cols), by_rows(width)],
        out_shape=[
            jax.ShapeDtypeStruct((rows, width), f32),
            jax.ShapeDtypeStruct((rows, width), bf16),
            jax.ShapeDtypeStruct((rows, cols), bf16),
            jax.ShapeDtypeStruct((rows, head_cols), bf16),
            jax.ShapeDtypeStruct((rows, width), f32),
        ],
        compiler_params=ROOMY,
        cost_estimate=NO_COST,
    )(bytes_rows, patch_rows, gain.reshape(1, width), w_qkv, w_o)


def attn_backward_kernel(
    x_ref,
    final_ref,
    own_ref,
    other_ref,
    gain_ref,
    qkv_ref,
    qkv_w_ref,
    o_w_ref,
    mid_ref,
    low_ref,
    qkv_grad_ref,
    out_ref,
    gain_grad_ref,
):
    rows = x_ref.shape[0]
    back, gain_grad = rms_back(x_ref[...], gain_ref[...], own_ref[...] + other_ref[...])
    mid = final_ref[...] + back
    mid_ref[...] = mid
    low_ref[...] = mid.astype(jnp.bfloat16)
    gain_grad = gain_grad.reshape(1, -1)

    @pl.when(pl.program_id(0) == 0)
    def _():
        gain_grad_ref[...] = gain_grad

    @pl.when(pl.program_id(0) > 0)
    def _():
        gain_grad_ref[...] += gain_grad

    mixed_grad = dot_plain(low_ref[...], o_w_ref[...]).astype(jnp.bfloat16)
    head_cols = mixed_grad.shape[1]
    block = 128
    same_patch = patch_lanes(block)
    causal = grid_iota((8, block), 0) <= grid_iota((8, block), 1) % 8
    lane = grid_iota((block, 128), 1) // AD
    places = head_places(rows, head_cols, block)
    probs = softmax_rows(all_scores(qkv_ref, places, lane, same_patch), causal)
    probs_grads = []
    for row_place, (query, unused, value) in places:
        values = qkv_ref[row_place, value : value + 128]
        out_grad = mixed_grad[row_place, query : query + 128]
        for h in range(2):
            own_grad = jnp.where(lane == h, out_grad, 0)
            probs_grads.append(folded(dot_trans(values, own_grad), same_patch))
    probs_grad = jnp.stack(probs_grads)
    inner = jnp.sum(probs * probs_grad, axis=1, keepdims=True)
    scores_grad = probs * (probs_grad - inner)
    for at, (row_place, cols) in enumerate(places):
        query, key, unused = cols
        queries = qkv_ref[row_place, query : query + 128]
        keys = qkv_ref[row_place, key : key + 128]
        out_grad = mixed_grad[row_place, query : query + 128]
        parts = []
        for h in range(2):
            own_scores = unfolded(scores_grad[2 * at + h], same_patch)
            parts.append(
                (
                    dot_left(own_scores, keys) * 0.125,
                    dot_plain(own_scores, queries) * 0.125,
                    dot_plain(unfolded(probs[2 * at + h], same_patch), out_grad),
                )
            )
        for j in range(3):
            grad = jnp.where(lane == 0, parts[0][j], parts[1][j])
            qkv_grad_ref[row_place, cols[j] : cols[j] + 128] = grad.astype(jnp.bfloat16)
    out_ref[...] = dot_trans(qkv_grad_ref[...], qkv_w_ref[...])


def attn_backward(x_rows, final_grad, own_part, other_part, gain, qkv, w_qkv, w_o):
    rows, width = x_rows.shape
    block = 256
    cols = w_qkv.shape[1]
    f32, bf16 = jnp.float32, jnp.bfloat16

    def by_rows(cols):
        return pl.BlockSpec((block, cols), lambda i: (i, 0))

    def whole(shape):
        return pl.BlockSpec(shape, lambda i: (0, 0))

    return pl.pallas_call(
        attn_backward_kernel,
        grid=(rows // block,),
        in_specs=[by_rows(width)] * 4
        + [whole((1, width)), by_rows(cols), whole(w_qkv.shape), whole(w_o.shape)],
        out_specs=[
            by_rows(width),
            by_rows(width),
            by_rows(cols),
            by_rows(width),
            whole((1, width)),
        ],
        out_shape=[
            jax.ShapeDtypeStruct((rows, width), f32),
            jax.ShapeDtypeStruct((rows, width), bf16),
            jax.ShapeDtypeStruct((rows, cols), bf16),
            jax.ShapeDtypeStruct((rows, width), f32),
            jax.ShapeDtypeStruct((1, width), f32),
        ],
        compiler_params=ROOMY,
        cost_estimate=NO_COST,
    )(x_rows, final_grad, own_part, other_part, gain.reshape(1, width), qkv, w_qkv, w_o)


def mlp_in_kernel(core_ref, x_ref, own_ref, other_ref, gain_ref, out_ref, low_ref, half_ref):
    x = x_ref[...] + (own_ref[...] + other_ref[...])
    out_ref[...] = x
    unit = x * rms_scale(x)
    low_ref[...] = (unit * gain_ref[...]).astype(jnp.bfloat16)
    width = half_ref.shape[1]
    half_ref[...] = jnp.where(core_ref[0] == 0, unit[:, :width], unit[:, width:])


def mlp_in(x_rows, own_part, other_part, gain):
    rows, width = x_rows.shape
    block = 128
    core = lax.axis_index("tp").astype(jnp.int32).reshape(1)

    def by_rows(cols):
        return pl.BlockSpec((block, cols), lambda i, ref: (i, 0))

    return pl.pallas_call(
        mlp_in_kernel,
        grid_spec=pltpu.PrefetchScalarGridSpec(
            num_scalar_prefetch=1,
            grid=(rows // block,),
            in_specs=[by_rows(width)] * 3 + [pl.BlockSpec((1, width), lambda i, ref: (0, 0))],
            out_specs=[by_rows(width), by_rows(width), by_rows(width // 2)],
        ),
        out_shape=[
            jax.ShapeDtypeStruct((rows, width), jnp.float32),
            jax.ShapeDtypeStruct((rows, width), jnp.bfloat16),
            jax.ShapeDtypeStruct((rows, width // 2), jnp.float32),
        ],
        compiler_params=ROOMY,
        cost_estimate=NO_COST,
    )(core, x_rows, own_part, other_part, gain.reshape(1, width))


def mlp_kernel(
    in_ref, grad_ref, gate_w_ref, up_w_ref, hidden_ref, gate_ref, up_ref, out_ref, total_ref
):
    hidden, gate, up = hidden_parts(
        in_ref[...], grad_ref[...], gate_w_ref[...], up_w_ref[...]
    )
    hidden_ref[...] = hidden
    gate_ref[...] = gate
    up_ref[...] = up
    part = dot_trans(gate, gate_w_ref[...]) + dot_trans(up, up_w_ref[...])
    step = pl.program_id(0)

    @pl.when(step == 0)
    def _():
        total_ref[...] = part

    @pl.when(step > 0)
    def _():
        total_ref[...] += part

    @pl.when(step == pl.num_programs(0) - 1)
    def _():
        out_ref[...] = total_ref[...]


def mlp_rows(mlp_low, grad_hidden, w_gate, w_up):
    rows, width = mlp_low.shape
    units = w_gate.shape[1]
    block = 512
    by_units = pl.BlockSpec((rows, block), lambda i: (0, i))
    by_weights = pl.BlockSpec((width, block), lambda i: (0, i))
    whole = pl.BlockSpec((rows, width), lambda i: (0, 0))
    low = jax.ShapeDtypeStruct((rows, units), jnp.bfloat16)
    return pl.pallas_call(
        mlp_kernel,
        grid=(units // block,),
        in_specs=[whole, by_units, by_weights, by_weights],
        out_specs=[by_units, by_units, by_units, whole],
        out_shape=[low, low, low, jax.ShapeDtypeStruct((rows, width), jnp.float32)],
        scratch_shapes=[pltpu.VMEM((rows, width), jnp.float32)],
        compiler_params=ROOMY,
        cost_estimate=NO_COST,
    )(mlp_low, grad_hidden, w_gate, w_up)


def feature_order(width):
    shape = (8 * width, 8 * width)
    row, col = grid_iota(shape, 0), grid_iota(shape, 1)
    return jnp.where(row == (col % 8) * width + col // 8, 1.0, 0.0).astype(jnp.bfloat16)


def patch_in_kernel(core_ref, bytes_ref, weight_ref, wide_ref, out_ref, rows_ref, order_ref):
    places, feature = wide_ref.shape[0], wide_ref.shape[1] // 8
    chunk = weight_ref.shape[1] // 8
    step = pl.program_id(0)

    @pl.when(step == 0)
    def _():
        order_ref[...] = feature_order(chunk)
        for at in range(feature // 128):
            low = at * 128
            rows_ref[at] = bytes_ref[:, low : low + 128].astype(jnp.float32)
            for j in range(8):
                wide_ref[:, j * feature + low : j * feature + low + 128] = rows_ref[
                    at, pl.ds(j, places, stride=8), :
                ]

    parts = [
        wide_ref[:, pl.ds(pl.multiple_of(j * feature + step * chunk, 128), chunk)]
        for j in range(8)
    ]
    by_byte = jnp.concatenate(parts, axis=1).astype(jnp.bfloat16)
    by_feature = dot_plain(by_byte, order_ref[...]).astype(jnp.bfloat16)
    part = dot_trans(by_feature, weight_ref[...])

    @pl.when(step == 0)
    def _():
        out_ref[...] = part

    @pl.when(step > 0)
    def _():
        out_ref[...] += part


def patch_in(byte_rows, w_patch):
    rows, model_width = byte_rows.shape
    out_width, cols = w_patch.shape
    feature, chunk = cols // 8, 128
    core = lax.axis_index("tp").astype(jnp.int32).reshape(1)
    f32 = jnp.float32
    return pl.pallas_call(
        patch_in_kernel,
        grid_spec=pltpu.PrefetchScalarGridSpec(
            num_scalar_prefetch=1,
            grid=(feature // chunk,),
            in_specs=[
                pl.BlockSpec((rows, feature), lambda i, ref: (0, ref[0])),
                pl.BlockSpec((out_width, 8 * chunk), lambda i, ref: (0, i)),
            ],
            out_specs=[
                pl.BlockSpec((rows // 8, cols), lambda i, ref: (0, 0)),
                pl.BlockSpec((rows // 8, out_width), lambda i, ref: (0, 0)),
            ],
            scratch_shapes=[
                pltpu.VMEM((feature // 128, rows, 128), f32),
                pltpu.VMEM((8 * chunk, 8 * chunk), jnp.bfloat16),
            ],
        ),
        out_shape=[
            jax.ShapeDtypeStruct((rows // 8, cols), f32),
            jax.ShapeDtypeStruct((rows // 8, out_width), f32),
        ],
        compiler_params=ROOMY,
        cost_estimate=NO_COST,
    )(core, byte_rows, w_patch)


def final_part_kernel(raw_ref, mask_ref, head_ref, out_ref):
    low = (raw_ref[...] * mask_ref[...]).astype(jnp.bfloat16)
    out_ref[...] = dot_trans(low, head_ref[...])


def final_part(raw, mask, w_head):
    rows, cols = raw.shape
    block = 512
    return pl.pallas_call(
        final_part_kernel,
        grid=(rows // block,),
        in_specs=[
            pl.BlockSpec((block, cols), lambda i: (i, 0)),
            pl.BlockSpec((block, 1), lambda i: (i, 0)),
            pl.BlockSpec(w_head.shape, lambda i: (0, 0)),
        ],
        out_specs=pl.BlockSpec((block, w_head.shape[0]), lambda i: (i, 0)),
        out_shape=jax.ShapeDtypeStruct((rows, w_head.shape[0]), jnp.float32),
        compiler_params=ROOMY,
        cost_estimate=NO_COST,
    )(raw, mask, w_head)


def final_sum_kernel(
    member_ref, own_ref, other_ref, weight_ref, low_ref, hidden_ref, mine_ref, mine_low_ref
):
    total = own_ref[...] + other_ref[...]
    low = total.astype(jnp.bfloat16)
    low_ref[...] = low
    hidden_ref[...] = dot_plain(low, weight_ref[...])

    @pl.when(pl.program_id(0) == member_ref[0])
    def _():
        mine_ref[...] = total
        mine_low_ref[...] = low


def final_sum(own, other, w_down, member):
    rows, width = own.shape
    block = rows // QUAD
    units = w_down.shape[1] // QUAD
    f32, bf16 = jnp.float32, jnp.bfloat16

    def by_rows(cols):
        return pl.BlockSpec((block, cols), lambda i, ref: (i, 0))

    mine = pl.BlockSpec((block, width), lambda i, ref: (0, 0))
    return pl.pallas_call(
        final_sum_kernel,
        grid_spec=pltpu.PrefetchScalarGridSpec(
            num_scalar_prefetch=1,
            grid=(QUAD,),
            in_specs=[by_rows(width)] * 2
            + [pl.BlockSpec((width, units), lambda i, ref: (0, ref[0]))],
            out_specs=[by_rows(width), by_rows(units), mine, mine],
        ),
        out_shape=[
            jax.ShapeDtypeStruct((rows, width), bf16),
            jax.ShapeDtypeStruct((rows, units), f32),
            jax.ShapeDtypeStruct((block, width), f32),
            jax.ShapeDtypeStruct((block, width), bf16),
        ],
        compiler_params=ROOMY,
        cost_estimate=NO_COST,
    )(member, own, other, w_down)


def group_mlp_kernel(
    place_ref,
    own_ref,
    other_ref,
    gain_ref,
    grad_ref,
    gate_w_ref,
    up_w_ref,
    in_ref,
    hidden_ref,
    gate_ref,
    up_ref,
):
    own, other = own_ref[0], other_ref[0]
    first = place_ref[1] == 0
    halves = [jnp.where(first, own, other), jnp.where(first, other, own)]
    low = (jnp.concatenate(halves, axis=1) * gain_ref[...]).astype(jnp.bfloat16)
    in_ref[...] = low
    hidden, gate, up = hidden_parts(low, grad_ref[...], gate_w_ref[...], up_w_ref[...])
    hidden_ref[...] = hidden
    gate_ref[...] = gate
    up_ref[...] = up


def group_mlp(own_half, other_half, gain, grad_hidden, w_gate, w_up, member):
    unused, rows, half = own_half.shape
    width, units = 2 * half, w_gate.shape[1] // QUAD
    bf16 = jnp.bfloat16
    place = jnp.concatenate([member, lax.axis_index("tp").astype(jnp.int32).reshape(1)])

    def by_rows(cols):
        return pl.BlockSpec((rows, cols), lambda i, ref: (i, 0))

    halves = pl.BlockSpec((1, rows, half), lambda i, ref: (i, 0, 0))
    weights = pl.BlockSpec((width, units), lambda i, ref: (0, ref[0]))
    low = jax.ShapeDtypeStruct((QUAD * rows, units), bf16)
    return pl.pallas_call(
        group_mlp_kernel,
        grid_spec=pltpu.PrefetchScalarGridSpec(
            num_scalar_prefetch=1,
            grid=(QUAD,),
            in_specs=[
                halves,
                halves,
                pl.BlockSpec((1, width), lambda i, ref: (0, 0)),
                by_rows(units),
                weights,
                weights,
            ],
            out_specs=[by_rows(width), by_rows(units), by_rows(units), by_rows(units)],
        ),
        out_shape=[jax.ShapeDtypeStruct((QUAD * rows, width), bf16), low, low, low],
        compiler_params=ROOMY,
        cost_estimate=NO_COST,
    )(place, own_half, other_half, gain.reshape(1, width), grad_hidden, w_gate, w_up)


def body(
    byte_states,
    lengths,
    w_patch,
    norm_global,
    w_in,
    conv_w,
    conv_b,
    dt_bias,
    a_log,
    d_skip,
    mix_gain,
    w_out,
    norm_attn,
    w_qkv,
    w_o,
    norm_mlp,
    w_gate,
    w_up,
    w_down,
    w_head,
    d_logits,
):
    streams, local_rows, model_width = byte_states.shape
    patch_count = local_rows // 8
    patch_total = streams * patch_count
    row_total = streams * local_rows
    feature = w_patch.shape[1] // 8
    inner_width = w_out.shape[1]
    channels = conv_w.shape[1]
    head_total = dt_bias.shape[0]
    head_cols = w_head.shape[1]
    parts = lax.axis_size("seq")
    tp_index = lax.axis_index("tp")
    seq_index = lax.axis_index("seq")
    places = parts * patch_count
    f32 = jnp.float32

    lanes = parts // streams
    width = inner_width // lanes
    full_head = inner_width // head_total
    own_heads = max(1, width // full_head)
    shared = max(1, full_head // width)
    head_size = width // own_heads
    own_stream = seq_index // lanes
    first_col = (seq_index % lanes) * width
    first_head = first_col // full_head

    seg_full = segment_ids(lengths, places)
    seg_own = lax.dynamic_slice_in_dim(seg_full, seq_index * patch_count, patch_count, 1)
    seg_stream = lax.dynamic_index_in_dim(seg_full, own_stream, 0, keepdims=False)
    valid = (seg_own < lengths.shape[0]).astype(f32).reshape(patch_total, 1)
    byte_valid = jnp.repeat(valid, 8, axis=0)

    member = (seq_index >> 2 & 1) * 2 + (seq_index & 1)
    raw_logits = d_logits.reshape(row_total, head_cols)
    raw_wide = raw_logits.astype(f32)
    group_valid = []
    for high in range(2):
        for low in range(2):
            device = (seq_index & ~5) | high << 2 | low
            group_seg = lax.dynamic_slice_in_dim(
                seg_full, device * patch_count, patch_count, 1
            )
            group_valid.append((group_seg < lengths.shape[0]).astype(f32))
    group_valid = jnp.stack(group_valid).reshape(QUAD, patch_total, 1)
    group_bytes_valid = jnp.repeat(group_valid.reshape(-1, 1), 8, axis=0)
    group_raw = side_trade(jnp.broadcast_to(raw_wide[None], (QUAD,) + raw_wide.shape))
    place_index = member.astype(jnp.int32).reshape(1)
    bytes_wide, patch_part = patch_in(byte_states.reshape(row_total, model_width), w_patch)
    patch_out = tp_sum(patch_part)
    gain_global = norm_global.astype(f32)
    unit_patch = patch_out * rms_scale(patch_out)
    u_low = (unit_patch * gain_global).astype(jnp.bfloat16)
    half_width = model_width // 2
    proj = dot_plain(u_low, w_in).reshape(streams, patch_count, -1)
    gate_in = proj[..., :inner_width]
    xbc = proj[..., inner_width : inner_width + channels]
    dt_raw = proj[..., inner_width + channels :]

    def by_lane(columns):
        split = columns.reshape(streams, patch_count, lanes, -1)
        return jnp.moveaxis(split, 2, 1).reshape(parts, patch_count, -1)

    def from_lanes(blocks):
        split = blocks.reshape(streams, lanes, patch_count, -1)
        return jnp.moveaxis(split, 1, 2).reshape(streams, patch_count, -1)

    def to_all_lanes(columns):
        wide = jnp.broadcast_to(
            columns[:, None], (streams, lanes, patch_count, columns.shape[-1])
        )
        return wide.reshape(parts, patch_count, -1)

    pad_width = 128 - own_heads
    dt_lanes = by_lane(jnp.repeat(dt_raw, shared, axis=2))
    sent = jnp.concatenate(
        [
            by_lane(xbc[..., :inner_width]),
            to_all_lanes(xbc[..., inner_width:]),
            jnp.pad(dt_lanes, ((0, 0), (0, 0), (0, pad_width))),
        ],
        axis=-1,
    )
    taken = trade(sent)
    grad_logits = after(raw_logits, sent) * byte_valid.astype(jnp.bfloat16)
    group_part = final_part(
        after(group_raw, sent).reshape(-1, head_cols), group_bytes_valid, w_head
    )
    group_final, group_grad_hidden, grad_final, grad_mlp_low = final_sum(
        group_part, swap(group_part, "tp", 1), w_down, place_index
    )
    grad_hidden = dot_plain(grad_mlp_low, w_down)
    hidden_part = w_gate.shape[1] // QUAD

    row_side = [
        [device for device in range(parts) if (device >> 1 & 1) == side] for side in range(2)
    ]
    bytes_all = lax.all_gather(
        bytes_wide, "seq", axis=0, axis_index_groups=row_side, tiled=True
    )
    unit_patch_half = lax.dynamic_slice_in_dim(unit_patch, tp_index * half_width, half_width, 1)
    unit_own = lax.all_gather(after(unit_patch_half, bytes_wide), "seq", axis=0, tiled=True)
    unit_other = swap(unit_own, "tp", 1)
    taken = after(taken, grad_hidden, group_grad_hidden).reshape(places, -1)
    scan_width = width + channels - inner_width

    def own_cols(param):
        mine = lax.dynamic_slice_in_dim(param, first_col, width, param.ndim - 1)
        return jnp.concatenate([mine, param[..., inner_width:]], axis=-1).astype(f32)

    def own_head(param):
        return lax.dynamic_slice_in_dim(param, first_head, own_heads, 0).astype(f32)

    use_kernel = places == 512 and width == 128
    if use_kernel:
        padded_seg = jnp.pad(seg_stream, (3, 0), constant_values=-1)
        same = jnp.stack(
            [(padded_seg[k : k + places] == seg_stream).astype(f32) for k in range(3)]
            + [jnp.zeros((places,), f32)] * 5,
            axis=1,
        )
        conv_pack = jnp.concatenate(
            [own_cols(conv_w), own_cols(conv_b)[None], jnp.zeros((3, scan_width), f32)]
        )
        head_pack = jnp.stack(
            [jnp.pad(own_head(dt_bias), (0, 128 - own_heads))]
            + [jnp.pad(own_head(a_log), (0, 128 - own_heads))]
            + [jnp.repeat(own_head(d_skip), head_size)]
            + [jnp.zeros((128,), f32)] * 5
        )
        scan_args = (taken, same, conv_pack, head_pack, seg_stream[:, None], seg_stream[None])
        scanned = scan_forward(scan_args, width)
    else:
        scan_args = (
            taken[:, :scan_width],
            taken[:, scan_width : scan_width + own_heads],
            own_cols(conv_w),
            own_cols(conv_b),
            own_head(dt_bias),
            own_head(a_log),
            own_head(d_skip),
        )
        scanned, scan_back = jax.vjp(partial(scan_heads, seg_stream, head_size), *scan_args)
    result = from_lanes(trade(scanned.reshape(parts, patch_count, width)))
    unit_normed, norm_back = jax.vjp(gated_unit, result, gate_in)
    mix_scale = mix_gain.astype(f32)
    normed_low = (unit_normed * mix_scale).reshape(patch_total, -1).astype(jnp.bfloat16)

    def to_group(whole, quarters):
        split = quarters.reshape(patch_total, QUAD, inner_width // QUAD)
        wide = jnp.broadcast_to(whole[None], (QUAD,) + whole.shape)
        return side_trade(jnp.concatenate([wide, jnp.moveaxis(split, 1, 0)], axis=-1))

    group_got = to_group(unit_patch, unit_normed)
    group_u = (group_got[..., :model_width] * gain_global).astype(jnp.bfloat16)
    own_scale = lax.dynamic_slice_in_dim(
        mix_scale, member * (inner_width // QUAD), inner_width // QUAD, 0
    )
    group_n = (group_got[..., model_width:] * own_scale).astype(jnp.bfloat16)
    group_u = group_u.reshape(-1, model_width)
    group_n = group_n.reshape(-1, inner_width // QUAD)
    global_out = patch_out + valid * tp_sum(dot_trans(normed_low, w_out))
    gain_attn = norm_attn.astype(f32)
    gain_mlp = norm_mlp.astype(f32)
    stream_in, attn_in, qkv, mixed_low, attn_part = attn_forward(
        byte_states.reshape(row_total, model_width), global_out, gain_attn, w_qkv, w_o
    )
    attn_part = after(attn_part, group_got)
    after_attn, mlp_low, unit_half = mlp_in(
        stream_in, attn_part, swap(attn_part, "tp", 1), gain_mlp
    )
    hidden_low, grad_gate_low, grad_up_low, grad_mlp_part = mlp_rows(
        after(mlp_low, unit_half), grad_hidden, w_gate, w_up
    )
    group_halves = side_trade(jnp.broadcast_to(unit_half[None], (QUAD,) + unit_half.shape))
    grad_mlp_other = swap(grad_mlp_part, "tp", 1)
    after_mlp = after_attn + tp_sum(dot_trans(after(hidden_low, grad_mlp_part), w_down))
    final_low = after_mlp.astype(jnp.bfloat16)
    logits = dot_plain(final_low, w_head) * byte_valid
    grad_mid, grad_attn_low, grad_qkv_low, grad_attn_part, grad_norm_mlp = attn_backward(
        after_attn, grad_final, grad_mlp_part, grad_mlp_other, gain_mlp, qkv, w_qkv, w_o
    )
    grad_norm_mlp = grad_norm_mlp.reshape(-1)
    grad_attn_in = tp_sum(grad_attn_part)

    attn_cut = 1024 if grad_qkv_low.shape[1] > 1024 else 128
    attn_in_late = after(attn_in, grad_attn_part, group_halves)
    attn_cols = grad_qkv_low.shape[1]
    attn_blocks = (
        grad_blocks([(attn_in_late, grad_qkv_low, 0, attn_cut)], 0, True),
        grad_blocks(
            [
                (attn_in_late, grad_qkv_low, attn_cut, attn_cols),
                (grad_attn_low, mixed_low, 0, mixed_low.shape[1]),
                (final_low, grad_logits, 0, head_cols),
            ],
            1,
            True,
        ),
    )
    attn_got = [to_partner(attn_blocks[first][0], first) for first in range(2)]
    grad_attn_in = after(grad_attn_in, attn_blocks[0][0], attn_blocks[1][0])
    back_attn, grad_norm_attn = rms_back(stream_in, gain_attn, grad_attn_in)
    grad_stream = grad_mid + back_attn
    grad_global = jnp.sum(grad_stream.reshape(patch_total, 8, model_width), axis=1)
    grad_mix_low = (grad_global * valid).astype(jnp.bfloat16)
    grad_normed = dot_plain(grad_mix_low, w_out).reshape(streams, patch_count, inner_width)
    grad_mix_gain = jnp.sum(grad_normed * unit_normed, axis=(0, 1))
    grad_result, grad_gate_in = norm_back(grad_normed * mix_scale)
    grad_z_low = grad_gate_in.reshape(patch_total, inner_width).astype(jnp.bfloat16)
    row_block = model_width // parts
    dealing = by_lane(grad_result)
    dealt = trade(dealing)
    own_half = after(group_halves, dealing, bytes_all)
    group_in, group_hidden, group_gate, group_up = group_mlp(
        own_half, swap(own_half, "tp", 1), gain_mlp, group_grad_hidden, w_gate, w_up, place_index
    )
    late_got = to_group(after(grad_global, dealing), grad_gate_in)
    group_mix = (late_got[..., :model_width] * group_valid).astype(jnp.bfloat16)
    group_mix = group_mix.reshape(-1, model_width)
    group_z = late_got[..., model_width:].reshape(-1, inner_width // QUAD)
    mlp_blocks = [
        grad_blocks(
            [(group_final, group_hidden, 0, hidden_part), (group_in, group_gate, 0, hidden_part)],
            1,
            False,
        ),
        grad_blocks(
            [
                (group_in, group_up, 0, hidden_part),
                (group_mix, group_n, 0, group_n.shape[1]),
                (group_u, group_z, 0, group_z.shape[1]),
            ],
            1,
            False,
        ),
    ]
    mlp_got = [to_partner(far, 1) for far, unused in mlp_blocks]
    dealt = after(dealt, mlp_blocks[0][0], mlp_blocks[1][0], *attn_got)
    dealt = dealt.reshape(places, width)
    grad_scanned = dealt[:, :width]
    attn_far = [after(attn_blocks[first][1], dealt)[1] + attn_got[first][1] for first in range(2)]
    attn_crossed = [to_partner(attn_far[first], 1 - first) for first in range(2)]
    grad_scanned = after(grad_scanned, *attn_far)
    if use_kernel:
        back_sent, conv_grads, head_grads = scan_backward(scan_args, grad_scanned)
        lane_grad = back_sent[:, : scan_width + own_heads]
        scan_params = (
            conv_grads[:4],
            conv_grads[4],
            head_grads[0, :own_heads],
            head_grads[1, :own_heads],
            head_grads[2, :own_heads],
        )
    else:
        scan_grads = scan_back(grad_scanned)
        back_sent = jnp.concatenate(
            [scan_grads[0], jnp.pad(scan_grads[1], ((0, 0), (0, pad_width)))], axis=-1
        )
        lane_grad = jnp.concatenate([scan_grads[0], scan_grads[1]], axis=-1)
        scan_params = scan_grads[2:]
    back_sent = back_sent.reshape(parts, patch_count, -1)
    back_taken = after(trade(back_sent), mlp_got[0], unit_other, *attn_crossed)
    grad_x = from_lanes(back_taken[..., :width])
    by_stream = back_taken.reshape(streams, lanes, patch_count, -1)
    grad_bc = jnp.sum(by_stream[..., width:scan_width], axis=1)
    grad_dt = from_lanes(back_taken[..., scan_width : scan_width + own_heads])
    grad_dt = jnp.sum(grad_dt.reshape(streams, patch_count, head_total, shared), axis=-1)
    grad_shared = jnp.concatenate([grad_bc, grad_dt], axis=-1).reshape(patch_total, -1)
    grad_proj_low = jnp.concatenate(
        [grad_z_low, grad_x.reshape(patch_total, -1).astype(jnp.bfloat16)]
        + [grad_shared.astype(jnp.bfloat16)],
        axis=-1,
    )
    grad_u_part = dot_trans(grad_proj_low, w_in)
    grad_u = tp_sum(grad_u_part)
    back_global, grad_norm_global = rms_back(patch_out, gain_global, grad_u)
    grad_patch = grad_global + back_global

    side_count = parts // 2
    my_side = seq_index >> 1 & 1
    by_block = jnp.moveaxis(grad_patch.reshape(patch_total, parts, row_block), 1, 0)
    by_block = by_block.reshape(parts // 4, 2, 2, patch_total, row_block)
    same_side = lax.dynamic_index_in_dim(by_block, my_side, 1, keepdims=False)
    other_side = lax.dynamic_index_in_dim(by_block, 1 - my_side, 1, keepdims=False)
    patch_rows = jnp.concatenate([same_side, other_side], axis=-1)
    patch_rows = patch_rows.reshape(side_count, patch_total, 2 * row_block)
    gain_part = grad_norm_global.reshape(-1, 2 * row_block)
    gain_count = gain_part.shape[0]
    patch_sent = jnp.concatenate(
        [patch_rows, jnp.broadcast_to(gain_part, (side_count,) + gain_part.shape)], axis=1
    )
    patch_taken = lax.all_to_all(
        patch_sent, "seq", 0, 0, axis_index_groups=row_side, tiled=True
    )

    gain_side = jnp.sum(patch_taken[:, patch_total:], axis=0)
    patch_cols = patch_taken[:, :patch_total].reshape(-1, 2 * row_block)
    patch_far = patch_far_grad(patch_cols, gain_side, bytes_all)
    def stream_part(halves):
        split = halves.reshape(parts, streams, patch_count, half_width)
        mine = lax.dynamic_index_in_dim(split, own_stream, 1, keepdims=False)
        return after(mine, patch_far).reshape(places, half_width)

    own_cut, other_cut = stream_part(unit_own), stream_part(unit_other)
    unit_stream = jnp.concatenate(
        [
            jnp.where(tp_index == 0, own_cut, other_cut),
            jnp.where(tp_index == 0, other_cut, own_cut),
        ],
        axis=1,
    )
    u_stream = (unit_stream * gain_global).astype(jnp.bfloat16)
    scan_width_grads = lane_grad[:, :scan_width]
    lane_high = lane_grad.astype(jnp.bfloat16)
    shared_low = scan_width_grads[:, width:] - lane_high[:, width:scan_width].astype(f32)
    lane_product = dot_left(u_stream, lane_high)
    shared_rest = dot_left(u_stream, shared_low.astype(jnp.bfloat16))
    small = (
        scan_params[0][:, :width],
        scan_params[1][:width],
        scan_params[0][:, width:],
        scan_params[1][width:],
        scan_params[2],
        scan_params[3],
        scan_params[4],
        grad_mix_gain,
        grad_norm_attn,
        grad_norm_mlp,
    )
    small_count = sum(part.size for part in small)
    shared_end = scan_width + own_heads
    fill = -(-small_count // row_block)
    fill += -(shared_end + fill) % 128
    flat = jnp.concatenate([part.reshape(-1) for part in small])
    flat = jnp.pad(flat, (0, fill * row_block - small_count)).reshape(1, row_block, fill)
    lane_sent = jnp.concatenate(
        [
            lane_product[:, :width].reshape(parts, row_block, -1),
            (lane_product[:, width:scan_width] + shared_rest).reshape(parts, row_block, -1),
            lane_product[:, scan_width:].reshape(parts, row_block, -1),
            jnp.broadcast_to(flat, (parts, row_block, fill)),
        ],
        axis=-1,
    )
    lane_got = trade(lane_sent)
    by_stream = jnp.sum(lane_got.reshape(streams, lanes, row_block, -1), axis=0)
    final_x = jnp.moveaxis(by_stream[..., :width], 0, 1).reshape(row_block, -1)
    final_bc = jnp.sum(by_stream[..., width:scan_width], axis=0)
    final_dt = jnp.moveaxis(by_stream[..., scan_width:shared_end], 0, 1)
    final_dt = jnp.sum(final_dt.reshape(row_block, head_total, shared), axis=-1)
    pieces = lane_got[..., shared_end:].reshape(parts, -1)
    by_small, at = [], 0
    for part in small:
        got = pieces[:, at : at + part.size].reshape((parts,) + part.shape)
        by_small.append(got)
        at += part.size

    def lane_cols(got):
        joined = jnp.sum(got.reshape((streams, lanes) + got.shape[1:]), axis=0)
        return jnp.moveaxis(joined, 0, -2).reshape(joined.shape[1:-1] + (-1,))

    def lane_heads(got):
        joined = jnp.sum(got.reshape(streams, lanes, -1), axis=0)
        return jnp.sum(joined.reshape(head_total, shared), axis=-1)

    small_sums = [
        jnp.concatenate([lane_cols(by_small[0]), jnp.sum(by_small[2], axis=0)], axis=-1),
        jnp.concatenate([lane_cols(by_small[1]), jnp.sum(by_small[3], axis=0)], axis=-1),
        lane_heads(by_small[4]),
        lane_heads(by_small[5]),
        lane_heads(by_small[6]),
    ] + [jnp.sum(got, axis=0) for got in by_small[7:]]

    mlp_finals = []
    for blocks, got, turn in zip(mlp_blocks, mlp_got, (back_taken, patch_taken)):
        part = after(blocks[1], turn) + got
        part = part.reshape((2,) * (seq_bits() - 1) + (row_block, -1))
        for bit in range(3, seq_bits()):
            far, near = halve(part, seq_bits() - 1 - bit, bit)
            part = near + to_partner(far, bit)
        mine = part.reshape(QUAD, row_block, -1)
        mlp_finals.append(jnp.moveaxis(side_trade(mine), 0, 1))

    def final_cols(final, low, count):
        return final[..., low : low + count].reshape(row_block, -1)

    quarter = inner_width // QUAD
    final_down = final_cols(mlp_finals[0], 0, hidden_part)
    final_gate = final_cols(mlp_finals[0], hidden_part, hidden_part)
    final_up = final_cols(mlp_finals[1], 0, hidden_part)
    final_out = final_cols(mlp_finals[1], hidden_part, quarter)
    final_z = final_cols(mlp_finals[1], hidden_part + quarter, quarter)
    part = jnp.concatenate(
        [
            after(attn_blocks[first][1], back_taken)[0] + attn_got[first][0] + attn_crossed[first]
            for first in range(2)
        ],
        axis=-1,
    )
    part = part.reshape((2,) * (seq_bits() - 2) + (row_block, -1))
    for bit in range(2, seq_bits()):
        far, near = halve(part, part.ndim - 3, bit)
        part = near + to_partner(far, bit)
    final_attn = part
    patch_got = to_partner(patch_far, 1)
    final_patch = patch_grad(patch_cols, patch_got, bytes_all)
    norm_global_sum = (gain_side + patch_got[row_block:, : 2 * row_block]).reshape(-1)
    grad_vec = dot_plain(after(grad_patch, patch_far).astype(jnp.bfloat16), w_patch)
    grad_vec = grad_vec.reshape(streams, patch_count, feature, 8)
    grad_own = jnp.swapaxes(grad_vec, 2, 3).reshape(streams, local_rows, feature)
    grad_rows = lax.dynamic_slice_in_dim(
        grad_stream.reshape(streams, local_rows, model_width), tp_index * feature, feature, 2
    )
    grad_bytes = grad_rows + grad_own

    qkv_cols, o_cols = w_qkv.shape[1], w_o.shape[1]
    return (
        logits.reshape(streams, local_rows, head_cols),
        grad_bytes,
        final_patch,
        norm_global_sum,
        jnp.concatenate([final_z, final_x, final_bc, final_dt], axis=1),
        small_sums[0],
        small_sums[1],
        small_sums[2],
        small_sums[3],
        small_sums[4],
        small_sums[5],
        final_out,
        small_sums[6],
        final_attn[:, :qkv_cols],
        final_attn[:, qkv_cols : qkv_cols + o_cols],
        small_sums[7],
        final_gate,
        final_up,
        final_down,
        final_attn[:, qkv_cols + o_cols :],
    )


def solution(mesh):
    in_specs = (
        P(None, "seq", None),
        P(),
        P(None, "tp"),
        P(),
        P(None, "tp"),
        P(None, "tp"),
        P("tp"),
        P("tp"),
        P("tp"),
        P("tp"),
        P("tp"),
        P(None, "tp"),
        P(),
        P(None, "tp"),
        P(None, "tp"),
        P(),
        P(None, "tp"),
        P(None, "tp"),
        P(None, "tp"),
        P(None, "tp"),
        P(None, "seq", "tp"),
    )
    out_specs = (
        P(None, "seq", "tp"),
        P(None, "seq", "tp"),
        P("seq", "tp"),
        P(),
        P("seq", "tp"),
        P(None, "tp"),
        P("tp"),
        P("tp"),
        P("tp"),
        P("tp"),
        P("tp"),
        P("seq", "tp"),
        P(),
        P("seq", "tp"),
        P("seq", "tp"),
        P(),
        P("seq", "tp"),
        P("seq", "tp"),
        P("seq", "tp"),
        P("seq", "tp"),
    )
    return jax.shard_map(body, mesh=mesh, in_specs=in_specs, out_specs=out_specs, check_vma=False)
```

```python
from functools import partial

import jax
import jax.numpy as jnp
from jax import lax
from jax.experimental import pallas as pl
from jax.experimental.pallas import tpu as pltpu
from jax.sharding import PartitionSpec as P

NS = 128
AD = 64
QUAD = 4


NO_COST = pl.CostEstimate(flops=1024, bytes_accessed=1024, transcendentals=0)
ROOMY = pltpu.CompilerParams(vmem_limit_bytes=56 * 1024 * 1024)

epsilon = 1e-05
highest = lax.Precision.HIGHEST
masked_score = -1e30


def dot_plain(left_side, right_side):
    return jnp.dot(left_side, right_side, preferred_element_type=jnp.float32)


def dot_trans(left_side, right_side):
    return lax.dot_general(
        left_side, right_side, (((1,), (1,)), ((), ())), preferred_element_type=jnp.float32
    )


def dot_left(left_side, right_side):
    return lax.dot_general(
        left_side, right_side, (((0,), (0,)), ((), ())), preferred_element_type=jnp.float32
    )


def rms_scale(values):
    return lax.rsqrt(jnp.mean(values * values, axis=-1, keepdims=True) + epsilon)


def hidden_parts(mlp_in, grad_hidden, w_gate, w_up):
    gate_proj = dot_plain(mlp_in, w_gate)
    up_proj = dot_plain(mlp_in, w_up)
    sigmoid_gate = jax.nn.sigmoid(gate_proj)
    hidden_low = (gate_proj * sigmoid_gate * up_proj).astype(jnp.bfloat16)
    grad_gate_low = (
        grad_hidden * up_proj * sigmoid_gate * (1.0 + gate_proj * (1.0 - sigmoid_gate))
    ).astype(jnp.bfloat16)
    grad_up_low = (grad_hidden * gate_proj * sigmoid_gate).astype(jnp.bfloat16)
    return (hidden_low, grad_gate_low, grad_up_low)


def rms_back(values, gain_values, grad_out):
    scale = rms_scale(values)
    scaled = gain_values * grad_out
    inner_mean = jnp.mean(values * scaled, axis=-1, keepdims=True)
    grad_values = scale * scaled - values * scale * scale * scale * inner_mean
    grad_gain = jnp.sum(values * scale * grad_out, axis=0)
    return (grad_values, grad_gain)


def swap(block, axis, mask):
    return lax.ppermute(block, axis, [(i, i ^ mask) for i in range(lax.axis_size(axis))])


def after(value, *earlier):
    return lax.optimization_barrier((value,) + earlier)[0]


def tp_sum(block):
    return block + swap(block, "tp", 1)


def to_partner(block, bit):
    return swap(block, "seq", 1 << bit)


def halve(part, axis, bit):
    mine = lax.axis_index("seq") >> bit & 1
    far = lax.dynamic_index_in_dim(part, 1 - mine, axis, keepdims=False)
    return far, lax.dynamic_index_in_dim(part, mine, axis, keepdims=False)


def seq_bits():
    return lax.axis_size("seq").bit_length() - 1


def side_trade(blocks):
    members = [
        [base | high << 2 | low for high in range(2) for low in range(2)]
        for base in range(lax.axis_size("seq"))
        if base & 5 == 0
    ]
    return lax.all_to_all(blocks, "seq", 0, 0, axis_index_groups=members, tiled=True)


def high_trade(blocks):
    groups = lax.axis_size("seq") // QUAD
    members = [[low + QUAD * high for high in range(groups)] for low in range(QUAD)]
    return lax.all_to_all(blocks, "seq", 0, 0, axis_index_groups=members, tiled=True)


def grad_blocks_kernel(pairs, first, relative, rows, member_ref, *refs):
    lefts, rights = refs[: len(pairs)], refs[len(pairs) : 2 * len(pairs)]
    far_ref, near_ref = refs[2 * len(pairs) :]
    other = 1 - first
    at = 0
    for left_ref, right_ref, (low, high) in zip(lefts, rights, pairs):
        got = dot_left(left_ref[...], right_ref[:, low:high].astype(jnp.bfloat16))
        places = slice(at, at + high - low)
        for block in range(got.shape[0] // rows):
            place, member = block // QUAD, block % QUAD
            part = got[block * rows : (block + 1) * rows]
            apart = member_ref[0] ^ member
            is_far = apart >> first & 1
            if relative:
                side = apart >> other & 1
            else:
                side = member >> other & 1

            @pl.when(is_far == 1)
            def _():
                if relative:
                    far_ref[side, place, :, places] = part
                else:
                    far_ref[place, side, :, places] = part

            @pl.when(is_far == 0)
            def _():
                if relative:
                    near_ref[side, place, :, places] = part
                else:
                    near_ref[place, side, :, places] = part

        at += high - low


def grad_blocks(terms, first, relative):
    parts = lax.axis_size("seq")
    groups = parts // QUAD
    model_width = terms[0][0].shape[1]
    rows = model_width // parts
    cols = max(128, QUAD * rows)
    places = cols // (QUAD * rows)
    pairs = [(low, high) for unused, unused_right, low, high in terms]
    total = sum(high - low for low, high in pairs)
    member = (lax.axis_index("seq") % QUAD).astype(jnp.int32).reshape(1)
    if relative:
        shape, block = (2, groups, rows, total), (2, places, rows, total)
        out_spec = pl.BlockSpec(block, lambda i, ref: (0, i, 0, 0))
    else:
        shape, block = (groups, 2, rows, total), (places, 2, rows, total)
        out_spec = pl.BlockSpec(block, lambda i, ref: (i, 0, 0, 0))
    out = jax.ShapeDtypeStruct(shape, jnp.float32)
    return pl.pallas_call(
        partial(grad_blocks_kernel, pairs, first, relative, rows),
        grid_spec=pltpu.PrefetchScalarGridSpec(
            num_scalar_prefetch=1,
            grid=(model_width // cols,),
            in_specs=[
                pl.BlockSpec((term[0].shape[0], cols), lambda i, ref: (0, i)) for term in terms
            ]
            + [pl.BlockSpec(term[1].shape, lambda i, ref: (0, 0)) for term in terms],
            out_specs=[out_spec, out_spec],
        ),
        out_shape=[out, out],
        compiler_params=ROOMY,
        cost_estimate=NO_COST,
    )(member, *[term[0] for term in terms], *[term[1] for term in terms])


def segment_ids(lengths, place_count):
    ends = jnp.cumsum(lengths // 8, dtype=jnp.int32)
    places = jnp.arange(place_count, dtype=jnp.int32)
    short_ids = jnp.sum(
        (places[:, None] >= ends[None, :]).astype(jnp.int32), axis=1, dtype=jnp.int32
    )
    return jnp.stack([jnp.zeros_like(short_ids), short_ids])


def scan_heads(seg_now, head_size, xbc, dt_raw, conv_weight, conv_bias, dt_shift, a_logs, skips):
    place_count = xbc.shape[0]
    conv_sum = conv_bias + conv_weight[3] * xbc
    for offset in range(3):
        distance = 3 - offset
        earlier = jnp.pad(xbc, ((distance, 0), (0, 0)))[:place_count]
        seg_earlier = jnp.pad(seg_now, (distance, 0), constant_values=-1)[:place_count]
        same_doc = (seg_earlier == seg_now).astype(jnp.float32)
        conv_sum = conv_sum + conv_weight[offset] * earlier * same_doc[:, None]
    active = jax.nn.silu(conv_sum)
    head_count = dt_raw.shape[1]
    inner = head_count * head_size
    values = active[:, :inner].reshape(place_count, head_count, head_size)
    in_keys = active[:, inner : inner + NS]
    out_keys = active[:, inner + NS :]
    step_sizes = jax.nn.softplus(dt_raw + dt_shift)
    decay_rates = -step_sizes * jnp.exp(a_logs)
    chunk = min(place_count, 512)
    triangle = jnp.tril(jnp.ones((chunk, chunk), jnp.float32))
    state = jnp.zeros((head_count, head_size, NS), jnp.float32)
    seg_last = jnp.int32(-1)
    outputs = []
    for start in range(0, place_count, chunk):
        stop = start + chunk
        x, b, c = values[start:stop], in_keys[start:stop], out_keys[start:stop]
        dt, seg = step_sizes[start:stop], seg_now[start:stop]
        cumulative = jnp.dot(triangle, decay_rates[start:stop], precision=highest)
        allowed = (triangle > 0.0) & (seg[:, None] == seg[None, :])
        ordered = cumulative.T
        gaps = ordered[:, :, None] - ordered[:, None, :]
        decays = jnp.where(allowed, jnp.exp(jnp.where(allowed, gaps, 0.0)), 0.0)
        crossing = jnp.einsum("pn,jn->pj", c, b, precision=highest)
        mixing = crossing[None] * decays * dt.T[:, None, :]
        result = jnp.einsum("hpj,jhd->phd", mixing, x, precision=highest)
        if start > 0:
            entering = jnp.exp(cumulative) * (seg == seg_last).astype(jnp.float32)[:, None]
            result = result + entering[..., None] * jnp.einsum(
                "pn,hdn->phd", c, state, precision=highest
            )
        if stop < place_count:
            last_same = (seg == seg[-1]).astype(jnp.float32)[:, None]
            weight = jnp.exp(cumulative[-1:] - cumulative) * last_same * dt
            through = jnp.exp(cumulative[-1]) * (seg[-1] == seg_last).astype(jnp.float32)
            state = through[:, None, None] * state + jnp.einsum(
                "jh,jhd,jn->hdn", weight, x, b, precision=highest
            )
            seg_last = seg[-1]
        outputs.append(result + skips[:, None] * x)
    return jnp.concatenate(outputs, axis=0).reshape(place_count, inner)


def gated_unit(result, gate_in):
    gated = result * jax.nn.silu(gate_in)
    return gated * rms_scale(gated)


def patch_far_kernel(grad_ref, gain_ref, bytes_ref, out_ref):
    half = grad_ref.shape[1] // 2
    grad_low = grad_ref[:, half:].astype(jnp.bfloat16)
    out_ref[:half] = dot_left(grad_low, bytes_ref[...].astype(jnp.bfloat16))
    out_ref[half:] = jnp.zeros((out_ref.shape[0] - half, out_ref.shape[1]), jnp.float32)

    @pl.when(pl.program_id(0) == 0)
    def _():
        out_ref[half:, : 2 * half] = gain_ref[...]


def patch_far_grad(grad_rows, gain_part, bytes_all):
    places, cols = grad_rows.shape
    total = bytes_all.shape[1]
    rows = cols // 2 + gain_part.shape[0]
    block = 1024
    return pl.pallas_call(
        patch_far_kernel,
        grid=(total // block,),
        in_specs=[
            pl.BlockSpec((places, cols), lambda i: (0, 0)),
            pl.BlockSpec(gain_part.shape, lambda i: (0, 0)),
            pl.BlockSpec((places, block), lambda i: (0, i)),
        ],
        out_specs=pl.BlockSpec((rows, block), lambda i: (0, i)),
        out_shape=jax.ShapeDtypeStruct((rows, total), jnp.float32),
        compiler_params=ROOMY,
        cost_estimate=NO_COST,
    )(grad_rows, gain_part, bytes_all)


def patch_grad_kernel(grad_ref, *refs):
    byte_refs, got_refs, out_ref, order_ref = refs[:8], refs[8:16], refs[16], refs[17]
    width = byte_refs[0].shape[1]

    @pl.when(pl.program_id(0) == 0)
    def _():
        order_ref[...] = feature_order(width)

    grad_low = grad_ref[:, : grad_ref.shape[1] // 2].astype(jnp.bfloat16)
    wide = jnp.concatenate([ref[...].astype(jnp.bfloat16) for ref in byte_refs], axis=1)
    rows = grad_low.shape[1]
    grad = dot_left(grad_low, wide)
    grad = grad + jnp.concatenate([ref[:rows] for ref in got_refs], axis=1)
    high = grad.astype(jnp.bfloat16)
    rest = grad - high.astype(jnp.float32)
    mid = rest.astype(jnp.bfloat16)
    low = (rest - mid.astype(jnp.float32)).astype(jnp.bfloat16)
    order = order_ref[...]
    out_ref[...] = dot_plain(high, order) + (dot_plain(mid, order) + dot_plain(low, order))


def patch_grad(grad_rows, got, bytes_all):
    places, cols = grad_rows.shape
    feature = bytes_all.shape[1] // 8
    chunk = 128
    steps = feature // chunk

    def byte_specs(rows):
        return [
            pl.BlockSpec((rows, chunk), partial(lambda j, i: (0, j * steps + i), j))
            for j in range(8)
        ]

    return pl.pallas_call(
        patch_grad_kernel,
        grid=(steps,),
        in_specs=[pl.BlockSpec((places, cols), lambda i: (0, 0))]
        + byte_specs(places)
        + byte_specs(got.shape[0]),
        out_specs=pl.BlockSpec((cols // 2, 8 * chunk), lambda i: (0, i)),
        out_shape=jax.ShapeDtypeStruct((cols // 2, 8 * feature), jnp.float32),
        scratch_shapes=[pltpu.VMEM((8 * chunk, 8 * chunk), jnp.bfloat16)],
        compiler_params=ROOMY,
        cost_estimate=NO_COST,
    )(grad_rows, *([bytes_all] * 8), *([got] * 8))


def trade(blocks):
    return lax.all_to_all(blocks, "seq", 0, 0, tiled=True)


def grid_iota(shape, axis):
    return lax.broadcasted_iota(jnp.int32, shape, axis)


def dot_fine(left_side, right_side, left_axis, right_axis):
    return lax.dot_general(
        left_side,
        right_side,
        (((left_axis,), (right_axis,)), ((), ())),
        preferred_element_type=jnp.float32,
        precision=highest,
    )


def shifted_down(block, distance):
    rows = grid_iota(block.shape, 0)
    return jnp.where(rows >= distance, pltpu.roll(block, distance, 0), 0.0)


def shifted_up(block, distance):
    count = block.shape[0]
    rows = grid_iota(block.shape, 0)
    return jnp.where(rows < count - distance, pltpu.roll(block, count - distance, 0), 0.0)


def scan_terms(taken_ref, same_ref, conv_ref, head_ref):
    places = taken_ref.shape[0]
    channels = conv_ref.shape[1]
    xbc = taken_ref[:, :channels]
    conv_sum = conv_ref[4:5] + conv_ref[3:4] * xbc
    for k in range(3):
        earlier = shifted_down(xbc, 3 - k) * same_ref[:, k : k + 1]
        conv_sum = conv_sum + conv_ref[k : k + 1] * earlier
    gate = jax.nn.sigmoid(conv_sum)
    active = conv_sum * gate
    raw = taken_ref[:, channels:] + head_ref[0:1]
    steps = jnp.maximum(raw, 0.0) + jnp.log1p(jnp.exp(-jnp.abs(raw)))
    rates = -steps * jnp.exp(head_ref[1:2])
    square = (places, places)
    triangle = jnp.where(grid_iota(square, 0) >= grid_iota(square, 1), 1.0, 0.0)
    running = dot_fine(triangle, rates, 1, 0)
    return xbc, conv_sum, gate, active, raw, steps, rates, triangle, running


def scan_forward_kernel(taken_ref, same_ref, conv_ref, head_ref, seg_col, seg_row, out_ref):
    places, width = out_ref.shape
    terms = scan_terms(taken_ref, same_ref, conv_ref, head_ref)
    active, steps, running = terms[3], terms[5], terms[8]
    values = active[:, :width]
    keys, reads = active[:, width : width + NS], active[:, width + NS :]
    steps_row, running_row = steps.T, running.T
    heads = width // 64
    rows = 128
    for first in range(0, places, rows):
        last = first + rows
        shape = (rows, last)
        allowed = (seg_col[first:last] == seg_row[:, :last]) & (
            grid_iota(shape, 0) + first >= grid_iota(shape, 1)
        )
        crossing = dot_fine(reads[first:last], keys[:last], 1, 1)
        lane = grid_iota((rows, width), 1) // 64
        total = head_ref[2:3] * values[first:last]
        for h in range(heads):
            gaps = running[first:last, h : h + 1] - running_row[h : h + 1, :last]
            decays = jnp.exp(jnp.where(allowed, gaps, masked_score))
            mixing = crossing * decays * steps_row[h : h + 1, :last]
            part = dot_fine(mixing, values[:last], 1, 0)
            total = total + jnp.where(lane == h, part, 0.0)
        out_ref[first:last] = total


def scan_backward_kernel(
    taken_ref,
    same_ref,
    conv_ref,
    head_ref,
    seg_col,
    seg_row,
    grad_ref,
    out_ref,
    conv_grad_ref,
    head_grad_ref,
    values_grad,
    keys_grad,
    reads_grad,
    rows_grad,
    cols_grad,
):
    places, width = values_grad.shape
    terms = scan_terms(taken_ref, same_ref, conv_ref, head_ref)
    xbc, conv_sum, gate, active, raw, steps, rates, triangle, running = terms
    channels = xbc.shape[1]
    values = active[:, :width]
    keys, reads = active[:, width : width + NS], active[:, width + NS :]
    steps_row, running_row = steps.T, running.T
    heads = width // 64
    rows = 128
    grad = grad_ref[...]
    values_grad[...] = head_ref[2:3] * grad
    keys_grad[...] = jnp.zeros_like(keys_grad)
    rows_grad[...] = jnp.zeros_like(rows_grad)
    cols_grad[...] = jnp.zeros_like(cols_grad)
    for first in range(0, places, rows):
        last = first + rows
        shape = (rows, last)
        allowed = (seg_col[first:last] == seg_row[:, :last]) & (
            grid_iota(shape, 0) + first >= grid_iota(shape, 1)
        )
        crossing = dot_fine(reads[first:last], keys[:last], 1, 1)
        crossing_grad = jnp.zeros(shape, jnp.float32)
        grad_rows = grad[first:last]
        lane = grid_iota((rows, width), 1) // 64
        wide_lane = grid_iota((last, width), 1) // 64
        column = grid_iota((rows, 128), 1)
        down = jnp.zeros((rows, 128), jnp.float32)
        for h in range(heads):
            gaps = running[first:last, h : h + 1] - running_row[h : h + 1, :last]
            decays = jnp.exp(jnp.where(allowed, gaps, masked_score))
            step_row = steps_row[h : h + 1, :last]
            weighted = decays * step_row
            mixing = crossing * weighted
            own_grad = jnp.where(lane == h, grad_rows, 0.0)
            mixing_grad = dot_fine(own_grad, values[:last], 1, 1)
            back = dot_fine(mixing, own_grad, 0, 0)
            values_grad[:last] += jnp.where(wide_lane == h, back, 0.0)
            crossing_grad = crossing_grad + mixing_grad * weighted
            step_part = jnp.sum(mixing_grad * crossing * decays, axis=0, keepdims=True)
            gap_part = mixing_grad * mixing
            down = jnp.where(column == h, jnp.sum(gap_part, axis=1, keepdims=True), down)
            cols_grad[h : h + 1, :last] += step_part
            cols_grad[heads + h : heads + h + 1, :last] += step_part * step_row
        rows_grad[first:last] += down
        reads_grad[first:last] = dot_fine(crossing_grad, keys[:last], 1, 0)
        keys_grad[:last] += dot_fine(crossing_grad, reads[first:last], 0, 0)
    turned = cols_grad[...].T
    column = grid_iota(turned.shape, 1)
    step_grad = jnp.where(column < heads, turned, 0.0)
    ended = pltpu.roll(turned, turned.shape[1] - heads, 1)
    running_grad = jnp.where(column < heads, rows_grad[...] - ended, 0.0)
    rates_grad = dot_fine(triangle, running_grad, 0, 0)
    step_grad = step_grad - rates_grad * jnp.exp(head_ref[1:2])
    raw_grad = step_grad * jax.nn.sigmoid(raw)
    out_ref[:, channels:] = raw_grad
    lane = grid_iota((places, width), 1) // 64
    product = jnp.sum(grad * values, axis=0, keepdims=True)
    head_grad_ref[...] = jnp.zeros_like(head_grad_ref)
    head_grad_ref[0:1] = jnp.sum(raw_grad, axis=0, keepdims=True)
    head_grad_ref[1:2] = jnp.sum(rates_grad * rates, axis=0, keepdims=True)
    skip_lane = grid_iota((1, width), 1)
    skip_grad = jnp.zeros((1, width), jnp.float32)
    for h in range(heads):
        own = jnp.sum(jnp.where(skip_lane // 64 == h, product, 0.0), axis=1, keepdims=True)
        skip_grad = jnp.where(skip_lane == h, own, skip_grad)
    head_grad_ref[2:3] = skip_grad
    active_grad = jnp.concatenate([values_grad[...], keys_grad[...], reads_grad[...]], axis=1)
    conv_grad = active_grad * gate * (1.0 + conv_sum * (1.0 - gate))
    back = conv_ref[3:4] * conv_grad
    conv_grad_ref[...] = jnp.zeros_like(conv_grad_ref)
    conv_grad_ref[3:4] = jnp.sum(conv_grad * xbc, axis=0, keepdims=True)
    conv_grad_ref[4:5] = jnp.sum(conv_grad, axis=0, keepdims=True)
    for k in range(3):
        kept = conv_grad * same_ref[:, k : k + 1]
        back = back + conv_ref[k : k + 1] * shifted_up(kept, 3 - k)
        conv_grad_ref[k : k + 1] = jnp.sum(
            kept * shifted_down(xbc, 3 - k), axis=0, keepdims=True
        )
    out_ref[:, :channels] = back


def scan_forward(args, width):
    places = args[0].shape[0]
    return pl.pallas_call(
        scan_forward_kernel,
        out_shape=jax.ShapeDtypeStruct((places, width), jnp.float32),
        compiler_params=ROOMY,
        cost_estimate=NO_COST,
    )(*args)


def scan_backward(args, grad):
    places, width = grad.shape
    channels = args[2].shape[1]
    f32 = jnp.float32
    return pl.pallas_call(
        scan_backward_kernel,
        out_shape=[
            jax.ShapeDtypeStruct((places, channels + 128), f32),
            jax.ShapeDtypeStruct((8, channels), f32),
            jax.ShapeDtypeStruct((8, 128), f32),
        ],
        scratch_shapes=[
            pltpu.VMEM((places, width), f32),
            pltpu.VMEM((places, NS), f32),
            pltpu.VMEM((places, NS), f32),
            pltpu.VMEM((places, 128), f32),
            pltpu.VMEM((128, places), f32),
        ],
        compiler_params=ROOMY,
        cost_estimate=NO_COST,
    )(*args, grad)


def patch_lanes(block):
    shape = (block // 8, 8, block)
    return grid_iota(shape, 0) == grid_iota(shape, 2) // 8


def folded(scores, same_patch):
    split = scores.reshape(same_patch.shape)
    return jnp.sum(jnp.where(same_patch, split, 0.0), axis=0)


def unfolded(rows, same_patch):
    spread = jnp.where(same_patch, rows[None], 0.0)
    return spread.reshape(-1, rows.shape[1]).astype(jnp.bfloat16)


def softmax_rows(scores, causal):
    scores = jnp.where(causal, scores, masked_score)
    top = jnp.max(scores, axis=1, keepdims=True)
    powers = jnp.exp(scores - top)
    return powers / jnp.sum(powers, axis=1, keepdims=True)


def head_places(rows, head_cols, block):
    return [
        (slice(first, first + block), [j * head_cols + pair * 128 for j in range(3)])
        for first in range(0, rows, block)
        for pair in range(head_cols // 128)
    ]


def all_scores(qkv_ref, places, lane, same_patch):
    scores = []
    for rows, (query, key, unused) in places:
        queries = qkv_ref[rows, query : query + 128] * 0.125
        keys = qkv_ref[rows, key : key + 128]
        for h in range(2):
            own = jnp.where(lane == h, queries, 0)
            scores.append(folded(dot_trans(keys, own), same_patch))
    return jnp.stack(scores)


def attn_forward_kernel(
    bytes_ref, patch_ref, gain_ref, qkv_w_ref, o_w_ref, x_ref, a_ref, qkv_ref, o_ref, out_ref
):
    rows = bytes_ref.shape[0]
    spread = jnp.broadcast_to(patch_ref[...][:, None], (rows // 8, 8, patch_ref.shape[1]))
    x = bytes_ref[...].astype(jnp.float32) + spread.reshape(bytes_ref.shape)
    x_ref[...] = x
    attn_in = (x * rms_scale(x) * gain_ref[...]).astype(jnp.bfloat16)
    a_ref[...] = attn_in
    qkv_ref[...] = dot_plain(attn_in, qkv_w_ref[...]).astype(jnp.bfloat16)
    head_cols = o_ref.shape[1]
    block = 128
    same_patch = patch_lanes(block)
    causal = grid_iota((8, block), 0) <= grid_iota((8, block), 1) % 8
    lane = grid_iota((block, 128), 1) // AD
    places = head_places(rows, head_cols, block)
    probs = softmax_rows(all_scores(qkv_ref, places, lane, same_patch), causal)
    for at, (row_place, (query, unused, value)) in enumerate(places):
        values = qkv_ref[row_place, value : value + 128]
        parts = [dot_left(unfolded(probs[2 * at + h], same_patch), values) for h in range(2)]
        total = jnp.where(lane == 0, parts[0], parts[1])
        o_ref[row_place, query : query + 128] = total.astype(jnp.bfloat16)
    out_ref[...] = dot_trans(o_ref[...], o_w_ref[...])


def attn_forward(bytes_rows, patch_rows, gain, w_qkv, w_o):
    rows, width = bytes_rows.shape
    block = 256
    cols, head_cols = w_qkv.shape[1], w_o.shape[1]
    f32, bf16 = jnp.float32, jnp.bfloat16

    def by_rows(cols):
        return pl.BlockSpec((block, cols), lambda i: (i, 0))

    def whole(shape):
        return pl.BlockSpec(shape, lambda i: (0, 0))

    return pl.pallas_call(
        attn_forward_kernel,
        grid=(rows // block,),
        in_specs=[
            by_rows(width),
            pl.BlockSpec((block // 8, width), lambda i: (i, 0)),
            whole((1, width)),
            whole(w_qkv.shape),
            whole(w_o.shape),
        ],
        out_specs=[by_rows(width), by_rows(width), by_rows(cols), by_rows(head_cols), by_rows(width)],
        out_shape=[
            jax.ShapeDtypeStruct((rows, width), f32),
            jax.ShapeDtypeStruct((rows, width), bf16),
            jax.ShapeDtypeStruct((rows, cols), bf16),
            jax.ShapeDtypeStruct((rows, head_cols), bf16),
            jax.ShapeDtypeStruct((rows, width), f32),
        ],
        compiler_params=ROOMY,
        cost_estimate=NO_COST,
    )(bytes_rows, patch_rows, gain.reshape(1, width), w_qkv, w_o)


def attn_backward_kernel(
    x_ref,
    final_ref,
    own_ref,
    other_ref,
    gain_ref,
    qkv_ref,
    qkv_w_ref,
    o_w_ref,
    mid_ref,
    low_ref,
    qkv_grad_ref,
    out_ref,
    gain_grad_ref,
):
    rows = x_ref.shape[0]
    back, gain_grad = rms_back(x_ref[...], gain_ref[...], own_ref[...] + other_ref[...])
    mid = final_ref[...] + back
    mid_ref[...] = mid
    low_ref[...] = mid.astype(jnp.bfloat16)
    gain_grad = gain_grad.reshape(1, -1)

    @pl.when(pl.program_id(0) == 0)
    def _():
        gain_grad_ref[...] = gain_grad

    @pl.when(pl.program_id(0) > 0)
    def _():
        gain_grad_ref[...] += gain_grad

    mixed_grad = dot_plain(low_ref[...], o_w_ref[...]).astype(jnp.bfloat16)
    head_cols = mixed_grad.shape[1]
    block = 128
    same_patch = patch_lanes(block)
    causal = grid_iota((8, block), 0) <= grid_iota((8, block), 1) % 8
    lane = grid_iota((block, 128), 1) // AD
    places = head_places(rows, head_cols, block)
    probs = softmax_rows(all_scores(qkv_ref, places, lane, same_patch), causal)
    probs_grads = []
    for row_place, (query, unused, value) in places:
        values = qkv_ref[row_place, value : value + 128]
        out_grad = mixed_grad[row_place, query : query + 128]
        for h in range(2):
            own_grad = jnp.where(lane == h, out_grad, 0)
            probs_grads.append(folded(dot_trans(values, own_grad), same_patch))
    probs_grad = jnp.stack(probs_grads)
    inner = jnp.sum(probs * probs_grad, axis=1, keepdims=True)
    scores_grad = probs * (probs_grad - inner)
    for at, (row_place, cols) in enumerate(places):
        query, key, unused = cols
        queries = qkv_ref[row_place, query : query + 128]
        keys = qkv_ref[row_place, key : key + 128]
        out_grad = mixed_grad[row_place, query : query + 128]
        parts = []
        for h in range(2):
            own_scores = unfolded(scores_grad[2 * at + h], same_patch)
            parts.append(
                (
                    dot_left(own_scores, keys) * 0.125,
                    dot_plain(own_scores, queries) * 0.125,
                    dot_plain(unfolded(probs[2 * at + h], same_patch), out_grad),
                )
            )
        for j in range(3):
            grad = jnp.where(lane == 0, parts[0][j], parts[1][j])
            qkv_grad_ref[row_place, cols[j] : cols[j] + 128] = grad.astype(jnp.bfloat16)
    out_ref[...] = dot_trans(qkv_grad_ref[...], qkv_w_ref[...])


def attn_backward(x_rows, final_grad, own_part, other_part, gain, qkv, w_qkv, w_o):
    rows, width = x_rows.shape
    block = 256
    cols = w_qkv.shape[1]
    f32, bf16 = jnp.float32, jnp.bfloat16

    def by_rows(cols):
        return pl.BlockSpec((block, cols), lambda i: (i, 0))

    def whole(shape):
        return pl.BlockSpec(shape, lambda i: (0, 0))

    return pl.pallas_call(
        attn_backward_kernel,
        grid=(rows // block,),
        in_specs=[by_rows(width)] * 4
        + [whole((1, width)), by_rows(cols), whole(w_qkv.shape), whole(w_o.shape)],
        out_specs=[
            by_rows(width),
            by_rows(width),
            by_rows(cols),
            by_rows(width),
            whole((1, width)),
        ],
        out_shape=[
            jax.ShapeDtypeStruct((rows, width), f32),
            jax.ShapeDtypeStruct((rows, width), bf16),
            jax.ShapeDtypeStruct((rows, cols), bf16),
            jax.ShapeDtypeStruct((rows, width), f32),
            jax.ShapeDtypeStruct((1, width), f32),
        ],
        compiler_params=ROOMY,
        cost_estimate=NO_COST,
    )(x_rows, final_grad, own_part, other_part, gain.reshape(1, width), qkv, w_qkv, w_o)


def mlp_in_kernel(core_ref, x_ref, own_ref, other_ref, gain_ref, out_ref, low_ref, half_ref):
    x = x_ref[...] + (own_ref[...] + other_ref[...])
    out_ref[...] = x
    unit = x * rms_scale(x)
    low_ref[...] = (unit * gain_ref[...]).astype(jnp.bfloat16)
    width = half_ref.shape[1]
    half_ref[...] = jnp.where(core_ref[0] == 0, unit[:, :width], unit[:, width:])


def mlp_in(x_rows, own_part, other_part, gain):
    rows, width = x_rows.shape
    block = 128
    core = lax.axis_index("tp").astype(jnp.int32).reshape(1)

    def by_rows(cols):
        return pl.BlockSpec((block, cols), lambda i, ref: (i, 0))

    return pl.pallas_call(
        mlp_in_kernel,
        grid_spec=pltpu.PrefetchScalarGridSpec(
            num_scalar_prefetch=1,
            grid=(rows // block,),
            in_specs=[by_rows(width)] * 3 + [pl.BlockSpec((1, width), lambda i, ref: (0, 0))],
            out_specs=[by_rows(width), by_rows(width), by_rows(width // 2)],
        ),
        out_shape=[
            jax.ShapeDtypeStruct((rows, width), jnp.float32),
            jax.ShapeDtypeStruct((rows, width), jnp.bfloat16),
            jax.ShapeDtypeStruct((rows, width // 2), jnp.float32),
        ],
        compiler_params=ROOMY,
        cost_estimate=NO_COST,
    )(core, x_rows, own_part, other_part, gain.reshape(1, width))


def units_in_halves(
    mlp_low, grad_ref, gate_w_ref, up_w_ref, hidden_ref, gate_ref, up_ref
):
    half = grad_ref.shape[1] // 2
    for at in range(2):
        cols = slice(at * half, (at + 1) * half)
        hidden, gate, up = hidden_parts(
            mlp_low, grad_ref[:, cols], gate_w_ref[:, cols], up_w_ref[:, cols]
        )
        hidden_ref[:, cols] = hidden
        gate_ref[:, cols] = gate
        up_ref[:, cols] = up


def mlp_kernel(
    in_ref, grad_ref, gate_w_ref, up_w_ref, hidden_ref, gate_ref, up_ref, out_ref, total_ref
):
    mlp_low = in_ref[...]
    units_in_halves(
        mlp_low, grad_ref, gate_w_ref, up_w_ref, hidden_ref, gate_ref, up_ref
    )
    part = dot_trans(gate_ref[...], gate_w_ref[...]) + dot_trans(up_ref[...], up_w_ref[...])
    step = pl.program_id(0)

    @pl.when(step == 0)
    def _():
        total_ref[...] = part

    @pl.when(step > 0)
    def _():
        total_ref[...] += part

    @pl.when(step == pl.num_programs(0) - 1)
    def _():
        out_ref[...] = total_ref[...]


def mlp_rows(mlp_low, grad_hidden, w_gate, w_up):
    rows, width = mlp_low.shape
    units = w_gate.shape[1]
    block = 512
    by_units = pl.BlockSpec((rows, block), lambda i: (0, i))
    by_weights = pl.BlockSpec((width, block), lambda i: (0, i))
    whole = pl.BlockSpec((rows, width), lambda i: (0, 0))
    low = jax.ShapeDtypeStruct((rows, units), jnp.bfloat16)
    return pl.pallas_call(
        mlp_kernel,
        grid=(units // block,),
        in_specs=[whole, by_units, by_weights, by_weights],
        out_specs=[by_units, by_units, by_units, whole],
        out_shape=[low, low, low, jax.ShapeDtypeStruct((rows, width), jnp.float32)],
        scratch_shapes=[pltpu.VMEM((rows, width), jnp.float32)],
        compiler_params=ROOMY,
        cost_estimate=NO_COST,
    )(mlp_low, grad_hidden, w_gate, w_up)


def feature_order(width):
    shape = (8 * width, 8 * width)
    row, col = grid_iota(shape, 0), grid_iota(shape, 1)
    return jnp.where(row == (col % 8) * width + col // 8, 1.0, 0.0).astype(jnp.bfloat16)


def patch_in_kernel(core_ref, bytes_ref, weight_ref, wide_ref, out_ref, rows_ref, order_ref):
    places, feature = wide_ref.shape[0], wide_ref.shape[1] // 8
    chunk = weight_ref.shape[1] // 8
    step = pl.program_id(0)

    @pl.when(step == 0)
    def _():
        order_ref[...] = feature_order(chunk)
        for at in range(feature // 128):
            low = at * 128
            rows_ref[at] = bytes_ref[:, low : low + 128].astype(jnp.float32)
            for j in range(8):
                wide_ref[:, j * feature + low : j * feature + low + 128] = rows_ref[
                    at, pl.ds(j, places, stride=8), :
                ]

    parts = [
        wide_ref[:, pl.ds(pl.multiple_of(j * feature + step * chunk, 128), chunk)]
        for j in range(8)
    ]
    by_byte = jnp.concatenate(parts, axis=1).astype(jnp.bfloat16)
    by_feature = dot_plain(by_byte, order_ref[...]).astype(jnp.bfloat16)
    part = dot_trans(by_feature, weight_ref[...])

    @pl.when(step == 0)
    def _():
        out_ref[...] = part

    @pl.when(step > 0)
    def _():
        out_ref[...] += part


def patch_in(byte_rows, w_patch):
    rows, model_width = byte_rows.shape
    out_width, cols = w_patch.shape
    feature, chunk = cols // 8, 128
    core = lax.axis_index("tp").astype(jnp.int32).reshape(1)
    f32 = jnp.float32
    return pl.pallas_call(
        patch_in_kernel,
        grid_spec=pltpu.PrefetchScalarGridSpec(
            num_scalar_prefetch=1,
            grid=(feature // chunk,),
            in_specs=[
                pl.BlockSpec((rows, feature), lambda i, ref: (0, ref[0])),
                pl.BlockSpec((out_width, 8 * chunk), lambda i, ref: (0, i)),
            ],
            out_specs=[
                pl.BlockSpec((rows // 8, cols), lambda i, ref: (0, 0)),
                pl.BlockSpec((rows // 8, out_width), lambda i, ref: (0, 0)),
            ],
            scratch_shapes=[
                pltpu.VMEM((feature // 128, rows, 128), f32),
                pltpu.VMEM((8 * chunk, 8 * chunk), jnp.bfloat16),
            ],
        ),
        out_shape=[
            jax.ShapeDtypeStruct((rows // 8, cols), f32),
            jax.ShapeDtypeStruct((rows // 8, out_width), f32),
        ],
        compiler_params=ROOMY,
        cost_estimate=NO_COST,
    )(core, byte_rows, w_patch)


def final_kernel(
    member_ref,
    own_ref,
    other_ref,
    mask_ref,
    own_head_ref,
    other_head_ref,
    weight_ref,
    low_ref,
    hidden_ref,
    mine_ref,
    mine_low_ref,
):
    own = (own_ref[...] * mask_ref[...]).astype(jnp.bfloat16)
    other = (other_ref[...] * mask_ref[...]).astype(jnp.bfloat16)
    other_head = other_head_ref[...].astype(jnp.bfloat16)
    total = dot_trans(own, own_head_ref[...]) + dot_trans(other, other_head)
    low = total.astype(jnp.bfloat16)
    low_ref[...] = low
    hidden_ref[...] = dot_plain(low, weight_ref[...])

    @pl.when(pl.program_id(0) == member_ref[0])
    def _():
        mine_ref[...] = total
        mine_low_ref[...] = low


def final_grads(own, other, mask, own_head, other_head, w_down, member):
    rows, cols = own.shape
    width = own_head.shape[0]
    block = rows // QUAD
    units = w_down.shape[1] // QUAD
    f32, bf16 = jnp.float32, jnp.bfloat16

    def by_rows(cols):
        return pl.BlockSpec((block, cols), lambda i, ref: (i, 0))

    head = pl.BlockSpec((width, cols), lambda i, ref: (0, 0))
    mine = pl.BlockSpec((block, width), lambda i, ref: (0, 0))
    return pl.pallas_call(
        final_kernel,
        grid_spec=pltpu.PrefetchScalarGridSpec(
            num_scalar_prefetch=1,
            grid=(QUAD,),
            in_specs=[by_rows(cols), by_rows(cols), by_rows(1), head, head]
            + [pl.BlockSpec((width, units), lambda i, ref: (0, ref[0]))],
            out_specs=[by_rows(width), by_rows(units), mine, mine],
        ),
        out_shape=[
            jax.ShapeDtypeStruct((rows, width), bf16),
            jax.ShapeDtypeStruct((rows, units), f32),
            jax.ShapeDtypeStruct((block, width), f32),
            jax.ShapeDtypeStruct((block, width), bf16),
        ],
        compiler_params=ROOMY,
        cost_estimate=NO_COST,
    )(member, own, other, mask, own_head, other_head, w_down)


def group_mlp_kernel(
    place_ref,
    own_ref,
    other_ref,
    gain_ref,
    grad_ref,
    gate_w_ref,
    up_w_ref,
    in_ref,
    hidden_ref,
    gate_ref,
    up_ref,
):
    own, other = own_ref[0], other_ref[0]
    first = place_ref[1] == 0
    halves = [jnp.where(first, own, other), jnp.where(first, other, own)]
    low = (jnp.concatenate(halves, axis=1) * gain_ref[...]).astype(jnp.bfloat16)
    in_ref[...] = low
    units_in_halves(low, grad_ref, gate_w_ref, up_w_ref, hidden_ref, gate_ref, up_ref)


def group_mlp(own_half, other_half, gain, grad_hidden, w_gate, w_up, member):
    unused, rows, half = own_half.shape
    width, units = 2 * half, w_gate.shape[1] // QUAD
    bf16 = jnp.bfloat16
    place = jnp.concatenate([member, lax.axis_index("tp").astype(jnp.int32).reshape(1)])

    def by_rows(cols):
        return pl.BlockSpec((rows, cols), lambda i, ref: (i, 0))

    halves = pl.BlockSpec((1, rows, half), lambda i, ref: (i, 0, 0))
    weights = pl.BlockSpec((width, units), lambda i, ref: (0, ref[0]))
    low = jax.ShapeDtypeStruct((QUAD * rows, units), bf16)
    return pl.pallas_call(
        group_mlp_kernel,
        grid_spec=pltpu.PrefetchScalarGridSpec(
            num_scalar_prefetch=1,
            grid=(QUAD,),
            in_specs=[
                halves,
                halves,
                pl.BlockSpec((1, width), lambda i, ref: (0, 0)),
                by_rows(units),
                weights,
                weights,
            ],
            out_specs=[by_rows(width), by_rows(units), by_rows(units), by_rows(units)],
        ),
        out_shape=[jax.ShapeDtypeStruct((QUAD * rows, width), bf16), low, low, low],
        compiler_params=ROOMY,
        cost_estimate=NO_COST,
    )(place, own_half, other_half, gain.reshape(1, width), grad_hidden, w_gate, w_up)


def body(
    byte_states,
    lengths,
    w_patch,
    norm_global,
    w_in,
    conv_w,
    conv_b,
    dt_bias,
    a_log,
    d_skip,
    mix_gain,
    w_out,
    norm_attn,
    w_qkv,
    w_o,
    norm_mlp,
    w_gate,
    w_up,
    w_down,
    w_head,
    d_logits,
):
    streams, local_rows, model_width = byte_states.shape
    patch_count = local_rows // 8
    patch_total = streams * patch_count
    row_total = streams * local_rows
    feature = w_patch.shape[1] // 8
    inner_width = w_out.shape[1]
    channels = conv_w.shape[1]
    head_total = dt_bias.shape[0]
    head_cols = w_head.shape[1]
    parts = lax.axis_size("seq")
    tp_index = lax.axis_index("tp")
    seq_index = lax.axis_index("seq")
    places = parts * patch_count
    f32 = jnp.float32

    lanes = parts // streams
    width = inner_width // lanes
    full_head = inner_width // head_total
    own_heads = max(1, width // full_head)
    shared = max(1, full_head // width)
    head_size = width // own_heads
    own_stream = seq_index // lanes
    first_col = (seq_index % lanes) * width
    first_head = first_col // full_head

    seg_full = segment_ids(lengths, places)
    seg_own = lax.dynamic_slice_in_dim(seg_full, seq_index * patch_count, patch_count, 1)
    seg_stream = lax.dynamic_index_in_dim(seg_full, own_stream, 0, keepdims=False)
    valid = (seg_own < lengths.shape[0]).astype(f32).reshape(patch_total, 1)
    byte_valid = jnp.repeat(valid, 8, axis=0)

    member = (seq_index >> 2 & 1) * 2 + (seq_index & 1)
    raw_logits = d_logits.reshape(row_total, head_cols)
    raw_wide = raw_logits.astype(f32)
    group_valid = []
    for high in range(2):
        for low in range(2):
            device = (seq_index & ~5) | high << 2 | low
            group_seg = lax.dynamic_slice_in_dim(
                seg_full, device * patch_count, patch_count, 1
            )
            group_valid.append((group_seg < lengths.shape[0]).astype(f32))
    group_valid = jnp.stack(group_valid).reshape(QUAD, patch_total, 1)
    group_bytes_valid = jnp.repeat(group_valid.reshape(-1, 1), 8, axis=0)
    group_raw = side_trade(jnp.broadcast_to(raw_wide[None], (QUAD,) + raw_wide.shape))
    group_raw = group_raw.reshape(-1, head_cols)
    other_raw = swap(group_raw, "tp", 1)
    other_head = swap(w_head.astype(f32), "tp", 1)
    place_index = member.astype(jnp.int32).reshape(1)
    bytes_wide, patch_part = patch_in(byte_states.reshape(row_total, model_width), w_patch)
    patch_out = tp_sum(patch_part)
    gain_global = norm_global.astype(f32)
    unit_patch = patch_out * rms_scale(patch_out)
    u_low = (unit_patch * gain_global).astype(jnp.bfloat16)
    half_width = model_width // 2
    proj = dot_plain(u_low, w_in).reshape(streams, patch_count, -1)
    gate_in = proj[..., :inner_width]
    xbc = proj[..., inner_width : inner_width + channels]
    dt_raw = proj[..., inner_width + channels :]

    def by_lane(columns):
        split = columns.reshape(streams, patch_count, lanes, -1)
        return jnp.moveaxis(split, 2, 1).reshape(parts, patch_count, -1)

    def from_lanes(blocks):
        split = blocks.reshape(streams, lanes, patch_count, -1)
        return jnp.moveaxis(split, 1, 2).reshape(streams, patch_count, -1)

    def to_all_lanes(columns):
        wide = jnp.broadcast_to(
            columns[:, None], (streams, lanes, patch_count, columns.shape[-1])
        )
        return wide.reshape(parts, patch_count, -1)

    pad_width = 128 - own_heads
    dt_lanes = by_lane(jnp.repeat(dt_raw, shared, axis=2))
    sent = jnp.concatenate(
        [
            by_lane(xbc[..., :inner_width]),
            to_all_lanes(xbc[..., inner_width:]),
            jnp.pad(dt_lanes, ((0, 0), (0, 0), (0, pad_width))),
        ],
        axis=-1,
    )
    taken = trade(sent)
    grad_logits = after(raw_logits, sent) * byte_valid.astype(jnp.bfloat16)
    group_final, group_grad_hidden, grad_final, grad_mlp_low = final_grads(
        after(group_raw, sent),
        other_raw,
        group_bytes_valid,
        w_head,
        other_head,
        w_down,
        place_index,
    )
    grad_hidden = dot_plain(grad_mlp_low, w_down)
    hidden_part = w_gate.shape[1] // QUAD

    row_side = [
        [device for device in range(parts) if (device >> 1 & 1) == side] for side in range(2)
    ]
    bytes_all = lax.all_gather(
        bytes_wide, "seq", axis=0, axis_index_groups=row_side, tiled=True
    )
    taken = after(taken, grad_hidden, group_grad_hidden).reshape(places, -1)
    scan_width = width + channels - inner_width

    def own_cols(param):
        mine = lax.dynamic_slice_in_dim(param, first_col, width, param.ndim - 1)
        return jnp.concatenate([mine, param[..., inner_width:]], axis=-1).astype(f32)

    def own_head(param):
        return lax.dynamic_slice_in_dim(param, first_head, own_heads, 0).astype(f32)

    use_kernel = places == 512 and width == 128
    if use_kernel:
        padded_seg = jnp.pad(seg_stream, (3, 0), constant_values=-1)
        same = jnp.stack(
            [(padded_seg[k : k + places] == seg_stream).astype(f32) for k in range(3)]
            + [jnp.zeros((places,), f32)] * 5,
            axis=1,
        )
        conv_pack = jnp.concatenate(
            [own_cols(conv_w), own_cols(conv_b)[None], jnp.zeros((3, scan_width), f32)]
        )
        head_pack = jnp.stack(
            [jnp.pad(own_head(dt_bias), (0, 128 - own_heads))]
            + [jnp.pad(own_head(a_log), (0, 128 - own_heads))]
            + [jnp.repeat(own_head(d_skip), head_size)]
            + [jnp.zeros((128,), f32)] * 5
        )
        scan_args = (taken, same, conv_pack, head_pack, seg_stream[:, None], seg_stream[None])
        scanned = scan_forward(scan_args, width)
    else:
        scan_args = (
            taken[:, :scan_width],
            taken[:, scan_width : scan_width + own_heads],
            own_cols(conv_w),
            own_cols(conv_b),
            own_head(dt_bias),
            own_head(a_log),
            own_head(d_skip),
        )
        scanned, scan_back = jax.vjp(partial(scan_heads, seg_stream, head_size), *scan_args)
    result = from_lanes(trade(scanned.reshape(parts, patch_count, width)))
    unit_normed, norm_back = jax.vjp(gated_unit, result, gate_in)
    mix_scale = mix_gain.astype(f32)
    normed_low = (unit_normed * mix_scale).reshape(patch_total, -1).astype(jnp.bfloat16)

    def to_group(whole, quarters):
        split = quarters.reshape(patch_total, QUAD, inner_width // QUAD)
        wide = jnp.broadcast_to(whole[None], (QUAD,) + whole.shape)
        return side_trade(jnp.concatenate([wide, jnp.moveaxis(split, 1, 0)], axis=-1))

    group_got = to_group(unit_patch, unit_normed)
    group_u = (group_got[..., :model_width] * gain_global).astype(jnp.bfloat16)
    own_scale = lax.dynamic_slice_in_dim(
        mix_scale, member * (inner_width // QUAD), inner_width // QUAD, 0
    )
    group_n = (group_got[..., model_width:] * own_scale).astype(jnp.bfloat16)
    group_u = group_u.reshape(-1, model_width)
    group_n = group_n.reshape(-1, inner_width // QUAD)
    global_out = patch_out + valid * tp_sum(dot_trans(normed_low, w_out))
    gain_attn = norm_attn.astype(f32)
    gain_mlp = norm_mlp.astype(f32)
    stream_in, attn_in, qkv, mixed_low, attn_part = attn_forward(
        byte_states.reshape(row_total, model_width), global_out, gain_attn, w_qkv, w_o
    )
    after_attn, mlp_low, unit_half = mlp_in(
        stream_in, attn_part, swap(attn_part, "tp", 1), gain_mlp
    )
    hidden_low, grad_gate_low, grad_up_low, grad_mlp_part = mlp_rows(
        after(mlp_low, unit_half), grad_hidden, w_gate, w_up
    )
    group_halves = side_trade(jnp.broadcast_to(unit_half[None], (QUAD,) + unit_half.shape))
    grad_mlp_other = after(swap(grad_mlp_part, "tp", 1), group_got)
    after_mlp = after_attn + tp_sum(dot_trans(after(hidden_low, grad_mlp_part), w_down))
    final_low = after_mlp.astype(jnp.bfloat16)
    logits = dot_plain(final_low, w_head) * byte_valid
    grad_mid, grad_attn_low, grad_qkv_low, grad_attn_part, grad_norm_mlp = attn_backward(
        after_attn, grad_final, grad_mlp_part, grad_mlp_other, gain_mlp, qkv, w_qkv, w_o
    )
    grad_norm_mlp = grad_norm_mlp.reshape(-1)
    grad_attn_in = tp_sum(grad_attn_part)

    attn_cut = 1024 if grad_qkv_low.shape[1] > 1024 else 128
    attn_in_late = after(attn_in, grad_attn_part, group_halves)
    attn_cols = grad_qkv_low.shape[1]
    attn_blocks = (
        grad_blocks([(attn_in_late, grad_qkv_low, 0, attn_cut)], 0, True),
        grad_blocks(
            [
                (attn_in_late, grad_qkv_low, attn_cut, attn_cols),
                (grad_attn_low, mixed_low, 0, mixed_low.shape[1]),
                (final_low, grad_logits, 0, head_cols),
            ],
            1,
            True,
        ),
    )
    attn_got = [to_partner(attn_blocks[first][0], first) for first in range(2)]
    grad_attn_in = after(grad_attn_in, attn_blocks[0][0], attn_blocks[1][0])
    back_attn, grad_norm_attn = rms_back(stream_in, gain_attn, grad_attn_in)
    grad_stream = grad_mid + back_attn
    grad_global = jnp.sum(grad_stream.reshape(patch_total, 8, model_width), axis=1)
    grad_mix_low = (grad_global * valid).astype(jnp.bfloat16)
    grad_normed = dot_plain(grad_mix_low, w_out).reshape(streams, patch_count, inner_width)
    grad_mix_gain = jnp.sum(grad_normed * unit_normed, axis=(0, 1))
    grad_result, grad_gate_in = norm_back(grad_normed * mix_scale)
    grad_z_low = grad_gate_in.reshape(patch_total, inner_width).astype(jnp.bfloat16)
    row_block = model_width // parts
    dealing = by_lane(grad_result)
    dealt = trade(dealing)
    own_half = after(group_halves, dealing, bytes_all)
    group_in, group_hidden, group_gate, group_up = group_mlp(
        own_half, swap(own_half, "tp", 1), gain_mlp, group_grad_hidden, w_gate, w_up, place_index
    )
    late_got = to_group(after(grad_global, dealing), grad_gate_in)
    group_mix = (late_got[..., :model_width] * group_valid).astype(jnp.bfloat16)
    group_mix = group_mix.reshape(-1, model_width)
    group_z = late_got[..., model_width:].reshape(-1, inner_width // QUAD)
    mlp_blocks = [
        grad_blocks(
            [(group_final, group_hidden, 0, hidden_part), (group_in, group_gate, 0, hidden_part)],
            1,
            False,
        ),
        grad_blocks(
            [
                (group_in, group_up, 0, hidden_part),
                (group_mix, group_n, 0, group_n.shape[1]),
                (group_u, group_z, 0, group_z.shape[1]),
            ],
            1,
            False,
        ),
    ]
    mlp_got = [to_partner(far, 1) for far, unused in mlp_blocks]
    dealt = after(dealt, mlp_blocks[0][0], mlp_blocks[1][0], *attn_got)
    dealt = dealt.reshape(places, width)
    grad_scanned = dealt[:, :width]
    attn_far = [after(attn_blocks[first][1], dealt)[1] + attn_got[first][1] for first in range(2)]
    attn_crossed = [to_partner(attn_far[first], 1 - first) for first in range(2)]
    grad_scanned = after(grad_scanned, *attn_far)
    if use_kernel:
        back_sent, conv_grads, head_grads = scan_backward(scan_args, grad_scanned)
        lane_grad = back_sent[:, : scan_width + own_heads]
        scan_params = (
            conv_grads[:4],
            conv_grads[4],
            head_grads[0, :own_heads],
            head_grads[1, :own_heads],
            head_grads[2, :own_heads],
        )
    else:
        scan_grads = scan_back(grad_scanned)
        back_sent = jnp.concatenate(
            [scan_grads[0], jnp.pad(scan_grads[1], ((0, 0), (0, pad_width)))], axis=-1
        )
        lane_grad = jnp.concatenate([scan_grads[0], scan_grads[1]], axis=-1)
        scan_params = scan_grads[2:]
    back_sent = back_sent.reshape(parts, patch_count, -1)
    back_taken = after(trade(back_sent), mlp_got[0], *attn_crossed)
    small = (
        scan_params[0][:, :width],
        scan_params[1][:width],
        scan_params[0][:, width:],
        scan_params[1][width:],
        scan_params[2],
        scan_params[3],
        scan_params[4],
        grad_mix_gain,
        grad_norm_attn,
        grad_norm_mlp,
    )
    small_count = sum(part.size for part in small)
    flat = jnp.concatenate([part.reshape(-1) for part in small])
    flat = jnp.pad(flat, (0, -small_count % 1024)).reshape(1, -1, 128)
    pieces = trade(jnp.broadcast_to(flat, (parts,) + flat.shape[1:])).reshape(parts, -1)
    by_small, at = [], 0
    for part in small:
        got = pieces[:, at : at + part.size].reshape((parts,) + part.shape)
        by_small.append(got)
        at += part.size

    def lane_cols(got):
        joined = jnp.sum(got.reshape((streams, lanes) + got.shape[1:]), axis=0)
        return jnp.moveaxis(joined, 0, -2).reshape(joined.shape[1:-1] + (-1,))

    def lane_heads(got):
        joined = jnp.sum(got.reshape(streams, lanes, -1), axis=0)
        return jnp.sum(joined.reshape(head_total, shared), axis=-1)

    small_sums = [
        jnp.concatenate([lane_cols(by_small[0]), jnp.sum(by_small[2], axis=0)], axis=-1),
        jnp.concatenate([lane_cols(by_small[1]), jnp.sum(by_small[3], axis=0)], axis=-1),
        lane_heads(by_small[4]),
        lane_heads(by_small[5]),
        lane_heads(by_small[6]),
    ] + [jnp.sum(got, axis=0) for got in by_small[7:]]

    grad_x = from_lanes(back_taken[..., :width])
    by_stream = back_taken.reshape(streams, lanes, patch_count, -1)
    grad_bc = jnp.sum(by_stream[..., width:scan_width], axis=1)
    grad_dt = from_lanes(back_taken[..., scan_width : scan_width + own_heads])
    grad_dt = jnp.sum(grad_dt.reshape(streams, patch_count, head_total, shared), axis=-1)
    attn_near = [
        after(attn_blocks[first][1], back_taken)[0] + attn_got[first][0] + attn_crossed[first]
        for first in range(2)
    ]
    grad_shared = jnp.concatenate([grad_bc, grad_dt], axis=-1).reshape(patch_total, -1)
    grad_proj_low = jnp.concatenate(
        [grad_z_low, grad_x.reshape(patch_total, -1).astype(jnp.bfloat16)]
        + [grad_shared.astype(jnp.bfloat16)],
        axis=-1,
    )
    grad_proj_low = after(grad_proj_low, *attn_near)
    grad_u_part = dot_trans(grad_proj_low, w_in)
    grad_u = tp_sum(grad_u_part)
    def quarters(columns):
        split = columns.reshape(patch_total, QUAD, -1)
        return jnp.moveaxis(split, 1, 0)

    rest = [quarters(columns) for columns in (grad_x, grad_bc, grad_dt)]
    rest_cols = [part.shape[-1] for part in rest]
    rest = after(jnp.concatenate(rest, axis=-1), grad_u_part)
    rest = jnp.pad(rest, ((0, 0), (0, 0), (0, -sum(rest_cols) % 128)))
    rest_blocks = grad_blocks(
        [(group_u, side_trade(rest).reshape(-1, rest.shape[-1]), 0, rest.shape[-1])], 1, False
    )
    rest_got = to_partner(rest_blocks[0], 1)
    back_global, grad_norm_global = rms_back(patch_out, gain_global, grad_u)
    grad_patch = grad_global + back_global
    side_count = parts // 2
    my_side = seq_index >> 1 & 1
    by_block = jnp.moveaxis(grad_patch.reshape(patch_total, parts, row_block), 1, 0)
    by_block = by_block.reshape(parts // 4, 2, 2, patch_total, row_block)
    same_side = lax.dynamic_index_in_dim(by_block, my_side, 1, keepdims=False)
    other_side = lax.dynamic_index_in_dim(by_block, 1 - my_side, 1, keepdims=False)
    patch_rows = jnp.concatenate([same_side, other_side], axis=-1)
    patch_rows = patch_rows.reshape(side_count, patch_total, 2 * row_block)
    gain_part = grad_norm_global.reshape(-1, 2 * row_block)
    gain_count = gain_part.shape[0]
    patch_sent = jnp.concatenate(
        [patch_rows, jnp.broadcast_to(gain_part, (side_count,) + gain_part.shape)], axis=1
    )
    patch_taken = lax.all_to_all(
        patch_sent, "seq", 0, 0, axis_index_groups=row_side, tiled=True
    )

    gain_side = jnp.sum(patch_taken[:, patch_total:], axis=0)
    patch_cols = patch_taken[:, :patch_total].reshape(-1, 2 * row_block)
    patch_far = patch_far_grad(patch_cols, gain_side, bytes_all)
    mlp_finals = []
    for blocks, got, turn in zip(
        mlp_blocks + [rest_blocks], mlp_got + [rest_got], (back_taken, patch_taken, patch_far)
    ):
        part = after(blocks[1], turn) + got
        part = part.reshape((2,) * (seq_bits() - 1) + (row_block, -1))
        for bit in range(3, seq_bits()):
            far, near = halve(part, seq_bits() - 1 - bit, bit)
            part = near + to_partner(far, bit)
        mine = part.reshape(QUAD, row_block, -1)
        mlp_finals.append(jnp.moveaxis(side_trade(mine), 0, 1))

    def final_cols(final, low, count):
        return final[..., low : low + count].reshape(row_block, -1)

    quarter = inner_width // QUAD
    final_down = final_cols(mlp_finals[0], 0, hidden_part)
    final_gate = final_cols(mlp_finals[0], hidden_part, hidden_part)
    final_up = final_cols(mlp_finals[1], 0, hidden_part)
    final_out = final_cols(mlp_finals[1], hidden_part, quarter)
    final_z = final_cols(mlp_finals[1], hidden_part + quarter, quarter)
    final_x = final_cols(mlp_finals[2], 0, rest_cols[0])
    final_bc = final_cols(mlp_finals[2], rest_cols[0], rest_cols[1])
    final_dt = final_cols(mlp_finals[2], rest_cols[0] + rest_cols[1], rest_cols[2])
    part = high_trade(jnp.concatenate(attn_near, axis=-1))
    final_attn = jnp.sum(part, axis=0)
    patch_got = to_partner(patch_far, 1)
    final_patch = patch_grad(patch_cols, patch_got, bytes_all)
    norm_global_sum = (gain_side + patch_got[row_block:, : 2 * row_block]).reshape(-1)
    grad_vec = dot_plain(after(grad_patch, patch_far).astype(jnp.bfloat16), w_patch)
    grad_vec = grad_vec.reshape(streams, patch_count, feature, 8)
    grad_own = jnp.swapaxes(grad_vec, 2, 3).reshape(streams, local_rows, feature)
    grad_rows = lax.dynamic_slice_in_dim(
        grad_stream.reshape(streams, local_rows, model_width), tp_index * feature, feature, 2
    )
    grad_bytes = grad_rows + grad_own

    qkv_cols, o_cols = w_qkv.shape[1], w_o.shape[1]
    return (
        logits.reshape(streams, local_rows, head_cols),
        grad_bytes,
        final_patch,
        norm_global_sum,
        jnp.concatenate([final_z, final_x, final_bc, final_dt], axis=1),
        small_sums[0],
        small_sums[1],
        small_sums[2],
        small_sums[3],
        small_sums[4],
        small_sums[5],
        final_out,
        small_sums[6],
        final_attn[:, :qkv_cols],
        final_attn[:, qkv_cols : qkv_cols + o_cols],
        small_sums[7],
        final_gate,
        final_up,
        final_down,
        final_attn[:, qkv_cols + o_cols :],
    )


def solution(mesh):
    in_specs = (
        P(None, "seq", None),
        P(),
        P(None, "tp"),
        P(),
        P(None, "tp"),
        P(None, "tp"),
        P("tp"),
        P("tp"),
        P("tp"),
        P("tp"),
        P("tp"),
        P(None, "tp"),
        P(),
        P(None, "tp"),
        P(None, "tp"),
        P(),
        P(None, "tp"),
        P(None, "tp"),
        P(None, "tp"),
        P(None, "tp"),
        P(None, "seq", "tp"),
    )
    out_specs = (
        P(None, "seq", "tp"),
        P(None, "seq", "tp"),
        P("seq", "tp"),
        P(),
        P("seq", "tp"),
        P(None, "tp"),
        P("tp"),
        P("tp"),
        P("tp"),
        P("tp"),
        P("tp"),
        P("seq", "tp"),
        P(),
        P("seq", "tp"),
        P("seq", "tp"),
        P(),
        P("seq", "tp"),
        P("seq", "tp"),
        P("seq", "tp"),
        P("seq", "tp"),
    )
    return jax.shard_map(body, mesh=mesh, in_specs=in_specs, out_specs=out_specs, check_vma=False)
```

```python
from functools import partial

import jax
import jax.numpy as jnp
from jax import lax
from jax.experimental import pallas as pl
from jax.experimental.pallas import tpu as pltpu
from jax.sharding import PartitionSpec as P

NS = 128
AD = 64
QUAD = 4


NO_COST = pl.CostEstimate(flops=1024, bytes_accessed=1024, transcendentals=0)
ROOMY = pltpu.CompilerParams(vmem_limit_bytes=56 * 1024 * 1024)

epsilon = 1e-05
highest = lax.Precision.HIGHEST
masked_score = -1e30


def dot_plain(left_side, right_side):
    return jnp.dot(left_side, right_side, preferred_element_type=jnp.float32)


def dot_trans(left_side, right_side):
    return lax.dot_general(
        left_side, right_side, (((1,), (1,)), ((), ())), preferred_element_type=jnp.float32
    )


def dot_left(left_side, right_side):
    return lax.dot_general(
        left_side, right_side, (((0,), (0,)), ((), ())), preferred_element_type=jnp.float32
    )


def rms_scale(values):
    return lax.rsqrt(jnp.mean(values * values, axis=-1, keepdims=True) + epsilon)


def hidden_parts(mlp_in, grad_hidden, w_gate, w_up):
    gate_proj = dot_plain(mlp_in, w_gate)
    up_proj = dot_plain(mlp_in, w_up)
    sigmoid_gate = jax.nn.sigmoid(gate_proj)
    hidden_low = (gate_proj * sigmoid_gate * up_proj).astype(jnp.bfloat16)
    grad_gate_low = (
        grad_hidden * up_proj * sigmoid_gate * (1.0 + gate_proj * (1.0 - sigmoid_gate))
    ).astype(jnp.bfloat16)
    grad_up_low = (grad_hidden * gate_proj * sigmoid_gate).astype(jnp.bfloat16)
    return (hidden_low, grad_gate_low, grad_up_low)


def rms_back(values, gain_values, grad_out):
    scale = rms_scale(values)
    scaled = gain_values * grad_out
    inner_mean = jnp.mean(values * scaled, axis=-1, keepdims=True)
    grad_values = scale * scaled - values * scale * scale * scale * inner_mean
    grad_gain = jnp.sum(values * scale * grad_out, axis=0)
    return (grad_values, grad_gain)


def swap(block, axis, mask):
    return lax.ppermute(block, axis, [(i, i ^ mask) for i in range(lax.axis_size(axis))])


def after(value, *earlier):
    return lax.optimization_barrier((value,) + earlier)[0]


def tp_sum(block):
    return block + swap(block, "tp", 1)


def to_partner(block, bit):
    return swap(block, "seq", 1 << bit)


def seq_bits():
    return lax.axis_size("seq").bit_length() - 1


def side_trade(blocks):
    members = [
        [base | high << 2 | low for high in range(2) for low in range(2)]
        for base in range(lax.axis_size("seq"))
        if base & 5 == 0
    ]
    return lax.all_to_all(blocks, "seq", 0, 0, axis_index_groups=members, tiled=True)


def add_kernel(index_ref, *refs):
    total = refs[0][...] + refs[1][...]
    refs[2][...] = total.reshape(refs[2].shape)


def add_side(near, got, side):
    unused, groups, rows, cols = near.shape
    index = jnp.zeros((1,), jnp.int32)
    block = pl.BlockSpec((1, 1, rows, cols), lambda i, ref: (side, i, 0, 0))
    return pl.pallas_call(
        add_kernel,
        grid_spec=pltpu.PrefetchScalarGridSpec(
            num_scalar_prefetch=1,
            grid=(groups,),
            in_specs=[block, block],
            out_specs=pl.BlockSpec((1, rows, cols), lambda i, ref: (i, 0, 0)),
        ),
        out_shape=jax.ShapeDtypeStruct((groups, rows, cols), jnp.float32),
        compiler_params=ROOMY,
        cost_estimate=NO_COST,
    )(index, near, got)


def near_kernel(index_ref, *refs):
    out_ref = refs[-1]
    at = 0
    for near_ref, got_ref, crossed_ref in zip(refs[0:-1:3], refs[1:-1:3], refs[2:-1:3]):
        cols = near_ref.shape[3]
        total = near_ref[0, 0] + got_ref[0, 0] + crossed_ref[0]
        out_ref[0, :, at : at + cols] = total
        at += cols


def near_sums(terms, high):
    unused, groups, rows, unused_cols = terms[0][0].shape
    cols = [term[0].shape[3] for term in terms]
    specs, operands = [], []
    for (near, got, crossed), count in zip(terms, cols):
        four = pl.BlockSpec((1, 1, rows, count), lambda i, ref: (0, ref[0] ^ i, 0, 0))
        three = pl.BlockSpec((1, rows, count), lambda i, ref: (ref[0] ^ i, 0, 0))
        specs += [four, four, three]
        operands += [near, got, crossed]
    return pl.pallas_call(
        near_kernel,
        grid_spec=pltpu.PrefetchScalarGridSpec(
            num_scalar_prefetch=1,
            grid=(groups,),
            in_specs=specs,
            out_specs=pl.BlockSpec((1, rows, sum(cols)), lambda i, ref: (i, 0, 0)),
        ),
        out_shape=jax.ShapeDtypeStruct((groups, rows, sum(cols)), jnp.float32),
        compiler_params=ROOMY,
        cost_estimate=NO_COST,
    )(high, *operands)


def split_kernel(index_ref, far_a, far_b, near_a, near_b, far_ref, near_ref):
    far_ref[...] = far_a[...] + far_b[...]
    near_ref[...] = near_a[...] + near_b[...]


def split_add(first, second, bit):
    half = first.shape[0] // 2
    rest = first.shape[1:]
    zeros = (0,) * len(rest)
    mine = (lax.axis_index("seq") >> bit & 1).astype(jnp.int32).reshape(1)
    far = pl.BlockSpec((1,) + rest, lambda i, ref: ((1 - ref[0]) * half + i,) + zeros)
    near = pl.BlockSpec((1,) + rest, lambda i, ref: (ref[0] * half + i,) + zeros)
    out = jax.ShapeDtypeStruct((half,) + rest, jnp.float32)
    block = pl.BlockSpec((1,) + rest, lambda i, ref: (i,) + zeros)
    return pl.pallas_call(
        split_kernel,
        grid_spec=pltpu.PrefetchScalarGridSpec(
            num_scalar_prefetch=1,
            grid=(half,),
            in_specs=[far, far, near, near],
            out_specs=[block, block],
        ),
        out_shape=[out, out],
        compiler_params=ROOMY,
        cost_estimate=NO_COST,
    )(mine, first, second, first, second)


def group_add(first, second):
    members, rows, cols = QUAD, first.shape[-2], first.shape[-1]
    block = pl.BlockSpec((1, rows, cols), lambda i, ref: (i, 0, 0))
    shape = (members, rows, cols)
    return pl.pallas_call(
        add_kernel,
        grid_spec=pltpu.PrefetchScalarGridSpec(
            num_scalar_prefetch=1, grid=(members,), in_specs=[block, block], out_specs=block
        ),
        out_shape=jax.ShapeDtypeStruct(shape, jnp.float32),
        compiler_params=ROOMY,
        cost_estimate=NO_COST,
    )(jnp.zeros((1,), jnp.int32), first.reshape(shape), second.reshape(shape))


def grad_blocks_kernel(pairs, first, relative, rows, member_ref, *refs):
    lefts, rights = refs[: len(pairs)], refs[len(pairs) : 2 * len(pairs)]
    far_ref, near_ref = refs[2 * len(pairs) :]
    other = 1 - first
    at = 0
    for left_ref, right_ref, (low, high) in zip(lefts, rights, pairs):
        got = dot_left(left_ref[...], right_ref[:, low:high].astype(jnp.bfloat16))
        places = slice(at, at + high - low)
        for block in range(got.shape[0] // rows):
            place, member = block // QUAD, block % QUAD
            part = got[block * rows : (block + 1) * rows]
            apart = member_ref[0] ^ member
            is_far = apart >> first & 1
            if relative:
                side = apart >> other & 1
            else:
                side = member >> other & 1

            @pl.when(is_far == 1)
            def _():
                if relative:
                    far_ref[side, place, :, places] = part
                else:
                    far_ref[place, side, :, places] = part

            @pl.when(is_far == 0)
            def _():
                if relative:
                    near_ref[side, place, :, places] = part
                else:
                    near_ref[place, side, :, places] = part

        at += high - low


def grad_blocks(terms, first, relative):
    parts = lax.axis_size("seq")
    groups = parts // QUAD
    model_width = terms[0][0].shape[1]
    rows = model_width // parts
    cols = max(128, QUAD * rows)
    places = cols // (QUAD * rows)
    pairs = [(low, high) for unused, unused_right, low, high in terms]
    total = sum(high - low for low, high in pairs)
    member = (lax.axis_index("seq") % QUAD).astype(jnp.int32).reshape(1)
    if relative:
        shape, block = (2, groups, rows, total), (2, places, rows, total)
        out_spec = pl.BlockSpec(block, lambda i, ref: (0, i, 0, 0))
    else:
        shape, block = (groups, 2, rows, total), (places, 2, rows, total)
        out_spec = pl.BlockSpec(block, lambda i, ref: (i, 0, 0, 0))
    out = jax.ShapeDtypeStruct(shape, jnp.float32)
    return pl.pallas_call(
        partial(grad_blocks_kernel, pairs, first, relative, rows),
        grid_spec=pltpu.PrefetchScalarGridSpec(
            num_scalar_prefetch=1,
            grid=(model_width // cols,),
            in_specs=[
                pl.BlockSpec((term[0].shape[0], cols), lambda i, ref: (0, i)) for term in terms
            ]
            + [pl.BlockSpec(term[1].shape, lambda i, ref: (0, 0)) for term in terms],
            out_specs=[out_spec, out_spec],
        ),
        out_shape=[out, out],
        compiler_params=ROOMY,
        cost_estimate=NO_COST,
    )(member, *[term[0] for term in terms], *[term[1] for term in terms])


def segment_ids(lengths, place_count):
    ends = jnp.cumsum(lengths // 8, dtype=jnp.int32)
    places = jnp.arange(place_count, dtype=jnp.int32)
    short_ids = jnp.sum(
        (places[:, None] >= ends[None, :]).astype(jnp.int32), axis=1, dtype=jnp.int32
    )
    return jnp.stack([jnp.zeros_like(short_ids), short_ids])


def scan_heads(seg_now, head_size, xbc, dt_raw, conv_weight, conv_bias, dt_shift, a_logs, skips):
    place_count = xbc.shape[0]
    conv_sum = conv_bias + conv_weight[3] * xbc
    for offset in range(3):
        distance = 3 - offset
        earlier = jnp.pad(xbc, ((distance, 0), (0, 0)))[:place_count]
        seg_earlier = jnp.pad(seg_now, (distance, 0), constant_values=-1)[:place_count]
        same_doc = (seg_earlier == seg_now).astype(jnp.float32)
        conv_sum = conv_sum + conv_weight[offset] * earlier * same_doc[:, None]
    active = jax.nn.silu(conv_sum)
    head_count = dt_raw.shape[1]
    inner = head_count * head_size
    values = active[:, :inner].reshape(place_count, head_count, head_size)
    in_keys = active[:, inner : inner + NS]
    out_keys = active[:, inner + NS :]
    step_sizes = jax.nn.softplus(dt_raw + dt_shift)
    decay_rates = -step_sizes * jnp.exp(a_logs)
    chunk = min(place_count, 512)
    triangle = jnp.tril(jnp.ones((chunk, chunk), jnp.float32))
    state = jnp.zeros((head_count, head_size, NS), jnp.float32)
    seg_last = jnp.int32(-1)
    outputs = []
    for start in range(0, place_count, chunk):
        stop = start + chunk
        x, b, c = values[start:stop], in_keys[start:stop], out_keys[start:stop]
        dt, seg = step_sizes[start:stop], seg_now[start:stop]
        cumulative = jnp.dot(triangle, decay_rates[start:stop], precision=highest)
        allowed = (triangle > 0.0) & (seg[:, None] == seg[None, :])
        ordered = cumulative.T
        gaps = ordered[:, :, None] - ordered[:, None, :]
        decays = jnp.where(allowed, jnp.exp(jnp.where(allowed, gaps, 0.0)), 0.0)
        crossing = jnp.einsum("pn,jn->pj", c, b, precision=highest)
        mixing = crossing[None] * decays * dt.T[:, None, :]
        result = jnp.einsum("hpj,jhd->phd", mixing, x, precision=highest)
        if start > 0:
            entering = jnp.exp(cumulative) * (seg == seg_last).astype(jnp.float32)[:, None]
            result = result + entering[..., None] * jnp.einsum(
                "pn,hdn->phd", c, state, precision=highest
            )
        if stop < place_count:
            last_same = (seg == seg[-1]).astype(jnp.float32)[:, None]
            weight = jnp.exp(cumulative[-1:] - cumulative) * last_same * dt
            through = jnp.exp(cumulative[-1]) * (seg[-1] == seg_last).astype(jnp.float32)
            state = through[:, None, None] * state + jnp.einsum(
                "jh,jhd,jn->hdn", weight, x, b, precision=highest
            )
            seg_last = seg[-1]
        outputs.append(result + skips[:, None] * x)
    return jnp.concatenate(outputs, axis=0).reshape(place_count, inner)


def gated_unit(result, gate_in):
    gated = result * jax.nn.silu(gate_in)
    return gated * rms_scale(gated)


def patch_far_kernel(grad_ref, gain_ref, bytes_ref, out_ref):
    half = grad_ref.shape[1] // 2
    grad_low = grad_ref[:, half:].astype(jnp.bfloat16)
    out_ref[:half] = dot_left(grad_low, bytes_ref[...].astype(jnp.bfloat16))
    out_ref[half:] = jnp.zeros((out_ref.shape[0] - half, out_ref.shape[1]), jnp.float32)

    @pl.when(pl.program_id(0) == 0)
    def _():
        out_ref[half:, : 2 * half] = gain_ref[...]


def patch_far_grad(grad_rows, gain_part, bytes_all):
    places, cols = grad_rows.shape
    total = bytes_all.shape[1]
    rows = cols // 2 + gain_part.shape[0]
    block = 1024
    return pl.pallas_call(
        patch_far_kernel,
        grid=(total // block,),
        in_specs=[
            pl.BlockSpec((places, cols), lambda i: (0, 0)),
            pl.BlockSpec(gain_part.shape, lambda i: (0, 0)),
            pl.BlockSpec((places, block), lambda i: (0, i)),
        ],
        out_specs=pl.BlockSpec((rows, block), lambda i: (0, i)),
        out_shape=jax.ShapeDtypeStruct((rows, total), jnp.float32),
        compiler_params=ROOMY,
        cost_estimate=NO_COST,
    )(grad_rows, gain_part, bytes_all)


def patch_grad_kernel(grad_ref, *refs):
    byte_refs, got_refs, out_ref, order_ref = refs[:8], refs[8:16], refs[16], refs[17]
    width = byte_refs[0].shape[1]

    @pl.when(pl.program_id(0) == 0)
    def _():
        order_ref[...] = feature_order(width)

    grad_low = grad_ref[:, : grad_ref.shape[1] // 2].astype(jnp.bfloat16)
    wide = jnp.concatenate([ref[...].astype(jnp.bfloat16) for ref in byte_refs], axis=1)
    rows = grad_low.shape[1]
    grad = dot_left(grad_low, wide)
    grad = grad + jnp.concatenate([ref[:rows] for ref in got_refs], axis=1)
    high = grad.astype(jnp.bfloat16)
    rest = grad - high.astype(jnp.float32)
    mid = rest.astype(jnp.bfloat16)
    low = (rest - mid.astype(jnp.float32)).astype(jnp.bfloat16)
    order = order_ref[...]
    out_ref[...] = dot_plain(high, order) + (dot_plain(mid, order) + dot_plain(low, order))


def patch_grad(grad_rows, got, bytes_all):
    places, cols = grad_rows.shape
    feature = bytes_all.shape[1] // 8
    chunk = 128
    steps = feature // chunk

    def byte_specs(rows):
        return [
            pl.BlockSpec((rows, chunk), partial(lambda j, i: (0, j * steps + i), j))
            for j in range(8)
        ]

    return pl.pallas_call(
        patch_grad_kernel,
        grid=(steps,),
        in_specs=[pl.BlockSpec((places, cols), lambda i: (0, 0))]
        + byte_specs(places)
        + byte_specs(got.shape[0]),
        out_specs=pl.BlockSpec((cols // 2, 8 * chunk), lambda i: (0, i)),
        out_shape=jax.ShapeDtypeStruct((cols // 2, 8 * feature), jnp.float32),
        scratch_shapes=[pltpu.VMEM((8 * chunk, 8 * chunk), jnp.bfloat16)],
        compiler_params=ROOMY,
        cost_estimate=NO_COST,
    )(grad_rows, *([bytes_all] * 8), *([got] * 8))


def trade(blocks):
    return lax.all_to_all(blocks, "seq", 0, 0, tiled=True)


def grid_iota(shape, axis):
    return lax.broadcasted_iota(jnp.int32, shape, axis)


def dot_fine(left_side, right_side, left_axis, right_axis):
    return lax.dot_general(
        left_side,
        right_side,
        (((left_axis,), (right_axis,)), ((), ())),
        preferred_element_type=jnp.float32,
        precision=highest,
    )


def shifted_down(block, distance):
    rows = grid_iota(block.shape, 0)
    return jnp.where(rows >= distance, pltpu.roll(block, distance, 0), 0.0)


def shifted_up(block, distance):
    count = block.shape[0]
    rows = grid_iota(block.shape, 0)
    return jnp.where(rows < count - distance, pltpu.roll(block, count - distance, 0), 0.0)


def scan_terms(taken_ref, same_ref, conv_ref, head_ref):
    places = taken_ref.shape[0]
    channels = conv_ref.shape[1]
    xbc = taken_ref[:, :channels]
    conv_sum = conv_ref[4:5] + conv_ref[3:4] * xbc
    for k in range(3):
        earlier = shifted_down(xbc, 3 - k) * same_ref[:, k : k + 1]
        conv_sum = conv_sum + conv_ref[k : k + 1] * earlier
    gate = jax.nn.sigmoid(conv_sum)
    active = conv_sum * gate
    raw = taken_ref[:, channels:] + head_ref[0:1]
    steps = jnp.maximum(raw, 0.0) + jnp.log1p(jnp.exp(-jnp.abs(raw)))
    rates = -steps * jnp.exp(head_ref[1:2])
    square = (places, places)
    triangle = jnp.where(grid_iota(square, 0) >= grid_iota(square, 1), 1.0, 0.0)
    running = dot_fine(triangle, rates, 1, 0)
    return xbc, conv_sum, gate, active, raw, steps, rates, triangle, running


def scan_forward_kernel(taken_ref, same_ref, conv_ref, head_ref, seg_col, seg_row, out_ref):
    places, width = out_ref.shape
    terms = scan_terms(taken_ref, same_ref, conv_ref, head_ref)
    active, steps, running = terms[3], terms[5], terms[8]
    values = active[:, :width]
    keys, reads = active[:, width : width + NS], active[:, width + NS :]
    steps_row, running_row = steps.T, running.T
    heads = width // 64
    rows = 128
    for first in range(0, places, rows):
        last = first + rows
        shape = (rows, last)
        allowed = (seg_col[first:last] == seg_row[:, :last]) & (
            grid_iota(shape, 0) + first >= grid_iota(shape, 1)
        )
        crossing = dot_fine(reads[first:last], keys[:last], 1, 1)
        lane = grid_iota((rows, width), 1) // 64
        total = head_ref[2:3] * values[first:last]
        for h in range(heads):
            gaps = running[first:last, h : h + 1] - running_row[h : h + 1, :last]
            decays = jnp.exp(jnp.where(allowed, gaps, masked_score))
            mixing = crossing * decays * steps_row[h : h + 1, :last]
            part = dot_fine(mixing, values[:last], 1, 0)
            total = total + jnp.where(lane == h, part, 0.0)
        out_ref[first:last] = total


def scan_backward_kernel(
    taken_ref,
    same_ref,
    conv_ref,
    head_ref,
    seg_col,
    seg_row,
    grad_ref,
    out_ref,
    conv_grad_ref,
    head_grad_ref,
    values_grad,
    keys_grad,
    reads_grad,
    rows_grad,
    cols_grad,
):
    places, width = values_grad.shape
    terms = scan_terms(taken_ref, same_ref, conv_ref, head_ref)
    xbc, conv_sum, gate, active, raw, steps, rates, triangle, running = terms
    channels = xbc.shape[1]
    values = active[:, :width]
    keys, reads = active[:, width : width + NS], active[:, width + NS :]
    steps_row, running_row = steps.T, running.T
    heads = width // 64
    rows = 128
    grad = grad_ref[...]
    values_grad[...] = head_ref[2:3] * grad
    keys_grad[...] = jnp.zeros_like(keys_grad)
    rows_grad[...] = jnp.zeros_like(rows_grad)
    cols_grad[...] = jnp.zeros_like(cols_grad)
    for first in range(0, places, rows):
        last = first + rows
        shape = (rows, last)
        allowed = (seg_col[first:last] == seg_row[:, :last]) & (
            grid_iota(shape, 0) + first >= grid_iota(shape, 1)
        )
        crossing = dot_fine(reads[first:last], keys[:last], 1, 1)
        crossing_grad = jnp.zeros(shape, jnp.float32)
        grad_rows = grad[first:last]
        lane = grid_iota((rows, width), 1) // 64
        wide_lane = grid_iota((last, width), 1) // 64
        column = grid_iota((rows, 128), 1)
        down = jnp.zeros((rows, 128), jnp.float32)
        for h in range(heads):
            gaps = running[first:last, h : h + 1] - running_row[h : h + 1, :last]
            decays = jnp.exp(jnp.where(allowed, gaps, masked_score))
            step_row = steps_row[h : h + 1, :last]
            weighted = decays * step_row
            mixing = crossing * weighted
            own_grad = jnp.where(lane == h, grad_rows, 0.0)
            mixing_grad = dot_fine(own_grad, values[:last], 1, 1)
            back = dot_fine(mixing, own_grad, 0, 0)
            values_grad[:last] += jnp.where(wide_lane == h, back, 0.0)
            crossing_grad = crossing_grad + mixing_grad * weighted
            step_part = jnp.sum(mixing_grad * crossing * decays, axis=0, keepdims=True)
            gap_part = mixing_grad * mixing
            down = jnp.where(column == h, jnp.sum(gap_part, axis=1, keepdims=True), down)
            cols_grad[h : h + 1, :last] += step_part
            cols_grad[heads + h : heads + h + 1, :last] += step_part * step_row
        rows_grad[first:last] += down
        reads_grad[first:last] = dot_fine(crossing_grad, keys[:last], 1, 0)
        keys_grad[:last] += dot_fine(crossing_grad, reads[first:last], 0, 0)
    turned = cols_grad[...].T
    column = grid_iota(turned.shape, 1)
    step_grad = jnp.where(column < heads, turned, 0.0)
    ended = pltpu.roll(turned, turned.shape[1] - heads, 1)
    running_grad = jnp.where(column < heads, rows_grad[...] - ended, 0.0)
    rates_grad = dot_fine(triangle, running_grad, 0, 0)
    step_grad = step_grad - rates_grad * jnp.exp(head_ref[1:2])
    raw_grad = step_grad * jax.nn.sigmoid(raw)
    out_ref[:, channels:] = raw_grad
    lane = grid_iota((places, width), 1) // 64
    product = jnp.sum(grad * values, axis=0, keepdims=True)
    head_grad_ref[...] = jnp.zeros_like(head_grad_ref)
    head_grad_ref[0:1] = jnp.sum(raw_grad, axis=0, keepdims=True)
    head_grad_ref[1:2] = jnp.sum(rates_grad * rates, axis=0, keepdims=True)
    skip_lane = grid_iota((1, width), 1)
    skip_grad = jnp.zeros((1, width), jnp.float32)
    for h in range(heads):
        own = jnp.sum(jnp.where(skip_lane // 64 == h, product, 0.0), axis=1, keepdims=True)
        skip_grad = jnp.where(skip_lane == h, own, skip_grad)
    head_grad_ref[2:3] = skip_grad
    active_grad = jnp.concatenate([values_grad[...], keys_grad[...], reads_grad[...]], axis=1)
    conv_grad = active_grad * gate * (1.0 + conv_sum * (1.0 - gate))
    back = conv_ref[3:4] * conv_grad
    conv_grad_ref[...] = jnp.zeros_like(conv_grad_ref)
    conv_grad_ref[3:4] = jnp.sum(conv_grad * xbc, axis=0, keepdims=True)
    conv_grad_ref[4:5] = jnp.sum(conv_grad, axis=0, keepdims=True)
    for k in range(3):
        kept = conv_grad * same_ref[:, k : k + 1]
        back = back + conv_ref[k : k + 1] * shifted_up(kept, 3 - k)
        conv_grad_ref[k : k + 1] = jnp.sum(
            kept * shifted_down(xbc, 3 - k), axis=0, keepdims=True
        )
    out_ref[:, :channels] = back


def scan_forward(args, width):
    places = args[0].shape[0]
    return pl.pallas_call(
        scan_forward_kernel,
        out_shape=jax.ShapeDtypeStruct((places, width), jnp.float32),
        compiler_params=ROOMY,
        cost_estimate=NO_COST,
    )(*args)


def scan_backward(args, grad):
    places, width = grad.shape
    channels = args[2].shape[1]
    f32 = jnp.float32
    return pl.pallas_call(
        scan_backward_kernel,
        out_shape=[
            jax.ShapeDtypeStruct((places, channels + 128), f32),
            jax.ShapeDtypeStruct((8, channels), f32),
            jax.ShapeDtypeStruct((8, 128), f32),
        ],
        scratch_shapes=[
            pltpu.VMEM((places, width), f32),
            pltpu.VMEM((places, NS), f32),
            pltpu.VMEM((places, NS), f32),
            pltpu.VMEM((places, 128), f32),
            pltpu.VMEM((128, places), f32),
        ],
        compiler_params=ROOMY,
        cost_estimate=NO_COST,
    )(*args, grad)


def patch_lanes(block):
    shape = (block // 8, 8, block)
    return grid_iota(shape, 0) == grid_iota(shape, 2) // 8


def folded(scores, same_patch):
    split = scores.reshape(same_patch.shape)
    return jnp.sum(jnp.where(same_patch, split, 0.0), axis=0)


def unfolded(rows, same_patch):
    spread = jnp.where(same_patch, rows[None], 0.0)
    return spread.reshape(-1, rows.shape[1]).astype(jnp.bfloat16)


def softmax_rows(scores, causal):
    scores = jnp.where(causal, scores, masked_score)
    top = jnp.max(scores, axis=1, keepdims=True)
    powers = jnp.exp(scores - top)
    return powers / jnp.sum(powers, axis=1, keepdims=True)


def head_places(rows, head_cols, block):
    return [
        (slice(first, first + block), [j * head_cols + pair * 128 for j in range(3)])
        for first in range(0, rows, block)
        for pair in range(head_cols // 128)
    ]


def all_scores(qkv_ref, places, lane, same_patch):
    scores = []
    for rows, (query, key, unused) in places:
        queries = qkv_ref[rows, query : query + 128] * 0.125
        keys = qkv_ref[rows, key : key + 128]
        for h in range(2):
            own = jnp.where(lane == h, queries, 0)
            scores.append(folded(dot_trans(keys, own), same_patch))
    return jnp.stack(scores)


def attn_forward_kernel(
    bytes_ref, patch_ref, gain_ref, qkv_w_ref, o_w_ref, x_ref, a_ref, qkv_ref, o_ref, out_ref
):
    rows = bytes_ref.shape[0]
    spread = jnp.broadcast_to(patch_ref[...][:, None], (rows // 8, 8, patch_ref.shape[1]))
    x = bytes_ref[...].astype(jnp.float32) + spread.reshape(bytes_ref.shape)
    x_ref[...] = x
    attn_in = (x * rms_scale(x) * gain_ref[...]).astype(jnp.bfloat16)
    a_ref[...] = attn_in
    qkv_ref[...] = dot_plain(attn_in, qkv_w_ref[...]).astype(jnp.bfloat16)
    head_cols = o_ref.shape[1]
    block = 128
    same_patch = patch_lanes(block)
    causal = grid_iota((8, block), 0) <= grid_iota((8, block), 1) % 8
    lane = grid_iota((block, 128), 1) // AD
    places = head_places(rows, head_cols, block)
    probs = softmax_rows(all_scores(qkv_ref, places, lane, same_patch), causal)
    for at, (row_place, (query, unused, value)) in enumerate(places):
        values = qkv_ref[row_place, value : value + 128]
        parts = [dot_left(unfolded(probs[2 * at + h], same_patch), values) for h in range(2)]
        total = jnp.where(lane == 0, parts[0], parts[1])
        o_ref[row_place, query : query + 128] = total.astype(jnp.bfloat16)
    out_ref[...] = dot_trans(o_ref[...], o_w_ref[...])


def attn_forward(bytes_rows, patch_rows, gain, w_qkv, w_o):
    rows, width = bytes_rows.shape
    block = 256
    cols, head_cols = w_qkv.shape[1], w_o.shape[1]
    f32, bf16 = jnp.float32, jnp.bfloat16

    def by_rows(cols):
        return pl.BlockSpec((block, cols), lambda i: (i, 0))

    def whole(shape):
        return pl.BlockSpec(shape, lambda i: (0, 0))

    return pl.pallas_call(
        attn_forward_kernel,
        grid=(rows // block,),
        in_specs=[
            by_rows(width),
            pl.BlockSpec((block // 8, width), lambda i: (i, 0)),
            whole((1, width)),
            whole(w_qkv.shape),
            whole(w_o.shape),
        ],
        out_specs=[by_rows(width), by_rows(width), by_rows(cols), by_rows(head_cols), by_rows(width)],
        out_shape=[
            jax.ShapeDtypeStruct((rows, width), f32),
            jax.ShapeDtypeStruct((rows, width), bf16),
            jax.ShapeDtypeStruct((rows, cols), bf16),
            jax.ShapeDtypeStruct((rows, head_cols), bf16),
            jax.ShapeDtypeStruct((rows, width), f32),
        ],
        compiler_params=ROOMY,
        cost_estimate=NO_COST,
    )(bytes_rows, patch_rows, gain.reshape(1, width), w_qkv, w_o)


def attn_backward_kernel(
    x_ref,
    final_ref,
    own_ref,
    other_ref,
    gain_ref,
    qkv_ref,
    qkv_w_ref,
    o_w_ref,
    mid_ref,
    low_ref,
    qkv_grad_ref,
    out_ref,
    gain_grad_ref,
):
    rows = x_ref.shape[0]
    back, gain_grad = rms_back(x_ref[...], gain_ref[...], own_ref[...] + other_ref[...])
    mid = final_ref[...] + back
    mid_ref[...] = mid
    low_ref[...] = mid.astype(jnp.bfloat16)
    gain_grad = gain_grad.reshape(1, -1)

    @pl.when(pl.program_id(0) == 0)
    def _():
        gain_grad_ref[...] = gain_grad

    @pl.when(pl.program_id(0) > 0)
    def _():
        gain_grad_ref[...] += gain_grad

    mixed_grad = dot_plain(low_ref[...], o_w_ref[...]).astype(jnp.bfloat16)
    head_cols = mixed_grad.shape[1]
    block = 128
    same_patch = patch_lanes(block)
    causal = grid_iota((8, block), 0) <= grid_iota((8, block), 1) % 8
    lane = grid_iota((block, 128), 1) // AD
    places = head_places(rows, head_cols, block)
    probs = softmax_rows(all_scores(qkv_ref, places, lane, same_patch), causal)
    probs_grads = []
    for row_place, (query, unused, value) in places:
        values = qkv_ref[row_place, value : value + 128]
        out_grad = mixed_grad[row_place, query : query + 128]
        for h in range(2):
            own_grad = jnp.where(lane == h, out_grad, 0)
            probs_grads.append(folded(dot_trans(values, own_grad), same_patch))
    probs_grad = jnp.stack(probs_grads)
    inner = jnp.sum(probs * probs_grad, axis=1, keepdims=True)
    scores_grad = probs * (probs_grad - inner)
    for at, (row_place, cols) in enumerate(places):
        query, key, unused = cols
        queries = qkv_ref[row_place, query : query + 128]
        keys = qkv_ref[row_place, key : key + 128]
        out_grad = mixed_grad[row_place, query : query + 128]
        parts = []
        for h in range(2):
            own_scores = unfolded(scores_grad[2 * at + h], same_patch)
            parts.append(
                (
                    dot_left(own_scores, keys) * 0.125,
                    dot_plain(own_scores, queries) * 0.125,
                    dot_plain(unfolded(probs[2 * at + h], same_patch), out_grad),
                )
            )
        for j in range(3):
            grad = jnp.where(lane == 0, parts[0][j], parts[1][j])
            qkv_grad_ref[row_place, cols[j] : cols[j] + 128] = grad.astype(jnp.bfloat16)
    out_ref[...] = dot_trans(qkv_grad_ref[...], qkv_w_ref[...])


def attn_backward(x_rows, final_grad, own_part, other_part, gain, qkv, w_qkv, w_o):
    rows, width = x_rows.shape
    block = 256
    cols = w_qkv.shape[1]
    f32, bf16 = jnp.float32, jnp.bfloat16

    def by_rows(cols):
        return pl.BlockSpec((block, cols), lambda i: (i, 0))

    def whole(shape):
        return pl.BlockSpec(shape, lambda i: (0, 0))

    return pl.pallas_call(
        attn_backward_kernel,
        grid=(rows // block,),
        in_specs=[by_rows(width)] * 4
        + [whole((1, width)), by_rows(cols), whole(w_qkv.shape), whole(w_o.shape)],
        out_specs=[
            by_rows(width),
            by_rows(width),
            by_rows(cols),
            by_rows(width),
            whole((1, width)),
        ],
        out_shape=[
            jax.ShapeDtypeStruct((rows, width), f32),
            jax.ShapeDtypeStruct((rows, width), bf16),
            jax.ShapeDtypeStruct((rows, cols), bf16),
            jax.ShapeDtypeStruct((rows, width), f32),
            jax.ShapeDtypeStruct((1, width), f32),
        ],
        compiler_params=ROOMY,
        cost_estimate=NO_COST,
    )(x_rows, final_grad, own_part, other_part, gain.reshape(1, width), qkv, w_qkv, w_o)


def mlp_in_kernel(core_ref, x_ref, own_ref, other_ref, gain_ref, out_ref, low_ref, half_ref):
    x = x_ref[...] + (own_ref[...] + other_ref[...])
    out_ref[...] = x
    unit = x * rms_scale(x)
    low_ref[...] = (unit * gain_ref[...]).astype(jnp.bfloat16)
    width = half_ref.shape[1]
    half_ref[...] = jnp.where(core_ref[0] == 0, unit[:, :width], unit[:, width:])


def mlp_in(x_rows, own_part, other_part, gain):
    rows, width = x_rows.shape
    block = 128
    core = lax.axis_index("tp").astype(jnp.int32).reshape(1)

    def by_rows(cols):
        return pl.BlockSpec((block, cols), lambda i, ref: (i, 0))

    return pl.pallas_call(
        mlp_in_kernel,
        grid_spec=pltpu.PrefetchScalarGridSpec(
            num_scalar_prefetch=1,
            grid=(rows // block,),
            in_specs=[by_rows(width)] * 3 + [pl.BlockSpec((1, width), lambda i, ref: (0, 0))],
            out_specs=[by_rows(width), by_rows(width), by_rows(width // 2)],
        ),
        out_shape=[
            jax.ShapeDtypeStruct((rows, width), jnp.float32),
            jax.ShapeDtypeStruct((rows, width), jnp.bfloat16),
            jax.ShapeDtypeStruct((rows, width // 2), jnp.float32),
        ],
        compiler_params=ROOMY,
        cost_estimate=NO_COST,
    )(core, x_rows, own_part, other_part, gain.reshape(1, width))


def units_in_halves(
    mlp_low, grad_ref, gate_w_ref, up_w_ref, hidden_ref, gate_ref, up_ref
):
    half = grad_ref.shape[1] // 2
    for at in range(2):
        cols = slice(at * half, (at + 1) * half)
        hidden, gate, up = hidden_parts(
            mlp_low, grad_ref[:, cols], gate_w_ref[:, cols], up_w_ref[:, cols]
        )
        hidden_ref[:, cols] = hidden
        gate_ref[:, cols] = gate
        up_ref[:, cols] = up


def mlp_kernel(
    in_ref, grad_ref, gate_w_ref, up_w_ref, hidden_ref, gate_ref, up_ref, out_ref, total_ref
):
    mlp_low = in_ref[...]
    units_in_halves(
        mlp_low, grad_ref, gate_w_ref, up_w_ref, hidden_ref, gate_ref, up_ref
    )
    part = dot_trans(gate_ref[...], gate_w_ref[...]) + dot_trans(up_ref[...], up_w_ref[...])
    step = pl.program_id(0)

    @pl.when(step == 0)
    def _():
        total_ref[...] = part

    @pl.when(step > 0)
    def _():
        total_ref[...] += part

    @pl.when(step == pl.num_programs(0) - 1)
    def _():
        out_ref[...] = total_ref[...]


def mlp_rows(mlp_low, grad_hidden, w_gate, w_up):
    rows, width = mlp_low.shape
    units = w_gate.shape[1]
    block = 512
    by_units = pl.BlockSpec((rows, block), lambda i: (0, i))
    by_weights = pl.BlockSpec((width, block), lambda i: (0, i))
    whole = pl.BlockSpec((rows, width), lambda i: (0, 0))
    low = jax.ShapeDtypeStruct((rows, units), jnp.bfloat16)
    return pl.pallas_call(
        mlp_kernel,
        grid=(units // block,),
        in_specs=[whole, by_units, by_weights, by_weights],
        out_specs=[by_units, by_units, by_units, whole],
        out_shape=[low, low, low, jax.ShapeDtypeStruct((rows, width), jnp.float32)],
        scratch_shapes=[pltpu.VMEM((rows, width), jnp.float32)],
        compiler_params=ROOMY,
        cost_estimate=NO_COST,
    )(mlp_low, grad_hidden, w_gate, w_up)


def feature_order(width):
    shape = (8 * width, 8 * width)
    row, col = grid_iota(shape, 0), grid_iota(shape, 1)
    return jnp.where(row == (col % 8) * width + col // 8, 1.0, 0.0).astype(jnp.bfloat16)


def patch_in_kernel(core_ref, bytes_ref, weight_ref, wide_ref, out_ref, rows_ref, order_ref):
    places, feature = wide_ref.shape[0], wide_ref.shape[1] // 8
    chunk = weight_ref.shape[1] // 8
    step = pl.program_id(0)

    @pl.when(step == 0)
    def _():
        order_ref[...] = feature_order(chunk)
        for at in range(feature // 128):
            low = at * 128
            rows_ref[at] = bytes_ref[:, low : low + 128].astype(jnp.float32)
            for j in range(8):
                wide_ref[:, j * feature + low : j * feature + low + 128] = rows_ref[
                    at, pl.ds(j, places, stride=8), :
                ]

    parts = [
        wide_ref[:, pl.ds(pl.multiple_of(j * feature + step * chunk, 128), chunk)]
        for j in range(8)
    ]
    by_byte = jnp.concatenate(parts, axis=1).astype(jnp.bfloat16)
    by_feature = dot_plain(by_byte, order_ref[...]).astype(jnp.bfloat16)
    part = dot_trans(by_feature, weight_ref[...])

    @pl.when(step == 0)
    def _():
        out_ref[...] = part

    @pl.when(step > 0)
    def _():
        out_ref[...] += part


def patch_in(byte_rows, w_patch):
    rows, model_width = byte_rows.shape
    out_width, cols = w_patch.shape
    feature, chunk = cols // 8, 128
    core = lax.axis_index("tp").astype(jnp.int32).reshape(1)
    f32 = jnp.float32
    return pl.pallas_call(
        patch_in_kernel,
        grid_spec=pltpu.PrefetchScalarGridSpec(
            num_scalar_prefetch=1,
            grid=(feature // chunk,),
            in_specs=[
                pl.BlockSpec((rows, feature), lambda i, ref: (0, ref[0])),
                pl.BlockSpec((out_width, 8 * chunk), lambda i, ref: (0, i)),
            ],
            out_specs=[
                pl.BlockSpec((rows // 8, cols), lambda i, ref: (0, 0)),
                pl.BlockSpec((rows // 8, out_width), lambda i, ref: (0, 0)),
            ],
            scratch_shapes=[
                pltpu.VMEM((feature // 128, rows, 128), f32),
                pltpu.VMEM((8 * chunk, 8 * chunk), jnp.bfloat16),
            ],
        ),
        out_shape=[
            jax.ShapeDtypeStruct((rows // 8, cols), f32),
            jax.ShapeDtypeStruct((rows // 8, out_width), f32),
        ],
        compiler_params=ROOMY,
        cost_estimate=NO_COST,
    )(core, byte_rows, w_patch)


def final_kernel(
    member_ref,
    own_ref,
    other_ref,
    mask_ref,
    own_head_ref,
    other_head_ref,
    weight_ref,
    low_ref,
    hidden_ref,
    mine_ref,
    mine_low_ref,
):
    own = (own_ref[...] * mask_ref[...]).astype(jnp.bfloat16)
    other = (other_ref[...] * mask_ref[...]).astype(jnp.bfloat16)
    other_head = other_head_ref[...].astype(jnp.bfloat16)
    total = dot_trans(own, own_head_ref[...]) + dot_trans(other, other_head)
    low = total.astype(jnp.bfloat16)
    low_ref[...] = low
    hidden_ref[...] = dot_plain(low, weight_ref[...])

    @pl.when(pl.program_id(0) == member_ref[0])
    def _():
        mine_ref[...] = total
        mine_low_ref[...] = low


def final_grads(own, other, mask, own_head, other_head, w_down, member):
    rows, cols = own.shape
    width = own_head.shape[0]
    block = rows // QUAD
    units = w_down.shape[1] // QUAD
    f32, bf16 = jnp.float32, jnp.bfloat16

    def by_rows(cols):
        return pl.BlockSpec((block, cols), lambda i, ref: (i, 0))

    head = pl.BlockSpec((width, cols), lambda i, ref: (0, 0))
    mine = pl.BlockSpec((block, width), lambda i, ref: (0, 0))
    return pl.pallas_call(
        final_kernel,
        grid_spec=pltpu.PrefetchScalarGridSpec(
            num_scalar_prefetch=1,
            grid=(QUAD,),
            in_specs=[by_rows(cols), by_rows(cols), by_rows(1), head, head]
            + [pl.BlockSpec((width, units), lambda i, ref: (0, ref[0]))],
            out_specs=[by_rows(width), by_rows(units), mine, mine],
        ),
        out_shape=[
            jax.ShapeDtypeStruct((rows, width), bf16),
            jax.ShapeDtypeStruct((rows, units), f32),
            jax.ShapeDtypeStruct((block, width), f32),
            jax.ShapeDtypeStruct((block, width), bf16),
        ],
        compiler_params=ROOMY,
        cost_estimate=NO_COST,
    )(member, own, other, mask, own_head, other_head, w_down)


def group_mlp_kernel(
    place_ref,
    own_ref,
    other_ref,
    gain_ref,
    grad_ref,
    gate_w_ref,
    up_w_ref,
    in_ref,
    hidden_ref,
    gate_ref,
    up_ref,
):
    own, other = own_ref[0], other_ref[0]
    first = place_ref[1] == 0
    halves = [jnp.where(first, own, other), jnp.where(first, other, own)]
    low = (jnp.concatenate(halves, axis=1) * gain_ref[...]).astype(jnp.bfloat16)
    in_ref[...] = low
    units_in_halves(low, grad_ref, gate_w_ref, up_w_ref, hidden_ref, gate_ref, up_ref)


def group_mlp(own_half, other_half, gain, grad_hidden, w_gate, w_up, member):
    rows, half = grad_hidden.shape[0] // QUAD, own_half.shape[2]
    width, units = 2 * half, w_gate.shape[1] // QUAD
    bf16 = jnp.bfloat16
    place = jnp.concatenate([member, lax.axis_index("tp").astype(jnp.int32).reshape(1)])

    def by_rows(cols):
        return pl.BlockSpec((rows, cols), lambda i, ref: (i, 0))

    halves = pl.BlockSpec((1, rows, half), lambda i, ref: (i, 0, 0))
    weights = pl.BlockSpec((width, units), lambda i, ref: (0, ref[0]))
    low = jax.ShapeDtypeStruct((QUAD * rows, units), bf16)
    return pl.pallas_call(
        group_mlp_kernel,
        grid_spec=pltpu.PrefetchScalarGridSpec(
            num_scalar_prefetch=1,
            grid=(QUAD,),
            in_specs=[
                halves,
                halves,
                pl.BlockSpec((1, width), lambda i, ref: (0, 0)),
                by_rows(units),
                weights,
                weights,
            ],
            out_specs=[by_rows(width), by_rows(units), by_rows(units), by_rows(units)],
        ),
        out_shape=[jax.ShapeDtypeStruct((QUAD * rows, width), bf16), low, low, low],
        compiler_params=ROOMY,
        cost_estimate=NO_COST,
    )(place, own_half, other_half, gain.reshape(1, width), grad_hidden, w_gate, w_up)


def bytes_grad_kernel(core_ref, grad_ref, weight_ref, stream_ref, out_ref, order_ref):
    places = grad_ref.shape[0]
    chunk = weight_ref.shape[1] // 8

    @pl.when(pl.program_id(0) == 0)
    def _():
        order_ref[...] = feature_order(chunk)

    by_feature = dot_plain(grad_ref[...].astype(jnp.bfloat16), weight_ref[...])
    high = by_feature.astype(jnp.bfloat16)
    rest = by_feature - high.astype(jnp.float32)
    mid = rest.astype(jnp.bfloat16)
    low = (rest - mid.astype(jnp.float32)).astype(jnp.bfloat16)
    order = order_ref[...]
    by_byte = dot_trans(high, order) + (dot_trans(mid, order) + dot_trans(low, order))
    for j in range(8):
        rows = pl.ds(j, places, stride=8)
        out_ref[rows, :] = stream_ref[rows, :] + by_byte[:, j * chunk : (j + 1) * chunk]


def bytes_grad(grad_patch, w_patch, grad_stream):
    places, width = grad_patch.shape
    rows = grad_stream.shape[0]
    cols = w_patch.shape[1]
    feature, chunk = cols // 8, 128
    core = lax.axis_index("tp").astype(jnp.int32).reshape(1)
    return pl.pallas_call(
        bytes_grad_kernel,
        grid_spec=pltpu.PrefetchScalarGridSpec(
            num_scalar_prefetch=1,
            grid=(feature // chunk,),
            in_specs=[
                pl.BlockSpec((places, width), lambda i, ref: (0, 0)),
                pl.BlockSpec((width, 8 * chunk), lambda i, ref: (0, i)),
                pl.BlockSpec((rows, chunk), lambda i, ref: (0, ref[0] * (feature // chunk) + i)),
            ],
            out_specs=pl.BlockSpec((rows, chunk), lambda i, ref: (0, i)),
            scratch_shapes=[pltpu.VMEM((8 * chunk, 8 * chunk), jnp.bfloat16)],
        ),
        out_shape=jax.ShapeDtypeStruct((rows, feature), jnp.float32),
        compiler_params=ROOMY,
        cost_estimate=NO_COST,
    )(core, grad_patch, w_patch, grad_stream)


def body(
    byte_states,
    lengths,
    w_patch,
    norm_global,
    w_in,
    conv_w,
    conv_b,
    dt_bias,
    a_log,
    d_skip,
    mix_gain,
    w_out,
    norm_attn,
    w_qkv,
    w_o,
    norm_mlp,
    w_gate,
    w_up,
    w_down,
    w_head,
    d_logits,
):
    streams, local_rows, model_width = byte_states.shape
    patch_count = local_rows // 8
    patch_total = streams * patch_count
    row_total = streams * local_rows
    feature = w_patch.shape[1] // 8
    inner_width = w_out.shape[1]
    channels = conv_w.shape[1]
    head_total = dt_bias.shape[0]
    head_cols = w_head.shape[1]
    parts = lax.axis_size("seq")
    tp_index = lax.axis_index("tp")
    seq_index = lax.axis_index("seq")
    places = parts * patch_count
    f32 = jnp.float32

    lanes = parts // streams
    width = inner_width // lanes
    full_head = inner_width // head_total
    own_heads = max(1, width // full_head)
    shared = max(1, full_head // width)
    head_size = width // own_heads
    own_stream = seq_index // lanes
    first_col = (seq_index % lanes) * width
    first_head = first_col // full_head

    seg_full = segment_ids(lengths, places)
    seg_own = lax.dynamic_slice_in_dim(seg_full, seq_index * patch_count, patch_count, 1)
    seg_stream = lax.dynamic_index_in_dim(seg_full, own_stream, 0, keepdims=False)
    valid = (seg_own < lengths.shape[0]).astype(f32).reshape(patch_total, 1)
    byte_valid = jnp.repeat(valid, 8, axis=0)

    member = (seq_index >> 2 & 1) * 2 + (seq_index & 1)
    raw_logits = d_logits.reshape(row_total, head_cols)
    raw_wide = raw_logits.astype(f32)
    group_valid = []
    for high in range(2):
        for low in range(2):
            device = (seq_index & ~5) | high << 2 | low
            group_seg = lax.dynamic_slice_in_dim(
                seg_full, device * patch_count, patch_count, 1
            )
            group_valid.append((group_seg < lengths.shape[0]).astype(f32))
    group_valid = jnp.stack(group_valid).reshape(QUAD, patch_total, 1)
    group_bytes_valid = jnp.repeat(group_valid.reshape(-1, 1), 8, axis=0)
    group_raw = side_trade(jnp.broadcast_to(raw_wide[None], (QUAD,) + raw_wide.shape))
    group_raw = group_raw.reshape(-1, head_cols)
    other_raw = swap(group_raw, "tp", 1)
    other_head = swap(w_head.astype(f32), "tp", 1)
    place_index = member.astype(jnp.int32).reshape(1)
    bytes_wide, patch_part = patch_in(byte_states.reshape(row_total, model_width), w_patch)
    patch_out = tp_sum(patch_part)
    gain_global = norm_global.astype(f32)
    unit_patch = patch_out * rms_scale(patch_out)
    u_low = (unit_patch * gain_global).astype(jnp.bfloat16)
    half_width = model_width // 2
    proj = dot_plain(u_low, w_in).reshape(streams, patch_count, -1)
    gate_in = proj[..., :inner_width]
    xbc = proj[..., inner_width : inner_width + channels]
    dt_raw = proj[..., inner_width + channels :]

    def by_lane(columns):
        split = columns.reshape(streams, patch_count, lanes, -1)
        return jnp.moveaxis(split, 2, 1).reshape(parts, patch_count, -1)

    def from_lanes(blocks):
        split = blocks.reshape(streams, lanes, patch_count, -1)
        return jnp.moveaxis(split, 1, 2).reshape(streams, patch_count, -1)

    def to_all_lanes(columns):
        wide = jnp.broadcast_to(
            columns[:, None], (streams, lanes, patch_count, columns.shape[-1])
        )
        return wide.reshape(parts, patch_count, -1)

    pad_width = 128 - own_heads
    dt_lanes = by_lane(jnp.repeat(dt_raw, shared, axis=2))
    sent = jnp.concatenate(
        [
            by_lane(xbc[..., :inner_width]),
            to_all_lanes(xbc[..., inner_width:]),
            jnp.pad(dt_lanes, ((0, 0), (0, 0), (0, pad_width))),
        ],
        axis=-1,
    )
    taken = trade(sent)
    grad_logits = after(raw_logits, sent) * byte_valid.astype(jnp.bfloat16)
    group_final, group_grad_hidden, grad_final, grad_mlp_low = final_grads(
        after(group_raw, sent),
        other_raw,
        group_bytes_valid,
        w_head,
        other_head,
        w_down,
        place_index,
    )
    grad_hidden = dot_plain(grad_mlp_low, w_down)
    hidden_part = w_gate.shape[1] // QUAD

    row_side = [
        [device for device in range(parts) if (device >> 1 & 1) == side] for side in range(2)
    ]
    bytes_all = lax.all_gather(
        bytes_wide, "seq", axis=0, axis_index_groups=row_side, tiled=True
    )
    taken = after(taken, grad_hidden, group_grad_hidden).reshape(places, -1)
    scan_width = width + channels - inner_width

    def own_cols(param):
        mine = lax.dynamic_slice_in_dim(param, first_col, width, param.ndim - 1)
        return jnp.concatenate([mine, param[..., inner_width:]], axis=-1).astype(f32)

    def own_head(param):
        return lax.dynamic_slice_in_dim(param, first_head, own_heads, 0).astype(f32)

    use_kernel = places == 512 and width == 128
    if use_kernel:
        padded_seg = jnp.pad(seg_stream, (3, 0), constant_values=-1)
        same = jnp.stack(
            [(padded_seg[k : k + places] == seg_stream).astype(f32) for k in range(3)]
            + [jnp.zeros((places,), f32)] * 5,
            axis=1,
        )
        conv_pack = jnp.concatenate(
            [own_cols(conv_w), own_cols(conv_b)[None], jnp.zeros((3, scan_width), f32)]
        )
        head_pack = jnp.stack(
            [jnp.pad(own_head(dt_bias), (0, 128 - own_heads))]
            + [jnp.pad(own_head(a_log), (0, 128 - own_heads))]
            + [jnp.repeat(own_head(d_skip), head_size)]
            + [jnp.zeros((128,), f32)] * 5
        )
        scan_args = (taken, same, conv_pack, head_pack, seg_stream[:, None], seg_stream[None])
        scanned = scan_forward(scan_args, width)
    else:
        scan_args = (
            taken[:, :scan_width],
            taken[:, scan_width : scan_width + own_heads],
            own_cols(conv_w),
            own_cols(conv_b),
            own_head(dt_bias),
            own_head(a_log),
            own_head(d_skip),
        )
        scanned, scan_back = jax.vjp(partial(scan_heads, seg_stream, head_size), *scan_args)
    result = from_lanes(trade(scanned.reshape(parts, patch_count, width)))
    unit_normed, norm_back = jax.vjp(gated_unit, result, gate_in)
    mix_scale = mix_gain.astype(f32)
    normed_low = (unit_normed * mix_scale).reshape(patch_total, -1).astype(jnp.bfloat16)


    def quarters(columns):
        split = columns.reshape(patch_total, QUAD, -1)
        return jnp.moveaxis(split, 1, 0)

    def by_apart(blocks):
        return [
            lax.dynamic_index_in_dim(blocks, member ^ apart, 0, keepdims=False)
            for apart in range(QUAD)
        ]

    normed_quarters = quarters(unit_normed)
    global_out = patch_out + valid * tp_sum(dot_trans(normed_low, w_out))
    gain_attn = norm_attn.astype(f32)
    gain_mlp = norm_mlp.astype(f32)
    stream_in, attn_in, qkv, mixed_low, attn_part = attn_forward(
        byte_states.reshape(row_total, model_width), global_out, gain_attn, w_qkv, w_o
    )
    after_attn, mlp_low, unit_half = mlp_in(
        stream_in, attn_part, swap(attn_part, "tp", 1), gain_mlp
    )
    hidden_low, grad_gate_low, grad_up_low, grad_mlp_part = mlp_rows(
        after(mlp_low, unit_half), grad_hidden, w_gate, w_up
    )
    half_width = model_width // 2
    to_all = jnp.concatenate([unit_half, unit_patch.reshape(-1, half_width)], axis=0)
    group_sent = jnp.concatenate(
        [
            jnp.broadcast_to(to_all[None], (QUAD,) + to_all.shape),
            normed_quarters.reshape(QUAD, -1, half_width),
        ],
        axis=1,
    )
    group_halves = side_trade(group_sent)
    grad_mlp_other = swap(grad_mlp_part, "tp", 1)
    after_mlp = after_attn + tp_sum(dot_trans(after(hidden_low, grad_mlp_part), w_down))
    final_low = after_mlp.astype(jnp.bfloat16)
    logits = dot_plain(final_low, w_head) * byte_valid
    grad_mid, grad_attn_low, grad_qkv_low, grad_attn_part, grad_norm_mlp = attn_backward(
        after_attn, grad_final, grad_mlp_part, grad_mlp_other, gain_mlp, qkv, w_qkv, w_o
    )
    grad_norm_mlp = grad_norm_mlp.reshape(-1)
    grad_attn_in = tp_sum(grad_attn_part)

    attn_cut = 1024 if grad_qkv_low.shape[1] > 1024 else 128
    attn_in_late = after(attn_in, grad_attn_part, group_halves)
    attn_cols = grad_qkv_low.shape[1]
    attn_blocks = (
        grad_blocks([(attn_in_late, grad_qkv_low, 0, attn_cut)], 0, True),
        grad_blocks(
            [
                (attn_in_late, grad_qkv_low, attn_cut, attn_cols),
                (grad_attn_low, mixed_low, 0, mixed_low.shape[1]),
                (final_low, grad_logits, 0, head_cols),
            ],
            1,
            True,
        ),
    )
    attn_got = [to_partner(attn_blocks[first][0], first) for first in range(2)]
    grad_attn_in = after(grad_attn_in, attn_blocks[0][0], attn_blocks[1][0])
    back_attn, grad_norm_attn = rms_back(stream_in, gain_attn, grad_attn_in)
    grad_stream = grad_mid + back_attn
    grad_global = jnp.sum(grad_stream.reshape(patch_total, 8, model_width), axis=1)
    grad_mix_low = (grad_global * valid).astype(jnp.bfloat16)
    grad_normed = dot_plain(grad_mix_low, w_out).reshape(streams, patch_count, inner_width)
    grad_mix_gain = jnp.sum(grad_normed * unit_normed, axis=(0, 1))
    grad_result, grad_gate_in = norm_back(grad_normed * mix_scale)
    grad_z_low = grad_gate_in.reshape(patch_total, inner_width).astype(jnp.bfloat16)
    row_block = model_width // parts
    dealing = by_lane(grad_result)
    dealt = trade(dealing)
    own_half = after(group_halves, dealing, bytes_all)
    group_in, group_hidden, group_gate, group_up = group_mlp(
        own_half, swap(own_half, "tp", 1), gain_mlp, group_grad_hidden, w_gate, w_up, place_index
    )
    group_rows = own_half[:, row_total : row_total + 2 * patch_total]
    group_rows = group_rows.reshape(QUAD, patch_total, model_width)
    group_u = jnp.concatenate(by_apart(group_rows), axis=0) * gain_global
    group_u = group_u.astype(jnp.bfloat16)
    quarter = inner_width // QUAD
    own_scale = lax.dynamic_slice_in_dim(mix_scale, member * quarter, quarter, 0)
    group_n = own_half[:, row_total + 2 * patch_total :].reshape(QUAD, patch_total, quarter)
    group_n = (jnp.concatenate(by_apart(group_n), axis=0) * own_scale).astype(jnp.bfloat16)

    def group_swap(blocks):
        moved = [swap(block, "seq", mask) for block, mask in zip(blocks[1:], (1, 4, 5))]
        return jnp.concatenate([blocks[0]] + moved, axis=0)

    late_sent = [
        jnp.concatenate([grad_global, part], axis=-1) for part in by_apart(quarters(grad_gate_in))
    ]
    late_got = group_swap(late_sent)
    apart_valid = jnp.concatenate(by_apart(group_valid), axis=0)
    group_mix = (late_got[:, :model_width] * apart_valid).astype(jnp.bfloat16)
    group_z = late_got[:, model_width:]
    mlp_blocks = [
        grad_blocks(
            [(group_final, group_hidden, 0, hidden_part), (group_in, group_gate, 0, hidden_part)],
            1,
            False,
        ),
        grad_blocks(
            [
                (group_in, group_up, 0, hidden_part),
                (group_mix, group_n, 0, group_n.shape[1]),
                (group_u, group_z, 0, group_z.shape[1]),
            ],
            1,
            False,
        ),
    ]
    mlp_got = [to_partner(far, 1) for far, unused in mlp_blocks]
    dealt = after(dealt, mlp_blocks[0][0], mlp_blocks[1][0], *attn_got)
    dealt = dealt.reshape(places, width)
    grad_scanned = dealt[:, :width]
    attn_far = [
        add_side(after(attn_blocks[first][1], dealt), attn_got[first], 1) for first in range(2)
    ]
    attn_crossed = [to_partner(attn_far[first], 1 - first) for first in range(2)]
    grad_scanned = after(grad_scanned, *attn_far)
    if use_kernel:
        back_sent, conv_grads, head_grads = scan_backward(scan_args, grad_scanned)
        lane_grad = back_sent[:, : scan_width + own_heads]
        scan_params = (
            conv_grads[:4],
            conv_grads[4],
            head_grads[0, :own_heads],
            head_grads[1, :own_heads],
            head_grads[2, :own_heads],
        )
    else:
        scan_grads = scan_back(grad_scanned)
        back_sent = jnp.concatenate(
            [scan_grads[0], jnp.pad(scan_grads[1], ((0, 0), (0, pad_width)))], axis=-1
        )
        lane_grad = jnp.concatenate([scan_grads[0], scan_grads[1]], axis=-1)
        scan_params = scan_grads[2:]
    back_sent = back_sent.reshape(parts, patch_count, -1)
    back_taken = after(trade(back_sent), mlp_got[0], *attn_crossed)
    grad_x = from_lanes(back_taken[..., :width])
    by_stream = back_taken.reshape(streams, lanes, patch_count, -1)
    grad_bc = jnp.sum(by_stream[..., width:scan_width], axis=1)
    grad_dt = from_lanes(back_taken[..., scan_width : scan_width + own_heads])
    grad_dt = jnp.sum(grad_dt.reshape(streams, patch_count, head_total, shared), axis=-1)
    high = (seq_index // QUAD).astype(jnp.int32).reshape(1)
    attn_near = near_sums(
        [
            (after(attn_blocks[first][1], back_taken), attn_got[first], attn_crossed[first])
            for first in range(2)
        ],
        high,
    )
    attn_high = [
        swap(attn_near[apart], "seq", QUAD * apart) for apart in range(1, parts // QUAD)
    ]
    grad_shared = jnp.concatenate([grad_bc, grad_dt], axis=-1).reshape(patch_total, -1)
    grad_proj_low = jnp.concatenate(
        [grad_z_low, grad_x.reshape(patch_total, -1).astype(jnp.bfloat16)]
        + [grad_shared.astype(jnp.bfloat16)],
        axis=-1,
    )
    grad_proj_low = after(grad_proj_low, attn_near)
    grad_u_part = dot_trans(grad_proj_low, w_in)
    grad_u = tp_sum(grad_u_part)
    rest = [quarters(columns) for columns in (grad_x, grad_bc, grad_dt)]
    rest_cols = [part.shape[-1] for part in rest]
    rest = after(jnp.concatenate(rest, axis=-1), grad_u_part)
    rest = jnp.pad(rest, ((0, 0), (0, 0), (0, -sum(rest_cols) % 128)))
    rest_blocks = grad_blocks(
        [(group_u, group_swap(by_apart(rest)), 0, rest.shape[-1])], 1, False
    )
    rest_got = to_partner(rest_blocks[0], 1)
    back_global, grad_norm_global = rms_back(patch_out, gain_global, grad_u)
    grad_patch = grad_global + back_global
    side_count = parts // 2
    my_side = seq_index >> 1 & 1
    by_block = jnp.moveaxis(grad_patch.reshape(patch_total, parts, row_block), 1, 0)
    by_block = by_block.reshape(parts // 4, 2, 2, patch_total, row_block)
    same_side = lax.dynamic_index_in_dim(by_block, my_side, 1, keepdims=False)
    other_side = lax.dynamic_index_in_dim(by_block, 1 - my_side, 1, keepdims=False)
    patch_rows = jnp.concatenate([same_side, other_side], axis=-1)
    patch_rows = patch_rows.reshape(side_count, patch_total, 2 * row_block)
    gain_part = grad_norm_global.reshape(-1, 2 * row_block)
    gain_count = gain_part.shape[0]
    patch_sent = jnp.concatenate(
        [patch_rows, jnp.broadcast_to(gain_part, (side_count,) + gain_part.shape)], axis=1
    )
    patch_taken = lax.all_to_all(
        patch_sent, "seq", 0, 0, axis_index_groups=row_side, tiled=True
    )

    gain_side = jnp.sum(patch_taken[:, patch_total:], axis=0)
    patch_cols = patch_taken[:, :patch_total].reshape(-1, 2 * row_block)
    patch_far = patch_far_grad(patch_cols, gain_side, bytes_all)
    small = (
        scan_params[0][:, :width],
        scan_params[1][:width],
        scan_params[0][:, width:],
        scan_params[1][width:],
        scan_params[2],
        scan_params[3],
        scan_params[4],
        grad_mix_gain,
        grad_norm_attn,
        grad_norm_mlp,
    )
    small_count = sum(part.size for part in small)
    flat = after(jnp.concatenate([part.reshape(-1) for part in small]), patch_far)
    flat = jnp.pad(flat, (0, -small_count % 1024)).reshape(1, -1, 128)
    pieces = trade(jnp.broadcast_to(flat, (parts,) + flat.shape[1:])).reshape(parts, -1)
    by_small, at = [], 0
    for part in small:
        got = pieces[:, at : at + part.size].reshape((parts,) + part.shape)
        by_small.append(got)
        at += part.size

    def lane_cols(got):
        joined = jnp.sum(got.reshape((streams, lanes) + got.shape[1:]), axis=0)
        return jnp.moveaxis(joined, 0, -2).reshape(joined.shape[1:-1] + (-1,))

    def lane_heads(got):
        joined = jnp.sum(got.reshape(streams, lanes, -1), axis=0)
        return jnp.sum(joined.reshape(head_total, shared), axis=-1)

    small_sums = [
        jnp.concatenate([lane_cols(by_small[0]), jnp.sum(by_small[2], axis=0)], axis=-1),
        jnp.concatenate([lane_cols(by_small[1]), jnp.sum(by_small[3], axis=0)], axis=-1),
        lane_heads(by_small[4]),
        lane_heads(by_small[5]),
        lane_heads(by_small[6]),
    ] + [jnp.sum(got, axis=0) for got in by_small[7:]]

    patch_got = to_partner(patch_far, 1)

    mlp_finals = []
    for blocks, got, turn in zip(
        mlp_blocks + [rest_blocks], mlp_got + [rest_got], (back_taken, patch_taken, patch_got)
    ):
        near = after(blocks[1], turn)
        for bit in reversed(range(3, seq_bits())):
            far, near = split_add(near, got, bit)
            got = to_partner(far, bit)
        mlp_finals.append(jnp.moveaxis(side_trade(group_add(near, got)), 0, 1))

    def final_cols(final, low, count):
        return final[..., low : low + count].reshape(row_block, -1)

    final_down = final_cols(mlp_finals[0], 0, hidden_part)
    final_gate = final_cols(mlp_finals[0], hidden_part, hidden_part)
    final_up = final_cols(mlp_finals[1], 0, hidden_part)
    final_out = final_cols(mlp_finals[1], hidden_part, quarter)
    final_z = final_cols(mlp_finals[1], hidden_part + quarter, quarter)
    final_x = final_cols(mlp_finals[2], 0, rest_cols[0])
    final_bc = final_cols(mlp_finals[2], rest_cols[0], rest_cols[1])
    final_dt = final_cols(mlp_finals[2], rest_cols[0] + rest_cols[1], rest_cols[2])
    final_patch = patch_grad(patch_cols, patch_got, bytes_all)
    final_attn = attn_near[0]
    for got in attn_high:
        final_attn = final_attn + after(got, final_patch)
    norm_global_sum = (gain_side + patch_got[row_block:, : 2 * row_block]).reshape(-1)
    grad_bytes = bytes_grad(after(grad_patch, patch_far), w_patch, grad_stream)
    grad_bytes = grad_bytes.reshape(streams, local_rows, feature)

    qkv_cols, o_cols = w_qkv.shape[1], w_o.shape[1]
    return (
        logits.reshape(streams, local_rows, head_cols),
        grad_bytes,
        final_patch,
        norm_global_sum,
        jnp.concatenate([final_z, final_x, final_bc, final_dt], axis=1),
        small_sums[0],
        small_sums[1],
        small_sums[2],
        small_sums[3],
        small_sums[4],
        small_sums[5],
        final_out,
        small_sums[6],
        final_attn[:, :qkv_cols],
        final_attn[:, qkv_cols : qkv_cols + o_cols],
        small_sums[7],
        final_gate,
        final_up,
        final_down,
        final_attn[:, qkv_cols + o_cols :],
    )


def solution(mesh):
    in_specs = (
        P(None, "seq", None),
        P(),
        P(None, "tp"),
        P(),
        P(None, "tp"),
        P(None, "tp"),
        P("tp"),
        P("tp"),
        P("tp"),
        P("tp"),
        P("tp"),
        P(None, "tp"),
        P(),
        P(None, "tp"),
        P(None, "tp"),
        P(),
        P(None, "tp"),
        P(None, "tp"),
        P(None, "tp"),
        P(None, "tp"),
        P(None, "seq", "tp"),
    )
    out_specs = (
        P(None, "seq", "tp"),
        P(None, "seq", "tp"),
        P("seq", "tp"),
        P(),
        P("seq", "tp"),
        P(None, "tp"),
        P("tp"),
        P("tp"),
        P("tp"),
        P("tp"),
        P("tp"),
        P("seq", "tp"),
        P(),
        P("seq", "tp"),
        P("seq", "tp"),
        P(),
        P("seq", "tp"),
        P("seq", "tp"),
        P("seq", "tp"),
        P("seq", "tp"),
    )
    return jax.shard_map(body, mesh=mesh, in_specs=in_specs, out_specs=out_specs, check_vma=False)
```

```python
from functools import partial

import jax
import jax.numpy as jnp
from jax import lax
from jax.experimental import pallas as pl
from jax.experimental.pallas import tpu as pltpu
from jax.sharding import PartitionSpec as P

NS = 128
AD = 64
QUAD = 4


NO_COST = pl.CostEstimate(flops=1024, bytes_accessed=1024, transcendentals=0)
ROOMY = pltpu.CompilerParams(vmem_limit_bytes=56 * 1024 * 1024)

epsilon = 1e-05
highest = lax.Precision.HIGHEST
masked_score = -1e30


def dot_plain(left_side, right_side):
    return jnp.dot(left_side, right_side, preferred_element_type=jnp.float32)


def dot_trans(left_side, right_side):
    return lax.dot_general(
        left_side, right_side, (((1,), (1,)), ((), ())), preferred_element_type=jnp.float32
    )


def dot_left(left_side, right_side):
    return lax.dot_general(
        left_side, right_side, (((0,), (0,)), ((), ())), preferred_element_type=jnp.float32
    )


def rms_scale(values):
    return lax.rsqrt(jnp.mean(values * values, axis=-1, keepdims=True) + epsilon)


def hidden_parts(mlp_in, grad_hidden, w_gate, w_up):
    gate_proj = dot_plain(mlp_in, w_gate)
    up_proj = dot_plain(mlp_in, w_up)
    sigmoid_gate = jax.nn.sigmoid(gate_proj)
    hidden_low = (gate_proj * sigmoid_gate * up_proj).astype(jnp.bfloat16)
    grad_gate_low = (
        grad_hidden * up_proj * sigmoid_gate * (1.0 + gate_proj * (1.0 - sigmoid_gate))
    ).astype(jnp.bfloat16)
    grad_up_low = (grad_hidden * gate_proj * sigmoid_gate).astype(jnp.bfloat16)
    return (hidden_low, grad_gate_low, grad_up_low)


def rms_back(values, gain_values, grad_out):
    scale = rms_scale(values)
    scaled = gain_values * grad_out
    inner_mean = jnp.mean(values * scaled, axis=-1, keepdims=True)
    grad_values = scale * scaled - values * scale * scale * scale * inner_mean
    grad_gain = jnp.sum(values * scale * grad_out, axis=0)
    return (grad_values, grad_gain)


def swap(block, axis, mask):
    return lax.ppermute(block, axis, [(i, i ^ mask) for i in range(lax.axis_size(axis))])


def after(value, *earlier):
    return lax.optimization_barrier((value,) + earlier)[0]


def tp_sum(block):
    return block + swap(block, "tp", 1)


def to_partner(block, bit):
    return swap(block, "seq", 1 << bit)


def seq_bits():
    return lax.axis_size("seq").bit_length() - 1


def side_trade(blocks):
    members = [
        [base | high << 2 | low for high in range(2) for low in range(2)]
        for base in range(lax.axis_size("seq"))
        if base & 5 == 0
    ]
    return lax.all_to_all(blocks, "seq", 0, 0, axis_index_groups=members, tiled=True)


def add_kernel(index_ref, *refs):
    total = refs[0][...] + refs[1][...]
    refs[2][...] = total.reshape(refs[2].shape)


def add_side(near, got, side):
    unused, groups, rows, cols = near.shape
    index = jnp.zeros((1,), jnp.int32)
    block = pl.BlockSpec((1, 1, rows, cols), lambda i, ref: (side, i, 0, 0))
    return pl.pallas_call(
        add_kernel,
        grid_spec=pltpu.PrefetchScalarGridSpec(
            num_scalar_prefetch=1,
            grid=(groups,),
            in_specs=[block, block],
            out_specs=pl.BlockSpec((1, rows, cols), lambda i, ref: (i, 0, 0)),
        ),
        out_shape=jax.ShapeDtypeStruct((groups, rows, cols), jnp.float32),
        compiler_params=ROOMY,
        cost_estimate=NO_COST,
    )(index, near, got)


def near_kernel(index_ref, *refs):
    out_ref = refs[-1]
    at = 0
    for near_ref, got_ref, crossed_ref in zip(refs[0:-1:3], refs[1:-1:3], refs[2:-1:3]):
        cols = near_ref.shape[3]
        total = near_ref[0, 0] + got_ref[0, 0] + crossed_ref[0]
        out_ref[0, :, at : at + cols] = total
        at += cols


def near_sums(terms, high):
    unused, groups, rows, unused_cols = terms[0][0].shape
    cols = [term[0].shape[3] for term in terms]
    specs, operands = [], []
    for (near, got, crossed), count in zip(terms, cols):
        four = pl.BlockSpec((1, 1, rows, count), lambda i, ref: (0, ref[0] ^ i, 0, 0))
        three = pl.BlockSpec((1, rows, count), lambda i, ref: (ref[0] ^ i, 0, 0))
        specs += [four, four, three]
        operands += [near, got, crossed]
    return pl.pallas_call(
        near_kernel,
        grid_spec=pltpu.PrefetchScalarGridSpec(
            num_scalar_prefetch=1,
            grid=(groups,),
            in_specs=specs,
            out_specs=pl.BlockSpec((1, rows, sum(cols)), lambda i, ref: (i, 0, 0)),
        ),
        out_shape=jax.ShapeDtypeStruct((groups, rows, sum(cols)), jnp.float32),
        compiler_params=ROOMY,
        cost_estimate=NO_COST,
    )(high, *operands)


def split_kernel(index_ref, far_a, far_b, near_a, near_b, far_ref, near_ref):
    far_ref[...] = far_a[...] + far_b[...]
    near_ref[...] = near_a[...] + near_b[...]


def split_add(first, second, bit):
    half = first.shape[0] // 2
    rest = first.shape[1:]
    zeros = (0,) * len(rest)
    mine = (lax.axis_index("seq") >> bit & 1).astype(jnp.int32).reshape(1)
    far = pl.BlockSpec((1,) + rest, lambda i, ref: ((1 - ref[0]) * half + i,) + zeros)
    near = pl.BlockSpec((1,) + rest, lambda i, ref: (ref[0] * half + i,) + zeros)
    out = jax.ShapeDtypeStruct((half,) + rest, jnp.float32)
    block = pl.BlockSpec((1,) + rest, lambda i, ref: (i,) + zeros)
    return pl.pallas_call(
        split_kernel,
        grid_spec=pltpu.PrefetchScalarGridSpec(
            num_scalar_prefetch=1,
            grid=(half,),
            in_specs=[far, far, near, near],
            out_specs=[block, block],
        ),
        out_shape=[out, out],
        compiler_params=ROOMY,
        cost_estimate=NO_COST,
    )(mine, first, second, first, second)


def group_add(first, second):
    members, rows, cols = QUAD, first.shape[-2], first.shape[-1]
    block = pl.BlockSpec((1, rows, cols), lambda i, ref: (i, 0, 0))
    shape = (members, rows, cols)
    return pl.pallas_call(
        add_kernel,
        grid_spec=pltpu.PrefetchScalarGridSpec(
            num_scalar_prefetch=1, grid=(members,), in_specs=[block, block], out_specs=block
        ),
        out_shape=jax.ShapeDtypeStruct(shape, jnp.float32),
        compiler_params=ROOMY,
        cost_estimate=NO_COST,
    )(jnp.zeros((1,), jnp.int32), first.reshape(shape), second.reshape(shape))


def grad_blocks_kernel(pairs, first, relative, rows, member_ref, *refs):
    lefts, rights = refs[: len(pairs)], refs[len(pairs) : 2 * len(pairs)]
    far_ref, near_ref = refs[2 * len(pairs) :]
    other = 1 - first
    at = 0
    for left_ref, right_ref, (low, high) in zip(lefts, rights, pairs):
        got = dot_left(left_ref[...], right_ref[:, low:high].astype(jnp.bfloat16))
        places = slice(at, at + high - low)
        for block in range(got.shape[0] // rows):
            place, member = block // QUAD, block % QUAD
            part = got[block * rows : (block + 1) * rows]
            apart = member_ref[0] ^ member
            is_far = apart >> first & 1
            if relative:
                side = apart >> other & 1
            else:
                side = member >> other & 1

            @pl.when(is_far == 1)
            def _():
                if relative:
                    far_ref[side, place, :, places] = part
                else:
                    far_ref[place, side, :, places] = part

            @pl.when(is_far == 0)
            def _():
                if relative:
                    near_ref[side, place, :, places] = part
                else:
                    near_ref[place, side, :, places] = part

        at += high - low


def grad_blocks(terms, first, relative):
    parts = lax.axis_size("seq")
    groups = parts // QUAD
    model_width = terms[0][0].shape[1]
    rows = model_width // parts
    cols = max(128, QUAD * rows)
    places = cols // (QUAD * rows)
    pairs = [(low, high) for unused, unused_right, low, high in terms]
    total = sum(high - low for low, high in pairs)
    member = (lax.axis_index("seq") % QUAD).astype(jnp.int32).reshape(1)
    if relative:
        shape, block = (2, groups, rows, total), (2, places, rows, total)
        out_spec = pl.BlockSpec(block, lambda i, ref: (0, i, 0, 0))
    else:
        shape, block = (groups, 2, rows, total), (places, 2, rows, total)
        out_spec = pl.BlockSpec(block, lambda i, ref: (i, 0, 0, 0))
    out = jax.ShapeDtypeStruct(shape, jnp.float32)
    return pl.pallas_call(
        partial(grad_blocks_kernel, pairs, first, relative, rows),
        grid_spec=pltpu.PrefetchScalarGridSpec(
            num_scalar_prefetch=1,
            grid=(model_width // cols,),
            in_specs=[
                pl.BlockSpec((term[0].shape[0], cols), lambda i, ref: (0, i)) for term in terms
            ]
            + [pl.BlockSpec(term[1].shape, lambda i, ref: (0, 0)) for term in terms],
            out_specs=[out_spec, out_spec],
        ),
        out_shape=[out, out],
        compiler_params=ROOMY,
        cost_estimate=NO_COST,
    )(member, *[term[0] for term in terms], *[term[1] for term in terms])


def segment_ids(lengths, place_count):
    ends = jnp.cumsum(lengths // 8, dtype=jnp.int32)
    places = jnp.arange(place_count, dtype=jnp.int32)
    short_ids = jnp.sum(
        (places[:, None] >= ends[None, :]).astype(jnp.int32), axis=1, dtype=jnp.int32
    )
    return jnp.stack([jnp.zeros_like(short_ids), short_ids])


def scan_heads(seg_now, head_size, xbc, dt_raw, conv_weight, conv_bias, dt_shift, a_logs, skips):
    place_count = xbc.shape[0]
    conv_sum = conv_bias + conv_weight[3] * xbc
    for offset in range(3):
        distance = 3 - offset
        earlier = jnp.pad(xbc, ((distance, 0), (0, 0)))[:place_count]
        seg_earlier = jnp.pad(seg_now, (distance, 0), constant_values=-1)[:place_count]
        same_doc = (seg_earlier == seg_now).astype(jnp.float32)
        conv_sum = conv_sum + conv_weight[offset] * earlier * same_doc[:, None]
    active = jax.nn.silu(conv_sum)
    head_count = dt_raw.shape[1]
    inner = head_count * head_size
    values = active[:, :inner].reshape(place_count, head_count, head_size)
    in_keys = active[:, inner : inner + NS]
    out_keys = active[:, inner + NS :]
    step_sizes = jax.nn.softplus(dt_raw + dt_shift)
    decay_rates = -step_sizes * jnp.exp(a_logs)
    chunk = min(place_count, 512)
    triangle = jnp.tril(jnp.ones((chunk, chunk), jnp.float32))
    state = jnp.zeros((head_count, head_size, NS), jnp.float32)
    seg_last = jnp.int32(-1)
    outputs = []
    for start in range(0, place_count, chunk):
        stop = start + chunk
        x, b, c = values[start:stop], in_keys[start:stop], out_keys[start:stop]
        dt, seg = step_sizes[start:stop], seg_now[start:stop]
        cumulative = jnp.dot(triangle, decay_rates[start:stop], precision=highest)
        allowed = (triangle > 0.0) & (seg[:, None] == seg[None, :])
        ordered = cumulative.T
        gaps = ordered[:, :, None] - ordered[:, None, :]
        decays = jnp.where(allowed, jnp.exp(jnp.where(allowed, gaps, 0.0)), 0.0)
        crossing = jnp.einsum("pn,jn->pj", c, b, precision=highest)
        mixing = crossing[None] * decays * dt.T[:, None, :]
        result = jnp.einsum("hpj,jhd->phd", mixing, x, precision=highest)
        if start > 0:
            entering = jnp.exp(cumulative) * (seg == seg_last).astype(jnp.float32)[:, None]
            result = result + entering[..., None] * jnp.einsum(
                "pn,hdn->phd", c, state, precision=highest
            )
        if stop < place_count:
            last_same = (seg == seg[-1]).astype(jnp.float32)[:, None]
            weight = jnp.exp(cumulative[-1:] - cumulative) * last_same * dt
            through = jnp.exp(cumulative[-1]) * (seg[-1] == seg_last).astype(jnp.float32)
            state = through[:, None, None] * state + jnp.einsum(
                "jh,jhd,jn->hdn", weight, x, b, precision=highest
            )
            seg_last = seg[-1]
        outputs.append(result + skips[:, None] * x)
    return jnp.concatenate(outputs, axis=0).reshape(place_count, inner)


def gated_unit(result, gate_in):
    gated = result * jax.nn.silu(gate_in)
    return gated * rms_scale(gated)


def patch_far_kernel(grad_ref, gain_ref, bytes_ref, out_ref):
    half = grad_ref.shape[1] // 2
    grad_low = grad_ref[:, half:].astype(jnp.bfloat16)
    out_ref[:half] = dot_left(grad_low, bytes_ref[...].astype(jnp.bfloat16))
    out_ref[half:] = jnp.zeros((out_ref.shape[0] - half, out_ref.shape[1]), jnp.float32)

    @pl.when(pl.program_id(0) == 0)
    def _():
        out_ref[half:, : 2 * half] = gain_ref[...]


def patch_far_grad(grad_rows, gain_part, bytes_all):
    places, cols = grad_rows.shape
    total = bytes_all.shape[1]
    rows = cols // 2 + gain_part.shape[0]
    block = 1024
    return pl.pallas_call(
        patch_far_kernel,
        grid=(total // block,),
        in_specs=[
            pl.BlockSpec((places, cols), lambda i: (0, 0)),
            pl.BlockSpec(gain_part.shape, lambda i: (0, 0)),
            pl.BlockSpec((places, block), lambda i: (0, i)),
        ],
        out_specs=pl.BlockSpec((rows, block), lambda i: (0, i)),
        out_shape=jax.ShapeDtypeStruct((rows, total), jnp.float32),
        compiler_params=ROOMY,
        cost_estimate=NO_COST,
    )(grad_rows, gain_part, bytes_all)


def patch_grad_kernel(grad_ref, *refs):
    byte_refs, got_refs, out_ref, order_ref = refs[:8], refs[8:16], refs[16], refs[17]
    width = byte_refs[0].shape[1]

    @pl.when(pl.program_id(0) == 0)
    def _():
        order_ref[...] = feature_order(width)

    grad_low = grad_ref[:, : grad_ref.shape[1] // 2].astype(jnp.bfloat16)
    wide = jnp.concatenate([ref[...].astype(jnp.bfloat16) for ref in byte_refs], axis=1)
    rows = grad_low.shape[1]
    grad = dot_left(grad_low, wide)
    grad = grad + jnp.concatenate([ref[:rows] for ref in got_refs], axis=1)
    high = grad.astype(jnp.bfloat16)
    rest = grad - high.astype(jnp.float32)
    mid = rest.astype(jnp.bfloat16)
    low = (rest - mid.astype(jnp.float32)).astype(jnp.bfloat16)
    order = order_ref[...]
    out_ref[...] = dot_plain(high, order) + (dot_plain(mid, order) + dot_plain(low, order))


def patch_grad(grad_rows, got, bytes_all):
    places, cols = grad_rows.shape
    feature = bytes_all.shape[1] // 8
    chunk = 128
    steps = feature // chunk

    def byte_specs(rows):
        return [
            pl.BlockSpec((rows, chunk), partial(lambda j, i: (0, j * steps + i), j))
            for j in range(8)
        ]

    return pl.pallas_call(
        patch_grad_kernel,
        grid=(steps,),
        in_specs=[pl.BlockSpec((places, cols), lambda i: (0, 0))]
        + byte_specs(places)
        + byte_specs(got.shape[0]),
        out_specs=pl.BlockSpec((cols // 2, 8 * chunk), lambda i: (0, i)),
        out_shape=jax.ShapeDtypeStruct((cols // 2, 8 * feature), jnp.float32),
        scratch_shapes=[pltpu.VMEM((8 * chunk, 8 * chunk), jnp.bfloat16)],
        compiler_params=ROOMY,
        cost_estimate=NO_COST,
    )(grad_rows, *([bytes_all] * 8), *([got] * 8))


def trade(blocks):
    return lax.all_to_all(blocks, "seq", 0, 0, tiled=True)


def grid_iota(shape, axis):
    return lax.broadcasted_iota(jnp.int32, shape, axis)


def dot_fine(left_side, right_side, left_axis, right_axis):
    return lax.dot_general(
        left_side,
        right_side,
        (((left_axis,), (right_axis,)), ((), ())),
        preferred_element_type=jnp.float32,
        precision=highest,
    )


def shifted_down(block, distance):
    rows = grid_iota(block.shape, 0)
    return jnp.where(rows >= distance, pltpu.roll(block, distance, 0), 0.0)


def shifted_up(block, distance):
    count = block.shape[0]
    rows = grid_iota(block.shape, 0)
    return jnp.where(rows < count - distance, pltpu.roll(block, count - distance, 0), 0.0)


def scan_terms(taken_ref, same_ref, conv_ref, head_ref):
    places = taken_ref.shape[0]
    channels = conv_ref.shape[1]
    xbc = taken_ref[:, :channels]
    conv_sum = conv_ref[4:5] + conv_ref[3:4] * xbc
    for k in range(3):
        earlier = shifted_down(xbc, 3 - k) * same_ref[:, k : k + 1]
        conv_sum = conv_sum + conv_ref[k : k + 1] * earlier
    gate = jax.nn.sigmoid(conv_sum)
    active = conv_sum * gate
    raw = taken_ref[:, channels:] + head_ref[0:1]
    steps = jnp.maximum(raw, 0.0) + jnp.log1p(jnp.exp(-jnp.abs(raw)))
    rates = -steps * jnp.exp(head_ref[1:2])
    square = (places, places)
    triangle = jnp.where(grid_iota(square, 0) >= grid_iota(square, 1), 1.0, 0.0)
    running = dot_fine(triangle, rates, 1, 0)
    return xbc, conv_sum, gate, active, raw, steps, rates, triangle, running


def scan_forward_kernel(taken_ref, same_ref, conv_ref, head_ref, seg_col, seg_row, out_ref):
    places, width = out_ref.shape
    terms = scan_terms(taken_ref, same_ref, conv_ref, head_ref)
    active, steps, running = terms[3], terms[5], terms[8]
    values = active[:, :width]
    keys, reads = active[:, width : width + NS], active[:, width + NS :]
    steps_row, running_row = steps.T, running.T
    heads = width // 64
    rows = 128
    for first in range(0, places, rows):
        last = first + rows
        shape = (rows, last)
        allowed = (seg_col[first:last] == seg_row[:, :last]) & (
            grid_iota(shape, 0) + first >= grid_iota(shape, 1)
        )
        crossing = dot_fine(reads[first:last], keys[:last], 1, 1)
        lane = grid_iota((rows, width), 1) // 64
        total = head_ref[2:3] * values[first:last]
        for h in range(heads):
            gaps = running[first:last, h : h + 1] - running_row[h : h + 1, :last]
            decays = jnp.exp(jnp.where(allowed, gaps, masked_score))
            mixing = crossing * decays * steps_row[h : h + 1, :last]
            part = dot_fine(mixing, values[:last], 1, 0)
            total = total + jnp.where(lane == h, part, 0.0)
        out_ref[first:last] = total


def scan_backward_kernel(
    taken_ref,
    same_ref,
    conv_ref,
    head_ref,
    seg_col,
    seg_row,
    grad_ref,
    out_ref,
    conv_grad_ref,
    head_grad_ref,
    values_grad,
    keys_grad,
    reads_grad,
    rows_grad,
    cols_grad,
):
    places, width = values_grad.shape
    terms = scan_terms(taken_ref, same_ref, conv_ref, head_ref)
    xbc, conv_sum, gate, active, raw, steps, rates, triangle, running = terms
    channels = xbc.shape[1]
    values = active[:, :width]
    keys, reads = active[:, width : width + NS], active[:, width + NS :]
    steps_row, running_row = steps.T, running.T
    heads = width // 64
    rows = 128
    grad = grad_ref[...]
    values_grad[...] = head_ref[2:3] * grad
    keys_grad[...] = jnp.zeros_like(keys_grad)
    rows_grad[...] = jnp.zeros_like(rows_grad)
    cols_grad[...] = jnp.zeros_like(cols_grad)
    for first in range(0, places, rows):
        last = first + rows
        shape = (rows, last)
        allowed = (seg_col[first:last] == seg_row[:, :last]) & (
            grid_iota(shape, 0) + first >= grid_iota(shape, 1)
        )
        crossing = dot_fine(reads[first:last], keys[:last], 1, 1)
        crossing_grad = jnp.zeros(shape, jnp.float32)
        grad_rows = grad[first:last]
        lane = grid_iota((rows, width), 1) // 64
        wide_lane = grid_iota((last, width), 1) // 64
        column = grid_iota((rows, 128), 1)
        down = jnp.zeros((rows, 128), jnp.float32)
        for h in range(heads):
            gaps = running[first:last, h : h + 1] - running_row[h : h + 1, :last]
            decays = jnp.exp(jnp.where(allowed, gaps, masked_score))
            step_row = steps_row[h : h + 1, :last]
            weighted = decays * step_row
            mixing = crossing * weighted
            own_grad = jnp.where(lane == h, grad_rows, 0.0)
            mixing_grad = dot_fine(own_grad, values[:last], 1, 1)
            back = dot_fine(mixing, own_grad, 0, 0)
            values_grad[:last] += jnp.where(wide_lane == h, back, 0.0)
            crossing_grad = crossing_grad + mixing_grad * weighted
            step_part = jnp.sum(mixing_grad * crossing * decays, axis=0, keepdims=True)
            gap_part = mixing_grad * mixing
            down = jnp.where(column == h, jnp.sum(gap_part, axis=1, keepdims=True), down)
            cols_grad[h : h + 1, :last] += step_part
            cols_grad[heads + h : heads + h + 1, :last] += step_part * step_row
        rows_grad[first:last] += down
        reads_grad[first:last] = dot_fine(crossing_grad, keys[:last], 1, 0)
        keys_grad[:last] += dot_fine(crossing_grad, reads[first:last], 0, 0)
    turned = cols_grad[...].T
    column = grid_iota(turned.shape, 1)
    step_grad = jnp.where(column < heads, turned, 0.0)
    ended = pltpu.roll(turned, turned.shape[1] - heads, 1)
    running_grad = jnp.where(column < heads, rows_grad[...] - ended, 0.0)
    rates_grad = dot_fine(triangle, running_grad, 0, 0)
    step_grad = step_grad - rates_grad * jnp.exp(head_ref[1:2])
    raw_grad = step_grad * jax.nn.sigmoid(raw)
    out_ref[:, channels:] = raw_grad
    lane = grid_iota((places, width), 1) // 64
    product = jnp.sum(grad * values, axis=0, keepdims=True)
    head_grad_ref[...] = jnp.zeros_like(head_grad_ref)
    head_grad_ref[0:1] = jnp.sum(raw_grad, axis=0, keepdims=True)
    head_grad_ref[1:2] = jnp.sum(rates_grad * rates, axis=0, keepdims=True)
    skip_lane = grid_iota((1, width), 1)
    skip_grad = jnp.zeros((1, width), jnp.float32)
    for h in range(heads):
        own = jnp.sum(jnp.where(skip_lane // 64 == h, product, 0.0), axis=1, keepdims=True)
        skip_grad = jnp.where(skip_lane == h, own, skip_grad)
    head_grad_ref[2:3] = skip_grad
    active_grad = jnp.concatenate([values_grad[...], keys_grad[...], reads_grad[...]], axis=1)
    conv_grad = active_grad * gate * (1.0 + conv_sum * (1.0 - gate))
    back = conv_ref[3:4] * conv_grad
    conv_grad_ref[...] = jnp.zeros_like(conv_grad_ref)
    conv_grad_ref[3:4] = jnp.sum(conv_grad * xbc, axis=0, keepdims=True)
    conv_grad_ref[4:5] = jnp.sum(conv_grad, axis=0, keepdims=True)
    for k in range(3):
        kept = conv_grad * same_ref[:, k : k + 1]
        back = back + conv_ref[k : k + 1] * shifted_up(kept, 3 - k)
        conv_grad_ref[k : k + 1] = jnp.sum(
            kept * shifted_down(xbc, 3 - k), axis=0, keepdims=True
        )
    out_ref[:, :channels] = back


def scan_forward(args, width):
    places = args[0].shape[0]
    return pl.pallas_call(
        scan_forward_kernel,
        out_shape=jax.ShapeDtypeStruct((places, width), jnp.float32),
        compiler_params=ROOMY,
        cost_estimate=NO_COST,
    )(*args)


def scan_backward(args, grad):
    places, width = grad.shape
    channels = args[2].shape[1]
    f32 = jnp.float32
    return pl.pallas_call(
        scan_backward_kernel,
        out_shape=[
            jax.ShapeDtypeStruct((places, channels + 128), f32),
            jax.ShapeDtypeStruct((8, channels), f32),
            jax.ShapeDtypeStruct((8, 128), f32),
        ],
        scratch_shapes=[
            pltpu.VMEM((places, width), f32),
            pltpu.VMEM((places, NS), f32),
            pltpu.VMEM((places, NS), f32),
            pltpu.VMEM((places, 128), f32),
            pltpu.VMEM((128, places), f32),
        ],
        compiler_params=ROOMY,
        cost_estimate=NO_COST,
    )(*args, grad)


def patch_lanes(block):
    shape = (block // 8, 8, block)
    return grid_iota(shape, 0) == grid_iota(shape, 2) // 8


def folded(scores, same_patch):
    split = scores.reshape(same_patch.shape)
    return jnp.sum(jnp.where(same_patch, split, 0.0), axis=0)


def unfolded(rows, same_patch):
    spread = jnp.where(same_patch, rows[None], 0.0)
    return spread.reshape(-1, rows.shape[1]).astype(jnp.bfloat16)


def softmax_rows(scores, causal):
    scores = jnp.where(causal, scores, masked_score)
    top = jnp.max(scores, axis=1, keepdims=True)
    powers = jnp.exp(scores - top)
    return powers / jnp.sum(powers, axis=1, keepdims=True)


def head_places(rows, head_cols, block):
    return [
        (slice(first, first + block), [j * head_cols + pair * 128 for j in range(3)])
        for first in range(0, rows, block)
        for pair in range(head_cols // 128)
    ]


def all_scores(qkv_ref, places, lane, same_patch):
    scores = []
    for rows, (query, key, unused) in places:
        queries = qkv_ref[rows, query : query + 128] * 0.125
        keys = qkv_ref[rows, key : key + 128]
        for h in range(2):
            own = jnp.where(lane == h, queries, 0)
            scores.append(folded(dot_trans(keys, own), same_patch))
    return jnp.stack(scores)


def attn_forward_kernel(
    bytes_ref, patch_ref, gain_ref, qkv_w_ref, o_w_ref, x_ref, a_ref, qkv_ref, o_ref, out_ref
):
    rows = bytes_ref.shape[0]
    spread = jnp.broadcast_to(patch_ref[...][:, None], (rows // 8, 8, patch_ref.shape[1]))
    x = bytes_ref[...].astype(jnp.float32) + spread.reshape(bytes_ref.shape)
    x_ref[...] = x
    attn_in = (x * rms_scale(x) * gain_ref[...]).astype(jnp.bfloat16)
    a_ref[...] = attn_in
    qkv_ref[...] = dot_plain(attn_in, qkv_w_ref[...]).astype(jnp.bfloat16)
    head_cols = o_ref.shape[1]
    block = 128
    same_patch = patch_lanes(block)
    causal = grid_iota((8, block), 0) <= grid_iota((8, block), 1) % 8
    lane = grid_iota((block, 128), 1) // AD
    places = head_places(rows, head_cols, block)
    probs = softmax_rows(all_scores(qkv_ref, places, lane, same_patch), causal)
    for at, (row_place, (query, unused, value)) in enumerate(places):
        values = qkv_ref[row_place, value : value + 128]
        parts = [dot_left(unfolded(probs[2 * at + h], same_patch), values) for h in range(2)]
        total = jnp.where(lane == 0, parts[0], parts[1])
        o_ref[row_place, query : query + 128] = total.astype(jnp.bfloat16)
    out_ref[...] = dot_trans(o_ref[...], o_w_ref[...])


def attn_forward(bytes_rows, patch_rows, gain, w_qkv, w_o):
    rows, width = bytes_rows.shape
    block = 256
    cols, head_cols = w_qkv.shape[1], w_o.shape[1]
    f32, bf16 = jnp.float32, jnp.bfloat16

    def by_rows(cols):
        return pl.BlockSpec((block, cols), lambda i: (i, 0))

    def whole(shape):
        return pl.BlockSpec(shape, lambda i: (0, 0))

    return pl.pallas_call(
        attn_forward_kernel,
        grid=(rows // block,),
        in_specs=[
            by_rows(width),
            pl.BlockSpec((block // 8, width), lambda i: (i, 0)),
            whole((1, width)),
            whole(w_qkv.shape),
            whole(w_o.shape),
        ],
        out_specs=[by_rows(width), by_rows(width), by_rows(cols), by_rows(head_cols), by_rows(width)],
        out_shape=[
            jax.ShapeDtypeStruct((rows, width), f32),
            jax.ShapeDtypeStruct((rows, width), bf16),
            jax.ShapeDtypeStruct((rows, cols), bf16),
            jax.ShapeDtypeStruct((rows, head_cols), bf16),
            jax.ShapeDtypeStruct((rows, width), f32),
        ],
        compiler_params=ROOMY,
        cost_estimate=NO_COST,
    )(bytes_rows, patch_rows, gain.reshape(1, width), w_qkv, w_o)


def attn_backward_kernel(
    x_ref,
    final_ref,
    own_ref,
    other_ref,
    gain_ref,
    qkv_ref,
    qkv_w_ref,
    o_w_ref,
    mid_ref,
    low_ref,
    qkv_grad_ref,
    out_ref,
    gain_grad_ref,
):
    rows = x_ref.shape[0]
    back, gain_grad = rms_back(x_ref[...], gain_ref[...], own_ref[...] + other_ref[...])
    mid = final_ref[...] + back
    mid_ref[...] = mid
    low_ref[...] = mid.astype(jnp.bfloat16)
    gain_grad = gain_grad.reshape(1, -1)

    @pl.when(pl.program_id(0) == 0)
    def _():
        gain_grad_ref[...] = gain_grad

    @pl.when(pl.program_id(0) > 0)
    def _():
        gain_grad_ref[...] += gain_grad

    mixed_grad = dot_plain(low_ref[...], o_w_ref[...]).astype(jnp.bfloat16)
    head_cols = mixed_grad.shape[1]
    block = 128
    same_patch = patch_lanes(block)
    causal = grid_iota((8, block), 0) <= grid_iota((8, block), 1) % 8
    lane = grid_iota((block, 128), 1) // AD
    places = head_places(rows, head_cols, block)
    probs = softmax_rows(all_scores(qkv_ref, places, lane, same_patch), causal)
    probs_grads = []
    for row_place, (query, unused, value) in places:
        values = qkv_ref[row_place, value : value + 128]
        out_grad = mixed_grad[row_place, query : query + 128]
        for h in range(2):
            own_grad = jnp.where(lane == h, out_grad, 0)
            probs_grads.append(folded(dot_trans(values, own_grad), same_patch))
    probs_grad = jnp.stack(probs_grads)
    inner = jnp.sum(probs * probs_grad, axis=1, keepdims=True)
    scores_grad = probs * (probs_grad - inner)
    for at, (row_place, cols) in enumerate(places):
        query, key, unused = cols
        queries = qkv_ref[row_place, query : query + 128]
        keys = qkv_ref[row_place, key : key + 128]
        out_grad = mixed_grad[row_place, query : query + 128]
        parts = []
        for h in range(2):
            own_scores = unfolded(scores_grad[2 * at + h], same_patch)
            parts.append(
                (
                    dot_left(own_scores, keys) * 0.125,
                    dot_plain(own_scores, queries) * 0.125,
                    dot_plain(unfolded(probs[2 * at + h], same_patch), out_grad),
                )
            )
        for j in range(3):
            grad = jnp.where(lane == 0, parts[0][j], parts[1][j])
            qkv_grad_ref[row_place, cols[j] : cols[j] + 128] = grad.astype(jnp.bfloat16)
    out_ref[...] = dot_trans(qkv_grad_ref[...], qkv_w_ref[...])


def attn_backward(x_rows, final_grad, own_part, other_part, gain, qkv, w_qkv, w_o):
    rows, width = x_rows.shape
    block = 256
    cols = w_qkv.shape[1]
    f32, bf16 = jnp.float32, jnp.bfloat16

    def by_rows(cols):
        return pl.BlockSpec((block, cols), lambda i: (i, 0))

    def whole(shape):
        return pl.BlockSpec(shape, lambda i: (0, 0))

    return pl.pallas_call(
        attn_backward_kernel,
        grid=(rows // block,),
        in_specs=[by_rows(width)] * 4
        + [whole((1, width)), by_rows(cols), whole(w_qkv.shape), whole(w_o.shape)],
        out_specs=[
            by_rows(width),
            by_rows(width),
            by_rows(cols),
            by_rows(width),
            whole((1, width)),
        ],
        out_shape=[
            jax.ShapeDtypeStruct((rows, width), f32),
            jax.ShapeDtypeStruct((rows, width), bf16),
            jax.ShapeDtypeStruct((rows, cols), bf16),
            jax.ShapeDtypeStruct((rows, width), f32),
            jax.ShapeDtypeStruct((1, width), f32),
        ],
        compiler_params=ROOMY,
        cost_estimate=NO_COST,
    )(x_rows, final_grad, own_part, other_part, gain.reshape(1, width), qkv, w_qkv, w_o)


def mlp_in_kernel(core_ref, x_ref, own_ref, other_ref, gain_ref, out_ref, low_ref, half_ref):
    x = x_ref[...] + (own_ref[...] + other_ref[...])
    out_ref[...] = x
    unit = x * rms_scale(x)
    low_ref[...] = (unit * gain_ref[...]).astype(jnp.bfloat16)
    width = half_ref.shape[1]
    half_ref[...] = jnp.where(core_ref[0] == 0, unit[:, :width], unit[:, width:])


def mlp_in(x_rows, own_part, other_part, gain):
    rows, width = x_rows.shape
    block = 128
    core = lax.axis_index("tp").astype(jnp.int32).reshape(1)

    def by_rows(cols):
        return pl.BlockSpec((block, cols), lambda i, ref: (i, 0))

    return pl.pallas_call(
        mlp_in_kernel,
        grid_spec=pltpu.PrefetchScalarGridSpec(
            num_scalar_prefetch=1,
            grid=(rows // block,),
            in_specs=[by_rows(width)] * 3 + [pl.BlockSpec((1, width), lambda i, ref: (0, 0))],
            out_specs=[by_rows(width), by_rows(width), by_rows(width // 2)],
        ),
        out_shape=[
            jax.ShapeDtypeStruct((rows, width), jnp.float32),
            jax.ShapeDtypeStruct((rows, width), jnp.bfloat16),
            jax.ShapeDtypeStruct((rows, width // 2), jnp.float32),
        ],
        compiler_params=ROOMY,
        cost_estimate=NO_COST,
    )(core, x_rows, own_part, other_part, gain.reshape(1, width))


def units_in_halves(
    mlp_low, grad_ref, gate_w_ref, up_w_ref, hidden_ref, gate_ref, up_ref
):
    half = grad_ref.shape[1] // 2
    for at in range(2):
        cols = slice(at * half, (at + 1) * half)
        hidden, gate, up = hidden_parts(
            mlp_low, grad_ref[:, cols], gate_w_ref[:, cols], up_w_ref[:, cols]
        )
        hidden_ref[:, cols] = hidden
        gate_ref[:, cols] = gate
        up_ref[:, cols] = up


def mlp_kernel(
    in_ref, grad_ref, gate_w_ref, up_w_ref, hidden_ref, gate_ref, up_ref, out_ref, total_ref
):
    mlp_low = in_ref[...]
    units_in_halves(
        mlp_low, grad_ref, gate_w_ref, up_w_ref, hidden_ref, gate_ref, up_ref
    )
    part = dot_trans(gate_ref[...], gate_w_ref[...]) + dot_trans(up_ref[...], up_w_ref[...])
    step = pl.program_id(0)

    @pl.when(step == 0)
    def _():
        total_ref[...] = part

    @pl.when(step > 0)
    def _():
        total_ref[...] += part

    @pl.when(step == pl.num_programs(0) - 1)
    def _():
        out_ref[...] = total_ref[...]


def mlp_rows(mlp_low, grad_hidden, w_gate, w_up):
    rows, width = mlp_low.shape
    units = w_gate.shape[1]
    block = 512
    by_units = pl.BlockSpec((rows, block), lambda i: (0, i))
    by_weights = pl.BlockSpec((width, block), lambda i: (0, i))
    whole = pl.BlockSpec((rows, width), lambda i: (0, 0))
    low = jax.ShapeDtypeStruct((rows, units), jnp.bfloat16)
    return pl.pallas_call(
        mlp_kernel,
        grid=(units // block,),
        in_specs=[whole, by_units, by_weights, by_weights],
        out_specs=[by_units, by_units, by_units, whole],
        out_shape=[low, low, low, jax.ShapeDtypeStruct((rows, width), jnp.float32)],
        scratch_shapes=[pltpu.VMEM((rows, width), jnp.float32)],
        compiler_params=ROOMY,
        cost_estimate=NO_COST,
    )(mlp_low, grad_hidden, w_gate, w_up)


def feature_order(width):
    shape = (8 * width, 8 * width)
    row, col = grid_iota(shape, 0), grid_iota(shape, 1)
    return jnp.where(row == (col % 8) * width + col // 8, 1.0, 0.0).astype(jnp.bfloat16)


def patch_in_kernel(core_ref, bytes_ref, weight_ref, wide_ref, out_ref, rows_ref, order_ref):
    places, feature = wide_ref.shape[0], wide_ref.shape[1] // 8
    chunk = weight_ref.shape[1] // 8
    step = pl.program_id(0)

    @pl.when(step == 0)
    def _():
        order_ref[...] = feature_order(chunk)
        for at in range(feature // 128):
            low = at * 128
            rows_ref[at] = bytes_ref[:, low : low + 128].astype(jnp.float32)
            for j in range(8):
                wide_ref[:, j * feature + low : j * feature + low + 128] = rows_ref[
                    at, pl.ds(j, places, stride=8), :
                ]

    parts = [
        wide_ref[:, pl.ds(pl.multiple_of(j * feature + step * chunk, 128), chunk)]
        for j in range(8)
    ]
    by_byte = jnp.concatenate(parts, axis=1).astype(jnp.bfloat16)
    by_feature = dot_plain(by_byte, order_ref[...]).astype(jnp.bfloat16)
    part = dot_trans(by_feature, weight_ref[...])

    @pl.when(step == 0)
    def _():
        out_ref[...] = part

    @pl.when(step > 0)
    def _():
        out_ref[...] += part


def patch_in(byte_rows, w_patch):
    rows, model_width = byte_rows.shape
    out_width, cols = w_patch.shape
    feature, chunk = cols // 8, 128
    core = lax.axis_index("tp").astype(jnp.int32).reshape(1)
    f32 = jnp.float32
    return pl.pallas_call(
        patch_in_kernel,
        grid_spec=pltpu.PrefetchScalarGridSpec(
            num_scalar_prefetch=1,
            grid=(feature // chunk,),
            in_specs=[
                pl.BlockSpec((rows, feature), lambda i, ref: (0, ref[0])),
                pl.BlockSpec((out_width, 8 * chunk), lambda i, ref: (0, i)),
            ],
            out_specs=[
                pl.BlockSpec((rows // 8, cols), lambda i, ref: (0, 0)),
                pl.BlockSpec((rows // 8, out_width), lambda i, ref: (0, 0)),
            ],
            scratch_shapes=[
                pltpu.VMEM((feature // 128, rows, 128), f32),
                pltpu.VMEM((8 * chunk, 8 * chunk), jnp.bfloat16),
            ],
        ),
        out_shape=[
            jax.ShapeDtypeStruct((rows // 8, cols), f32),
            jax.ShapeDtypeStruct((rows // 8, out_width), f32),
        ],
        compiler_params=ROOMY,
        cost_estimate=NO_COST,
    )(core, byte_rows, w_patch)


def final_kernel(
    member_ref,
    own_ref,
    other_ref,
    mask_ref,
    own_head_ref,
    other_head_ref,
    weight_ref,
    low_ref,
    hidden_ref,
    mine_ref,
    mine_low_ref,
):
    own = (own_ref[...] * mask_ref[...]).astype(jnp.bfloat16)
    other = (other_ref[...] * mask_ref[...]).astype(jnp.bfloat16)
    other_head = other_head_ref[...].astype(jnp.bfloat16)
    total = dot_trans(own, own_head_ref[...]) + dot_trans(other, other_head)
    low = total.astype(jnp.bfloat16)
    low_ref[...] = low
    hidden_ref[...] = dot_plain(low, weight_ref[...])

    @pl.when(pl.program_id(0) == member_ref[0])
    def _():
        mine_ref[...] = total
        mine_low_ref[...] = low


def final_grads(own, other, mask, own_head, other_head, w_down, member):
    rows, cols = own.shape
    width = own_head.shape[0]
    block = rows // QUAD
    units = w_down.shape[1] // QUAD
    f32, bf16 = jnp.float32, jnp.bfloat16

    def by_rows(cols):
        return pl.BlockSpec((block, cols), lambda i, ref: (i, 0))

    head = pl.BlockSpec((width, cols), lambda i, ref: (0, 0))
    mine = pl.BlockSpec((block, width), lambda i, ref: (0, 0))
    return pl.pallas_call(
        final_kernel,
        grid_spec=pltpu.PrefetchScalarGridSpec(
            num_scalar_prefetch=1,
            grid=(QUAD,),
            in_specs=[by_rows(cols), by_rows(cols), by_rows(1), head, head]
            + [pl.BlockSpec((width, units), lambda i, ref: (0, ref[0]))],
            out_specs=[by_rows(width), by_rows(units), mine, mine],
        ),
        out_shape=[
            jax.ShapeDtypeStruct((rows, width), bf16),
            jax.ShapeDtypeStruct((rows, units), f32),
            jax.ShapeDtypeStruct((block, width), f32),
            jax.ShapeDtypeStruct((block, width), bf16),
        ],
        compiler_params=ROOMY,
        cost_estimate=NO_COST,
    )(member, own, other, mask, own_head, other_head, w_down)


def group_mlp_kernel(
    place_ref,
    own_ref,
    other_ref,
    gain_ref,
    grad_ref,
    gate_w_ref,
    up_w_ref,
    in_ref,
    hidden_ref,
    gate_ref,
    up_ref,
):
    own, other = own_ref[0], other_ref[0]
    first = place_ref[1] == 0
    halves = [jnp.where(first, own, other), jnp.where(first, other, own)]
    low = (jnp.concatenate(halves, axis=1) * gain_ref[...]).astype(jnp.bfloat16)
    in_ref[...] = low
    units_in_halves(low, grad_ref, gate_w_ref, up_w_ref, hidden_ref, gate_ref, up_ref)


def group_mlp(own_half, other_half, gain, grad_hidden, w_gate, w_up, member):
    rows, half = grad_hidden.shape[0] // QUAD, own_half.shape[2]
    width, units = 2 * half, w_gate.shape[1] // QUAD
    bf16 = jnp.bfloat16
    place = jnp.concatenate([member, lax.axis_index("tp").astype(jnp.int32).reshape(1)])

    def by_rows(cols):
        return pl.BlockSpec((rows, cols), lambda i, ref: (i, 0))

    halves = pl.BlockSpec((1, rows, half), lambda i, ref: (i, 0, 0))
    weights = pl.BlockSpec((width, units), lambda i, ref: (0, ref[0]))
    low = jax.ShapeDtypeStruct((QUAD * rows, units), bf16)
    return pl.pallas_call(
        group_mlp_kernel,
        grid_spec=pltpu.PrefetchScalarGridSpec(
            num_scalar_prefetch=1,
            grid=(QUAD,),
            in_specs=[
                halves,
                halves,
                pl.BlockSpec((1, width), lambda i, ref: (0, 0)),
                by_rows(units),
                weights,
                weights,
            ],
            out_specs=[by_rows(width), by_rows(units), by_rows(units), by_rows(units)],
        ),
        out_shape=[jax.ShapeDtypeStruct((QUAD * rows, width), bf16), low, low, low],
        compiler_params=ROOMY,
        cost_estimate=NO_COST,
    )(place, own_half, other_half, gain.reshape(1, width), grad_hidden, w_gate, w_up)


def bytes_grad_kernel(core_ref, grad_ref, weight_ref, stream_ref, out_ref, order_ref):
    places = grad_ref.shape[0]
    chunk = weight_ref.shape[1] // 8

    @pl.when(pl.program_id(0) == 0)
    def _():
        order_ref[...] = feature_order(chunk)

    by_feature = dot_plain(grad_ref[...].astype(jnp.bfloat16), weight_ref[...])
    high = by_feature.astype(jnp.bfloat16)
    rest = by_feature - high.astype(jnp.float32)
    mid = rest.astype(jnp.bfloat16)
    low = (rest - mid.astype(jnp.float32)).astype(jnp.bfloat16)
    order = order_ref[...]
    by_byte = dot_trans(high, order) + (dot_trans(mid, order) + dot_trans(low, order))
    for j in range(8):
        rows = pl.ds(j, places, stride=8)
        out_ref[rows, :] = stream_ref[rows, :] + by_byte[:, j * chunk : (j + 1) * chunk]


def bytes_grad(grad_patch, w_patch, grad_stream):
    places, width = grad_patch.shape
    rows = grad_stream.shape[0]
    cols = w_patch.shape[1]
    feature, chunk = cols // 8, 128
    core = lax.axis_index("tp").astype(jnp.int32).reshape(1)
    return pl.pallas_call(
        bytes_grad_kernel,
        grid_spec=pltpu.PrefetchScalarGridSpec(
            num_scalar_prefetch=1,
            grid=(feature // chunk,),
            in_specs=[
                pl.BlockSpec((places, width), lambda i, ref: (0, 0)),
                pl.BlockSpec((width, 8 * chunk), lambda i, ref: (0, i)),
                pl.BlockSpec((rows, chunk), lambda i, ref: (0, ref[0] * (feature // chunk) + i)),
            ],
            out_specs=pl.BlockSpec((rows, chunk), lambda i, ref: (0, i)),
            scratch_shapes=[pltpu.VMEM((8 * chunk, 8 * chunk), jnp.bfloat16)],
        ),
        out_shape=jax.ShapeDtypeStruct((rows, feature), jnp.float32),
        compiler_params=ROOMY,
        cost_estimate=NO_COST,
    )(core, grad_patch, w_patch, grad_stream)


def body(
    byte_states,
    lengths,
    w_patch,
    norm_global,
    w_in,
    conv_w,
    conv_b,
    dt_bias,
    a_log,
    d_skip,
    mix_gain,
    w_out,
    norm_attn,
    w_qkv,
    w_o,
    norm_mlp,
    w_gate,
    w_up,
    w_down,
    w_head,
    d_logits,
):
    streams, local_rows, model_width = byte_states.shape
    patch_count = local_rows // 8
    patch_total = streams * patch_count
    row_total = streams * local_rows
    feature = w_patch.shape[1] // 8
    inner_width = w_out.shape[1]
    channels = conv_w.shape[1]
    head_total = dt_bias.shape[0]
    head_cols = w_head.shape[1]
    parts = lax.axis_size("seq")
    tp_index = lax.axis_index("tp")
    seq_index = lax.axis_index("seq")
    places = parts * patch_count
    f32 = jnp.float32

    lanes = parts // streams
    width = inner_width // lanes
    full_head = inner_width // head_total
    own_heads = max(1, width // full_head)
    shared = max(1, full_head // width)
    head_size = width // own_heads
    own_stream = seq_index // lanes
    first_col = (seq_index % lanes) * width
    first_head = first_col // full_head

    seg_full = segment_ids(lengths, places)
    seg_own = lax.dynamic_slice_in_dim(seg_full, seq_index * patch_count, patch_count, 1)
    seg_stream = lax.dynamic_index_in_dim(seg_full, own_stream, 0, keepdims=False)
    valid = (seg_own < lengths.shape[0]).astype(f32).reshape(patch_total, 1)
    byte_valid = jnp.repeat(valid, 8, axis=0)

    member = (seq_index >> 2 & 1) * 2 + (seq_index & 1)
    raw_logits = d_logits.reshape(row_total, head_cols)
    raw_wide = raw_logits.astype(f32)
    group_valid = []
    for high in range(2):
        for low in range(2):
            device = (seq_index & ~5) | high << 2 | low
            group_seg = lax.dynamic_slice_in_dim(
                seg_full, device * patch_count, patch_count, 1
            )
            group_valid.append((group_seg < lengths.shape[0]).astype(f32))
    group_valid = jnp.stack(group_valid).reshape(QUAD, patch_total, 1)
    group_bytes_valid = jnp.repeat(group_valid.reshape(-1, 1), 8, axis=0)
    group_raw = side_trade(jnp.broadcast_to(raw_wide[None], (QUAD,) + raw_wide.shape))
    group_raw = group_raw.reshape(-1, head_cols)
    other_raw = swap(group_raw, "tp", 1)
    other_head = swap(w_head.astype(f32), "tp", 1)
    place_index = member.astype(jnp.int32).reshape(1)
    bytes_wide, patch_part = patch_in(byte_states.reshape(row_total, model_width), w_patch)
    patch_out = tp_sum(patch_part)
    gain_global = norm_global.astype(f32)
    unit_patch = patch_out * rms_scale(patch_out)
    u_low = (unit_patch * gain_global).astype(jnp.bfloat16)
    half_width = model_width // 2
    proj = dot_plain(u_low, w_in).reshape(streams, patch_count, -1)
    gate_in = proj[..., :inner_width]
    xbc = proj[..., inner_width : inner_width + channels]
    dt_raw = proj[..., inner_width + channels :]

    def by_lane(columns):
        split = columns.reshape(streams, patch_count, lanes, -1)
        return jnp.moveaxis(split, 2, 1).reshape(parts, patch_count, -1)

    def from_lanes(blocks):
        split = blocks.reshape(streams, lanes, patch_count, -1)
        return jnp.moveaxis(split, 1, 2).reshape(streams, patch_count, -1)

    def to_all_lanes(columns):
        wide = jnp.broadcast_to(
            columns[:, None], (streams, lanes, patch_count, columns.shape[-1])
        )
        return wide.reshape(parts, patch_count, -1)

    pad_width = 128 - own_heads
    dt_lanes = by_lane(jnp.repeat(dt_raw, shared, axis=2))
    sent = jnp.concatenate(
        [
            by_lane(xbc[..., :inner_width]),
            to_all_lanes(xbc[..., inner_width:]),
            jnp.pad(dt_lanes, ((0, 0), (0, 0), (0, pad_width))),
        ],
        axis=-1,
    )
    taken = trade(sent)
    grad_logits = after(raw_logits, sent) * byte_valid.astype(jnp.bfloat16)
    group_final, group_grad_hidden, grad_final, grad_mlp_low = final_grads(
        after(group_raw, sent),
        other_raw,
        group_bytes_valid,
        w_head,
        other_head,
        w_down,
        place_index,
    )
    grad_hidden = dot_plain(grad_mlp_low, w_down)
    hidden_part = w_gate.shape[1] // QUAD

    row_side = [
        [device for device in range(parts) if (device & 1) == side] for side in range(2)
    ]
    bytes_all = lax.all_gather(
        bytes_wide, "seq", axis=0, axis_index_groups=row_side, tiled=True
    )
    taken = after(taken, grad_hidden, group_grad_hidden).reshape(places, -1)
    scan_width = width + channels - inner_width

    def own_cols(param):
        mine = lax.dynamic_slice_in_dim(param, first_col, width, param.ndim - 1)
        return jnp.concatenate([mine, param[..., inner_width:]], axis=-1).astype(f32)

    def own_head(param):
        return lax.dynamic_slice_in_dim(param, first_head, own_heads, 0).astype(f32)

    use_kernel = places == 512 and width == 128
    if use_kernel:
        padded_seg = jnp.pad(seg_stream, (3, 0), constant_values=-1)
        same = jnp.stack(
            [(padded_seg[k : k + places] == seg_stream).astype(f32) for k in range(3)]
            + [jnp.zeros((places,), f32)] * 5,
            axis=1,
        )
        conv_pack = jnp.concatenate(
            [own_cols(conv_w), own_cols(conv_b)[None], jnp.zeros((3, scan_width), f32)]
        )
        head_pack = jnp.stack(
            [jnp.pad(own_head(dt_bias), (0, 128 - own_heads))]
            + [jnp.pad(own_head(a_log), (0, 128 - own_heads))]
            + [jnp.repeat(own_head(d_skip), head_size)]
            + [jnp.zeros((128,), f32)] * 5
        )
        scan_args = (taken, same, conv_pack, head_pack, seg_stream[:, None], seg_stream[None])
        scanned = scan_forward(scan_args, width)
    else:
        scan_args = (
            taken[:, :scan_width],
            taken[:, scan_width : scan_width + own_heads],
            own_cols(conv_w),
            own_cols(conv_b),
            own_head(dt_bias),
            own_head(a_log),
            own_head(d_skip),
        )
        scanned, scan_back = jax.vjp(partial(scan_heads, seg_stream, head_size), *scan_args)
    result = from_lanes(trade(scanned.reshape(parts, patch_count, width)))
    unit_normed, norm_back = jax.vjp(gated_unit, result, gate_in)
    mix_scale = mix_gain.astype(f32)
    normed_low = (unit_normed * mix_scale).reshape(patch_total, -1).astype(jnp.bfloat16)


    def quarters(columns):
        split = columns.reshape(patch_total, QUAD, -1)
        return jnp.moveaxis(split, 1, 0)

    def by_apart(blocks):
        return [
            lax.dynamic_index_in_dim(blocks, member ^ apart, 0, keepdims=False)
            for apart in range(QUAD)
        ]

    normed_quarters = quarters(unit_normed)
    global_out = patch_out + valid * tp_sum(dot_trans(normed_low, w_out))
    gain_attn = norm_attn.astype(f32)
    gain_mlp = norm_mlp.astype(f32)
    stream_in, attn_in, qkv, mixed_low, attn_part = attn_forward(
        byte_states.reshape(row_total, model_width), global_out, gain_attn, w_qkv, w_o
    )
    after_attn, mlp_low, unit_half = mlp_in(
        stream_in, attn_part, swap(attn_part, "tp", 1), gain_mlp
    )
    hidden_low, grad_gate_low, grad_up_low, grad_mlp_part = mlp_rows(
        after(mlp_low, unit_half), grad_hidden, w_gate, w_up
    )
    half_width = model_width // 2
    to_all = jnp.concatenate([unit_half, unit_patch.reshape(-1, half_width)], axis=0)
    group_sent = jnp.concatenate(
        [
            jnp.broadcast_to(to_all[None], (QUAD,) + to_all.shape),
            normed_quarters.reshape(QUAD, -1, half_width),
        ],
        axis=1,
    )
    group_halves = side_trade(group_sent)
    grad_mlp_other = swap(grad_mlp_part, "tp", 1)
    after_mlp = after_attn + tp_sum(dot_trans(after(hidden_low, grad_mlp_part), w_down))
    final_low = after_mlp.astype(jnp.bfloat16)
    logits = dot_plain(final_low, w_head) * byte_valid
    grad_mid, grad_attn_low, grad_qkv_low, grad_attn_part, grad_norm_mlp = attn_backward(
        after_attn, grad_final, grad_mlp_part, grad_mlp_other, gain_mlp, qkv, w_qkv, w_o
    )
    grad_norm_mlp = grad_norm_mlp.reshape(-1)
    grad_attn_in = tp_sum(grad_attn_part)

    back_attn, grad_norm_attn = rms_back(stream_in, gain_attn, grad_attn_in)
    grad_stream = grad_mid + back_attn
    grad_global = jnp.sum(grad_stream.reshape(patch_total, 8, model_width), axis=1)
    grad_mix_low = (grad_global * valid).astype(jnp.bfloat16)
    grad_normed = dot_plain(grad_mix_low, w_out).reshape(streams, patch_count, inner_width)
    grad_mix_gain = jnp.sum(grad_normed * unit_normed, axis=(0, 1))
    grad_result, grad_gate_in = norm_back(grad_normed * mix_scale)
    grad_z_low = grad_gate_in.reshape(patch_total, inner_width).astype(jnp.bfloat16)
    row_block = model_width // parts
    dealing = by_lane(grad_result)
    dealt = trade(dealing)
    def group_swap(blocks):
        moved = [swap(block, "seq", mask) for block, mask in zip(blocks[1:], (1, 4, 5))]
        return jnp.concatenate([blocks[0]] + moved, axis=0)

    late_sent = [
        jnp.concatenate([grad_global, part], axis=-1) for part in by_apart(quarters(grad_gate_in))
    ]
    late_got = group_swap(late_sent)
    apart_valid = jnp.concatenate(by_apart(group_valid), axis=0)
    group_mix = (late_got[:, :model_width] * apart_valid).astype(jnp.bfloat16)
    group_z = late_got[:, model_width:]
    attn_cut = 1024 if grad_qkv_low.shape[1] > 1024 else 128
    attn_in_late = after(attn_in, late_got)
    attn_cols = grad_qkv_low.shape[1]
    attn_blocks = (
        grad_blocks([(attn_in_late, grad_qkv_low, 0, attn_cut)], 0, True),
        grad_blocks(
            [
                (attn_in_late, grad_qkv_low, attn_cut, attn_cols),
                (grad_attn_low, mixed_low, 0, mixed_low.shape[1]),
                (final_low, grad_logits, 0, head_cols),
            ],
            1,
            True,
        ),
    )
    attn_got = [to_partner(attn_blocks[first][0], first) for first in range(2)]
    dealt = after(dealt, bytes_all, attn_blocks[0][0], attn_blocks[1][0])
    grad_scanned = dealt.reshape(places, width)
    if use_kernel:
        back_sent, conv_grads, head_grads = scan_backward(scan_args, grad_scanned)
        lane_grad = back_sent[:, : scan_width + own_heads]
        scan_params = (
            conv_grads[:4],
            conv_grads[4],
            head_grads[0, :own_heads],
            head_grads[1, :own_heads],
            head_grads[2, :own_heads],
        )
    else:
        scan_grads = scan_back(grad_scanned)
        back_sent = jnp.concatenate(
            [scan_grads[0], jnp.pad(scan_grads[1], ((0, 0), (0, pad_width)))], axis=-1
        )
        lane_grad = jnp.concatenate([scan_grads[0], scan_grads[1]], axis=-1)
        scan_params = scan_grads[2:]
    back_sent = back_sent.reshape(parts, patch_count, -1)
    back_taken = trade(back_sent)
    own_half = after(group_halves, back_sent)
    group_in, group_hidden, group_gate, group_up = group_mlp(
        own_half, swap(own_half, "tp", 1), gain_mlp, group_grad_hidden, w_gate, w_up, place_index
    )
    group_rows = own_half[:, row_total : row_total + 2 * patch_total]
    group_rows = group_rows.reshape(QUAD, patch_total, model_width)
    group_u = jnp.concatenate(by_apart(group_rows), axis=0) * gain_global
    group_u = group_u.astype(jnp.bfloat16)
    quarter = inner_width // QUAD
    own_scale = lax.dynamic_slice_in_dim(mix_scale, member * quarter, quarter, 0)
    group_n = own_half[:, row_total + 2 * patch_total :].reshape(QUAD, patch_total, quarter)
    group_n = (jnp.concatenate(by_apart(group_n), axis=0) * own_scale).astype(jnp.bfloat16)

    mlp_blocks = [
        grad_blocks(
            [(group_final, group_hidden, 0, hidden_part), (group_in, group_gate, 0, hidden_part)],
            1,
            False,
        ),
        grad_blocks(
            [
                (group_in, group_up, 0, hidden_part),
                (group_mix, group_n, 0, group_n.shape[1]),
                (group_u, group_z, 0, group_z.shape[1]),
            ],
            1,
            False,
        ),
    ]
    mlp_got = [to_partner(far, 1) for far, unused in mlp_blocks]
    back_taken = after(back_taken, mlp_blocks[0][0], mlp_blocks[1][0])
    grad_x = from_lanes(back_taken[..., :width])
    by_stream = back_taken.reshape(streams, lanes, patch_count, -1)
    grad_bc = jnp.sum(by_stream[..., width:scan_width], axis=1)
    grad_dt = from_lanes(back_taken[..., scan_width : scan_width + own_heads])
    grad_dt = jnp.sum(grad_dt.reshape(streams, patch_count, head_total, shared), axis=-1)
    grad_shared = jnp.concatenate([grad_bc, grad_dt], axis=-1).reshape(patch_total, -1)
    grad_proj_low = jnp.concatenate(
        [grad_z_low, grad_x.reshape(patch_total, -1).astype(jnp.bfloat16)]
        + [grad_shared.astype(jnp.bfloat16)],
        axis=-1,
    )
    grad_u_part = dot_trans(grad_proj_low, w_in)
    attn_far = [
        add_side(after(attn_blocks[first][1], grad_u_part), attn_got[first], 1)
        for first in range(2)
    ]
    attn_crossed = [to_partner(attn_far[first], 1 - first) for first in range(2)]
    grad_u = after(tp_sum(grad_u_part), *attn_far)
    rest = [quarters(columns) for columns in (grad_x, grad_bc, grad_dt)]
    rest_cols = [part.shape[-1] for part in rest]
    rest = after(jnp.concatenate(rest, axis=-1), grad_u_part)
    rest = jnp.pad(rest, ((0, 0), (0, 0), (0, -sum(rest_cols) % 128)))
    rest_blocks = grad_blocks(
        [(group_u, group_swap(by_apart(rest)), 0, rest.shape[-1])], 1, False
    )
    rest_got = to_partner(rest_blocks[0], 1)
    back_global, grad_norm_global = rms_back(patch_out, gain_global, grad_u)
    grad_patch = grad_global + back_global
    side_count = parts // 2
    my_side = seq_index & 1
    by_block = jnp.moveaxis(grad_patch.reshape(patch_total, parts, row_block), 1, 0)
    by_block = by_block.reshape(side_count, 2, patch_total, row_block)
    same_side = lax.dynamic_index_in_dim(by_block, my_side, 1, keepdims=False)
    other_side = lax.dynamic_index_in_dim(by_block, 1 - my_side, 1, keepdims=False)
    patch_rows = jnp.concatenate([same_side, other_side], axis=-1)
    patch_rows = patch_rows.reshape(side_count, patch_total, 2 * row_block)
    gain_part = grad_norm_global.reshape(-1, 2 * row_block)
    gain_count = gain_part.shape[0]
    patch_sent = jnp.concatenate(
        [patch_rows, jnp.broadcast_to(gain_part, (side_count,) + gain_part.shape)], axis=1
    )
    patch_taken = lax.all_to_all(
        after(patch_sent, mlp_got[0]), "seq", 0, 0, axis_index_groups=row_side, tiled=True
    )

    patch_taken = after(patch_taken, rest_blocks[0])
    high = (seq_index // QUAD).astype(jnp.int32).reshape(1)
    attn_near = near_sums(
        [
            (after(attn_blocks[first][1], patch_taken), attn_got[first], attn_crossed[first])
            for first in range(2)
        ],
        high,
    )
    attn_high = [
        swap(attn_near[apart], "seq", QUAD * apart) for apart in range(1, parts // QUAD)
    ]
    gain_side = jnp.sum(patch_taken[:, patch_total:], axis=0)
    patch_cols = patch_taken[:, :patch_total].reshape(-1, 2 * row_block)
    patch_far = patch_far_grad(after(patch_cols, attn_near), gain_side, bytes_all)
    small = (
        scan_params[0][:, :width],
        scan_params[1][:width],
        scan_params[0][:, width:],
        scan_params[1][width:],
        scan_params[2],
        scan_params[3],
        scan_params[4],
        grad_mix_gain,
        grad_norm_attn,
        grad_norm_mlp,
    )
    small_count = sum(part.size for part in small)
    flat = after(jnp.concatenate([part.reshape(-1) for part in small]), patch_far)
    flat = jnp.pad(flat, (0, -small_count % 1024)).reshape(1, -1, 128)
    pieces = trade(jnp.broadcast_to(flat, (parts,) + flat.shape[1:])).reshape(parts, -1)
    by_small, at = [], 0
    for part in small:
        got = pieces[:, at : at + part.size].reshape((parts,) + part.shape)
        by_small.append(got)
        at += part.size

    def lane_cols(got):
        joined = jnp.sum(got.reshape((streams, lanes) + got.shape[1:]), axis=0)
        return jnp.moveaxis(joined, 0, -2).reshape(joined.shape[1:-1] + (-1,))

    def lane_heads(got):
        joined = jnp.sum(got.reshape(streams, lanes, -1), axis=0)
        return jnp.sum(joined.reshape(head_total, shared), axis=-1)

    small_sums = [
        jnp.concatenate([lane_cols(by_small[0]), jnp.sum(by_small[2], axis=0)], axis=-1),
        jnp.concatenate([lane_cols(by_small[1]), jnp.sum(by_small[3], axis=0)], axis=-1),
        lane_heads(by_small[4]),
        lane_heads(by_small[5]),
        lane_heads(by_small[6]),
    ] + [jnp.sum(got, axis=0) for got in by_small[7:]]

    patch_got = to_partner(patch_far, 0)

    mlp_finals = []
    for blocks, got, turn in zip(
        mlp_blocks + [rest_blocks], mlp_got + [rest_got], (patch_far, patch_got, patch_got)
    ):
        near = after(blocks[1], turn)
        for bit in reversed(range(3, seq_bits())):
            far, near = split_add(near, got, bit)
            got = to_partner(far, bit)
        mlp_finals.append(jnp.moveaxis(side_trade(group_add(near, got)), 0, 1))

    def final_cols(final, low, count):
        return final[..., low : low + count].reshape(row_block, -1)

    final_down = final_cols(mlp_finals[0], 0, hidden_part)
    final_gate = final_cols(mlp_finals[0], hidden_part, hidden_part)
    final_up = final_cols(mlp_finals[1], 0, hidden_part)
    final_out = final_cols(mlp_finals[1], hidden_part, quarter)
    final_z = final_cols(mlp_finals[1], hidden_part + quarter, quarter)
    final_x = final_cols(mlp_finals[2], 0, rest_cols[0])
    final_bc = final_cols(mlp_finals[2], rest_cols[0], rest_cols[1])
    final_dt = final_cols(mlp_finals[2], rest_cols[0] + rest_cols[1], rest_cols[2])
    final_patch = patch_grad(patch_cols, patch_got, bytes_all)
    final_attn = attn_near[0]
    for got in attn_high:
        final_attn = final_attn + after(got, patch_got)
    norm_global_sum = (gain_side + patch_got[row_block:, : 2 * row_block]).reshape(-1)
    grad_bytes = bytes_grad(after(grad_patch, patch_far), w_patch, grad_stream)
    grad_bytes = grad_bytes.reshape(streams, local_rows, feature)

    qkv_cols, o_cols = w_qkv.shape[1], w_o.shape[1]
    return (
        logits.reshape(streams, local_rows, head_cols),
        grad_bytes,
        final_patch,
        norm_global_sum,
        jnp.concatenate([final_z, final_x, final_bc, final_dt], axis=1),
        small_sums[0],
        small_sums[1],
        small_sums[2],
        small_sums[3],
        small_sums[4],
        small_sums[5],
        final_out,
        small_sums[6],
        final_attn[:, :qkv_cols],
        final_attn[:, qkv_cols : qkv_cols + o_cols],
        small_sums[7],
        final_gate,
        final_up,
        final_down,
        final_attn[:, qkv_cols + o_cols :],
    )


def solution(mesh):
    in_specs = (
        P(None, "seq", None),
        P(),
        P(None, "tp"),
        P(),
        P(None, "tp"),
        P(None, "tp"),
        P("tp"),
        P("tp"),
        P("tp"),
        P("tp"),
        P("tp"),
        P(None, "tp"),
        P(),
        P(None, "tp"),
        P(None, "tp"),
        P(),
        P(None, "tp"),
        P(None, "tp"),
        P(None, "tp"),
        P(None, "tp"),
        P(None, "seq", "tp"),
    )
    out_specs = (
        P(None, "seq", "tp"),
        P(None, "seq", "tp"),
        P("seq", "tp"),
        P(),
        P("seq", "tp"),
        P(None, "tp"),
        P("tp"),
        P("tp"),
        P("tp"),
        P("tp"),
        P("tp"),
        P("seq", "tp"),
        P(),
        P("seq", "tp"),
        P("seq", "tp"),
        P(),
        P("seq", "tp"),
        P("seq", "tp"),
        P("seq", "tp"),
        P("seq", "tp"),
    )
    return jax.shard_map(body, mesh=mesh, in_specs=in_specs, out_specs=out_specs, check_vma=False)
```

```python
from functools import partial

import jax
import jax.numpy as jnp
from jax import lax
from jax.experimental import pallas as pl
from jax.experimental.pallas import tpu as pltpu
from jax.sharding import PartitionSpec as P

NS = 128
AD = 64
QUAD = 4


NO_COST = pl.CostEstimate(flops=1024, bytes_accessed=1024, transcendentals=0)
ROOMY = pltpu.CompilerParams(vmem_limit_bytes=56 * 1024 * 1024)

epsilon = 1e-05
highest = lax.Precision.HIGHEST
masked_score = -1e30


def dot_plain(left_side, right_side):
    return jnp.dot(left_side, right_side, preferred_element_type=jnp.float32)


def dot_trans(left_side, right_side):
    return lax.dot_general(
        left_side, right_side, (((1,), (1,)), ((), ())), preferred_element_type=jnp.float32
    )


def dot_left(left_side, right_side):
    return lax.dot_general(
        left_side, right_side, (((0,), (0,)), ((), ())), preferred_element_type=jnp.float32
    )


def rms_scale(values):
    return lax.rsqrt(jnp.mean(values * values, axis=-1, keepdims=True) + epsilon)


def hidden_parts(mlp_in, grad_hidden, w_gate, w_up):
    gate_proj = dot_plain(mlp_in, w_gate)
    up_proj = dot_plain(mlp_in, w_up)
    sigmoid_gate = jax.nn.sigmoid(gate_proj)
    hidden_low = (gate_proj * sigmoid_gate * up_proj).astype(jnp.bfloat16)
    grad_gate_low = (
        grad_hidden * up_proj * sigmoid_gate * (1.0 + gate_proj * (1.0 - sigmoid_gate))
    ).astype(jnp.bfloat16)
    grad_up_low = (grad_hidden * gate_proj * sigmoid_gate).astype(jnp.bfloat16)
    return (hidden_low, grad_gate_low, grad_up_low)


def rms_back(values, gain_values, grad_out):
    scale = rms_scale(values)
    scaled = gain_values * grad_out
    inner_mean = jnp.mean(values * scaled, axis=-1, keepdims=True)
    grad_values = scale * scaled - values * scale * scale * scale * inner_mean
    grad_gain = jnp.sum(values * scale * grad_out, axis=0)
    return (grad_values, grad_gain)


def swap(block, axis, mask):
    return lax.ppermute(block, axis, [(i, i ^ mask) for i in range(lax.axis_size(axis))])


def after(value, *earlier):
    return lax.optimization_barrier((value,) + earlier)[0]


def tp_sum(block):
    return block + swap(block, "tp", 1)


def to_partner(block, bit):
    return swap(block, "seq", 1 << bit)


def seq_bits():
    return lax.axis_size("seq").bit_length() - 1


def side_trade(blocks):
    members = [
        [base | high << 2 | low for high in range(2) for low in range(2)]
        for base in range(lax.axis_size("seq"))
        if base & 5 == 0
    ]
    return lax.all_to_all(blocks, "seq", 0, 0, axis_index_groups=members, tiled=True)


def add_kernel(index_ref, *refs):
    total = refs[0][...] + refs[1][...]
    refs[2][...] = total.reshape(refs[2].shape)


def add_side(near, got, side):
    unused, groups, rows, cols = near.shape
    index = jnp.zeros((1,), jnp.int32)
    block = pl.BlockSpec((1, 1, rows, cols), lambda i, ref: (side, i, 0, 0))
    return pl.pallas_call(
        add_kernel,
        grid_spec=pltpu.PrefetchScalarGridSpec(
            num_scalar_prefetch=1,
            grid=(groups,),
            in_specs=[block, block],
            out_specs=pl.BlockSpec((1, rows, cols), lambda i, ref: (i, 0, 0)),
        ),
        out_shape=jax.ShapeDtypeStruct((groups, rows, cols), jnp.float32),
        compiler_params=ROOMY,
        cost_estimate=NO_COST,
    )(index, near, got)


def near_kernel(index_ref, *refs):
    out_ref = refs[-1]
    at = 0
    for near_ref, got_ref, crossed_ref in zip(refs[0:-1:3], refs[1:-1:3], refs[2:-1:3]):
        cols = near_ref.shape[3]
        total = near_ref[0, 0] + got_ref[0, 0] + crossed_ref[0]
        out_ref[0, :, at : at + cols] = total
        at += cols


def near_sums(terms, high):
    unused, groups, rows, unused_cols = terms[0][0].shape
    cols = [term[0].shape[3] for term in terms]
    specs, operands = [], []
    for (near, got, crossed), count in zip(terms, cols):
        four = pl.BlockSpec((1, 1, rows, count), lambda i, ref: (0, ref[0] ^ i, 0, 0))
        three = pl.BlockSpec((1, rows, count), lambda i, ref: (ref[0] ^ i, 0, 0))
        specs += [four, four, three]
        operands += [near, got, crossed]
    return pl.pallas_call(
        near_kernel,
        grid_spec=pltpu.PrefetchScalarGridSpec(
            num_scalar_prefetch=1,
            grid=(groups,),
            in_specs=specs,
            out_specs=pl.BlockSpec((1, rows, sum(cols)), lambda i, ref: (i, 0, 0)),
        ),
        out_shape=jax.ShapeDtypeStruct((groups, rows, sum(cols)), jnp.float32),
        compiler_params=ROOMY,
        cost_estimate=NO_COST,
    )(high, *operands)


def split_kernel(index_ref, far_a, far_b, near_a, near_b, far_ref, near_ref):
    far_ref[...] = far_a[...] + far_b[...]
    near_ref[...] = near_a[...] + near_b[...]


def split_add(first, second, bit):
    half = first.shape[0] // 2
    rest = first.shape[1:]
    zeros = (0,) * len(rest)
    mine = (lax.axis_index("seq") >> bit & 1).astype(jnp.int32).reshape(1)
    far = pl.BlockSpec((1,) + rest, lambda i, ref: ((1 - ref[0]) * half + i,) + zeros)
    near = pl.BlockSpec((1,) + rest, lambda i, ref: (ref[0] * half + i,) + zeros)
    out = jax.ShapeDtypeStruct((half,) + rest, jnp.float32)
    block = pl.BlockSpec((1,) + rest, lambda i, ref: (i,) + zeros)
    return pl.pallas_call(
        split_kernel,
        grid_spec=pltpu.PrefetchScalarGridSpec(
            num_scalar_prefetch=1,
            grid=(half,),
            in_specs=[far, far, near, near],
            out_specs=[block, block],
        ),
        out_shape=[out, out],
        compiler_params=ROOMY,
        cost_estimate=NO_COST,
    )(mine, first, second, first, second)


def group_add(first, second):
    members, rows, cols = QUAD, first.shape[-2], first.shape[-1]
    block = pl.BlockSpec((1, rows, cols), lambda i, ref: (i, 0, 0))
    shape = (members, rows, cols)
    return pl.pallas_call(
        add_kernel,
        grid_spec=pltpu.PrefetchScalarGridSpec(
            num_scalar_prefetch=1, grid=(members,), in_specs=[block, block], out_specs=block
        ),
        out_shape=jax.ShapeDtypeStruct(shape, jnp.float32),
        compiler_params=ROOMY,
        cost_estimate=NO_COST,
    )(jnp.zeros((1,), jnp.int32), first.reshape(shape), second.reshape(shape))


def grad_blocks_kernel(pairs, first, relative, rows, member_ref, *refs):
    lefts, rights = refs[: len(pairs)], refs[len(pairs) : 2 * len(pairs)]
    far_ref, near_ref = refs[2 * len(pairs) :]
    other = 1 - first
    at = 0
    for left_ref, right_ref, (low, high) in zip(lefts, rights, pairs):
        got = dot_left(left_ref[...], right_ref[:, low:high].astype(jnp.bfloat16))
        places = slice(at, at + high - low)
        for block in range(got.shape[0] // rows):
            place, member = block // QUAD, block % QUAD
            part = got[block * rows : (block + 1) * rows]
            apart = member_ref[0] ^ member
            is_far = apart >> first & 1
            if relative:
                side = apart >> other & 1
            else:
                side = member >> other & 1

            @pl.when(is_far == 1)
            def _():
                if relative:
                    far_ref[side, place, :, places] = part
                else:
                    far_ref[place, side, :, places] = part

            @pl.when(is_far == 0)
            def _():
                if relative:
                    near_ref[side, place, :, places] = part
                else:
                    near_ref[place, side, :, places] = part

        at += high - low


def grad_blocks(terms, first, relative):
    parts = lax.axis_size("seq")
    groups = parts // QUAD
    model_width = terms[0][0].shape[1]
    rows = model_width // parts
    cols = max(128, QUAD * rows)
    places = cols // (QUAD * rows)
    pairs = [(low, high) for unused, unused_right, low, high in terms]
    total = sum(high - low for low, high in pairs)
    member = (lax.axis_index("seq") % QUAD).astype(jnp.int32).reshape(1)
    if relative:
        shape, block = (2, groups, rows, total), (2, places, rows, total)
        out_spec = pl.BlockSpec(block, lambda i, ref: (0, i, 0, 0))
    else:
        shape, block = (groups, 2, rows, total), (places, 2, rows, total)
        out_spec = pl.BlockSpec(block, lambda i, ref: (i, 0, 0, 0))
    out = jax.ShapeDtypeStruct(shape, jnp.float32)
    return pl.pallas_call(
        partial(grad_blocks_kernel, pairs, first, relative, rows),
        grid_spec=pltpu.PrefetchScalarGridSpec(
            num_scalar_prefetch=1,
            grid=(model_width // cols,),
            in_specs=[
                pl.BlockSpec((term[0].shape[0], cols), lambda i, ref: (0, i)) for term in terms
            ]
            + [pl.BlockSpec(term[1].shape, lambda i, ref: (0, 0)) for term in terms],
            out_specs=[out_spec, out_spec],
        ),
        out_shape=[out, out],
        compiler_params=ROOMY,
        cost_estimate=NO_COST,
    )(member, *[term[0] for term in terms], *[term[1] for term in terms])


def segment_ids(lengths, place_count):
    ends = jnp.cumsum(lengths // 8, dtype=jnp.int32)
    places = jnp.arange(place_count, dtype=jnp.int32)
    short_ids = jnp.sum(
        (places[:, None] >= ends[None, :]).astype(jnp.int32), axis=1, dtype=jnp.int32
    )
    return jnp.stack([jnp.zeros_like(short_ids), short_ids])


def scan_heads(seg_now, head_size, xbc, dt_raw, conv_weight, conv_bias, dt_shift, a_logs, skips):
    place_count = xbc.shape[0]
    conv_sum = conv_bias + conv_weight[3] * xbc
    for offset in range(3):
        distance = 3 - offset
        earlier = jnp.pad(xbc, ((distance, 0), (0, 0)))[:place_count]
        seg_earlier = jnp.pad(seg_now, (distance, 0), constant_values=-1)[:place_count]
        same_doc = (seg_earlier == seg_now).astype(jnp.float32)
        conv_sum = conv_sum + conv_weight[offset] * earlier * same_doc[:, None]
    active = jax.nn.silu(conv_sum)
    head_count = dt_raw.shape[1]
    inner = head_count * head_size
    values = active[:, :inner].reshape(place_count, head_count, head_size)
    in_keys = active[:, inner : inner + NS]
    out_keys = active[:, inner + NS :]
    step_sizes = jax.nn.softplus(dt_raw + dt_shift)
    decay_rates = -step_sizes * jnp.exp(a_logs)
    chunk = min(place_count, 512)
    triangle = jnp.tril(jnp.ones((chunk, chunk), jnp.float32))
    state = jnp.zeros((head_count, head_size, NS), jnp.float32)
    seg_last = jnp.int32(-1)
    outputs = []
    for start in range(0, place_count, chunk):
        stop = start + chunk
        x, b, c = values[start:stop], in_keys[start:stop], out_keys[start:stop]
        dt, seg = step_sizes[start:stop], seg_now[start:stop]
        cumulative = jnp.dot(triangle, decay_rates[start:stop], precision=highest)
        allowed = (triangle > 0.0) & (seg[:, None] == seg[None, :])
        ordered = cumulative.T
        gaps = ordered[:, :, None] - ordered[:, None, :]
        decays = jnp.where(allowed, jnp.exp(jnp.where(allowed, gaps, 0.0)), 0.0)
        crossing = jnp.einsum("pn,jn->pj", c, b, precision=highest)
        mixing = crossing[None] * decays * dt.T[:, None, :]
        result = jnp.einsum("hpj,jhd->phd", mixing, x, precision=highest)
        if start > 0:
            entering = jnp.exp(cumulative) * (seg == seg_last).astype(jnp.float32)[:, None]
            result = result + entering[..., None] * jnp.einsum(
                "pn,hdn->phd", c, state, precision=highest
            )
        if stop < place_count:
            last_same = (seg == seg[-1]).astype(jnp.float32)[:, None]
            weight = jnp.exp(cumulative[-1:] - cumulative) * last_same * dt
            through = jnp.exp(cumulative[-1]) * (seg[-1] == seg_last).astype(jnp.float32)
            state = through[:, None, None] * state + jnp.einsum(
                "jh,jhd,jn->hdn", weight, x, b, precision=highest
            )
            seg_last = seg[-1]
        outputs.append(result + skips[:, None] * x)
    return jnp.concatenate(outputs, axis=0).reshape(place_count, inner)


def gated_unit(result, gate_in):
    gated = result * jax.nn.silu(gate_in)
    return gated * rms_scale(gated)


def patch_far_kernel(grad_ref, gain_ref, bytes_ref, out_ref):
    half = grad_ref.shape[1] // 2
    grad_low = grad_ref[:, half:].astype(jnp.bfloat16)
    out_ref[:half] = dot_left(grad_low, bytes_ref[...].astype(jnp.bfloat16))
    out_ref[half:] = jnp.zeros((out_ref.shape[0] - half, out_ref.shape[1]), jnp.float32)

    @pl.when(pl.program_id(0) == 0)
    def _():
        out_ref[half:, : 2 * half] = gain_ref[...]


def patch_far_grad(grad_rows, gain_part, bytes_all):
    places, cols = grad_rows.shape
    total = bytes_all.shape[1]
    rows = cols // 2 + gain_part.shape[0]
    block = 1024
    return pl.pallas_call(
        patch_far_kernel,
        grid=(total // block,),
        in_specs=[
            pl.BlockSpec((places, cols), lambda i: (0, 0)),
            pl.BlockSpec(gain_part.shape, lambda i: (0, 0)),
            pl.BlockSpec((places, block), lambda i: (0, i)),
        ],
        out_specs=pl.BlockSpec((rows, block), lambda i: (0, i)),
        out_shape=jax.ShapeDtypeStruct((rows, total), jnp.float32),
        compiler_params=ROOMY,
        cost_estimate=NO_COST,
    )(grad_rows, gain_part, bytes_all)


def patch_grad_kernel(grad_ref, *refs):
    byte_refs, got_refs, out_ref, order_ref = refs[:8], refs[8:16], refs[16], refs[17]
    width = byte_refs[0].shape[1]

    @pl.when(pl.program_id(0) == 0)
    def _():
        order_ref[...] = feature_order(width)

    grad_low = grad_ref[:, : grad_ref.shape[1] // 2].astype(jnp.bfloat16)
    wide = jnp.concatenate([ref[...].astype(jnp.bfloat16) for ref in byte_refs], axis=1)
    rows = grad_low.shape[1]
    grad = dot_left(grad_low, wide)
    grad = grad + jnp.concatenate([ref[:rows] for ref in got_refs], axis=1)
    high = grad.astype(jnp.bfloat16)
    rest = grad - high.astype(jnp.float32)
    mid = rest.astype(jnp.bfloat16)
    low = (rest - mid.astype(jnp.float32)).astype(jnp.bfloat16)
    order = order_ref[...]
    out_ref[...] = dot_plain(high, order) + (dot_plain(mid, order) + dot_plain(low, order))


def patch_grad(grad_rows, got, bytes_all):
    places, cols = grad_rows.shape
    feature = bytes_all.shape[1] // 8
    chunk = 128
    steps = feature // chunk

    def byte_specs(rows):
        return [
            pl.BlockSpec((rows, chunk), partial(lambda j, i: (0, j * steps + i), j))
            for j in range(8)
        ]

    return pl.pallas_call(
        patch_grad_kernel,
        grid=(steps,),
        in_specs=[pl.BlockSpec((places, cols), lambda i: (0, 0))]
        + byte_specs(places)
        + byte_specs(got.shape[0]),
        out_specs=pl.BlockSpec((cols // 2, 8 * chunk), lambda i: (0, i)),
        out_shape=jax.ShapeDtypeStruct((cols // 2, 8 * feature), jnp.float32),
        scratch_shapes=[pltpu.VMEM((8 * chunk, 8 * chunk), jnp.bfloat16)],
        compiler_params=ROOMY,
        cost_estimate=NO_COST,
    )(grad_rows, *([bytes_all] * 8), *([got] * 8))


def trade(blocks):
    return lax.all_to_all(blocks, "seq", 0, 0, tiled=True)


def grid_iota(shape, axis):
    return lax.broadcasted_iota(jnp.int32, shape, axis)


def dot_fine(left_side, right_side, left_axis, right_axis):
    return lax.dot_general(
        left_side,
        right_side,
        (((left_axis,), (right_axis,)), ((), ())),
        preferred_element_type=jnp.float32,
        precision=highest,
    )


def shifted_down(block, distance):
    rows = grid_iota(block.shape, 0)
    return jnp.where(rows >= distance, pltpu.roll(block, distance, 0), 0.0)


def shifted_up(block, distance):
    count = block.shape[0]
    rows = grid_iota(block.shape, 0)
    return jnp.where(rows < count - distance, pltpu.roll(block, count - distance, 0), 0.0)


def scan_terms(taken_ref, same_ref, conv_ref, head_ref):
    places = taken_ref.shape[0]
    channels = conv_ref.shape[1]
    xbc = taken_ref[:, :channels]
    conv_sum = conv_ref[4:5] + conv_ref[3:4] * xbc
    for k in range(3):
        earlier = shifted_down(xbc, 3 - k) * same_ref[:, k : k + 1]
        conv_sum = conv_sum + conv_ref[k : k + 1] * earlier
    gate = jax.nn.sigmoid(conv_sum)
    active = conv_sum * gate
    raw = taken_ref[:, channels:] + head_ref[0:1]
    steps = jnp.maximum(raw, 0.0) + jnp.log1p(jnp.exp(-jnp.abs(raw)))
    rates = -steps * jnp.exp(head_ref[1:2])
    square = (places, places)
    triangle = jnp.where(grid_iota(square, 0) >= grid_iota(square, 1), 1.0, 0.0)
    running = dot_fine(triangle, rates, 1, 0)
    return xbc, conv_sum, gate, active, raw, steps, rates, triangle, running


def scan_forward_kernel(taken_ref, same_ref, conv_ref, head_ref, seg_col, seg_row, out_ref):
    places, width = out_ref.shape
    terms = scan_terms(taken_ref, same_ref, conv_ref, head_ref)
    active, steps, running = terms[3], terms[5], terms[8]
    values = active[:, :width]
    keys, reads = active[:, width : width + NS], active[:, width + NS :]
    steps_row, running_row = steps.T, running.T
    heads = width // 64
    rows = 128
    for first in range(0, places, rows):
        last = first + rows
        shape = (rows, last)
        allowed = (seg_col[first:last] == seg_row[:, :last]) & (
            grid_iota(shape, 0) + first >= grid_iota(shape, 1)
        )
        crossing = dot_fine(reads[first:last], keys[:last], 1, 1)
        lane = grid_iota((rows, width), 1) // 64
        total = head_ref[2:3] * values[first:last]
        for h in range(heads):
            gaps = running[first:last, h : h + 1] - running_row[h : h + 1, :last]
            decays = jnp.exp(jnp.where(allowed, gaps, masked_score))
            mixing = crossing * decays * steps_row[h : h + 1, :last]
            part = dot_fine(mixing, values[:last], 1, 0)
            total = total + jnp.where(lane == h, part, 0.0)
        out_ref[first:last] = total


def scan_backward_kernel(
    taken_ref,
    same_ref,
    conv_ref,
    head_ref,
    seg_col,
    seg_row,
    grad_ref,
    out_ref,
    conv_grad_ref,
    head_grad_ref,
    values_grad,
    keys_grad,
    reads_grad,
    rows_grad,
    cols_grad,
):
    places, width = values_grad.shape
    terms = scan_terms(taken_ref, same_ref, conv_ref, head_ref)
    xbc, conv_sum, gate, active, raw, steps, rates, triangle, running = terms
    channels = xbc.shape[1]
    values = active[:, :width]
    keys, reads = active[:, width : width + NS], active[:, width + NS :]
    steps_row, running_row = steps.T, running.T
    heads = width // 64
    rows = 128
    grad = grad_ref[...]
    values_grad[...] = head_ref[2:3] * grad
    keys_grad[...] = jnp.zeros_like(keys_grad)
    rows_grad[...] = jnp.zeros_like(rows_grad)
    cols_grad[...] = jnp.zeros_like(cols_grad)
    for first in range(0, places, rows):
        last = first + rows
        shape = (rows, last)
        allowed = (seg_col[first:last] == seg_row[:, :last]) & (
            grid_iota(shape, 0) + first >= grid_iota(shape, 1)
        )
        crossing = dot_fine(reads[first:last], keys[:last], 1, 1)
        crossing_grad = jnp.zeros(shape, jnp.float32)
        grad_rows = grad[first:last]
        lane = grid_iota((rows, width), 1) // 64
        wide_lane = grid_iota((last, width), 1) // 64
        column = grid_iota((rows, 128), 1)
        down = jnp.zeros((rows, 128), jnp.float32)
        for h in range(heads):
            gaps = running[first:last, h : h + 1] - running_row[h : h + 1, :last]
            decays = jnp.exp(jnp.where(allowed, gaps, masked_score))
            step_row = steps_row[h : h + 1, :last]
            weighted = decays * step_row
            mixing = crossing * weighted
            own_grad = jnp.where(lane == h, grad_rows, 0.0)
            mixing_grad = dot_fine(own_grad, values[:last], 1, 1)
            back = dot_fine(mixing, own_grad, 0, 0)
            values_grad[:last] += jnp.where(wide_lane == h, back, 0.0)
            crossing_grad = crossing_grad + mixing_grad * weighted
            step_part = jnp.sum(mixing_grad * crossing * decays, axis=0, keepdims=True)
            gap_part = mixing_grad * mixing
            down = jnp.where(column == h, jnp.sum(gap_part, axis=1, keepdims=True), down)
            cols_grad[h : h + 1, :last] += step_part
            cols_grad[heads + h : heads + h + 1, :last] += step_part * step_row
        rows_grad[first:last] += down
        reads_grad[first:last] = dot_fine(crossing_grad, keys[:last], 1, 0)
        keys_grad[:last] += dot_fine(crossing_grad, reads[first:last], 0, 0)
    turned = cols_grad[...].T
    column = grid_iota(turned.shape, 1)
    step_grad = jnp.where(column < heads, turned, 0.0)
    ended = pltpu.roll(turned, turned.shape[1] - heads, 1)
    running_grad = jnp.where(column < heads, rows_grad[...] - ended, 0.0)
    rates_grad = dot_fine(triangle, running_grad, 0, 0)
    step_grad = step_grad - rates_grad * jnp.exp(head_ref[1:2])
    raw_grad = step_grad * jax.nn.sigmoid(raw)
    out_ref[:, channels:] = raw_grad
    lane = grid_iota((places, width), 1) // 64
    product = jnp.sum(grad * values, axis=0, keepdims=True)
    head_grad_ref[...] = jnp.zeros_like(head_grad_ref)
    head_grad_ref[0:1] = jnp.sum(raw_grad, axis=0, keepdims=True)
    head_grad_ref[1:2] = jnp.sum(rates_grad * rates, axis=0, keepdims=True)
    skip_lane = grid_iota((1, width), 1)
    skip_grad = jnp.zeros((1, width), jnp.float32)
    for h in range(heads):
        own = jnp.sum(jnp.where(skip_lane // 64 == h, product, 0.0), axis=1, keepdims=True)
        skip_grad = jnp.where(skip_lane == h, own, skip_grad)
    head_grad_ref[2:3] = skip_grad
    active_grad = jnp.concatenate([values_grad[...], keys_grad[...], reads_grad[...]], axis=1)
    conv_grad = active_grad * gate * (1.0 + conv_sum * (1.0 - gate))
    back = conv_ref[3:4] * conv_grad
    conv_grad_ref[...] = jnp.zeros_like(conv_grad_ref)
    conv_grad_ref[3:4] = jnp.sum(conv_grad * xbc, axis=0, keepdims=True)
    conv_grad_ref[4:5] = jnp.sum(conv_grad, axis=0, keepdims=True)
    for k in range(3):
        kept = conv_grad * same_ref[:, k : k + 1]
        back = back + conv_ref[k : k + 1] * shifted_up(kept, 3 - k)
        conv_grad_ref[k : k + 1] = jnp.sum(
            kept * shifted_down(xbc, 3 - k), axis=0, keepdims=True
        )
    out_ref[:, :channels] = back


def scan_forward(args, width):
    places = args[0].shape[0]
    return pl.pallas_call(
        scan_forward_kernel,
        out_shape=jax.ShapeDtypeStruct((places, width), jnp.float32),
        compiler_params=ROOMY,
        cost_estimate=NO_COST,
    )(*args)


def scan_backward(args, grad):
    places, width = grad.shape
    channels = args[2].shape[1]
    f32 = jnp.float32
    return pl.pallas_call(
        scan_backward_kernel,
        out_shape=[
            jax.ShapeDtypeStruct((places, channels + 128), f32),
            jax.ShapeDtypeStruct((8, channels), f32),
            jax.ShapeDtypeStruct((8, 128), f32),
        ],
        scratch_shapes=[
            pltpu.VMEM((places, width), f32),
            pltpu.VMEM((places, NS), f32),
            pltpu.VMEM((places, NS), f32),
            pltpu.VMEM((places, 128), f32),
            pltpu.VMEM((128, places), f32),
        ],
        compiler_params=ROOMY,
        cost_estimate=NO_COST,
    )(*args, grad)


def patch_lanes(block):
    shape = (block // 8, 8, block)
    return grid_iota(shape, 0) == grid_iota(shape, 2) // 8


def folded(scores, same_patch):
    split = scores.reshape(same_patch.shape)
    return jnp.sum(jnp.where(same_patch, split, 0.0), axis=0)


def unfolded(rows, same_patch):
    spread = jnp.where(same_patch, rows[None], 0.0)
    return spread.reshape(-1, rows.shape[1]).astype(jnp.bfloat16)


def softmax_rows(scores, causal):
    scores = jnp.where(causal, scores, masked_score)
    top = jnp.max(scores, axis=1, keepdims=True)
    powers = jnp.exp(scores - top)
    return powers / jnp.sum(powers, axis=1, keepdims=True)


def head_places(rows, head_cols, block):
    return [
        (slice(first, first + block), [j * head_cols + pair * 128 for j in range(3)])
        for first in range(0, rows, block)
        for pair in range(head_cols // 128)
    ]


def all_scores(qkv_ref, places, lane, same_patch):
    scores = []
    for rows, (query, key, unused) in places:
        queries = qkv_ref[rows, query : query + 128] * 0.125
        keys = qkv_ref[rows, key : key + 128]
        for h in range(2):
            own = jnp.where(lane == h, queries, 0)
            scores.append(folded(dot_trans(keys, own), same_patch))
    return jnp.stack(scores)


def attn_forward_kernel(
    bytes_ref, patch_ref, gain_ref, qkv_w_ref, o_w_ref, x_ref, a_ref, qkv_ref, o_ref, out_ref
):
    rows = bytes_ref.shape[0]
    spread = jnp.broadcast_to(patch_ref[...][:, None], (rows // 8, 8, patch_ref.shape[1]))
    x = bytes_ref[...].astype(jnp.float32) + spread.reshape(bytes_ref.shape)
    x_ref[...] = x
    attn_in = (x * rms_scale(x) * gain_ref[...]).astype(jnp.bfloat16)
    a_ref[...] = attn_in
    qkv_ref[...] = dot_plain(attn_in, qkv_w_ref[...]).astype(jnp.bfloat16)
    head_cols = o_ref.shape[1]
    block = 128
    same_patch = patch_lanes(block)
    causal = grid_iota((8, block), 0) <= grid_iota((8, block), 1) % 8
    lane = grid_iota((block, 128), 1) // AD
    places = head_places(rows, head_cols, block)
    probs = softmax_rows(all_scores(qkv_ref, places, lane, same_patch), causal)
    for at, (row_place, (query, unused, value)) in enumerate(places):
        values = qkv_ref[row_place, value : value + 128]
        parts = [dot_left(unfolded(probs[2 * at + h], same_patch), values) for h in range(2)]
        total = jnp.where(lane == 0, parts[0], parts[1])
        o_ref[row_place, query : query + 128] = total.astype(jnp.bfloat16)
    out_ref[...] = dot_trans(o_ref[...], o_w_ref[...])


def attn_forward(bytes_rows, patch_rows, gain, w_qkv, w_o):
    rows, width = bytes_rows.shape
    block = 256
    cols, head_cols = w_qkv.shape[1], w_o.shape[1]
    f32, bf16 = jnp.float32, jnp.bfloat16

    def by_rows(cols):
        return pl.BlockSpec((block, cols), lambda i: (i, 0))

    def whole(shape):
        return pl.BlockSpec(shape, lambda i: (0, 0))

    return pl.pallas_call(
        attn_forward_kernel,
        grid=(rows // block,),
        in_specs=[
            by_rows(width),
            pl.BlockSpec((block // 8, width), lambda i: (i, 0)),
            whole((1, width)),
            whole(w_qkv.shape),
            whole(w_o.shape),
        ],
        out_specs=[by_rows(width), by_rows(width), by_rows(cols), by_rows(head_cols), by_rows(width)],
        out_shape=[
            jax.ShapeDtypeStruct((rows, width), f32),
            jax.ShapeDtypeStruct((rows, width), bf16),
            jax.ShapeDtypeStruct((rows, cols), bf16),
            jax.ShapeDtypeStruct((rows, head_cols), bf16),
            jax.ShapeDtypeStruct((rows, width), f32),
        ],
        compiler_params=ROOMY,
        cost_estimate=NO_COST,
    )(bytes_rows, patch_rows, gain.reshape(1, width), w_qkv, w_o)


def attn_backward_kernel(
    x_ref,
    final_ref,
    own_ref,
    other_ref,
    gain_ref,
    qkv_ref,
    qkv_w_ref,
    o_w_ref,
    mid_ref,
    low_ref,
    qkv_grad_ref,
    out_ref,
    gain_grad_ref,
):
    rows = x_ref.shape[0]
    back, gain_grad = rms_back(x_ref[...], gain_ref[...], own_ref[...] + other_ref[...])
    mid = final_ref[...] + back
    mid_ref[...] = mid
    low_ref[...] = mid.astype(jnp.bfloat16)
    gain_grad = gain_grad.reshape(1, -1)

    @pl.when(pl.program_id(0) == 0)
    def _():
        gain_grad_ref[...] = gain_grad

    @pl.when(pl.program_id(0) > 0)
    def _():
        gain_grad_ref[...] += gain_grad

    mixed_grad = dot_plain(low_ref[...], o_w_ref[...]).astype(jnp.bfloat16)
    head_cols = mixed_grad.shape[1]
    block = 128
    same_patch = patch_lanes(block)
    causal = grid_iota((8, block), 0) <= grid_iota((8, block), 1) % 8
    lane = grid_iota((block, 128), 1) // AD
    places = head_places(rows, head_cols, block)
    probs = softmax_rows(all_scores(qkv_ref, places, lane, same_patch), causal)
    probs_grads = []
    for row_place, (query, unused, value) in places:
        values = qkv_ref[row_place, value : value + 128]
        out_grad = mixed_grad[row_place, query : query + 128]
        for h in range(2):
            own_grad = jnp.where(lane == h, out_grad, 0)
            probs_grads.append(folded(dot_trans(values, own_grad), same_patch))
    probs_grad = jnp.stack(probs_grads)
    inner = jnp.sum(probs * probs_grad, axis=1, keepdims=True)
    scores_grad = probs * (probs_grad - inner)
    for at, (row_place, cols) in enumerate(places):
        query, key, unused = cols
        queries = qkv_ref[row_place, query : query + 128]
        keys = qkv_ref[row_place, key : key + 128]
        out_grad = mixed_grad[row_place, query : query + 128]
        parts = []
        for h in range(2):
            own_scores = unfolded(scores_grad[2 * at + h], same_patch)
            parts.append(
                (
                    dot_left(own_scores, keys) * 0.125,
                    dot_plain(own_scores, queries) * 0.125,
                    dot_plain(unfolded(probs[2 * at + h], same_patch), out_grad),
                )
            )
        for j in range(3):
            grad = jnp.where(lane == 0, parts[0][j], parts[1][j])
            qkv_grad_ref[row_place, cols[j] : cols[j] + 128] = grad.astype(jnp.bfloat16)
    out_ref[...] = dot_trans(qkv_grad_ref[...], qkv_w_ref[...])


def attn_backward(x_rows, final_grad, own_part, other_part, gain, qkv, w_qkv, w_o):
    rows, width = x_rows.shape
    block = 256
    cols = w_qkv.shape[1]
    f32, bf16 = jnp.float32, jnp.bfloat16

    def by_rows(cols):
        return pl.BlockSpec((block, cols), lambda i: (i, 0))

    def whole(shape):
        return pl.BlockSpec(shape, lambda i: (0, 0))

    return pl.pallas_call(
        attn_backward_kernel,
        grid=(rows // block,),
        in_specs=[by_rows(width)] * 4
        + [whole((1, width)), by_rows(cols), whole(w_qkv.shape), whole(w_o.shape)],
        out_specs=[
            by_rows(width),
            by_rows(width),
            by_rows(cols),
            by_rows(width),
            whole((1, width)),
        ],
        out_shape=[
            jax.ShapeDtypeStruct((rows, width), f32),
            jax.ShapeDtypeStruct((rows, width), bf16),
            jax.ShapeDtypeStruct((rows, cols), bf16),
            jax.ShapeDtypeStruct((rows, width), f32),
            jax.ShapeDtypeStruct((1, width), f32),
        ],
        compiler_params=ROOMY,
        cost_estimate=NO_COST,
    )(x_rows, final_grad, own_part, other_part, gain.reshape(1, width), qkv, w_qkv, w_o)


def mlp_in_kernel(core_ref, x_ref, own_ref, other_ref, gain_ref, out_ref, low_ref, half_ref):
    x = x_ref[...] + (own_ref[...] + other_ref[...])
    out_ref[...] = x
    unit = x * rms_scale(x)
    low_ref[...] = (unit * gain_ref[...]).astype(jnp.bfloat16)
    width = half_ref.shape[1]
    half_ref[...] = jnp.where(core_ref[0] == 0, unit[:, :width], unit[:, width:])


def mlp_in(x_rows, own_part, other_part, gain):
    rows, width = x_rows.shape
    block = 128
    core = lax.axis_index("tp").astype(jnp.int32).reshape(1)

    def by_rows(cols):
        return pl.BlockSpec((block, cols), lambda i, ref: (i, 0))

    return pl.pallas_call(
        mlp_in_kernel,
        grid_spec=pltpu.PrefetchScalarGridSpec(
            num_scalar_prefetch=1,
            grid=(rows // block,),
            in_specs=[by_rows(width)] * 3 + [pl.BlockSpec((1, width), lambda i, ref: (0, 0))],
            out_specs=[by_rows(width), by_rows(width), by_rows(width // 2)],
        ),
        out_shape=[
            jax.ShapeDtypeStruct((rows, width), jnp.float32),
            jax.ShapeDtypeStruct((rows, width), jnp.bfloat16),
            jax.ShapeDtypeStruct((rows, width // 2), jnp.float32),
        ],
        compiler_params=ROOMY,
        cost_estimate=NO_COST,
    )(core, x_rows, own_part, other_part, gain.reshape(1, width))


def units_in_halves(
    mlp_low, grad_ref, gate_w_ref, up_w_ref, hidden_ref, gate_ref, up_ref
):
    half = grad_ref.shape[1] // 2
    for at in range(2):
        cols = slice(at * half, (at + 1) * half)
        hidden, gate, up = hidden_parts(
            mlp_low, grad_ref[:, cols], gate_w_ref[:, cols], up_w_ref[:, cols]
        )
        hidden_ref[:, cols] = hidden
        gate_ref[:, cols] = gate
        up_ref[:, cols] = up


def mlp_kernel(
    in_ref, grad_ref, gate_w_ref, up_w_ref, hidden_ref, gate_ref, up_ref, out_ref, total_ref
):
    mlp_low = in_ref[...]
    units_in_halves(
        mlp_low, grad_ref, gate_w_ref, up_w_ref, hidden_ref, gate_ref, up_ref
    )
    part = dot_trans(gate_ref[...], gate_w_ref[...]) + dot_trans(up_ref[...], up_w_ref[...])
    step = pl.program_id(0)

    @pl.when(step == 0)
    def _():
        total_ref[...] = part

    @pl.when(step > 0)
    def _():
        total_ref[...] += part

    @pl.when(step == pl.num_programs(0) - 1)
    def _():
        out_ref[...] = total_ref[...]


def mlp_rows(mlp_low, grad_hidden, w_gate, w_up):
    rows, width = mlp_low.shape
    units = w_gate.shape[1]
    block = 512
    by_units = pl.BlockSpec((rows, block), lambda i: (0, i))
    by_weights = pl.BlockSpec((width, block), lambda i: (0, i))
    whole = pl.BlockSpec((rows, width), lambda i: (0, 0))
    low = jax.ShapeDtypeStruct((rows, units), jnp.bfloat16)
    return pl.pallas_call(
        mlp_kernel,
        grid=(units // block,),
        in_specs=[whole, by_units, by_weights, by_weights],
        out_specs=[by_units, by_units, by_units, whole],
        out_shape=[low, low, low, jax.ShapeDtypeStruct((rows, width), jnp.float32)],
        scratch_shapes=[pltpu.VMEM((rows, width), jnp.float32)],
        compiler_params=ROOMY,
        cost_estimate=NO_COST,
    )(mlp_low, grad_hidden, w_gate, w_up)


def feature_order(width):
    shape = (8 * width, 8 * width)
    row, col = grid_iota(shape, 0), grid_iota(shape, 1)
    return jnp.where(row == (col % 8) * width + col // 8, 1.0, 0.0).astype(jnp.bfloat16)


def patch_in_kernel(core_ref, bytes_ref, weight_ref, wide_ref, out_ref, rows_ref, order_ref):
    places, feature = wide_ref.shape[0], wide_ref.shape[1] // 8
    chunk = weight_ref.shape[1] // 8
    step = pl.program_id(0)

    @pl.when(step == 0)
    def _():
        order_ref[...] = feature_order(chunk)
        for at in range(feature // 128):
            low = at * 128
            rows_ref[at] = bytes_ref[:, low : low + 128].astype(jnp.float32)
            for j in range(8):
                wide_ref[:, j * feature + low : j * feature + low + 128] = rows_ref[
                    at, pl.ds(j, places, stride=8), :
                ]

    parts = [
        wide_ref[:, pl.ds(pl.multiple_of(j * feature + step * chunk, 128), chunk)]
        for j in range(8)
    ]
    by_byte = jnp.concatenate(parts, axis=1).astype(jnp.bfloat16)
    by_feature = dot_plain(by_byte, order_ref[...]).astype(jnp.bfloat16)
    part = dot_trans(by_feature, weight_ref[...])

    @pl.when(step == 0)
    def _():
        out_ref[...] = part

    @pl.when(step > 0)
    def _():
        out_ref[...] += part


def patch_in(byte_rows, w_patch):
    rows, model_width = byte_rows.shape
    out_width, cols = w_patch.shape
    feature, chunk = cols // 8, 128
    core = lax.axis_index("tp").astype(jnp.int32).reshape(1)
    f32 = jnp.float32
    return pl.pallas_call(
        patch_in_kernel,
        grid_spec=pltpu.PrefetchScalarGridSpec(
            num_scalar_prefetch=1,
            grid=(feature // chunk,),
            in_specs=[
                pl.BlockSpec((rows, feature), lambda i, ref: (0, ref[0])),
                pl.BlockSpec((out_width, 8 * chunk), lambda i, ref: (0, i)),
            ],
            out_specs=[
                pl.BlockSpec((rows // 8, cols), lambda i, ref: (0, 0)),
                pl.BlockSpec((rows // 8, out_width), lambda i, ref: (0, 0)),
            ],
            scratch_shapes=[
                pltpu.VMEM((feature // 128, rows, 128), f32),
                pltpu.VMEM((8 * chunk, 8 * chunk), jnp.bfloat16),
            ],
        ),
        out_shape=[
            jax.ShapeDtypeStruct((rows // 8, cols), f32),
            jax.ShapeDtypeStruct((rows // 8, out_width), f32),
        ],
        compiler_params=ROOMY,
        cost_estimate=NO_COST,
    )(core, byte_rows, w_patch)


def final_kernel(
    member_ref,
    own_ref,
    other_ref,
    mask_ref,
    own_head_ref,
    other_head_ref,
    weight_ref,
    low_ref,
    hidden_ref,
    mine_ref,
    mine_low_ref,
):
    own = (own_ref[...] * mask_ref[...]).astype(jnp.bfloat16)
    other = (other_ref[...] * mask_ref[...]).astype(jnp.bfloat16)
    other_head = other_head_ref[...].astype(jnp.bfloat16)
    total = dot_trans(own, own_head_ref[...]) + dot_trans(other, other_head)
    low = total.astype(jnp.bfloat16)
    low_ref[...] = low
    hidden_ref[...] = dot_plain(low, weight_ref[...])

    @pl.when(pl.program_id(0) == member_ref[0])
    def _():
        mine_ref[...] = total
        mine_low_ref[...] = low


def final_grads(own, other, mask, own_head, other_head, w_down, member):
    rows, cols = own.shape
    width = own_head.shape[0]
    block = rows // QUAD
    units = w_down.shape[1] // QUAD
    f32, bf16 = jnp.float32, jnp.bfloat16

    def by_rows(cols):
        return pl.BlockSpec((block, cols), lambda i, ref: (i, 0))

    head = pl.BlockSpec((width, cols), lambda i, ref: (0, 0))
    mine = pl.BlockSpec((block, width), lambda i, ref: (0, 0))
    return pl.pallas_call(
        final_kernel,
        grid_spec=pltpu.PrefetchScalarGridSpec(
            num_scalar_prefetch=1,
            grid=(QUAD,),
            in_specs=[by_rows(cols), by_rows(cols), by_rows(1), head, head]
            + [pl.BlockSpec((width, units), lambda i, ref: (0, ref[0]))],
            out_specs=[by_rows(width), by_rows(units), mine, mine],
        ),
        out_shape=[
            jax.ShapeDtypeStruct((rows, width), bf16),
            jax.ShapeDtypeStruct((rows, units), f32),
            jax.ShapeDtypeStruct((block, width), f32),
            jax.ShapeDtypeStruct((block, width), bf16),
        ],
        compiler_params=ROOMY,
        cost_estimate=NO_COST,
    )(member, own, other, mask, own_head, other_head, w_down)


def group_mlp_kernel(
    place_ref,
    own_ref,
    other_ref,
    gain_ref,
    grad_ref,
    gate_w_ref,
    up_w_ref,
    in_ref,
    hidden_ref,
    gate_ref,
    up_ref,
):
    own, other = own_ref[0], other_ref[0]
    first = place_ref[1] == 0
    halves = [jnp.where(first, own, other), jnp.where(first, other, own)]
    low = (jnp.concatenate(halves, axis=1) * gain_ref[...]).astype(jnp.bfloat16)
    in_ref[...] = low
    units_in_halves(low, grad_ref, gate_w_ref, up_w_ref, hidden_ref, gate_ref, up_ref)


def group_mlp(own_half, other_half, gain, grad_hidden, w_gate, w_up, member):
    rows, half = grad_hidden.shape[0] // QUAD, own_half.shape[2]
    width, units = 2 * half, w_gate.shape[1] // QUAD
    bf16 = jnp.bfloat16
    place = jnp.concatenate([member, lax.axis_index("tp").astype(jnp.int32).reshape(1)])

    def by_rows(cols):
        return pl.BlockSpec((rows, cols), lambda i, ref: (i, 0))

    halves = pl.BlockSpec((1, rows, half), lambda i, ref: (i ^ ref[0], 0, 0))
    weights = pl.BlockSpec((width, units), lambda i, ref: (0, ref[0]))
    low = jax.ShapeDtypeStruct((QUAD * rows, units), bf16)
    return pl.pallas_call(
        group_mlp_kernel,
        grid_spec=pltpu.PrefetchScalarGridSpec(
            num_scalar_prefetch=1,
            grid=(QUAD,),
            in_specs=[
                halves,
                halves,
                pl.BlockSpec((1, width), lambda i, ref: (0, 0)),
                by_rows(units),
                weights,
                weights,
            ],
            out_specs=[by_rows(width), by_rows(units), by_rows(units), by_rows(units)],
        ),
        out_shape=[jax.ShapeDtypeStruct((QUAD * rows, width), bf16), low, low, low],
        compiler_params=ROOMY,
        cost_estimate=NO_COST,
    )(place, own_half, other_half, gain.reshape(1, width), grad_hidden, w_gate, w_up)


def bytes_grad_kernel(core_ref, grad_ref, weight_ref, stream_ref, out_ref, order_ref):
    places = grad_ref.shape[0]
    chunk = weight_ref.shape[1] // 8

    @pl.when(pl.program_id(0) == 0)
    def _():
        order_ref[...] = feature_order(chunk)

    by_feature = dot_plain(grad_ref[...].astype(jnp.bfloat16), weight_ref[...])
    high = by_feature.astype(jnp.bfloat16)
    rest = by_feature - high.astype(jnp.float32)
    mid = rest.astype(jnp.bfloat16)
    low = (rest - mid.astype(jnp.float32)).astype(jnp.bfloat16)
    order = order_ref[...]
    by_byte = dot_trans(high, order) + (dot_trans(mid, order) + dot_trans(low, order))
    for j in range(8):
        rows = pl.ds(j, places, stride=8)
        out_ref[rows, :] = stream_ref[rows, :] + by_byte[:, j * chunk : (j + 1) * chunk]


def bytes_grad(grad_patch, w_patch, grad_stream):
    places, width = grad_patch.shape
    rows = grad_stream.shape[0]
    cols = w_patch.shape[1]
    feature, chunk = cols // 8, 128
    core = lax.axis_index("tp").astype(jnp.int32).reshape(1)
    return pl.pallas_call(
        bytes_grad_kernel,
        grid_spec=pltpu.PrefetchScalarGridSpec(
            num_scalar_prefetch=1,
            grid=(feature // chunk,),
            in_specs=[
                pl.BlockSpec((places, width), lambda i, ref: (0, 0)),
                pl.BlockSpec((width, 8 * chunk), lambda i, ref: (0, i)),
                pl.BlockSpec((rows, chunk), lambda i, ref: (0, ref[0] * (feature // chunk) + i)),
            ],
            out_specs=pl.BlockSpec((rows, chunk), lambda i, ref: (0, i)),
            scratch_shapes=[pltpu.VMEM((8 * chunk, 8 * chunk), jnp.bfloat16)],
        ),
        out_shape=jax.ShapeDtypeStruct((rows, feature), jnp.float32),
        compiler_params=ROOMY,
        cost_estimate=NO_COST,
    )(core, grad_patch, w_patch, grad_stream)


def body(
    byte_states,
    lengths,
    w_patch,
    norm_global,
    w_in,
    conv_w,
    conv_b,
    dt_bias,
    a_log,
    d_skip,
    mix_gain,
    w_out,
    norm_attn,
    w_qkv,
    w_o,
    norm_mlp,
    w_gate,
    w_up,
    w_down,
    w_head,
    d_logits,
):
    streams, local_rows, model_width = byte_states.shape
    patch_count = local_rows // 8
    patch_total = streams * patch_count
    row_total = streams * local_rows
    feature = w_patch.shape[1] // 8
    inner_width = w_out.shape[1]
    channels = conv_w.shape[1]
    head_total = dt_bias.shape[0]
    head_cols = w_head.shape[1]
    parts = lax.axis_size("seq")
    tp_index = lax.axis_index("tp")
    seq_index = lax.axis_index("seq")
    places = parts * patch_count
    f32 = jnp.float32

    lanes = parts // streams
    width = inner_width // lanes
    full_head = inner_width // head_total
    own_heads = max(1, width // full_head)
    shared = max(1, full_head // width)
    head_size = width // own_heads
    own_stream = seq_index // lanes
    first_col = (seq_index % lanes) * width
    first_head = first_col // full_head

    seg_full = segment_ids(lengths, places)
    seg_own = lax.dynamic_slice_in_dim(seg_full, seq_index * patch_count, patch_count, 1)
    seg_stream = lax.dynamic_index_in_dim(seg_full, own_stream, 0, keepdims=False)
    valid = (seg_own < lengths.shape[0]).astype(f32).reshape(patch_total, 1)
    byte_valid = jnp.repeat(valid, 8, axis=0)

    member = (seq_index >> 2 & 1) * 2 + (seq_index & 1)
    raw_logits = d_logits.reshape(row_total, head_cols)
    raw_wide = raw_logits.astype(f32)
    group_valid = []
    for high in range(2):
        for low in range(2):
            device = (seq_index & ~5) | high << 2 | low
            group_seg = lax.dynamic_slice_in_dim(
                seg_full, device * patch_count, patch_count, 1
            )
            group_valid.append((group_seg < lengths.shape[0]).astype(f32))
    group_valid = jnp.stack(group_valid).reshape(QUAD, patch_total, 1)
    group_bytes_valid = jnp.repeat(group_valid.reshape(-1, 1), 8, axis=0)
    group_raw = side_trade(jnp.broadcast_to(raw_wide[None], (QUAD,) + raw_wide.shape))
    group_raw = group_raw.reshape(-1, head_cols)
    other_raw = swap(group_raw, "tp", 1)
    other_head = swap(w_head.astype(f32), "tp", 1)
    place_index = member.astype(jnp.int32).reshape(1)
    bytes_wide, patch_part = patch_in(byte_states.reshape(row_total, model_width), w_patch)
    patch_out = tp_sum(patch_part)
    gain_global = norm_global.astype(f32)
    unit_patch = patch_out * rms_scale(patch_out)
    u_low = (unit_patch * gain_global).astype(jnp.bfloat16)
    half_width = model_width // 2
    proj = dot_plain(u_low, w_in).reshape(streams, patch_count, -1)
    gate_in = proj[..., :inner_width]
    xbc = proj[..., inner_width : inner_width + channels]
    dt_raw = proj[..., inner_width + channels :]

    def by_lane(columns):
        split = columns.reshape(streams, patch_count, lanes, -1)
        return jnp.moveaxis(split, 2, 1).reshape(parts, patch_count, -1)

    def from_lanes(blocks):
        split = blocks.reshape(streams, lanes, patch_count, -1)
        return jnp.moveaxis(split, 1, 2).reshape(streams, patch_count, -1)

    def to_all_lanes(columns):
        wide = jnp.broadcast_to(
            columns[:, None], (streams, lanes, patch_count, columns.shape[-1])
        )
        return wide.reshape(parts, patch_count, -1)

    pad_width = 128 - own_heads
    dt_lanes = by_lane(jnp.repeat(dt_raw, shared, axis=2))
    sent = jnp.concatenate(
        [
            by_lane(xbc[..., :inner_width]),
            to_all_lanes(xbc[..., inner_width:]),
            jnp.pad(dt_lanes, ((0, 0), (0, 0), (0, pad_width))),
        ],
        axis=-1,
    )
    taken = trade(sent)
    grad_logits = after(raw_logits, sent) * byte_valid.astype(jnp.bfloat16)
    group_final, group_grad_hidden, grad_final, grad_mlp_low = final_grads(
        after(group_raw, sent),
        other_raw,
        group_bytes_valid,
        w_head,
        other_head,
        w_down,
        place_index,
    )
    grad_hidden = dot_plain(grad_mlp_low, w_down)
    hidden_part = w_gate.shape[1] // QUAD

    row_side = [
        [device for device in range(parts) if (device & 1) == side] for side in range(2)
    ]
    bytes_all = lax.all_gather(
        bytes_wide, "seq", axis=0, axis_index_groups=row_side, tiled=True
    )
    taken = after(taken, grad_hidden, group_grad_hidden).reshape(places, -1)
    scan_width = width + channels - inner_width

    def own_cols(param):
        mine = lax.dynamic_slice_in_dim(param, first_col, width, param.ndim - 1)
        return jnp.concatenate([mine, param[..., inner_width:]], axis=-1).astype(f32)

    def own_head(param):
        return lax.dynamic_slice_in_dim(param, first_head, own_heads, 0).astype(f32)

    use_kernel = places == 512 and width == 128
    if use_kernel:
        padded_seg = jnp.pad(seg_stream, (3, 0), constant_values=-1)
        same = jnp.stack(
            [(padded_seg[k : k + places] == seg_stream).astype(f32) for k in range(3)]
            + [jnp.zeros((places,), f32)] * 5,
            axis=1,
        )
        conv_pack = jnp.concatenate(
            [own_cols(conv_w), own_cols(conv_b)[None], jnp.zeros((3, scan_width), f32)]
        )
        head_pack = jnp.stack(
            [jnp.pad(own_head(dt_bias), (0, 128 - own_heads))]
            + [jnp.pad(own_head(a_log), (0, 128 - own_heads))]
            + [jnp.repeat(own_head(d_skip), head_size)]
            + [jnp.zeros((128,), f32)] * 5
        )
        scan_args = (taken, same, conv_pack, head_pack, seg_stream[:, None], seg_stream[None])
        scanned = scan_forward(scan_args, width)
    else:
        scan_args = (
            taken[:, :scan_width],
            taken[:, scan_width : scan_width + own_heads],
            own_cols(conv_w),
            own_cols(conv_b),
            own_head(dt_bias),
            own_head(a_log),
            own_head(d_skip),
        )
        scanned, scan_back = jax.vjp(partial(scan_heads, seg_stream, head_size), *scan_args)
    result = from_lanes(trade(scanned.reshape(parts, patch_count, width)))
    unit_normed, norm_back = jax.vjp(gated_unit, result, gate_in)
    mix_scale = mix_gain.astype(f32)
    normed_low = (unit_normed * mix_scale).reshape(patch_total, -1).astype(jnp.bfloat16)


    def quarters(columns):
        split = columns.reshape(patch_total, QUAD, -1)
        return jnp.moveaxis(split, 1, 0)

    def by_apart(blocks):
        return [
            lax.dynamic_index_in_dim(blocks, member ^ apart, 0, keepdims=False)
            for apart in range(QUAD)
        ]

    def group_swap(blocks):
        moved = [swap(block, "seq", mask) for block, mask in zip(blocks[1:], (1, 4, 5))]
        return jnp.concatenate([blocks[0]] + moved, axis=0)

    early_got = group_swap(
        [
            jnp.concatenate([unit_patch, part], axis=-1)
            for part in by_apart(quarters(unit_normed))
        ]
    )
    global_out = patch_out + valid * tp_sum(dot_trans(normed_low, w_out))
    gain_attn = norm_attn.astype(f32)
    gain_mlp = norm_mlp.astype(f32)
    stream_in, attn_in, qkv, mixed_low, attn_part = attn_forward(
        byte_states.reshape(row_total, model_width), global_out, gain_attn, w_qkv, w_o
    )
    after_attn, mlp_low, unit_half = mlp_in(
        stream_in, attn_part, swap(attn_part, "tp", 1), gain_mlp
    )
    hidden_low, grad_gate_low, grad_up_low, grad_mlp_part = mlp_rows(
        after(mlp_low, unit_half), grad_hidden, w_gate, w_up
    )
    near_halves = [swap(unit_half, "seq", mask) for mask in (1, 4, 5)]
    grad_mlp_other = swap(grad_mlp_part, "tp", 1)
    after_mlp = after_attn + tp_sum(dot_trans(after(hidden_low, grad_mlp_part), w_down))
    final_low = after_mlp.astype(jnp.bfloat16)
    logits = dot_plain(final_low, w_head) * byte_valid
    grad_mid, grad_attn_low, grad_qkv_low, grad_attn_part, grad_norm_mlp = attn_backward(
        after_attn, grad_final, grad_mlp_part, grad_mlp_other, gain_mlp, qkv, w_qkv, w_o
    )
    grad_norm_mlp = grad_norm_mlp.reshape(-1)
    grad_attn_in = tp_sum(grad_attn_part)

    back_attn, grad_norm_attn = rms_back(stream_in, gain_attn, grad_attn_in)
    grad_stream = grad_mid + back_attn
    grad_global = jnp.sum(grad_stream.reshape(patch_total, 8, model_width), axis=1)
    grad_mix_low = (grad_global * valid).astype(jnp.bfloat16)
    grad_normed = dot_plain(grad_mix_low, w_out).reshape(streams, patch_count, inner_width)
    grad_mix_gain = jnp.sum(grad_normed * unit_normed, axis=(0, 1))
    grad_result, grad_gate_in = norm_back(grad_normed * mix_scale)
    grad_z_low = grad_gate_in.reshape(patch_total, inner_width).astype(jnp.bfloat16)
    row_block = model_width // parts
    dealing = after(by_lane(grad_result), bytes_all)
    dealt = trade(dealing)
    late_sent = [
        jnp.concatenate([grad_global, part], axis=-1) for part in by_apart(quarters(grad_gate_in))
    ]
    late_got = group_swap(late_sent)
    apart_valid = jnp.concatenate(by_apart(group_valid), axis=0)
    group_mix = (late_got[:, :model_width] * apart_valid).astype(jnp.bfloat16)
    group_z = late_got[:, model_width:]
    attn_cut = 1024 if grad_qkv_low.shape[1] > 1024 else 128
    attn_in_late = after(attn_in, dealing)
    attn_cols = grad_qkv_low.shape[1]
    attn_blocks = (
        grad_blocks([(attn_in_late, grad_qkv_low, 0, attn_cut)], 0, True),
        grad_blocks(
            [
                (attn_in_late, grad_qkv_low, attn_cut, attn_cols),
                (grad_attn_low, mixed_low, 0, mixed_low.shape[1]),
                (final_low, grad_logits, 0, head_cols),
            ],
            1,
            True,
        ),
    )
    attn_got = [to_partner(attn_blocks[first][0], first) for first in range(2)]
    dealt = after(dealt, attn_blocks[0][0], attn_blocks[1][0], *near_halves[:2])
    grad_scanned = dealt.reshape(places, width)
    if use_kernel:
        back_sent, conv_grads, head_grads = scan_backward(scan_args, grad_scanned)
        lane_grad = back_sent[:, : scan_width + own_heads]
        scan_params = (
            conv_grads[:4],
            conv_grads[4],
            head_grads[0, :own_heads],
            head_grads[1, :own_heads],
            head_grads[2, :own_heads],
        )
    else:
        scan_grads = scan_back(grad_scanned)
        back_sent = jnp.concatenate(
            [scan_grads[0], jnp.pad(scan_grads[1], ((0, 0), (0, pad_width)))], axis=-1
        )
        lane_grad = jnp.concatenate([scan_grads[0], scan_grads[1]], axis=-1)
        scan_params = scan_grads[2:]
    back_sent = back_sent.reshape(parts, patch_count, -1)
    back_taken = trade(back_sent)
    own_half = after(jnp.stack([unit_half] + near_halves), back_sent)
    group_in, group_hidden, group_gate, group_up = group_mlp(
        own_half, swap(own_half, "tp", 1), gain_mlp, group_grad_hidden, w_gate, w_up, place_index
    )
    late_early = after(early_got, back_sent)
    group_u = (late_early[:, :model_width] * gain_global).astype(jnp.bfloat16)
    quarter = inner_width // QUAD
    own_scale = lax.dynamic_slice_in_dim(mix_scale, member * quarter, quarter, 0)
    group_n = (late_early[:, model_width:] * own_scale).astype(jnp.bfloat16)
    mlp_blocks = [
        grad_blocks(
            [(group_final, group_hidden, 0, hidden_part), (group_in, group_gate, 0, hidden_part)],
            1,
            False,
        ),
        grad_blocks(
            [
                (group_in, group_up, 0, hidden_part),
                (group_mix, group_n, 0, group_n.shape[1]),
                (group_u, group_z, 0, group_z.shape[1]),
            ],
            1,
            False,
        ),
    ]
    mlp_got = [to_partner(far, 1) for far, unused in mlp_blocks]
    back_taken = after(back_taken, mlp_blocks[0][0], mlp_blocks[1][0])
    grad_x = from_lanes(back_taken[..., :width])
    by_stream = back_taken.reshape(streams, lanes, patch_count, -1)
    grad_bc = jnp.sum(by_stream[..., width:scan_width], axis=1)
    grad_dt = from_lanes(back_taken[..., scan_width : scan_width + own_heads])
    grad_dt = jnp.sum(grad_dt.reshape(streams, patch_count, head_total, shared), axis=-1)
    grad_shared = jnp.concatenate([grad_bc, grad_dt], axis=-1).reshape(patch_total, -1)
    grad_proj_low = jnp.concatenate(
        [grad_z_low, grad_x.reshape(patch_total, -1).astype(jnp.bfloat16)]
        + [grad_shared.astype(jnp.bfloat16)],
        axis=-1,
    )
    grad_u_part = dot_trans(grad_proj_low, w_in)
    attn_far = [
        add_side(after(attn_blocks[first][1], grad_u_part), attn_got[first], 1)
        for first in range(2)
    ]
    attn_crossed = [to_partner(attn_far[first], 1 - first) for first in range(2)]
    grad_u = after(tp_sum(grad_u_part), *attn_far)
    rest = [quarters(columns) for columns in (grad_x, grad_bc, grad_dt)]
    rest_cols = [part.shape[-1] for part in rest]
    rest = after(jnp.concatenate(rest, axis=-1), grad_u_part)
    rest = jnp.pad(rest, ((0, 0), (0, 0), (0, -sum(rest_cols) % 128)))
    rest_blocks = grad_blocks(
        [(group_u, group_swap(by_apart(rest)), 0, rest.shape[-1])], 1, False
    )
    high = (seq_index // QUAD).astype(jnp.int32).reshape(1)
    attn_near = near_sums(
        [
            (after(attn_blocks[first][1], grad_u), attn_got[first], attn_crossed[first])
            for first in range(2)
        ],
        high,
    )
    attn_high = [
        swap(attn_near[apart], "seq", QUAD * apart) for apart in range(1, parts // QUAD)
    ]
    final_attn = attn_near[0]
    for got in attn_high:
        final_attn = final_attn + got
    back_global, grad_norm_global = rms_back(patch_out, gain_global, grad_u)
    grad_patch = grad_global + back_global
    side_count = parts // 2
    my_side = seq_index & 1
    by_block = jnp.moveaxis(grad_patch.reshape(patch_total, parts, row_block), 1, 0)
    by_block = by_block.reshape(side_count, 2, patch_total, row_block)
    same_side = lax.dynamic_index_in_dim(by_block, my_side, 1, keepdims=False)
    other_side = lax.dynamic_index_in_dim(by_block, 1 - my_side, 1, keepdims=False)
    patch_rows = jnp.concatenate([same_side, other_side], axis=-1)
    patch_rows = patch_rows.reshape(side_count, patch_total, 2 * row_block)
    gain_part = grad_norm_global.reshape(-1, 2 * row_block)
    gain_count = gain_part.shape[0]
    patch_sent = jnp.concatenate(
        [patch_rows, jnp.broadcast_to(gain_part, (side_count,) + gain_part.shape)], axis=1
    )
    patch_taken = lax.all_to_all(
        after(patch_sent, mlp_got[0], final_attn), "seq", 0, 0, axis_index_groups=row_side, tiled=True
    )

    patch_taken = after(patch_taken, rest_blocks[0])
    gain_side = jnp.sum(patch_taken[:, patch_total:], axis=0)
    patch_cols = patch_taken[:, :patch_total].reshape(-1, 2 * row_block)
    patch_far = patch_far_grad(patch_cols, gain_side, bytes_all)
    small = (
        scan_params[0][:, :width],
        scan_params[1][:width],
        scan_params[0][:, width:],
        scan_params[1][width:],
        scan_params[2],
        scan_params[3],
        scan_params[4],
        grad_mix_gain,
        grad_norm_attn,
        grad_norm_mlp,
    )
    small_count = sum(part.size for part in small)
    flat = after(jnp.concatenate([part.reshape(-1) for part in small]), patch_far)
    flat = jnp.pad(flat, (0, -small_count % 1024)).reshape(1, -1, 128)
    pieces = trade(jnp.broadcast_to(flat, (parts,) + flat.shape[1:])).reshape(parts, -1)
    by_small, at = [], 0
    for part in small:
        got = pieces[:, at : at + part.size].reshape((parts,) + part.shape)
        by_small.append(got)
        at += part.size

    def lane_cols(got):
        joined = jnp.sum(got.reshape((streams, lanes) + got.shape[1:]), axis=0)
        return jnp.moveaxis(joined, 0, -2).reshape(joined.shape[1:-1] + (-1,))

    def lane_heads(got):
        joined = jnp.sum(got.reshape(streams, lanes, -1), axis=0)
        return jnp.sum(joined.reshape(head_total, shared), axis=-1)

    small_sums = [
        jnp.concatenate([lane_cols(by_small[0]), jnp.sum(by_small[2], axis=0)], axis=-1),
        jnp.concatenate([lane_cols(by_small[1]), jnp.sum(by_small[3], axis=0)], axis=-1),
        lane_heads(by_small[4]),
        lane_heads(by_small[5]),
        lane_heads(by_small[6]),
    ] + [jnp.sum(got, axis=0) for got in by_small[7:]]

    patch_got = to_partner(patch_far, 0)

    rest_got = to_partner(after(rest_blocks[0], patch_sent), 1)
    mlp_finals = []
    turns = (patch_sent,)
    for blocks, got in zip(mlp_blocks + [rest_blocks], mlp_got + [rest_got]):
        near = after(blocks[1], *turns)
        for bit in reversed(range(3, seq_bits())):
            far, near = split_add(near, got, bit)
            got = to_partner(far, bit)
        turns = (patch_far, far)
        mlp_finals.append(jnp.moveaxis(side_trade(group_add(near, got)), 0, 1))

    def final_cols(final, low, count):
        return final[..., low : low + count].reshape(row_block, -1)

    final_down = final_cols(mlp_finals[0], 0, hidden_part)
    final_gate = final_cols(mlp_finals[0], hidden_part, hidden_part)
    final_up = final_cols(mlp_finals[1], 0, hidden_part)
    final_out = final_cols(mlp_finals[1], hidden_part, quarter)
    final_z = final_cols(mlp_finals[1], hidden_part + quarter, quarter)
    final_x = final_cols(mlp_finals[2], 0, rest_cols[0])
    final_bc = final_cols(mlp_finals[2], rest_cols[0], rest_cols[1])
    final_dt = final_cols(mlp_finals[2], rest_cols[0] + rest_cols[1], rest_cols[2])
    final_patch = patch_grad(patch_cols, patch_got, bytes_all)
    norm_global_sum = (gain_side + patch_got[row_block:, : 2 * row_block]).reshape(-1)
    grad_bytes = bytes_grad(after(grad_patch, patch_far), w_patch, grad_stream)
    grad_bytes = grad_bytes.reshape(streams, local_rows, feature)

    qkv_cols, o_cols = w_qkv.shape[1], w_o.shape[1]
    return (
        logits.reshape(streams, local_rows, head_cols),
        grad_bytes,
        final_patch,
        norm_global_sum,
        jnp.concatenate([final_z, final_x, final_bc, final_dt], axis=1),
        small_sums[0],
        small_sums[1],
        small_sums[2],
        small_sums[3],
        small_sums[4],
        small_sums[5],
        final_out,
        small_sums[6],
        final_attn[:, :qkv_cols],
        final_attn[:, qkv_cols : qkv_cols + o_cols],
        small_sums[7],
        final_gate,
        final_up,
        final_down,
        final_attn[:, qkv_cols + o_cols :],
    )


def solution(mesh):
    in_specs = (
        P(None, "seq", None),
        P(),
        P(None, "tp"),
        P(),
        P(None, "tp"),
        P(None, "tp"),
        P("tp"),
        P("tp"),
        P("tp"),
        P("tp"),
        P("tp"),
        P(None, "tp"),
        P(),
        P(None, "tp"),
        P(None, "tp"),
        P(),
        P(None, "tp"),
        P(None, "tp"),
        P(None, "tp"),
        P(None, "tp"),
        P(None, "seq", "tp"),
    )
    out_specs = (
        P(None, "seq", "tp"),
        P(None, "seq", "tp"),
        P("seq", "tp"),
        P(),
        P("seq", "tp"),
        P(None, "tp"),
        P("tp"),
        P("tp"),
        P("tp"),
        P("tp"),
        P("tp"),
        P("seq", "tp"),
        P(),
        P("seq", "tp"),
        P("seq", "tp"),
        P(),
        P("seq", "tp"),
        P("seq", "tp"),
        P("seq", "tp"),
        P("seq", "tp"),
    )
    return jax.shard_map(body, mesh=mesh, in_specs=in_specs, out_specs=out_specs, check_vma=False)
```

```python
from functools import partial

import jax
import jax.numpy as jnp
from jax import lax
from jax.experimental import pallas as pl
from jax.experimental.pallas import tpu as pltpu
from jax.sharding import PartitionSpec as P

NS = 128
AD = 64
QUAD = 4


NO_COST = pl.CostEstimate(flops=1024, bytes_accessed=1024, transcendentals=0)
ROOMY = pltpu.CompilerParams(vmem_limit_bytes=56 * 1024 * 1024)

epsilon = 1e-05
highest = lax.Precision.HIGHEST
masked_score = -1e30


def dot_plain(left_side, right_side):
    return jnp.dot(left_side, right_side, preferred_element_type=jnp.float32)


def dot_trans(left_side, right_side):
    return lax.dot_general(
        left_side, right_side, (((1,), (1,)), ((), ())), preferred_element_type=jnp.float32
    )


def dot_left(left_side, right_side):
    return lax.dot_general(
        left_side, right_side, (((0,), (0,)), ((), ())), preferred_element_type=jnp.float32
    )


def rms_scale(values):
    return lax.rsqrt(jnp.mean(values * values, axis=-1, keepdims=True) + epsilon)


def hidden_parts(mlp_in, grad_hidden, w_gate, w_up):
    gate_proj = dot_plain(mlp_in, w_gate)
    up_proj = dot_plain(mlp_in, w_up)
    sigmoid_gate = jax.nn.sigmoid(gate_proj)
    hidden_low = (gate_proj * sigmoid_gate * up_proj).astype(jnp.bfloat16)
    grad_gate_low = (
        grad_hidden * up_proj * sigmoid_gate * (1.0 + gate_proj * (1.0 - sigmoid_gate))
    ).astype(jnp.bfloat16)
    grad_up_low = (grad_hidden * gate_proj * sigmoid_gate).astype(jnp.bfloat16)
    return (hidden_low, grad_gate_low, grad_up_low)


def rms_back(values, gain_values, grad_out):
    scale = rms_scale(values)
    scaled = gain_values * grad_out
    inner_mean = jnp.mean(values * scaled, axis=-1, keepdims=True)
    grad_values = scale * scaled - values * scale * scale * scale * inner_mean
    grad_gain = jnp.sum(values * scale * grad_out, axis=0)
    return (grad_values, grad_gain)


def swap(block, axis, mask):
    return lax.ppermute(block, axis, [(i, i ^ mask) for i in range(lax.axis_size(axis))])


def after(value, *earlier):
    return lax.optimization_barrier((value,) + earlier)[0]


def tp_sum(block):
    return block + swap(block, "tp", 1)


def to_partner(block, bit):
    return swap(block, "seq", 1 << bit)


def seq_bits():
    return lax.axis_size("seq").bit_length() - 1


def group_size():
    return lax.axis_size("seq") // QUAD


def group_trade(blocks):
    members = [[low + QUAD * high for high in range(group_size())] for low in range(QUAD)]
    return lax.all_to_all(blocks, "seq", 0, 0, axis_index_groups=members, tiled=True)


def add_kernel(index_ref, *refs):
    total = refs[0][...] + refs[1][...]
    refs[2][...] = total.reshape(refs[2].shape)


def add_side(near, got, side):
    unused, groups, rows, cols = near.shape
    index = jnp.zeros((1,), jnp.int32)
    block = pl.BlockSpec((1, 1, rows, cols), lambda i, ref: (side, i, 0, 0))
    return pl.pallas_call(
        add_kernel,
        grid_spec=pltpu.PrefetchScalarGridSpec(
            num_scalar_prefetch=1,
            grid=(groups,),
            in_specs=[block, block],
            out_specs=pl.BlockSpec((1, rows, cols), lambda i, ref: (i, 0, 0)),
        ),
        out_shape=jax.ShapeDtypeStruct((groups, rows, cols), jnp.float32),
        compiler_params=ROOMY,
        cost_estimate=NO_COST,
    )(index, near, got)


def near_kernel(index_ref, *refs):
    out_ref = refs[-1]
    at = 0
    for near_ref, got_ref, crossed_ref in zip(refs[0:-1:3], refs[1:-1:3], refs[2:-1:3]):
        cols = near_ref.shape[3]
        total = near_ref[0, 0] + got_ref[0, 0] + crossed_ref[0]
        out_ref[0, :, at : at + cols] = total
        at += cols


def near_sums(terms, high):
    unused, groups, rows, unused_cols = terms[0][0].shape
    cols = [term[0].shape[3] for term in terms]
    specs, operands = [], []
    for (near, got, crossed), count in zip(terms, cols):
        four = pl.BlockSpec((1, 1, rows, count), lambda i, ref: (0, ref[0] ^ i, 0, 0))
        three = pl.BlockSpec((1, rows, count), lambda i, ref: (ref[0] ^ i, 0, 0))
        specs += [four, four, three]
        operands += [near, got, crossed]
    return pl.pallas_call(
        near_kernel,
        grid_spec=pltpu.PrefetchScalarGridSpec(
            num_scalar_prefetch=1,
            grid=(groups,),
            in_specs=specs,
            out_specs=pl.BlockSpec((1, rows, sum(cols)), lambda i, ref: (i, 0, 0)),
        ),
        out_shape=jax.ShapeDtypeStruct((groups, rows, sum(cols)), jnp.float32),
        compiler_params=ROOMY,
        cost_estimate=NO_COST,
    )(high, *operands)


def grad_blocks_kernel(pairs, first, relative, rows, member_ref, *refs):
    lefts, rights = refs[: len(pairs)], refs[len(pairs) : 2 * len(pairs)]
    far_ref, near_ref = refs[2 * len(pairs) :]
    other = 1 - first
    at = 0
    for left_ref, right_ref, (low, high) in zip(lefts, rights, pairs):
        got = dot_left(left_ref[...], right_ref[:, low:high].astype(jnp.bfloat16))
        places = slice(at, at + high - low)
        for block in range(got.shape[0] // rows):
            place, member = block // QUAD, block % QUAD
            part = got[block * rows : (block + 1) * rows]
            apart = member_ref[0] ^ member
            is_far = apart >> first & 1
            if relative:
                side = apart >> other & 1
            else:
                side = member >> other & 1

            @pl.when(is_far == 1)
            def _():
                if relative:
                    far_ref[side, place, :, places] = part
                else:
                    far_ref[place, side, :, places] = part

            @pl.when(is_far == 0)
            def _():
                if relative:
                    near_ref[side, place, :, places] = part
                else:
                    near_ref[place, side, :, places] = part

        at += high - low


def grad_blocks(terms, first, relative):
    parts = lax.axis_size("seq")
    groups = parts // QUAD
    model_width = terms[0][0].shape[1]
    rows = model_width // parts
    cols = max(128, QUAD * rows)
    places = cols // (QUAD * rows)
    pairs = [(low, high) for unused, unused_right, low, high in terms]
    total = sum(high - low for low, high in pairs)
    member = (lax.axis_index("seq") % QUAD).astype(jnp.int32).reshape(1)
    if relative:
        shape, block = (2, groups, rows, total), (2, places, rows, total)
        out_spec = pl.BlockSpec(block, lambda i, ref: (0, i, 0, 0))
    else:
        shape, block = (groups, 2, rows, total), (places, 2, rows, total)
        out_spec = pl.BlockSpec(block, lambda i, ref: (i, 0, 0, 0))
    out = jax.ShapeDtypeStruct(shape, jnp.float32)
    return pl.pallas_call(
        partial(grad_blocks_kernel, pairs, first, relative, rows),
        grid_spec=pltpu.PrefetchScalarGridSpec(
            num_scalar_prefetch=1,
            grid=(model_width // cols,),
            in_specs=[
                pl.BlockSpec((term[0].shape[0], cols), lambda i, ref: (0, i)) for term in terms
            ]
            + [pl.BlockSpec(term[1].shape, lambda i, ref: (0, 0)) for term in terms],
            out_specs=[out_spec, out_spec],
        ),
        out_shape=[out, out],
        compiler_params=ROOMY,
        cost_estimate=NO_COST,
    )(member, *[term[0] for term in terms], *[term[1] for term in terms])


def segment_ids(lengths, place_count):
    ends = jnp.cumsum(lengths // 8, dtype=jnp.int32)
    places = jnp.arange(place_count, dtype=jnp.int32)
    short_ids = jnp.sum(
        (places[:, None] >= ends[None, :]).astype(jnp.int32), axis=1, dtype=jnp.int32
    )
    return jnp.stack([jnp.zeros_like(short_ids), short_ids])


def scan_heads(seg_now, head_size, xbc, dt_raw, conv_weight, conv_bias, dt_shift, a_logs, skips):
    place_count = xbc.shape[0]
    conv_sum = conv_bias + conv_weight[3] * xbc
    for offset in range(3):
        distance = 3 - offset
        earlier = jnp.pad(xbc, ((distance, 0), (0, 0)))[:place_count]
        seg_earlier = jnp.pad(seg_now, (distance, 0), constant_values=-1)[:place_count]
        same_doc = (seg_earlier == seg_now).astype(jnp.float32)
        conv_sum = conv_sum + conv_weight[offset] * earlier * same_doc[:, None]
    active = jax.nn.silu(conv_sum)
    head_count = dt_raw.shape[1]
    inner = head_count * head_size
    values = active[:, :inner].reshape(place_count, head_count, head_size)
    in_keys = active[:, inner : inner + NS]
    out_keys = active[:, inner + NS :]
    step_sizes = jax.nn.softplus(dt_raw + dt_shift)
    decay_rates = -step_sizes * jnp.exp(a_logs)
    chunk = min(place_count, 512)
    triangle = jnp.tril(jnp.ones((chunk, chunk), jnp.float32))
    state = jnp.zeros((head_count, head_size, NS), jnp.float32)
    seg_last = jnp.int32(-1)
    outputs = []
    for start in range(0, place_count, chunk):
        stop = start + chunk
        x, b, c = values[start:stop], in_keys[start:stop], out_keys[start:stop]
        dt, seg = step_sizes[start:stop], seg_now[start:stop]
        cumulative = jnp.dot(triangle, decay_rates[start:stop], precision=highest)
        allowed = (triangle > 0.0) & (seg[:, None] == seg[None, :])
        ordered = cumulative.T
        gaps = ordered[:, :, None] - ordered[:, None, :]
        decays = jnp.where(allowed, jnp.exp(jnp.where(allowed, gaps, 0.0)), 0.0)
        crossing = jnp.einsum("pn,jn->pj", c, b, precision=highest)
        mixing = crossing[None] * decays * dt.T[:, None, :]
        result = jnp.einsum("hpj,jhd->phd", mixing, x, precision=highest)
        if start > 0:
            entering = jnp.exp(cumulative) * (seg == seg_last).astype(jnp.float32)[:, None]
            result = result + entering[..., None] * jnp.einsum(
                "pn,hdn->phd", c, state, precision=highest
            )
        if stop < place_count:
            last_same = (seg == seg[-1]).astype(jnp.float32)[:, None]
            weight = jnp.exp(cumulative[-1:] - cumulative) * last_same * dt
            through = jnp.exp(cumulative[-1]) * (seg[-1] == seg_last).astype(jnp.float32)
            state = through[:, None, None] * state + jnp.einsum(
                "jh,jhd,jn->hdn", weight, x, b, precision=highest
            )
            seg_last = seg[-1]
        outputs.append(result + skips[:, None] * x)
    return jnp.concatenate(outputs, axis=0).reshape(place_count, inner)


def gated_unit(result, gate_in):
    gated = result * jax.nn.silu(gate_in)
    return gated * rms_scale(gated)


def patch_far_kernel(grad_ref, gain_ref, bytes_ref, out_ref):
    half = grad_ref.shape[1] // 2
    grad_low = grad_ref[:, half:].astype(jnp.bfloat16)
    out_ref[:half] = dot_left(grad_low, bytes_ref[...].astype(jnp.bfloat16))
    out_ref[half:] = jnp.zeros((out_ref.shape[0] - half, out_ref.shape[1]), jnp.float32)

    @pl.when(pl.program_id(0) == 0)
    def _():
        out_ref[half:, : 2 * half] = gain_ref[...]


def patch_far_grad(grad_rows, gain_part, bytes_all):
    places, cols = grad_rows.shape
    total = bytes_all.shape[1]
    rows = cols // 2 + gain_part.shape[0]
    block = 1024
    return pl.pallas_call(
        patch_far_kernel,
        grid=(total // block,),
        in_specs=[
            pl.BlockSpec((places, cols), lambda i: (0, 0)),
            pl.BlockSpec(gain_part.shape, lambda i: (0, 0)),
            pl.BlockSpec((places, block), lambda i: (0, i)),
        ],
        out_specs=pl.BlockSpec((rows, block), lambda i: (0, i)),
        out_shape=jax.ShapeDtypeStruct((rows, total), jnp.float32),
        compiler_params=ROOMY,
        cost_estimate=NO_COST,
    )(grad_rows, gain_part, bytes_all)


def patch_grad_kernel(grad_ref, *refs):
    byte_refs, got_refs, out_ref, order_ref = refs[:8], refs[8:16], refs[16], refs[17]
    width = byte_refs[0].shape[1]

    @pl.when(pl.program_id(0) == 0)
    def _():
        order_ref[...] = feature_order(width)

    grad_low = grad_ref[:, : grad_ref.shape[1] // 2].astype(jnp.bfloat16)
    wide = jnp.concatenate([ref[...].astype(jnp.bfloat16) for ref in byte_refs], axis=1)
    rows = grad_low.shape[1]
    grad = dot_left(grad_low, wide)
    grad = grad + jnp.concatenate([ref[:rows] for ref in got_refs], axis=1)
    high = grad.astype(jnp.bfloat16)
    rest = grad - high.astype(jnp.float32)
    mid = rest.astype(jnp.bfloat16)
    low = (rest - mid.astype(jnp.float32)).astype(jnp.bfloat16)
    order = order_ref[...]
    out_ref[...] = dot_plain(high, order) + (dot_plain(mid, order) + dot_plain(low, order))


def patch_grad(grad_rows, got, bytes_all):
    places, cols = grad_rows.shape
    feature = bytes_all.shape[1] // 8
    chunk = 128
    steps = feature // chunk

    def byte_specs(rows):
        return [
            pl.BlockSpec((rows, chunk), partial(lambda j, i: (0, j * steps + i), j))
            for j in range(8)
        ]

    return pl.pallas_call(
        patch_grad_kernel,
        grid=(steps,),
        in_specs=[pl.BlockSpec((places, cols), lambda i: (0, 0))]
        + byte_specs(places)
        + byte_specs(got.shape[0]),
        out_specs=pl.BlockSpec((cols // 2, 8 * chunk), lambda i: (0, i)),
        out_shape=jax.ShapeDtypeStruct((cols // 2, 8 * feature), jnp.float32),
        scratch_shapes=[pltpu.VMEM((8 * chunk, 8 * chunk), jnp.bfloat16)],
        compiler_params=ROOMY,
        cost_estimate=NO_COST,
    )(grad_rows, *([bytes_all] * 8), *([got] * 8))


def trade(blocks):
    return lax.all_to_all(blocks, "seq", 0, 0, tiled=True)


def grid_iota(shape, axis):
    return lax.broadcasted_iota(jnp.int32, shape, axis)


def dot_fine(left_side, right_side, left_axis, right_axis):
    return lax.dot_general(
        left_side,
        right_side,
        (((left_axis,), (right_axis,)), ((), ())),
        preferred_element_type=jnp.float32,
        precision=highest,
    )


def shifted_down(block, distance):
    rows = grid_iota(block.shape, 0)
    return jnp.where(rows >= distance, pltpu.roll(block, distance, 0), 0.0)


def shifted_up(block, distance):
    count = block.shape[0]
    rows = grid_iota(block.shape, 0)
    return jnp.where(rows < count - distance, pltpu.roll(block, count - distance, 0), 0.0)


def scan_terms(taken_ref, same_ref, conv_ref, head_ref):
    places = taken_ref.shape[0]
    channels = conv_ref.shape[1]
    xbc = taken_ref[:, :channels]
    conv_sum = conv_ref[4:5] + conv_ref[3:4] * xbc
    for k in range(3):
        earlier = shifted_down(xbc, 3 - k) * same_ref[:, k : k + 1]
        conv_sum = conv_sum + conv_ref[k : k + 1] * earlier
    gate = jax.nn.sigmoid(conv_sum)
    active = conv_sum * gate
    raw = taken_ref[:, channels:] + head_ref[0:1]
    steps = jnp.maximum(raw, 0.0) + jnp.log1p(jnp.exp(-jnp.abs(raw)))
    rates = -steps * jnp.exp(head_ref[1:2])
    square = (places, places)
    triangle = jnp.where(grid_iota(square, 0) >= grid_iota(square, 1), 1.0, 0.0)
    running = dot_fine(triangle, rates, 1, 0)
    return xbc, conv_sum, gate, active, raw, steps, rates, triangle, running


def scan_forward_kernel(taken_ref, same_ref, conv_ref, head_ref, seg_col, seg_row, out_ref):
    places, width = out_ref.shape
    terms = scan_terms(taken_ref, same_ref, conv_ref, head_ref)
    active, steps, running = terms[3], terms[5], terms[8]
    values = active[:, :width]
    keys, reads = active[:, width : width + NS], active[:, width + NS :]
    steps_row, running_row = steps.T, running.T
    heads = width // 64
    rows = 128
    for first in range(0, places, rows):
        last = first + rows
        shape = (rows, last)
        allowed = (seg_col[first:last] == seg_row[:, :last]) & (
            grid_iota(shape, 0) + first >= grid_iota(shape, 1)
        )
        crossing = dot_fine(reads[first:last], keys[:last], 1, 1)
        lane = grid_iota((rows, width), 1) // 64
        total = head_ref[2:3] * values[first:last]
        for h in range(heads):
            gaps = running[first:last, h : h + 1] - running_row[h : h + 1, :last]
            decays = jnp.exp(jnp.where(allowed, gaps, masked_score))
            mixing = crossing * decays * steps_row[h : h + 1, :last]
            part = dot_fine(mixing, values[:last], 1, 0)
            total = total + jnp.where(lane == h, part, 0.0)
        out_ref[first:last] = total


def scan_backward_kernel(
    taken_ref,
    same_ref,
    conv_ref,
    head_ref,
    seg_col,
    seg_row,
    grad_ref,
    out_ref,
    conv_grad_ref,
    head_grad_ref,
    values_grad,
    keys_grad,
    reads_grad,
    rows_grad,
    cols_grad,
):
    places, width = values_grad.shape
    terms = scan_terms(taken_ref, same_ref, conv_ref, head_ref)
    xbc, conv_sum, gate, active, raw, steps, rates, triangle, running = terms
    channels = xbc.shape[1]
    values = active[:, :width]
    keys, reads = active[:, width : width + NS], active[:, width + NS :]
    steps_row, running_row = steps.T, running.T
    heads = width // 64
    rows = 128
    grad = grad_ref[...]
    values_grad[...] = head_ref[2:3] * grad
    keys_grad[...] = jnp.zeros_like(keys_grad)
    rows_grad[...] = jnp.zeros_like(rows_grad)
    cols_grad[...] = jnp.zeros_like(cols_grad)
    for first in range(0, places, rows):
        last = first + rows
        shape = (rows, last)
        allowed = (seg_col[first:last] == seg_row[:, :last]) & (
            grid_iota(shape, 0) + first >= grid_iota(shape, 1)
        )
        crossing = dot_fine(reads[first:last], keys[:last], 1, 1)
        crossing_grad = jnp.zeros(shape, jnp.float32)
        grad_rows = grad[first:last]
        lane = grid_iota((rows, width), 1) // 64
        wide_lane = grid_iota((last, width), 1) // 64
        column = grid_iota((rows, 128), 1)
        down = jnp.zeros((rows, 128), jnp.float32)
        for h in range(heads):
            gaps = running[first:last, h : h + 1] - running_row[h : h + 1, :last]
            decays = jnp.exp(jnp.where(allowed, gaps, masked_score))
            step_row = steps_row[h : h + 1, :last]
            weighted = decays * step_row
            mixing = crossing * weighted
            own_grad = jnp.where(lane == h, grad_rows, 0.0)
            mixing_grad = dot_fine(own_grad, values[:last], 1, 1)
            back = dot_fine(mixing, own_grad, 0, 0)
            values_grad[:last] += jnp.where(wide_lane == h, back, 0.0)
            crossing_grad = crossing_grad + mixing_grad * weighted
            step_part = jnp.sum(mixing_grad * crossing * decays, axis=0, keepdims=True)
            gap_part = mixing_grad * mixing
            down = jnp.where(column == h, jnp.sum(gap_part, axis=1, keepdims=True), down)
            cols_grad[h : h + 1, :last] += step_part
            cols_grad[heads + h : heads + h + 1, :last] += step_part * step_row
        rows_grad[first:last] += down
        reads_grad[first:last] = dot_fine(crossing_grad, keys[:last], 1, 0)
        keys_grad[:last] += dot_fine(crossing_grad, reads[first:last], 0, 0)
    turned = cols_grad[...].T
    column = grid_iota(turned.shape, 1)
    step_grad = jnp.where(column < heads, turned, 0.0)
    ended = pltpu.roll(turned, turned.shape[1] - heads, 1)
    running_grad = jnp.where(column < heads, rows_grad[...] - ended, 0.0)
    rates_grad = dot_fine(triangle, running_grad, 0, 0)
    step_grad = step_grad - rates_grad * jnp.exp(head_ref[1:2])
    raw_grad = step_grad * jax.nn.sigmoid(raw)
    out_ref[:, channels:] = raw_grad
    lane = grid_iota((places, width), 1) // 64
    product = jnp.sum(grad * values, axis=0, keepdims=True)
    head_grad_ref[...] = jnp.zeros_like(head_grad_ref)
    head_grad_ref[0:1] = jnp.sum(raw_grad, axis=0, keepdims=True)
    head_grad_ref[1:2] = jnp.sum(rates_grad * rates, axis=0, keepdims=True)
    skip_lane = grid_iota((1, width), 1)
    skip_grad = jnp.zeros((1, width), jnp.float32)
    for h in range(heads):
        own = jnp.sum(jnp.where(skip_lane // 64 == h, product, 0.0), axis=1, keepdims=True)
        skip_grad = jnp.where(skip_lane == h, own, skip_grad)
    head_grad_ref[2:3] = skip_grad
    active_grad = jnp.concatenate([values_grad[...], keys_grad[...], reads_grad[...]], axis=1)
    conv_grad = active_grad * gate * (1.0 + conv_sum * (1.0 - gate))
    back = conv_ref[3:4] * conv_grad
    conv_grad_ref[...] = jnp.zeros_like(conv_grad_ref)
    conv_grad_ref[3:4] = jnp.sum(conv_grad * xbc, axis=0, keepdims=True)
    conv_grad_ref[4:5] = jnp.sum(conv_grad, axis=0, keepdims=True)
    for k in range(3):
        kept = conv_grad * same_ref[:, k : k + 1]
        back = back + conv_ref[k : k + 1] * shifted_up(kept, 3 - k)
        conv_grad_ref[k : k + 1] = jnp.sum(
            kept * shifted_down(xbc, 3 - k), axis=0, keepdims=True
        )
    out_ref[:, :channels] = back


def scan_forward(args, width):
    places = args[0].shape[0]
    return pl.pallas_call(
        scan_forward_kernel,
        out_shape=jax.ShapeDtypeStruct((places, width), jnp.float32),
        compiler_params=ROOMY,
        cost_estimate=NO_COST,
    )(*args)


def scan_backward(args, grad):
    places, width = grad.shape
    channels = args[2].shape[1]
    f32 = jnp.float32
    return pl.pallas_call(
        scan_backward_kernel,
        out_shape=[
            jax.ShapeDtypeStruct((places, channels + 128), f32),
            jax.ShapeDtypeStruct((8, channels), f32),
            jax.ShapeDtypeStruct((8, 128), f32),
        ],
        scratch_shapes=[
            pltpu.VMEM((places, width), f32),
            pltpu.VMEM((places, NS), f32),
            pltpu.VMEM((places, NS), f32),
            pltpu.VMEM((places, 128), f32),
            pltpu.VMEM((128, places), f32),
        ],
        compiler_params=ROOMY,
        cost_estimate=NO_COST,
    )(*args, grad)


def patch_lanes(block):
    shape = (block // 8, 8, block)
    return grid_iota(shape, 0) == grid_iota(shape, 2) // 8


def folded(scores, same_patch):
    split = scores.reshape(same_patch.shape)
    return jnp.sum(jnp.where(same_patch, split, 0.0), axis=0)


def unfolded(rows, same_patch):
    spread = jnp.where(same_patch, rows[None], 0.0)
    return spread.reshape(-1, rows.shape[1]).astype(jnp.bfloat16)


def softmax_rows(scores, causal):
    scores = jnp.where(causal, scores, masked_score)
    top = jnp.max(scores, axis=1, keepdims=True)
    powers = jnp.exp(scores - top)
    return powers / jnp.sum(powers, axis=1, keepdims=True)


def head_places(rows, head_cols, block):
    return [
        (slice(first, first + block), [j * head_cols + pair * 128 for j in range(3)])
        for first in range(0, rows, block)
        for pair in range(head_cols // 128)
    ]


def all_scores(qkv_ref, places, lane, same_patch):
    scores = []
    for rows, (query, key, unused) in places:
        queries = qkv_ref[rows, query : query + 128] * 0.125
        keys = qkv_ref[rows, key : key + 128]
        for h in range(2):
            own = jnp.where(lane == h, queries, 0)
            scores.append(folded(dot_trans(keys, own), same_patch))
    return jnp.stack(scores)


def attn_forward_kernel(
    bytes_ref, patch_ref, gain_ref, qkv_w_ref, o_w_ref, x_ref, a_ref, qkv_ref, o_ref, out_ref
):
    rows = bytes_ref.shape[0]
    spread = jnp.broadcast_to(patch_ref[...][:, None], (rows // 8, 8, patch_ref.shape[1]))
    x = bytes_ref[...].astype(jnp.float32) + spread.reshape(bytes_ref.shape)
    x_ref[...] = x
    attn_in = (x * rms_scale(x) * gain_ref[...]).astype(jnp.bfloat16)
    a_ref[...] = attn_in
    qkv_ref[...] = dot_plain(attn_in, qkv_w_ref[...]).astype(jnp.bfloat16)
    head_cols = o_ref.shape[1]
    block = 128
    same_patch = patch_lanes(block)
    causal = grid_iota((8, block), 0) <= grid_iota((8, block), 1) % 8
    lane = grid_iota((block, 128), 1) // AD
    places = head_places(rows, head_cols, block)
    probs = softmax_rows(all_scores(qkv_ref, places, lane, same_patch), causal)
    for at, (row_place, (query, unused, value)) in enumerate(places):
        values = qkv_ref[row_place, value : value + 128]
        parts = [dot_left(unfolded(probs[2 * at + h], same_patch), values) for h in range(2)]
        total = jnp.where(lane == 0, parts[0], parts[1])
        o_ref[row_place, query : query + 128] = total.astype(jnp.bfloat16)
    out_ref[...] = dot_trans(o_ref[...], o_w_ref[...])


def attn_forward(bytes_rows, patch_rows, gain, w_qkv, w_o):
    rows, width = bytes_rows.shape
    block = 256
    cols, head_cols = w_qkv.shape[1], w_o.shape[1]
    f32, bf16 = jnp.float32, jnp.bfloat16

    def by_rows(cols):
        return pl.BlockSpec((block, cols), lambda i: (i, 0))

    def whole(shape):
        return pl.BlockSpec(shape, lambda i: (0, 0))

    return pl.pallas_call(
        attn_forward_kernel,
        grid=(rows // block,),
        in_specs=[
            by_rows(width),
            pl.BlockSpec((block // 8, width), lambda i: (i, 0)),
            whole((1, width)),
            whole(w_qkv.shape),
            whole(w_o.shape),
        ],
        out_specs=[by_rows(width), by_rows(width), by_rows(cols), by_rows(head_cols), by_rows(width)],
        out_shape=[
            jax.ShapeDtypeStruct((rows, width), f32),
            jax.ShapeDtypeStruct((rows, width), bf16),
            jax.ShapeDtypeStruct((rows, cols), bf16),
            jax.ShapeDtypeStruct((rows, head_cols), bf16),
            jax.ShapeDtypeStruct((rows, width), f32),
        ],
        compiler_params=ROOMY,
        cost_estimate=NO_COST,
    )(bytes_rows, patch_rows, gain.reshape(1, width), w_qkv, w_o)


def attn_backward_kernel(
    x_ref,
    final_ref,
    own_ref,
    other_ref,
    gain_ref,
    qkv_ref,
    qkv_w_ref,
    o_w_ref,
    mid_ref,
    low_ref,
    qkv_grad_ref,
    out_ref,
    gain_grad_ref,
):
    rows = x_ref.shape[0]
    back, gain_grad = rms_back(x_ref[...], gain_ref[...], own_ref[...] + other_ref[...])
    mid = final_ref[...] + back
    mid_ref[...] = mid
    low_ref[...] = mid.astype(jnp.bfloat16)
    gain_grad = gain_grad.reshape(1, -1)

    @pl.when(pl.program_id(0) == 0)
    def _():
        gain_grad_ref[...] = gain_grad

    @pl.when(pl.program_id(0) > 0)
    def _():
        gain_grad_ref[...] += gain_grad

    mixed_grad = dot_plain(low_ref[...], o_w_ref[...]).astype(jnp.bfloat16)
    head_cols = mixed_grad.shape[1]
    block = 128
    same_patch = patch_lanes(block)
    causal = grid_iota((8, block), 0) <= grid_iota((8, block), 1) % 8
    lane = grid_iota((block, 128), 1) // AD
    places = head_places(rows, head_cols, block)
    probs = softmax_rows(all_scores(qkv_ref, places, lane, same_patch), causal)
    probs_grads = []
    for row_place, (query, unused, value) in places:
        values = qkv_ref[row_place, value : value + 128]
        out_grad = mixed_grad[row_place, query : query + 128]
        for h in range(2):
            own_grad = jnp.where(lane == h, out_grad, 0)
            probs_grads.append(folded(dot_trans(values, own_grad), same_patch))
    probs_grad = jnp.stack(probs_grads)
    inner = jnp.sum(probs * probs_grad, axis=1, keepdims=True)
    scores_grad = probs * (probs_grad - inner)
    for at, (row_place, cols) in enumerate(places):
        query, key, unused = cols
        queries = qkv_ref[row_place, query : query + 128]
        keys = qkv_ref[row_place, key : key + 128]
        out_grad = mixed_grad[row_place, query : query + 128]
        parts = []
        for h in range(2):
            own_scores = unfolded(scores_grad[2 * at + h], same_patch)
            parts.append(
                (
                    dot_left(own_scores, keys) * 0.125,
                    dot_plain(own_scores, queries) * 0.125,
                    dot_plain(unfolded(probs[2 * at + h], same_patch), out_grad),
                )
            )
        for j in range(3):
            grad = jnp.where(lane == 0, parts[0][j], parts[1][j])
            qkv_grad_ref[row_place, cols[j] : cols[j] + 128] = grad.astype(jnp.bfloat16)
    out_ref[...] = dot_trans(qkv_grad_ref[...], qkv_w_ref[...])


def attn_backward(x_rows, final_grad, own_part, other_part, gain, qkv, w_qkv, w_o):
    rows, width = x_rows.shape
    block = 256
    cols = w_qkv.shape[1]
    f32, bf16 = jnp.float32, jnp.bfloat16

    def by_rows(cols):
        return pl.BlockSpec((block, cols), lambda i: (i, 0))

    def whole(shape):
        return pl.BlockSpec(shape, lambda i: (0, 0))

    return pl.pallas_call(
        attn_backward_kernel,
        grid=(rows // block,),
        in_specs=[by_rows(width)] * 4
        + [whole((1, width)), by_rows(cols), whole(w_qkv.shape), whole(w_o.shape)],
        out_specs=[
            by_rows(width),
            by_rows(width),
            by_rows(cols),
            by_rows(width),
            whole((1, width)),
        ],
        out_shape=[
            jax.ShapeDtypeStruct((rows, width), f32),
            jax.ShapeDtypeStruct((rows, width), bf16),
            jax.ShapeDtypeStruct((rows, cols), bf16),
            jax.ShapeDtypeStruct((rows, width), f32),
            jax.ShapeDtypeStruct((1, width), f32),
        ],
        compiler_params=ROOMY,
        cost_estimate=NO_COST,
    )(x_rows, final_grad, own_part, other_part, gain.reshape(1, width), qkv, w_qkv, w_o)


def mlp_in_kernel(core_ref, x_ref, own_ref, other_ref, gain_ref, out_ref, low_ref, half_ref):
    x = x_ref[...] + (own_ref[...] + other_ref[...])
    out_ref[...] = x
    unit = x * rms_scale(x)
    low_ref[...] = (unit * gain_ref[...]).astype(jnp.bfloat16)
    width = half_ref.shape[1]
    half_ref[...] = jnp.where(core_ref[0] == 0, unit[:, :width], unit[:, width:])


def mlp_in(x_rows, own_part, other_part, gain):
    rows, width = x_rows.shape
    block = 128
    core = lax.axis_index("tp").astype(jnp.int32).reshape(1)

    def by_rows(cols):
        return pl.BlockSpec((block, cols), lambda i, ref: (i, 0))

    return pl.pallas_call(
        mlp_in_kernel,
        grid_spec=pltpu.PrefetchScalarGridSpec(
            num_scalar_prefetch=1,
            grid=(rows // block,),
            in_specs=[by_rows(width)] * 3 + [pl.BlockSpec((1, width), lambda i, ref: (0, 0))],
            out_specs=[by_rows(width), by_rows(width), by_rows(width // 2)],
        ),
        out_shape=[
            jax.ShapeDtypeStruct((rows, width), jnp.float32),
            jax.ShapeDtypeStruct((rows, width), jnp.bfloat16),
            jax.ShapeDtypeStruct((rows, width // 2), jnp.float32),
        ],
        compiler_params=ROOMY,
        cost_estimate=NO_COST,
    )(core, x_rows, own_part, other_part, gain.reshape(1, width))


def units_in_halves(
    mlp_low, grad_ref, gate_w_ref, up_w_ref, hidden_ref, gate_ref, up_ref
):
    half = grad_ref.shape[1] // 2
    for at in range(2):
        cols = slice(at * half, (at + 1) * half)
        hidden, gate, up = hidden_parts(
            mlp_low, grad_ref[:, cols], gate_w_ref[:, cols], up_w_ref[:, cols]
        )
        hidden_ref[:, cols] = hidden
        gate_ref[:, cols] = gate
        up_ref[:, cols] = up


def mlp_kernel(
    in_ref, grad_ref, gate_w_ref, up_w_ref, hidden_ref, gate_ref, up_ref, out_ref, total_ref
):
    mlp_low = in_ref[...]
    units_in_halves(
        mlp_low, grad_ref, gate_w_ref, up_w_ref, hidden_ref, gate_ref, up_ref
    )
    part = dot_trans(gate_ref[...], gate_w_ref[...]) + dot_trans(up_ref[...], up_w_ref[...])
    step = pl.program_id(0)

    @pl.when(step == 0)
    def _():
        total_ref[...] = part

    @pl.when(step > 0)
    def _():
        total_ref[...] += part

    @pl.when(step == pl.num_programs(0) - 1)
    def _():
        out_ref[...] = total_ref[...]


def mlp_rows(mlp_low, grad_hidden, w_gate, w_up):
    rows, width = mlp_low.shape
    units = w_gate.shape[1]
    block = 512
    by_units = pl.BlockSpec((rows, block), lambda i: (0, i))
    by_weights = pl.BlockSpec((width, block), lambda i: (0, i))
    whole = pl.BlockSpec((rows, width), lambda i: (0, 0))
    low = jax.ShapeDtypeStruct((rows, units), jnp.bfloat16)
    return pl.pallas_call(
        mlp_kernel,
        grid=(units // block,),
        in_specs=[whole, by_units, by_weights, by_weights],
        out_specs=[by_units, by_units, by_units, whole],
        out_shape=[low, low, low, jax.ShapeDtypeStruct((rows, width), jnp.float32)],
        scratch_shapes=[pltpu.VMEM((rows, width), jnp.float32)],
        compiler_params=ROOMY,
        cost_estimate=NO_COST,
    )(mlp_low, grad_hidden, w_gate, w_up)


def feature_order(width):
    shape = (8 * width, 8 * width)
    row, col = grid_iota(shape, 0), grid_iota(shape, 1)
    return jnp.where(row == (col % 8) * width + col // 8, 1.0, 0.0).astype(jnp.bfloat16)


def patch_in_kernel(core_ref, bytes_ref, weight_ref, wide_ref, out_ref, rows_ref, order_ref):
    places, feature = wide_ref.shape[0], wide_ref.shape[1] // 8
    chunk = weight_ref.shape[1] // 8
    step = pl.program_id(0)

    @pl.when(step == 0)
    def _():
        order_ref[...] = feature_order(chunk)
        for at in range(feature // 128):
            low = at * 128
            rows_ref[at] = bytes_ref[:, low : low + 128].astype(jnp.float32)
            for j in range(8):
                wide_ref[:, j * feature + low : j * feature + low + 128] = rows_ref[
                    at, pl.ds(j, places, stride=8), :
                ]

    parts = [
        wide_ref[:, pl.ds(pl.multiple_of(j * feature + step * chunk, 128), chunk)]
        for j in range(8)
    ]
    by_byte = jnp.concatenate(parts, axis=1).astype(jnp.bfloat16)
    by_feature = dot_plain(by_byte, order_ref[...]).astype(jnp.bfloat16)
    part = dot_trans(by_feature, weight_ref[...])

    @pl.when(step == 0)
    def _():
        out_ref[...] = part

    @pl.when(step > 0)
    def _():
        out_ref[...] += part


def patch_in(byte_rows, w_patch):
    rows, model_width = byte_rows.shape
    out_width, cols = w_patch.shape
    feature, chunk = cols // 8, 128
    core = lax.axis_index("tp").astype(jnp.int32).reshape(1)
    f32 = jnp.float32
    return pl.pallas_call(
        patch_in_kernel,
        grid_spec=pltpu.PrefetchScalarGridSpec(
            num_scalar_prefetch=1,
            grid=(feature // chunk,),
            in_specs=[
                pl.BlockSpec((rows, feature), lambda i, ref: (0, ref[0])),
                pl.BlockSpec((out_width, 8 * chunk), lambda i, ref: (0, i)),
            ],
            out_specs=[
                pl.BlockSpec((rows // 8, cols), lambda i, ref: (0, 0)),
                pl.BlockSpec((rows // 8, out_width), lambda i, ref: (0, 0)),
            ],
            scratch_shapes=[
                pltpu.VMEM((feature // 128, rows, 128), f32),
                pltpu.VMEM((8 * chunk, 8 * chunk), jnp.bfloat16),
            ],
        ),
        out_shape=[
            jax.ShapeDtypeStruct((rows // 8, cols), f32),
            jax.ShapeDtypeStruct((rows // 8, out_width), f32),
        ],
        compiler_params=ROOMY,
        cost_estimate=NO_COST,
    )(core, byte_rows, w_patch)


def final_kernel(
    member_ref,
    own_ref,
    other_ref,
    mask_ref,
    own_head_ref,
    other_head_ref,
    weight_ref,
    low_ref,
    hidden_ref,
    mine_ref,
    mine_low_ref,
):
    own = (own_ref[...] * mask_ref[...]).astype(jnp.bfloat16)
    other = (other_ref[...] * mask_ref[...]).astype(jnp.bfloat16)
    other_head = other_head_ref[...].astype(jnp.bfloat16)
    total = dot_trans(own, own_head_ref[...]) + dot_trans(other, other_head)
    low = total.astype(jnp.bfloat16)
    low_ref[...] = low
    hidden_ref[...] = dot_plain(low, weight_ref[...])

    @pl.when(pl.program_id(0) == member_ref[0])
    def _():
        mine_ref[...] = total
        mine_low_ref[...] = low


def final_grads(own, other, mask, own_head, other_head, w_down, member):
    rows, cols = own.shape
    width = own_head.shape[0]
    block = rows // group_size()
    units = w_down.shape[1] // group_size()
    f32, bf16 = jnp.float32, jnp.bfloat16

    def by_rows(cols):
        return pl.BlockSpec((block, cols), lambda i, ref: (i, 0))

    head = pl.BlockSpec((width, cols), lambda i, ref: (0, 0))
    mine = pl.BlockSpec((block, width), lambda i, ref: (0, 0))
    return pl.pallas_call(
        final_kernel,
        grid_spec=pltpu.PrefetchScalarGridSpec(
            num_scalar_prefetch=1,
            grid=(group_size(),),
            in_specs=[by_rows(cols), by_rows(cols), by_rows(1), head, head]
            + [pl.BlockSpec((width, units), lambda i, ref: (0, ref[0]))],
            out_specs=[by_rows(width), by_rows(units), mine, mine],
        ),
        out_shape=[
            jax.ShapeDtypeStruct((rows, width), bf16),
            jax.ShapeDtypeStruct((rows, units), f32),
            jax.ShapeDtypeStruct((block, width), f32),
            jax.ShapeDtypeStruct((block, width), bf16),
        ],
        compiler_params=ROOMY,
        cost_estimate=NO_COST,
    )(member, own, other, mask, own_head, other_head, w_down)


def group_mlp_kernel(
    place_ref,
    own_ref,
    other_ref,
    gain_ref,
    grad_ref,
    gate_w_ref,
    up_w_ref,
    in_ref,
    hidden_ref,
    gate_ref,
    up_ref,
):
    own, other = own_ref[0], other_ref[0]
    first = place_ref[1] == 0
    halves = [jnp.where(first, own, other), jnp.where(first, other, own)]
    low = (jnp.concatenate(halves, axis=1) * gain_ref[...]).astype(jnp.bfloat16)
    in_ref[...] = low
    units_in_halves(low, grad_ref, gate_w_ref, up_w_ref, hidden_ref, gate_ref, up_ref)


def group_mlp(own_half, other_half, gain, grad_hidden, w_gate, w_up, member):
    rows, half = grad_hidden.shape[0] // group_size(), own_half.shape[2]
    width, units = 2 * half, w_gate.shape[1] // group_size()
    bf16 = jnp.bfloat16
    place = jnp.concatenate([member, lax.axis_index("tp").astype(jnp.int32).reshape(1)])

    def by_rows(cols):
        return pl.BlockSpec((rows, cols), lambda i, ref: (i, 0))

    halves = pl.BlockSpec((1, rows, half), lambda i, ref: (i ^ ref[0], 0, 0))
    weights = pl.BlockSpec((width, units), lambda i, ref: (0, ref[0]))
    low = jax.ShapeDtypeStruct((group_size() * rows, units), bf16)
    return pl.pallas_call(
        group_mlp_kernel,
        grid_spec=pltpu.PrefetchScalarGridSpec(
            num_scalar_prefetch=1,
            grid=(group_size(),),
            in_specs=[
                halves,
                halves,
                pl.BlockSpec((1, width), lambda i, ref: (0, 0)),
                by_rows(units),
                weights,
                weights,
            ],
            out_specs=[by_rows(width), by_rows(units), by_rows(units), by_rows(units)],
        ),
        out_shape=[jax.ShapeDtypeStruct((group_size() * rows, width), bf16), low, low, low],
        compiler_params=ROOMY,
        cost_estimate=NO_COST,
    )(place, own_half, other_half, gain.reshape(1, width), grad_hidden, w_gate, w_up)


def bytes_grad_kernel(core_ref, grad_ref, weight_ref, stream_ref, out_ref, order_ref):
    places = grad_ref.shape[0]
    chunk = weight_ref.shape[1] // 8

    @pl.when(pl.program_id(0) == 0)
    def _():
        order_ref[...] = feature_order(chunk)

    by_feature = dot_plain(grad_ref[...].astype(jnp.bfloat16), weight_ref[...])
    high = by_feature.astype(jnp.bfloat16)
    rest = by_feature - high.astype(jnp.float32)
    mid = rest.astype(jnp.bfloat16)
    low = (rest - mid.astype(jnp.float32)).astype(jnp.bfloat16)
    order = order_ref[...]
    by_byte = dot_trans(high, order) + (dot_trans(mid, order) + dot_trans(low, order))
    for j in range(8):
        rows = pl.ds(j, places, stride=8)
        out_ref[rows, :] = stream_ref[rows, :] + by_byte[:, j * chunk : (j + 1) * chunk]


def bytes_grad(grad_patch, w_patch, grad_stream):
    places, width = grad_patch.shape
    rows = grad_stream.shape[0]
    cols = w_patch.shape[1]
    feature, chunk = cols // 8, 128
    core = lax.axis_index("tp").astype(jnp.int32).reshape(1)
    return pl.pallas_call(
        bytes_grad_kernel,
        grid_spec=pltpu.PrefetchScalarGridSpec(
            num_scalar_prefetch=1,
            grid=(feature // chunk,),
            in_specs=[
                pl.BlockSpec((places, width), lambda i, ref: (0, 0)),
                pl.BlockSpec((width, 8 * chunk), lambda i, ref: (0, i)),
                pl.BlockSpec((rows, chunk), lambda i, ref: (0, ref[0] * (feature // chunk) + i)),
            ],
            out_specs=pl.BlockSpec((rows, chunk), lambda i, ref: (0, i)),
            scratch_shapes=[pltpu.VMEM((8 * chunk, 8 * chunk), jnp.bfloat16)],
        ),
        out_shape=jax.ShapeDtypeStruct((rows, feature), jnp.float32),
        compiler_params=ROOMY,
        cost_estimate=NO_COST,
    )(core, grad_patch, w_patch, grad_stream)


def body(
    byte_states,
    lengths,
    w_patch,
    norm_global,
    w_in,
    conv_w,
    conv_b,
    dt_bias,
    a_log,
    d_skip,
    mix_gain,
    w_out,
    norm_attn,
    w_qkv,
    w_o,
    norm_mlp,
    w_gate,
    w_up,
    w_down,
    w_head,
    d_logits,
):
    streams, local_rows, model_width = byte_states.shape
    patch_count = local_rows // 8
    patch_total = streams * patch_count
    row_total = streams * local_rows
    feature = w_patch.shape[1] // 8
    inner_width = w_out.shape[1]
    channels = conv_w.shape[1]
    head_total = dt_bias.shape[0]
    head_cols = w_head.shape[1]
    parts = lax.axis_size("seq")
    tp_index = lax.axis_index("tp")
    seq_index = lax.axis_index("seq")
    places = parts * patch_count
    f32 = jnp.float32

    lanes = parts // streams
    width = inner_width // lanes
    full_head = inner_width // head_total
    own_heads = max(1, width // full_head)
    shared = max(1, full_head // width)
    head_size = width // own_heads
    own_stream = seq_index // lanes
    first_col = (seq_index % lanes) * width
    first_head = first_col // full_head

    seg_full = segment_ids(lengths, places)
    seg_own = lax.dynamic_slice_in_dim(seg_full, seq_index * patch_count, patch_count, 1)
    seg_stream = lax.dynamic_index_in_dim(seg_full, own_stream, 0, keepdims=False)
    valid = (seg_own < lengths.shape[0]).astype(f32).reshape(patch_total, 1)
    byte_valid = jnp.repeat(valid, 8, axis=0)

    member, members = seq_index // QUAD, group_size()
    raw_logits = d_logits.reshape(row_total, head_cols)
    raw_wide = raw_logits.astype(f32)
    group_valid = []
    for high in range(members):
        device = seq_index % QUAD + QUAD * high
        group_seg = lax.dynamic_slice_in_dim(seg_full, device * patch_count, patch_count, 1)
        group_valid.append((group_seg < lengths.shape[0]).astype(f32))
    group_valid = jnp.stack(group_valid).reshape(members, patch_total, 1)
    group_bytes_valid = jnp.repeat(group_valid.reshape(-1, 1), 8, axis=0)
    group_raw = group_trade(jnp.broadcast_to(raw_wide[None], (members,) + raw_wide.shape))
    group_raw = group_raw.reshape(-1, head_cols)
    other_raw = swap(group_raw, "tp", 1)
    other_head = swap(w_head.astype(f32), "tp", 1)
    place_index = member.astype(jnp.int32).reshape(1)
    bytes_wide, patch_part = patch_in(byte_states.reshape(row_total, model_width), w_patch)
    patch_out = tp_sum(patch_part)
    gain_global = norm_global.astype(f32)
    unit_patch = patch_out * rms_scale(patch_out)
    u_low = (unit_patch * gain_global).astype(jnp.bfloat16)
    half_width = model_width // 2
    proj = dot_plain(u_low, w_in).reshape(streams, patch_count, -1)
    gate_in = proj[..., :inner_width]
    xbc = proj[..., inner_width : inner_width + channels]
    dt_raw = proj[..., inner_width + channels :]

    def by_lane(columns):
        split = columns.reshape(streams, patch_count, lanes, -1)
        return jnp.moveaxis(split, 2, 1).reshape(parts, patch_count, -1)

    def from_lanes(blocks):
        split = blocks.reshape(streams, lanes, patch_count, -1)
        return jnp.moveaxis(split, 1, 2).reshape(streams, patch_count, -1)

    def to_all_lanes(columns):
        wide = jnp.broadcast_to(
            columns[:, None], (streams, lanes, patch_count, columns.shape[-1])
        )
        return wide.reshape(parts, patch_count, -1)

    pad_width = 128 - own_heads
    dt_lanes = by_lane(jnp.repeat(dt_raw, shared, axis=2))
    sent = jnp.concatenate(
        [
            by_lane(xbc[..., :inner_width]),
            to_all_lanes(xbc[..., inner_width:]),
            jnp.pad(dt_lanes, ((0, 0), (0, 0), (0, pad_width))),
        ],
        axis=-1,
    )
    taken = trade(sent)
    grad_logits = after(raw_logits, sent) * byte_valid.astype(jnp.bfloat16)
    group_final, group_grad_hidden, grad_final, grad_mlp_low = final_grads(
        after(group_raw, sent),
        other_raw,
        group_bytes_valid,
        w_head,
        other_head,
        w_down,
        place_index,
    )
    grad_hidden = dot_plain(grad_mlp_low, w_down)
    hidden_part = w_gate.shape[1] // members

    row_side = [
        [device for device in range(parts) if (device & 1) == side] for side in range(2)
    ]
    bytes_all = lax.all_gather(
        bytes_wide, "seq", axis=0, axis_index_groups=row_side, tiled=True
    )
    taken = after(taken, grad_hidden, group_grad_hidden).reshape(places, -1)
    scan_width = width + channels - inner_width

    def own_cols(param):
        mine = lax.dynamic_slice_in_dim(param, first_col, width, param.ndim - 1)
        return jnp.concatenate([mine, param[..., inner_width:]], axis=-1).astype(f32)

    def own_head(param):
        return lax.dynamic_slice_in_dim(param, first_head, own_heads, 0).astype(f32)

    use_kernel = places == 512 and width == 128
    if use_kernel:
        padded_seg = jnp.pad(seg_stream, (3, 0), constant_values=-1)
        same = jnp.stack(
            [(padded_seg[k : k + places] == seg_stream).astype(f32) for k in range(3)]
            + [jnp.zeros((places,), f32)] * 5,
            axis=1,
        )
        conv_pack = jnp.concatenate(
            [own_cols(conv_w), own_cols(conv_b)[None], jnp.zeros((3, scan_width), f32)]
        )
        head_pack = jnp.stack(
            [jnp.pad(own_head(dt_bias), (0, 128 - own_heads))]
            + [jnp.pad(own_head(a_log), (0, 128 - own_heads))]
            + [jnp.repeat(own_head(d_skip), head_size)]
            + [jnp.zeros((128,), f32)] * 5
        )
        scan_args = (taken, same, conv_pack, head_pack, seg_stream[:, None], seg_stream[None])
        scanned = scan_forward(scan_args, width)
    else:
        scan_args = (
            taken[:, :scan_width],
            taken[:, scan_width : scan_width + own_heads],
            own_cols(conv_w),
            own_cols(conv_b),
            own_head(dt_bias),
            own_head(a_log),
            own_head(d_skip),
        )
        scanned, scan_back = jax.vjp(partial(scan_heads, seg_stream, head_size), *scan_args)
    result = from_lanes(trade(scanned.reshape(parts, patch_count, width)))
    unit_normed, norm_back = jax.vjp(gated_unit, result, gate_in)
    mix_scale = mix_gain.astype(f32)
    normed_low = (unit_normed * mix_scale).reshape(patch_total, -1).astype(jnp.bfloat16)


    def quarters(columns):
        split = columns.reshape(patch_total, members, -1)
        return jnp.moveaxis(split, 1, 0)

    def by_apart(blocks):
        return [
            lax.dynamic_index_in_dim(blocks, member ^ apart, 0, keepdims=False)
            for apart in range(members)
        ]

    def group_swap(blocks):
        return [blocks[0]] + [swap(blocks[k], "seq", QUAD * k) for k in range(1, members)]

    def joined(blocks, turn):
        return jnp.concatenate([after(block, turn) for block in blocks], axis=0)

    early_got = group_swap(
        [
            jnp.concatenate([unit_patch, part], axis=-1)
            for part in by_apart(quarters(unit_normed))
        ]
    )
    global_out = patch_out + valid * tp_sum(dot_trans(normed_low, w_out))
    gain_attn = norm_attn.astype(f32)
    gain_mlp = norm_mlp.astype(f32)
    stream_in, attn_in, qkv, mixed_low, attn_part = attn_forward(
        byte_states.reshape(row_total, model_width), global_out, gain_attn, w_qkv, w_o
    )
    after_attn, mlp_low, unit_half = mlp_in(
        stream_in, attn_part, swap(attn_part, "tp", 1), gain_mlp
    )
    hidden_low, grad_gate_low, grad_up_low, grad_mlp_part = mlp_rows(
        after(mlp_low, unit_half), grad_hidden, w_gate, w_up
    )
    near_halves = [swap(unit_half, "seq", QUAD * apart) for apart in range(1, members)]
    grad_mlp_other = swap(grad_mlp_part, "tp", 1)
    after_mlp = after_attn + tp_sum(dot_trans(after(hidden_low, grad_mlp_part), w_down))
    final_low = after_mlp.astype(jnp.bfloat16)
    logits = dot_plain(final_low, w_head) * byte_valid
    grad_mid, grad_attn_low, grad_qkv_low, grad_attn_part, grad_norm_mlp = attn_backward(
        after_attn, grad_final, grad_mlp_part, grad_mlp_other, gain_mlp, qkv, w_qkv, w_o
    )
    grad_norm_mlp = grad_norm_mlp.reshape(-1)
    grad_attn_in = tp_sum(grad_attn_part)

    back_attn, grad_norm_attn = rms_back(stream_in, gain_attn, grad_attn_in)
    grad_stream = grad_mid + back_attn
    grad_global = jnp.sum(grad_stream.reshape(patch_total, 8, model_width), axis=1)
    grad_mix_low = (grad_global * valid).astype(jnp.bfloat16)
    grad_normed = dot_plain(grad_mix_low, w_out).reshape(streams, patch_count, inner_width)
    grad_mix_gain = jnp.sum(grad_normed * unit_normed, axis=(0, 1))
    grad_result, grad_gate_in = norm_back(grad_normed * mix_scale)
    grad_z_low = grad_gate_in.reshape(patch_total, inner_width).astype(jnp.bfloat16)
    row_block = model_width // parts
    dealing = after(by_lane(grad_result), bytes_all)
    dealt = trade(dealing)
    late_sent = [
        jnp.concatenate([grad_global, part], axis=-1) for part in by_apart(quarters(grad_gate_in))
    ]
    late_got = group_swap(late_sent)
    attn_cut = 1024 if grad_qkv_low.shape[1] > 1024 else 128
    attn_in_late = after(attn_in, dealing)
    attn_cols = grad_qkv_low.shape[1]
    attn_blocks = (
        grad_blocks([(attn_in_late, grad_qkv_low, 0, attn_cut)], 0, True),
        grad_blocks(
            [
                (attn_in_late, grad_qkv_low, attn_cut, attn_cols),
                (grad_attn_low, mixed_low, 0, mixed_low.shape[1]),
                (final_low, grad_logits, 0, head_cols),
            ],
            1,
            True,
        ),
    )
    attn_got = [to_partner(attn_blocks[first][0], first) for first in range(2)]
    dealt = after(dealt, attn_blocks[0][0], attn_blocks[1][0], near_halves[0])
    grad_scanned = dealt.reshape(places, width)
    if use_kernel:
        back_sent, conv_grads, head_grads = scan_backward(scan_args, grad_scanned)
        lane_grad = back_sent[:, : scan_width + own_heads]
        scan_params = (
            conv_grads[:4],
            conv_grads[4],
            head_grads[0, :own_heads],
            head_grads[1, :own_heads],
            head_grads[2, :own_heads],
        )
    else:
        scan_grads = scan_back(grad_scanned)
        back_sent = jnp.concatenate(
            [scan_grads[0], jnp.pad(scan_grads[1], ((0, 0), (0, pad_width)))], axis=-1
        )
        lane_grad = jnp.concatenate([scan_grads[0], scan_grads[1]], axis=-1)
        scan_params = scan_grads[2:]
    back_sent = after(back_sent, *near_halves[1:2]).reshape(parts, patch_count, -1)
    back_taken = trade(back_sent)
    own_half = jnp.stack([unit_half] + [after(half, back_sent) for half in near_halves])
    group_in, group_hidden, group_gate, group_up = group_mlp(
        own_half, swap(own_half, "tp", 1), gain_mlp, group_grad_hidden, w_gate, w_up, place_index
    )
    late_got = joined(late_got, group_hidden)
    apart_valid = jnp.concatenate(by_apart(group_valid), axis=0)
    group_mix = (late_got[:, :model_width] * apart_valid).astype(jnp.bfloat16)
    group_z = late_got[:, model_width:]
    late_early = joined(early_got, group_hidden)
    group_u = (late_early[:, :model_width] * gain_global).astype(jnp.bfloat16)
    quarter = inner_width // members
    own_scale = lax.dynamic_slice_in_dim(mix_scale, member * quarter, quarter, 0)
    group_n = (late_early[:, model_width:] * own_scale).astype(jnp.bfloat16)
    mlp_blocks = [
        grad_blocks(
            [(group_final, group_hidden, 0, hidden_part), (group_in, group_gate, 0, hidden_part)],
            0,
            True,
        ),
        grad_blocks(
            [
                (group_in, group_up, 0, hidden_part),
                (group_mix, group_n, 0, group_n.shape[1]),
                (group_u, group_z, 0, group_z.shape[1]),
            ],
            1,
            True,
        ),
    ]
    mlp_got = [to_partner(mlp_blocks[first][0], first) for first in range(2)]
    back_taken = after(back_taken, mlp_blocks[0][0], mlp_blocks[1][0])
    grad_x = from_lanes(back_taken[..., :width])
    by_stream = back_taken.reshape(streams, lanes, patch_count, -1)
    grad_bc = jnp.sum(by_stream[..., width:scan_width], axis=1)
    grad_dt = from_lanes(back_taken[..., scan_width : scan_width + own_heads])
    grad_dt = jnp.sum(grad_dt.reshape(streams, patch_count, head_total, shared), axis=-1)
    grad_shared = jnp.concatenate([grad_bc, grad_dt], axis=-1).reshape(patch_total, -1)
    grad_proj_low = jnp.concatenate(
        [grad_z_low, grad_x.reshape(patch_total, -1).astype(jnp.bfloat16)]
        + [grad_shared.astype(jnp.bfloat16)],
        axis=-1,
    )
    grad_u_part = dot_trans(grad_proj_low, w_in)
    attn_far = [
        add_side(after(attn_blocks[first][1], grad_u_part), attn_got[first], 1)
        for first in range(2)
    ]
    attn_crossed = [to_partner(attn_far[first], 1 - first) for first in range(2)]
    grad_u = after(tp_sum(grad_u_part), *attn_far)
    rest = [quarters(columns) for columns in (grad_x, grad_bc, grad_dt)]
    rest_cols = [part.shape[-1] for part in rest]
    rest = after(jnp.concatenate(rest, axis=-1), grad_u_part)
    rest = jnp.pad(rest, ((0, 0), (0, 0), (0, -sum(rest_cols) % 128)))
    rest_blocks = grad_blocks(
        [(group_u, joined(group_swap(by_apart(rest)), grad_u_part), 0, rest.shape[-1])], 0, True
    )
    back_global, grad_norm_global = rms_back(patch_out, gain_global, grad_u)
    grad_patch = grad_global + back_global
    side_count = parts // 2
    my_side = seq_index & 1
    by_block = jnp.moveaxis(grad_patch.reshape(patch_total, parts, row_block), 1, 0)
    by_block = by_block.reshape(side_count, 2, patch_total, row_block)
    same_side = lax.dynamic_index_in_dim(by_block, my_side, 1, keepdims=False)
    other_side = lax.dynamic_index_in_dim(by_block, 1 - my_side, 1, keepdims=False)
    patch_rows = jnp.concatenate([same_side, other_side], axis=-1)
    patch_rows = patch_rows.reshape(side_count, patch_total, 2 * row_block)
    gain_part = grad_norm_global.reshape(-1, 2 * row_block)
    gain_count = gain_part.shape[0]
    patch_sent = jnp.concatenate(
        [patch_rows, jnp.broadcast_to(gain_part, (side_count,) + gain_part.shape)], axis=1
    )
    patch_taken = lax.all_to_all(
        patch_sent, "seq", 0, 0, axis_index_groups=row_side, tiled=True
    )

    mlp_far = [
        add_side(after(mlp_blocks[first][1], patch_sent), mlp_got[first], 1)
        for first in range(2)
    ]
    mlp_crossed = [to_partner(mlp_far[first], 1 - first) for first in range(2)]
    patch_taken = after(patch_taken, rest_blocks[0], *mlp_far)
    gain_side = jnp.sum(patch_taken[:, patch_total:], axis=0)
    patch_cols = patch_taken[:, :patch_total].reshape(-1, 2 * row_block)
    patch_far = patch_far_grad(patch_cols, gain_side, bytes_all)
    small = (
        scan_params[0][:, :width],
        scan_params[1][:width],
        scan_params[0][:, width:],
        scan_params[1][width:],
        scan_params[2],
        scan_params[3],
        scan_params[4],
        grad_mix_gain,
        grad_norm_attn,
        grad_norm_mlp,
    )
    small_count = sum(part.size for part in small)
    flat = after(jnp.concatenate([part.reshape(-1) for part in small]), patch_far)
    flat = jnp.pad(flat, (0, -small_count % 1024)).reshape(1, -1, 128)
    pieces = trade(jnp.broadcast_to(flat, (parts,) + flat.shape[1:])).reshape(parts, -1)
    by_small, at = [], 0
    for part in small:
        got = pieces[:, at : at + part.size].reshape((parts,) + part.shape)
        by_small.append(got)
        at += part.size

    def lane_cols(got):
        joined = jnp.sum(got.reshape((streams, lanes) + got.shape[1:]), axis=0)
        return jnp.moveaxis(joined, 0, -2).reshape(joined.shape[1:-1] + (-1,))

    def lane_heads(got):
        joined = jnp.sum(got.reshape(streams, lanes, -1), axis=0)
        return jnp.sum(joined.reshape(head_total, shared), axis=-1)

    small_sums = [
        jnp.concatenate([lane_cols(by_small[0]), jnp.sum(by_small[2], axis=0)], axis=-1),
        jnp.concatenate([lane_cols(by_small[1]), jnp.sum(by_small[3], axis=0)], axis=-1),
        lane_heads(by_small[4]),
        lane_heads(by_small[5]),
        lane_heads(by_small[6]),
    ] + [jnp.sum(got, axis=0) for got in by_small[7:]]

    patch_got = to_partner(patch_far, 0)

    high = (seq_index // QUAD).astype(jnp.int32).reshape(1)
    attn_near = near_sums(
        [
            (after(attn_blocks[first][1], patch_far), attn_got[first], attn_crossed[first])
            for first in range(2)
        ],
        high,
    )
    attn_high = [
        swap(attn_near[apart], "seq", QUAD * apart) for apart in range(1, parts // QUAD)
    ]
    rest_got = to_partner(after(rest_blocks[0], patch_far), 0)
    start = jnp.zeros((1,), jnp.int32)
    mlp_near = [
        near_sums(
            [(after(mlp_blocks[first][1], attn_near, patch_got), mlp_got[first], mlp_crossed[first])],
            start,
        )
        for first in range(2)
    ]
    rest_far = add_side(after(rest_blocks[1], mlp_near[0]), rest_got, 1)
    rest_crossed = to_partner(rest_far, 1)
    rest_near = near_sums(
        [(after(rest_blocks[1], mlp_near[1]), rest_got, rest_crossed)], start
    )
    mlp_finals = [
        jnp.moveaxis(group_trade(part), 0, 1) for part in mlp_near + [rest_near]
    ]
    final_attn = attn_near[0]
    for got in attn_high:
        final_attn = final_attn + after(got, *mlp_near)

    def final_cols(final, low, count):
        return final[..., low : low + count].reshape(row_block, -1)

    final_down = final_cols(mlp_finals[0], 0, hidden_part)
    final_gate = final_cols(mlp_finals[0], hidden_part, hidden_part)
    final_up = final_cols(mlp_finals[1], 0, hidden_part)
    final_out = final_cols(mlp_finals[1], hidden_part, quarter)
    final_z = final_cols(mlp_finals[1], hidden_part + quarter, quarter)
    final_x = final_cols(mlp_finals[2], 0, rest_cols[0])
    final_bc = final_cols(mlp_finals[2], rest_cols[0], rest_cols[1])
    final_dt = final_cols(mlp_finals[2], rest_cols[0] + rest_cols[1], rest_cols[2])
    final_patch = patch_grad(patch_cols, patch_got, bytes_all)
    norm_global_sum = (gain_side + patch_got[row_block:, : 2 * row_block]).reshape(-1)
    grad_bytes = bytes_grad(after(grad_patch, patch_far), w_patch, grad_stream)
    grad_bytes = grad_bytes.reshape(streams, local_rows, feature)

    qkv_cols, o_cols = w_qkv.shape[1], w_o.shape[1]
    return (
        logits.reshape(streams, local_rows, head_cols),
        grad_bytes,
        final_patch,
        norm_global_sum,
        jnp.concatenate([final_z, final_x, final_bc, final_dt], axis=1),
        small_sums[0],
        small_sums[1],
        small_sums[2],
        small_sums[3],
        small_sums[4],
        small_sums[5],
        final_out,
        small_sums[6],
        final_attn[:, :qkv_cols],
        final_attn[:, qkv_cols : qkv_cols + o_cols],
        small_sums[7],
        final_gate,
        final_up,
        final_down,
        final_attn[:, qkv_cols + o_cols :],
    )


def solution(mesh):
    in_specs = (
        P(None, "seq", None),
        P(),
        P(None, "tp"),
        P(),
        P(None, "tp"),
        P(None, "tp"),
        P("tp"),
        P("tp"),
        P("tp"),
        P("tp"),
        P("tp"),
        P(None, "tp"),
        P(),
        P(None, "tp"),
        P(None, "tp"),
        P(),
        P(None, "tp"),
        P(None, "tp"),
        P(None, "tp"),
        P(None, "tp"),
        P(None, "seq", "tp"),
    )
    out_specs = (
        P(None, "seq", "tp"),
        P(None, "seq", "tp"),
        P("seq", "tp"),
        P(),
        P("seq", "tp"),
        P(None, "tp"),
        P("tp"),
        P("tp"),
        P("tp"),
        P("tp"),
        P("tp"),
        P("seq", "tp"),
        P(),
        P("seq", "tp"),
        P("seq", "tp"),
        P(),
        P("seq", "tp"),
        P("seq", "tp"),
        P("seq", "tp"),
        P("seq", "tp"),
    )
    return jax.shard_map(body, mesh=mesh, in_specs=in_specs, out_specs=out_specs, check_vma=False)
```

```python
from functools import partial

import jax
import jax.numpy as jnp
from jax import lax
from jax.experimental import pallas as pl
from jax.experimental.pallas import tpu as pltpu
from jax.sharding import PartitionSpec as P

NS = 128
AD = 64
QUAD = 4


NO_COST = pl.CostEstimate(flops=1024, bytes_accessed=1024, transcendentals=0)
ROOMY = pltpu.CompilerParams(vmem_limit_bytes=56 * 1024 * 1024)

epsilon = 1e-05
highest = lax.Precision.HIGHEST
masked_score = -1e30


def dot_plain(left_side, right_side):
    return jnp.dot(left_side, right_side, preferred_element_type=jnp.float32)


def dot_trans(left_side, right_side):
    return lax.dot_general(
        left_side, right_side, (((1,), (1,)), ((), ())), preferred_element_type=jnp.float32
    )


def dot_left(left_side, right_side):
    return lax.dot_general(
        left_side, right_side, (((0,), (0,)), ((), ())), preferred_element_type=jnp.float32
    )


def rms_scale(values):
    return lax.rsqrt(jnp.mean(values * values, axis=-1, keepdims=True) + epsilon)


def hidden_parts(mlp_in, grad_hidden, w_gate, w_up):
    gate_proj = dot_plain(mlp_in, w_gate)
    up_proj = dot_plain(mlp_in, w_up)
    sigmoid_gate = jax.nn.sigmoid(gate_proj)
    hidden_low = (gate_proj * sigmoid_gate * up_proj).astype(jnp.bfloat16)
    grad_gate_low = (
        grad_hidden * up_proj * sigmoid_gate * (1.0 + gate_proj * (1.0 - sigmoid_gate))
    ).astype(jnp.bfloat16)
    grad_up_low = (grad_hidden * gate_proj * sigmoid_gate).astype(jnp.bfloat16)
    return (hidden_low, grad_gate_low, grad_up_low)


def rms_back(values, gain_values, grad_out):
    scale = rms_scale(values)
    scaled = gain_values * grad_out
    inner_mean = jnp.mean(values * scaled, axis=-1, keepdims=True)
    grad_values = scale * scaled - values * scale * scale * scale * inner_mean
    grad_gain = jnp.sum(values * scale * grad_out, axis=0)
    return (grad_values, grad_gain)


def swap(block, axis, mask):
    return lax.ppermute(block, axis, [(i, i ^ mask) for i in range(lax.axis_size(axis))])


def after(value, *earlier):
    return lax.optimization_barrier((value,) + earlier)[0]


def tp_sum(block):
    return block + swap(block, "tp", 1)


def to_partner(block, bit):
    return swap(block, "seq", 1 << bit)


def seq_bits():
    return lax.axis_size("seq").bit_length() - 1


def group_size():
    return lax.axis_size("seq") // QUAD


def group_trade(blocks):
    members = [[low + QUAD * high for high in range(group_size())] for low in range(QUAD)]
    return lax.all_to_all(blocks, "seq", 0, 0, axis_index_groups=members, tiled=True)


def add_kernel(index_ref, *refs):
    total = refs[0][...] + refs[1][...]
    refs[2][...] = total.reshape(refs[2].shape)


def add_side(near, got, side):
    unused, groups, rows, cols = near.shape
    index = jnp.zeros((1,), jnp.int32)
    block = pl.BlockSpec((1, 1, rows, cols), lambda i, ref: (side, i, 0, 0))
    return pl.pallas_call(
        add_kernel,
        grid_spec=pltpu.PrefetchScalarGridSpec(
            num_scalar_prefetch=1,
            grid=(groups,),
            in_specs=[block, block],
            out_specs=pl.BlockSpec((1, rows, cols), lambda i, ref: (i, 0, 0)),
        ),
        out_shape=jax.ShapeDtypeStruct((groups, rows, cols), jnp.float32),
        compiler_params=ROOMY,
        cost_estimate=NO_COST,
    )(index, near, got)


def near_kernel(index_ref, *refs):
    out_ref = refs[-1]
    at = 0
    for near_ref, got_ref, crossed_ref in zip(refs[0:-1:3], refs[1:-1:3], refs[2:-1:3]):
        cols = near_ref.shape[3]
        total = near_ref[0, 0] + got_ref[0, 0] + crossed_ref[0]
        out_ref[0, :, at : at + cols] = total
        at += cols


def near_sums(terms, high):
    unused, groups, rows, unused_cols = terms[0][0].shape
    cols = [term[0].shape[3] for term in terms]
    specs, operands = [], []
    for (near, got, crossed), count in zip(terms, cols):
        four = pl.BlockSpec((1, 1, rows, count), lambda i, ref: (0, ref[0] ^ i, 0, 0))
        three = pl.BlockSpec((1, rows, count), lambda i, ref: (ref[0] ^ i, 0, 0))
        specs += [four, four, three]
        operands += [near, got, crossed]
    return pl.pallas_call(
        near_kernel,
        grid_spec=pltpu.PrefetchScalarGridSpec(
            num_scalar_prefetch=1,
            grid=(groups,),
            in_specs=specs,
            out_specs=pl.BlockSpec((1, rows, sum(cols)), lambda i, ref: (i, 0, 0)),
        ),
        out_shape=jax.ShapeDtypeStruct((groups, rows, sum(cols)), jnp.float32),
        compiler_params=ROOMY,
        cost_estimate=NO_COST,
    )(high, *operands)


def grad_blocks_kernel(pairs, first, relative, rows, member_ref, *refs):
    lefts, rights = refs[: len(pairs)], refs[len(pairs) : 2 * len(pairs)]
    far_ref, near_ref = refs[2 * len(pairs) :]
    other = 1 - first
    at = 0
    for left_ref, right_ref, (low, high) in zip(lefts, rights, pairs):
        got = dot_left(left_ref[...], right_ref[:, low:high].astype(jnp.bfloat16))
        places = slice(at, at + high - low)
        for block in range(got.shape[0] // rows):
            place, member = block // QUAD, block % QUAD
            part = got[block * rows : (block + 1) * rows]
            apart = member_ref[0] ^ member
            is_far = apart >> first & 1
            if relative:
                side = apart >> other & 1
            else:
                side = member >> other & 1

            @pl.when(is_far == 1)
            def _():
                if relative:
                    far_ref[side, place, :, places] = part
                else:
                    far_ref[place, side, :, places] = part

            @pl.when(is_far == 0)
            def _():
                if relative:
                    near_ref[side, place, :, places] = part
                else:
                    near_ref[place, side, :, places] = part

        at += high - low


def grad_blocks(terms, first, relative):
    parts = lax.axis_size("seq")
    groups = parts // QUAD
    model_width = terms[0][0].shape[1]
    rows = model_width // parts
    cols = max(128, QUAD * rows)
    places = cols // (QUAD * rows)
    pairs = [(low, high) for unused, unused_right, low, high in terms]
    total = sum(high - low for low, high in pairs)
    member = (lax.axis_index("seq") % QUAD).astype(jnp.int32).reshape(1)
    if relative:
        shape, block = (2, groups, rows, total), (2, places, rows, total)
        out_spec = pl.BlockSpec(block, lambda i, ref: (0, i, 0, 0))
    else:
        shape, block = (groups, 2, rows, total), (places, 2, rows, total)
        out_spec = pl.BlockSpec(block, lambda i, ref: (i, 0, 0, 0))
    out = jax.ShapeDtypeStruct(shape, jnp.float32)
    return pl.pallas_call(
        partial(grad_blocks_kernel, pairs, first, relative, rows),
        grid_spec=pltpu.PrefetchScalarGridSpec(
            num_scalar_prefetch=1,
            grid=(model_width // cols,),
            in_specs=[
                pl.BlockSpec((term[0].shape[0], cols), lambda i, ref: (0, i)) for term in terms
            ]
            + [pl.BlockSpec(term[1].shape, lambda i, ref: (0, 0)) for term in terms],
            out_specs=[out_spec, out_spec],
        ),
        out_shape=[out, out],
        compiler_params=ROOMY,
        cost_estimate=NO_COST,
    )(member, *[term[0] for term in terms], *[term[1] for term in terms])


def segment_ids(lengths, place_count):
    ends = jnp.cumsum(lengths // 8, dtype=jnp.int32)
    places = jnp.arange(place_count, dtype=jnp.int32)
    short_ids = jnp.sum(
        (places[:, None] >= ends[None, :]).astype(jnp.int32), axis=1, dtype=jnp.int32
    )
    return jnp.stack([jnp.zeros_like(short_ids), short_ids])


def scan_heads(seg_now, head_size, xbc, dt_raw, conv_weight, conv_bias, dt_shift, a_logs, skips):
    place_count = xbc.shape[0]
    conv_sum = conv_bias + conv_weight[3] * xbc
    for offset in range(3):
        distance = 3 - offset
        earlier = jnp.pad(xbc, ((distance, 0), (0, 0)))[:place_count]
        seg_earlier = jnp.pad(seg_now, (distance, 0), constant_values=-1)[:place_count]
        same_doc = (seg_earlier == seg_now).astype(jnp.float32)
        conv_sum = conv_sum + conv_weight[offset] * earlier * same_doc[:, None]
    active = jax.nn.silu(conv_sum)
    head_count = dt_raw.shape[1]
    inner = head_count * head_size
    values = active[:, :inner].reshape(place_count, head_count, head_size)
    in_keys = active[:, inner : inner + NS]
    out_keys = active[:, inner + NS :]
    step_sizes = jax.nn.softplus(dt_raw + dt_shift)
    decay_rates = -step_sizes * jnp.exp(a_logs)
    chunk = min(place_count, 512)
    triangle = jnp.tril(jnp.ones((chunk, chunk), jnp.float32))
    state = jnp.zeros((head_count, head_size, NS), jnp.float32)
    seg_last = jnp.int32(-1)
    outputs = []
    for start in range(0, place_count, chunk):
        stop = start + chunk
        x, b, c = values[start:stop], in_keys[start:stop], out_keys[start:stop]
        dt, seg = step_sizes[start:stop], seg_now[start:stop]
        cumulative = jnp.dot(triangle, decay_rates[start:stop], precision=highest)
        allowed = (triangle > 0.0) & (seg[:, None] == seg[None, :])
        ordered = cumulative.T
        gaps = ordered[:, :, None] - ordered[:, None, :]
        decays = jnp.where(allowed, jnp.exp(jnp.where(allowed, gaps, 0.0)), 0.0)
        crossing = jnp.einsum("pn,jn->pj", c, b, precision=highest)
        mixing = crossing[None] * decays * dt.T[:, None, :]
        result = jnp.einsum("hpj,jhd->phd", mixing, x, precision=highest)
        if start > 0:
            entering = jnp.exp(cumulative) * (seg == seg_last).astype(jnp.float32)[:, None]
            result = result + entering[..., None] * jnp.einsum(
                "pn,hdn->phd", c, state, precision=highest
            )
        if stop < place_count:
            last_same = (seg == seg[-1]).astype(jnp.float32)[:, None]
            weight = jnp.exp(cumulative[-1:] - cumulative) * last_same * dt
            through = jnp.exp(cumulative[-1]) * (seg[-1] == seg_last).astype(jnp.float32)
            state = through[:, None, None] * state + jnp.einsum(
                "jh,jhd,jn->hdn", weight, x, b, precision=highest
            )
            seg_last = seg[-1]
        outputs.append(result + skips[:, None] * x)
    return jnp.concatenate(outputs, axis=0).reshape(place_count, inner)


def gated_unit(result, gate_in):
    gated = result * jax.nn.silu(gate_in)
    return gated * rms_scale(gated)


def patch_far_kernel(grad_ref, gain_ref, bytes_ref, out_ref):
    half = grad_ref.shape[1] // 2
    grad_low = grad_ref[:, half:].astype(jnp.bfloat16)
    out_ref[:half] = dot_left(grad_low, bytes_ref[...].astype(jnp.bfloat16))
    out_ref[half:] = jnp.zeros((out_ref.shape[0] - half, out_ref.shape[1]), jnp.float32)

    @pl.when(pl.program_id(0) == 0)
    def _():
        out_ref[half:, : 2 * half] = gain_ref[...]


def patch_far_grad(grad_rows, gain_part, bytes_all):
    places, cols = grad_rows.shape
    total = bytes_all.shape[1]
    rows = cols // 2 + gain_part.shape[0]
    block = 1024
    return pl.pallas_call(
        patch_far_kernel,
        grid=(total // block,),
        in_specs=[
            pl.BlockSpec((places, cols), lambda i: (0, 0)),
            pl.BlockSpec(gain_part.shape, lambda i: (0, 0)),
            pl.BlockSpec((places, block), lambda i: (0, i)),
        ],
        out_specs=pl.BlockSpec((rows, block), lambda i: (0, i)),
        out_shape=jax.ShapeDtypeStruct((rows, total), jnp.float32),
        compiler_params=ROOMY,
        cost_estimate=NO_COST,
    )(grad_rows, gain_part, bytes_all)


def patch_grad_kernel(grad_ref, *refs):
    byte_refs, got_refs, out_ref, order_ref = refs[:8], refs[8:16], refs[16], refs[17]
    width = byte_refs[0].shape[1]

    @pl.when(pl.program_id(0) == 0)
    def _():
        order_ref[...] = feature_order(width)

    grad_low = grad_ref[:, : grad_ref.shape[1] // 2].astype(jnp.bfloat16)
    wide = jnp.concatenate([ref[...].astype(jnp.bfloat16) for ref in byte_refs], axis=1)
    rows = grad_low.shape[1]
    grad = dot_left(grad_low, wide)
    grad = grad + jnp.concatenate([ref[:rows] for ref in got_refs], axis=1)
    high = grad.astype(jnp.bfloat16)
    rest = grad - high.astype(jnp.float32)
    mid = rest.astype(jnp.bfloat16)
    low = (rest - mid.astype(jnp.float32)).astype(jnp.bfloat16)
    order = order_ref[...]
    out_ref[...] = dot_plain(high, order) + (dot_plain(mid, order) + dot_plain(low, order))


def patch_grad(grad_rows, got, bytes_all):
    places, cols = grad_rows.shape
    feature = bytes_all.shape[1] // 8
    chunk = 128
    steps = feature // chunk

    def byte_specs(rows):
        return [
            pl.BlockSpec((rows, chunk), partial(lambda j, i: (0, j * steps + i), j))
            for j in range(8)
        ]

    return pl.pallas_call(
        patch_grad_kernel,
        grid=(steps,),
        in_specs=[pl.BlockSpec((places, cols), lambda i: (0, 0))]
        + byte_specs(places)
        + byte_specs(got.shape[0]),
        out_specs=pl.BlockSpec((cols // 2, 8 * chunk), lambda i: (0, i)),
        out_shape=jax.ShapeDtypeStruct((cols // 2, 8 * feature), jnp.float32),
        scratch_shapes=[pltpu.VMEM((8 * chunk, 8 * chunk), jnp.bfloat16)],
        compiler_params=ROOMY,
        cost_estimate=NO_COST,
    )(grad_rows, *([bytes_all] * 8), *([got] * 8))


def trade(blocks):
    return lax.all_to_all(blocks, "seq", 0, 0, tiled=True)


def grid_iota(shape, axis):
    return lax.broadcasted_iota(jnp.int32, shape, axis)


def dot_fine(left_side, right_side, left_axis, right_axis):
    return lax.dot_general(
        left_side,
        right_side,
        (((left_axis,), (right_axis,)), ((), ())),
        preferred_element_type=jnp.float32,
        precision=highest,
    )


def shifted_down(block, distance):
    rows = grid_iota(block.shape, 0)
    return jnp.where(rows >= distance, pltpu.roll(block, distance, 0), 0.0)


def shifted_up(block, distance):
    count = block.shape[0]
    rows = grid_iota(block.shape, 0)
    return jnp.where(rows < count - distance, pltpu.roll(block, count - distance, 0), 0.0)


def scan_terms(taken_ref, same_ref, conv_ref, head_ref):
    places = taken_ref.shape[0]
    channels = conv_ref.shape[1]
    xbc = taken_ref[:, :channels]
    conv_sum = conv_ref[4:5] + conv_ref[3:4] * xbc
    for k in range(3):
        earlier = shifted_down(xbc, 3 - k) * same_ref[:, k : k + 1]
        conv_sum = conv_sum + conv_ref[k : k + 1] * earlier
    gate = jax.nn.sigmoid(conv_sum)
    active = conv_sum * gate
    raw = taken_ref[:, channels:] + head_ref[0:1]
    steps = jnp.maximum(raw, 0.0) + jnp.log1p(jnp.exp(-jnp.abs(raw)))
    rates = -steps * jnp.exp(head_ref[1:2])
    square = (places, places)
    triangle = jnp.where(grid_iota(square, 0) >= grid_iota(square, 1), 1.0, 0.0)
    running = dot_fine(triangle, rates, 1, 0)
    return xbc, conv_sum, gate, active, raw, steps, rates, triangle, running


def scan_forward_kernel(taken_ref, same_ref, conv_ref, head_ref, seg_col, seg_row, out_ref):
    places, width = out_ref.shape
    terms = scan_terms(taken_ref, same_ref, conv_ref, head_ref)
    active, steps, running = terms[3], terms[5], terms[8]
    values = active[:, :width]
    keys, reads = active[:, width : width + NS], active[:, width + NS :]
    steps_row, running_row = steps.T, running.T
    heads = width // 64
    rows = 128
    for first in range(0, places, rows):
        last = first + rows
        shape = (rows, last)
        allowed = (seg_col[first:last] == seg_row[:, :last]) & (
            grid_iota(shape, 0) + first >= grid_iota(shape, 1)
        )
        crossing = dot_fine(reads[first:last], keys[:last], 1, 1)
        lane = grid_iota((rows, width), 1) // 64
        total = head_ref[2:3] * values[first:last]
        for h in range(heads):
            gaps = running[first:last, h : h + 1] - running_row[h : h + 1, :last]
            decays = jnp.exp(jnp.where(allowed, gaps, masked_score))
            mixing = crossing * decays * steps_row[h : h + 1, :last]
            part = dot_fine(mixing, values[:last], 1, 0)
            total = total + jnp.where(lane == h, part, 0.0)
        out_ref[first:last] = total


def scan_backward_kernel(
    taken_ref,
    same_ref,
    conv_ref,
    head_ref,
    seg_col,
    seg_row,
    grad_ref,
    out_ref,
    conv_grad_ref,
    head_grad_ref,
    values_grad,
    keys_grad,
    reads_grad,
    rows_grad,
    cols_grad,
):
    places, width = values_grad.shape
    terms = scan_terms(taken_ref, same_ref, conv_ref, head_ref)
    xbc, conv_sum, gate, active, raw, steps, rates, triangle, running = terms
    channels = xbc.shape[1]
    values = active[:, :width]
    keys, reads = active[:, width : width + NS], active[:, width + NS :]
    steps_row, running_row = steps.T, running.T
    heads = width // 64
    rows = 128
    grad = grad_ref[...]
    values_grad[...] = head_ref[2:3] * grad
    keys_grad[...] = jnp.zeros_like(keys_grad)
    rows_grad[...] = jnp.zeros_like(rows_grad)
    cols_grad[...] = jnp.zeros_like(cols_grad)
    for first in range(0, places, rows):
        last = first + rows
        shape = (rows, last)
        allowed = (seg_col[first:last] == seg_row[:, :last]) & (
            grid_iota(shape, 0) + first >= grid_iota(shape, 1)
        )
        crossing = dot_fine(reads[first:last], keys[:last], 1, 1)
        crossing_grad = jnp.zeros(shape, jnp.float32)
        grad_rows = grad[first:last]
        lane = grid_iota((rows, width), 1) // 64
        wide_lane = grid_iota((last, width), 1) // 64
        column = grid_iota((rows, 128), 1)
        down = jnp.zeros((rows, 128), jnp.float32)
        for h in range(heads):
            gaps = running[first:last, h : h + 1] - running_row[h : h + 1, :last]
            decays = jnp.exp(jnp.where(allowed, gaps, masked_score))
            step_row = steps_row[h : h + 1, :last]
            weighted = decays * step_row
            mixing = crossing * weighted
            own_grad = jnp.where(lane == h, grad_rows, 0.0)
            mixing_grad = dot_fine(own_grad, values[:last], 1, 1)
            back = dot_fine(mixing, own_grad, 0, 0)
            values_grad[:last] += jnp.where(wide_lane == h, back, 0.0)
            crossing_grad = crossing_grad + mixing_grad * weighted
            step_part = jnp.sum(mixing_grad * crossing * decays, axis=0, keepdims=True)
            gap_part = mixing_grad * mixing
            down = jnp.where(column == h, jnp.sum(gap_part, axis=1, keepdims=True), down)
            cols_grad[h : h + 1, :last] += step_part
            cols_grad[heads + h : heads + h + 1, :last] += step_part * step_row
        rows_grad[first:last] += down
        reads_grad[first:last] = dot_fine(crossing_grad, keys[:last], 1, 0)
        keys_grad[:last] += dot_fine(crossing_grad, reads[first:last], 0, 0)
    turned = cols_grad[...].T
    column = grid_iota(turned.shape, 1)
    step_grad = jnp.where(column < heads, turned, 0.0)
    ended = pltpu.roll(turned, turned.shape[1] - heads, 1)
    running_grad = jnp.where(column < heads, rows_grad[...] - ended, 0.0)
    rates_grad = dot_fine(triangle, running_grad, 0, 0)
    step_grad = step_grad - rates_grad * jnp.exp(head_ref[1:2])
    raw_grad = step_grad * jax.nn.sigmoid(raw)
    out_ref[:, channels:] = raw_grad
    lane = grid_iota((places, width), 1) // 64
    product = jnp.sum(grad * values, axis=0, keepdims=True)
    head_grad_ref[...] = jnp.zeros_like(head_grad_ref)
    head_grad_ref[0:1] = jnp.sum(raw_grad, axis=0, keepdims=True)
    head_grad_ref[1:2] = jnp.sum(rates_grad * rates, axis=0, keepdims=True)
    skip_lane = grid_iota((1, width), 1)
    skip_grad = jnp.zeros((1, width), jnp.float32)
    for h in range(heads):
        own = jnp.sum(jnp.where(skip_lane // 64 == h, product, 0.0), axis=1, keepdims=True)
        skip_grad = jnp.where(skip_lane == h, own, skip_grad)
    head_grad_ref[2:3] = skip_grad
    active_grad = jnp.concatenate([values_grad[...], keys_grad[...], reads_grad[...]], axis=1)
    conv_grad = active_grad * gate * (1.0 + conv_sum * (1.0 - gate))
    back = conv_ref[3:4] * conv_grad
    conv_grad_ref[...] = jnp.zeros_like(conv_grad_ref)
    conv_grad_ref[3:4] = jnp.sum(conv_grad * xbc, axis=0, keepdims=True)
    conv_grad_ref[4:5] = jnp.sum(conv_grad, axis=0, keepdims=True)
    for k in range(3):
        kept = conv_grad * same_ref[:, k : k + 1]
        back = back + conv_ref[k : k + 1] * shifted_up(kept, 3 - k)
        conv_grad_ref[k : k + 1] = jnp.sum(
            kept * shifted_down(xbc, 3 - k), axis=0, keepdims=True
        )
    out_ref[:, :channels] = back


def scan_forward(args, width):
    places = args[0].shape[0]
    return pl.pallas_call(
        scan_forward_kernel,
        out_shape=jax.ShapeDtypeStruct((places, width), jnp.float32),
        compiler_params=ROOMY,
        cost_estimate=NO_COST,
    )(*args)


def scan_backward(args, grad):
    places, width = grad.shape
    channels = args[2].shape[1]
    f32 = jnp.float32
    return pl.pallas_call(
        scan_backward_kernel,
        out_shape=[
            jax.ShapeDtypeStruct((places, channels + 128), f32),
            jax.ShapeDtypeStruct((8, channels), f32),
            jax.ShapeDtypeStruct((8, 128), f32),
        ],
        scratch_shapes=[
            pltpu.VMEM((places, width), f32),
            pltpu.VMEM((places, NS), f32),
            pltpu.VMEM((places, NS), f32),
            pltpu.VMEM((places, 128), f32),
            pltpu.VMEM((128, places), f32),
        ],
        compiler_params=ROOMY,
        cost_estimate=NO_COST,
    )(*args, grad)


def patch_lanes(block):
    shape = (block // 8, 8, block)
    return grid_iota(shape, 0) == grid_iota(shape, 2) // 8


def folded(scores, same_patch):
    split = scores.reshape(same_patch.shape)
    return jnp.sum(jnp.where(same_patch, split, 0.0), axis=0)


def unfolded(rows, same_patch):
    spread = jnp.where(same_patch, rows[None], 0.0)
    return spread.reshape(-1, rows.shape[1]).astype(jnp.bfloat16)


def softmax_rows(scores, causal):
    scores = jnp.where(causal, scores, masked_score)
    top = jnp.max(scores, axis=1, keepdims=True)
    powers = jnp.exp(scores - top)
    return powers / jnp.sum(powers, axis=1, keepdims=True)


def head_places(rows, head_cols, block):
    return [
        (slice(first, first + block), [j * head_cols + pair * 128 for j in range(3)])
        for first in range(0, rows, block)
        for pair in range(head_cols // 128)
    ]


def all_scores(qkv_ref, places, lane, same_patch):
    scores = []
    for rows, (query, key, unused) in places:
        queries = qkv_ref[rows, query : query + 128] * 0.125
        keys = qkv_ref[rows, key : key + 128]
        for h in range(2):
            own = jnp.where(lane == h, queries, 0)
            scores.append(folded(dot_trans(keys, own), same_patch))
    return jnp.stack(scores)


def attn_forward_kernel(
    bytes_ref, patch_ref, gain_ref, qkv_w_ref, o_w_ref, x_ref, a_ref, qkv_ref, o_ref, out_ref
):
    rows = bytes_ref.shape[0]
    spread = jnp.broadcast_to(patch_ref[...][:, None], (rows // 8, 8, patch_ref.shape[1]))
    x = bytes_ref[...].astype(jnp.float32) + spread.reshape(bytes_ref.shape)
    x_ref[...] = x
    attn_in = (x * rms_scale(x) * gain_ref[...]).astype(jnp.bfloat16)
    a_ref[...] = attn_in
    qkv_ref[...] = dot_plain(attn_in, qkv_w_ref[...]).astype(jnp.bfloat16)
    head_cols = o_ref.shape[1]
    block = 128
    same_patch = patch_lanes(block)
    causal = grid_iota((8, block), 0) <= grid_iota((8, block), 1) % 8
    lane = grid_iota((block, 128), 1) // AD
    places = head_places(rows, head_cols, block)
    probs = softmax_rows(all_scores(qkv_ref, places, lane, same_patch), causal)
    for at, (row_place, (query, unused, value)) in enumerate(places):
        values = qkv_ref[row_place, value : value + 128]
        parts = [dot_left(unfolded(probs[2 * at + h], same_patch), values) for h in range(2)]
        total = jnp.where(lane == 0, parts[0], parts[1])
        o_ref[row_place, query : query + 128] = total.astype(jnp.bfloat16)
    out_ref[...] = dot_trans(o_ref[...], o_w_ref[...])


def attn_forward(bytes_rows, patch_rows, gain, w_qkv, w_o):
    rows, width = bytes_rows.shape
    block = 256
    cols, head_cols = w_qkv.shape[1], w_o.shape[1]
    f32, bf16 = jnp.float32, jnp.bfloat16

    def by_rows(cols):
        return pl.BlockSpec((block, cols), lambda i: (i, 0))

    def whole(shape):
        return pl.BlockSpec(shape, lambda i: (0, 0))

    return pl.pallas_call(
        attn_forward_kernel,
        grid=(rows // block,),
        in_specs=[
            by_rows(width),
            pl.BlockSpec((block // 8, width), lambda i: (i, 0)),
            whole((1, width)),
            whole(w_qkv.shape),
            whole(w_o.shape),
        ],
        out_specs=[by_rows(width), by_rows(width), by_rows(cols), by_rows(head_cols), by_rows(width)],
        out_shape=[
            jax.ShapeDtypeStruct((rows, width), f32),
            jax.ShapeDtypeStruct((rows, width), bf16),
            jax.ShapeDtypeStruct((rows, cols), bf16),
            jax.ShapeDtypeStruct((rows, head_cols), bf16),
            jax.ShapeDtypeStruct((rows, width), f32),
        ],
        compiler_params=ROOMY,
        cost_estimate=NO_COST,
    )(bytes_rows, patch_rows, gain.reshape(1, width), w_qkv, w_o)


def attn_backward_kernel(
    x_ref,
    final_ref,
    own_ref,
    other_ref,
    gain_ref,
    qkv_ref,
    qkv_w_ref,
    o_w_ref,
    mid_ref,
    low_ref,
    qkv_grad_ref,
    out_ref,
    gain_grad_ref,
):
    rows = x_ref.shape[0]
    back, gain_grad = rms_back(x_ref[...], gain_ref[...], own_ref[...] + other_ref[...])
    mid = final_ref[...] + back
    mid_ref[...] = mid
    low_ref[...] = mid.astype(jnp.bfloat16)
    gain_grad = gain_grad.reshape(1, -1)

    @pl.when(pl.program_id(0) == 0)
    def _():
        gain_grad_ref[...] = gain_grad

    @pl.when(pl.program_id(0) > 0)
    def _():
        gain_grad_ref[...] += gain_grad

    mixed_grad = dot_plain(low_ref[...], o_w_ref[...]).astype(jnp.bfloat16)
    head_cols = mixed_grad.shape[1]
    block = 128
    same_patch = patch_lanes(block)
    causal = grid_iota((8, block), 0) <= grid_iota((8, block), 1) % 8
    lane = grid_iota((block, 128), 1) // AD
    places = head_places(rows, head_cols, block)
    probs = softmax_rows(all_scores(qkv_ref, places, lane, same_patch), causal)
    probs_grads = []
    for row_place, (query, unused, value) in places:
        values = qkv_ref[row_place, value : value + 128]
        out_grad = mixed_grad[row_place, query : query + 128]
        for h in range(2):
            own_grad = jnp.where(lane == h, out_grad, 0)
            probs_grads.append(folded(dot_trans(values, own_grad), same_patch))
    probs_grad = jnp.stack(probs_grads)
    inner = jnp.sum(probs * probs_grad, axis=1, keepdims=True)
    scores_grad = probs * (probs_grad - inner)
    for at, (row_place, cols) in enumerate(places):
        query, key, unused = cols
        queries = qkv_ref[row_place, query : query + 128]
        keys = qkv_ref[row_place, key : key + 128]
        out_grad = mixed_grad[row_place, query : query + 128]
        parts = []
        for h in range(2):
            own_scores = unfolded(scores_grad[2 * at + h], same_patch)
            parts.append(
                (
                    dot_left(own_scores, keys) * 0.125,
                    dot_plain(own_scores, queries) * 0.125,
                    dot_plain(unfolded(probs[2 * at + h], same_patch), out_grad),
                )
            )
        for j in range(3):
            grad = jnp.where(lane == 0, parts[0][j], parts[1][j])
            qkv_grad_ref[row_place, cols[j] : cols[j] + 128] = grad.astype(jnp.bfloat16)
    out_ref[...] = dot_trans(qkv_grad_ref[...], qkv_w_ref[...])


def attn_backward(x_rows, final_grad, own_part, other_part, gain, qkv, w_qkv, w_o):
    rows, width = x_rows.shape
    block = 256
    cols = w_qkv.shape[1]
    f32, bf16 = jnp.float32, jnp.bfloat16

    def by_rows(cols):
        return pl.BlockSpec((block, cols), lambda i: (i, 0))

    def whole(shape):
        return pl.BlockSpec(shape, lambda i: (0, 0))

    return pl.pallas_call(
        attn_backward_kernel,
        grid=(rows // block,),
        in_specs=[by_rows(width)] * 4
        + [whole((1, width)), by_rows(cols), whole(w_qkv.shape), whole(w_o.shape)],
        out_specs=[
            by_rows(width),
            by_rows(width),
            by_rows(cols),
            by_rows(width),
            whole((1, width)),
        ],
        out_shape=[
            jax.ShapeDtypeStruct((rows, width), f32),
            jax.ShapeDtypeStruct((rows, width), bf16),
            jax.ShapeDtypeStruct((rows, cols), bf16),
            jax.ShapeDtypeStruct((rows, width), f32),
            jax.ShapeDtypeStruct((1, width), f32),
        ],
        compiler_params=ROOMY,
        cost_estimate=NO_COST,
    )(x_rows, final_grad, own_part, other_part, gain.reshape(1, width), qkv, w_qkv, w_o)


def mlp_in_kernel(core_ref, x_ref, own_ref, other_ref, gain_ref, out_ref, low_ref, half_ref):
    x = x_ref[...] + (own_ref[...] + other_ref[...])
    out_ref[...] = x
    unit = x * rms_scale(x)
    low_ref[...] = (unit * gain_ref[...]).astype(jnp.bfloat16)
    width = half_ref.shape[1]
    half_ref[...] = jnp.where(core_ref[0] == 0, unit[:, :width], unit[:, width:])


def mlp_in(x_rows, own_part, other_part, gain):
    rows, width = x_rows.shape
    block = 128
    core = lax.axis_index("tp").astype(jnp.int32).reshape(1)

    def by_rows(cols):
        return pl.BlockSpec((block, cols), lambda i, ref: (i, 0))

    return pl.pallas_call(
        mlp_in_kernel,
        grid_spec=pltpu.PrefetchScalarGridSpec(
            num_scalar_prefetch=1,
            grid=(rows // block,),
            in_specs=[by_rows(width)] * 3 + [pl.BlockSpec((1, width), lambda i, ref: (0, 0))],
            out_specs=[by_rows(width), by_rows(width), by_rows(width // 2)],
        ),
        out_shape=[
            jax.ShapeDtypeStruct((rows, width), jnp.float32),
            jax.ShapeDtypeStruct((rows, width), jnp.bfloat16),
            jax.ShapeDtypeStruct((rows, width // 2), jnp.float32),
        ],
        compiler_params=ROOMY,
        cost_estimate=NO_COST,
    )(core, x_rows, own_part, other_part, gain.reshape(1, width))


def units_in_halves(
    mlp_low, grad_ref, gate_w_ref, up_w_ref, hidden_ref, gate_ref, up_ref
):
    half = grad_ref.shape[1] // 2
    for at in range(2):
        cols = slice(at * half, (at + 1) * half)
        hidden, gate, up = hidden_parts(
            mlp_low, grad_ref[:, cols], gate_w_ref[:, cols], up_w_ref[:, cols]
        )
        hidden_ref[:, cols] = hidden
        gate_ref[:, cols] = gate
        up_ref[:, cols] = up


def mlp_kernel(
    in_ref, grad_ref, gate_w_ref, up_w_ref, hidden_ref, gate_ref, up_ref, out_ref, total_ref
):
    mlp_low = in_ref[...]
    units_in_halves(
        mlp_low, grad_ref, gate_w_ref, up_w_ref, hidden_ref, gate_ref, up_ref
    )
    part = dot_trans(gate_ref[...], gate_w_ref[...]) + dot_trans(up_ref[...], up_w_ref[...])
    step = pl.program_id(0)

    @pl.when(step == 0)
    def _():
        total_ref[...] = part

    @pl.when(step > 0)
    def _():
        total_ref[...] += part

    @pl.when(step == pl.num_programs(0) - 1)
    def _():
        out_ref[...] = total_ref[...]


def mlp_rows(mlp_low, grad_hidden, w_gate, w_up):
    rows, width = mlp_low.shape
    units = w_gate.shape[1]
    block = 512
    by_units = pl.BlockSpec((rows, block), lambda i: (0, i))
    by_weights = pl.BlockSpec((width, block), lambda i: (0, i))
    whole = pl.BlockSpec((rows, width), lambda i: (0, 0))
    low = jax.ShapeDtypeStruct((rows, units), jnp.bfloat16)
    return pl.pallas_call(
        mlp_kernel,
        grid=(units // block,),
        in_specs=[whole, by_units, by_weights, by_weights],
        out_specs=[by_units, by_units, by_units, whole],
        out_shape=[low, low, low, jax.ShapeDtypeStruct((rows, width), jnp.float32)],
        scratch_shapes=[pltpu.VMEM((rows, width), jnp.float32)],
        compiler_params=ROOMY,
        cost_estimate=NO_COST,
    )(mlp_low, grad_hidden, w_gate, w_up)


def feature_order(width):
    shape = (8 * width, 8 * width)
    row, col = grid_iota(shape, 0), grid_iota(shape, 1)
    return jnp.where(row == (col % 8) * width + col // 8, 1.0, 0.0).astype(jnp.bfloat16)


def patch_in_kernel(core_ref, bytes_ref, weight_ref, wide_ref, out_ref, rows_ref, order_ref):
    places, feature = wide_ref.shape[0], wide_ref.shape[1] // 8
    chunk = weight_ref.shape[1] // 8
    step = pl.program_id(0)

    @pl.when(step == 0)
    def _():
        order_ref[...] = feature_order(chunk)
        for at in range(feature // 128):
            low = at * 128
            rows_ref[at] = bytes_ref[:, low : low + 128].astype(jnp.float32)
            for j in range(8):
                wide_ref[:, j * feature + low : j * feature + low + 128] = rows_ref[
                    at, pl.ds(j, places, stride=8), :
                ]

    parts = [
        wide_ref[:, pl.ds(pl.multiple_of(j * feature + step * chunk, 128), chunk)]
        for j in range(8)
    ]
    by_byte = jnp.concatenate(parts, axis=1).astype(jnp.bfloat16)
    by_feature = dot_plain(by_byte, order_ref[...]).astype(jnp.bfloat16)
    part = dot_trans(by_feature, weight_ref[...])

    @pl.when(step == 0)
    def _():
        out_ref[...] = part

    @pl.when(step > 0)
    def _():
        out_ref[...] += part


def patch_in(byte_rows, w_patch):
    rows, model_width = byte_rows.shape
    out_width, cols = w_patch.shape
    feature, chunk = cols // 8, 128
    core = lax.axis_index("tp").astype(jnp.int32).reshape(1)
    f32 = jnp.float32
    return pl.pallas_call(
        patch_in_kernel,
        grid_spec=pltpu.PrefetchScalarGridSpec(
            num_scalar_prefetch=1,
            grid=(feature // chunk,),
            in_specs=[
                pl.BlockSpec((rows, feature), lambda i, ref: (0, ref[0])),
                pl.BlockSpec((out_width, 8 * chunk), lambda i, ref: (0, i)),
            ],
            out_specs=[
                pl.BlockSpec((rows // 8, cols), lambda i, ref: (0, 0)),
                pl.BlockSpec((rows // 8, out_width), lambda i, ref: (0, 0)),
            ],
            scratch_shapes=[
                pltpu.VMEM((feature // 128, rows, 128), f32),
                pltpu.VMEM((8 * chunk, 8 * chunk), jnp.bfloat16),
            ],
        ),
        out_shape=[
            jax.ShapeDtypeStruct((rows // 8, cols), f32),
            jax.ShapeDtypeStruct((rows // 8, out_width), f32),
        ],
        compiler_params=ROOMY,
        cost_estimate=NO_COST,
    )(core, byte_rows, w_patch)


def final_kernel(
    member_ref,
    own_ref,
    other_ref,
    mask_ref,
    own_head_ref,
    other_head_ref,
    weight_ref,
    low_ref,
    hidden_ref,
    mine_ref,
    mine_low_ref,
):
    own = (own_ref[...] * mask_ref[...]).astype(jnp.bfloat16)
    other = (other_ref[...] * mask_ref[...]).astype(jnp.bfloat16)
    other_head = other_head_ref[...].astype(jnp.bfloat16)
    total = dot_trans(own, own_head_ref[...]) + dot_trans(other, other_head)
    low = total.astype(jnp.bfloat16)
    low_ref[...] = low
    hidden_ref[...] = dot_plain(low, weight_ref[...])

    @pl.when(pl.program_id(0) == 0)
    def _():
        mine_ref[...] = total
        mine_low_ref[...] = low


def final_grads(own, other, mask, own_head, other_head, w_down, member):
    rows, cols = own.shape
    width = own_head.shape[0]
    block = rows // group_size()
    units = w_down.shape[1] // group_size()
    f32, bf16 = jnp.float32, jnp.bfloat16

    def by_rows(cols):
        return pl.BlockSpec((block, cols), lambda i, ref: (i, 0))

    head = pl.BlockSpec((width, cols), lambda i, ref: (0, 0))
    mine = pl.BlockSpec((block, width), lambda i, ref: (0, 0))
    return pl.pallas_call(
        final_kernel,
        grid_spec=pltpu.PrefetchScalarGridSpec(
            num_scalar_prefetch=1,
            grid=(group_size(),),
            in_specs=[by_rows(cols), by_rows(cols), by_rows(1), head, head]
            + [pl.BlockSpec((width, units), lambda i, ref: (0, ref[0]))],
            out_specs=[by_rows(width), by_rows(units), mine, mine],
        ),
        out_shape=[
            jax.ShapeDtypeStruct((rows, width), bf16),
            jax.ShapeDtypeStruct((rows, units), f32),
            jax.ShapeDtypeStruct((block, width), f32),
            jax.ShapeDtypeStruct((block, width), bf16),
        ],
        compiler_params=ROOMY,
        cost_estimate=NO_COST,
    )(member, own, other, mask, own_head, other_head, w_down)


def group_mlp_kernel(
    place_ref,
    own_ref,
    other_ref,
    gain_ref,
    grad_ref,
    gate_w_ref,
    up_w_ref,
    in_ref,
    hidden_ref,
    gate_ref,
    up_ref,
):
    own, other = own_ref[0], other_ref[0]
    first = place_ref[1] == 0
    halves = [jnp.where(first, own, other), jnp.where(first, other, own)]
    low = (jnp.concatenate(halves, axis=1) * gain_ref[...]).astype(jnp.bfloat16)
    in_ref[...] = low
    units_in_halves(low, grad_ref, gate_w_ref, up_w_ref, hidden_ref, gate_ref, up_ref)


def group_mlp(own_half, other_half, gain, grad_hidden, w_gate, w_up, member):
    rows, half = grad_hidden.shape[0] // group_size(), own_half.shape[2]
    width, units = 2 * half, w_gate.shape[1] // group_size()
    bf16 = jnp.bfloat16
    place = jnp.concatenate([member, lax.axis_index("tp").astype(jnp.int32).reshape(1)])

    def by_rows(cols):
        return pl.BlockSpec((rows, cols), lambda i, ref: (i, 0))

    halves = pl.BlockSpec((1, rows, half), lambda i, ref: (i ^ ref[0], 0, 0))
    weights = pl.BlockSpec((width, units), lambda i, ref: (0, ref[0]))
    low = jax.ShapeDtypeStruct((group_size() * rows, units), bf16)
    return pl.pallas_call(
        group_mlp_kernel,
        grid_spec=pltpu.PrefetchScalarGridSpec(
            num_scalar_prefetch=1,
            grid=(group_size(),),
            in_specs=[
                halves,
                halves,
                pl.BlockSpec((1, width), lambda i, ref: (0, 0)),
                by_rows(units),
                weights,
                weights,
            ],
            out_specs=[by_rows(width), by_rows(units), by_rows(units), by_rows(units)],
        ),
        out_shape=[jax.ShapeDtypeStruct((group_size() * rows, width), bf16), low, low, low],
        compiler_params=ROOMY,
        cost_estimate=NO_COST,
    )(place, own_half, other_half, gain.reshape(1, width), grad_hidden, w_gate, w_up)


def bytes_grad_kernel(core_ref, grad_ref, weight_ref, stream_ref, out_ref, order_ref):
    places = grad_ref.shape[0]
    chunk = weight_ref.shape[1] // 8

    @pl.when(pl.program_id(0) == 0)
    def _():
        order_ref[...] = feature_order(chunk)

    by_feature = dot_plain(grad_ref[...].astype(jnp.bfloat16), weight_ref[...])
    high = by_feature.astype(jnp.bfloat16)
    rest = by_feature - high.astype(jnp.float32)
    mid = rest.astype(jnp.bfloat16)
    low = (rest - mid.astype(jnp.float32)).astype(jnp.bfloat16)
    order = order_ref[...]
    by_byte = dot_trans(high, order) + (dot_trans(mid, order) + dot_trans(low, order))
    for j in range(8):
        rows = pl.ds(j, places, stride=8)
        out_ref[rows, :] = stream_ref[rows, :] + by_byte[:, j * chunk : (j + 1) * chunk]


def bytes_grad(grad_patch, w_patch, grad_stream):
    places, width = grad_patch.shape
    rows = grad_stream.shape[0]
    cols = w_patch.shape[1]
    feature, chunk = cols // 8, 128
    core = lax.axis_index("tp").astype(jnp.int32).reshape(1)
    return pl.pallas_call(
        bytes_grad_kernel,
        grid_spec=pltpu.PrefetchScalarGridSpec(
            num_scalar_prefetch=1,
            grid=(feature // chunk,),
            in_specs=[
                pl.BlockSpec((places, width), lambda i, ref: (0, 0)),
                pl.BlockSpec((width, 8 * chunk), lambda i, ref: (0, i)),
                pl.BlockSpec((rows, chunk), lambda i, ref: (0, ref[0] * (feature // chunk) + i)),
            ],
            out_specs=pl.BlockSpec((rows, chunk), lambda i, ref: (0, i)),
            scratch_shapes=[pltpu.VMEM((8 * chunk, 8 * chunk), jnp.bfloat16)],
        ),
        out_shape=jax.ShapeDtypeStruct((rows, feature), jnp.float32),
        compiler_params=ROOMY,
        cost_estimate=NO_COST,
    )(core, grad_patch, w_patch, grad_stream)


def body(
    byte_states,
    lengths,
    w_patch,
    norm_global,
    w_in,
    conv_w,
    conv_b,
    dt_bias,
    a_log,
    d_skip,
    mix_gain,
    w_out,
    norm_attn,
    w_qkv,
    w_o,
    norm_mlp,
    w_gate,
    w_up,
    w_down,
    w_head,
    d_logits,
):
    streams, local_rows, model_width = byte_states.shape
    patch_count = local_rows // 8
    patch_total = streams * patch_count
    row_total = streams * local_rows
    feature = w_patch.shape[1] // 8
    inner_width = w_out.shape[1]
    channels = conv_w.shape[1]
    head_total = dt_bias.shape[0]
    head_cols = w_head.shape[1]
    parts = lax.axis_size("seq")
    tp_index = lax.axis_index("tp")
    seq_index = lax.axis_index("seq")
    places = parts * patch_count
    f32 = jnp.float32

    lanes = parts // streams
    width = inner_width // lanes
    full_head = inner_width // head_total
    own_heads = max(1, width // full_head)
    shared = max(1, full_head // width)
    head_size = width // own_heads
    own_stream = seq_index // lanes
    first_col = (seq_index % lanes) * width
    first_head = first_col // full_head

    seg_full = segment_ids(lengths, places)
    seg_own = lax.dynamic_slice_in_dim(seg_full, seq_index * patch_count, patch_count, 1)
    seg_stream = lax.dynamic_index_in_dim(seg_full, own_stream, 0, keepdims=False)
    valid = (seg_own < lengths.shape[0]).astype(f32).reshape(patch_total, 1)
    byte_valid = jnp.repeat(valid, 8, axis=0)

    member, members = seq_index // QUAD, group_size()
    raw_logits = d_logits.reshape(row_total, head_cols)
    raw_wide = raw_logits.astype(f32)
    group_valid = []
    for apart in range(members):
        device = seq_index ^ QUAD * apart
        group_seg = lax.dynamic_slice_in_dim(seg_full, device * patch_count, patch_count, 1)
        group_valid.append((group_seg < lengths.shape[0]).astype(f32))
    group_valid = jnp.stack(group_valid).reshape(members, patch_total, 1)
    group_bytes_valid = jnp.repeat(group_valid.reshape(-1, 1), 8, axis=0)
    group_raw = jnp.concatenate(
        [raw_wide] + [swap(raw_wide, "seq", QUAD * apart) for apart in range(1, members)], axis=0
    )
    other_raw = swap(group_raw, "tp", 1)
    other_head = swap(w_head.astype(f32), "tp", 1)
    place_index = member.astype(jnp.int32).reshape(1)
    bytes_wide, patch_part = patch_in(byte_states.reshape(row_total, model_width), w_patch)
    patch_out = tp_sum(patch_part)
    gain_global = norm_global.astype(f32)
    unit_patch = patch_out * rms_scale(patch_out)
    u_low = (unit_patch * gain_global).astype(jnp.bfloat16)
    half_width = model_width // 2
    proj = dot_plain(u_low, w_in).reshape(streams, patch_count, -1)
    gate_in = proj[..., :inner_width]
    xbc = proj[..., inner_width : inner_width + channels]
    dt_raw = proj[..., inner_width + channels :]

    def by_lane(columns):
        split = columns.reshape(streams, patch_count, lanes, -1)
        return jnp.moveaxis(split, 2, 1).reshape(parts, patch_count, -1)

    def from_lanes(blocks):
        split = blocks.reshape(streams, lanes, patch_count, -1)
        return jnp.moveaxis(split, 1, 2).reshape(streams, patch_count, -1)

    def to_all_lanes(columns):
        wide = jnp.broadcast_to(
            columns[:, None], (streams, lanes, patch_count, columns.shape[-1])
        )
        return wide.reshape(parts, patch_count, -1)

    pad_width = 128 - own_heads
    dt_lanes = by_lane(jnp.repeat(dt_raw, shared, axis=2))
    sent = jnp.concatenate(
        [
            by_lane(xbc[..., :inner_width]),
            to_all_lanes(xbc[..., inner_width:]),
            jnp.pad(dt_lanes, ((0, 0), (0, 0), (0, pad_width))),
        ],
        axis=-1,
    )
    taken = trade(sent)
    grad_logits = after(raw_logits, sent) * byte_valid.astype(jnp.bfloat16)
    group_final, group_grad_hidden, grad_final, grad_mlp_low = final_grads(
        after(group_raw, sent),
        other_raw,
        group_bytes_valid,
        w_head,
        other_head,
        w_down,
        place_index,
    )
    grad_hidden = dot_plain(grad_mlp_low, w_down)
    hidden_part = w_gate.shape[1] // members

    row_side = [
        [device for device in range(parts) if (device & 1) == side] for side in range(2)
    ]
    bytes_all = lax.all_gather(
        bytes_wide, "seq", axis=0, axis_index_groups=row_side, tiled=True
    )
    taken = after(taken, grad_hidden, group_grad_hidden).reshape(places, -1)
    scan_width = width + channels - inner_width

    def own_cols(param):
        mine = lax.dynamic_slice_in_dim(param, first_col, width, param.ndim - 1)
        return jnp.concatenate([mine, param[..., inner_width:]], axis=-1).astype(f32)

    def own_head(param):
        return lax.dynamic_slice_in_dim(param, first_head, own_heads, 0).astype(f32)

    use_kernel = places == 512 and width == 128
    if use_kernel:
        padded_seg = jnp.pad(seg_stream, (3, 0), constant_values=-1)
        same = jnp.stack(
            [(padded_seg[k : k + places] == seg_stream).astype(f32) for k in range(3)]
            + [jnp.zeros((places,), f32)] * 5,
            axis=1,
        )
        conv_pack = jnp.concatenate(
            [own_cols(conv_w), own_cols(conv_b)[None], jnp.zeros((3, scan_width), f32)]
        )
        head_pack = jnp.stack(
            [jnp.pad(own_head(dt_bias), (0, 128 - own_heads))]
            + [jnp.pad(own_head(a_log), (0, 128 - own_heads))]
            + [jnp.repeat(own_head(d_skip), head_size)]
            + [jnp.zeros((128,), f32)] * 5
        )
        scan_args = (taken, same, conv_pack, head_pack, seg_stream[:, None], seg_stream[None])
        scanned = scan_forward(scan_args, width)
    else:
        scan_args = (
            taken[:, :scan_width],
            taken[:, scan_width : scan_width + own_heads],
            own_cols(conv_w),
            own_cols(conv_b),
            own_head(dt_bias),
            own_head(a_log),
            own_head(d_skip),
        )
        scanned, scan_back = jax.vjp(partial(scan_heads, seg_stream, head_size), *scan_args)
    result = from_lanes(trade(scanned.reshape(parts, patch_count, width)))
    unit_normed, norm_back = jax.vjp(gated_unit, result, gate_in)
    mix_scale = mix_gain.astype(f32)
    normed_low = (unit_normed * mix_scale).reshape(patch_total, -1).astype(jnp.bfloat16)


    def quarters(columns):
        split = columns.reshape(patch_total, members, -1)
        return jnp.moveaxis(split, 1, 0)

    def by_apart(blocks):
        return [
            lax.dynamic_index_in_dim(blocks, member ^ apart, 0, keepdims=False)
            for apart in range(members)
        ]

    def group_swap(blocks):
        return [blocks[0]] + [swap(blocks[k], "seq", QUAD * k) for k in range(1, members)]

    def joined(blocks, turn):
        return jnp.concatenate([after(block, turn) for block in blocks], axis=0)

    early_got = group_swap(
        [
            jnp.concatenate([unit_patch, part], axis=-1)
            for part in by_apart(quarters(unit_normed))
        ]
    )
    global_out = patch_out + valid * tp_sum(dot_trans(normed_low, w_out))
    gain_attn = norm_attn.astype(f32)
    gain_mlp = norm_mlp.astype(f32)
    stream_in, attn_in, qkv, mixed_low, attn_part = attn_forward(
        byte_states.reshape(row_total, model_width), global_out, gain_attn, w_qkv, w_o
    )
    after_attn, mlp_low, unit_half = mlp_in(
        stream_in, attn_part, swap(attn_part, "tp", 1), gain_mlp
    )
    hidden_low, grad_gate_low, grad_up_low, grad_mlp_part = mlp_rows(
        after(mlp_low, unit_half), grad_hidden, w_gate, w_up
    )
    group_halves = group_trade(jnp.broadcast_to(unit_half[None], (members,) + unit_half.shape))
    grad_mlp_other = after(swap(grad_mlp_part, "tp", 1), *early_got[1:])
    after_mlp = after_attn + tp_sum(dot_trans(after(hidden_low, grad_mlp_part), w_down))
    final_low = after_mlp.astype(jnp.bfloat16)
    logits = dot_plain(final_low, w_head) * byte_valid
    grad_mid, grad_attn_low, grad_qkv_low, grad_attn_part, grad_norm_mlp = attn_backward(
        after_attn, grad_final, grad_mlp_part, grad_mlp_other, gain_mlp, qkv, w_qkv, w_o
    )
    grad_norm_mlp = grad_norm_mlp.reshape(-1)
    grad_attn_in = tp_sum(grad_attn_part)

    back_attn, grad_norm_attn = rms_back(stream_in, gain_attn, grad_attn_in)
    grad_stream = grad_mid + back_attn
    grad_global = jnp.sum(grad_stream.reshape(patch_total, 8, model_width), axis=1)
    grad_mix_low = (grad_global * valid).astype(jnp.bfloat16)
    grad_normed = dot_plain(grad_mix_low, w_out).reshape(streams, patch_count, inner_width)
    grad_mix_gain = jnp.sum(grad_normed * unit_normed, axis=(0, 1))
    grad_result, grad_gate_in = norm_back(grad_normed * mix_scale)
    grad_z_low = grad_gate_in.reshape(patch_total, inner_width).astype(jnp.bfloat16)
    row_block = model_width // parts
    dealing = after(by_lane(grad_result), bytes_all, group_halves)
    dealt = trade(dealing)
    late_sent = [
        jnp.concatenate([grad_global, part], axis=-1) for part in by_apart(quarters(grad_gate_in))
    ]
    late_got = group_swap(late_sent)
    attn_cut = 1024 if grad_qkv_low.shape[1] > 1024 else 128
    attn_in_late = after(attn_in, dealing)
    attn_cols = grad_qkv_low.shape[1]
    attn_blocks = (
        grad_blocks([(attn_in_late, grad_qkv_low, 0, attn_cut)], 0, True),
        grad_blocks(
            [
                (attn_in_late, grad_qkv_low, attn_cut, attn_cols),
                (grad_attn_low, mixed_low, 0, mixed_low.shape[1]),
                (final_low, grad_logits, 0, head_cols),
            ],
            1,
            True,
        ),
    )
    attn_got = [to_partner(attn_blocks[first][0], first) for first in range(2)]
    dealt = after(dealt, attn_blocks[0][0], attn_blocks[1][0])
    grad_scanned = dealt.reshape(places, width)
    if use_kernel:
        back_sent, conv_grads, head_grads = scan_backward(scan_args, grad_scanned)
        lane_grad = back_sent[:, : scan_width + own_heads]
        scan_params = (
            conv_grads[:4],
            conv_grads[4],
            head_grads[0, :own_heads],
            head_grads[1, :own_heads],
            head_grads[2, :own_heads],
        )
    else:
        scan_grads = scan_back(grad_scanned)
        back_sent = jnp.concatenate(
            [scan_grads[0], jnp.pad(scan_grads[1], ((0, 0), (0, pad_width)))], axis=-1
        )
        lane_grad = jnp.concatenate([scan_grads[0], scan_grads[1]], axis=-1)
        scan_params = scan_grads[2:]
    back_sent = back_sent.reshape(parts, patch_count, -1)
    back_taken = trade(back_sent)
    own_half = after(group_halves, back_sent)
    group_in, group_hidden, group_gate, group_up = group_mlp(
        own_half, swap(own_half, "tp", 1), gain_mlp, group_grad_hidden, w_gate, w_up, place_index
    )
    attn_far = [
        add_side(after(attn_blocks[first][1], group_hidden), attn_got[first], 1)
        for first in range(2)
    ]
    attn_crossed = [to_partner(attn_far[first], 1 - first) for first in range(2)]
    first_set = grad_blocks(
        [
            (after(group_final, *attn_far), group_hidden, 0, hidden_part),
            (group_in, group_gate, 0, hidden_part),
        ],
        0,
        True,
    )
    late_got = joined(late_got, first_set[0])
    apart_valid = group_valid.reshape(-1, 1)
    group_mix = (late_got[:, :model_width] * apart_valid).astype(jnp.bfloat16)
    group_z = late_got[:, model_width:]
    late_early = joined(early_got, first_set[0])
    group_u = (late_early[:, :model_width] * gain_global).astype(jnp.bfloat16)
    quarter = inner_width // members
    own_scale = lax.dynamic_slice_in_dim(mix_scale, member * quarter, quarter, 0)
    group_n = (late_early[:, model_width:] * own_scale).astype(jnp.bfloat16)
    mlp_blocks = [
        first_set,
        grad_blocks(
            [
                (group_in, group_up, 0, hidden_part),
                (group_mix, group_n, 0, group_n.shape[1]),
                (group_u, group_z, 0, group_z.shape[1]),
            ],
            1,
            True,
        ),
    ]
    mlp_got = [to_partner(mlp_blocks[first][0], first) for first in range(2)]
    back_taken = after(back_taken, mlp_blocks[0][0], mlp_blocks[1][0])
    grad_x = from_lanes(back_taken[..., :width])
    by_stream = back_taken.reshape(streams, lanes, patch_count, -1)
    grad_bc = jnp.sum(by_stream[..., width:scan_width], axis=1)
    grad_dt = from_lanes(back_taken[..., scan_width : scan_width + own_heads])
    grad_dt = jnp.sum(grad_dt.reshape(streams, patch_count, head_total, shared), axis=-1)
    grad_shared = jnp.concatenate([grad_bc, grad_dt], axis=-1).reshape(patch_total, -1)
    grad_proj_low = jnp.concatenate(
        [grad_z_low, grad_x.reshape(patch_total, -1).astype(jnp.bfloat16)]
        + [grad_shared.astype(jnp.bfloat16)],
        axis=-1,
    )
    grad_u_part = dot_trans(grad_proj_low, w_in)
    high = (seq_index // QUAD).astype(jnp.int32).reshape(1)
    attn_near = near_sums(
        [
            (after(attn_blocks[first][1], grad_u_part), attn_got[first], attn_crossed[first])
            for first in range(2)
        ],
        high,
    )
    attn_high = [
        swap(attn_near[apart], "seq", QUAD * apart) for apart in range(1, parts // QUAD)
    ]
    grad_u = tp_sum(grad_u_part)
    rest = [quarters(columns) for columns in (grad_x, grad_bc, grad_dt)]
    rest_cols = [part.shape[-1] for part in rest]
    rest = after(jnp.concatenate(rest, axis=-1), grad_u_part)
    rest = jnp.pad(rest, ((0, 0), (0, 0), (0, -sum(rest_cols) % 128)))
    rest_blocks = grad_blocks(
        [(group_u, joined(group_swap(by_apart(rest)), grad_u_part), 0, rest.shape[-1])], 0, True
    )
    back_global, grad_norm_global = rms_back(patch_out, gain_global, grad_u)
    grad_patch = grad_global + back_global
    side_count = parts // 2
    my_side = seq_index & 1
    by_block = jnp.moveaxis(grad_patch.reshape(patch_total, parts, row_block), 1, 0)
    by_block = by_block.reshape(side_count, 2, patch_total, row_block)
    same_side = lax.dynamic_index_in_dim(by_block, my_side, 1, keepdims=False)
    other_side = lax.dynamic_index_in_dim(by_block, 1 - my_side, 1, keepdims=False)
    patch_rows = jnp.concatenate([same_side, other_side], axis=-1)
    patch_rows = patch_rows.reshape(side_count, patch_total, 2 * row_block)
    gain_part = grad_norm_global.reshape(-1, 2 * row_block)
    gain_count = gain_part.shape[0]
    patch_sent = jnp.concatenate(
        [patch_rows, jnp.broadcast_to(gain_part, (side_count,) + gain_part.shape)], axis=1
    )
    patch_taken = lax.all_to_all(
        patch_sent, "seq", 0, 0, axis_index_groups=row_side, tiled=True
    )

    mlp_far = [
        add_side(after(mlp_blocks[first][1], patch_sent), mlp_got[first], 1)
        for first in range(2)
    ]
    mlp_crossed = [to_partner(mlp_far[first], 1 - first) for first in range(2)]
    patch_taken = after(patch_taken, rest_blocks[0], *mlp_far)
    gain_side = jnp.sum(patch_taken[:, patch_total:], axis=0)
    patch_cols = patch_taken[:, :patch_total].reshape(-1, 2 * row_block)
    patch_far = patch_far_grad(patch_cols, gain_side, bytes_all)
    small = (
        scan_params[0][:, :width],
        scan_params[1][:width],
        scan_params[0][:, width:],
        scan_params[1][width:],
        scan_params[2],
        scan_params[3],
        scan_params[4],
        grad_mix_gain,
        grad_norm_attn,
        grad_norm_mlp,
    )
    small_count = sum(part.size for part in small)
    flat = after(jnp.concatenate([part.reshape(-1) for part in small]), patch_far)
    flat = jnp.pad(flat, (0, -small_count % 1024)).reshape(1, -1, 128)
    pieces = trade(jnp.broadcast_to(flat, (parts,) + flat.shape[1:])).reshape(parts, -1)
    by_small, at = [], 0
    for part in small:
        got = pieces[:, at : at + part.size].reshape((parts,) + part.shape)
        by_small.append(got)
        at += part.size

    def lane_cols(got):
        joined = jnp.sum(got.reshape((streams, lanes) + got.shape[1:]), axis=0)
        return jnp.moveaxis(joined, 0, -2).reshape(joined.shape[1:-1] + (-1,))

    def lane_heads(got):
        joined = jnp.sum(got.reshape(streams, lanes, -1), axis=0)
        return jnp.sum(joined.reshape(head_total, shared), axis=-1)

    small_sums = [
        jnp.concatenate([lane_cols(by_small[0]), jnp.sum(by_small[2], axis=0)], axis=-1),
        jnp.concatenate([lane_cols(by_small[1]), jnp.sum(by_small[3], axis=0)], axis=-1),
        lane_heads(by_small[4]),
        lane_heads(by_small[5]),
        lane_heads(by_small[6]),
    ] + [jnp.sum(got, axis=0) for got in by_small[7:]]

    patch_got = to_partner(patch_far, 0)

    rest_got = to_partner(after(rest_blocks[0], patch_far), 0)
    start = jnp.zeros((1,), jnp.int32)
    final_attn = attn_near[0]
    for got in attn_high:
        final_attn = final_attn + after(got, patch_far)
    mlp_near = [
        near_sums(
            [(after(mlp_blocks[first][1], final_attn, patch_got), mlp_got[first], mlp_crossed[first])],
            start,
        )
        for first in range(2)
    ]
    rest_far = add_side(after(rest_blocks[1], mlp_near[0]), rest_got, 1)
    rest_crossed = to_partner(rest_far, 1)
    rest_near = near_sums(
        [(after(rest_blocks[1], mlp_near[1]), rest_got, rest_crossed)], start
    )
    mlp_finals = [
        jnp.moveaxis(group_trade(part), 0, 1) for part in mlp_near + [rest_near]
    ]
    def final_cols(final, low, count):
        return final[..., low : low + count].reshape(row_block, -1)

    final_down = final_cols(mlp_finals[0], 0, hidden_part)
    final_gate = final_cols(mlp_finals[0], hidden_part, hidden_part)
    final_up = final_cols(mlp_finals[1], 0, hidden_part)
    final_out = final_cols(mlp_finals[1], hidden_part, quarter)
    final_z = final_cols(mlp_finals[1], hidden_part + quarter, quarter)
    final_x = final_cols(mlp_finals[2], 0, rest_cols[0])
    final_bc = final_cols(mlp_finals[2], rest_cols[0], rest_cols[1])
    final_dt = final_cols(mlp_finals[2], rest_cols[0] + rest_cols[1], rest_cols[2])
    final_patch = patch_grad(patch_cols, patch_got, bytes_all)
    norm_global_sum = (gain_side + patch_got[row_block:, : 2 * row_block]).reshape(-1)
    grad_bytes = bytes_grad(after(grad_patch, patch_far), w_patch, grad_stream)
    grad_bytes = grad_bytes.reshape(streams, local_rows, feature)

    qkv_cols, o_cols = w_qkv.shape[1], w_o.shape[1]
    return (
        logits.reshape(streams, local_rows, head_cols),
        grad_bytes,
        final_patch,
        norm_global_sum,
        jnp.concatenate([final_z, final_x, final_bc, final_dt], axis=1),
        small_sums[0],
        small_sums[1],
        small_sums[2],
        small_sums[3],
        small_sums[4],
        small_sums[5],
        final_out,
        small_sums[6],
        final_attn[:, :qkv_cols],
        final_attn[:, qkv_cols : qkv_cols + o_cols],
        small_sums[7],
        final_gate,
        final_up,
        final_down,
        final_attn[:, qkv_cols + o_cols :],
    )


def solution(mesh):
    in_specs = (
        P(None, "seq", None),
        P(),
        P(None, "tp"),
        P(),
        P(None, "tp"),
        P(None, "tp"),
        P("tp"),
        P("tp"),
        P("tp"),
        P("tp"),
        P("tp"),
        P(None, "tp"),
        P(),
        P(None, "tp"),
        P(None, "tp"),
        P(),
        P(None, "tp"),
        P(None, "tp"),
        P(None, "tp"),
        P(None, "tp"),
        P(None, "seq", "tp"),
    )
    out_specs = (
        P(None, "seq", "tp"),
        P(None, "seq", "tp"),
        P("seq", "tp"),
        P(),
        P("seq", "tp"),
        P(None, "tp"),
        P("tp"),
        P("tp"),
        P("tp"),
        P("tp"),
        P("tp"),
        P("seq", "tp"),
        P(),
        P("seq", "tp"),
        P("seq", "tp"),
        P(),
        P("seq", "tp"),
        P("seq", "tp"),
        P("seq", "tp"),
        P("seq", "tp"),
    )
    return jax.shard_map(body, mesh=mesh, in_specs=in_specs, out_specs=out_specs, check_vma=False)
```

```python
from functools import partial

import jax
import jax.numpy as jnp
from jax import lax
from jax.experimental import pallas as pl
from jax.experimental.pallas import tpu as pltpu
from jax.sharding import PartitionSpec as P

NS = 128
AD = 64
QUAD = 4


NO_COST = pl.CostEstimate(flops=1024, bytes_accessed=1024, transcendentals=0)
ROOMY = pltpu.CompilerParams(vmem_limit_bytes=56 * 1024 * 1024)

epsilon = 1e-05
highest = lax.Precision.HIGHEST
masked_score = -1e30


def dot_plain(left_side, right_side):
    return jnp.dot(left_side, right_side, preferred_element_type=jnp.float32)


def dot_trans(left_side, right_side):
    return lax.dot_general(
        left_side, right_side, (((1,), (1,)), ((), ())), preferred_element_type=jnp.float32
    )


def dot_left(left_side, right_side):
    return lax.dot_general(
        left_side, right_side, (((0,), (0,)), ((), ())), preferred_element_type=jnp.float32
    )


def rms_scale(values):
    return lax.rsqrt(jnp.mean(values * values, axis=-1, keepdims=True) + epsilon)


def hidden_parts(mlp_in, grad_hidden, w_gate, w_up):
    gate_proj = dot_plain(mlp_in, w_gate)
    up_proj = dot_plain(mlp_in, w_up)
    sigmoid_gate = jax.nn.sigmoid(gate_proj)
    hidden_low = (gate_proj * sigmoid_gate * up_proj).astype(jnp.bfloat16)
    grad_gate_low = (
        grad_hidden * up_proj * sigmoid_gate * (1.0 + gate_proj * (1.0 - sigmoid_gate))
    ).astype(jnp.bfloat16)
    grad_up_low = (grad_hidden * gate_proj * sigmoid_gate).astype(jnp.bfloat16)
    return (hidden_low, grad_gate_low, grad_up_low)


def rms_back(values, gain_values, grad_out):
    scale = rms_scale(values)
    scaled = gain_values * grad_out
    inner_mean = jnp.mean(values * scaled, axis=-1, keepdims=True)
    grad_values = scale * scaled - values * scale * scale * scale * inner_mean
    grad_gain = jnp.sum(values * scale * grad_out, axis=0)
    return (grad_values, grad_gain)


def swap(block, axis, mask):
    return lax.ppermute(block, axis, [(i, i ^ mask) for i in range(lax.axis_size(axis))])


def after(value, *earlier):
    return lax.optimization_barrier((value,) + earlier)[0]


def tp_sum(block):
    return block + swap(block, "tp", 1)


def to_partner(block, bit):
    return swap(block, "seq", 1 << bit)


def seq_bits():
    return lax.axis_size("seq").bit_length() - 1


def group_size():
    return lax.axis_size("seq") // QUAD


def group_trade(blocks):
    members = [[low + QUAD * high for high in range(group_size())] for low in range(QUAD)]
    return lax.all_to_all(blocks, "seq", 0, 0, axis_index_groups=members, tiled=True)


def add_kernel(index_ref, *refs):
    total = refs[0][...] + refs[1][...]
    refs[2][...] = total.reshape(refs[2].shape)


def add_side(near, got, side):
    unused, groups, rows, cols = near.shape
    index = jnp.zeros((1,), jnp.int32)
    block = pl.BlockSpec((1, 1, rows, cols), lambda i, ref: (side, i, 0, 0))
    return pl.pallas_call(
        add_kernel,
        grid_spec=pltpu.PrefetchScalarGridSpec(
            num_scalar_prefetch=1,
            grid=(groups,),
            in_specs=[block, block],
            out_specs=pl.BlockSpec((1, rows, cols), lambda i, ref: (i, 0, 0)),
        ),
        out_shape=jax.ShapeDtypeStruct((groups, rows, cols), jnp.float32),
        compiler_params=ROOMY,
        cost_estimate=NO_COST,
    )(index, near, got)


def near_kernel(index_ref, *refs):
    out_ref = refs[-1]
    at = 0
    for near_ref, got_ref, crossed_ref in zip(refs[0:-1:3], refs[1:-1:3], refs[2:-1:3]):
        cols = near_ref.shape[3]
        total = near_ref[0, 0] + got_ref[0, 0] + crossed_ref[0]
        out_ref[0, :, at : at + cols] = total
        at += cols


def near_sums(terms, high):
    unused, groups, rows, unused_cols = terms[0][0].shape
    cols = [term[0].shape[3] for term in terms]
    specs, operands = [], []
    for (near, got, crossed), count in zip(terms, cols):
        four = pl.BlockSpec((1, 1, rows, count), lambda i, ref: (0, ref[0] ^ i, 0, 0))
        three = pl.BlockSpec((1, rows, count), lambda i, ref: (ref[0] ^ i, 0, 0))
        specs += [four, four, three]
        operands += [near, got, crossed]
    return pl.pallas_call(
        near_kernel,
        grid_spec=pltpu.PrefetchScalarGridSpec(
            num_scalar_prefetch=1,
            grid=(groups,),
            in_specs=specs,
            out_specs=pl.BlockSpec((1, rows, sum(cols)), lambda i, ref: (i, 0, 0)),
        ),
        out_shape=jax.ShapeDtypeStruct((groups, rows, sum(cols)), jnp.float32),
        compiler_params=ROOMY,
        cost_estimate=NO_COST,
    )(high, *operands)


def grad_blocks_kernel(pairs, first, relative, rows, member_ref, *refs):
    lefts, rights = refs[: len(pairs)], refs[len(pairs) : 2 * len(pairs)]
    far_ref, near_ref = refs[2 * len(pairs) :]
    other = 1 - first
    at = 0
    for left_ref, right_ref, (low, high) in zip(lefts, rights, pairs):
        got = dot_left(left_ref[...], right_ref[:, low:high].astype(jnp.bfloat16))
        places = slice(at, at + high - low)
        for block in range(got.shape[0] // rows):
            place, member = block // QUAD, block % QUAD
            part = got[block * rows : (block + 1) * rows]
            apart = member_ref[0] ^ member
            is_far = apart >> first & 1
            if relative:
                side = apart >> other & 1
            else:
                side = member >> other & 1

            @pl.when(is_far == 1)
            def _():
                if relative:
                    far_ref[side, place, :, places] = part
                else:
                    far_ref[place, side, :, places] = part

            @pl.when(is_far == 0)
            def _():
                if relative:
                    near_ref[side, place, :, places] = part
                else:
                    near_ref[place, side, :, places] = part

        at += high - low


def grad_blocks(terms, first, relative):
    parts = lax.axis_size("seq")
    groups = parts // QUAD
    model_width = terms[0][0].shape[1]
    rows = model_width // parts
    cols = max(128, QUAD * rows)
    places = cols // (QUAD * rows)
    pairs = [(low, high) for unused, unused_right, low, high in terms]
    total = sum(high - low for low, high in pairs)
    member = (lax.axis_index("seq") % QUAD).astype(jnp.int32).reshape(1)
    if relative:
        shape, block = (2, groups, rows, total), (2, places, rows, total)
        out_spec = pl.BlockSpec(block, lambda i, ref: (0, i, 0, 0))
    else:
        shape, block = (groups, 2, rows, total), (places, 2, rows, total)
        out_spec = pl.BlockSpec(block, lambda i, ref: (i, 0, 0, 0))
    out = jax.ShapeDtypeStruct(shape, jnp.float32)
    return pl.pallas_call(
        partial(grad_blocks_kernel, pairs, first, relative, rows),
        grid_spec=pltpu.PrefetchScalarGridSpec(
            num_scalar_prefetch=1,
            grid=(model_width // cols,),
            in_specs=[
                pl.BlockSpec((term[0].shape[0], cols), lambda i, ref: (0, i)) for term in terms
            ]
            + [pl.BlockSpec(term[1].shape, lambda i, ref: (0, 0)) for term in terms],
            out_specs=[out_spec, out_spec],
        ),
        out_shape=[out, out],
        compiler_params=ROOMY,
        cost_estimate=NO_COST,
    )(member, *[term[0] for term in terms], *[term[1] for term in terms])


def segment_ids(lengths, place_count):
    ends = jnp.cumsum(lengths // 8, dtype=jnp.int32)
    places = jnp.arange(place_count, dtype=jnp.int32)
    short_ids = jnp.sum(
        (places[:, None] >= ends[None, :]).astype(jnp.int32), axis=1, dtype=jnp.int32
    )
    return jnp.stack([jnp.zeros_like(short_ids), short_ids])


def scan_heads(seg_now, head_size, xbc, dt_raw, conv_weight, conv_bias, dt_shift, a_logs, skips):
    place_count = xbc.shape[0]
    conv_sum = conv_bias + conv_weight[3] * xbc
    for offset in range(3):
        distance = 3 - offset
        earlier = jnp.pad(xbc, ((distance, 0), (0, 0)))[:place_count]
        seg_earlier = jnp.pad(seg_now, (distance, 0), constant_values=-1)[:place_count]
        same_doc = (seg_earlier == seg_now).astype(jnp.float32)
        conv_sum = conv_sum + conv_weight[offset] * earlier * same_doc[:, None]
    active = jax.nn.silu(conv_sum)
    head_count = dt_raw.shape[1]
    inner = head_count * head_size
    values = active[:, :inner].reshape(place_count, head_count, head_size)
    in_keys = active[:, inner : inner + NS]
    out_keys = active[:, inner + NS :]
    step_sizes = jax.nn.softplus(dt_raw + dt_shift)
    decay_rates = -step_sizes * jnp.exp(a_logs)
    chunk = min(place_count, 512)
    triangle = jnp.tril(jnp.ones((chunk, chunk), jnp.float32))
    state = jnp.zeros((head_count, head_size, NS), jnp.float32)
    seg_last = jnp.int32(-1)
    outputs = []
    for start in range(0, place_count, chunk):
        stop = start + chunk
        x, b, c = values[start:stop], in_keys[start:stop], out_keys[start:stop]
        dt, seg = step_sizes[start:stop], seg_now[start:stop]
        cumulative = jnp.dot(triangle, decay_rates[start:stop], precision=highest)
        allowed = (triangle > 0.0) & (seg[:, None] == seg[None, :])
        ordered = cumulative.T
        gaps = ordered[:, :, None] - ordered[:, None, :]
        decays = jnp.where(allowed, jnp.exp(jnp.where(allowed, gaps, 0.0)), 0.0)
        crossing = jnp.einsum("pn,jn->pj", c, b, precision=highest)
        mixing = crossing[None] * decays * dt.T[:, None, :]
        result = jnp.einsum("hpj,jhd->phd", mixing, x, precision=highest)
        if start > 0:
            entering = jnp.exp(cumulative) * (seg == seg_last).astype(jnp.float32)[:, None]
            result = result + entering[..., None] * jnp.einsum(
                "pn,hdn->phd", c, state, precision=highest
            )
        if stop < place_count:
            last_same = (seg == seg[-1]).astype(jnp.float32)[:, None]
            weight = jnp.exp(cumulative[-1:] - cumulative) * last_same * dt
            through = jnp.exp(cumulative[-1]) * (seg[-1] == seg_last).astype(jnp.float32)
            state = through[:, None, None] * state + jnp.einsum(
                "jh,jhd,jn->hdn", weight, x, b, precision=highest
            )
            seg_last = seg[-1]
        outputs.append(result + skips[:, None] * x)
    return jnp.concatenate(outputs, axis=0).reshape(place_count, inner)


def gated_unit(result, gate_in):
    gated = result * jax.nn.silu(gate_in)
    return gated * rms_scale(gated)


def patch_far_kernel(grad_ref, gain_ref, bytes_ref, out_ref):
    half = grad_ref.shape[1] // 2
    grad_low = grad_ref[:, half:].astype(jnp.bfloat16)
    out_ref[:half] = dot_left(grad_low, bytes_ref[...].astype(jnp.bfloat16))
    out_ref[half:] = jnp.zeros((out_ref.shape[0] - half, out_ref.shape[1]), jnp.float32)

    @pl.when(pl.program_id(0) == 0)
    def _():
        out_ref[half:, : 2 * half] = gain_ref[...]


def patch_far_grad(grad_rows, gain_part, bytes_all):
    places, cols = grad_rows.shape
    total = bytes_all.shape[1]
    rows = cols // 2 + gain_part.shape[0]
    block = 1024
    return pl.pallas_call(
        patch_far_kernel,
        grid=(total // block,),
        in_specs=[
            pl.BlockSpec((places, cols), lambda i: (0, 0)),
            pl.BlockSpec(gain_part.shape, lambda i: (0, 0)),
            pl.BlockSpec((places, block), lambda i: (0, i)),
        ],
        out_specs=pl.BlockSpec((rows, block), lambda i: (0, i)),
        out_shape=jax.ShapeDtypeStruct((rows, total), jnp.float32),
        compiler_params=ROOMY,
        cost_estimate=NO_COST,
    )(grad_rows, gain_part, bytes_all)


def patch_grad_kernel(grad_ref, *refs):
    byte_refs, got_refs, out_ref, order_ref = refs[:8], refs[8:16], refs[16], refs[17]
    width = byte_refs[0].shape[1]

    @pl.when(pl.program_id(0) == 0)
    def _():
        order_ref[...] = feature_order(width)

    grad_low = grad_ref[:, : grad_ref.shape[1] // 2].astype(jnp.bfloat16)
    wide = jnp.concatenate([ref[...].astype(jnp.bfloat16) for ref in byte_refs], axis=1)
    rows = grad_low.shape[1]
    grad = dot_left(grad_low, wide)
    grad = grad + jnp.concatenate([ref[:rows] for ref in got_refs], axis=1)
    high = grad.astype(jnp.bfloat16)
    rest = grad - high.astype(jnp.float32)
    mid = rest.astype(jnp.bfloat16)
    low = (rest - mid.astype(jnp.float32)).astype(jnp.bfloat16)
    order = order_ref[...]
    out_ref[...] = dot_plain(high, order) + (dot_plain(mid, order) + dot_plain(low, order))


def patch_grad(grad_rows, got, bytes_all):
    places, cols = grad_rows.shape
    feature = bytes_all.shape[1] // 8
    chunk = 128
    steps = feature // chunk

    def byte_specs(rows):
        return [
            pl.BlockSpec((rows, chunk), partial(lambda j, i: (0, j * steps + i), j))
            for j in range(8)
        ]

    return pl.pallas_call(
        patch_grad_kernel,
        grid=(steps,),
        in_specs=[pl.BlockSpec((places, cols), lambda i: (0, 0))]
        + byte_specs(places)
        + byte_specs(got.shape[0]),
        out_specs=pl.BlockSpec((cols // 2, 8 * chunk), lambda i: (0, i)),
        out_shape=jax.ShapeDtypeStruct((cols // 2, 8 * feature), jnp.float32),
        scratch_shapes=[pltpu.VMEM((8 * chunk, 8 * chunk), jnp.bfloat16)],
        compiler_params=ROOMY,
        cost_estimate=NO_COST,
    )(grad_rows, *([bytes_all] * 8), *([got] * 8))


def trade(blocks):
    return lax.all_to_all(blocks, "seq", 0, 0, tiled=True)


def grid_iota(shape, axis):
    return lax.broadcasted_iota(jnp.int32, shape, axis)


def dot_fine(left_side, right_side, left_axis, right_axis):
    return lax.dot_general(
        left_side,
        right_side,
        (((left_axis,), (right_axis,)), ((), ())),
        preferred_element_type=jnp.float32,
        precision=highest,
    )


def shifted_down(block, distance):
    rows = grid_iota(block.shape, 0)
    return jnp.where(rows >= distance, pltpu.roll(block, distance, 0), 0.0)


def shifted_up(block, distance):
    count = block.shape[0]
    rows = grid_iota(block.shape, 0)
    return jnp.where(rows < count - distance, pltpu.roll(block, count - distance, 0), 0.0)


def scan_terms(taken_ref, same_ref, conv_ref, head_ref):
    places = taken_ref.shape[0]
    channels = conv_ref.shape[1]
    xbc = taken_ref[:, :channels]
    conv_sum = conv_ref[4:5] + conv_ref[3:4] * xbc
    for k in range(3):
        earlier = shifted_down(xbc, 3 - k) * same_ref[:, k : k + 1]
        conv_sum = conv_sum + conv_ref[k : k + 1] * earlier
    gate = jax.nn.sigmoid(conv_sum)
    active = conv_sum * gate
    raw = taken_ref[:, channels:] + head_ref[0:1]
    steps = jnp.maximum(raw, 0.0) + jnp.log1p(jnp.exp(-jnp.abs(raw)))
    rates = -steps * jnp.exp(head_ref[1:2])
    square = (places, places)
    triangle = jnp.where(grid_iota(square, 0) >= grid_iota(square, 1), 1.0, 0.0)
    running = dot_fine(triangle, rates, 1, 0)
    return xbc, conv_sum, gate, active, raw, steps, rates, triangle, running


def scan_forward_kernel(taken_ref, same_ref, conv_ref, head_ref, seg_col, seg_row, out_ref):
    places, width = out_ref.shape
    terms = scan_terms(taken_ref, same_ref, conv_ref, head_ref)
    active, steps, running = terms[3], terms[5], terms[8]
    values = active[:, :width]
    keys, reads = active[:, width : width + NS], active[:, width + NS :]
    steps_row, running_row = steps.T, running.T
    heads = width // 64
    rows = 128
    for first in range(0, places, rows):
        last = first + rows
        shape = (rows, last)
        allowed = (seg_col[first:last] == seg_row[:, :last]) & (
            grid_iota(shape, 0) + first >= grid_iota(shape, 1)
        )
        crossing = dot_fine(reads[first:last], keys[:last], 1, 1)
        lane = grid_iota((rows, width), 1) // 64
        total = head_ref[2:3] * values[first:last]
        for h in range(heads):
            gaps = running[first:last, h : h + 1] - running_row[h : h + 1, :last]
            decays = jnp.exp(jnp.where(allowed, gaps, masked_score))
            mixing = crossing * decays * steps_row[h : h + 1, :last]
            part = dot_fine(mixing, values[:last], 1, 0)
            total = total + jnp.where(lane == h, part, 0.0)
        out_ref[first:last] = total


def scan_backward_kernel(
    taken_ref,
    same_ref,
    conv_ref,
    head_ref,
    seg_col,
    seg_row,
    grad_ref,
    out_ref,
    conv_grad_ref,
    head_grad_ref,
    values_grad,
    keys_grad,
    reads_grad,
    rows_grad,
    cols_grad,
):
    places, width = values_grad.shape
    terms = scan_terms(taken_ref, same_ref, conv_ref, head_ref)
    xbc, conv_sum, gate, active, raw, steps, rates, triangle, running = terms
    channels = xbc.shape[1]
    values = active[:, :width]
    keys, reads = active[:, width : width + NS], active[:, width + NS :]
    steps_row, running_row = steps.T, running.T
    heads = width // 64
    rows = 128
    grad = grad_ref[...]
    values_grad[...] = head_ref[2:3] * grad
    keys_grad[...] = jnp.zeros_like(keys_grad)
    rows_grad[...] = jnp.zeros_like(rows_grad)
    cols_grad[...] = jnp.zeros_like(cols_grad)
    for first in range(0, places, rows):
        last = first + rows
        shape = (rows, last)
        allowed = (seg_col[first:last] == seg_row[:, :last]) & (
            grid_iota(shape, 0) + first >= grid_iota(shape, 1)
        )
        crossing = dot_fine(reads[first:last], keys[:last], 1, 1)
        crossing_grad = jnp.zeros(shape, jnp.float32)
        grad_rows = grad[first:last]
        lane = grid_iota((rows, width), 1) // 64
        wide_lane = grid_iota((last, width), 1) // 64
        column = grid_iota((rows, 128), 1)
        down = jnp.zeros((rows, 128), jnp.float32)
        for h in range(heads):
            gaps = running[first:last, h : h + 1] - running_row[h : h + 1, :last]
            decays = jnp.exp(jnp.where(allowed, gaps, masked_score))
            step_row = steps_row[h : h + 1, :last]
            weighted = decays * step_row
            mixing = crossing * weighted
            own_grad = jnp.where(lane == h, grad_rows, 0.0)
            mixing_grad = dot_fine(own_grad, values[:last], 1, 1)
            back = dot_fine(mixing, own_grad, 0, 0)
            values_grad[:last] += jnp.where(wide_lane == h, back, 0.0)
            crossing_grad = crossing_grad + mixing_grad * weighted
            step_part = jnp.sum(mixing_grad * crossing * decays, axis=0, keepdims=True)
            gap_part = mixing_grad * mixing
            down = jnp.where(column == h, jnp.sum(gap_part, axis=1, keepdims=True), down)
            cols_grad[h : h + 1, :last] += step_part
            cols_grad[heads + h : heads + h + 1, :last] += step_part * step_row
        rows_grad[first:last] += down
        reads_grad[first:last] = dot_fine(crossing_grad, keys[:last], 1, 0)
        keys_grad[:last] += dot_fine(crossing_grad, reads[first:last], 0, 0)
    turned = cols_grad[...].T
    column = grid_iota(turned.shape, 1)
    step_grad = jnp.where(column < heads, turned, 0.0)
    ended = pltpu.roll(turned, turned.shape[1] - heads, 1)
    running_grad = jnp.where(column < heads, rows_grad[...] - ended, 0.0)
    rates_grad = dot_fine(triangle, running_grad, 0, 0)
    step_grad = step_grad - rates_grad * jnp.exp(head_ref[1:2])
    raw_grad = step_grad * jax.nn.sigmoid(raw)
    out_ref[:, channels:] = raw_grad
    lane = grid_iota((places, width), 1) // 64
    product = jnp.sum(grad * values, axis=0, keepdims=True)
    head_grad_ref[...] = jnp.zeros_like(head_grad_ref)
    head_grad_ref[0:1] = jnp.sum(raw_grad, axis=0, keepdims=True)
    head_grad_ref[1:2] = jnp.sum(rates_grad * rates, axis=0, keepdims=True)
    skip_lane = grid_iota((1, width), 1)
    skip_grad = jnp.zeros((1, width), jnp.float32)
    for h in range(heads):
        own = jnp.sum(jnp.where(skip_lane // 64 == h, product, 0.0), axis=1, keepdims=True)
        skip_grad = jnp.where(skip_lane == h, own, skip_grad)
    head_grad_ref[2:3] = skip_grad
    active_grad = jnp.concatenate([values_grad[...], keys_grad[...], reads_grad[...]], axis=1)
    conv_grad = active_grad * gate * (1.0 + conv_sum * (1.0 - gate))
    back = conv_ref[3:4] * conv_grad
    conv_grad_ref[...] = jnp.zeros_like(conv_grad_ref)
    conv_grad_ref[3:4] = jnp.sum(conv_grad * xbc, axis=0, keepdims=True)
    conv_grad_ref[4:5] = jnp.sum(conv_grad, axis=0, keepdims=True)
    for k in range(3):
        kept = conv_grad * same_ref[:, k : k + 1]
        back = back + conv_ref[k : k + 1] * shifted_up(kept, 3 - k)
        conv_grad_ref[k : k + 1] = jnp.sum(
            kept * shifted_down(xbc, 3 - k), axis=0, keepdims=True
        )
    out_ref[:, :channels] = back


def scan_forward(args, width):
    places = args[0].shape[0]
    return pl.pallas_call(
        scan_forward_kernel,
        out_shape=jax.ShapeDtypeStruct((places, width), jnp.float32),
        compiler_params=ROOMY,
        cost_estimate=NO_COST,
    )(*args)


def scan_backward(args, grad):
    places, width = grad.shape
    channels = args[2].shape[1]
    f32 = jnp.float32
    return pl.pallas_call(
        scan_backward_kernel,
        out_shape=[
            jax.ShapeDtypeStruct((places, channels + 128), f32),
            jax.ShapeDtypeStruct((8, channels), f32),
            jax.ShapeDtypeStruct((8, 128), f32),
        ],
        scratch_shapes=[
            pltpu.VMEM((places, width), f32),
            pltpu.VMEM((places, NS), f32),
            pltpu.VMEM((places, NS), f32),
            pltpu.VMEM((places, 128), f32),
            pltpu.VMEM((128, places), f32),
        ],
        compiler_params=ROOMY,
        cost_estimate=NO_COST,
    )(*args, grad)


def patch_lanes(block):
    shape = (block // 8, 8, block)
    return grid_iota(shape, 0) == grid_iota(shape, 2) // 8


def folded(scores, same_patch):
    split = scores.reshape(same_patch.shape)
    return jnp.sum(jnp.where(same_patch, split, 0.0), axis=0)


def unfolded(rows, same_patch):
    spread = jnp.where(same_patch, rows[None], 0.0)
    return spread.reshape(-1, rows.shape[1]).astype(jnp.bfloat16)


def softmax_rows(scores, causal):
    scores = jnp.where(causal, scores, masked_score)
    top = jnp.max(scores, axis=1, keepdims=True)
    powers = jnp.exp(scores - top)
    return powers / jnp.sum(powers, axis=1, keepdims=True)


def head_places(rows, head_cols, block):
    return [
        (slice(first, first + block), [j * head_cols + pair * 128 for j in range(3)])
        for first in range(0, rows, block)
        for pair in range(head_cols // 128)
    ]


def all_scores(qkv_ref, places, lane, same_patch):
    scores = []
    for rows, (query, key, unused) in places:
        queries = qkv_ref[rows, query : query + 128] * 0.125
        keys = qkv_ref[rows, key : key + 128]
        for h in range(2):
            own = jnp.where(lane == h, queries, 0)
            scores.append(folded(dot_trans(keys, own), same_patch))
    return jnp.stack(scores)


def attn_forward_kernel(
    bytes_ref, patch_ref, gain_ref, qkv_w_ref, o_w_ref, x_ref, a_ref, qkv_ref, o_ref, out_ref
):
    rows = bytes_ref.shape[0]
    spread = jnp.broadcast_to(patch_ref[...][:, None], (rows // 8, 8, patch_ref.shape[1]))
    x = bytes_ref[...].astype(jnp.float32) + spread.reshape(bytes_ref.shape)
    x_ref[...] = x
    attn_in = (x * rms_scale(x) * gain_ref[...]).astype(jnp.bfloat16)
    a_ref[...] = attn_in
    qkv_ref[...] = dot_plain(attn_in, qkv_w_ref[...]).astype(jnp.bfloat16)
    head_cols = o_ref.shape[1]
    block = 128
    same_patch = patch_lanes(block)
    causal = grid_iota((8, block), 0) <= grid_iota((8, block), 1) % 8
    lane = grid_iota((block, 128), 1) // AD
    places = head_places(rows, head_cols, block)
    probs = softmax_rows(all_scores(qkv_ref, places, lane, same_patch), causal)
    for at, (row_place, (query, unused, value)) in enumerate(places):
        values = qkv_ref[row_place, value : value + 128]
        parts = [dot_left(unfolded(probs[2 * at + h], same_patch), values) for h in range(2)]
        total = jnp.where(lane == 0, parts[0], parts[1])
        o_ref[row_place, query : query + 128] = total.astype(jnp.bfloat16)
    out_ref[...] = dot_trans(o_ref[...], o_w_ref[...])


def attn_forward(bytes_rows, patch_rows, gain, w_qkv, w_o):
    rows, width = bytes_rows.shape
    block = 256
    cols, head_cols = w_qkv.shape[1], w_o.shape[1]
    f32, bf16 = jnp.float32, jnp.bfloat16

    def by_rows(cols):
        return pl.BlockSpec((block, cols), lambda i: (i, 0))

    def whole(shape):
        return pl.BlockSpec(shape, lambda i: (0, 0))

    return pl.pallas_call(
        attn_forward_kernel,
        grid=(rows // block,),
        in_specs=[
            by_rows(width),
            pl.BlockSpec((block // 8, width), lambda i: (i, 0)),
            whole((1, width)),
            whole(w_qkv.shape),
            whole(w_o.shape),
        ],
        out_specs=[by_rows(width), by_rows(width), by_rows(cols), by_rows(head_cols), by_rows(width)],
        out_shape=[
            jax.ShapeDtypeStruct((rows, width), f32),
            jax.ShapeDtypeStruct((rows, width), bf16),
            jax.ShapeDtypeStruct((rows, cols), bf16),
            jax.ShapeDtypeStruct((rows, head_cols), bf16),
            jax.ShapeDtypeStruct((rows, width), f32),
        ],
        compiler_params=ROOMY,
        cost_estimate=NO_COST,
    )(bytes_rows, patch_rows, gain.reshape(1, width), w_qkv, w_o)


def attn_backward_kernel(
    x_ref,
    final_ref,
    own_ref,
    other_ref,
    gain_ref,
    qkv_ref,
    qkv_w_ref,
    o_w_ref,
    mid_ref,
    low_ref,
    qkv_grad_ref,
    out_ref,
    gain_grad_ref,
):
    rows = x_ref.shape[0]
    back, gain_grad = rms_back(x_ref[...], gain_ref[...], own_ref[...] + other_ref[...])
    mid = final_ref[...] + back
    mid_ref[...] = mid
    low_ref[...] = mid.astype(jnp.bfloat16)
    gain_grad = gain_grad.reshape(1, -1)

    @pl.when(pl.program_id(0) == 0)
    def _():
        gain_grad_ref[...] = gain_grad

    @pl.when(pl.program_id(0) > 0)
    def _():
        gain_grad_ref[...] += gain_grad

    mixed_grad = dot_plain(low_ref[...], o_w_ref[...]).astype(jnp.bfloat16)
    head_cols = mixed_grad.shape[1]
    block = 128
    same_patch = patch_lanes(block)
    causal = grid_iota((8, block), 0) <= grid_iota((8, block), 1) % 8
    lane = grid_iota((block, 128), 1) // AD
    places = head_places(rows, head_cols, block)
    probs = softmax_rows(all_scores(qkv_ref, places, lane, same_patch), causal)
    probs_grads = []
    for row_place, (query, unused, value) in places:
        values = qkv_ref[row_place, value : value + 128]
        out_grad = mixed_grad[row_place, query : query + 128]
        for h in range(2):
            own_grad = jnp.where(lane == h, out_grad, 0)
            probs_grads.append(folded(dot_trans(values, own_grad), same_patch))
    probs_grad = jnp.stack(probs_grads)
    inner = jnp.sum(probs * probs_grad, axis=1, keepdims=True)
    scores_grad = probs * (probs_grad - inner)
    for at, (row_place, cols) in enumerate(places):
        query, key, unused = cols
        queries = qkv_ref[row_place, query : query + 128]
        keys = qkv_ref[row_place, key : key + 128]
        out_grad = mixed_grad[row_place, query : query + 128]
        parts = []
        for h in range(2):
            own_scores = unfolded(scores_grad[2 * at + h], same_patch)
            parts.append(
                (
                    dot_left(own_scores, keys) * 0.125,
                    dot_plain(own_scores, queries) * 0.125,
                    dot_plain(unfolded(probs[2 * at + h], same_patch), out_grad),
                )
            )
        for j in range(3):
            grad = jnp.where(lane == 0, parts[0][j], parts[1][j])
            qkv_grad_ref[row_place, cols[j] : cols[j] + 128] = grad.astype(jnp.bfloat16)
    out_ref[...] = dot_trans(qkv_grad_ref[...], qkv_w_ref[...])


def attn_backward(x_rows, final_grad, own_part, other_part, gain, qkv, w_qkv, w_o):
    rows, width = x_rows.shape
    block = 256
    cols = w_qkv.shape[1]
    f32, bf16 = jnp.float32, jnp.bfloat16

    def by_rows(cols):
        return pl.BlockSpec((block, cols), lambda i: (i, 0))

    def whole(shape):
        return pl.BlockSpec(shape, lambda i: (0, 0))

    return pl.pallas_call(
        attn_backward_kernel,
        grid=(rows // block,),
        in_specs=[by_rows(width)] * 4
        + [whole((1, width)), by_rows(cols), whole(w_qkv.shape), whole(w_o.shape)],
        out_specs=[
            by_rows(width),
            by_rows(width),
            by_rows(cols),
            by_rows(width),
            whole((1, width)),
        ],
        out_shape=[
            jax.ShapeDtypeStruct((rows, width), f32),
            jax.ShapeDtypeStruct((rows, width), bf16),
            jax.ShapeDtypeStruct((rows, cols), bf16),
            jax.ShapeDtypeStruct((rows, width), f32),
            jax.ShapeDtypeStruct((1, width), f32),
        ],
        compiler_params=ROOMY,
        cost_estimate=NO_COST,
    )(x_rows, final_grad, own_part, other_part, gain.reshape(1, width), qkv, w_qkv, w_o)


def mlp_in_kernel(core_ref, x_ref, own_ref, other_ref, gain_ref, out_ref, low_ref, half_ref):
    x = x_ref[...] + (own_ref[...] + other_ref[...])
    out_ref[...] = x
    unit = x * rms_scale(x)
    low_ref[...] = (unit * gain_ref[...]).astype(jnp.bfloat16)
    width = half_ref.shape[1]
    half_ref[...] = jnp.where(core_ref[0] == 0, unit[:, :width], unit[:, width:])


def mlp_in(x_rows, own_part, other_part, gain):
    rows, width = x_rows.shape
    block = 128
    core = lax.axis_index("tp").astype(jnp.int32).reshape(1)

    def by_rows(cols):
        return pl.BlockSpec((block, cols), lambda i, ref: (i, 0))

    return pl.pallas_call(
        mlp_in_kernel,
        grid_spec=pltpu.PrefetchScalarGridSpec(
            num_scalar_prefetch=1,
            grid=(rows // block,),
            in_specs=[by_rows(width)] * 3 + [pl.BlockSpec((1, width), lambda i, ref: (0, 0))],
            out_specs=[by_rows(width), by_rows(width), by_rows(width // 2)],
        ),
        out_shape=[
            jax.ShapeDtypeStruct((rows, width), jnp.float32),
            jax.ShapeDtypeStruct((rows, width), jnp.bfloat16),
            jax.ShapeDtypeStruct((rows, width // 2), jnp.float32),
        ],
        compiler_params=ROOMY,
        cost_estimate=NO_COST,
    )(core, x_rows, own_part, other_part, gain.reshape(1, width))


def units_in_halves(
    mlp_low, grad_ref, gate_w_ref, up_w_ref, hidden_ref, gate_ref, up_ref
):
    half = grad_ref.shape[1] // 2
    for at in range(2):
        cols = slice(at * half, (at + 1) * half)
        hidden, gate, up = hidden_parts(
            mlp_low, grad_ref[:, cols], gate_w_ref[:, cols], up_w_ref[:, cols]
        )
        hidden_ref[:, cols] = hidden
        gate_ref[:, cols] = gate
        up_ref[:, cols] = up


def mlp_kernel(
    in_ref, grad_ref, gate_w_ref, up_w_ref, hidden_ref, gate_ref, up_ref, out_ref, total_ref
):
    mlp_low = in_ref[...]
    units_in_halves(
        mlp_low, grad_ref, gate_w_ref, up_w_ref, hidden_ref, gate_ref, up_ref
    )
    part = dot_trans(gate_ref[...], gate_w_ref[...]) + dot_trans(up_ref[...], up_w_ref[...])
    step = pl.program_id(0)

    @pl.when(step == 0)
    def _():
        total_ref[...] = part

    @pl.when(step > 0)
    def _():
        total_ref[...] += part

    @pl.when(step == pl.num_programs(0) - 1)
    def _():
        out_ref[...] = total_ref[...]


def mlp_rows(mlp_low, grad_hidden, w_gate, w_up):
    rows, width = mlp_low.shape
    units = w_gate.shape[1]
    block = 512
    by_units = pl.BlockSpec((rows, block), lambda i: (0, i))
    by_weights = pl.BlockSpec((width, block), lambda i: (0, i))
    whole = pl.BlockSpec((rows, width), lambda i: (0, 0))
    low = jax.ShapeDtypeStruct((rows, units), jnp.bfloat16)
    return pl.pallas_call(
        mlp_kernel,
        grid=(units // block,),
        in_specs=[whole, by_units, by_weights, by_weights],
        out_specs=[by_units, by_units, by_units, whole],
        out_shape=[low, low, low, jax.ShapeDtypeStruct((rows, width), jnp.float32)],
        scratch_shapes=[pltpu.VMEM((rows, width), jnp.float32)],
        compiler_params=ROOMY,
        cost_estimate=NO_COST,
    )(mlp_low, grad_hidden, w_gate, w_up)


def feature_order(width):
    shape = (8 * width, 8 * width)
    row, col = grid_iota(shape, 0), grid_iota(shape, 1)
    return jnp.where(row == (col % 8) * width + col // 8, 1.0, 0.0).astype(jnp.bfloat16)


def patch_in_kernel(core_ref, bytes_ref, weight_ref, wide_ref, out_ref, rows_ref, order_ref):
    places, feature = wide_ref.shape[0], wide_ref.shape[1] // 8
    chunk = weight_ref.shape[1] // 8
    step = pl.program_id(0)

    @pl.when(step == 0)
    def _():
        order_ref[...] = feature_order(chunk)
        for at in range(feature // 128):
            low = at * 128
            rows_ref[at] = bytes_ref[:, low : low + 128].astype(jnp.float32)
            for j in range(8):
                wide_ref[:, j * feature + low : j * feature + low + 128] = rows_ref[
                    at, pl.ds(j, places, stride=8), :
                ]

    parts = [
        wide_ref[:, pl.ds(pl.multiple_of(j * feature + step * chunk, 128), chunk)]
        for j in range(8)
    ]
    by_byte = jnp.concatenate(parts, axis=1).astype(jnp.bfloat16)
    by_feature = dot_plain(by_byte, order_ref[...]).astype(jnp.bfloat16)
    part = dot_trans(by_feature, weight_ref[...])

    @pl.when(step == 0)
    def _():
        out_ref[...] = part

    @pl.when(step > 0)
    def _():
        out_ref[...] += part


def patch_in(byte_rows, w_patch):
    rows, model_width = byte_rows.shape
    out_width, cols = w_patch.shape
    feature, chunk = cols // 8, 128
    core = lax.axis_index("tp").astype(jnp.int32).reshape(1)
    f32 = jnp.float32
    return pl.pallas_call(
        patch_in_kernel,
        grid_spec=pltpu.PrefetchScalarGridSpec(
            num_scalar_prefetch=1,
            grid=(feature // chunk,),
            in_specs=[
                pl.BlockSpec((rows, feature), lambda i, ref: (0, ref[0])),
                pl.BlockSpec((out_width, 8 * chunk), lambda i, ref: (0, i)),
            ],
            out_specs=[
                pl.BlockSpec((rows // 8, cols), lambda i, ref: (0, 0)),
                pl.BlockSpec((rows // 8, out_width), lambda i, ref: (0, 0)),
            ],
            scratch_shapes=[
                pltpu.VMEM((feature // 128, rows, 128), f32),
                pltpu.VMEM((8 * chunk, 8 * chunk), jnp.bfloat16),
            ],
        ),
        out_shape=[
            jax.ShapeDtypeStruct((rows // 8, cols), f32),
            jax.ShapeDtypeStruct((rows // 8, out_width), f32),
        ],
        compiler_params=ROOMY,
        cost_estimate=NO_COST,
    )(core, byte_rows, w_patch)


def final_kernel(
    member_ref,
    own_ref,
    other_ref,
    mask_ref,
    own_head_ref,
    other_head_ref,
    weight_ref,
    low_ref,
    hidden_ref,
    mine_ref,
    mine_low_ref,
):
    own = (own_ref[...] * mask_ref[...]).astype(jnp.bfloat16)
    other = (other_ref[...] * mask_ref[...]).astype(jnp.bfloat16)
    other_head = other_head_ref[...].astype(jnp.bfloat16)
    total = dot_trans(own, own_head_ref[...]) + dot_trans(other, other_head)
    low = total.astype(jnp.bfloat16)
    low_ref[...] = low
    hidden_ref[...] = dot_plain(low, weight_ref[...])

    @pl.when(pl.program_id(0) == 0)
    def _():
        mine_ref[...] = total
        mine_low_ref[...] = low


def final_grads(own, other, mask, own_head, other_head, w_down, member):
    rows, cols = own.shape
    width = own_head.shape[0]
    block = rows // group_size()
    units = w_down.shape[1] // group_size()
    f32, bf16 = jnp.float32, jnp.bfloat16

    def by_rows(cols):
        return pl.BlockSpec((block, cols), lambda i, ref: (i, 0))

    head = pl.BlockSpec((width, cols), lambda i, ref: (0, 0))
    mine = pl.BlockSpec((block, width), lambda i, ref: (0, 0))
    return pl.pallas_call(
        final_kernel,
        grid_spec=pltpu.PrefetchScalarGridSpec(
            num_scalar_prefetch=1,
            grid=(group_size(),),
            in_specs=[by_rows(cols), by_rows(cols), by_rows(1), head, head]
            + [pl.BlockSpec((width, units), lambda i, ref: (0, ref[0]))],
            out_specs=[by_rows(width), by_rows(units), mine, mine],
        ),
        out_shape=[
            jax.ShapeDtypeStruct((rows, width), bf16),
            jax.ShapeDtypeStruct((rows, units), f32),
            jax.ShapeDtypeStruct((block, width), f32),
            jax.ShapeDtypeStruct((block, width), bf16),
        ],
        compiler_params=ROOMY,
        cost_estimate=NO_COST,
    )(member, own, other, mask, own_head, other_head, w_down)


def group_mlp_kernel(
    place_ref,
    own_ref,
    other_ref,
    gain_ref,
    grad_ref,
    gate_w_ref,
    up_w_ref,
    in_ref,
    hidden_ref,
    gate_ref,
    up_ref,
):
    own, other = own_ref[0], other_ref[0]
    first = place_ref[1] == 0
    halves = [jnp.where(first, own, other), jnp.where(first, other, own)]
    low = (jnp.concatenate(halves, axis=1) * gain_ref[...]).astype(jnp.bfloat16)
    in_ref[...] = low
    units_in_halves(low, grad_ref, gate_w_ref, up_w_ref, hidden_ref, gate_ref, up_ref)


def group_mlp(own_half, other_half, gain, grad_hidden, w_gate, w_up, member):
    rows, half = grad_hidden.shape[0] // group_size(), own_half.shape[2]
    width, units = 2 * half, w_gate.shape[1] // group_size()
    bf16 = jnp.bfloat16
    place = jnp.concatenate([member, lax.axis_index("tp").astype(jnp.int32).reshape(1)])

    def by_rows(cols):
        return pl.BlockSpec((rows, cols), lambda i, ref: (i, 0))

    halves = pl.BlockSpec((1, rows, half), lambda i, ref: (i ^ ref[0], 0, 0))
    weights = pl.BlockSpec((width, units), lambda i, ref: (0, ref[0]))
    low = jax.ShapeDtypeStruct((group_size() * rows, units), bf16)
    return pl.pallas_call(
        group_mlp_kernel,
        grid_spec=pltpu.PrefetchScalarGridSpec(
            num_scalar_prefetch=1,
            grid=(group_size(),),
            in_specs=[
                halves,
                halves,
                pl.BlockSpec((1, width), lambda i, ref: (0, 0)),
                by_rows(units),
                weights,
                weights,
            ],
            out_specs=[by_rows(width), by_rows(units), by_rows(units), by_rows(units)],
        ),
        out_shape=[jax.ShapeDtypeStruct((group_size() * rows, width), bf16), low, low, low],
        compiler_params=ROOMY,
        cost_estimate=NO_COST,
    )(place, own_half, other_half, gain.reshape(1, width), grad_hidden, w_gate, w_up)


def bytes_grad_kernel(core_ref, grad_ref, weight_ref, stream_ref, out_ref, order_ref):
    places = grad_ref.shape[0]
    chunk = weight_ref.shape[1] // 8

    @pl.when(pl.program_id(0) == 0)
    def _():
        order_ref[...] = feature_order(chunk)

    by_feature = dot_plain(grad_ref[...].astype(jnp.bfloat16), weight_ref[...])
    high = by_feature.astype(jnp.bfloat16)
    rest = by_feature - high.astype(jnp.float32)
    mid = rest.astype(jnp.bfloat16)
    low = (rest - mid.astype(jnp.float32)).astype(jnp.bfloat16)
    order = order_ref[...]
    by_byte = dot_trans(high, order) + (dot_trans(mid, order) + dot_trans(low, order))
    for j in range(8):
        rows = pl.ds(j, places, stride=8)
        out_ref[rows, :] = stream_ref[rows, :] + by_byte[:, j * chunk : (j + 1) * chunk]


def bytes_grad(grad_patch, w_patch, grad_stream):
    places, width = grad_patch.shape
    rows = grad_stream.shape[0]
    cols = w_patch.shape[1]
    feature, chunk = cols // 8, 128
    core = lax.axis_index("tp").astype(jnp.int32).reshape(1)
    return pl.pallas_call(
        bytes_grad_kernel,
        grid_spec=pltpu.PrefetchScalarGridSpec(
            num_scalar_prefetch=1,
            grid=(feature // chunk,),
            in_specs=[
                pl.BlockSpec((places, width), lambda i, ref: (0, 0)),
                pl.BlockSpec((width, 8 * chunk), lambda i, ref: (0, i)),
                pl.BlockSpec((rows, chunk), lambda i, ref: (0, ref[0] * (feature // chunk) + i)),
            ],
            out_specs=pl.BlockSpec((rows, chunk), lambda i, ref: (0, i)),
            scratch_shapes=[pltpu.VMEM((8 * chunk, 8 * chunk), jnp.bfloat16)],
        ),
        out_shape=jax.ShapeDtypeStruct((rows, feature), jnp.float32),
        compiler_params=ROOMY,
        cost_estimate=NO_COST,
    )(core, grad_patch, w_patch, grad_stream)


def body(
    byte_states,
    lengths,
    w_patch,
    norm_global,
    w_in,
    conv_w,
    conv_b,
    dt_bias,
    a_log,
    d_skip,
    mix_gain,
    w_out,
    norm_attn,
    w_qkv,
    w_o,
    norm_mlp,
    w_gate,
    w_up,
    w_down,
    w_head,
    d_logits,
):
    streams, local_rows, model_width = byte_states.shape
    patch_count = local_rows // 8
    patch_total = streams * patch_count
    row_total = streams * local_rows
    feature = w_patch.shape[1] // 8
    inner_width = w_out.shape[1]
    channels = conv_w.shape[1]
    head_total = dt_bias.shape[0]
    head_cols = w_head.shape[1]
    parts = lax.axis_size("seq")
    tp_index = lax.axis_index("tp")
    seq_index = lax.axis_index("seq")
    places = parts * patch_count
    f32 = jnp.float32

    lanes = parts // streams
    width = inner_width // lanes
    full_head = inner_width // head_total
    own_heads = max(1, width // full_head)
    shared = max(1, full_head // width)
    head_size = width // own_heads
    own_stream = seq_index // lanes
    first_col = (seq_index % lanes) * width
    first_head = first_col // full_head

    seg_full = segment_ids(lengths, places)
    seg_own = lax.dynamic_slice_in_dim(seg_full, seq_index * patch_count, patch_count, 1)
    seg_stream = lax.dynamic_index_in_dim(seg_full, own_stream, 0, keepdims=False)
    valid = (seg_own < lengths.shape[0]).astype(f32).reshape(patch_total, 1)
    byte_valid = jnp.repeat(valid, 8, axis=0)

    member, members = seq_index // QUAD, group_size()
    raw_logits = d_logits.reshape(row_total, head_cols)
    raw_wide = raw_logits.astype(f32)
    group_valid = []
    for apart in range(members):
        device = seq_index ^ QUAD * apart
        group_seg = lax.dynamic_slice_in_dim(seg_full, device * patch_count, patch_count, 1)
        group_valid.append((group_seg < lengths.shape[0]).astype(f32))
    group_valid = jnp.stack(group_valid).reshape(members, patch_total, 1)
    group_bytes_valid = jnp.repeat(group_valid.reshape(-1, 1), 8, axis=0)
    apart_raw = [swap(raw_wide, "seq", QUAD * apart) for apart in range(1, members)]
    other_head = swap(w_head.astype(f32), "tp", 1)
    place_index = member.astype(jnp.int32).reshape(1)
    bytes_wide, patch_part = patch_in(byte_states.reshape(row_total, model_width), w_patch)
    patch_out = tp_sum(patch_part)
    gain_global = norm_global.astype(f32)
    unit_patch = patch_out * rms_scale(patch_out)
    u_low = (unit_patch * gain_global).astype(jnp.bfloat16)
    half_width = model_width // 2
    proj = dot_plain(u_low, w_in).reshape(streams, patch_count, -1)
    gate_in = proj[..., :inner_width]
    xbc = proj[..., inner_width : inner_width + channels]
    dt_raw = proj[..., inner_width + channels :]

    def by_lane(columns):
        split = columns.reshape(streams, patch_count, lanes, -1)
        return jnp.moveaxis(split, 2, 1).reshape(parts, patch_count, -1)

    def from_lanes(blocks):
        split = blocks.reshape(streams, lanes, patch_count, -1)
        return jnp.moveaxis(split, 1, 2).reshape(streams, patch_count, -1)

    def to_all_lanes(columns):
        wide = jnp.broadcast_to(
            columns[:, None], (streams, lanes, patch_count, columns.shape[-1])
        )
        return wide.reshape(parts, patch_count, -1)

    pad_width = 128 - own_heads
    dt_lanes = by_lane(jnp.repeat(dt_raw, shared, axis=2))
    sent = jnp.concatenate(
        [
            by_lane(xbc[..., :inner_width]),
            to_all_lanes(xbc[..., inner_width:]),
            jnp.pad(dt_lanes, ((0, 0), (0, 0), (0, pad_width))),
        ],
        axis=-1,
    )
    taken = trade(sent)
    row_side = [
        [device for device in range(parts) if (device & 1) == side] for side in range(2)
    ]
    bytes_all = lax.all_gather(
        bytes_wide, "seq", axis=0, axis_index_groups=row_side, tiled=True
    )
    taken = after(taken, bytes_wide).reshape(places, -1)
    scan_width = width + channels - inner_width

    def own_cols(param):
        mine = lax.dynamic_slice_in_dim(param, first_col, width, param.ndim - 1)
        return jnp.concatenate([mine, param[..., inner_width:]], axis=-1).astype(f32)

    def own_head(param):
        return lax.dynamic_slice_in_dim(param, first_head, own_heads, 0).astype(f32)

    use_kernel = places == 512 and width == 128
    if use_kernel:
        padded_seg = jnp.pad(seg_stream, (3, 0), constant_values=-1)
        same = jnp.stack(
            [(padded_seg[k : k + places] == seg_stream).astype(f32) for k in range(3)]
            + [jnp.zeros((places,), f32)] * 5,
            axis=1,
        )
        conv_pack = jnp.concatenate(
            [own_cols(conv_w), own_cols(conv_b)[None], jnp.zeros((3, scan_width), f32)]
        )
        head_pack = jnp.stack(
            [jnp.pad(own_head(dt_bias), (0, 128 - own_heads))]
            + [jnp.pad(own_head(a_log), (0, 128 - own_heads))]
            + [jnp.repeat(own_head(d_skip), head_size)]
            + [jnp.zeros((128,), f32)] * 5
        )
        scan_args = (taken, same, conv_pack, head_pack, seg_stream[:, None], seg_stream[None])
        scanned = scan_forward(scan_args, width)
    else:
        scan_args = (
            taken[:, :scan_width],
            taken[:, scan_width : scan_width + own_heads],
            own_cols(conv_w),
            own_cols(conv_b),
            own_head(dt_bias),
            own_head(a_log),
            own_head(d_skip),
        )
        scanned, scan_back = jax.vjp(partial(scan_heads, seg_stream, head_size), *scan_args)
    result = trade(scanned.reshape(parts, patch_count, width))
    group_raw = jnp.concatenate(
        [raw_wide] + [after(raw, scanned) for raw in apart_raw], axis=0
    )
    other_raw = swap(group_raw, "tp", 1)
    grad_logits = raw_logits * byte_valid.astype(jnp.bfloat16)
    group_final, group_grad_hidden, grad_final, grad_mlp_low = final_grads(
        group_raw,
        other_raw,
        group_bytes_valid,
        w_head,
        other_head,
        w_down,
        place_index,
    )
    grad_hidden = dot_plain(grad_mlp_low, w_down)
    hidden_part = w_gate.shape[1] // members

    result = from_lanes(after(result, group_grad_hidden, grad_hidden))
    unit_normed, norm_back = jax.vjp(gated_unit, result, gate_in)
    mix_scale = mix_gain.astype(f32)
    normed_low = (unit_normed * mix_scale).reshape(patch_total, -1).astype(jnp.bfloat16)


    def quarters(columns):
        split = columns.reshape(patch_total, members, -1)
        return jnp.moveaxis(split, 1, 0)

    def by_apart(blocks):
        return [
            lax.dynamic_index_in_dim(blocks, member ^ apart, 0, keepdims=False)
            for apart in range(members)
        ]

    def group_swap(blocks):
        return [blocks[0]] + [swap(blocks[k], "seq", QUAD * k) for k in range(1, members)]

    def joined(blocks, turn):
        return jnp.concatenate([after(block, turn) for block in blocks], axis=0)

    early_got = group_swap(
        [
            jnp.concatenate([unit_patch, part], axis=-1)
            for part in by_apart(quarters(unit_normed))
        ]
    )
    global_out = patch_out + valid * tp_sum(dot_trans(normed_low, w_out))
    gain_attn = norm_attn.astype(f32)
    gain_mlp = norm_mlp.astype(f32)
    stream_in, attn_in, qkv, mixed_low, attn_part = attn_forward(
        byte_states.reshape(row_total, model_width), global_out, gain_attn, w_qkv, w_o
    )
    after_attn, mlp_low, unit_half = mlp_in(
        stream_in, attn_part, swap(attn_part, "tp", 1), gain_mlp
    )
    hidden_low, grad_gate_low, grad_up_low, grad_mlp_part = mlp_rows(
        after(mlp_low, unit_half), grad_hidden, w_gate, w_up
    )
    group_halves = group_trade(jnp.broadcast_to(unit_half[None], (members,) + unit_half.shape))
    grad_mlp_other = swap(grad_mlp_part, "tp", 1)
    after_mlp = after_attn + tp_sum(dot_trans(after(hidden_low, grad_mlp_part), w_down))
    final_low = after_mlp.astype(jnp.bfloat16)
    logits = dot_plain(final_low, w_head) * byte_valid
    grad_mid, grad_attn_low, grad_qkv_low, grad_attn_part, grad_norm_mlp = attn_backward(
        after_attn, grad_final, grad_mlp_part, grad_mlp_other, gain_mlp, qkv, w_qkv, w_o
    )
    grad_norm_mlp = grad_norm_mlp.reshape(-1)
    grad_attn_in = tp_sum(grad_attn_part)

    back_attn, grad_norm_attn = rms_back(stream_in, gain_attn, grad_attn_in)
    grad_stream = grad_mid + back_attn
    grad_global = jnp.sum(grad_stream.reshape(patch_total, 8, model_width), axis=1)
    grad_mix_low = (grad_global * valid).astype(jnp.bfloat16)
    grad_normed = dot_plain(grad_mix_low, w_out).reshape(streams, patch_count, inner_width)
    grad_mix_gain = jnp.sum(grad_normed * unit_normed, axis=(0, 1))
    grad_result, grad_gate_in = norm_back(grad_normed * mix_scale)
    grad_z_low = grad_gate_in.reshape(patch_total, inner_width).astype(jnp.bfloat16)
    row_block = model_width // parts
    dealing = after(by_lane(grad_result), bytes_all, group_halves)
    dealt = trade(dealing)
    late_sent = [
        jnp.concatenate([grad_global, part], axis=-1) for part in by_apart(quarters(grad_gate_in))
    ]
    late_got = group_swap(late_sent)
    attn_cut = 1024 if grad_qkv_low.shape[1] > 1024 else 128
    attn_in_late = after(attn_in, dealing)
    attn_cols = grad_qkv_low.shape[1]
    attn_blocks = (
        grad_blocks([(attn_in_late, grad_qkv_low, 0, attn_cut)], 0, True),
        grad_blocks(
            [
                (attn_in_late, grad_qkv_low, attn_cut, attn_cols),
                (grad_attn_low, mixed_low, 0, mixed_low.shape[1]),
                (final_low, grad_logits, 0, head_cols),
            ],
            1,
            True,
        ),
    )
    attn_got = [to_partner(attn_blocks[first][0], first) for first in range(2)]
    dealt = after(dealt, attn_blocks[0][0], attn_blocks[1][0])
    grad_scanned = dealt.reshape(places, width)
    if use_kernel:
        back_sent, conv_grads, head_grads = scan_backward(scan_args, grad_scanned)
        lane_grad = back_sent[:, : scan_width + own_heads]
        scan_params = (
            conv_grads[:4],
            conv_grads[4],
            head_grads[0, :own_heads],
            head_grads[1, :own_heads],
            head_grads[2, :own_heads],
        )
    else:
        scan_grads = scan_back(grad_scanned)
        back_sent = jnp.concatenate(
            [scan_grads[0], jnp.pad(scan_grads[1], ((0, 0), (0, pad_width)))], axis=-1
        )
        lane_grad = jnp.concatenate([scan_grads[0], scan_grads[1]], axis=-1)
        scan_params = scan_grads[2:]
    back_sent = back_sent.reshape(parts, patch_count, -1)
    back_taken = trade(back_sent)
    own_half = after(group_halves, back_sent)
    group_in, group_hidden, group_gate, group_up = group_mlp(
        own_half, swap(own_half, "tp", 1), gain_mlp, group_grad_hidden, w_gate, w_up, place_index
    )
    first_set = grad_blocks(
        [
            (group_final, group_hidden, 0, hidden_part),
            (group_in, group_gate, 0, hidden_part),
        ],
        0,
        True,
    )
    late_got = joined(late_got, first_set[0])
    apart_valid = group_valid.reshape(-1, 1)
    group_mix = (late_got[:, :model_width] * apart_valid).astype(jnp.bfloat16)
    group_z = late_got[:, model_width:]
    late_early = joined(early_got, first_set[0])
    group_u = (late_early[:, :model_width] * gain_global).astype(jnp.bfloat16)
    quarter = inner_width // members
    own_scale = lax.dynamic_slice_in_dim(mix_scale, member * quarter, quarter, 0)
    group_n = (late_early[:, model_width:] * own_scale).astype(jnp.bfloat16)
    attn_far = [
        add_side(after(attn_blocks[first][1], first_set[0]), attn_got[first], 1)
        for first in range(2)
    ]
    attn_crossed = [to_partner(attn_far[first], 1 - first) for first in range(2)]
    mlp_blocks = [
        first_set,
        grad_blocks(
            [
                (group_in, after(group_up, *attn_far), 0, hidden_part),
                (group_mix, group_n, 0, group_n.shape[1]),
                (group_u, group_z, 0, group_z.shape[1]),
            ],
            1,
            True,
        ),
    ]
    mlp_got = [to_partner(mlp_blocks[first][0], first) for first in range(2)]
    back_taken = after(back_taken, mlp_blocks[0][0], mlp_blocks[1][0])
    grad_x = from_lanes(back_taken[..., :width])
    by_stream = back_taken.reshape(streams, lanes, patch_count, -1)
    grad_bc = jnp.sum(by_stream[..., width:scan_width], axis=1)
    grad_dt = from_lanes(back_taken[..., scan_width : scan_width + own_heads])
    grad_dt = jnp.sum(grad_dt.reshape(streams, patch_count, head_total, shared), axis=-1)
    grad_shared = jnp.concatenate([grad_bc, grad_dt], axis=-1).reshape(patch_total, -1)
    grad_proj_low = jnp.concatenate(
        [grad_z_low, grad_x.reshape(patch_total, -1).astype(jnp.bfloat16)]
        + [grad_shared.astype(jnp.bfloat16)],
        axis=-1,
    )
    grad_u_part = dot_trans(grad_proj_low, w_in)
    grad_u = tp_sum(grad_u_part)
    rest = [quarters(columns) for columns in (grad_x, grad_bc, grad_dt)]
    rest_cols = [part.shape[-1] for part in rest]
    rest = after(jnp.concatenate(rest, axis=-1), grad_u_part)
    rest = jnp.pad(rest, ((0, 0), (0, 0), (0, -sum(rest_cols) % 128)))
    rest_blocks = grad_blocks(
        [(group_u, joined(group_swap(by_apart(rest)), grad_u_part), 0, rest.shape[-1])], 0, True
    )
    back_global, grad_norm_global = rms_back(patch_out, gain_global, grad_u)
    grad_patch = grad_global + back_global
    side_count = parts // 2
    my_side = seq_index & 1
    by_block = jnp.moveaxis(grad_patch.reshape(patch_total, parts, row_block), 1, 0)
    by_block = by_block.reshape(side_count, 2, patch_total, row_block)
    same_side = lax.dynamic_index_in_dim(by_block, my_side, 1, keepdims=False)
    other_side = lax.dynamic_index_in_dim(by_block, 1 - my_side, 1, keepdims=False)
    patch_rows = jnp.concatenate([same_side, other_side], axis=-1)
    patch_rows = patch_rows.reshape(side_count, patch_total, 2 * row_block)
    gain_part = grad_norm_global.reshape(-1, 2 * row_block)
    gain_count = gain_part.shape[0]
    patch_sent = jnp.concatenate(
        [patch_rows, jnp.broadcast_to(gain_part, (side_count,) + gain_part.shape)], axis=1
    )
    patch_taken = lax.all_to_all(
        patch_sent, "seq", 0, 0, axis_index_groups=row_side, tiled=True
    )

    mlp_far = [
        add_side(after(mlp_blocks[first][1], patch_sent), mlp_got[first], 1)
        for first in range(2)
    ]
    mlp_crossed = [to_partner(mlp_far[first], 1 - first) for first in range(2)]
    patch_taken = after(patch_taken, rest_blocks[0], *mlp_far)
    gain_side = jnp.sum(patch_taken[:, patch_total:], axis=0)
    patch_cols = patch_taken[:, :patch_total].reshape(-1, 2 * row_block)
    patch_far = patch_far_grad(patch_cols, gain_side, bytes_all)
    small = (
        scan_params[0][:, :width],
        scan_params[1][:width],
        scan_params[0][:, width:],
        scan_params[1][width:],
        scan_params[2],
        scan_params[3],
        scan_params[4],
        grad_mix_gain,
        grad_norm_attn,
        grad_norm_mlp,
    )
    small_count = sum(part.size for part in small)
    flat = after(jnp.concatenate([part.reshape(-1) for part in small]), patch_far)
    flat = jnp.pad(flat, (0, -small_count % 1024)).reshape(1, -1, 128)
    pieces = trade(jnp.broadcast_to(flat, (parts,) + flat.shape[1:])).reshape(parts, -1)
    by_small, at = [], 0
    for part in small:
        got = pieces[:, at : at + part.size].reshape((parts,) + part.shape)
        by_small.append(got)
        at += part.size

    def lane_cols(got):
        joined = jnp.sum(got.reshape((streams, lanes) + got.shape[1:]), axis=0)
        return jnp.moveaxis(joined, 0, -2).reshape(joined.shape[1:-1] + (-1,))

    def lane_heads(got):
        joined = jnp.sum(got.reshape(streams, lanes, -1), axis=0)
        return jnp.sum(joined.reshape(head_total, shared), axis=-1)

    small_sums = [
        jnp.concatenate([lane_cols(by_small[0]), jnp.sum(by_small[2], axis=0)], axis=-1),
        jnp.concatenate([lane_cols(by_small[1]), jnp.sum(by_small[3], axis=0)], axis=-1),
        lane_heads(by_small[4]),
        lane_heads(by_small[5]),
        lane_heads(by_small[6]),
    ] + [jnp.sum(got, axis=0) for got in by_small[7:]]

    patch_got = to_partner(patch_far, 0)

    high = (seq_index // QUAD).astype(jnp.int32).reshape(1)
    attn_near = near_sums(
        [
            (after(attn_blocks[first][1], patch_far), attn_got[first], attn_crossed[first])
            for first in range(2)
        ],
        high,
    )
    attn_high = [
        swap(attn_near[apart], "seq", QUAD * apart) for apart in range(1, parts // QUAD)
    ]
    rest_got = to_partner(after(rest_blocks[0], patch_far), 0)
    start = jnp.zeros((1,), jnp.int32)
    mlp_near = [
        near_sums(
            [(after(mlp_blocks[first][1], attn_near, patch_got), mlp_got[first], mlp_crossed[first])],
            start,
        )
        for first in range(2)
    ]
    final_attn = attn_near[0]
    for got in attn_high:
        final_attn = final_attn + after(got, *mlp_near)
    rest_far = add_side(after(rest_blocks[1], *mlp_near), rest_got, 1)
    rest_crossed = to_partner(rest_far, 1)
    rest_near = near_sums(
        [(after(rest_blocks[1], final_attn), rest_got, rest_crossed)], start
    )
    mlp_finals = [
        jnp.moveaxis(group_trade(part), 0, 1) for part in mlp_near + [rest_near]
    ]
    def final_cols(final, low, count):
        return final[..., low : low + count].reshape(row_block, -1)

    final_down = final_cols(mlp_finals[0], 0, hidden_part)
    final_gate = final_cols(mlp_finals[0], hidden_part, hidden_part)
    final_up = final_cols(mlp_finals[1], 0, hidden_part)
    final_out = final_cols(mlp_finals[1], hidden_part, quarter)
    final_z = final_cols(mlp_finals[1], hidden_part + quarter, quarter)
    final_x = final_cols(mlp_finals[2], 0, rest_cols[0])
    final_bc = final_cols(mlp_finals[2], rest_cols[0], rest_cols[1])
    final_dt = final_cols(mlp_finals[2], rest_cols[0] + rest_cols[1], rest_cols[2])
    final_patch = patch_grad(patch_cols, patch_got, bytes_all)
    norm_global_sum = (gain_side + patch_got[row_block:, : 2 * row_block]).reshape(-1)
    grad_bytes = bytes_grad(after(grad_patch, patch_far), w_patch, grad_stream)
    grad_bytes = grad_bytes.reshape(streams, local_rows, feature)

    qkv_cols, o_cols = w_qkv.shape[1], w_o.shape[1]
    return (
        logits.reshape(streams, local_rows, head_cols),
        grad_bytes,
        final_patch,
        norm_global_sum,
        jnp.concatenate([final_z, final_x, final_bc, final_dt], axis=1),
        small_sums[0],
        small_sums[1],
        small_sums[2],
        small_sums[3],
        small_sums[4],
        small_sums[5],
        final_out,
        small_sums[6],
        final_attn[:, :qkv_cols],
        final_attn[:, qkv_cols : qkv_cols + o_cols],
        small_sums[7],
        final_gate,
        final_up,
        final_down,
        final_attn[:, qkv_cols + o_cols :],
    )


def solution(mesh):
    in_specs = (
        P(None, "seq", None),
        P(),
        P(None, "tp"),
        P(),
        P(None, "tp"),
        P(None, "tp"),
        P("tp"),
        P("tp"),
        P("tp"),
        P("tp"),
        P("tp"),
        P(None, "tp"),
        P(),
        P(None, "tp"),
        P(None, "tp"),
        P(),
        P(None, "tp"),
        P(None, "tp"),
        P(None, "tp"),
        P(None, "tp"),
        P(None, "seq", "tp"),
    )
    out_specs = (
        P(None, "seq", "tp"),
        P(None, "seq", "tp"),
        P("seq", "tp"),
        P(),
        P("seq", "tp"),
        P(None, "tp"),
        P("tp"),
        P("tp"),
        P("tp"),
        P("tp"),
        P("tp"),
        P("seq", "tp"),
        P(),
        P("seq", "tp"),
        P("seq", "tp"),
        P(),
        P("seq", "tp"),
        P("seq", "tp"),
        P("seq", "tp"),
        P("seq", "tp"),
    )
    return jax.shard_map(body, mesh=mesh, in_specs=in_specs, out_specs=out_specs, check_vma=False)
```

```python
from functools import partial

import jax
import jax.numpy as jnp
from jax import lax
from jax.experimental import pallas as pl
from jax.experimental.pallas import tpu as pltpu
from jax.sharding import PartitionSpec as P

NS = 128
AD = 64
QUAD = 4


NO_COST = pl.CostEstimate(flops=1024, bytes_accessed=1024, transcendentals=0)
ROOMY = pltpu.CompilerParams(vmem_limit_bytes=56 * 1024 * 1024)

epsilon = 1e-05
highest = lax.Precision.HIGHEST
masked_score = -1e30


def dot_plain(left_side, right_side):
    return jnp.dot(left_side, right_side, preferred_element_type=jnp.float32)


def dot_trans(left_side, right_side):
    return lax.dot_general(
        left_side, right_side, (((1,), (1,)), ((), ())), preferred_element_type=jnp.float32
    )


def dot_left(left_side, right_side):
    return lax.dot_general(
        left_side, right_side, (((0,), (0,)), ((), ())), preferred_element_type=jnp.float32
    )


def rms_scale(values):
    return lax.rsqrt(jnp.mean(values * values, axis=-1, keepdims=True) + epsilon)


def hidden_parts(mlp_in, grad_hidden, w_gate, w_up):
    gate_proj = dot_plain(mlp_in, w_gate)
    up_proj = dot_plain(mlp_in, w_up)
    sigmoid_gate = jax.nn.sigmoid(gate_proj)
    hidden_low = (gate_proj * sigmoid_gate * up_proj).astype(jnp.bfloat16)
    grad_gate_low = (
        grad_hidden * up_proj * sigmoid_gate * (1.0 + gate_proj * (1.0 - sigmoid_gate))
    ).astype(jnp.bfloat16)
    grad_up_low = (grad_hidden * gate_proj * sigmoid_gate).astype(jnp.bfloat16)
    return (hidden_low, grad_gate_low, grad_up_low)


def rms_back(values, gain_values, grad_out):
    scale = rms_scale(values)
    scaled = gain_values * grad_out
    inner_mean = jnp.mean(values * scaled, axis=-1, keepdims=True)
    grad_values = scale * scaled - values * scale * scale * scale * inner_mean
    grad_gain = jnp.sum(values * scale * grad_out, axis=0)
    return (grad_values, grad_gain)


def swap(block, axis, mask):
    return lax.ppermute(block, axis, [(i, i ^ mask) for i in range(lax.axis_size(axis))])


def after(value, *earlier):
    return lax.optimization_barrier((value,) + earlier)[0]


def tp_sum(block):
    return block + swap(block, "tp", 1)


def to_partner(block, bit):
    return swap(block, "seq", 1 << bit)


def seq_bits():
    return lax.axis_size("seq").bit_length() - 1


def group_size():
    return lax.axis_size("seq") // QUAD


def group_trade(blocks):
    members = [[low + QUAD * high for high in range(group_size())] for low in range(QUAD)]
    return lax.all_to_all(blocks, "seq", 0, 0, axis_index_groups=members, tiled=True)


def add_kernel(index_ref, *refs):
    total = refs[0][...] + refs[1][...]
    refs[2][...] = total.reshape(refs[2].shape)


def add_side(near, got, side):
    unused, groups, rows, cols = near.shape
    index = jnp.zeros((1,), jnp.int32)
    block = pl.BlockSpec((1, 1, rows, cols), lambda i, ref: (side, i, 0, 0))
    return pl.pallas_call(
        add_kernel,
        grid_spec=pltpu.PrefetchScalarGridSpec(
            num_scalar_prefetch=1,
            grid=(groups,),
            in_specs=[block, block],
            out_specs=pl.BlockSpec((1, rows, cols), lambda i, ref: (i, 0, 0)),
        ),
        out_shape=jax.ShapeDtypeStruct((groups, rows, cols), jnp.float32),
        compiler_params=ROOMY,
        cost_estimate=NO_COST,
    )(index, near, got)


def near_kernel(index_ref, *refs):
    out_ref = refs[-1]
    at = 0
    for near_ref, got_ref, crossed_ref in zip(refs[0:-1:3], refs[1:-1:3], refs[2:-1:3]):
        cols = near_ref.shape[3]
        total = near_ref[0, 0] + got_ref[0, 0] + crossed_ref[0]
        out_ref[0, :, at : at + cols] = total
        at += cols


def near_sums(terms, high):
    unused, groups, rows, unused_cols = terms[0][0].shape
    cols = [term[0].shape[3] for term in terms]
    specs, operands = [], []
    for (near, got, crossed), count in zip(terms, cols):
        four = pl.BlockSpec((1, 1, rows, count), lambda i, ref: (0, ref[0] ^ i, 0, 0))
        three = pl.BlockSpec((1, rows, count), lambda i, ref: (ref[0] ^ i, 0, 0))
        specs += [four, four, three]
        operands += [near, got, crossed]
    return pl.pallas_call(
        near_kernel,
        grid_spec=pltpu.PrefetchScalarGridSpec(
            num_scalar_prefetch=1,
            grid=(groups,),
            in_specs=specs,
            out_specs=pl.BlockSpec((1, rows, sum(cols)), lambda i, ref: (i, 0, 0)),
        ),
        out_shape=jax.ShapeDtypeStruct((groups, rows, sum(cols)), jnp.float32),
        compiler_params=ROOMY,
        cost_estimate=NO_COST,
    )(high, *operands)


def grad_blocks_kernel(pairs, first, relative, rows, member_ref, *refs):
    lefts, rights = refs[: len(pairs)], refs[len(pairs) : 2 * len(pairs)]
    far_ref, near_ref = refs[2 * len(pairs) :]
    other = 1 - first
    at = 0
    for left_ref, right_ref, (low, high) in zip(lefts, rights, pairs):
        got = dot_left(left_ref[...], right_ref[:, low:high].astype(jnp.bfloat16))
        places = slice(at, at + high - low)
        for block in range(got.shape[0] // rows):
            place, member = block // QUAD, block % QUAD
            part = got[block * rows : (block + 1) * rows]
            apart = member_ref[0] ^ member
            is_far = apart >> first & 1
            if relative:
                side = apart >> other & 1
            else:
                side = member >> other & 1

            @pl.when(is_far == 1)
            def _():
                if relative:
                    far_ref[side, place, :, places] = part
                else:
                    far_ref[place, side, :, places] = part

            @pl.when(is_far == 0)
            def _():
                if relative:
                    near_ref[side, place, :, places] = part
                else:
                    near_ref[place, side, :, places] = part

        at += high - low


def grad_blocks(terms, first, relative):
    parts = lax.axis_size("seq")
    groups = parts // QUAD
    model_width = terms[0][0].shape[1]
    rows = model_width // parts
    cols = max(128, QUAD * rows)
    places = cols // (QUAD * rows)
    pairs = [(low, high) for unused, unused_right, low, high in terms]
    total = sum(high - low for low, high in pairs)
    member = (lax.axis_index("seq") % QUAD).astype(jnp.int32).reshape(1)
    if relative:
        shape, block = (2, groups, rows, total), (2, places, rows, total)
        out_spec = pl.BlockSpec(block, lambda i, ref: (0, i, 0, 0))
    else:
        shape, block = (groups, 2, rows, total), (places, 2, rows, total)
        out_spec = pl.BlockSpec(block, lambda i, ref: (i, 0, 0, 0))
    out = jax.ShapeDtypeStruct(shape, jnp.float32)
    return pl.pallas_call(
        partial(grad_blocks_kernel, pairs, first, relative, rows),
        grid_spec=pltpu.PrefetchScalarGridSpec(
            num_scalar_prefetch=1,
            grid=(model_width // cols,),
            in_specs=[
                pl.BlockSpec((term[0].shape[0], cols), lambda i, ref: (0, i)) for term in terms
            ]
            + [pl.BlockSpec(term[1].shape, lambda i, ref: (0, 0)) for term in terms],
            out_specs=[out_spec, out_spec],
        ),
        out_shape=[out, out],
        compiler_params=ROOMY,
        cost_estimate=NO_COST,
    )(member, *[term[0] for term in terms], *[term[1] for term in terms])


def segment_ids(lengths, place_count):
    ends = jnp.cumsum(lengths // 8, dtype=jnp.int32)
    places = jnp.arange(place_count, dtype=jnp.int32)
    short_ids = jnp.sum(
        (places[:, None] >= ends[None, :]).astype(jnp.int32), axis=1, dtype=jnp.int32
    )
    return jnp.stack([jnp.zeros_like(short_ids), short_ids])


def scan_heads(seg_now, head_size, xbc, dt_raw, conv_weight, conv_bias, dt_shift, a_logs, skips):
    place_count = xbc.shape[0]
    conv_sum = conv_bias + conv_weight[3] * xbc
    for offset in range(3):
        distance = 3 - offset
        earlier = jnp.pad(xbc, ((distance, 0), (0, 0)))[:place_count]
        seg_earlier = jnp.pad(seg_now, (distance, 0), constant_values=-1)[:place_count]
        same_doc = (seg_earlier == seg_now).astype(jnp.float32)
        conv_sum = conv_sum + conv_weight[offset] * earlier * same_doc[:, None]
    active = jax.nn.silu(conv_sum)
    head_count = dt_raw.shape[1]
    inner = head_count * head_size
    values = active[:, :inner].reshape(place_count, head_count, head_size)
    in_keys = active[:, inner : inner + NS]
    out_keys = active[:, inner + NS :]
    step_sizes = jax.nn.softplus(dt_raw + dt_shift)
    decay_rates = -step_sizes * jnp.exp(a_logs)
    chunk = min(place_count, 512)
    triangle = jnp.tril(jnp.ones((chunk, chunk), jnp.float32))
    state = jnp.zeros((head_count, head_size, NS), jnp.float32)
    seg_last = jnp.int32(-1)
    outputs = []
    for start in range(0, place_count, chunk):
        stop = start + chunk
        x, b, c = values[start:stop], in_keys[start:stop], out_keys[start:stop]
        dt, seg = step_sizes[start:stop], seg_now[start:stop]
        cumulative = jnp.dot(triangle, decay_rates[start:stop], precision=highest)
        allowed = (triangle > 0.0) & (seg[:, None] == seg[None, :])
        ordered = cumulative.T
        gaps = ordered[:, :, None] - ordered[:, None, :]
        decays = jnp.where(allowed, jnp.exp(jnp.where(allowed, gaps, 0.0)), 0.0)
        crossing = jnp.einsum("pn,jn->pj", c, b, precision=highest)
        mixing = crossing[None] * decays * dt.T[:, None, :]
        result = jnp.einsum("hpj,jhd->phd", mixing, x, precision=highest)
        if start > 0:
            entering = jnp.exp(cumulative) * (seg == seg_last).astype(jnp.float32)[:, None]
            result = result + entering[..., None] * jnp.einsum(
                "pn,hdn->phd", c, state, precision=highest
            )
        if stop < place_count:
            last_same = (seg == seg[-1]).astype(jnp.float32)[:, None]
            weight = jnp.exp(cumulative[-1:] - cumulative) * last_same * dt
            through = jnp.exp(cumulative[-1]) * (seg[-1] == seg_last).astype(jnp.float32)
            state = through[:, None, None] * state + jnp.einsum(
                "jh,jhd,jn->hdn", weight, x, b, precision=highest
            )
            seg_last = seg[-1]
        outputs.append(result + skips[:, None] * x)
    return jnp.concatenate(outputs, axis=0).reshape(place_count, inner)


def gated_unit(result, gate_in):
    gated = result * jax.nn.silu(gate_in)
    return gated * rms_scale(gated)


def patch_far_kernel(grad_ref, gain_ref, bytes_ref, out_ref):
    half = grad_ref.shape[1] // 2
    grad_low = grad_ref[:, half:].astype(jnp.bfloat16)
    out_ref[:half] = dot_left(grad_low, bytes_ref[...].astype(jnp.bfloat16))
    out_ref[half:] = jnp.zeros((out_ref.shape[0] - half, out_ref.shape[1]), jnp.float32)

    @pl.when(pl.program_id(0) == 0)
    def _():
        out_ref[half:, : 2 * half] = gain_ref[...]


def patch_far_grad(grad_rows, gain_part, bytes_all):
    places, cols = grad_rows.shape
    total = bytes_all.shape[1]
    rows = cols // 2 + gain_part.shape[0]
    block = 1024
    return pl.pallas_call(
        patch_far_kernel,
        grid=(total // block,),
        in_specs=[
            pl.BlockSpec((places, cols), lambda i: (0, 0)),
            pl.BlockSpec(gain_part.shape, lambda i: (0, 0)),
            pl.BlockSpec((places, block), lambda i: (0, i)),
        ],
        out_specs=pl.BlockSpec((rows, block), lambda i: (0, i)),
        out_shape=jax.ShapeDtypeStruct((rows, total), jnp.float32),
        compiler_params=ROOMY,
        cost_estimate=NO_COST,
    )(grad_rows, gain_part, bytes_all)


def patch_grad_kernel(grad_ref, *refs):
    byte_refs, got_refs, out_ref, order_ref = refs[:8], refs[8:16], refs[16], refs[17]
    width = byte_refs[0].shape[1]

    @pl.when(pl.program_id(0) == 0)
    def _():
        order_ref[...] = feature_order(width)

    grad_low = grad_ref[:, : grad_ref.shape[1] // 2].astype(jnp.bfloat16)
    wide = jnp.concatenate([ref[...].astype(jnp.bfloat16) for ref in byte_refs], axis=1)
    rows = grad_low.shape[1]
    grad = dot_left(grad_low, wide)
    grad = grad + jnp.concatenate([ref[:rows] for ref in got_refs], axis=1)
    high = grad.astype(jnp.bfloat16)
    rest = grad - high.astype(jnp.float32)
    mid = rest.astype(jnp.bfloat16)
    low = (rest - mid.astype(jnp.float32)).astype(jnp.bfloat16)
    order = order_ref[...]
    out_ref[...] = dot_plain(high, order) + (dot_plain(mid, order) + dot_plain(low, order))


def patch_grad(grad_rows, got, bytes_all):
    places, cols = grad_rows.shape
    feature = bytes_all.shape[1] // 8
    chunk = 128
    steps = feature // chunk

    def byte_specs(rows):
        return [
            pl.BlockSpec((rows, chunk), partial(lambda j, i: (0, j * steps + i), j))
            for j in range(8)
        ]

    return pl.pallas_call(
        patch_grad_kernel,
        grid=(steps,),
        in_specs=[pl.BlockSpec((places, cols), lambda i: (0, 0))]
        + byte_specs(places)
        + byte_specs(got.shape[0]),
        out_specs=pl.BlockSpec((cols // 2, 8 * chunk), lambda i: (0, i)),
        out_shape=jax.ShapeDtypeStruct((cols // 2, 8 * feature), jnp.float32),
        scratch_shapes=[pltpu.VMEM((8 * chunk, 8 * chunk), jnp.bfloat16)],
        compiler_params=ROOMY,
        cost_estimate=NO_COST,
    )(grad_rows, *([bytes_all] * 8), *([got] * 8))


def trade(blocks):
    return lax.all_to_all(blocks, "seq", 0, 0, tiled=True)


def grid_iota(shape, axis):
    return lax.broadcasted_iota(jnp.int32, shape, axis)


def dot_fine(left_side, right_side, left_axis, right_axis):
    return lax.dot_general(
        left_side,
        right_side,
        (((left_axis,), (right_axis,)), ((), ())),
        preferred_element_type=jnp.float32,
        precision=highest,
    )


def shifted_down(block, distance):
    rows = grid_iota(block.shape, 0)
    return jnp.where(rows >= distance, pltpu.roll(block, distance, 0), 0.0)


def shifted_up(block, distance):
    count = block.shape[0]
    rows = grid_iota(block.shape, 0)
    return jnp.where(rows < count - distance, pltpu.roll(block, count - distance, 0), 0.0)


def scan_terms(taken_ref, same_ref, conv_ref, head_ref):
    places = taken_ref.shape[0]
    channels = conv_ref.shape[1]
    xbc = taken_ref[:, :channels]
    conv_sum = conv_ref[4:5] + conv_ref[3:4] * xbc
    for k in range(3):
        earlier = shifted_down(xbc, 3 - k) * same_ref[:, k : k + 1]
        conv_sum = conv_sum + conv_ref[k : k + 1] * earlier
    gate = jax.nn.sigmoid(conv_sum)
    active = conv_sum * gate
    raw = taken_ref[:, channels:] + head_ref[0:1]
    steps = jnp.maximum(raw, 0.0) + jnp.log1p(jnp.exp(-jnp.abs(raw)))
    rates = -steps * jnp.exp(head_ref[1:2])
    square = (places, places)
    triangle = jnp.where(grid_iota(square, 0) >= grid_iota(square, 1), 1.0, 0.0)
    running = dot_fine(triangle, rates, 1, 0)
    return xbc, conv_sum, gate, active, raw, steps, rates, triangle, running


def scan_forward_kernel(taken_ref, same_ref, conv_ref, head_ref, seg_col, seg_row, out_ref):
    places, width = out_ref.shape
    terms = scan_terms(taken_ref, same_ref, conv_ref, head_ref)
    active, steps, running = terms[3], terms[5], terms[8]
    values = active[:, :width]
    keys, reads = active[:, width : width + NS], active[:, width + NS :]
    steps_row, running_row = steps.T, running.T
    heads = width // 64
    rows = 128
    for first in range(0, places, rows):
        last = first + rows
        shape = (rows, last)
        allowed = (seg_col[first:last] == seg_row[:, :last]) & (
            grid_iota(shape, 0) + first >= grid_iota(shape, 1)
        )
        crossing = dot_fine(reads[first:last], keys[:last], 1, 1)
        lane = grid_iota((rows, width), 1) // 64
        total = head_ref[2:3] * values[first:last]
        for h in range(heads):
            gaps = running[first:last, h : h + 1] - running_row[h : h + 1, :last]
            decays = jnp.exp(jnp.where(allowed, gaps, masked_score))
            mixing = crossing * decays * steps_row[h : h + 1, :last]
            part = dot_fine(mixing, values[:last], 1, 0)
            total = total + jnp.where(lane == h, part, 0.0)
        out_ref[first:last] = total


def scan_backward_kernel(
    taken_ref,
    same_ref,
    conv_ref,
    head_ref,
    seg_col,
    seg_row,
    grad_ref,
    out_ref,
    conv_grad_ref,
    head_grad_ref,
    values_grad,
    keys_grad,
    reads_grad,
    rows_grad,
    cols_grad,
):
    places, width = values_grad.shape
    terms = scan_terms(taken_ref, same_ref, conv_ref, head_ref)
    xbc, conv_sum, gate, active, raw, steps, rates, triangle, running = terms
    channels = xbc.shape[1]
    values = active[:, :width]
    keys, reads = active[:, width : width + NS], active[:, width + NS :]
    steps_row, running_row = steps.T, running.T
    heads = width // 64
    rows = 128
    grad = grad_ref[...]
    values_grad[...] = head_ref[2:3] * grad
    keys_grad[...] = jnp.zeros_like(keys_grad)
    rows_grad[...] = jnp.zeros_like(rows_grad)
    cols_grad[...] = jnp.zeros_like(cols_grad)
    for first in range(0, places, rows):
        last = first + rows
        shape = (rows, last)
        allowed = (seg_col[first:last] == seg_row[:, :last]) & (
            grid_iota(shape, 0) + first >= grid_iota(shape, 1)
        )
        crossing = dot_fine(reads[first:last], keys[:last], 1, 1)
        crossing_grad = jnp.zeros(shape, jnp.float32)
        grad_rows = grad[first:last]
        lane = grid_iota((rows, width), 1) // 64
        wide_lane = grid_iota((last, width), 1) // 64
        column = grid_iota((rows, 128), 1)
        down = jnp.zeros((rows, 128), jnp.float32)
        for h in range(heads):
            gaps = running[first:last, h : h + 1] - running_row[h : h + 1, :last]
            decays = jnp.exp(jnp.where(allowed, gaps, masked_score))
            step_row = steps_row[h : h + 1, :last]
            weighted = decays * step_row
            mixing = crossing * weighted
            own_grad = jnp.where(lane == h, grad_rows, 0.0)
            mixing_grad = dot_fine(own_grad, values[:last], 1, 1)
            back = dot_fine(mixing, own_grad, 0, 0)
            values_grad[:last] += jnp.where(wide_lane == h, back, 0.0)
            crossing_grad = crossing_grad + mixing_grad * weighted
            step_part = jnp.sum(mixing_grad * crossing * decays, axis=0, keepdims=True)
            gap_part = mixing_grad * mixing
            down = jnp.where(column == h, jnp.sum(gap_part, axis=1, keepdims=True), down)
            cols_grad[h : h + 1, :last] += step_part
            cols_grad[heads + h : heads + h + 1, :last] += step_part * step_row
        rows_grad[first:last] += down
        reads_grad[first:last] = dot_fine(crossing_grad, keys[:last], 1, 0)
        keys_grad[:last] += dot_fine(crossing_grad, reads[first:last], 0, 0)
    turned = cols_grad[...].T
    column = grid_iota(turned.shape, 1)
    step_grad = jnp.where(column < heads, turned, 0.0)
    ended = pltpu.roll(turned, turned.shape[1] - heads, 1)
    running_grad = jnp.where(column < heads, rows_grad[...] - ended, 0.0)
    rates_grad = dot_fine(triangle, running_grad, 0, 0)
    step_grad = step_grad - rates_grad * jnp.exp(head_ref[1:2])
    raw_grad = step_grad * jax.nn.sigmoid(raw)
    out_ref[:, channels:] = raw_grad
    lane = grid_iota((places, width), 1) // 64
    product = jnp.sum(grad * values, axis=0, keepdims=True)
    head_grad_ref[...] = jnp.zeros_like(head_grad_ref)
    head_grad_ref[0:1] = jnp.sum(raw_grad, axis=0, keepdims=True)
    head_grad_ref[1:2] = jnp.sum(rates_grad * rates, axis=0, keepdims=True)
    skip_lane = grid_iota((1, width), 1)
    skip_grad = jnp.zeros((1, width), jnp.float32)
    for h in range(heads):
        own = jnp.sum(jnp.where(skip_lane // 64 == h, product, 0.0), axis=1, keepdims=True)
        skip_grad = jnp.where(skip_lane == h, own, skip_grad)
    head_grad_ref[2:3] = skip_grad
    active_grad = jnp.concatenate([values_grad[...], keys_grad[...], reads_grad[...]], axis=1)
    conv_grad = active_grad * gate * (1.0 + conv_sum * (1.0 - gate))
    back = conv_ref[3:4] * conv_grad
    conv_grad_ref[...] = jnp.zeros_like(conv_grad_ref)
    conv_grad_ref[3:4] = jnp.sum(conv_grad * xbc, axis=0, keepdims=True)
    conv_grad_ref[4:5] = jnp.sum(conv_grad, axis=0, keepdims=True)
    for k in range(3):
        kept = conv_grad * same_ref[:, k : k + 1]
        back = back + conv_ref[k : k + 1] * shifted_up(kept, 3 - k)
        conv_grad_ref[k : k + 1] = jnp.sum(
            kept * shifted_down(xbc, 3 - k), axis=0, keepdims=True
        )
    out_ref[:, :channels] = back


def scan_forward(args, width):
    places = args[0].shape[0]
    return pl.pallas_call(
        scan_forward_kernel,
        out_shape=jax.ShapeDtypeStruct((places, width), jnp.float32),
        compiler_params=ROOMY,
        cost_estimate=NO_COST,
    )(*args)


def scan_backward(args, grad):
    places, width = grad.shape
    channels = args[2].shape[1]
    f32 = jnp.float32
    return pl.pallas_call(
        scan_backward_kernel,
        out_shape=[
            jax.ShapeDtypeStruct((places, channels + 128), f32),
            jax.ShapeDtypeStruct((8, channels), f32),
            jax.ShapeDtypeStruct((8, 128), f32),
        ],
        scratch_shapes=[
            pltpu.VMEM((places, width), f32),
            pltpu.VMEM((places, NS), f32),
            pltpu.VMEM((places, NS), f32),
            pltpu.VMEM((places, 128), f32),
            pltpu.VMEM((128, places), f32),
        ],
        compiler_params=ROOMY,
        cost_estimate=NO_COST,
    )(*args, grad)


def patch_lanes(block):
    shape = (block // 8, 8, block)
    return grid_iota(shape, 0) == grid_iota(shape, 2) // 8


def folded(scores, same_patch):
    split = scores.reshape(same_patch.shape)
    return jnp.sum(jnp.where(same_patch, split, 0.0), axis=0)


def unfolded(rows, same_patch):
    spread = jnp.where(same_patch, rows[None], 0.0)
    return spread.reshape(-1, rows.shape[1]).astype(jnp.bfloat16)


def softmax_rows(scores, causal):
    scores = jnp.where(causal, scores, masked_score)
    top = jnp.max(scores, axis=1, keepdims=True)
    powers = jnp.exp(scores - top)
    return powers / jnp.sum(powers, axis=1, keepdims=True)


def head_places(rows, head_cols, block):
    return [
        (slice(first, first + block), [j * head_cols + pair * 128 for j in range(3)])
        for first in range(0, rows, block)
        for pair in range(head_cols // 128)
    ]


def all_scores(qkv_ref, places, lane, same_patch):
    scores = []
    for rows, (query, key, unused) in places:
        queries = qkv_ref[rows, query : query + 128] * 0.125
        keys = qkv_ref[rows, key : key + 128]
        for h in range(2):
            own = jnp.where(lane == h, queries, 0)
            scores.append(folded(dot_trans(keys, own), same_patch))
    return jnp.stack(scores)


def attn_forward_kernel(
    bytes_ref, patch_ref, gain_ref, qkv_w_ref, o_w_ref, x_ref, a_ref, qkv_ref, o_ref, out_ref
):
    rows = bytes_ref.shape[0]
    spread = jnp.broadcast_to(patch_ref[...][:, None], (rows // 8, 8, patch_ref.shape[1]))
    x = bytes_ref[...].astype(jnp.float32) + spread.reshape(bytes_ref.shape)
    x_ref[...] = x
    attn_in = (x * rms_scale(x) * gain_ref[...]).astype(jnp.bfloat16)
    a_ref[...] = attn_in
    qkv_ref[...] = dot_plain(attn_in, qkv_w_ref[...]).astype(jnp.bfloat16)
    head_cols = o_ref.shape[1]
    block = 128
    same_patch = patch_lanes(block)
    causal = grid_iota((8, block), 0) <= grid_iota((8, block), 1) % 8
    lane = grid_iota((block, 128), 1) // AD
    places = head_places(rows, head_cols, block)
    probs = softmax_rows(all_scores(qkv_ref, places, lane, same_patch), causal)
    for at, (row_place, (query, unused, value)) in enumerate(places):
        values = qkv_ref[row_place, value : value + 128]
        parts = [dot_left(unfolded(probs[2 * at + h], same_patch), values) for h in range(2)]
        total = jnp.where(lane == 0, parts[0], parts[1])
        o_ref[row_place, query : query + 128] = total.astype(jnp.bfloat16)
    out_ref[...] = dot_trans(o_ref[...], o_w_ref[...])


def attn_forward(bytes_rows, patch_rows, gain, w_qkv, w_o):
    rows, width = bytes_rows.shape
    block = 256
    cols, head_cols = w_qkv.shape[1], w_o.shape[1]
    f32, bf16 = jnp.float32, jnp.bfloat16

    def by_rows(cols):
        return pl.BlockSpec((block, cols), lambda i: (i, 0))

    def whole(shape):
        return pl.BlockSpec(shape, lambda i: (0, 0))

    return pl.pallas_call(
        attn_forward_kernel,
        grid=(rows // block,),
        in_specs=[
            by_rows(width),
            pl.BlockSpec((block // 8, width), lambda i: (i, 0)),
            whole((1, width)),
            whole(w_qkv.shape),
            whole(w_o.shape),
        ],
        out_specs=[by_rows(width), by_rows(width), by_rows(cols), by_rows(head_cols), by_rows(width)],
        out_shape=[
            jax.ShapeDtypeStruct((rows, width), f32),
            jax.ShapeDtypeStruct((rows, width), bf16),
            jax.ShapeDtypeStruct((rows, cols), bf16),
            jax.ShapeDtypeStruct((rows, head_cols), bf16),
            jax.ShapeDtypeStruct((rows, width), f32),
        ],
        compiler_params=ROOMY,
        cost_estimate=NO_COST,
    )(bytes_rows, patch_rows, gain.reshape(1, width), w_qkv, w_o)


def attn_backward_kernel(
    x_ref,
    final_ref,
    own_ref,
    other_ref,
    gain_ref,
    qkv_ref,
    qkv_w_ref,
    o_w_ref,
    mid_ref,
    low_ref,
    qkv_grad_ref,
    out_ref,
    gain_grad_ref,
):
    rows = x_ref.shape[0]
    back, gain_grad = rms_back(x_ref[...], gain_ref[...], own_ref[...] + other_ref[...])
    mid = final_ref[...] + back
    mid_ref[...] = mid
    low_ref[...] = mid.astype(jnp.bfloat16)
    gain_grad = gain_grad.reshape(1, -1)

    @pl.when(pl.program_id(0) == 0)
    def _():
        gain_grad_ref[...] = gain_grad

    @pl.when(pl.program_id(0) > 0)
    def _():
        gain_grad_ref[...] += gain_grad

    mixed_grad = dot_plain(low_ref[...], o_w_ref[...]).astype(jnp.bfloat16)
    head_cols = mixed_grad.shape[1]
    block = 128
    same_patch = patch_lanes(block)
    causal = grid_iota((8, block), 0) <= grid_iota((8, block), 1) % 8
    lane = grid_iota((block, 128), 1) // AD
    places = head_places(rows, head_cols, block)
    probs = softmax_rows(all_scores(qkv_ref, places, lane, same_patch), causal)
    probs_grads = []
    for row_place, (query, unused, value) in places:
        values = qkv_ref[row_place, value : value + 128]
        out_grad = mixed_grad[row_place, query : query + 128]
        for h in range(2):
            own_grad = jnp.where(lane == h, out_grad, 0)
            probs_grads.append(folded(dot_trans(values, own_grad), same_patch))
    probs_grad = jnp.stack(probs_grads)
    inner = jnp.sum(probs * probs_grad, axis=1, keepdims=True)
    scores_grad = probs * (probs_grad - inner)
    for at, (row_place, cols) in enumerate(places):
        query, key, unused = cols
        queries = qkv_ref[row_place, query : query + 128]
        keys = qkv_ref[row_place, key : key + 128]
        out_grad = mixed_grad[row_place, query : query + 128]
        parts = []
        for h in range(2):
            own_scores = unfolded(scores_grad[2 * at + h], same_patch)
            parts.append(
                (
                    dot_left(own_scores, keys) * 0.125,
                    dot_plain(own_scores, queries) * 0.125,
                    dot_plain(unfolded(probs[2 * at + h], same_patch), out_grad),
                )
            )
        for j in range(3):
            grad = jnp.where(lane == 0, parts[0][j], parts[1][j])
            qkv_grad_ref[row_place, cols[j] : cols[j] + 128] = grad.astype(jnp.bfloat16)
    out_ref[...] = dot_trans(qkv_grad_ref[...], qkv_w_ref[...])


def attn_backward(x_rows, final_grad, own_part, other_part, gain, qkv, w_qkv, w_o):
    rows, width = x_rows.shape
    block = 256
    cols = w_qkv.shape[1]
    f32, bf16 = jnp.float32, jnp.bfloat16

    def by_rows(cols):
        return pl.BlockSpec((block, cols), lambda i: (i, 0))

    def whole(shape):
        return pl.BlockSpec(shape, lambda i: (0, 0))

    return pl.pallas_call(
        attn_backward_kernel,
        grid=(rows // block,),
        in_specs=[by_rows(width)] * 4
        + [whole((1, width)), by_rows(cols), whole(w_qkv.shape), whole(w_o.shape)],
        out_specs=[
            by_rows(width),
            by_rows(width),
            by_rows(cols),
            by_rows(width),
            whole((1, width)),
        ],
        out_shape=[
            jax.ShapeDtypeStruct((rows, width), f32),
            jax.ShapeDtypeStruct((rows, width), bf16),
            jax.ShapeDtypeStruct((rows, cols), bf16),
            jax.ShapeDtypeStruct((rows, width), f32),
            jax.ShapeDtypeStruct((1, width), f32),
        ],
        compiler_params=ROOMY,
        cost_estimate=NO_COST,
    )(x_rows, final_grad, own_part, other_part, gain.reshape(1, width), qkv, w_qkv, w_o)


def mlp_in_kernel(core_ref, x_ref, own_ref, other_ref, gain_ref, out_ref, low_ref, half_ref):
    x = x_ref[...] + (own_ref[...] + other_ref[...])
    out_ref[...] = x
    unit = x * rms_scale(x)
    low_ref[...] = (unit * gain_ref[...]).astype(jnp.bfloat16)
    width = half_ref.shape[1]
    half_ref[...] = jnp.where(core_ref[0] == 0, unit[:, :width], unit[:, width:])


def mlp_in(x_rows, own_part, other_part, gain):
    rows, width = x_rows.shape
    block = 128
    core = lax.axis_index("tp").astype(jnp.int32).reshape(1)

    def by_rows(cols):
        return pl.BlockSpec((block, cols), lambda i, ref: (i, 0))

    return pl.pallas_call(
        mlp_in_kernel,
        grid_spec=pltpu.PrefetchScalarGridSpec(
            num_scalar_prefetch=1,
            grid=(rows // block,),
            in_specs=[by_rows(width)] * 3 + [pl.BlockSpec((1, width), lambda i, ref: (0, 0))],
            out_specs=[by_rows(width), by_rows(width), by_rows(width // 2)],
        ),
        out_shape=[
            jax.ShapeDtypeStruct((rows, width), jnp.float32),
            jax.ShapeDtypeStruct((rows, width), jnp.bfloat16),
            jax.ShapeDtypeStruct((rows, width // 2), jnp.float32),
        ],
        compiler_params=ROOMY,
        cost_estimate=NO_COST,
    )(core, x_rows, own_part, other_part, gain.reshape(1, width))


def units_in_halves(
    mlp_low, grad_ref, gate_w_ref, up_w_ref, hidden_ref, gate_ref, up_ref
):
    half = grad_ref.shape[1] // 2
    for at in range(2):
        cols = slice(at * half, (at + 1) * half)
        hidden, gate, up = hidden_parts(
            mlp_low, grad_ref[:, cols], gate_w_ref[:, cols], up_w_ref[:, cols]
        )
        hidden_ref[:, cols] = hidden
        gate_ref[:, cols] = gate
        up_ref[:, cols] = up


def mlp_kernel(
    in_ref, grad_ref, gate_w_ref, up_w_ref, hidden_ref, gate_ref, up_ref, out_ref, total_ref
):
    mlp_low = in_ref[...]
    units_in_halves(
        mlp_low, grad_ref, gate_w_ref, up_w_ref, hidden_ref, gate_ref, up_ref
    )
    part = dot_trans(gate_ref[...], gate_w_ref[...]) + dot_trans(up_ref[...], up_w_ref[...])
    step = pl.program_id(0)

    @pl.when(step == 0)
    def _():
        total_ref[...] = part

    @pl.when(step > 0)
    def _():
        total_ref[...] += part

    @pl.when(step == pl.num_programs(0) - 1)
    def _():
        out_ref[...] = total_ref[...]


def mlp_rows(mlp_low, grad_hidden, w_gate, w_up):
    rows, width = mlp_low.shape
    units = w_gate.shape[1]
    block = 512
    by_units = pl.BlockSpec((rows, block), lambda i: (0, i))
    by_weights = pl.BlockSpec((width, block), lambda i: (0, i))
    whole = pl.BlockSpec((rows, width), lambda i: (0, 0))
    low = jax.ShapeDtypeStruct((rows, units), jnp.bfloat16)
    return pl.pallas_call(
        mlp_kernel,
        grid=(units // block,),
        in_specs=[whole, by_units, by_weights, by_weights],
        out_specs=[by_units, by_units, by_units, whole],
        out_shape=[low, low, low, jax.ShapeDtypeStruct((rows, width), jnp.float32)],
        scratch_shapes=[pltpu.VMEM((rows, width), jnp.float32)],
        compiler_params=ROOMY,
        cost_estimate=NO_COST,
    )(mlp_low, grad_hidden, w_gate, w_up)


def feature_order(width):
    shape = (8 * width, 8 * width)
    row, col = grid_iota(shape, 0), grid_iota(shape, 1)
    return jnp.where(row == (col % 8) * width + col // 8, 1.0, 0.0).astype(jnp.bfloat16)


def patch_in_kernel(core_ref, bytes_ref, weight_ref, wide_ref, out_ref, rows_ref, order_ref):
    places, feature = wide_ref.shape[0], wide_ref.shape[1] // 8
    chunk = weight_ref.shape[1] // 8
    step = pl.program_id(0)

    @pl.when(step == 0)
    def _():
        order_ref[...] = feature_order(chunk)
        for at in range(feature // 128):
            low = at * 128
            rows_ref[at] = bytes_ref[:, low : low + 128].astype(jnp.float32)
            for j in range(8):
                wide_ref[:, j * feature + low : j * feature + low + 128] = rows_ref[
                    at, pl.ds(j, places, stride=8), :
                ]

    parts = [
        wide_ref[:, pl.ds(pl.multiple_of(j * feature + step * chunk, 128), chunk)]
        for j in range(8)
    ]
    by_byte = jnp.concatenate(parts, axis=1).astype(jnp.bfloat16)
    by_feature = dot_plain(by_byte, order_ref[...]).astype(jnp.bfloat16)
    part = dot_trans(by_feature, weight_ref[...])

    @pl.when(step == 0)
    def _():
        out_ref[...] = part

    @pl.when(step > 0)
    def _():
        out_ref[...] += part


def patch_in(byte_rows, w_patch):
    rows, model_width = byte_rows.shape
    out_width, cols = w_patch.shape
    feature, chunk = cols // 8, 128
    core = lax.axis_index("tp").astype(jnp.int32).reshape(1)
    f32 = jnp.float32
    return pl.pallas_call(
        patch_in_kernel,
        grid_spec=pltpu.PrefetchScalarGridSpec(
            num_scalar_prefetch=1,
            grid=(feature // chunk,),
            in_specs=[
                pl.BlockSpec((rows, feature), lambda i, ref: (0, ref[0])),
                pl.BlockSpec((out_width, 8 * chunk), lambda i, ref: (0, i)),
            ],
            out_specs=[
                pl.BlockSpec((rows // 8, cols), lambda i, ref: (0, 0)),
                pl.BlockSpec((rows // 8, out_width), lambda i, ref: (0, 0)),
            ],
            scratch_shapes=[
                pltpu.VMEM((feature // 128, rows, 128), f32),
                pltpu.VMEM((8 * chunk, 8 * chunk), jnp.bfloat16),
            ],
        ),
        out_shape=[
            jax.ShapeDtypeStruct((rows // 8, cols), f32),
            jax.ShapeDtypeStruct((rows // 8, out_width), f32),
        ],
        compiler_params=ROOMY,
        cost_estimate=NO_COST,
    )(core, byte_rows, w_patch)


def final_kernel(
    member_ref,
    own_ref,
    other_ref,
    mask_ref,
    own_head_ref,
    other_head_ref,
    weight_ref,
    low_ref,
    hidden_ref,
    mine_ref,
    mine_low_ref,
):
    own = (own_ref[...] * mask_ref[...]).astype(jnp.bfloat16)
    other = (other_ref[...] * mask_ref[...]).astype(jnp.bfloat16)
    other_head = other_head_ref[...].astype(jnp.bfloat16)
    total = dot_trans(own, own_head_ref[...]) + dot_trans(other, other_head)
    low = total.astype(jnp.bfloat16)
    low_ref[...] = low
    hidden_ref[...] = dot_plain(low, weight_ref[...])

    @pl.when(pl.program_id(0) == 0)
    def _():
        mine_ref[...] = total
        mine_low_ref[...] = low


def final_grads(own, other, mask, own_head, other_head, w_down, member, count):
    rows, cols = own.shape
    width = own_head.shape[0]
    block = rows // count
    units = w_down.shape[1] // group_size()
    f32, bf16 = jnp.float32, jnp.bfloat16

    def by_rows(cols):
        return pl.BlockSpec((block, cols), lambda i, ref: (i, 0))

    head = pl.BlockSpec((width, cols), lambda i, ref: (0, 0))
    mine = pl.BlockSpec((block, width), lambda i, ref: (0, 0))
    return pl.pallas_call(
        final_kernel,
        grid_spec=pltpu.PrefetchScalarGridSpec(
            num_scalar_prefetch=1,
            grid=(count,),
            in_specs=[by_rows(cols), by_rows(cols), by_rows(1), head, head]
            + [pl.BlockSpec((width, units), lambda i, ref: (0, ref[0]))],
            out_specs=[by_rows(width), by_rows(units), mine, mine],
        ),
        out_shape=[
            jax.ShapeDtypeStruct((rows, width), bf16),
            jax.ShapeDtypeStruct((rows, units), f32),
            jax.ShapeDtypeStruct((block, width), f32),
            jax.ShapeDtypeStruct((block, width), bf16),
        ],
        compiler_params=ROOMY,
        cost_estimate=NO_COST,
    )(member, own, other, mask, own_head, other_head, w_down)


def group_mlp_kernel(
    place_ref,
    own_ref,
    other_ref,
    gain_ref,
    grad_ref,
    gate_w_ref,
    up_w_ref,
    in_ref,
    hidden_ref,
    gate_ref,
    up_ref,
):
    own, other = own_ref[0], other_ref[0]
    first = place_ref[1] == 0
    halves = [jnp.where(first, own, other), jnp.where(first, other, own)]
    low = (jnp.concatenate(halves, axis=1) * gain_ref[...]).astype(jnp.bfloat16)
    in_ref[...] = low
    units_in_halves(low, grad_ref, gate_w_ref, up_w_ref, hidden_ref, gate_ref, up_ref)


def group_mlp(own_half, other_half, gain, grad_hidden, w_gate, w_up, member):
    rows, half = grad_hidden.shape[0] // group_size(), own_half.shape[2]
    width, units = 2 * half, w_gate.shape[1] // group_size()
    bf16 = jnp.bfloat16
    place = jnp.concatenate([member, lax.axis_index("tp").astype(jnp.int32).reshape(1)])

    def by_rows(cols):
        return pl.BlockSpec((rows, cols), lambda i, ref: (i, 0))

    halves = pl.BlockSpec((1, rows, half), lambda i, ref: (i ^ ref[0], 0, 0))
    weights = pl.BlockSpec((width, units), lambda i, ref: (0, ref[0]))
    low = jax.ShapeDtypeStruct((group_size() * rows, units), bf16)
    return pl.pallas_call(
        group_mlp_kernel,
        grid_spec=pltpu.PrefetchScalarGridSpec(
            num_scalar_prefetch=1,
            grid=(group_size(),),
            in_specs=[
                halves,
                halves,
                pl.BlockSpec((1, width), lambda i, ref: (0, 0)),
                by_rows(units),
                weights,
                weights,
            ],
            out_specs=[by_rows(width), by_rows(units), by_rows(units), by_rows(units)],
        ),
        out_shape=[jax.ShapeDtypeStruct((group_size() * rows, width), bf16), low, low, low],
        compiler_params=ROOMY,
        cost_estimate=NO_COST,
    )(place, own_half, other_half, gain.reshape(1, width), grad_hidden, w_gate, w_up)


def bytes_grad_kernel(core_ref, grad_ref, weight_ref, stream_ref, out_ref, order_ref):
    places = grad_ref.shape[0]
    chunk = weight_ref.shape[1] // 8

    @pl.when(pl.program_id(0) == 0)
    def _():
        order_ref[...] = feature_order(chunk)

    by_feature = dot_plain(grad_ref[...].astype(jnp.bfloat16), weight_ref[...])
    high = by_feature.astype(jnp.bfloat16)
    rest = by_feature - high.astype(jnp.float32)
    mid = rest.astype(jnp.bfloat16)
    low = (rest - mid.astype(jnp.float32)).astype(jnp.bfloat16)
    order = order_ref[...]
    by_byte = dot_trans(high, order) + (dot_trans(mid, order) + dot_trans(low, order))
    for j in range(8):
        rows = pl.ds(j, places, stride=8)
        out_ref[rows, :] = stream_ref[rows, :] + by_byte[:, j * chunk : (j + 1) * chunk]


def bytes_grad(grad_patch, w_patch, grad_stream):
    places, width = grad_patch.shape
    rows = grad_stream.shape[0]
    cols = w_patch.shape[1]
    feature, chunk = cols // 8, 128
    core = lax.axis_index("tp").astype(jnp.int32).reshape(1)
    return pl.pallas_call(
        bytes_grad_kernel,
        grid_spec=pltpu.PrefetchScalarGridSpec(
            num_scalar_prefetch=1,
            grid=(feature // chunk,),
            in_specs=[
                pl.BlockSpec((places, width), lambda i, ref: (0, 0)),
                pl.BlockSpec((width, 8 * chunk), lambda i, ref: (0, i)),
                pl.BlockSpec((rows, chunk), lambda i, ref: (0, ref[0] * (feature // chunk) + i)),
            ],
            out_specs=pl.BlockSpec((rows, chunk), lambda i, ref: (0, i)),
            scratch_shapes=[pltpu.VMEM((8 * chunk, 8 * chunk), jnp.bfloat16)],
        ),
        out_shape=jax.ShapeDtypeStruct((rows, feature), jnp.float32),
        compiler_params=ROOMY,
        cost_estimate=NO_COST,
    )(core, grad_patch, w_patch, grad_stream)


def body(
    byte_states,
    lengths,
    w_patch,
    norm_global,
    w_in,
    conv_w,
    conv_b,
    dt_bias,
    a_log,
    d_skip,
    mix_gain,
    w_out,
    norm_attn,
    w_qkv,
    w_o,
    norm_mlp,
    w_gate,
    w_up,
    w_down,
    w_head,
    d_logits,
):
    streams, local_rows, model_width = byte_states.shape
    patch_count = local_rows // 8
    patch_total = streams * patch_count
    row_total = streams * local_rows
    feature = w_patch.shape[1] // 8
    inner_width = w_out.shape[1]
    channels = conv_w.shape[1]
    head_total = dt_bias.shape[0]
    head_cols = w_head.shape[1]
    parts = lax.axis_size("seq")
    tp_index = lax.axis_index("tp")
    seq_index = lax.axis_index("seq")
    places = parts * patch_count
    f32 = jnp.float32

    lanes = parts // streams
    width = inner_width // lanes
    full_head = inner_width // head_total
    own_heads = max(1, width // full_head)
    shared = max(1, full_head // width)
    head_size = width // own_heads
    own_stream = seq_index // lanes
    first_col = (seq_index % lanes) * width
    first_head = first_col // full_head

    seg_full = segment_ids(lengths, places)
    seg_own = lax.dynamic_slice_in_dim(seg_full, seq_index * patch_count, patch_count, 1)
    seg_stream = lax.dynamic_index_in_dim(seg_full, own_stream, 0, keepdims=False)
    valid = (seg_own < lengths.shape[0]).astype(f32).reshape(patch_total, 1)
    byte_valid = jnp.repeat(valid, 8, axis=0)

    member, members = seq_index // QUAD, group_size()
    raw_logits = d_logits.reshape(row_total, head_cols)
    raw_wide = raw_logits.astype(f32)
    group_valid = []
    for apart in range(members):
        device = seq_index ^ QUAD * apart
        group_seg = lax.dynamic_slice_in_dim(seg_full, device * patch_count, patch_count, 1)
        group_valid.append((group_seg < lengths.shape[0]).astype(f32))
    group_valid = jnp.stack(group_valid).reshape(members, patch_total, 1)
    group_bytes_valid = jnp.repeat(group_valid.reshape(-1, 1), 8, axis=0)
    apart_raw = [swap(raw_wide, "seq", QUAD * apart) for apart in range(1, members)]
    other_head = swap(w_head.astype(f32), "tp", 1)
    place_index = member.astype(jnp.int32).reshape(1)
    bytes_wide, patch_part = patch_in(byte_states.reshape(row_total, model_width), w_patch)
    patch_out = tp_sum(patch_part)
    gain_global = norm_global.astype(f32)
    unit_patch = patch_out * rms_scale(patch_out)
    u_low = (unit_patch * gain_global).astype(jnp.bfloat16)
    half_width = model_width // 2
    proj = dot_plain(u_low, w_in).reshape(streams, patch_count, -1)
    gate_in = proj[..., :inner_width]
    xbc = proj[..., inner_width : inner_width + channels]
    dt_raw = proj[..., inner_width + channels :]

    def by_lane(columns):
        split = columns.reshape(streams, patch_count, lanes, -1)
        return jnp.moveaxis(split, 2, 1).reshape(parts, patch_count, -1)

    def from_lanes(blocks):
        split = blocks.reshape(streams, lanes, patch_count, -1)
        return jnp.moveaxis(split, 1, 2).reshape(streams, patch_count, -1)

    def to_all_lanes(columns):
        wide = jnp.broadcast_to(
            columns[:, None], (streams, lanes, patch_count, columns.shape[-1])
        )
        return wide.reshape(parts, patch_count, -1)

    pad_width = 128 - own_heads
    dt_lanes = by_lane(jnp.repeat(dt_raw, shared, axis=2))
    sent = jnp.concatenate(
        [
            by_lane(xbc[..., :inner_width]),
            to_all_lanes(xbc[..., inner_width:]),
            jnp.pad(dt_lanes, ((0, 0), (0, 0), (0, pad_width))),
        ],
        axis=-1,
    )
    taken = trade(sent)
    grad_logits = raw_logits * byte_valid.astype(jnp.bfloat16)
    unused, unused_part, grad_final, grad_mlp_low = final_grads(
        after(raw_wide, sent),
        swap(raw_wide, "tp", 1),
        byte_valid,
        w_head,
        other_head,
        w_down,
        place_index,
        1,
    )
    grad_hidden = dot_plain(grad_mlp_low, w_down)
    hidden_part = w_gate.shape[1] // members

    row_side = [
        [device for device in range(parts) if (device & 1) == side] for side in range(2)
    ]
    bytes_all = lax.all_gather(
        bytes_wide, "seq", axis=0, axis_index_groups=row_side, tiled=True
    )
    taken = after(taken, bytes_wide, grad_hidden).reshape(places, -1)
    scan_width = width + channels - inner_width

    def own_cols(param):
        mine = lax.dynamic_slice_in_dim(param, first_col, width, param.ndim - 1)
        return jnp.concatenate([mine, param[..., inner_width:]], axis=-1).astype(f32)

    def own_head(param):
        return lax.dynamic_slice_in_dim(param, first_head, own_heads, 0).astype(f32)

    use_kernel = places == 512 and width == 128
    if use_kernel:
        padded_seg = jnp.pad(seg_stream, (3, 0), constant_values=-1)
        same = jnp.stack(
            [(padded_seg[k : k + places] == seg_stream).astype(f32) for k in range(3)]
            + [jnp.zeros((places,), f32)] * 5,
            axis=1,
        )
        conv_pack = jnp.concatenate(
            [own_cols(conv_w), own_cols(conv_b)[None], jnp.zeros((3, scan_width), f32)]
        )
        head_pack = jnp.stack(
            [jnp.pad(own_head(dt_bias), (0, 128 - own_heads))]
            + [jnp.pad(own_head(a_log), (0, 128 - own_heads))]
            + [jnp.repeat(own_head(d_skip), head_size)]
            + [jnp.zeros((128,), f32)] * 5
        )
        scan_args = (taken, same, conv_pack, head_pack, seg_stream[:, None], seg_stream[None])
        scanned = scan_forward(scan_args, width)
    else:
        scan_args = (
            taken[:, :scan_width],
            taken[:, scan_width : scan_width + own_heads],
            own_cols(conv_w),
            own_cols(conv_b),
            own_head(dt_bias),
            own_head(a_log),
            own_head(d_skip),
        )
        scanned, scan_back = jax.vjp(partial(scan_heads, seg_stream, head_size), *scan_args)
    result = trade(scanned.reshape(parts, patch_count, width))
    result = from_lanes(result)
    unit_normed, norm_back = jax.vjp(gated_unit, result, gate_in)
    mix_scale = mix_gain.astype(f32)
    normed_low = (unit_normed * mix_scale).reshape(patch_total, -1).astype(jnp.bfloat16)


    def quarters(columns):
        split = columns.reshape(patch_total, members, -1)
        return jnp.moveaxis(split, 1, 0)

    def by_apart(blocks):
        return [
            lax.dynamic_index_in_dim(blocks, member ^ apart, 0, keepdims=False)
            for apart in range(members)
        ]

    def group_swap(blocks):
        return [blocks[0]] + [swap(blocks[k], "seq", QUAD * k) for k in range(1, members)]

    def joined(blocks, turn):
        return jnp.concatenate([after(block, turn) for block in blocks], axis=0)

    early_got = group_swap(
        [
            jnp.concatenate([unit_patch, part], axis=-1)
            for part in by_apart(quarters(unit_normed))
        ]
    )
    global_out = patch_out + valid * tp_sum(dot_trans(normed_low, w_out))
    gain_attn = norm_attn.astype(f32)
    gain_mlp = norm_mlp.astype(f32)
    stream_in, attn_in, qkv, mixed_low, attn_part = attn_forward(
        byte_states.reshape(row_total, model_width), global_out, gain_attn, w_qkv, w_o
    )
    after_attn, mlp_low, unit_half = mlp_in(
        stream_in, attn_part, swap(attn_part, "tp", 1), gain_mlp
    )
    hidden_low, grad_gate_low, grad_up_low, grad_mlp_part = mlp_rows(
        after(mlp_low, unit_half), grad_hidden, w_gate, w_up
    )
    group_halves = group_trade(jnp.broadcast_to(unit_half[None], (members,) + unit_half.shape))
    grad_mlp_other = swap(grad_mlp_part, "tp", 1)
    after_mlp = after_attn + tp_sum(dot_trans(after(hidden_low, grad_mlp_part), w_down))
    final_low = after_mlp.astype(jnp.bfloat16)
    logits = dot_plain(final_low, w_head) * byte_valid
    grad_mid, grad_attn_low, grad_qkv_low, grad_attn_part, grad_norm_mlp = attn_backward(
        after_attn, grad_final, grad_mlp_part, grad_mlp_other, gain_mlp, qkv, w_qkv, w_o
    )
    grad_norm_mlp = grad_norm_mlp.reshape(-1)
    grad_attn_in = tp_sum(grad_attn_part)

    back_attn, grad_norm_attn = rms_back(stream_in, gain_attn, grad_attn_in)
    grad_stream = grad_mid + back_attn
    grad_global = jnp.sum(grad_stream.reshape(patch_total, 8, model_width), axis=1)
    grad_mix_low = (grad_global * valid).astype(jnp.bfloat16)
    grad_normed = dot_plain(grad_mix_low, w_out).reshape(streams, patch_count, inner_width)
    grad_mix_gain = jnp.sum(grad_normed * unit_normed, axis=(0, 1))
    grad_result, grad_gate_in = norm_back(grad_normed * mix_scale)
    grad_z_low = grad_gate_in.reshape(patch_total, inner_width).astype(jnp.bfloat16)
    row_block = model_width // parts
    group_raw = jnp.concatenate(
        [raw_wide] + [after(raw, grad_normed) for raw in apart_raw], axis=0
    )
    other_raw = swap(group_raw, "tp", 1)
    group_final, group_grad_hidden, unused, unused_part = final_grads(
        group_raw,
        other_raw,
        group_bytes_valid,
        w_head,
        other_head,
        w_down,
        place_index,
        members,
    )
    dealing = after(by_lane(grad_result), bytes_all, group_halves)
    dealt = trade(dealing)
    late_sent = [
        jnp.concatenate([grad_global, part], axis=-1) for part in by_apart(quarters(grad_gate_in))
    ]
    late_got = group_swap(late_sent)
    attn_cut = 1024 if grad_qkv_low.shape[1] > 1024 else 128
    attn_in_late = after(attn_in, dealing)
    attn_cols = grad_qkv_low.shape[1]
    attn_blocks = (
        grad_blocks([(attn_in_late, grad_qkv_low, 0, attn_cut)], 0, True),
        grad_blocks(
            [
                (attn_in_late, grad_qkv_low, attn_cut, attn_cols),
                (grad_attn_low, mixed_low, 0, mixed_low.shape[1]),
                (final_low, grad_logits, 0, head_cols),
            ],
            1,
            True,
        ),
    )
    attn_got = [to_partner(attn_blocks[first][0], first) for first in range(2)]
    dealt = after(dealt, attn_blocks[0][0], attn_blocks[1][0])
    grad_scanned = dealt.reshape(places, width)
    if use_kernel:
        back_sent, conv_grads, head_grads = scan_backward(scan_args, grad_scanned)
        lane_grad = back_sent[:, : scan_width + own_heads]
        scan_params = (
            conv_grads[:4],
            conv_grads[4],
            head_grads[0, :own_heads],
            head_grads[1, :own_heads],
            head_grads[2, :own_heads],
        )
    else:
        scan_grads = scan_back(grad_scanned)
        back_sent = jnp.concatenate(
            [scan_grads[0], jnp.pad(scan_grads[1], ((0, 0), (0, pad_width)))], axis=-1
        )
        lane_grad = jnp.concatenate([scan_grads[0], scan_grads[1]], axis=-1)
        scan_params = scan_grads[2:]
    back_sent = back_sent.reshape(parts, patch_count, -1)
    back_taken = trade(back_sent)
    own_half = after(group_halves, back_sent)
    group_in, group_hidden, group_gate, group_up = group_mlp(
        own_half, swap(own_half, "tp", 1), gain_mlp, group_grad_hidden, w_gate, w_up, place_index
    )
    first_set = grad_blocks(
        [
            (group_final, group_hidden, 0, hidden_part),
            (group_in, group_gate, 0, hidden_part),
        ],
        0,
        True,
    )
    late_got = joined(late_got, first_set[0])
    apart_valid = group_valid.reshape(-1, 1)
    group_mix = (late_got[:, :model_width] * apart_valid).astype(jnp.bfloat16)
    group_z = late_got[:, model_width:]
    late_early = joined(early_got, first_set[0])
    group_u = (late_early[:, :model_width] * gain_global).astype(jnp.bfloat16)
    quarter = inner_width // members
    own_scale = lax.dynamic_slice_in_dim(mix_scale, member * quarter, quarter, 0)
    group_n = (late_early[:, model_width:] * own_scale).astype(jnp.bfloat16)
    attn_far = [
        add_side(after(attn_blocks[first][1], first_set[0]), attn_got[first], 1)
        for first in range(2)
    ]
    attn_crossed = [to_partner(attn_far[first], 1 - first) for first in range(2)]
    mlp_blocks = [
        first_set,
        grad_blocks(
            [
                (group_in, after(group_up, *attn_far), 0, hidden_part),
                (group_mix, group_n, 0, group_n.shape[1]),
                (group_u, group_z, 0, group_z.shape[1]),
            ],
            1,
            True,
        ),
    ]
    mlp_got = [to_partner(mlp_blocks[first][0], first) for first in range(2)]
    back_taken = after(back_taken, mlp_blocks[0][0], mlp_blocks[1][0])
    grad_x = from_lanes(back_taken[..., :width])
    by_stream = back_taken.reshape(streams, lanes, patch_count, -1)
    grad_bc = jnp.sum(by_stream[..., width:scan_width], axis=1)
    grad_dt = from_lanes(back_taken[..., scan_width : scan_width + own_heads])
    grad_dt = jnp.sum(grad_dt.reshape(streams, patch_count, head_total, shared), axis=-1)
    grad_shared = jnp.concatenate([grad_bc, grad_dt], axis=-1).reshape(patch_total, -1)
    grad_proj_low = jnp.concatenate(
        [grad_z_low, grad_x.reshape(patch_total, -1).astype(jnp.bfloat16)]
        + [grad_shared.astype(jnp.bfloat16)],
        axis=-1,
    )
    grad_u_part = dot_trans(grad_proj_low, w_in)
    grad_u = tp_sum(grad_u_part)
    back_global, grad_norm_global = rms_back(patch_out, gain_global, grad_u)
    grad_patch = grad_global + back_global
    side_count = parts // 2
    my_side = seq_index & 1
    by_block = jnp.moveaxis(grad_patch.reshape(patch_total, parts, row_block), 1, 0)
    by_block = by_block.reshape(side_count, 2, patch_total, row_block)
    same_side = lax.dynamic_index_in_dim(by_block, my_side, 1, keepdims=False)
    other_side = lax.dynamic_index_in_dim(by_block, 1 - my_side, 1, keepdims=False)
    patch_rows = jnp.concatenate([same_side, other_side], axis=-1)
    patch_rows = patch_rows.reshape(side_count, patch_total, 2 * row_block)
    gain_part = grad_norm_global.reshape(-1, 2 * row_block)
    gain_count = gain_part.shape[0]
    patch_sent = jnp.concatenate(
        [patch_rows, jnp.broadcast_to(gain_part, (side_count,) + gain_part.shape)], axis=1
    )
    patch_taken = lax.all_to_all(
        patch_sent, "seq", 0, 0, axis_index_groups=row_side, tiled=True
    )

    mlp_far = [
        add_side(after(mlp_blocks[first][1], patch_sent), mlp_got[first], 1)
        for first in range(2)
    ]
    mlp_crossed = [to_partner(mlp_far[first], 1 - first) for first in range(2)]
    patch_taken = after(patch_taken, *mlp_far)
    gain_side = jnp.sum(patch_taken[:, patch_total:], axis=0)
    patch_cols = patch_taken[:, :patch_total].reshape(-1, 2 * row_block)
    patch_far = patch_far_grad(patch_cols, gain_side, bytes_all)
    small = (
        scan_params[0][:, :width],
        scan_params[1][:width],
        scan_params[0][:, width:],
        scan_params[1][width:],
        scan_params[2],
        scan_params[3],
        scan_params[4],
        grad_mix_gain,
        grad_norm_attn,
        grad_norm_mlp,
    )
    small_count = sum(part.size for part in small)
    flat = after(jnp.concatenate([part.reshape(-1) for part in small]), patch_far)
    flat = jnp.pad(flat, (0, -small_count % 1024)).reshape(1, -1, 128)
    pieces = trade(jnp.broadcast_to(flat, (parts,) + flat.shape[1:])).reshape(parts, -1)
    by_small, at = [], 0
    for part in small:
        got = pieces[:, at : at + part.size].reshape((parts,) + part.shape)
        by_small.append(got)
        at += part.size

    def lane_cols(got):
        joined = jnp.sum(got.reshape((streams, lanes) + got.shape[1:]), axis=0)
        return jnp.moveaxis(joined, 0, -2).reshape(joined.shape[1:-1] + (-1,))

    def lane_heads(got):
        joined = jnp.sum(got.reshape(streams, lanes, -1), axis=0)
        return jnp.sum(joined.reshape(head_total, shared), axis=-1)

    small_sums = [
        jnp.concatenate([lane_cols(by_small[0]), jnp.sum(by_small[2], axis=0)], axis=-1),
        jnp.concatenate([lane_cols(by_small[1]), jnp.sum(by_small[3], axis=0)], axis=-1),
        lane_heads(by_small[4]),
        lane_heads(by_small[5]),
        lane_heads(by_small[6]),
    ] + [jnp.sum(got, axis=0) for got in by_small[7:]]

    patch_got = to_partner(patch_far, 0)

    high = (seq_index // QUAD).astype(jnp.int32).reshape(1)
    attn_near = near_sums(
        [
            (after(attn_blocks[first][1], patch_far), attn_got[first], attn_crossed[first])
            for first in range(2)
        ],
        high,
    )
    attn_high = [
        swap(attn_near[apart], "seq", QUAD * apart) for apart in range(1, parts // QUAD)
    ]
    rest = [quarters(columns) for columns in (grad_x, grad_bc, grad_dt)]
    rest_cols = [part.shape[-1] for part in rest]
    rest = after(jnp.concatenate(rest, axis=-1), patch_far)
    rest = jnp.pad(rest, ((0, 0), (0, 0), (0, -sum(rest_cols) % 128)))
    rest_blocks = grad_blocks(
        [(group_u, joined(group_swap(by_apart(rest)), patch_far), 0, rest.shape[-1])], 0, True
    )
    rest_got = to_partner(after(rest_blocks[0], patch_far), 0)
    start = jnp.zeros((1,), jnp.int32)
    mlp_near = [
        near_sums(
            [(after(mlp_blocks[first][1], attn_near, patch_got), mlp_got[first], mlp_crossed[first])],
            start,
        )
        for first in range(2)
    ]
    final_attn = attn_near[0]
    for got in attn_high:
        final_attn = final_attn + after(got, *mlp_near)
    rest_far = add_side(after(rest_blocks[1], *mlp_near), rest_got, 1)
    rest_crossed = to_partner(rest_far, 1)
    mlp_finals = [jnp.moveaxis(group_trade(part), 0, 1) for part in mlp_near]
    rest_near = near_sums(
        [(after(rest_blocks[1], final_attn, *mlp_finals), rest_got, rest_crossed)], start
    )
    mlp_finals.append(jnp.moveaxis(group_trade(rest_near), 0, 1))

    def final_cols(final, low, count):
        return final[..., low : low + count].reshape(row_block, -1)

    final_down = final_cols(mlp_finals[0], 0, hidden_part)
    final_gate = final_cols(mlp_finals[0], hidden_part, hidden_part)
    final_up = final_cols(mlp_finals[1], 0, hidden_part)
    final_out = final_cols(mlp_finals[1], hidden_part, quarter)
    final_z = final_cols(mlp_finals[1], hidden_part + quarter, quarter)
    final_x = final_cols(mlp_finals[2], 0, rest_cols[0])
    final_bc = final_cols(mlp_finals[2], rest_cols[0], rest_cols[1])
    final_dt = final_cols(mlp_finals[2], rest_cols[0] + rest_cols[1], rest_cols[2])
    final_patch = patch_grad(patch_cols, patch_got, bytes_all)
    norm_global_sum = (gain_side + patch_got[row_block:, : 2 * row_block]).reshape(-1)
    grad_bytes = bytes_grad(after(grad_patch, patch_far), w_patch, grad_stream)
    grad_bytes = grad_bytes.reshape(streams, local_rows, feature)

    qkv_cols, o_cols = w_qkv.shape[1], w_o.shape[1]
    return (
        logits.reshape(streams, local_rows, head_cols),
        grad_bytes,
        final_patch,
        norm_global_sum,
        jnp.concatenate([final_z, final_x, final_bc, final_dt], axis=1),
        small_sums[0],
        small_sums[1],
        small_sums[2],
        small_sums[3],
        small_sums[4],
        small_sums[5],
        final_out,
        small_sums[6],
        final_attn[:, :qkv_cols],
        final_attn[:, qkv_cols : qkv_cols + o_cols],
        small_sums[7],
        final_gate,
        final_up,
        final_down,
        final_attn[:, qkv_cols + o_cols :],
    )


def solution(mesh):
    in_specs = (
        P(None, "seq", None),
        P(),
        P(None, "tp"),
        P(),
        P(None, "tp"),
        P(None, "tp"),
        P("tp"),
        P("tp"),
        P("tp"),
        P("tp"),
        P("tp"),
        P(None, "tp"),
        P(),
        P(None, "tp"),
        P(None, "tp"),
        P(),
        P(None, "tp"),
        P(None, "tp"),
        P(None, "tp"),
        P(None, "tp"),
        P(None, "seq", "tp"),
    )
    out_specs = (
        P(None, "seq", "tp"),
        P(None, "seq", "tp"),
        P("seq", "tp"),
        P(),
        P("seq", "tp"),
        P(None, "tp"),
        P("tp"),
        P("tp"),
        P("tp"),
        P("tp"),
        P("tp"),
        P("seq", "tp"),
        P(),
        P("seq", "tp"),
        P("seq", "tp"),
        P(),
        P("seq", "tp"),
        P("seq", "tp"),
        P("seq", "tp"),
        P("seq", "tp"),
    )
    return jax.shard_map(body, mesh=mesh, in_specs=in_specs, out_specs=out_specs, check_vma=False)
```

```python
from functools import partial

import jax
import jax.numpy as jnp
from jax import lax
from jax.experimental import pallas as pl
from jax.experimental.pallas import tpu as pltpu
from jax.sharding import PartitionSpec as P

NS = 128
AD = 64
QUAD = 4


NO_COST = pl.CostEstimate(flops=1024, bytes_accessed=1024, transcendentals=0)
ROOMY = pltpu.CompilerParams(vmem_limit_bytes=56 * 1024 * 1024)

epsilon = 1e-05
highest = lax.Precision.HIGHEST
masked_score = -1e30


def dot_plain(left_side, right_side):
    return jnp.dot(left_side, right_side, preferred_element_type=jnp.float32)


def dot_trans(left_side, right_side):
    return lax.dot_general(
        left_side, right_side, (((1,), (1,)), ((), ())), preferred_element_type=jnp.float32
    )


def dot_left(left_side, right_side):
    return lax.dot_general(
        left_side, right_side, (((0,), (0,)), ((), ())), preferred_element_type=jnp.float32
    )


def rms_scale(values):
    return lax.rsqrt(jnp.mean(values * values, axis=-1, keepdims=True) + epsilon)


def hidden_parts(mlp_in, grad_hidden, w_gate, w_up):
    gate_proj = dot_plain(mlp_in, w_gate)
    up_proj = dot_plain(mlp_in, w_up)
    sigmoid_gate = jax.nn.sigmoid(gate_proj)
    hidden_low = (gate_proj * sigmoid_gate * up_proj).astype(jnp.bfloat16)
    grad_gate_low = (
        grad_hidden * up_proj * sigmoid_gate * (1.0 + gate_proj * (1.0 - sigmoid_gate))
    ).astype(jnp.bfloat16)
    grad_up_low = (grad_hidden * gate_proj * sigmoid_gate).astype(jnp.bfloat16)
    return (hidden_low, grad_gate_low, grad_up_low)


def rms_back(values, gain_values, grad_out):
    scale = rms_scale(values)
    scaled = gain_values * grad_out
    inner_mean = jnp.mean(values * scaled, axis=-1, keepdims=True)
    grad_values = scale * scaled - values * scale * scale * scale * inner_mean
    grad_gain = jnp.sum(values * scale * grad_out, axis=0)
    return (grad_values, grad_gain)


def swap(block, axis, mask):
    return lax.ppermute(block, axis, [(i, i ^ mask) for i in range(lax.axis_size(axis))])


def after(value, *earlier):
    return lax.optimization_barrier((value,) + earlier)[0]


def tp_sum(block):
    return block + swap(block, "tp", 1)


def to_partner(block, bit):
    return swap(block, "seq", 1 << bit)


def seq_bits():
    return lax.axis_size("seq").bit_length() - 1


def group_size():
    return lax.axis_size("seq") // QUAD


def group_trade(blocks):
    members = [[low + QUAD * high for high in range(group_size())] for low in range(QUAD)]
    return lax.all_to_all(blocks, "seq", 0, 0, axis_index_groups=members, tiled=True)


def add_kernel(index_ref, *refs):
    total = refs[0][...] + refs[1][...]
    refs[2][...] = total.reshape(refs[2].shape)


def add_side(near, got, side):
    unused, groups, rows, cols = near.shape
    index = jnp.zeros((1,), jnp.int32)
    block = pl.BlockSpec((1, 1, rows, cols), lambda i, ref: (side, i, 0, 0))
    return pl.pallas_call(
        add_kernel,
        grid_spec=pltpu.PrefetchScalarGridSpec(
            num_scalar_prefetch=1,
            grid=(groups,),
            in_specs=[block, block],
            out_specs=pl.BlockSpec((1, rows, cols), lambda i, ref: (i, 0, 0)),
        ),
        out_shape=jax.ShapeDtypeStruct((groups, rows, cols), jnp.float32),
        compiler_params=ROOMY,
        cost_estimate=NO_COST,
    )(index, near, got)


def near_kernel(index_ref, *refs):
    out_ref = refs[-1]
    at = 0
    for near_ref, got_ref, crossed_ref in zip(refs[0:-1:3], refs[1:-1:3], refs[2:-1:3]):
        cols = near_ref.shape[3]
        total = near_ref[0, 0] + got_ref[0, 0] + crossed_ref[0]
        out_ref[0, :, at : at + cols] = total
        at += cols


def near_sums(terms, high):
    unused, groups, rows, unused_cols = terms[0][0].shape
    cols = [term[0].shape[3] for term in terms]
    specs, operands = [], []
    for (near, got, crossed), count in zip(terms, cols):
        four = pl.BlockSpec((1, 1, rows, count), lambda i, ref: (0, ref[0] ^ i, 0, 0))
        three = pl.BlockSpec((1, rows, count), lambda i, ref: (ref[0] ^ i, 0, 0))
        specs += [four, four, three]
        operands += [near, got, crossed]
    return pl.pallas_call(
        near_kernel,
        grid_spec=pltpu.PrefetchScalarGridSpec(
            num_scalar_prefetch=1,
            grid=(groups,),
            in_specs=specs,
            out_specs=pl.BlockSpec((1, rows, sum(cols)), lambda i, ref: (i, 0, 0)),
        ),
        out_shape=jax.ShapeDtypeStruct((groups, rows, sum(cols)), jnp.float32),
        compiler_params=ROOMY,
        cost_estimate=NO_COST,
    )(high, *operands)


def grad_blocks_kernel(pairs, first, relative, rows, member_ref, *refs):
    lefts, rights = refs[: len(pairs)], refs[len(pairs) : 2 * len(pairs)]
    far_ref, near_ref = refs[2 * len(pairs) :]
    other = 1 - first
    at = 0
    for left_ref, right_ref, (low, high) in zip(lefts, rights, pairs):
        got = dot_left(left_ref[...], right_ref[:, low:high].astype(jnp.bfloat16))
        places = slice(at, at + high - low)
        for block in range(got.shape[0] // rows):
            place, member = block // QUAD, block % QUAD
            part = got[block * rows : (block + 1) * rows]
            apart = member_ref[0] ^ member
            is_far = apart >> first & 1
            if relative:
                side = apart >> other & 1
            else:
                side = member >> other & 1

            @pl.when(is_far == 1)
            def _():
                if relative:
                    far_ref[side, place, :, places] = part
                else:
                    far_ref[place, side, :, places] = part

            @pl.when(is_far == 0)
            def _():
                if relative:
                    near_ref[side, place, :, places] = part
                else:
                    near_ref[place, side, :, places] = part

        at += high - low


def grad_blocks(terms, first, relative):
    parts = lax.axis_size("seq")
    groups = parts // QUAD
    model_width = terms[0][0].shape[1]
    rows = model_width // parts
    cols = max(128, QUAD * rows)
    places = cols // (QUAD * rows)
    pairs = [(low, high) for unused, unused_right, low, high in terms]
    total = sum(high - low for low, high in pairs)
    member = (lax.axis_index("seq") % QUAD).astype(jnp.int32).reshape(1)
    if relative:
        shape, block = (2, groups, rows, total), (2, places, rows, total)
        out_spec = pl.BlockSpec(block, lambda i, ref: (0, i, 0, 0))
    else:
        shape, block = (groups, 2, rows, total), (places, 2, rows, total)
        out_spec = pl.BlockSpec(block, lambda i, ref: (i, 0, 0, 0))
    out = jax.ShapeDtypeStruct(shape, jnp.float32)
    return pl.pallas_call(
        partial(grad_blocks_kernel, pairs, first, relative, rows),
        grid_spec=pltpu.PrefetchScalarGridSpec(
            num_scalar_prefetch=1,
            grid=(model_width // cols,),
            in_specs=[
                pl.BlockSpec((term[0].shape[0], cols), lambda i, ref: (0, i)) for term in terms
            ]
            + [pl.BlockSpec(term[1].shape, lambda i, ref: (0, 0)) for term in terms],
            out_specs=[out_spec, out_spec],
        ),
        out_shape=[out, out],
        compiler_params=ROOMY,
        cost_estimate=NO_COST,
    )(member, *[term[0] for term in terms], *[term[1] for term in terms])


def segment_ids(lengths, place_count):
    ends = jnp.cumsum(lengths // 8, dtype=jnp.int32)
    places = jnp.arange(place_count, dtype=jnp.int32)
    short_ids = jnp.sum(
        (places[:, None] >= ends[None, :]).astype(jnp.int32), axis=1, dtype=jnp.int32
    )
    return jnp.stack([jnp.zeros_like(short_ids), short_ids])


def scan_heads(seg_now, head_size, xbc, dt_raw, conv_weight, conv_bias, dt_shift, a_logs, skips):
    place_count = xbc.shape[0]
    conv_sum = conv_bias + conv_weight[3] * xbc
    for offset in range(3):
        distance = 3 - offset
        earlier = jnp.pad(xbc, ((distance, 0), (0, 0)))[:place_count]
        seg_earlier = jnp.pad(seg_now, (distance, 0), constant_values=-1)[:place_count]
        same_doc = (seg_earlier == seg_now).astype(jnp.float32)
        conv_sum = conv_sum + conv_weight[offset] * earlier * same_doc[:, None]
    active = jax.nn.silu(conv_sum)
    head_count = dt_raw.shape[1]
    inner = head_count * head_size
    values = active[:, :inner].reshape(place_count, head_count, head_size)
    in_keys = active[:, inner : inner + NS]
    out_keys = active[:, inner + NS :]
    step_sizes = jax.nn.softplus(dt_raw + dt_shift)
    decay_rates = -step_sizes * jnp.exp(a_logs)
    chunk = min(place_count, 512)
    triangle = jnp.tril(jnp.ones((chunk, chunk), jnp.float32))
    state = jnp.zeros((head_count, head_size, NS), jnp.float32)
    seg_last = jnp.int32(-1)
    outputs = []
    for start in range(0, place_count, chunk):
        stop = start + chunk
        x, b, c = values[start:stop], in_keys[start:stop], out_keys[start:stop]
        dt, seg = step_sizes[start:stop], seg_now[start:stop]
        cumulative = jnp.dot(triangle, decay_rates[start:stop], precision=highest)
        allowed = (triangle > 0.0) & (seg[:, None] == seg[None, :])
        ordered = cumulative.T
        gaps = ordered[:, :, None] - ordered[:, None, :]
        decays = jnp.where(allowed, jnp.exp(jnp.where(allowed, gaps, 0.0)), 0.0)
        crossing = jnp.einsum("pn,jn->pj", c, b, precision=highest)
        mixing = crossing[None] * decays * dt.T[:, None, :]
        result = jnp.einsum("hpj,jhd->phd", mixing, x, precision=highest)
        if start > 0:
            entering = jnp.exp(cumulative) * (seg == seg_last).astype(jnp.float32)[:, None]
            result = result + entering[..., None] * jnp.einsum(
                "pn,hdn->phd", c, state, precision=highest
            )
        if stop < place_count:
            last_same = (seg == seg[-1]).astype(jnp.float32)[:, None]
            weight = jnp.exp(cumulative[-1:] - cumulative) * last_same * dt
            through = jnp.exp(cumulative[-1]) * (seg[-1] == seg_last).astype(jnp.float32)
            state = through[:, None, None] * state + jnp.einsum(
                "jh,jhd,jn->hdn", weight, x, b, precision=highest
            )
            seg_last = seg[-1]
        outputs.append(result + skips[:, None] * x)
    return jnp.concatenate(outputs, axis=0).reshape(place_count, inner)


def gated_unit(result, gate_in):
    gated = result * jax.nn.silu(gate_in)
    return gated * rms_scale(gated)


def patch_far_kernel(grad_ref, gain_ref, bytes_ref, out_ref):
    half = grad_ref.shape[1] // 2
    grad_low = grad_ref[:, half:].astype(jnp.bfloat16)
    out_ref[:half] = dot_left(grad_low, bytes_ref[...].astype(jnp.bfloat16))
    out_ref[half:] = jnp.zeros((out_ref.shape[0] - half, out_ref.shape[1]), jnp.float32)

    @pl.when(pl.program_id(0) == 0)
    def _():
        out_ref[half:, : 2 * half] = gain_ref[...]


def patch_far_grad(grad_rows, gain_part, bytes_all):
    places, cols = grad_rows.shape
    total = bytes_all.shape[1]
    rows = cols // 2 + gain_part.shape[0]
    block = 1024
    return pl.pallas_call(
        patch_far_kernel,
        grid=(total // block,),
        in_specs=[
            pl.BlockSpec((places, cols), lambda i: (0, 0)),
            pl.BlockSpec(gain_part.shape, lambda i: (0, 0)),
            pl.BlockSpec((places, block), lambda i: (0, i)),
        ],
        out_specs=pl.BlockSpec((rows, block), lambda i: (0, i)),
        out_shape=jax.ShapeDtypeStruct((rows, total), jnp.float32),
        compiler_params=ROOMY,
        cost_estimate=NO_COST,
    )(grad_rows, gain_part, bytes_all)


def patch_grad_kernel(grad_ref, *refs):
    byte_refs, got_refs, out_ref, order_ref = refs[:8], refs[8:16], refs[16], refs[17]
    width = byte_refs[0].shape[1]

    @pl.when(pl.program_id(0) == 0)
    def _():
        order_ref[...] = feature_order(width)

    grad_low = grad_ref[:, : grad_ref.shape[1] // 2].astype(jnp.bfloat16)
    wide = jnp.concatenate([ref[...].astype(jnp.bfloat16) for ref in byte_refs], axis=1)
    rows = grad_low.shape[1]
    grad = dot_left(grad_low, wide)
    grad = grad + jnp.concatenate([ref[:rows] for ref in got_refs], axis=1)
    high = grad.astype(jnp.bfloat16)
    rest = grad - high.astype(jnp.float32)
    mid = rest.astype(jnp.bfloat16)
    low = (rest - mid.astype(jnp.float32)).astype(jnp.bfloat16)
    order = order_ref[...]
    out_ref[...] = dot_plain(high, order) + (dot_plain(mid, order) + dot_plain(low, order))


def patch_grad(grad_rows, got, bytes_all):
    places, cols = grad_rows.shape
    feature = bytes_all.shape[1] // 8
    chunk = 128
    steps = feature // chunk

    def byte_specs(rows):
        return [
            pl.BlockSpec((rows, chunk), partial(lambda j, i: (0, j * steps + i), j))
            for j in range(8)
        ]

    return pl.pallas_call(
        patch_grad_kernel,
        grid=(steps,),
        in_specs=[pl.BlockSpec((places, cols), lambda i: (0, 0))]
        + byte_specs(places)
        + byte_specs(got.shape[0]),
        out_specs=pl.BlockSpec((cols // 2, 8 * chunk), lambda i: (0, i)),
        out_shape=jax.ShapeDtypeStruct((cols // 2, 8 * feature), jnp.float32),
        scratch_shapes=[pltpu.VMEM((8 * chunk, 8 * chunk), jnp.bfloat16)],
        compiler_params=ROOMY,
        cost_estimate=NO_COST,
    )(grad_rows, *([bytes_all] * 8), *([got] * 8))


def trade(blocks):
    return lax.all_to_all(blocks, "seq", 0, 0, tiled=True)


def grid_iota(shape, axis):
    return lax.broadcasted_iota(jnp.int32, shape, axis)


def dot_fine(left_side, right_side, left_axis, right_axis):
    return lax.dot_general(
        left_side,
        right_side,
        (((left_axis,), (right_axis,)), ((), ())),
        preferred_element_type=jnp.float32,
        precision=highest,
    )


def shifted_down(block, distance):
    rows = grid_iota(block.shape, 0)
    return jnp.where(rows >= distance, pltpu.roll(block, distance, 0), 0.0)


def shifted_up(block, distance):
    count = block.shape[0]
    rows = grid_iota(block.shape, 0)
    return jnp.where(rows < count - distance, pltpu.roll(block, count - distance, 0), 0.0)


def scan_terms(taken_ref, same_ref, conv_ref, head_ref):
    places = taken_ref.shape[0]
    channels = conv_ref.shape[1]
    xbc = taken_ref[:, :channels]
    conv_sum = conv_ref[4:5] + conv_ref[3:4] * xbc
    for k in range(3):
        earlier = shifted_down(xbc, 3 - k) * same_ref[:, k : k + 1]
        conv_sum = conv_sum + conv_ref[k : k + 1] * earlier
    gate = jax.nn.sigmoid(conv_sum)
    active = conv_sum * gate
    raw = taken_ref[:, channels:] + head_ref[0:1]
    steps = jnp.maximum(raw, 0.0) + jnp.log1p(jnp.exp(-jnp.abs(raw)))
    rates = -steps * jnp.exp(head_ref[1:2])
    square = (places, places)
    triangle = jnp.where(grid_iota(square, 0) >= grid_iota(square, 1), 1.0, 0.0)
    running = dot_fine(triangle, rates, 1, 0)
    return xbc, conv_sum, gate, active, raw, steps, rates, triangle, running


def scan_forward_kernel(taken_ref, same_ref, conv_ref, head_ref, seg_col, seg_row, out_ref):
    places, width = out_ref.shape
    terms = scan_terms(taken_ref, same_ref, conv_ref, head_ref)
    active, steps, running = terms[3], terms[5], terms[8]
    values = active[:, :width]
    keys, reads = active[:, width : width + NS], active[:, width + NS :]
    steps_row, running_row = steps.T, running.T
    heads = width // 64
    rows = 128
    for first in range(0, places, rows):
        last = first + rows
        shape = (rows, last)
        allowed = (seg_col[first:last] == seg_row[:, :last]) & (
            grid_iota(shape, 0) + first >= grid_iota(shape, 1)
        )
        crossing = dot_fine(reads[first:last], keys[:last], 1, 1)
        lane = grid_iota((rows, width), 1) // 64
        total = head_ref[2:3] * values[first:last]
        for h in range(heads):
            gaps = running[first:last, h : h + 1] - running_row[h : h + 1, :last]
            decays = jnp.exp(jnp.where(allowed, gaps, masked_score))
            mixing = crossing * decays * steps_row[h : h + 1, :last]
            part = dot_fine(mixing, values[:last], 1, 0)
            total = total + jnp.where(lane == h, part, 0.0)
        out_ref[first:last] = total


def scan_backward_kernel(
    taken_ref,
    same_ref,
    conv_ref,
    head_ref,
    seg_col,
    seg_row,
    grad_ref,
    out_ref,
    conv_grad_ref,
    head_grad_ref,
    values_grad,
    keys_grad,
    reads_grad,
    rows_grad,
    cols_grad,
):
    places, width = values_grad.shape
    terms = scan_terms(taken_ref, same_ref, conv_ref, head_ref)
    xbc, conv_sum, gate, active, raw, steps, rates, triangle, running = terms
    channels = xbc.shape[1]
    values = active[:, :width]
    keys, reads = active[:, width : width + NS], active[:, width + NS :]
    steps_row, running_row = steps.T, running.T
    heads = width // 64
    rows = 128
    grad = grad_ref[...]
    values_grad[...] = head_ref[2:3] * grad
    keys_grad[...] = jnp.zeros_like(keys_grad)
    rows_grad[...] = jnp.zeros_like(rows_grad)
    cols_grad[...] = jnp.zeros_like(cols_grad)
    for first in range(0, places, rows):
        last = first + rows
        shape = (rows, last)
        allowed = (seg_col[first:last] == seg_row[:, :last]) & (
            grid_iota(shape, 0) + first >= grid_iota(shape, 1)
        )
        crossing = dot_fine(reads[first:last], keys[:last], 1, 1)
        crossing_grad = jnp.zeros(shape, jnp.float32)
        grad_rows = grad[first:last]
        lane = grid_iota((rows, width), 1) // 64
        wide_lane = grid_iota((last, width), 1) // 64
        column = grid_iota((rows, 128), 1)
        down = jnp.zeros((rows, 128), jnp.float32)
        for h in range(heads):
            gaps = running[first:last, h : h + 1] - running_row[h : h + 1, :last]
            decays = jnp.exp(jnp.where(allowed, gaps, masked_score))
            step_row = steps_row[h : h + 1, :last]
            weighted = decays * step_row
            mixing = crossing * weighted
            own_grad = jnp.where(lane == h, grad_rows, 0.0)
            mixing_grad = dot_fine(own_grad, values[:last], 1, 1)
            back = dot_fine(mixing, own_grad, 0, 0)
            values_grad[:last] += jnp.where(wide_lane == h, back, 0.0)
            crossing_grad = crossing_grad + mixing_grad * weighted
            step_part = jnp.sum(mixing_grad * crossing * decays, axis=0, keepdims=True)
            gap_part = mixing_grad * mixing
            down = jnp.where(column == h, jnp.sum(gap_part, axis=1, keepdims=True), down)
            cols_grad[h : h + 1, :last] += step_part
            cols_grad[heads + h : heads + h + 1, :last] += step_part * step_row
        rows_grad[first:last] += down
        reads_grad[first:last] = dot_fine(crossing_grad, keys[:last], 1, 0)
        keys_grad[:last] += dot_fine(crossing_grad, reads[first:last], 0, 0)
    turned = cols_grad[...].T
    column = grid_iota(turned.shape, 1)
    step_grad = jnp.where(column < heads, turned, 0.0)
    ended = pltpu.roll(turned, turned.shape[1] - heads, 1)
    running_grad = jnp.where(column < heads, rows_grad[...] - ended, 0.0)
    rates_grad = dot_fine(triangle, running_grad, 0, 0)
    step_grad = step_grad - rates_grad * jnp.exp(head_ref[1:2])
    raw_grad = step_grad * jax.nn.sigmoid(raw)
    out_ref[:, channels:] = raw_grad
    lane = grid_iota((places, width), 1) // 64
    product = jnp.sum(grad * values, axis=0, keepdims=True)
    head_grad_ref[...] = jnp.zeros_like(head_grad_ref)
    head_grad_ref[0:1] = jnp.sum(raw_grad, axis=0, keepdims=True)
    head_grad_ref[1:2] = jnp.sum(rates_grad * rates, axis=0, keepdims=True)
    skip_lane = grid_iota((1, width), 1)
    skip_grad = jnp.zeros((1, width), jnp.float32)
    for h in range(heads):
        own = jnp.sum(jnp.where(skip_lane // 64 == h, product, 0.0), axis=1, keepdims=True)
        skip_grad = jnp.where(skip_lane == h, own, skip_grad)
    head_grad_ref[2:3] = skip_grad
    active_grad = jnp.concatenate([values_grad[...], keys_grad[...], reads_grad[...]], axis=1)
    conv_grad = active_grad * gate * (1.0 + conv_sum * (1.0 - gate))
    back = conv_ref[3:4] * conv_grad
    conv_grad_ref[...] = jnp.zeros_like(conv_grad_ref)
    conv_grad_ref[3:4] = jnp.sum(conv_grad * xbc, axis=0, keepdims=True)
    conv_grad_ref[4:5] = jnp.sum(conv_grad, axis=0, keepdims=True)
    for k in range(3):
        kept = conv_grad * same_ref[:, k : k + 1]
        back = back + conv_ref[k : k + 1] * shifted_up(kept, 3 - k)
        conv_grad_ref[k : k + 1] = jnp.sum(
            kept * shifted_down(xbc, 3 - k), axis=0, keepdims=True
        )
    out_ref[:, :channels] = back


def scan_forward(args, width):
    places = args[0].shape[0]
    return pl.pallas_call(
        scan_forward_kernel,
        out_shape=jax.ShapeDtypeStruct((places, width), jnp.float32),
        compiler_params=ROOMY,
        cost_estimate=NO_COST,
    )(*args)


def scan_backward(args, grad):
    places, width = grad.shape
    channels = args[2].shape[1]
    f32 = jnp.float32
    return pl.pallas_call(
        scan_backward_kernel,
        out_shape=[
            jax.ShapeDtypeStruct((places, channels + 128), f32),
            jax.ShapeDtypeStruct((8, channels), f32),
            jax.ShapeDtypeStruct((8, 128), f32),
        ],
        scratch_shapes=[
            pltpu.VMEM((places, width), f32),
            pltpu.VMEM((places, NS), f32),
            pltpu.VMEM((places, NS), f32),
            pltpu.VMEM((places, 128), f32),
            pltpu.VMEM((128, places), f32),
        ],
        compiler_params=ROOMY,
        cost_estimate=NO_COST,
    )(*args, grad)


def patch_lanes(block):
    shape = (block // 8, 8, block)
    return grid_iota(shape, 0) == grid_iota(shape, 2) // 8


def folded(scores, same_patch):
    split = scores.reshape(same_patch.shape)
    return jnp.sum(jnp.where(same_patch, split, 0.0), axis=0)


def unfolded(rows, same_patch):
    spread = jnp.where(same_patch, rows[None], 0.0)
    return spread.reshape(-1, rows.shape[1]).astype(jnp.bfloat16)


def softmax_rows(scores, causal):
    scores = jnp.where(causal, scores, masked_score)
    top = jnp.max(scores, axis=1, keepdims=True)
    powers = jnp.exp(scores - top)
    return powers / jnp.sum(powers, axis=1, keepdims=True)


def head_places(rows, head_cols, block):
    return [
        (slice(first, first + block), [j * head_cols + pair * 128 for j in range(3)])
        for first in range(0, rows, block)
        for pair in range(head_cols // 128)
    ]


def all_scores(qkv_ref, places, lane, same_patch):
    scores = []
    for rows, (query, key, unused) in places:
        queries = qkv_ref[rows, query : query + 128] * 0.125
        keys = qkv_ref[rows, key : key + 128]
        for h in range(2):
            own = jnp.where(lane == h, queries, 0)
            scores.append(folded(dot_trans(keys, own), same_patch))
    return jnp.stack(scores)


def attn_forward_kernel(
    bytes_ref, patch_ref, gain_ref, qkv_w_ref, o_w_ref, x_ref, a_ref, qkv_ref, o_ref, out_ref
):
    rows = bytes_ref.shape[0]
    spread = jnp.broadcast_to(patch_ref[...][:, None], (rows // 8, 8, patch_ref.shape[1]))
    x = bytes_ref[...].astype(jnp.float32) + spread.reshape(bytes_ref.shape)
    x_ref[...] = x
    attn_in = (x * rms_scale(x) * gain_ref[...]).astype(jnp.bfloat16)
    a_ref[...] = attn_in
    qkv_ref[...] = dot_plain(attn_in, qkv_w_ref[...]).astype(jnp.bfloat16)
    head_cols = o_ref.shape[1]
    block = 128
    same_patch = patch_lanes(block)
    causal = grid_iota((8, block), 0) <= grid_iota((8, block), 1) % 8
    lane = grid_iota((block, 128), 1) // AD
    places = head_places(rows, head_cols, block)
    probs = softmax_rows(all_scores(qkv_ref, places, lane, same_patch), causal)
    for at, (row_place, (query, unused, value)) in enumerate(places):
        values = qkv_ref[row_place, value : value + 128]
        parts = [dot_left(unfolded(probs[2 * at + h], same_patch), values) for h in range(2)]
        total = jnp.where(lane == 0, parts[0], parts[1])
        o_ref[row_place, query : query + 128] = total.astype(jnp.bfloat16)
    out_ref[...] = dot_trans(o_ref[...], o_w_ref[...])


def attn_forward(bytes_rows, patch_rows, gain, w_qkv, w_o):
    rows, width = bytes_rows.shape
    block = 256
    cols, head_cols = w_qkv.shape[1], w_o.shape[1]
    f32, bf16 = jnp.float32, jnp.bfloat16

    def by_rows(cols):
        return pl.BlockSpec((block, cols), lambda i: (i, 0))

    def whole(shape):
        return pl.BlockSpec(shape, lambda i: (0, 0))

    return pl.pallas_call(
        attn_forward_kernel,
        grid=(rows // block,),
        in_specs=[
            by_rows(width),
            pl.BlockSpec((block // 8, width), lambda i: (i, 0)),
            whole((1, width)),
            whole(w_qkv.shape),
            whole(w_o.shape),
        ],
        out_specs=[by_rows(width), by_rows(width), by_rows(cols), by_rows(head_cols), by_rows(width)],
        out_shape=[
            jax.ShapeDtypeStruct((rows, width), f32),
            jax.ShapeDtypeStruct((rows, width), bf16),
            jax.ShapeDtypeStruct((rows, cols), bf16),
            jax.ShapeDtypeStruct((rows, head_cols), bf16),
            jax.ShapeDtypeStruct((rows, width), f32),
        ],
        compiler_params=ROOMY,
        cost_estimate=NO_COST,
    )(bytes_rows, patch_rows, gain.reshape(1, width), w_qkv, w_o)


def attn_backward_kernel(
    x_ref,
    final_ref,
    own_ref,
    other_ref,
    gain_ref,
    qkv_ref,
    qkv_w_ref,
    o_w_ref,
    mid_ref,
    low_ref,
    qkv_grad_ref,
    out_ref,
    gain_grad_ref,
):
    rows = x_ref.shape[0]
    back, gain_grad = rms_back(x_ref[...], gain_ref[...], own_ref[...] + other_ref[...])
    mid = final_ref[...] + back
    mid_ref[...] = mid
    low_ref[...] = mid.astype(jnp.bfloat16)
    gain_grad = gain_grad.reshape(1, -1)

    @pl.when(pl.program_id(0) == 0)
    def _():
        gain_grad_ref[...] = gain_grad

    @pl.when(pl.program_id(0) > 0)
    def _():
        gain_grad_ref[...] += gain_grad

    mixed_grad = dot_plain(low_ref[...], o_w_ref[...]).astype(jnp.bfloat16)
    head_cols = mixed_grad.shape[1]
    block = 128
    same_patch = patch_lanes(block)
    causal = grid_iota((8, block), 0) <= grid_iota((8, block), 1) % 8
    lane = grid_iota((block, 128), 1) // AD
    places = head_places(rows, head_cols, block)
    probs = softmax_rows(all_scores(qkv_ref, places, lane, same_patch), causal)
    probs_grads = []
    for row_place, (query, unused, value) in places:
        values = qkv_ref[row_place, value : value + 128]
        out_grad = mixed_grad[row_place, query : query + 128]
        for h in range(2):
            own_grad = jnp.where(lane == h, out_grad, 0)
            probs_grads.append(folded(dot_trans(values, own_grad), same_patch))
    probs_grad = jnp.stack(probs_grads)
    inner = jnp.sum(probs * probs_grad, axis=1, keepdims=True)
    scores_grad = probs * (probs_grad - inner)
    for at, (row_place, cols) in enumerate(places):
        query, key, unused = cols
        queries = qkv_ref[row_place, query : query + 128]
        keys = qkv_ref[row_place, key : key + 128]
        out_grad = mixed_grad[row_place, query : query + 128]
        parts = []
        for h in range(2):
            own_scores = unfolded(scores_grad[2 * at + h], same_patch)
            parts.append(
                (
                    dot_left(own_scores, keys) * 0.125,
                    dot_plain(own_scores, queries) * 0.125,
                    dot_plain(unfolded(probs[2 * at + h], same_patch), out_grad),
                )
            )
        for j in range(3):
            grad = jnp.where(lane == 0, parts[0][j], parts[1][j])
            qkv_grad_ref[row_place, cols[j] : cols[j] + 128] = grad.astype(jnp.bfloat16)
    out_ref[...] = dot_trans(qkv_grad_ref[...], qkv_w_ref[...])


def attn_backward(x_rows, final_grad, own_part, other_part, gain, qkv, w_qkv, w_o):
    rows, width = x_rows.shape
    block = 256
    cols = w_qkv.shape[1]
    f32, bf16 = jnp.float32, jnp.bfloat16

    def by_rows(cols):
        return pl.BlockSpec((block, cols), lambda i: (i, 0))

    def whole(shape):
        return pl.BlockSpec(shape, lambda i: (0, 0))

    return pl.pallas_call(
        attn_backward_kernel,
        grid=(rows // block,),
        in_specs=[by_rows(width)] * 4
        + [whole((1, width)), by_rows(cols), whole(w_qkv.shape), whole(w_o.shape)],
        out_specs=[
            by_rows(width),
            by_rows(width),
            by_rows(cols),
            by_rows(width),
            whole((1, width)),
        ],
        out_shape=[
            jax.ShapeDtypeStruct((rows, width), f32),
            jax.ShapeDtypeStruct((rows, width), bf16),
            jax.ShapeDtypeStruct((rows, cols), bf16),
            jax.ShapeDtypeStruct((rows, width), f32),
            jax.ShapeDtypeStruct((1, width), f32),
        ],
        compiler_params=ROOMY,
        cost_estimate=NO_COST,
    )(x_rows, final_grad, own_part, other_part, gain.reshape(1, width), qkv, w_qkv, w_o)


def mlp_in_kernel(core_ref, x_ref, own_ref, other_ref, gain_ref, out_ref, low_ref, half_ref):
    x = x_ref[...] + (own_ref[...] + other_ref[...])
    out_ref[...] = x
    unit = x * rms_scale(x)
    low_ref[...] = (unit * gain_ref[...]).astype(jnp.bfloat16)
    width = half_ref.shape[1]
    half_ref[...] = jnp.where(core_ref[0] == 0, unit[:, :width], unit[:, width:])


def mlp_in(x_rows, own_part, other_part, gain):
    rows, width = x_rows.shape
    block = 128
    core = lax.axis_index("tp").astype(jnp.int32).reshape(1)

    def by_rows(cols):
        return pl.BlockSpec((block, cols), lambda i, ref: (i, 0))

    return pl.pallas_call(
        mlp_in_kernel,
        grid_spec=pltpu.PrefetchScalarGridSpec(
            num_scalar_prefetch=1,
            grid=(rows // block,),
            in_specs=[by_rows(width)] * 3 + [pl.BlockSpec((1, width), lambda i, ref: (0, 0))],
            out_specs=[by_rows(width), by_rows(width), by_rows(width // 2)],
        ),
        out_shape=[
            jax.ShapeDtypeStruct((rows, width), jnp.float32),
            jax.ShapeDtypeStruct((rows, width), jnp.bfloat16),
            jax.ShapeDtypeStruct((rows, width // 2), jnp.float32),
        ],
        compiler_params=ROOMY,
        cost_estimate=NO_COST,
    )(core, x_rows, own_part, other_part, gain.reshape(1, width))


def units_in_halves(
    mlp_low, grad_ref, gate_w_ref, up_w_ref, hidden_ref, gate_ref, up_ref
):
    half = grad_ref.shape[1] // 2
    for at in range(2):
        cols = slice(at * half, (at + 1) * half)
        hidden, gate, up = hidden_parts(
            mlp_low, grad_ref[:, cols], gate_w_ref[:, cols], up_w_ref[:, cols]
        )
        hidden_ref[:, cols] = hidden
        gate_ref[:, cols] = gate
        up_ref[:, cols] = up


def mlp_kernel(
    in_ref, grad_ref, gate_w_ref, up_w_ref, hidden_ref, gate_ref, up_ref, out_ref, total_ref
):
    mlp_low = in_ref[...]
    units_in_halves(
        mlp_low, grad_ref, gate_w_ref, up_w_ref, hidden_ref, gate_ref, up_ref
    )
    part = dot_trans(gate_ref[...], gate_w_ref[...]) + dot_trans(up_ref[...], up_w_ref[...])
    step = pl.program_id(0)

    @pl.when(step == 0)
    def _():
        total_ref[...] = part

    @pl.when(step > 0)
    def _():
        total_ref[...] += part

    @pl.when(step == pl.num_programs(0) - 1)
    def _():
        out_ref[...] = total_ref[...]


def mlp_rows(mlp_low, grad_hidden, w_gate, w_up):
    rows, width = mlp_low.shape
    units = w_gate.shape[1]
    block = 512
    by_units = pl.BlockSpec((rows, block), lambda i: (0, i))
    by_weights = pl.BlockSpec((width, block), lambda i: (0, i))
    whole = pl.BlockSpec((rows, width), lambda i: (0, 0))
    low = jax.ShapeDtypeStruct((rows, units), jnp.bfloat16)
    return pl.pallas_call(
        mlp_kernel,
        grid=(units // block,),
        in_specs=[whole, by_units, by_weights, by_weights],
        out_specs=[by_units, by_units, by_units, whole],
        out_shape=[low, low, low, jax.ShapeDtypeStruct((rows, width), jnp.float32)],
        scratch_shapes=[pltpu.VMEM((rows, width), jnp.float32)],
        compiler_params=ROOMY,
        cost_estimate=NO_COST,
    )(mlp_low, grad_hidden, w_gate, w_up)


def feature_order(width):
    shape = (8 * width, 8 * width)
    row, col = grid_iota(shape, 0), grid_iota(shape, 1)
    return jnp.where(row == (col % 8) * width + col // 8, 1.0, 0.0).astype(jnp.bfloat16)


def patch_in_kernel(core_ref, bytes_ref, weight_ref, wide_ref, out_ref, rows_ref, order_ref):
    places, feature = wide_ref.shape[0], wide_ref.shape[1] // 8
    chunk = weight_ref.shape[1] // 8
    step = pl.program_id(0)

    @pl.when(step == 0)
    def _():
        order_ref[...] = feature_order(chunk)
        for at in range(feature // 128):
            low = at * 128
            rows_ref[at] = bytes_ref[:, low : low + 128].astype(jnp.float32)
            for j in range(8):
                wide_ref[:, j * feature + low : j * feature + low + 128] = rows_ref[
                    at, pl.ds(j, places, stride=8), :
                ]

    parts = [
        wide_ref[:, pl.ds(pl.multiple_of(j * feature + step * chunk, 128), chunk)]
        for j in range(8)
    ]
    by_byte = jnp.concatenate(parts, axis=1).astype(jnp.bfloat16)
    by_feature = dot_plain(by_byte, order_ref[...]).astype(jnp.bfloat16)
    part = dot_trans(by_feature, weight_ref[...])

    @pl.when(step == 0)
    def _():
        out_ref[...] = part

    @pl.when(step > 0)
    def _():
        out_ref[...] += part


def patch_in(byte_rows, w_patch):
    rows, model_width = byte_rows.shape
    out_width, cols = w_patch.shape
    feature, chunk = cols // 8, 128
    core = lax.axis_index("tp").astype(jnp.int32).reshape(1)
    f32 = jnp.float32
    return pl.pallas_call(
        patch_in_kernel,
        grid_spec=pltpu.PrefetchScalarGridSpec(
            num_scalar_prefetch=1,
            grid=(feature // chunk,),
            in_specs=[
                pl.BlockSpec((rows, feature), lambda i, ref: (0, ref[0])),
                pl.BlockSpec((out_width, 8 * chunk), lambda i, ref: (0, i)),
            ],
            out_specs=[
                pl.BlockSpec((rows // 8, cols), lambda i, ref: (0, 0)),
                pl.BlockSpec((rows // 8, out_width), lambda i, ref: (0, 0)),
            ],
            scratch_shapes=[
                pltpu.VMEM((feature // 128, rows, 128), f32),
                pltpu.VMEM((8 * chunk, 8 * chunk), jnp.bfloat16),
            ],
        ),
        out_shape=[
            jax.ShapeDtypeStruct((rows // 8, cols), f32),
            jax.ShapeDtypeStruct((rows // 8, out_width), f32),
        ],
        compiler_params=ROOMY,
        cost_estimate=NO_COST,
    )(core, byte_rows, w_patch)


def final_kernel(
    member_ref,
    own_ref,
    other_ref,
    mask_ref,
    own_head_ref,
    other_head_ref,
    weight_ref,
    low_ref,
    hidden_ref,
    mine_ref,
    mine_low_ref,
):
    own = (own_ref[...] * mask_ref[...]).astype(jnp.bfloat16)
    other = (other_ref[...] * mask_ref[...]).astype(jnp.bfloat16)
    other_head = other_head_ref[...].astype(jnp.bfloat16)
    total = dot_trans(own, own_head_ref[...]) + dot_trans(other, other_head)
    low = total.astype(jnp.bfloat16)
    low_ref[...] = low
    hidden_ref[...] = dot_plain(low, weight_ref[...])

    @pl.when(pl.program_id(0) == 0)
    def _():
        mine_ref[...] = total
        mine_low_ref[...] = low


def final_grads(own, other, mask, own_head, other_head, w_down, member, count):
    rows, cols = own.shape
    width = own_head.shape[0]
    block = rows // count
    units = w_down.shape[1] // group_size()
    f32, bf16 = jnp.float32, jnp.bfloat16

    def by_rows(cols):
        return pl.BlockSpec((block, cols), lambda i, ref: (i, 0))

    head = pl.BlockSpec((width, cols), lambda i, ref: (0, 0))
    mine = pl.BlockSpec((block, width), lambda i, ref: (0, 0))
    return pl.pallas_call(
        final_kernel,
        grid_spec=pltpu.PrefetchScalarGridSpec(
            num_scalar_prefetch=1,
            grid=(count,),
            in_specs=[by_rows(cols), by_rows(cols), by_rows(1), head, head]
            + [pl.BlockSpec((width, units), lambda i, ref: (0, ref[0]))],
            out_specs=[by_rows(width), by_rows(units), mine, mine],
        ),
        out_shape=[
            jax.ShapeDtypeStruct((rows, width), bf16),
            jax.ShapeDtypeStruct((rows, units), f32),
            jax.ShapeDtypeStruct((block, width), f32),
            jax.ShapeDtypeStruct((block, width), bf16),
        ],
        compiler_params=ROOMY,
        cost_estimate=NO_COST,
    )(member, own, other, mask, own_head, other_head, w_down)


def group_mlp_kernel(
    place_ref,
    own_ref,
    other_ref,
    gain_ref,
    grad_ref,
    gate_w_ref,
    up_w_ref,
    in_ref,
    hidden_ref,
    gate_ref,
    up_ref,
):
    own, other = own_ref[0], other_ref[0]
    first = place_ref[1] == 0
    halves = [jnp.where(first, own, other), jnp.where(first, other, own)]
    low = (jnp.concatenate(halves, axis=1) * gain_ref[...]).astype(jnp.bfloat16)
    in_ref[...] = low
    units_in_halves(low, grad_ref, gate_w_ref, up_w_ref, hidden_ref, gate_ref, up_ref)


def group_mlp(own_half, other_half, gain, grad_hidden, w_gate, w_up, member):
    rows, half = grad_hidden.shape[0] // group_size(), own_half.shape[2]
    width, units = 2 * half, w_gate.shape[1] // group_size()
    bf16 = jnp.bfloat16
    place = jnp.concatenate([member, lax.axis_index("tp").astype(jnp.int32).reshape(1)])

    def by_rows(cols):
        return pl.BlockSpec((rows, cols), lambda i, ref: (i, 0))

    halves = pl.BlockSpec((1, rows, half), lambda i, ref: (i ^ ref[0], 0, 0))
    weights = pl.BlockSpec((width, units), lambda i, ref: (0, ref[0]))
    low = jax.ShapeDtypeStruct((group_size() * rows, units), bf16)
    return pl.pallas_call(
        group_mlp_kernel,
        grid_spec=pltpu.PrefetchScalarGridSpec(
            num_scalar_prefetch=1,
            grid=(group_size(),),
            in_specs=[
                halves,
                halves,
                pl.BlockSpec((1, width), lambda i, ref: (0, 0)),
                by_rows(units),
                weights,
                weights,
            ],
            out_specs=[by_rows(width), by_rows(units), by_rows(units), by_rows(units)],
        ),
        out_shape=[jax.ShapeDtypeStruct((group_size() * rows, width), bf16), low, low, low],
        compiler_params=ROOMY,
        cost_estimate=NO_COST,
    )(place, own_half, other_half, gain.reshape(1, width), grad_hidden, w_gate, w_up)


def bytes_grad_kernel(core_ref, grad_ref, weight_ref, stream_ref, out_ref, order_ref):
    places = grad_ref.shape[0]
    chunk = weight_ref.shape[1] // 8

    @pl.when(pl.program_id(0) == 0)
    def _():
        order_ref[...] = feature_order(chunk)

    by_feature = dot_plain(grad_ref[...].astype(jnp.bfloat16), weight_ref[...])
    high = by_feature.astype(jnp.bfloat16)
    rest = by_feature - high.astype(jnp.float32)
    mid = rest.astype(jnp.bfloat16)
    low = (rest - mid.astype(jnp.float32)).astype(jnp.bfloat16)
    order = order_ref[...]
    by_byte = dot_trans(high, order) + (dot_trans(mid, order) + dot_trans(low, order))
    for j in range(8):
        rows = pl.ds(j, places, stride=8)
        out_ref[rows, :] = stream_ref[rows, :] + by_byte[:, j * chunk : (j + 1) * chunk]


def bytes_grad(grad_patch, w_patch, grad_stream):
    places, width = grad_patch.shape
    rows = grad_stream.shape[0]
    cols = w_patch.shape[1]
    feature, chunk = cols // 8, 128
    core = lax.axis_index("tp").astype(jnp.int32).reshape(1)
    return pl.pallas_call(
        bytes_grad_kernel,
        grid_spec=pltpu.PrefetchScalarGridSpec(
            num_scalar_prefetch=1,
            grid=(feature // chunk,),
            in_specs=[
                pl.BlockSpec((places, width), lambda i, ref: (0, 0)),
                pl.BlockSpec((width, 8 * chunk), lambda i, ref: (0, i)),
                pl.BlockSpec((rows, chunk), lambda i, ref: (0, ref[0] * (feature // chunk) + i)),
            ],
            out_specs=pl.BlockSpec((rows, chunk), lambda i, ref: (0, i)),
            scratch_shapes=[pltpu.VMEM((8 * chunk, 8 * chunk), jnp.bfloat16)],
        ),
        out_shape=jax.ShapeDtypeStruct((rows, feature), jnp.float32),
        compiler_params=ROOMY,
        cost_estimate=NO_COST,
    )(core, grad_patch, w_patch, grad_stream)


def body(
    byte_states,
    lengths,
    w_patch,
    norm_global,
    w_in,
    conv_w,
    conv_b,
    dt_bias,
    a_log,
    d_skip,
    mix_gain,
    w_out,
    norm_attn,
    w_qkv,
    w_o,
    norm_mlp,
    w_gate,
    w_up,
    w_down,
    w_head,
    d_logits,
):
    streams, local_rows, model_width = byte_states.shape
    patch_count = local_rows // 8
    patch_total = streams * patch_count
    row_total = streams * local_rows
    feature = w_patch.shape[1] // 8
    inner_width = w_out.shape[1]
    channels = conv_w.shape[1]
    head_total = dt_bias.shape[0]
    head_cols = w_head.shape[1]
    parts = lax.axis_size("seq")
    tp_index = lax.axis_index("tp")
    seq_index = lax.axis_index("seq")
    places = parts * patch_count
    f32 = jnp.float32

    lanes = parts // streams
    width = inner_width // lanes
    full_head = inner_width // head_total
    own_heads = max(1, width // full_head)
    shared = max(1, full_head // width)
    head_size = width // own_heads
    own_stream = seq_index // lanes
    first_col = (seq_index % lanes) * width
    first_head = first_col // full_head

    seg_full = segment_ids(lengths, places)
    seg_own = lax.dynamic_slice_in_dim(seg_full, seq_index * patch_count, patch_count, 1)
    seg_stream = lax.dynamic_index_in_dim(seg_full, own_stream, 0, keepdims=False)
    valid = (seg_own < lengths.shape[0]).astype(f32).reshape(patch_total, 1)
    byte_valid = jnp.repeat(valid, 8, axis=0)

    member, members = seq_index // QUAD, group_size()
    raw_logits = d_logits.reshape(row_total, head_cols)
    raw_wide = raw_logits.astype(f32)
    group_valid = []
    for apart in range(members):
        device = seq_index ^ QUAD * apart
        group_seg = lax.dynamic_slice_in_dim(seg_full, device * patch_count, patch_count, 1)
        group_valid.append((group_seg < lengths.shape[0]).astype(f32))
    group_valid = jnp.stack(group_valid).reshape(members, patch_total, 1)
    group_bytes_valid = jnp.repeat(group_valid.reshape(-1, 1), 8, axis=0)
    apart_raw = [swap(raw_wide, "seq", QUAD * apart) for apart in range(1, members)]
    other_head = swap(w_head.astype(f32), "tp", 1)
    place_index = member.astype(jnp.int32).reshape(1)
    bytes_wide, patch_part = patch_in(byte_states.reshape(row_total, model_width), w_patch)
    patch_out = tp_sum(patch_part)
    gain_global = norm_global.astype(f32)
    unit_patch = patch_out * rms_scale(patch_out)
    u_low = (unit_patch * gain_global).astype(jnp.bfloat16)
    half_width = model_width // 2
    proj = dot_plain(u_low, w_in).reshape(streams, patch_count, -1)
    gate_in = proj[..., :inner_width]
    xbc = proj[..., inner_width : inner_width + channels]
    dt_raw = proj[..., inner_width + channels :]

    def by_lane(columns):
        split = columns.reshape(streams, patch_count, lanes, -1)
        return jnp.moveaxis(split, 2, 1).reshape(parts, patch_count, -1)

    def from_lanes(blocks):
        split = blocks.reshape(streams, lanes, patch_count, -1)
        return jnp.moveaxis(split, 1, 2).reshape(streams, patch_count, -1)

    def to_all_lanes(columns):
        wide = jnp.broadcast_to(
            columns[:, None], (streams, lanes, patch_count, columns.shape[-1])
        )
        return wide.reshape(parts, patch_count, -1)

    pad_width = 128 - own_heads
    dt_lanes = by_lane(jnp.repeat(dt_raw, shared, axis=2))
    sent = jnp.concatenate(
        [
            by_lane(xbc[..., :inner_width]),
            to_all_lanes(xbc[..., inner_width:]),
            jnp.pad(dt_lanes, ((0, 0), (0, 0), (0, pad_width))),
        ],
        axis=-1,
    )
    taken = trade(sent)
    grad_logits = raw_logits * byte_valid.astype(jnp.bfloat16)
    unused, unused_part, grad_final, grad_mlp_low = final_grads(
        after(raw_wide, sent),
        swap(raw_wide, "tp", 1),
        byte_valid,
        w_head,
        other_head,
        w_down,
        place_index,
        1,
    )
    grad_hidden = dot_plain(grad_mlp_low, w_down)
    hidden_part = w_gate.shape[1] // members

    row_side = [
        [device for device in range(parts) if (device & 1) == side] for side in range(2)
    ]
    bytes_all = lax.all_gather(
        bytes_wide, "seq", axis=0, axis_index_groups=row_side, tiled=True
    )
    taken = after(taken, bytes_wide, grad_hidden).reshape(places, -1)
    scan_width = width + channels - inner_width

    def own_cols(param):
        mine = lax.dynamic_slice_in_dim(param, first_col, width, param.ndim - 1)
        return jnp.concatenate([mine, param[..., inner_width:]], axis=-1).astype(f32)

    def own_head(param):
        return lax.dynamic_slice_in_dim(param, first_head, own_heads, 0).astype(f32)

    use_kernel = places == 512 and width == 128
    if use_kernel:
        padded_seg = jnp.pad(seg_stream, (3, 0), constant_values=-1)
        same = jnp.stack(
            [(padded_seg[k : k + places] == seg_stream).astype(f32) for k in range(3)]
            + [jnp.zeros((places,), f32)] * 5,
            axis=1,
        )
        conv_pack = jnp.concatenate(
            [own_cols(conv_w), own_cols(conv_b)[None], jnp.zeros((3, scan_width), f32)]
        )
        head_pack = jnp.stack(
            [jnp.pad(own_head(dt_bias), (0, 128 - own_heads))]
            + [jnp.pad(own_head(a_log), (0, 128 - own_heads))]
            + [jnp.repeat(own_head(d_skip), head_size)]
            + [jnp.zeros((128,), f32)] * 5
        )
        scan_args = (taken, same, conv_pack, head_pack, seg_stream[:, None], seg_stream[None])
        scanned = scan_forward(scan_args, width)
    else:
        scan_args = (
            taken[:, :scan_width],
            taken[:, scan_width : scan_width + own_heads],
            own_cols(conv_w),
            own_cols(conv_b),
            own_head(dt_bias),
            own_head(a_log),
            own_head(d_skip),
        )
        scanned, scan_back = jax.vjp(partial(scan_heads, seg_stream, head_size), *scan_args)
    result = trade(scanned.reshape(parts, patch_count, width))
    result = from_lanes(result)
    unit_normed, norm_back = jax.vjp(gated_unit, result, gate_in)
    mix_scale = mix_gain.astype(f32)
    normed_low = (unit_normed * mix_scale).reshape(patch_total, -1).astype(jnp.bfloat16)


    def quarters(columns):
        split = columns.reshape(patch_total, members, -1)
        return jnp.moveaxis(split, 1, 0)

    def by_apart(blocks):
        return [
            lax.dynamic_index_in_dim(blocks, member ^ apart, 0, keepdims=False)
            for apart in range(members)
        ]

    def group_swap(blocks):
        return [blocks[0]] + [swap(blocks[k], "seq", QUAD * k) for k in range(1, members)]

    def joined(blocks, turn):
        return jnp.concatenate([after(block, turn) for block in blocks], axis=0)

    early_got = group_swap(
        [
            jnp.concatenate([unit_patch, part], axis=-1)
            for part in by_apart(quarters(unit_normed))
        ]
    )
    global_out = patch_out + valid * tp_sum(dot_trans(normed_low, w_out))
    gain_attn = norm_attn.astype(f32)
    gain_mlp = norm_mlp.astype(f32)
    stream_in, attn_in, qkv, mixed_low, attn_part = attn_forward(
        byte_states.reshape(row_total, model_width), global_out, gain_attn, w_qkv, w_o
    )
    after_attn, mlp_low, unit_half = mlp_in(
        stream_in, attn_part, swap(attn_part, "tp", 1), gain_mlp
    )
    hidden_low, grad_gate_low, grad_up_low, grad_mlp_part = mlp_rows(
        after(mlp_low, unit_half, *apart_raw), grad_hidden, w_gate, w_up
    )
    group_halves = group_trade(jnp.broadcast_to(unit_half[None], (members,) + unit_half.shape))
    grad_mlp_other = swap(grad_mlp_part, "tp", 1)
    after_mlp = after_attn + tp_sum(dot_trans(after(hidden_low, grad_mlp_part), w_down))
    final_low = after_mlp.astype(jnp.bfloat16)
    logits = dot_plain(final_low, w_head) * byte_valid
    grad_mid, grad_attn_low, grad_qkv_low, grad_attn_part, grad_norm_mlp = attn_backward(
        after_attn, grad_final, grad_mlp_part, grad_mlp_other, gain_mlp, qkv, w_qkv, w_o
    )
    grad_norm_mlp = grad_norm_mlp.reshape(-1)
    grad_attn_in = tp_sum(grad_attn_part)

    back_attn, grad_norm_attn = rms_back(stream_in, gain_attn, grad_attn_in)
    grad_stream = grad_mid + back_attn
    grad_global = jnp.sum(grad_stream.reshape(patch_total, 8, model_width), axis=1)
    grad_mix_low = (grad_global * valid).astype(jnp.bfloat16)
    grad_normed = dot_plain(grad_mix_low, w_out).reshape(streams, patch_count, inner_width)
    grad_mix_gain = jnp.sum(grad_normed * unit_normed, axis=(0, 1))
    grad_result, grad_gate_in = norm_back(grad_normed * mix_scale)
    grad_z_low = grad_gate_in.reshape(patch_total, inner_width).astype(jnp.bfloat16)
    row_block = model_width // parts
    group_raw = jnp.concatenate(
        [raw_wide] + [after(raw, grad_attn_part) for raw in apart_raw], axis=0
    )
    other_raw = swap(group_raw, "tp", 1)
    group_final, group_grad_hidden, unused, unused_part = final_grads(
        group_raw,
        other_raw,
        group_bytes_valid,
        w_head,
        other_head,
        w_down,
        place_index,
        members,
    )
    dealing = after(by_lane(grad_result), bytes_all, group_grad_hidden, group_halves)
    dealt = trade(dealing)
    late_sent = [
        jnp.concatenate([grad_global, part], axis=-1) for part in by_apart(quarters(grad_gate_in))
    ]
    late_got = group_swap(late_sent)
    attn_cut = 1024 if grad_qkv_low.shape[1] > 1024 else 128
    attn_in_late = after(attn_in, dealing)
    attn_cols = grad_qkv_low.shape[1]
    attn_blocks = (
        grad_blocks([(attn_in_late, grad_qkv_low, 0, attn_cut)], 0, True),
        grad_blocks(
            [
                (attn_in_late, grad_qkv_low, attn_cut, attn_cols),
                (grad_attn_low, mixed_low, 0, mixed_low.shape[1]),
                (final_low, grad_logits, 0, head_cols),
            ],
            1,
            True,
        ),
    )
    attn_got = [to_partner(attn_blocks[first][0], first) for first in range(2)]
    dealt = after(dealt, attn_blocks[0][0], attn_blocks[1][0])
    grad_scanned = dealt.reshape(places, width)
    if use_kernel:
        back_sent, conv_grads, head_grads = scan_backward(scan_args, grad_scanned)
        lane_grad = back_sent[:, : scan_width + own_heads]
        scan_params = (
            conv_grads[:4],
            conv_grads[4],
            head_grads[0, :own_heads],
            head_grads[1, :own_heads],
            head_grads[2, :own_heads],
        )
    else:
        scan_grads = scan_back(grad_scanned)
        back_sent = jnp.concatenate(
            [scan_grads[0], jnp.pad(scan_grads[1], ((0, 0), (0, pad_width)))], axis=-1
        )
        lane_grad = jnp.concatenate([scan_grads[0], scan_grads[1]], axis=-1)
        scan_params = scan_grads[2:]
    back_sent = back_sent.reshape(parts, patch_count, -1)
    back_taken = trade(back_sent)
    own_half = after(group_halves, back_sent)
    group_in, group_hidden, group_gate, group_up = group_mlp(
        own_half, swap(own_half, "tp", 1), gain_mlp, group_grad_hidden, w_gate, w_up, place_index
    )
    first_set = grad_blocks(
        [
            (group_final, group_hidden, 0, hidden_part),
            (group_in, group_gate, 0, hidden_part),
        ],
        0,
        True,
    )
    late_got = joined(late_got, first_set[0])
    apart_valid = group_valid.reshape(-1, 1)
    group_mix = (late_got[:, :model_width] * apart_valid).astype(jnp.bfloat16)
    group_z = late_got[:, model_width:]
    late_early = joined(early_got, first_set[0])
    group_u = (late_early[:, :model_width] * gain_global).astype(jnp.bfloat16)
    quarter = inner_width // members
    own_scale = lax.dynamic_slice_in_dim(mix_scale, member * quarter, quarter, 0)
    group_n = (late_early[:, model_width:] * own_scale).astype(jnp.bfloat16)
    attn_far = [
        add_side(after(attn_blocks[first][1], first_set[0]), attn_got[first], 1)
        for first in range(2)
    ]
    attn_crossed = [to_partner(attn_far[first], 1 - first) for first in range(2)]
    mlp_blocks = [
        first_set,
        grad_blocks(
            [
                (group_in, after(group_up, *attn_far), 0, hidden_part),
                (group_mix, group_n, 0, group_n.shape[1]),
                (group_u, group_z, 0, group_z.shape[1]),
            ],
            1,
            True,
        ),
    ]
    mlp_got = [to_partner(mlp_blocks[first][0], first) for first in range(2)]
    back_taken = after(back_taken, mlp_blocks[0][0], mlp_blocks[1][0])
    grad_x = from_lanes(back_taken[..., :width])
    by_stream = back_taken.reshape(streams, lanes, patch_count, -1)
    grad_bc = jnp.sum(by_stream[..., width:scan_width], axis=1)
    grad_dt = from_lanes(back_taken[..., scan_width : scan_width + own_heads])
    grad_dt = jnp.sum(grad_dt.reshape(streams, patch_count, head_total, shared), axis=-1)
    grad_shared = jnp.concatenate([grad_bc, grad_dt], axis=-1).reshape(patch_total, -1)
    grad_proj_low = jnp.concatenate(
        [grad_z_low, grad_x.reshape(patch_total, -1).astype(jnp.bfloat16)]
        + [grad_shared.astype(jnp.bfloat16)],
        axis=-1,
    )
    grad_u_part = dot_trans(grad_proj_low, w_in)
    grad_u = tp_sum(grad_u_part)
    back_global, grad_norm_global = rms_back(patch_out, gain_global, grad_u)
    grad_patch = grad_global + back_global
    side_count = parts // 2
    my_side = seq_index & 1
    by_block = jnp.moveaxis(grad_patch.reshape(patch_total, parts, row_block), 1, 0)
    by_block = by_block.reshape(side_count, 2, patch_total, row_block)
    same_side = lax.dynamic_index_in_dim(by_block, my_side, 1, keepdims=False)
    other_side = lax.dynamic_index_in_dim(by_block, 1 - my_side, 1, keepdims=False)
    patch_rows = jnp.concatenate([same_side, other_side], axis=-1)
    patch_rows = patch_rows.reshape(side_count, patch_total, 2 * row_block)
    gain_part = grad_norm_global.reshape(-1, 2 * row_block)
    gain_count = gain_part.shape[0]
    patch_sent = jnp.concatenate(
        [patch_rows, jnp.broadcast_to(gain_part, (side_count,) + gain_part.shape)], axis=1
    )
    patch_taken = lax.all_to_all(
        patch_sent, "seq", 0, 0, axis_index_groups=row_side, tiled=True
    )

    mlp_far = [
        add_side(after(mlp_blocks[first][1], patch_sent), mlp_got[first], 1)
        for first in range(2)
    ]
    mlp_crossed = [to_partner(mlp_far[first], 1 - first) for first in range(2)]
    patch_taken = after(patch_taken, *mlp_far)
    gain_side = jnp.sum(patch_taken[:, patch_total:], axis=0)
    patch_cols = patch_taken[:, :patch_total].reshape(-1, 2 * row_block)
    patch_far = patch_far_grad(patch_cols, gain_side, bytes_all)
    patch_got = to_partner(patch_far, 0)

    high = (seq_index // QUAD).astype(jnp.int32).reshape(1)
    attn_near = near_sums(
        [
            (after(attn_blocks[first][1], patch_far, *mlp_crossed), attn_got[first], attn_crossed[first])
            for first in range(2)
        ],
        high,
    )
    attn_high = [
        swap(attn_near[apart], "seq", QUAD * apart) for apart in range(1, parts // QUAD)
    ]
    start = jnp.zeros((1,), jnp.int32)
    mlp_near = [
        near_sums(
            [(after(mlp_blocks[first][1], attn_near, patch_got), mlp_got[first], mlp_crossed[first])],
            start,
        )
        for first in range(2)
    ]
    rest = [quarters(columns) for columns in (grad_x, grad_bc, grad_dt)]
    rest_cols = [part.shape[-1] for part in rest]
    rest = after(jnp.concatenate(rest, axis=-1), *mlp_near)
    rest = jnp.pad(rest, ((0, 0), (0, 0), (0, -sum(rest_cols) % 128)))
    rest_blocks = grad_blocks(
        [(group_u, joined(group_swap(by_apart(rest)), mlp_near[0]), 0, rest.shape[-1])], 0, True
    )
    rest_got = to_partner(rest_blocks[0], 0)
    final_attn = attn_near[0]
    for got in attn_high:
        final_attn = final_attn + after(got, *mlp_near)
    rest_far = add_side(after(rest_blocks[1], *mlp_near), rest_got, 1)
    rest_crossed = to_partner(rest_far, 1)
    mlp_finals = [jnp.moveaxis(group_trade(part), 0, 1) for part in mlp_near]
    rest_near = near_sums(
        [(after(rest_blocks[1], final_attn, *mlp_finals), rest_got, rest_crossed)], start
    )
    mlp_finals.append(jnp.moveaxis(group_trade(rest_near), 0, 1))

    small = (
        scan_params[0][:, :width],
        scan_params[1][:width],
        scan_params[0][:, width:],
        scan_params[1][width:],
        scan_params[2],
        scan_params[3],
        scan_params[4],
        grad_mix_gain,
        grad_norm_attn,
        grad_norm_mlp,
    )
    small_count = sum(part.size for part in small)
    flat = after(jnp.concatenate([part.reshape(-1) for part in small]), *mlp_near)
    flat = jnp.pad(flat, (0, -small_count % 1024)).reshape(1, -1, 128)
    pieces = trade(jnp.broadcast_to(flat, (parts,) + flat.shape[1:])).reshape(parts, -1)
    by_small, at = [], 0
    for part in small:
        got = pieces[:, at : at + part.size].reshape((parts,) + part.shape)
        by_small.append(got)
        at += part.size

    def lane_cols(got):
        joined = jnp.sum(got.reshape((streams, lanes) + got.shape[1:]), axis=0)
        return jnp.moveaxis(joined, 0, -2).reshape(joined.shape[1:-1] + (-1,))

    def lane_heads(got):
        joined = jnp.sum(got.reshape(streams, lanes, -1), axis=0)
        return jnp.sum(joined.reshape(head_total, shared), axis=-1)

    small_sums = [
        jnp.concatenate([lane_cols(by_small[0]), jnp.sum(by_small[2], axis=0)], axis=-1),
        jnp.concatenate([lane_cols(by_small[1]), jnp.sum(by_small[3], axis=0)], axis=-1),
        lane_heads(by_small[4]),
        lane_heads(by_small[5]),
        lane_heads(by_small[6]),
    ] + [jnp.sum(got, axis=0) for got in by_small[7:]]

    def final_cols(final, low, count):
        return final[..., low : low + count].reshape(row_block, -1)

    final_down = final_cols(mlp_finals[0], 0, hidden_part)
    final_gate = final_cols(mlp_finals[0], hidden_part, hidden_part)
    final_up = final_cols(mlp_finals[1], 0, hidden_part)
    final_out = final_cols(mlp_finals[1], hidden_part, quarter)
    final_z = final_cols(mlp_finals[1], hidden_part + quarter, quarter)
    final_x = final_cols(mlp_finals[2], 0, rest_cols[0])
    final_bc = final_cols(mlp_finals[2], rest_cols[0], rest_cols[1])
    final_dt = final_cols(mlp_finals[2], rest_cols[0] + rest_cols[1], rest_cols[2])
    final_patch = patch_grad(patch_cols, patch_got, bytes_all)
    norm_global_sum = (gain_side + patch_got[row_block:, : 2 * row_block]).reshape(-1)
    grad_bytes = bytes_grad(after(grad_patch, patch_far), w_patch, grad_stream)
    grad_bytes = grad_bytes.reshape(streams, local_rows, feature)

    qkv_cols, o_cols = w_qkv.shape[1], w_o.shape[1]
    return (
        logits.reshape(streams, local_rows, head_cols),
        grad_bytes,
        final_patch,
        norm_global_sum,
        jnp.concatenate([final_z, final_x, final_bc, final_dt], axis=1),
        small_sums[0],
        small_sums[1],
        small_sums[2],
        small_sums[3],
        small_sums[4],
        small_sums[5],
        final_out,
        small_sums[6],
        final_attn[:, :qkv_cols],
        final_attn[:, qkv_cols : qkv_cols + o_cols],
        small_sums[7],
        final_gate,
        final_up,
        final_down,
        final_attn[:, qkv_cols + o_cols :],
    )


def solution(mesh):
    in_specs = (
        P(None, "seq", None),
        P(),
        P(None, "tp"),
        P(),
        P(None, "tp"),
        P(None, "tp"),
        P("tp"),
        P("tp"),
        P("tp"),
        P("tp"),
        P("tp"),
        P(None, "tp"),
        P(),
        P(None, "tp"),
        P(None, "tp"),
        P(),
        P(None, "tp"),
        P(None, "tp"),
        P(None, "tp"),
        P(None, "tp"),
        P(None, "seq", "tp"),
    )
    out_specs = (
        P(None, "seq", "tp"),
        P(None, "seq", "tp"),
        P("seq", "tp"),
        P(),
        P("seq", "tp"),
        P(None, "tp"),
        P("tp"),
        P("tp"),
        P("tp"),
        P("tp"),
        P("tp"),
        P("seq", "tp"),
        P(),
        P("seq", "tp"),
        P("seq", "tp"),
        P(),
        P("seq", "tp"),
        P("seq", "tp"),
        P("seq", "tp"),
        P("seq", "tp"),
    )
    return jax.shard_map(body, mesh=mesh, in_specs=in_specs, out_specs=out_specs, check_vma=False)
```

```python
from functools import partial

import jax
import jax.numpy as jnp
from jax import lax
from jax.experimental import pallas as pl
from jax.experimental.pallas import tpu as pltpu
from jax.sharding import PartitionSpec as P

NS = 128
AD = 64
QUAD = 4


NO_COST = pl.CostEstimate(flops=1024, bytes_accessed=1024, transcendentals=0)
ROOMY = pltpu.CompilerParams(vmem_limit_bytes=56 * 1024 * 1024)

epsilon = 1e-05
highest = lax.Precision.HIGHEST
masked_score = -1e30


def dot_plain(left_side, right_side):
    return jnp.dot(left_side, right_side, preferred_element_type=jnp.float32)


def dot_trans(left_side, right_side):
    return lax.dot_general(
        left_side, right_side, (((1,), (1,)), ((), ())), preferred_element_type=jnp.float32
    )


def dot_left(left_side, right_side):
    return lax.dot_general(
        left_side, right_side, (((0,), (0,)), ((), ())), preferred_element_type=jnp.float32
    )


def rms_scale(values):
    return lax.rsqrt(jnp.mean(values * values, axis=-1, keepdims=True) + epsilon)


def hidden_parts(mlp_in, grad_hidden, w_gate, w_up):
    gate_proj = dot_plain(mlp_in, w_gate)
    up_proj = dot_plain(mlp_in, w_up)
    sigmoid_gate = jax.nn.sigmoid(gate_proj)
    hidden_low = (gate_proj * sigmoid_gate * up_proj).astype(jnp.bfloat16)
    grad_gate_low = (
        grad_hidden * up_proj * sigmoid_gate * (1.0 + gate_proj * (1.0 - sigmoid_gate))
    ).astype(jnp.bfloat16)
    grad_up_low = (grad_hidden * gate_proj * sigmoid_gate).astype(jnp.bfloat16)
    return (hidden_low, grad_gate_low, grad_up_low)


def rms_back(values, gain_values, grad_out):
    scale = rms_scale(values)
    scaled = gain_values * grad_out
    inner_mean = jnp.mean(values * scaled, axis=-1, keepdims=True)
    grad_values = scale * scaled - values * scale * scale * scale * inner_mean
    grad_gain = jnp.sum(values * scale * grad_out, axis=0)
    return (grad_values, grad_gain)


def swap(block, axis, mask):
    return lax.ppermute(block, axis, [(i, i ^ mask) for i in range(lax.axis_size(axis))])


def after(value, *earlier):
    return lax.optimization_barrier((value,) + earlier)[0]


def tp_sum(block):
    return block + swap(block, "tp", 1)


def to_partner(block, bit):
    return swap(block, "seq", 1 << bit)


def seq_bits():
    return lax.axis_size("seq").bit_length() - 1


def group_size():
    return lax.axis_size("seq") // QUAD


def group_trade(blocks):
    members = [[low + QUAD * high for high in range(group_size())] for low in range(QUAD)]
    return lax.all_to_all(blocks, "seq", 0, 0, axis_index_groups=members, tiled=True)


def add_kernel(index_ref, *refs):
    total = refs[0][...] + refs[1][...]
    refs[2][...] = total.reshape(refs[2].shape)


def add_side(near, got, side):
    unused, groups, rows, cols = near.shape
    index = jnp.zeros((1,), jnp.int32)
    block = pl.BlockSpec((1, 1, rows, cols), lambda i, ref: (side, i, 0, 0))
    return pl.pallas_call(
        add_kernel,
        grid_spec=pltpu.PrefetchScalarGridSpec(
            num_scalar_prefetch=1,
            grid=(groups,),
            in_specs=[block, block],
            out_specs=pl.BlockSpec((1, rows, cols), lambda i, ref: (i, 0, 0)),
        ),
        out_shape=jax.ShapeDtypeStruct((groups, rows, cols), jnp.float32),
        compiler_params=ROOMY,
        cost_estimate=NO_COST,
    )(index, near, got)


def near_kernel(index_ref, *refs):
    out_ref = refs[-1]
    at = 0
    for near_ref, got_ref, crossed_ref in zip(refs[0:-1:3], refs[1:-1:3], refs[2:-1:3]):
        cols = near_ref.shape[3]
        total = near_ref[0, 0] + got_ref[0, 0] + crossed_ref[0]
        out_ref[0, :, at : at + cols] = total
        at += cols


def near_sums(terms, high):
    unused, groups, rows, unused_cols = terms[0][0].shape
    cols = [term[0].shape[3] for term in terms]
    specs, operands = [], []
    for (near, got, crossed), count in zip(terms, cols):
        four = pl.BlockSpec((1, 1, rows, count), lambda i, ref: (0, ref[0] ^ i, 0, 0))
        three = pl.BlockSpec((1, rows, count), lambda i, ref: (ref[0] ^ i, 0, 0))
        specs += [four, four, three]
        operands += [near, got, crossed]
    return pl.pallas_call(
        near_kernel,
        grid_spec=pltpu.PrefetchScalarGridSpec(
            num_scalar_prefetch=1,
            grid=(groups,),
            in_specs=specs,
            out_specs=pl.BlockSpec((1, rows, sum(cols)), lambda i, ref: (i, 0, 0)),
        ),
        out_shape=jax.ShapeDtypeStruct((groups, rows, sum(cols)), jnp.float32),
        compiler_params=ROOMY,
        cost_estimate=NO_COST,
    )(high, *operands)


def grad_blocks_kernel(pairs, first, relative, rows, member_ref, *refs):
    lefts, rights = refs[: len(pairs)], refs[len(pairs) : 2 * len(pairs)]
    far_ref, near_ref = refs[2 * len(pairs) :]
    other = 1 - first
    at = 0
    for left_ref, right_ref, (low, high) in zip(lefts, rights, pairs):
        got = dot_left(left_ref[...], right_ref[:, low:high].astype(jnp.bfloat16))
        places = slice(at, at + high - low)
        for block in range(got.shape[0] // rows):
            place, member = block // QUAD, block % QUAD
            part = got[block * rows : (block + 1) * rows]
            apart = member_ref[0] ^ member
            is_far = apart >> first & 1
            if relative:
                side = apart >> other & 1
            else:
                side = member >> other & 1

            @pl.when(is_far == 1)
            def _():
                if relative:
                    far_ref[side, place, :, places] = part
                else:
                    far_ref[place, side, :, places] = part

            @pl.when(is_far == 0)
            def _():
                if relative:
                    near_ref[side, place, :, places] = part
                else:
                    near_ref[place, side, :, places] = part

        at += high - low


def grad_blocks(terms, first, relative):
    parts = lax.axis_size("seq")
    groups = parts // QUAD
    model_width = terms[0][0].shape[1]
    rows = model_width // parts
    cols = max(128, QUAD * rows)
    places = cols // (QUAD * rows)
    pairs = [(low, high) for unused, unused_right, low, high in terms]
    total = sum(high - low for low, high in pairs)
    member = (lax.axis_index("seq") % QUAD).astype(jnp.int32).reshape(1)
    if relative:
        shape, block = (2, groups, rows, total), (2, places, rows, total)
        out_spec = pl.BlockSpec(block, lambda i, ref: (0, i, 0, 0))
    else:
        shape, block = (groups, 2, rows, total), (places, 2, rows, total)
        out_spec = pl.BlockSpec(block, lambda i, ref: (i, 0, 0, 0))
    out = jax.ShapeDtypeStruct(shape, jnp.float32)
    return pl.pallas_call(
        partial(grad_blocks_kernel, pairs, first, relative, rows),
        grid_spec=pltpu.PrefetchScalarGridSpec(
            num_scalar_prefetch=1,
            grid=(model_width // cols,),
            in_specs=[
                pl.BlockSpec((term[0].shape[0], cols), lambda i, ref: (0, i)) for term in terms
            ]
            + [pl.BlockSpec(term[1].shape, lambda i, ref: (0, 0)) for term in terms],
            out_specs=[out_spec, out_spec],
        ),
        out_shape=[out, out],
        compiler_params=ROOMY,
        cost_estimate=NO_COST,
    )(member, *[term[0] for term in terms], *[term[1] for term in terms])


def segment_ids(lengths, place_count):
    ends = jnp.cumsum(lengths // 8, dtype=jnp.int32)
    places = jnp.arange(place_count, dtype=jnp.int32)
    short_ids = jnp.sum(
        (places[:, None] >= ends[None, :]).astype(jnp.int32), axis=1, dtype=jnp.int32
    )
    return jnp.stack([jnp.zeros_like(short_ids), short_ids])


def scan_heads(seg_now, head_size, xbc, dt_raw, conv_weight, conv_bias, dt_shift, a_logs, skips):
    place_count = xbc.shape[0]
    conv_sum = conv_bias + conv_weight[3] * xbc
    for offset in range(3):
        distance = 3 - offset
        earlier = jnp.pad(xbc, ((distance, 0), (0, 0)))[:place_count]
        seg_earlier = jnp.pad(seg_now, (distance, 0), constant_values=-1)[:place_count]
        same_doc = (seg_earlier == seg_now).astype(jnp.float32)
        conv_sum = conv_sum + conv_weight[offset] * earlier * same_doc[:, None]
    active = jax.nn.silu(conv_sum)
    head_count = dt_raw.shape[1]
    inner = head_count * head_size
    values = active[:, :inner].reshape(place_count, head_count, head_size)
    in_keys = active[:, inner : inner + NS]
    out_keys = active[:, inner + NS :]
    step_sizes = jax.nn.softplus(dt_raw + dt_shift)
    decay_rates = -step_sizes * jnp.exp(a_logs)
    chunk = min(place_count, 512)
    triangle = jnp.tril(jnp.ones((chunk, chunk), jnp.float32))
    state = jnp.zeros((head_count, head_size, NS), jnp.float32)
    seg_last = jnp.int32(-1)
    outputs = []
    for start in range(0, place_count, chunk):
        stop = start + chunk
        x, b, c = values[start:stop], in_keys[start:stop], out_keys[start:stop]
        dt, seg = step_sizes[start:stop], seg_now[start:stop]
        cumulative = jnp.dot(triangle, decay_rates[start:stop], precision=highest)
        allowed = (triangle > 0.0) & (seg[:, None] == seg[None, :])
        ordered = cumulative.T
        gaps = ordered[:, :, None] - ordered[:, None, :]
        decays = jnp.where(allowed, jnp.exp(jnp.where(allowed, gaps, 0.0)), 0.0)
        crossing = jnp.einsum("pn,jn->pj", c, b, precision=highest)
        mixing = crossing[None] * decays * dt.T[:, None, :]
        result = jnp.einsum("hpj,jhd->phd", mixing, x, precision=highest)
        if start > 0:
            entering = jnp.exp(cumulative) * (seg == seg_last).astype(jnp.float32)[:, None]
            result = result + entering[..., None] * jnp.einsum(
                "pn,hdn->phd", c, state, precision=highest
            )
        if stop < place_count:
            last_same = (seg == seg[-1]).astype(jnp.float32)[:, None]
            weight = jnp.exp(cumulative[-1:] - cumulative) * last_same * dt
            through = jnp.exp(cumulative[-1]) * (seg[-1] == seg_last).astype(jnp.float32)
            state = through[:, None, None] * state + jnp.einsum(
                "jh,jhd,jn->hdn", weight, x, b, precision=highest
            )
            seg_last = seg[-1]
        outputs.append(result + skips[:, None] * x)
    return jnp.concatenate(outputs, axis=0).reshape(place_count, inner)


def gated_unit(result, gate_in):
    gated = result * jax.nn.silu(gate_in)
    return gated * rms_scale(gated)


def patch_far_kernel(grad_ref, gain_ref, bytes_ref, out_ref):
    half = grad_ref.shape[1] // 2
    grad_low = grad_ref[:, half:].astype(jnp.bfloat16)
    out_ref[:half] = dot_left(grad_low, bytes_ref[...].astype(jnp.bfloat16))
    out_ref[half:] = jnp.zeros((out_ref.shape[0] - half, out_ref.shape[1]), jnp.float32)

    @pl.when(pl.program_id(0) == 0)
    def _():
        out_ref[half:, : 2 * half] = gain_ref[...]


def patch_far_grad(grad_rows, gain_part, bytes_all):
    places, cols = grad_rows.shape
    total = bytes_all.shape[1]
    rows = cols // 2 + gain_part.shape[0]
    block = 1024
    return pl.pallas_call(
        patch_far_kernel,
        grid=(total // block,),
        in_specs=[
            pl.BlockSpec((places, cols), lambda i: (0, 0)),
            pl.BlockSpec(gain_part.shape, lambda i: (0, 0)),
            pl.BlockSpec((places, block), lambda i: (0, i)),
        ],
        out_specs=pl.BlockSpec((rows, block), lambda i: (0, i)),
        out_shape=jax.ShapeDtypeStruct((rows, total), jnp.float32),
        compiler_params=ROOMY,
        cost_estimate=NO_COST,
    )(grad_rows, gain_part, bytes_all)


def patch_grad_kernel(grad_ref, *refs):
    byte_refs, got_refs, out_ref, order_ref = refs[:8], refs[8:16], refs[16], refs[17]
    width = byte_refs[0].shape[1]

    @pl.when(pl.program_id(0) == 0)
    def _():
        order_ref[...] = feature_order(width)

    grad_low = grad_ref[:, : grad_ref.shape[1] // 2].astype(jnp.bfloat16)
    wide = jnp.concatenate([ref[...].astype(jnp.bfloat16) for ref in byte_refs], axis=1)
    rows = grad_low.shape[1]
    grad = dot_left(grad_low, wide)
    grad = grad + jnp.concatenate([ref[:rows] for ref in got_refs], axis=1)
    high = grad.astype(jnp.bfloat16)
    rest = grad - high.astype(jnp.float32)
    mid = rest.astype(jnp.bfloat16)
    low = (rest - mid.astype(jnp.float32)).astype(jnp.bfloat16)
    order = order_ref[...]
    out_ref[...] = dot_plain(high, order) + (dot_plain(mid, order) + dot_plain(low, order))


def patch_grad(grad_rows, got, bytes_all):
    places, cols = grad_rows.shape
    feature = bytes_all.shape[1] // 8
    chunk = 128
    steps = feature // chunk

    def byte_specs(rows):
        return [
            pl.BlockSpec((rows, chunk), partial(lambda j, i: (0, j * steps + i), j))
            for j in range(8)
        ]

    return pl.pallas_call(
        patch_grad_kernel,
        grid=(steps,),
        in_specs=[pl.BlockSpec((places, cols), lambda i: (0, 0))]
        + byte_specs(places)
        + byte_specs(got.shape[0]),
        out_specs=pl.BlockSpec((cols // 2, 8 * chunk), lambda i: (0, i)),
        out_shape=jax.ShapeDtypeStruct((cols // 2, 8 * feature), jnp.float32),
        scratch_shapes=[pltpu.VMEM((8 * chunk, 8 * chunk), jnp.bfloat16)],
        compiler_params=ROOMY,
        cost_estimate=NO_COST,
    )(grad_rows, *([bytes_all] * 8), *([got] * 8))


def trade(blocks):
    return lax.all_to_all(blocks, "seq", 0, 0, tiled=True)


def grid_iota(shape, axis):
    return lax.broadcasted_iota(jnp.int32, shape, axis)


def dot_fine(left_side, right_side, left_axis, right_axis):
    return lax.dot_general(
        left_side,
        right_side,
        (((left_axis,), (right_axis,)), ((), ())),
        preferred_element_type=jnp.float32,
        precision=highest,
    )


def shifted_down(block, distance):
    rows = grid_iota(block.shape, 0)
    return jnp.where(rows >= distance, pltpu.roll(block, distance, 0), 0.0)


def shifted_up(block, distance):
    count = block.shape[0]
    rows = grid_iota(block.shape, 0)
    return jnp.where(rows < count - distance, pltpu.roll(block, count - distance, 0), 0.0)


def scan_terms(taken_ref, same_ref, conv_ref, head_ref):
    places = taken_ref.shape[0]
    channels = conv_ref.shape[1]
    xbc = taken_ref[:, :channels]
    conv_sum = conv_ref[4:5] + conv_ref[3:4] * xbc
    for k in range(3):
        earlier = shifted_down(xbc, 3 - k) * same_ref[:, k : k + 1]
        conv_sum = conv_sum + conv_ref[k : k + 1] * earlier
    gate = jax.nn.sigmoid(conv_sum)
    active = conv_sum * gate
    raw = taken_ref[:, channels:] + head_ref[0:1]
    steps = jnp.maximum(raw, 0.0) + jnp.log1p(jnp.exp(-jnp.abs(raw)))
    rates = -steps * jnp.exp(head_ref[1:2])
    square = (places, places)
    triangle = jnp.where(grid_iota(square, 0) >= grid_iota(square, 1), 1.0, 0.0)
    running = dot_fine(triangle, rates, 1, 0)
    return xbc, conv_sum, gate, active, raw, steps, rates, triangle, running


def scan_forward_kernel(taken_ref, same_ref, conv_ref, head_ref, seg_col, seg_row, out_ref):
    places, width = out_ref.shape
    terms = scan_terms(taken_ref, same_ref, conv_ref, head_ref)
    active, steps, running = terms[3], terms[5], terms[8]
    values = active[:, :width]
    keys, reads = active[:, width : width + NS], active[:, width + NS :]
    steps_row, running_row = steps.T, running.T
    heads = width // 64
    rows = 128
    for first in range(0, places, rows):
        last = first + rows
        shape = (rows, last)
        allowed = (seg_col[first:last] == seg_row[:, :last]) & (
            grid_iota(shape, 0) + first >= grid_iota(shape, 1)
        )
        crossing = dot_fine(reads[first:last], keys[:last], 1, 1)
        lane = grid_iota((rows, width), 1) // 64
        total = head_ref[2:3] * values[first:last]
        for h in range(heads):
            gaps = running[first:last, h : h + 1] - running_row[h : h + 1, :last]
            decays = jnp.exp(jnp.where(allowed, gaps, masked_score))
            mixing = crossing * decays * steps_row[h : h + 1, :last]
            part = dot_fine(mixing, values[:last], 1, 0)
            total = total + jnp.where(lane == h, part, 0.0)
        out_ref[first:last] = total


def scan_backward_kernel(
    taken_ref,
    same_ref,
    conv_ref,
    head_ref,
    seg_col,
    seg_row,
    grad_ref,
    out_ref,
    conv_grad_ref,
    head_grad_ref,
    values_grad,
    keys_grad,
    reads_grad,
    rows_grad,
    cols_grad,
):
    places, width = values_grad.shape
    terms = scan_terms(taken_ref, same_ref, conv_ref, head_ref)
    xbc, conv_sum, gate, active, raw, steps, rates, triangle, running = terms
    channels = xbc.shape[1]
    values = active[:, :width]
    keys, reads = active[:, width : width + NS], active[:, width + NS :]
    steps_row, running_row = steps.T, running.T
    heads = width // 64
    rows = 128
    grad = grad_ref[...]
    values_grad[...] = head_ref[2:3] * grad
    keys_grad[...] = jnp.zeros_like(keys_grad)
    rows_grad[...] = jnp.zeros_like(rows_grad)
    cols_grad[...] = jnp.zeros_like(cols_grad)
    for first in range(0, places, rows):
        last = first + rows
        shape = (rows, last)
        allowed = (seg_col[first:last] == seg_row[:, :last]) & (
            grid_iota(shape, 0) + first >= grid_iota(shape, 1)
        )
        crossing = dot_fine(reads[first:last], keys[:last], 1, 1)
        crossing_grad = jnp.zeros(shape, jnp.float32)
        grad_rows = grad[first:last]
        lane = grid_iota((rows, width), 1) // 64
        wide_lane = grid_iota((last, width), 1) // 64
        column = grid_iota((rows, 128), 1)
        down = jnp.zeros((rows, 128), jnp.float32)
        for h in range(heads):
            gaps = running[first:last, h : h + 1] - running_row[h : h + 1, :last]
            decays = jnp.exp(jnp.where(allowed, gaps, masked_score))
            step_row = steps_row[h : h + 1, :last]
            weighted = decays * step_row
            mixing = crossing * weighted
            own_grad = jnp.where(lane == h, grad_rows, 0.0)
            mixing_grad = dot_fine(own_grad, values[:last], 1, 1)
            back = dot_fine(mixing, own_grad, 0, 0)
            values_grad[:last] += jnp.where(wide_lane == h, back, 0.0)
            crossing_grad = crossing_grad + mixing_grad * weighted
            step_part = jnp.sum(mixing_grad * crossing * decays, axis=0, keepdims=True)
            gap_part = mixing_grad * mixing
            down = jnp.where(column == h, jnp.sum(gap_part, axis=1, keepdims=True), down)
            cols_grad[h : h + 1, :last] += step_part
            cols_grad[heads + h : heads + h + 1, :last] += step_part * step_row
        rows_grad[first:last] += down
        reads_grad[first:last] = dot_fine(crossing_grad, keys[:last], 1, 0)
        keys_grad[:last] += dot_fine(crossing_grad, reads[first:last], 0, 0)
    turned = cols_grad[...].T
    column = grid_iota(turned.shape, 1)
    step_grad = jnp.where(column < heads, turned, 0.0)
    ended = pltpu.roll(turned, turned.shape[1] - heads, 1)
    running_grad = jnp.where(column < heads, rows_grad[...] - ended, 0.0)
    rates_grad = dot_fine(triangle, running_grad, 0, 0)
    step_grad = step_grad - rates_grad * jnp.exp(head_ref[1:2])
    raw_grad = step_grad * jax.nn.sigmoid(raw)
    out_ref[:, channels:] = raw_grad
    lane = grid_iota((places, width), 1) // 64
    product = jnp.sum(grad * values, axis=0, keepdims=True)
    head_grad_ref[...] = jnp.zeros_like(head_grad_ref)
    head_grad_ref[0:1] = jnp.sum(raw_grad, axis=0, keepdims=True)
    head_grad_ref[1:2] = jnp.sum(rates_grad * rates, axis=0, keepdims=True)
    skip_lane = grid_iota((1, width), 1)
    skip_grad = jnp.zeros((1, width), jnp.float32)
    for h in range(heads):
        own = jnp.sum(jnp.where(skip_lane // 64 == h, product, 0.0), axis=1, keepdims=True)
        skip_grad = jnp.where(skip_lane == h, own, skip_grad)
    head_grad_ref[2:3] = skip_grad
    active_grad = jnp.concatenate([values_grad[...], keys_grad[...], reads_grad[...]], axis=1)
    conv_grad = active_grad * gate * (1.0 + conv_sum * (1.0 - gate))
    back = conv_ref[3:4] * conv_grad
    conv_grad_ref[...] = jnp.zeros_like(conv_grad_ref)
    conv_grad_ref[3:4] = jnp.sum(conv_grad * xbc, axis=0, keepdims=True)
    conv_grad_ref[4:5] = jnp.sum(conv_grad, axis=0, keepdims=True)
    for k in range(3):
        kept = conv_grad * same_ref[:, k : k + 1]
        back = back + conv_ref[k : k + 1] * shifted_up(kept, 3 - k)
        conv_grad_ref[k : k + 1] = jnp.sum(
            kept * shifted_down(xbc, 3 - k), axis=0, keepdims=True
        )
    out_ref[:, :channels] = back


def scan_forward(args, width):
    places = args[0].shape[0]
    return pl.pallas_call(
        scan_forward_kernel,
        out_shape=jax.ShapeDtypeStruct((places, width), jnp.float32),
        compiler_params=ROOMY,
        cost_estimate=NO_COST,
    )(*args)


def scan_backward(args, grad):
    places, width = grad.shape
    channels = args[2].shape[1]
    f32 = jnp.float32
    return pl.pallas_call(
        scan_backward_kernel,
        out_shape=[
            jax.ShapeDtypeStruct((places, channels + 128), f32),
            jax.ShapeDtypeStruct((8, channels), f32),
            jax.ShapeDtypeStruct((8, 128), f32),
        ],
        scratch_shapes=[
            pltpu.VMEM((places, width), f32),
            pltpu.VMEM((places, NS), f32),
            pltpu.VMEM((places, NS), f32),
            pltpu.VMEM((places, 128), f32),
            pltpu.VMEM((128, places), f32),
        ],
        compiler_params=ROOMY,
        cost_estimate=NO_COST,
    )(*args, grad)


def patch_lanes(block):
    shape = (block // 8, 8, block)
    return grid_iota(shape, 0) == grid_iota(shape, 2) // 8


def folded(scores, same_patch):
    split = scores.reshape(same_patch.shape)
    return jnp.sum(jnp.where(same_patch, split, 0.0), axis=0)


def unfolded(rows, same_patch):
    spread = jnp.where(same_patch, rows[None], 0.0)
    return spread.reshape(-1, rows.shape[1]).astype(jnp.bfloat16)


def softmax_rows(scores, causal):
    scores = jnp.where(causal, scores, masked_score)
    top = jnp.max(scores, axis=1, keepdims=True)
    powers = jnp.exp(scores - top)
    return powers / jnp.sum(powers, axis=1, keepdims=True)


def head_places(rows, head_cols, block):
    return [
        (slice(first, first + block), [j * head_cols + pair * 128 for j in range(3)])
        for first in range(0, rows, block)
        for pair in range(head_cols // 128)
    ]


def all_scores(qkv_ref, places, lane, same_patch):
    scores = []
    for rows, (query, key, unused) in places:
        queries = qkv_ref[rows, query : query + 128] * 0.125
        keys = qkv_ref[rows, key : key + 128]
        for h in range(2):
            own = jnp.where(lane == h, queries, 0)
            scores.append(folded(dot_trans(keys, own), same_patch))
    return jnp.stack(scores)


def attn_forward_kernel(
    bytes_ref, patch_ref, gain_ref, qkv_w_ref, o_w_ref, x_ref, a_ref, qkv_ref, o_ref, out_ref
):
    rows = bytes_ref.shape[0]
    spread = jnp.broadcast_to(patch_ref[...][:, None], (rows // 8, 8, patch_ref.shape[1]))
    x = bytes_ref[...].astype(jnp.float32) + spread.reshape(bytes_ref.shape)
    x_ref[...] = x
    attn_in = (x * rms_scale(x) * gain_ref[...]).astype(jnp.bfloat16)
    a_ref[...] = attn_in
    qkv_ref[...] = dot_plain(attn_in, qkv_w_ref[...]).astype(jnp.bfloat16)
    head_cols = o_ref.shape[1]
    block = 128
    same_patch = patch_lanes(block)
    causal = grid_iota((8, block), 0) <= grid_iota((8, block), 1) % 8
    lane = grid_iota((block, 128), 1) // AD
    places = head_places(rows, head_cols, block)
    probs = softmax_rows(all_scores(qkv_ref, places, lane, same_patch), causal)
    for at, (row_place, (query, unused, value)) in enumerate(places):
        values = qkv_ref[row_place, value : value + 128]
        parts = [dot_left(unfolded(probs[2 * at + h], same_patch), values) for h in range(2)]
        total = jnp.where(lane == 0, parts[0], parts[1])
        o_ref[row_place, query : query + 128] = total.astype(jnp.bfloat16)
    out_ref[...] = dot_trans(o_ref[...], o_w_ref[...])


def attn_forward(bytes_rows, patch_rows, gain, w_qkv, w_o):
    rows, width = bytes_rows.shape
    block = 256
    cols, head_cols = w_qkv.shape[1], w_o.shape[1]
    f32, bf16 = jnp.float32, jnp.bfloat16

    def by_rows(cols):
        return pl.BlockSpec((block, cols), lambda i: (i, 0))

    def whole(shape):
        return pl.BlockSpec(shape, lambda i: (0, 0))

    return pl.pallas_call(
        attn_forward_kernel,
        grid=(rows // block,),
        in_specs=[
            by_rows(width),
            pl.BlockSpec((block // 8, width), lambda i: (i, 0)),
            whole((1, width)),
            whole(w_qkv.shape),
            whole(w_o.shape),
        ],
        out_specs=[by_rows(width), by_rows(width), by_rows(cols), by_rows(head_cols), by_rows(width)],
        out_shape=[
            jax.ShapeDtypeStruct((rows, width), f32),
            jax.ShapeDtypeStruct((rows, width), bf16),
            jax.ShapeDtypeStruct((rows, cols), bf16),
            jax.ShapeDtypeStruct((rows, head_cols), bf16),
            jax.ShapeDtypeStruct((rows, width), f32),
        ],
        compiler_params=ROOMY,
        cost_estimate=NO_COST,
    )(bytes_rows, patch_rows, gain.reshape(1, width), w_qkv, w_o)


def attn_backward_kernel(
    x_ref,
    final_ref,
    own_ref,
    other_ref,
    gain_ref,
    qkv_ref,
    qkv_w_ref,
    o_w_ref,
    mid_ref,
    low_ref,
    qkv_grad_ref,
    out_ref,
    gain_grad_ref,
):
    rows = x_ref.shape[0]
    back, gain_grad = rms_back(x_ref[...], gain_ref[...], own_ref[...] + other_ref[...])
    mid = final_ref[...] + back
    mid_ref[...] = mid
    low_ref[...] = mid.astype(jnp.bfloat16)
    gain_grad = gain_grad.reshape(1, -1)

    @pl.when(pl.program_id(0) == 0)
    def _():
        gain_grad_ref[...] = gain_grad

    @pl.when(pl.program_id(0) > 0)
    def _():
        gain_grad_ref[...] += gain_grad

    mixed_grad = dot_plain(low_ref[...], o_w_ref[...]).astype(jnp.bfloat16)
    head_cols = mixed_grad.shape[1]
    block = 128
    same_patch = patch_lanes(block)
    causal = grid_iota((8, block), 0) <= grid_iota((8, block), 1) % 8
    lane = grid_iota((block, 128), 1) // AD
    places = head_places(rows, head_cols, block)
    probs = softmax_rows(all_scores(qkv_ref, places, lane, same_patch), causal)
    probs_grads = []
    for row_place, (query, unused, value) in places:
        values = qkv_ref[row_place, value : value + 128]
        out_grad = mixed_grad[row_place, query : query + 128]
        for h in range(2):
            own_grad = jnp.where(lane == h, out_grad, 0)
            probs_grads.append(folded(dot_trans(values, own_grad), same_patch))
    probs_grad = jnp.stack(probs_grads)
    inner = jnp.sum(probs * probs_grad, axis=1, keepdims=True)
    scores_grad = probs * (probs_grad - inner)
    for at, (row_place, cols) in enumerate(places):
        query, key, unused = cols
        queries = qkv_ref[row_place, query : query + 128]
        keys = qkv_ref[row_place, key : key + 128]
        out_grad = mixed_grad[row_place, query : query + 128]
        parts = []
        for h in range(2):
            own_scores = unfolded(scores_grad[2 * at + h], same_patch)
            parts.append(
                (
                    dot_left(own_scores, keys) * 0.125,
                    dot_plain(own_scores, queries) * 0.125,
                    dot_plain(unfolded(probs[2 * at + h], same_patch), out_grad),
                )
            )
        for j in range(3):
            grad = jnp.where(lane == 0, parts[0][j], parts[1][j])
            qkv_grad_ref[row_place, cols[j] : cols[j] + 128] = grad.astype(jnp.bfloat16)
    out_ref[...] = dot_trans(qkv_grad_ref[...], qkv_w_ref[...])


def attn_backward(x_rows, final_grad, own_part, other_part, gain, qkv, w_qkv, w_o):
    rows, width = x_rows.shape
    block = 256
    cols = w_qkv.shape[1]
    f32, bf16 = jnp.float32, jnp.bfloat16

    def by_rows(cols):
        return pl.BlockSpec((block, cols), lambda i: (i, 0))

    def whole(shape):
        return pl.BlockSpec(shape, lambda i: (0, 0))

    return pl.pallas_call(
        attn_backward_kernel,
        grid=(rows // block,),
        in_specs=[by_rows(width)] * 4
        + [whole((1, width)), by_rows(cols), whole(w_qkv.shape), whole(w_o.shape)],
        out_specs=[
            by_rows(width),
            by_rows(width),
            by_rows(cols),
            by_rows(width),
            whole((1, width)),
        ],
        out_shape=[
            jax.ShapeDtypeStruct((rows, width), f32),
            jax.ShapeDtypeStruct((rows, width), bf16),
            jax.ShapeDtypeStruct((rows, cols), bf16),
            jax.ShapeDtypeStruct((rows, width), f32),
            jax.ShapeDtypeStruct((1, width), f32),
        ],
        compiler_params=ROOMY,
        cost_estimate=NO_COST,
    )(x_rows, final_grad, own_part, other_part, gain.reshape(1, width), qkv, w_qkv, w_o)


def mlp_in_kernel(core_ref, x_ref, own_ref, other_ref, gain_ref, out_ref, low_ref, half_ref):
    x = x_ref[...] + (own_ref[...] + other_ref[...])
    out_ref[...] = x
    unit = x * rms_scale(x)
    low_ref[...] = (unit * gain_ref[...]).astype(jnp.bfloat16)
    width = half_ref.shape[1]
    half_ref[...] = jnp.where(core_ref[0] == 0, unit[:, :width], unit[:, width:])


def mlp_in(x_rows, own_part, other_part, gain):
    rows, width = x_rows.shape
    block = 128
    core = lax.axis_index("tp").astype(jnp.int32).reshape(1)

    def by_rows(cols):
        return pl.BlockSpec((block, cols), lambda i, ref: (i, 0))

    return pl.pallas_call(
        mlp_in_kernel,
        grid_spec=pltpu.PrefetchScalarGridSpec(
            num_scalar_prefetch=1,
            grid=(rows // block,),
            in_specs=[by_rows(width)] * 3 + [pl.BlockSpec((1, width), lambda i, ref: (0, 0))],
            out_specs=[by_rows(width), by_rows(width), by_rows(width // 2)],
        ),
        out_shape=[
            jax.ShapeDtypeStruct((rows, width), jnp.float32),
            jax.ShapeDtypeStruct((rows, width), jnp.bfloat16),
            jax.ShapeDtypeStruct((rows, width // 2), jnp.float32),
        ],
        compiler_params=ROOMY,
        cost_estimate=NO_COST,
    )(core, x_rows, own_part, other_part, gain.reshape(1, width))


def units_in_halves(
    mlp_low, grad_ref, gate_w_ref, up_w_ref, hidden_ref, gate_ref, up_ref
):
    half = grad_ref.shape[1] // 2
    for at in range(2):
        cols = slice(at * half, (at + 1) * half)
        hidden, gate, up = hidden_parts(
            mlp_low, grad_ref[:, cols], gate_w_ref[:, cols], up_w_ref[:, cols]
        )
        hidden_ref[:, cols] = hidden
        gate_ref[:, cols] = gate
        up_ref[:, cols] = up


def mlp_kernel(
    in_ref, grad_ref, gate_w_ref, up_w_ref, hidden_ref, gate_ref, up_ref, out_ref, total_ref
):
    mlp_low = in_ref[...]
    units_in_halves(
        mlp_low, grad_ref, gate_w_ref, up_w_ref, hidden_ref, gate_ref, up_ref
    )
    part = dot_trans(gate_ref[...], gate_w_ref[...]) + dot_trans(up_ref[...], up_w_ref[...])
    step = pl.program_id(0)

    @pl.when(step == 0)
    def _():
        total_ref[...] = part

    @pl.when(step > 0)
    def _():
        total_ref[...] += part

    @pl.when(step == pl.num_programs(0) - 1)
    def _():
        out_ref[...] = total_ref[...]


def mlp_rows(mlp_low, grad_hidden, w_gate, w_up):
    rows, width = mlp_low.shape
    units = w_gate.shape[1]
    block = 512
    by_units = pl.BlockSpec((rows, block), lambda i: (0, i))
    by_weights = pl.BlockSpec((width, block), lambda i: (0, i))
    whole = pl.BlockSpec((rows, width), lambda i: (0, 0))
    low = jax.ShapeDtypeStruct((rows, units), jnp.bfloat16)
    return pl.pallas_call(
        mlp_kernel,
        grid=(units // block,),
        in_specs=[whole, by_units, by_weights, by_weights],
        out_specs=[by_units, by_units, by_units, whole],
        out_shape=[low, low, low, jax.ShapeDtypeStruct((rows, width), jnp.float32)],
        scratch_shapes=[pltpu.VMEM((rows, width), jnp.float32)],
        compiler_params=ROOMY,
        cost_estimate=NO_COST,
    )(mlp_low, grad_hidden, w_gate, w_up)


def feature_order(width):
    shape = (8 * width, 8 * width)
    row, col = grid_iota(shape, 0), grid_iota(shape, 1)
    return jnp.where(row == (col % 8) * width + col // 8, 1.0, 0.0).astype(jnp.bfloat16)


def patch_in_kernel(core_ref, bytes_ref, weight_ref, wide_ref, out_ref, rows_ref, order_ref):
    places, feature = wide_ref.shape[0], wide_ref.shape[1] // 8
    chunk = weight_ref.shape[1] // 8
    step = pl.program_id(0)

    @pl.when(step == 0)
    def _():
        order_ref[...] = feature_order(chunk)
        for at in range(feature // 128):
            low = at * 128
            rows_ref[at] = bytes_ref[:, low : low + 128].astype(jnp.float32)
            for j in range(8):
                wide_ref[:, j * feature + low : j * feature + low + 128] = rows_ref[
                    at, pl.ds(j, places, stride=8), :
                ]

    parts = [
        wide_ref[:, pl.ds(pl.multiple_of(j * feature + step * chunk, 128), chunk)]
        for j in range(8)
    ]
    by_byte = jnp.concatenate(parts, axis=1).astype(jnp.bfloat16)
    by_feature = dot_plain(by_byte, order_ref[...]).astype(jnp.bfloat16)
    part = dot_trans(by_feature, weight_ref[...])

    @pl.when(step == 0)
    def _():
        out_ref[...] = part

    @pl.when(step > 0)
    def _():
        out_ref[...] += part


def patch_in(byte_rows, w_patch):
    rows, model_width = byte_rows.shape
    out_width, cols = w_patch.shape
    feature, chunk = cols // 8, 128
    core = lax.axis_index("tp").astype(jnp.int32).reshape(1)
    f32 = jnp.float32
    return pl.pallas_call(
        patch_in_kernel,
        grid_spec=pltpu.PrefetchScalarGridSpec(
            num_scalar_prefetch=1,
            grid=(feature // chunk,),
            in_specs=[
                pl.BlockSpec((rows, feature), lambda i, ref: (0, ref[0])),
                pl.BlockSpec((out_width, 8 * chunk), lambda i, ref: (0, i)),
            ],
            out_specs=[
                pl.BlockSpec((rows // 8, cols), lambda i, ref: (0, 0)),
                pl.BlockSpec((rows // 8, out_width), lambda i, ref: (0, 0)),
            ],
            scratch_shapes=[
                pltpu.VMEM((feature // 128, rows, 128), f32),
                pltpu.VMEM((8 * chunk, 8 * chunk), jnp.bfloat16),
            ],
        ),
        out_shape=[
            jax.ShapeDtypeStruct((rows // 8, cols), f32),
            jax.ShapeDtypeStruct((rows // 8, out_width), f32),
        ],
        compiler_params=ROOMY,
        cost_estimate=NO_COST,
    )(core, byte_rows, w_patch)


def final_kernel(
    member_ref,
    own_ref,
    other_ref,
    mask_ref,
    own_head_ref,
    other_head_ref,
    weight_ref,
    low_ref,
    hidden_ref,
    mine_ref,
    mine_low_ref,
):
    own = (own_ref[...] * mask_ref[...]).astype(jnp.bfloat16)
    other = (other_ref[...] * mask_ref[...]).astype(jnp.bfloat16)
    other_head = other_head_ref[...].astype(jnp.bfloat16)
    total = dot_trans(own, own_head_ref[...]) + dot_trans(other, other_head)
    low = total.astype(jnp.bfloat16)
    low_ref[...] = low
    hidden_ref[...] = dot_plain(low, weight_ref[...])

    @pl.when(pl.program_id(0) == 0)
    def _():
        mine_ref[...] = total
        mine_low_ref[...] = low


def final_grads(own, other, mask, own_head, other_head, w_down, member, count):
    rows, cols = own.shape
    width = own_head.shape[0]
    block = rows // count
    units = w_down.shape[1] // group_size()
    f32, bf16 = jnp.float32, jnp.bfloat16

    def by_rows(cols):
        return pl.BlockSpec((block, cols), lambda i, ref: (i, 0))

    head = pl.BlockSpec((width, cols), lambda i, ref: (0, 0))
    mine = pl.BlockSpec((block, width), lambda i, ref: (0, 0))
    return pl.pallas_call(
        final_kernel,
        grid_spec=pltpu.PrefetchScalarGridSpec(
            num_scalar_prefetch=1,
            grid=(count,),
            in_specs=[by_rows(cols), by_rows(cols), by_rows(1), head, head]
            + [pl.BlockSpec((width, units), lambda i, ref: (0, ref[0]))],
            out_specs=[by_rows(width), by_rows(units), mine, mine],
        ),
        out_shape=[
            jax.ShapeDtypeStruct((rows, width), bf16),
            jax.ShapeDtypeStruct((rows, units), f32),
            jax.ShapeDtypeStruct((block, width), f32),
            jax.ShapeDtypeStruct((block, width), bf16),
        ],
        compiler_params=ROOMY,
        cost_estimate=NO_COST,
    )(member, own, other, mask, own_head, other_head, w_down)


def group_mlp_kernel(
    place_ref,
    own_ref,
    other_ref,
    gain_ref,
    grad_ref,
    gate_w_ref,
    up_w_ref,
    in_ref,
    hidden_ref,
    gate_ref,
    up_ref,
):
    own, other = own_ref[0], other_ref[0]
    first = place_ref[1] == 0
    halves = [jnp.where(first, own, other), jnp.where(first, other, own)]
    low = (jnp.concatenate(halves, axis=1) * gain_ref[...]).astype(jnp.bfloat16)
    in_ref[...] = low
    units_in_halves(low, grad_ref, gate_w_ref, up_w_ref, hidden_ref, gate_ref, up_ref)


def group_mlp(own_half, other_half, gain, grad_hidden, w_gate, w_up, member):
    rows, half = grad_hidden.shape[0] // group_size(), own_half.shape[2]
    width, units = 2 * half, w_gate.shape[1] // group_size()
    bf16 = jnp.bfloat16
    place = jnp.concatenate([member, lax.axis_index("tp").astype(jnp.int32).reshape(1)])

    def by_rows(cols):
        return pl.BlockSpec((rows, cols), lambda i, ref: (i, 0))

    halves = pl.BlockSpec((1, rows, half), lambda i, ref: (i ^ ref[0], 0, 0))
    weights = pl.BlockSpec((width, units), lambda i, ref: (0, ref[0]))
    low = jax.ShapeDtypeStruct((group_size() * rows, units), bf16)
    return pl.pallas_call(
        group_mlp_kernel,
        grid_spec=pltpu.PrefetchScalarGridSpec(
            num_scalar_prefetch=1,
            grid=(group_size(),),
            in_specs=[
                halves,
                halves,
                pl.BlockSpec((1, width), lambda i, ref: (0, 0)),
                by_rows(units),
                weights,
                weights,
            ],
            out_specs=[by_rows(width), by_rows(units), by_rows(units), by_rows(units)],
        ),
        out_shape=[jax.ShapeDtypeStruct((group_size() * rows, width), bf16), low, low, low],
        compiler_params=ROOMY,
        cost_estimate=NO_COST,
    )(place, own_half, other_half, gain.reshape(1, width), grad_hidden, w_gate, w_up)


def bytes_grad_kernel(core_ref, grad_ref, weight_ref, stream_ref, out_ref, order_ref):
    places = grad_ref.shape[0]
    chunk = weight_ref.shape[1] // 8

    @pl.when(pl.program_id(0) == 0)
    def _():
        order_ref[...] = feature_order(chunk)

    by_feature = dot_plain(grad_ref[...].astype(jnp.bfloat16), weight_ref[...])
    high = by_feature.astype(jnp.bfloat16)
    rest = by_feature - high.astype(jnp.float32)
    mid = rest.astype(jnp.bfloat16)
    low = (rest - mid.astype(jnp.float32)).astype(jnp.bfloat16)
    order = order_ref[...]
    by_byte = dot_trans(high, order) + (dot_trans(mid, order) + dot_trans(low, order))
    for j in range(8):
        rows = pl.ds(j, places, stride=8)
        out_ref[rows, :] = stream_ref[rows, :] + by_byte[:, j * chunk : (j + 1) * chunk]


def bytes_grad(grad_patch, w_patch, grad_stream):
    places, width = grad_patch.shape
    rows = grad_stream.shape[0]
    cols = w_patch.shape[1]
    feature, chunk = cols // 8, 128
    core = lax.axis_index("tp").astype(jnp.int32).reshape(1)
    return pl.pallas_call(
        bytes_grad_kernel,
        grid_spec=pltpu.PrefetchScalarGridSpec(
            num_scalar_prefetch=1,
            grid=(feature // chunk,),
            in_specs=[
                pl.BlockSpec((places, width), lambda i, ref: (0, 0)),
                pl.BlockSpec((width, 8 * chunk), lambda i, ref: (0, i)),
                pl.BlockSpec((rows, chunk), lambda i, ref: (0, ref[0] * (feature // chunk) + i)),
            ],
            out_specs=pl.BlockSpec((rows, chunk), lambda i, ref: (0, i)),
            scratch_shapes=[pltpu.VMEM((8 * chunk, 8 * chunk), jnp.bfloat16)],
        ),
        out_shape=jax.ShapeDtypeStruct((rows, feature), jnp.float32),
        compiler_params=ROOMY,
        cost_estimate=NO_COST,
    )(core, grad_patch, w_patch, grad_stream)


def body(
    byte_states,
    lengths,
    w_patch,
    norm_global,
    w_in,
    conv_w,
    conv_b,
    dt_bias,
    a_log,
    d_skip,
    mix_gain,
    w_out,
    norm_attn,
    w_qkv,
    w_o,
    norm_mlp,
    w_gate,
    w_up,
    w_down,
    w_head,
    d_logits,
):
    streams, local_rows, model_width = byte_states.shape
    patch_count = local_rows // 8
    patch_total = streams * patch_count
    row_total = streams * local_rows
    feature = w_patch.shape[1] // 8
    inner_width = w_out.shape[1]
    channels = conv_w.shape[1]
    head_total = dt_bias.shape[0]
    head_cols = w_head.shape[1]
    parts = lax.axis_size("seq")
    tp_index = lax.axis_index("tp")
    seq_index = lax.axis_index("seq")
    places = parts * patch_count
    f32 = jnp.float32

    lanes = parts // streams
    width = inner_width // lanes
    full_head = inner_width // head_total
    own_heads = max(1, width // full_head)
    shared = max(1, full_head // width)
    head_size = width // own_heads
    own_stream = seq_index // lanes
    first_col = (seq_index % lanes) * width
    first_head = first_col // full_head

    seg_full = segment_ids(lengths, places)
    seg_own = lax.dynamic_slice_in_dim(seg_full, seq_index * patch_count, patch_count, 1)
    seg_stream = lax.dynamic_index_in_dim(seg_full, own_stream, 0, keepdims=False)
    valid = (seg_own < lengths.shape[0]).astype(f32).reshape(patch_total, 1)
    byte_valid = jnp.repeat(valid, 8, axis=0)

    member, members = seq_index // QUAD, group_size()
    raw_logits = d_logits.reshape(row_total, head_cols)
    raw_wide = raw_logits.astype(f32)
    group_valid = []
    for apart in range(members):
        device = seq_index ^ QUAD * apart
        group_seg = lax.dynamic_slice_in_dim(seg_full, device * patch_count, patch_count, 1)
        group_valid.append((group_seg < lengths.shape[0]).astype(f32))
    group_valid = jnp.stack(group_valid).reshape(members, patch_total, 1)
    group_bytes_valid = jnp.repeat(group_valid.reshape(-1, 1), 8, axis=0)
    apart_raw = [swap(raw_wide, "seq", QUAD * apart) for apart in range(1, members)]
    other_head = swap(w_head.astype(f32), "tp", 1)
    place_index = member.astype(jnp.int32).reshape(1)
    bytes_wide, patch_part = patch_in(byte_states.reshape(row_total, model_width), w_patch)
    patch_out = tp_sum(patch_part)
    gain_global = norm_global.astype(f32)
    unit_patch = patch_out * rms_scale(patch_out)
    u_low = (unit_patch * gain_global).astype(jnp.bfloat16)
    half_width = model_width // 2
    proj = dot_plain(u_low, w_in).reshape(streams, patch_count, -1)
    gate_in = proj[..., :inner_width]
    xbc = proj[..., inner_width : inner_width + channels]
    dt_raw = proj[..., inner_width + channels :]

    def by_lane(columns):
        split = columns.reshape(streams, patch_count, lanes, -1)
        return jnp.moveaxis(split, 2, 1).reshape(parts, patch_count, -1)

    def from_lanes(blocks):
        split = blocks.reshape(streams, lanes, patch_count, -1)
        return jnp.moveaxis(split, 1, 2).reshape(streams, patch_count, -1)

    def to_all_lanes(columns):
        wide = jnp.broadcast_to(
            columns[:, None], (streams, lanes, patch_count, columns.shape[-1])
        )
        return wide.reshape(parts, patch_count, -1)

    pad_width = 128 - own_heads
    dt_lanes = by_lane(jnp.repeat(dt_raw, shared, axis=2))
    sent = jnp.concatenate(
        [
            by_lane(xbc[..., :inner_width]),
            to_all_lanes(xbc[..., inner_width:]),
            jnp.pad(dt_lanes, ((0, 0), (0, 0), (0, pad_width))),
        ],
        axis=-1,
    )
    taken = trade(sent)
    grad_logits = raw_logits * byte_valid.astype(jnp.bfloat16)
    unused, unused_part, grad_final, grad_mlp_low = final_grads(
        after(raw_wide, sent),
        swap(raw_wide, "tp", 1),
        byte_valid,
        w_head,
        other_head,
        w_down,
        place_index,
        1,
    )
    grad_hidden = dot_plain(grad_mlp_low, w_down)
    hidden_part = w_gate.shape[1] // members

    row_side = [
        [device for device in range(parts) if (device & 1) == side] for side in range(2)
    ]
    bytes_all = lax.all_gather(
        bytes_wide, "seq", axis=0, axis_index_groups=row_side, tiled=True
    )
    taken = after(taken, bytes_wide, grad_hidden).reshape(places, -1)
    scan_width = width + channels - inner_width

    def own_cols(param):
        mine = lax.dynamic_slice_in_dim(param, first_col, width, param.ndim - 1)
        return jnp.concatenate([mine, param[..., inner_width:]], axis=-1).astype(f32)

    def own_head(param):
        return lax.dynamic_slice_in_dim(param, first_head, own_heads, 0).astype(f32)

    use_kernel = places == 512 and width == 128
    if use_kernel:
        padded_seg = jnp.pad(seg_stream, (3, 0), constant_values=-1)
        same = jnp.stack(
            [(padded_seg[k : k + places] == seg_stream).astype(f32) for k in range(3)]
            + [jnp.zeros((places,), f32)] * 5,
            axis=1,
        )
        conv_pack = jnp.concatenate(
            [own_cols(conv_w), own_cols(conv_b)[None], jnp.zeros((3, scan_width), f32)]
        )
        head_pack = jnp.stack(
            [jnp.pad(own_head(dt_bias), (0, 128 - own_heads))]
            + [jnp.pad(own_head(a_log), (0, 128 - own_heads))]
            + [jnp.repeat(own_head(d_skip), head_size)]
            + [jnp.zeros((128,), f32)] * 5
        )
        scan_args = (taken, same, conv_pack, head_pack, seg_stream[:, None], seg_stream[None])
        scanned = scan_forward(scan_args, width)
    else:
        scan_args = (
            taken[:, :scan_width],
            taken[:, scan_width : scan_width + own_heads],
            own_cols(conv_w),
            own_cols(conv_b),
            own_head(dt_bias),
            own_head(a_log),
            own_head(d_skip),
        )
        scanned, scan_back = jax.vjp(partial(scan_heads, seg_stream, head_size), *scan_args)
    result = trade(scanned.reshape(parts, patch_count, width))
    result = from_lanes(result)
    unit_normed, norm_back = jax.vjp(gated_unit, result, gate_in)
    mix_scale = mix_gain.astype(f32)
    normed_low = (unit_normed * mix_scale).reshape(patch_total, -1).astype(jnp.bfloat16)


    def quarters(columns):
        split = columns.reshape(patch_total, members, -1)
        return jnp.moveaxis(split, 1, 0)

    def by_apart(blocks):
        return [
            lax.dynamic_index_in_dim(blocks, member ^ apart, 0, keepdims=False)
            for apart in range(members)
        ]

    def group_swap(blocks):
        return [blocks[0]] + [swap(blocks[k], "seq", QUAD * k) for k in range(1, members)]

    def joined(blocks, turn):
        return jnp.concatenate([after(block, turn) for block in blocks], axis=0)

    early_got = group_swap(
        [
            jnp.concatenate([unit_patch, part], axis=-1)
            for part in by_apart(quarters(unit_normed))
        ]
    )
    global_out = patch_out + valid * tp_sum(dot_trans(normed_low, w_out))
    gain_attn = norm_attn.astype(f32)
    gain_mlp = norm_mlp.astype(f32)
    stream_in, attn_in, qkv, mixed_low, attn_part = attn_forward(
        byte_states.reshape(row_total, model_width), global_out, gain_attn, w_qkv, w_o
    )
    after_attn, mlp_low, unit_half = mlp_in(
        stream_in, attn_part, swap(attn_part, "tp", 1), gain_mlp
    )
    hidden_low, grad_gate_low, grad_up_low, grad_mlp_part = mlp_rows(
        after(mlp_low, unit_half), grad_hidden, w_gate, w_up
    )
    group_halves = group_trade(jnp.broadcast_to(unit_half[None], (members,) + unit_half.shape))
    grad_mlp_other = swap(grad_mlp_part, "tp", 1)
    after_mlp = after_attn + tp_sum(dot_trans(after(hidden_low, grad_mlp_part), w_down))
    final_low = after_mlp.astype(jnp.bfloat16)
    logits = dot_plain(final_low, w_head) * byte_valid
    grad_mid, grad_attn_low, grad_qkv_low, grad_attn_part, grad_norm_mlp = attn_backward(
        after_attn, grad_final, grad_mlp_part, grad_mlp_other, gain_mlp, qkv, w_qkv, w_o
    )
    grad_norm_mlp = grad_norm_mlp.reshape(-1)
    grad_attn_in = tp_sum(grad_attn_part)

    back_attn, grad_norm_attn = rms_back(stream_in, gain_attn, grad_attn_in)
    grad_stream = grad_mid + back_attn
    grad_global = jnp.sum(grad_stream.reshape(patch_total, 8, model_width), axis=1)
    grad_mix_low = (grad_global * valid).astype(jnp.bfloat16)
    grad_normed = dot_plain(grad_mix_low, w_out).reshape(streams, patch_count, inner_width)
    grad_mix_gain = jnp.sum(grad_normed * unit_normed, axis=(0, 1))
    grad_result, grad_gate_in = norm_back(grad_normed * mix_scale)
    grad_z_low = grad_gate_in.reshape(patch_total, inner_width).astype(jnp.bfloat16)
    row_block = model_width // parts
    group_raw = jnp.concatenate(
        [raw_wide] + [after(raw, grad_normed) for raw in apart_raw], axis=0
    )
    other_raw = swap(group_raw, "tp", 1)
    group_final, group_grad_hidden, unused, unused_part = final_grads(
        group_raw,
        other_raw,
        group_bytes_valid,
        w_head,
        other_head,
        w_down,
        place_index,
        members,
    )
    dealing = after(by_lane(grad_result), bytes_all, group_grad_hidden, group_halves)
    dealt = trade(dealing)
    late_sent = [
        jnp.concatenate([grad_global, part], axis=-1) for part in by_apart(quarters(grad_gate_in))
    ]
    late_got = group_swap(late_sent)
    attn_cut = 1024 if grad_qkv_low.shape[1] > 1024 else 128
    attn_in_late = after(attn_in, dealing)
    attn_cols = grad_qkv_low.shape[1]
    attn_blocks = (
        grad_blocks([(attn_in_late, grad_qkv_low, 0, attn_cut)], 0, True),
        grad_blocks(
            [
                (attn_in_late, grad_qkv_low, attn_cut, attn_cols),
                (grad_attn_low, mixed_low, 0, mixed_low.shape[1]),
                (final_low, grad_logits, 0, head_cols),
            ],
            1,
            True,
        ),
    )
    attn_got = [to_partner(attn_blocks[first][0], first) for first in range(2)]
    dealt = after(dealt, attn_blocks[0][0], attn_blocks[1][0])
    grad_scanned = dealt.reshape(places, width)
    if use_kernel:
        back_sent, conv_grads, head_grads = scan_backward(scan_args, grad_scanned)
        lane_grad = back_sent[:, : scan_width + own_heads]
        scan_params = (
            conv_grads[:4],
            conv_grads[4],
            head_grads[0, :own_heads],
            head_grads[1, :own_heads],
            head_grads[2, :own_heads],
        )
    else:
        scan_grads = scan_back(grad_scanned)
        back_sent = jnp.concatenate(
            [scan_grads[0], jnp.pad(scan_grads[1], ((0, 0), (0, pad_width)))], axis=-1
        )
        lane_grad = jnp.concatenate([scan_grads[0], scan_grads[1]], axis=-1)
        scan_params = scan_grads[2:]
    back_sent = back_sent.reshape(parts, patch_count, -1)
    back_taken = trade(back_sent)
    own_half = after(group_halves, back_sent)
    group_in, group_hidden, group_gate, group_up = group_mlp(
        own_half, swap(own_half, "tp", 1), gain_mlp, group_grad_hidden, w_gate, w_up, place_index
    )
    first_set = grad_blocks(
        [
            (group_final, group_hidden, 0, hidden_part),
            (group_in, group_gate, 0, hidden_part),
        ],
        0,
        True,
    )
    late_got = joined(late_got, first_set[0])
    apart_valid = group_valid.reshape(-1, 1)
    group_mix = (late_got[:, :model_width] * apart_valid).astype(jnp.bfloat16)
    group_z = late_got[:, model_width:]
    late_early = joined(early_got, first_set[0])
    group_u = (late_early[:, :model_width] * gain_global).astype(jnp.bfloat16)
    quarter = inner_width // members
    own_scale = lax.dynamic_slice_in_dim(mix_scale, member * quarter, quarter, 0)
    group_n = (late_early[:, model_width:] * own_scale).astype(jnp.bfloat16)
    attn_far = [
        add_side(after(attn_blocks[first][1], first_set[0]), attn_got[first], 1)
        for first in range(2)
    ]
    attn_crossed = [to_partner(attn_far[first], 1 - first) for first in range(2)]
    mlp_blocks = [
        first_set,
        grad_blocks(
            [
                (group_in, after(group_up, *attn_far), 0, hidden_part),
                (group_mix, group_n, 0, group_n.shape[1]),
                (group_u, group_z, 0, group_z.shape[1]),
            ],
            1,
            True,
        ),
    ]
    mlp_got = [to_partner(mlp_blocks[first][0], first) for first in range(2)]
    back_taken = after(back_taken, mlp_blocks[0][0], mlp_blocks[1][0])
    grad_x = from_lanes(back_taken[..., :width])
    by_stream = back_taken.reshape(streams, lanes, patch_count, -1)
    grad_bc = jnp.sum(by_stream[..., width:scan_width], axis=1)
    grad_dt = from_lanes(back_taken[..., scan_width : scan_width + own_heads])
    grad_dt = jnp.sum(grad_dt.reshape(streams, patch_count, head_total, shared), axis=-1)
    grad_shared = jnp.concatenate([grad_bc, grad_dt], axis=-1).reshape(patch_total, -1)
    grad_proj_low = jnp.concatenate(
        [grad_z_low, grad_x.reshape(patch_total, -1).astype(jnp.bfloat16)]
        + [grad_shared.astype(jnp.bfloat16)],
        axis=-1,
    )
    grad_u_part = dot_trans(grad_proj_low, w_in)
    grad_u = tp_sum(grad_u_part)
    rest = [quarters(columns) for columns in (grad_x, grad_bc, grad_dt)]
    rest_cols = [part.shape[-1] for part in rest]
    rest = after(jnp.concatenate(rest, axis=-1), grad_u_part)
    rest = jnp.pad(rest, ((0, 0), (0, 0), (0, -sum(rest_cols) % 128)))
    rest_blocks = grad_blocks(
        [(group_u, joined(group_swap(by_apart(rest)), grad_u_part), 0, rest.shape[-1])], 0, True
    )
    back_global, grad_norm_global = rms_back(patch_out, gain_global, grad_u)
    grad_patch = grad_global + back_global
    side_count = parts // 2
    my_side = seq_index & 1
    by_block = jnp.moveaxis(grad_patch.reshape(patch_total, parts, row_block), 1, 0)
    by_block = by_block.reshape(side_count, 2, patch_total, row_block)
    same_side = lax.dynamic_index_in_dim(by_block, my_side, 1, keepdims=False)
    other_side = lax.dynamic_index_in_dim(by_block, 1 - my_side, 1, keepdims=False)
    patch_rows = jnp.concatenate([same_side, other_side], axis=-1)
    patch_rows = patch_rows.reshape(side_count, patch_total, 2 * row_block)
    gain_part = grad_norm_global.reshape(-1, 2 * row_block)
    gain_count = gain_part.shape[0]
    patch_sent = jnp.concatenate(
        [patch_rows, jnp.broadcast_to(gain_part, (side_count,) + gain_part.shape)], axis=1
    )
    patch_taken = lax.all_to_all(
        patch_sent, "seq", 0, 0, axis_index_groups=row_side, tiled=True
    )

    mlp_far = [
        add_side(after(mlp_blocks[first][1], patch_sent), mlp_got[first], 1)
        for first in range(2)
    ]
    mlp_crossed = [to_partner(mlp_far[first], 1 - first) for first in range(2)]
    patch_taken = after(patch_taken, rest_blocks[0], *mlp_far)
    gain_side = jnp.sum(patch_taken[:, patch_total:], axis=0)
    patch_cols = patch_taken[:, :patch_total].reshape(-1, 2 * row_block)
    patch_far = patch_far_grad(patch_cols, gain_side, bytes_all)
    small = (
        scan_params[0][:, :width],
        scan_params[1][:width],
        scan_params[0][:, width:],
        scan_params[1][width:],
        scan_params[2],
        scan_params[3],
        scan_params[4],
        grad_mix_gain,
        grad_norm_attn,
        grad_norm_mlp,
    )
    small_count = sum(part.size for part in small)
    flat = after(jnp.concatenate([part.reshape(-1) for part in small]), patch_far)
    flat = jnp.pad(flat, (0, -small_count % 1024)).reshape(1, -1, 128)
    pieces = trade(jnp.broadcast_to(flat, (parts,) + flat.shape[1:])).reshape(parts, -1)
    by_small, at = [], 0
    for part in small:
        got = pieces[:, at : at + part.size].reshape((parts,) + part.shape)
        by_small.append(got)
        at += part.size

    def lane_cols(got):
        joined = jnp.sum(got.reshape((streams, lanes) + got.shape[1:]), axis=0)
        return jnp.moveaxis(joined, 0, -2).reshape(joined.shape[1:-1] + (-1,))

    def lane_heads(got):
        joined = jnp.sum(got.reshape(streams, lanes, -1), axis=0)
        return jnp.sum(joined.reshape(head_total, shared), axis=-1)

    small_sums = [
        jnp.concatenate([lane_cols(by_small[0]), jnp.sum(by_small[2], axis=0)], axis=-1),
        jnp.concatenate([lane_cols(by_small[1]), jnp.sum(by_small[3], axis=0)], axis=-1),
        lane_heads(by_small[4]),
        lane_heads(by_small[5]),
        lane_heads(by_small[6]),
    ] + [jnp.sum(got, axis=0) for got in by_small[7:]]

    patch_got = to_partner(patch_far, 0)

    high = (seq_index // QUAD).astype(jnp.int32).reshape(1)
    attn_near = near_sums(
        [
            (after(attn_blocks[first][1], patch_far), attn_got[first], attn_crossed[first])
            for first in range(2)
        ],
        high,
    )
    attn_high = [
        swap(attn_near[apart], "seq", QUAD * apart) for apart in range(1, parts // QUAD)
    ]
    rest_got = to_partner(after(rest_blocks[0], patch_far), 0)
    start = jnp.zeros((1,), jnp.int32)
    mlp_near = [
        near_sums(
            [(after(mlp_blocks[first][1], attn_near, patch_got), mlp_got[first], mlp_crossed[first])],
            start,
        )
        for first in range(2)
    ]
    final_attn = attn_near[0]
    for got in attn_high:
        final_attn = final_attn + after(got, *mlp_near)
    rest_far = add_side(after(rest_blocks[1], *mlp_near), rest_got, 1)
    rest_crossed = to_partner(rest_far, 1)
    mlp_finals = [jnp.moveaxis(group_trade(part), 0, 1) for part in mlp_near]
    rest_near = near_sums(
        [(after(rest_blocks[1], final_attn, *mlp_finals), rest_got, rest_crossed)], start
    )
    mlp_finals.append(jnp.moveaxis(group_trade(rest_near), 0, 1))

    def final_cols(final, low, count):
        return final[..., low : low + count].reshape(row_block, -1)

    final_down = final_cols(mlp_finals[0], 0, hidden_part)
    final_gate = final_cols(mlp_finals[0], hidden_part, hidden_part)
    final_up = final_cols(mlp_finals[1], 0, hidden_part)
    final_out = final_cols(mlp_finals[1], hidden_part, quarter)
    final_z = final_cols(mlp_finals[1], hidden_part + quarter, quarter)
    final_x = final_cols(mlp_finals[2], 0, rest_cols[0])
    final_bc = final_cols(mlp_finals[2], rest_cols[0], rest_cols[1])
    final_dt = final_cols(mlp_finals[2], rest_cols[0] + rest_cols[1], rest_cols[2])
    final_patch = patch_grad(patch_cols, patch_got, bytes_all)
    norm_global_sum = (gain_side + patch_got[row_block:, : 2 * row_block]).reshape(-1)
    grad_bytes = bytes_grad(after(grad_patch, patch_far), w_patch, grad_stream)
    grad_bytes = grad_bytes.reshape(streams, local_rows, feature)

    qkv_cols, o_cols = w_qkv.shape[1], w_o.shape[1]
    return (
        logits.reshape(streams, local_rows, head_cols),
        grad_bytes,
        final_patch,
        norm_global_sum,
        jnp.concatenate([final_z, final_x, final_bc, final_dt], axis=1),
        small_sums[0],
        small_sums[1],
        small_sums[2],
        small_sums[3],
        small_sums[4],
        small_sums[5],
        final_out,
        small_sums[6],
        final_attn[:, :qkv_cols],
        final_attn[:, qkv_cols : qkv_cols + o_cols],
        small_sums[7],
        final_gate,
        final_up,
        final_down,
        final_attn[:, qkv_cols + o_cols :],
    )


def solution(mesh):
    in_specs = (
        P(None, "seq", None),
        P(),
        P(None, "tp"),
        P(),
        P(None, "tp"),
        P(None, "tp"),
        P("tp"),
        P("tp"),
        P("tp"),
        P("tp"),
        P("tp"),
        P(None, "tp"),
        P(),
        P(None, "tp"),
        P(None, "tp"),
        P(),
        P(None, "tp"),
        P(None, "tp"),
        P(None, "tp"),
        P(None, "tp"),
        P(None, "seq", "tp"),
    )
    out_specs = (
        P(None, "seq", "tp"),
        P(None, "seq", "tp"),
        P("seq", "tp"),
        P(),
        P("seq", "tp"),
        P(None, "tp"),
        P("tp"),
        P("tp"),
        P("tp"),
        P("tp"),
        P("tp"),
        P("seq", "tp"),
        P(),
        P("seq", "tp"),
        P("seq", "tp"),
        P(),
        P("seq", "tp"),
        P("seq", "tp"),
        P("seq", "tp"),
        P("seq", "tp"),
    )
    return jax.shard_map(body, mesh=mesh, in_specs=in_specs, out_specs=out_specs, check_vma=False)
```
